32 devices in a mesh: dp: 32 (over z, y, x, core).
Axes of the slice: x: 2, y: 2, z: 4, core: 2. Of those that a mesh axis runs over, the one named last changes fastest.
Arguments:
- images: bfloat16 [2048, 8, 8, 256], P('dp'), may hold values from -50 to 50
- valid_slot: int32 [2048], P('dp'), may hold values from 0 to 1, as said below
- labels: int32 [2048], P('dp'), may hold values from 0 to 9
- conv_one: float32 [2304, 512], replicated, may hold values from -0.125 to 0.125
- conv_two: float32 [4608, 512], replicated, may hold values from -0.09375 to 0.09375
- shortcut: float32 [256, 512], replicated, may hold values from -0.375 to 0.375
- classifier: float32 [512, 10], replicated, may hold values from -0.75 to 0.75
- norm_params: float32 [6, 512], replicated, may hold values from -1.7 to 1.7, as said below
- row_state: float32 [32, 7680], P('dp'), as said below
- col_state: float32 [32, 1546], P('dp'), as said below
- bn_moment: float32 [32, 3072], P('dp'), as said below
Outputs:
- loss_sum: float32 [], replicated
- valid_count: float32 [], replicated
- new_weights: float32 [3678208], P('dp')
- weight_copies: bfloat16 [3678208], replicated
- vote_sum: float32 [3678208], P('dp')
- row_state_new: float32 [32, 7680], P('dp')
- col_state_new: float32 [32, 1546], P('dp')
- bn_moment_new: float32 [32, 3072], P('dp')
The draws below stay inside these ranges and needn't reach their ends.
Inputs may be any that keep to these rules, and one draw needn't show every extreme that they name: `valid_slot`: valid slots become more frequent from the first worker to the last; the last slot is always valid. `norm_params`: gains positive. `row_state`: positive. `col_state`: positive. `bn_moment`: positive.
All inputs are finite; a program needn't handle non-finite values.
Results may differ from the reference program's by a relative error of at most 0.007.
Values may be sent and summed in bfloat16 or wider, within the bound.
A program may use at most 192 MiB of HBM per device.

```python
import math
import jax
import jax.numpy as jnp
from jax import lax

C_IN = 256
C = 512
CLS = 10
SIDE = 4
STEP = 10
SLOTS = 64
WORKERS = 32
IMAGES = 2048
ROWS_ALL = 7680
COLS_ALL = 1546
PARAMS = 3678208


def draw_images(key, part):
    key = jax.random.fold_in(key, 11)
    keys = jax.random.split(key, 3)
    workers = IMAGES // SLOTS
    place = (jnp.arange(IMAGES) // SLOTS).astype(jnp.float32) / max(workers - 1, 1)
    shape_all = (IMAGES, 2 * SIDE, 2 * SIDE, C_IN)
    base = jax.random.truncated_normal(keys[0], -4.0, 4.0, shape_all, jnp.float32)
    rising = 1.0 + 2.0 * place
    per_image = jnp.exp(jax.random.uniform(keys[1], (IMAGES,), jnp.float32, math.log(0.6), math.log(1.6)))
    per_channel = jnp.exp(jax.random.uniform(keys[2], (C_IN,), jnp.float32, math.log(0.4), math.log(2.5)))
    values = base * (rising * per_image)[:, None, None, None] * per_channel
    return values.astype(jnp.bfloat16)


def draw_valid_slot(key, part):
    key = jax.random.fold_in(key, 12)
    workers = IMAGES // SLOTS
    slot_place = jnp.arange(IMAGES, dtype=jnp.int32) // SLOTS
    ticket = jax.random.randint(key, (IMAGES,), 0, 3 * workers)
    chosen = (ticket < workers + 2 * slot_place).astype(jnp.int32)
    return jnp.where(jnp.arange(IMAGES, dtype=jnp.int32) == IMAGES - 1, 1, chosen).astype(jnp.int32)


def draw_norm_params(key, part):
    key = jax.random.fold_in(key, 13)
    keys = jax.random.split(key, 2)
    gains = jnp.exp(jax.random.uniform(keys[0], (3, C), jnp.float32, math.log(0.6), math.log(1.6)))
    shifts = 0.4 * jax.random.truncated_normal(keys[1], -4.0, 4.0, (3, C), jnp.float32)
    return jnp.stack([gains[0], shifts[0], gains[1], shifts[1], gains[2], shifts[2]]).astype(jnp.float32)


def state_spread(key, shape_all):
    return jnp.exp(jax.random.uniform(key, shape_all, jnp.float32, math.log(0.1), math.log(0.75)))


def draw_row_state(key, part):
    key = jax.random.fold_in(key, 14)
    workers = IMAGES // SLOTS
    conv_square = 0.0005 / (SLOTS * workers * workers)
    head_square = 0.05 / (SLOTS * workers * workers)
    place = jnp.arange(ROWS_ALL)
    level = jnp.where(place < 9 * C_IN + 9 * C + C_IN, conv_square, head_square)
    return (state_spread(key, (WORKERS, ROWS_ALL)) * level[None, :]).astype(jnp.float32)


def draw_col_state(key, part):
    key = jax.random.fold_in(key, 15)
    workers = IMAGES // SLOTS
    conv_square = 0.0005 / (SLOTS * workers * workers)
    head_square = 0.05 / (SLOTS * workers * workers)
    place = jnp.arange(COLS_ALL)
    level = jnp.where(place < 3 * C, conv_square, head_square)
    return (state_spread(key, (WORKERS, COLS_ALL)) * level[None, :]).astype(jnp.float32)


def draw_bn_moment(key, part):
    key = jax.random.fold_in(key, 16)
    workers = IMAGES // SLOTS
    conv_square = 0.0005 / (SLOTS * workers * workers)
    return (state_spread(key, (WORKERS, 6 * C)) * conv_square).astype(jnp.float32)


def with_ends(values, stream_key, low, high):
    shape = values.shape
    index_at = [jax.random.randint(jax.random.fold_in(stream_key, axis), (), 0, shape[axis]) for axis in range(len(shape))]
    values = values.at[tuple(index_at)].set(low)
    longest = shape.index(max(shape))
    index_at[longest] = (index_at[longest] + 1) % shape[longest]
    return values.at[tuple(index_at)].set(high)


def centred(rng, dims, deviation, most, kind=jnp.bfloat16):
    drawn = deviation * jax.random.normal(rng, dims, jnp.float32)
    return jnp.clip(drawn, min=-most, max=most).astype(kind)


def setup_inputs(seed: int = 0) -> dict:
    seeds = jax.random.split(jax.random.key(seed), 12)
    images = draw_images(jax.random.fold_in(seeds[11], 71), 0)
    valid_slot = draw_valid_slot(jax.random.fold_in(seeds[11], 71), 0)
    labels = with_ends(jax.random.randint(seeds[2], (IMAGES,), 0, CLS), jax.random.fold_in(seeds[2], 1), 0, CLS - 1).astype(jnp.int32)
    conv_one = centred(seeds[3], (9 * C_IN, C), (9 * C_IN) ** -0.5, 0.125, jnp.float32)
    conv_two = centred(seeds[4], (9 * C, C), (9 * C) ** -0.5, 0.09375, jnp.float32)
    shortcut = centred(seeds[5], (C_IN, C), C_IN ** -0.5, 0.375, jnp.float32)
    classifier = centred(seeds[6], (C, CLS), (C // 9) ** -0.5, 0.75, jnp.float32)
    norm_params = draw_norm_params(jax.random.fold_in(seeds[11], 71), 0)
    row_state = draw_row_state(jax.random.fold_in(seeds[11], 71), 0)
    col_state = draw_col_state(jax.random.fold_in(seeds[11], 71), 0)
    bn_moment = draw_bn_moment(jax.random.fold_in(seeds[11], 71), 0)
    return dict(images=images, valid_slot=valid_slot, labels=labels, conv_one=conv_one, conv_two=conv_two, shortcut=shortcut, classifier=classifier, norm_params=norm_params, row_state=row_state, col_state=col_state, bn_moment=bn_moment)


@jax.custom_vjp
def low(v):
    return lax.optimization_barrier(v.astype(jnp.bfloat16)).astype(jnp.float32)

@jax.custom_vjp
def low_back(v):
    return v

def low_keep(v):
    return (low(v), None)

def low_pass(kept, grad):
    return (grad,)

def back_keep(v):
    return (v, None)

def back_low(kept, grad):
    return (low(grad),)
low.defvjp(low_keep, low_pass)
low_back.defvjp(back_keep, back_low)
EPS_NORM = 1e-05
EPS_ROW = 1e-30
EPS_SCALE = 0.001

def product_high(left, right):
    return jnp.dot(left, right, precision=lax.Precision.HIGHEST, preferred_element_type=jnp.float32)

def patches_strided(image_block):
    out_side = image_block.shape[1] // 2
    padded = jnp.pad(image_block, ((0, 0), (1, 1), (1, 1), (0, 0)))
    pieces = [padded[:, row_off:row_off + 2 * out_side:2, col_off:col_off + 2 * out_side:2, :] for row_off in range(3) for col_off in range(3)]
    return jnp.concatenate(pieces, axis=3)

def patches_same(activity):
    out_side = activity.shape[1]
    padded = jnp.pad(activity, ((0, 0), (1, 1), (1, 1), (0, 0)))
    pieces = [padded[:, row_off:row_off + out_side, col_off:col_off + out_side, :] for row_off in range(3) for col_off in range(3)]
    return jnp.concatenate(pieces, axis=3)

def settle(sum_plain, sum_square, pixels):
    mean_value = sum_plain / pixels
    return (mean_value, lax.rsqrt(sum_square / pixels - mean_value * mean_value + EPS_NORM))

def first_convs(conv_one, shortcut, image_block):
    row_count = image_block.shape[0] * SIDE * SIDE
    patches = patches_strided(image_block).reshape(row_count, -1)
    main_pre = product_high(patches, low(conv_one))
    side_pre = product_high(image_block[:, ::2, ::2, :].reshape(row_count, -1), low(shortcut))
    return (main_pre, side_pre)

def second_conv(main_pre, norm_one, norm_params, conv_two, slot_count):
    hidden_one = (main_pre - norm_one[0]) * norm_one[1] * norm_params[0] + norm_params[1]
    active = low(jax.nn.silu(hidden_one)).reshape(slot_count, SIDE, SIDE, -1)
    return product_high(patches_same(active).reshape(slot_count * SIDE * SIDE, -1), low(conv_two))

def worker_loss(weights, image_block, slot_weight, label_block, norms, denominator):
    conv_one, conv_two, shortcut, classifier, norm_params = weights
    norm_one, norm_two, norm_side = norms
    slot_count = image_block.shape[0]
    main_pre, side_pre = first_convs(conv_one, shortcut, image_block)
    main_pre = low_back(main_pre)
    side_pre = low_back(side_pre)
    main_two = low_back(second_conv(main_pre, norm_one, norm_params, conv_two, slot_count))
    hidden_two = (main_two - norm_two[0]) * norm_two[1] * norm_params[2] + norm_params[3]
    hidden_side = (side_pre - norm_side[0]) * norm_side[1] * norm_params[4] + norm_params[5]
    joined = jax.nn.silu(hidden_two + hidden_side).reshape(slot_count, SIDE * SIDE, -1)
    pooled = low(lax.optimization_barrier(jnp.mean(joined, axis=1)))
    logits = low_back(product_high(pooled, low(classifier)))
    largest = lax.optimization_barrier(jnp.max(logits, axis=1, keepdims=True))
    log_total = largest[:, 0] + jnp.log(lax.optimization_barrier(jnp.sum(jnp.exp(logits - largest), axis=1)))
    picked = lax.optimization_barrier(jnp.sum(jnp.where(label_block[:, None] == jnp.arange(CLS)[None, :], logits, 0.0), axis=1))
    local_sum = jnp.sum(slot_weight * (log_total - picked))
    return (local_sum / denominator, local_sum)

def soft_sign(step_raw):
    clip_by = jnp.maximum(1.0, jnp.sqrt(jnp.mean(step_raw * step_raw)))
    return jnp.tanh(step_raw / clip_by)

def make_votes(grads, rows_old, cols_old, moment_old):
    decay_rate = 1.0 - STEP ** (-0.8)
    row_sizes = [9 * C_IN, 9 * C, C_IN, C]
    col_sizes = [C, C, C, CLS]
    votes, rows_new, cols_new = ([], [], [])
    row_at, col_at = (0, 0)
    for matrix, row_size, col_size in zip(grads[:4], row_sizes, col_sizes):
        square = matrix * matrix + EPS_ROW
        row_part = decay_rate * rows_old[row_at:row_at + row_size] + (1.0 - decay_rate) * lax.optimization_barrier(jnp.mean(square, axis=1))
        col_part = decay_rate * cols_old[col_at:col_at + col_size] + (1.0 - decay_rate) * lax.optimization_barrier(jnp.mean(square, axis=0))
        second = row_part[:, None] * col_part[None, :] / jnp.mean(row_part)
        votes.append(soft_sign(matrix * lax.rsqrt(second)).reshape(-1))
        rows_new.append(row_part)
        cols_new.append(col_part)
        row_at += row_size
        col_at += col_size
    flat_norm = grads[4].reshape(-1)
    moment_new = decay_rate * moment_old + (1.0 - decay_rate) * (flat_norm * flat_norm + EPS_ROW)
    votes.append(soft_sign(flat_norm * lax.rsqrt(moment_new)))
    return (jnp.concatenate(votes), jnp.concatenate(rows_new), jnp.concatenate(cols_new), moment_new)

def reference(images, valid_slot, labels, conv_one, conv_two, shortcut, classifier, norm_params, row_state, col_state, bn_moment):
    workers = IMAGES // SLOTS
    weights = (conv_one, conv_two, shortcut, classifier, norm_params)
    image_blocks = images.reshape(workers, SLOTS, 2 * SIDE, 2 * SIDE, C_IN)
    slot_weights = valid_slot.astype(jnp.float32).reshape(workers, SLOTS)
    label_blocks = labels.reshape(workers, SLOTS)

    def sums_first(carry, item):
        image_block, slot_weight = item
        main_pre, side_pre = first_convs(conv_one, shortcut, image_block.astype(jnp.float32))
        pixel_weight = jnp.repeat(slot_weight, SIDE * SIDE)[:, None]
        terms = (jnp.sum(slot_weight), lax.optimization_barrier(jnp.sum(pixel_weight * main_pre, axis=0)), lax.optimization_barrier(jnp.sum(pixel_weight * main_pre * main_pre, axis=0)), lax.optimization_barrier(jnp.sum(pixel_weight * side_pre, axis=0)), lax.optimization_barrier(jnp.sum(pixel_weight * side_pre * side_pre, axis=0)))
        return (tuple((old_term + new_term for old_term, new_term in zip(carry, terms))), None)
    zero_row = jnp.zeros((C,), jnp.float32)
    first, _ = lax.scan(sums_first, (jnp.zeros((), jnp.float32), zero_row, zero_row, zero_row, zero_row), (image_blocks, slot_weights))
    valid_count = first[0]
    denominator = jnp.maximum(valid_count, 1.0)
    pixels = denominator * (SIDE * SIDE)
    norm_one = settle(first[1], first[2], pixels)
    norm_side = settle(first[3], first[4], pixels)

    def sums_second(carry, item):
        image_block, slot_weight = item
        main_pre, side_pre = first_convs(conv_one, shortcut, image_block.astype(jnp.float32))
        main_two = second_conv(main_pre, norm_one, norm_params, conv_two, SLOTS)
        pixel_weight = jnp.repeat(slot_weight, SIDE * SIDE)[:, None]
        return ((carry[0] + lax.optimization_barrier(jnp.sum(pixel_weight * main_two, axis=0)), carry[1] + lax.optimization_barrier(jnp.sum(pixel_weight * main_two * main_two, axis=0))), None)
    second, _ = lax.scan(sums_second, (zero_row, zero_row), (image_blocks, slot_weights))
    norm_two = settle(second[0], second[1], pixels)
    norms = (norm_one, norm_two, norm_side)

    def worker_step(vote_total, item):
        image_block, slot_weight, label_block, rows_old, cols_old, moment_old = item

        def loss_of(params):
            return worker_loss(params, image_block.astype(jnp.float32), slot_weight, label_block, norms, denominator)
        loss_value, pull_back, local_sum = jax.vjp(loss_of, weights, has_aux=True)
        grads = pull_back(jnp.ones((), jnp.float32))[0]
        votes, rows_new, cols_new, moment_new = make_votes(grads, rows_old, cols_old, moment_old)
        return (vote_total + votes, (local_sum, rows_new, cols_new, moment_new))
    vote_sum, (local_sums, rows_out, cols_out, moment_out) = lax.scan(worker_step, jnp.zeros((PARAMS,), jnp.float32), (image_blocks, slot_weights, label_blocks, row_state, col_state, bn_moment))
    majority = jnp.tanh(vote_sum / math.sqrt(workers))
    flat_old = jnp.concatenate([weight.reshape(-1) for weight in weights])
    scales = jnp.concatenate([jnp.maximum(EPS_SCALE, jnp.sqrt(jnp.mean(weight * weight))) * jnp.ones((weight.size,), jnp.float32) for weight in weights])
    new_weights = flat_old - scales * majority
    return (jnp.sum(local_sums), valid_count, new_weights, new_weights.astype(jnp.bfloat16), vote_sum, rows_out, cols_out, moment_out)
```

```python
import functools
import math

import jax
import jax.numpy as jnp
from jax import lax
from jax.experimental import pallas as pl
from jax.experimental.pallas import tpu as pltpu
from jax.sharding import PartitionSpec as P

STEP = 10
MESH = pl.DeviceIdType.MESH

EPS_NORM = 1e-05
EPS_ROW = 1e-30
EPS_SCALE = 0.001
FORWARD_DIMS = ("NHWC", "HWIO", "NHWC")
WEIGHT_DIMS = ("CHWN", "IHWO", "HWNC")
OWN = 224
HALF = 112
TAIL = 16
PIECE = 32


def conv_apply(maps, kernel, stride, margin):
    return lax.conv_general_dilated(
        maps,
        kernel,
        (stride, stride),
        ((margin, margin), (margin, margin)),
        dimension_numbers=FORWARD_DIMS,
        preferred_element_type=jnp.float32,
    )


def conv_weight_grad(maps, grad_out, stride, low_pad, high_pad):
    result = lax.conv_general_dilated(
        maps,
        grad_out,
        (1, 1),
        ((low_pad, high_pad), (low_pad, high_pad)),
        rhs_dilation=(stride, stride),
        dimension_numbers=WEIGHT_DIMS,
        preferred_element_type=jnp.float32,
    )
    return result.reshape(-1, result.shape[3])


def silu_slope(values):
    sigmoid_part = jax.nn.sigmoid(values)
    return sigmoid_part * (1.0 + values * (1.0 - sigmoid_part))


def settle(sum_plain, sum_square, pixels):
    mean_value = sum_plain / pixels
    return (mean_value, lax.rsqrt(sum_square / pixels - mean_value * mean_value + EPS_NORM))


def first_section(images, kernel_one, kernel_short):
    row_count = images.shape[0] * (images.shape[1] // 2) ** 2
    main_pre = conv_apply(images, kernel_one, 2, 1).reshape(row_count, -1)
    side_pre = conv_apply(images, kernel_short, 2, 0).reshape(row_count, -1)
    return (main_pre, side_pre)


def second_section(main_pre, norm_one, norm_params, kernel_two, slot_count, out_side):
    hidden_one = (main_pre - norm_one[0]) * norm_one[1] * norm_params[0] + norm_params[1]
    active = (
        jax.nn.silu(hidden_one).astype(jnp.bfloat16).reshape(slot_count, out_side, out_side, -1)
    )
    main_two = conv_apply(active, kernel_two, 1, 1).reshape(slot_count * out_side * out_side, -1)
    return (hidden_one, active, main_two)


def masked_moments(pixel_weight, values):
    return (jnp.sum(pixel_weight * values, axis=0), jnp.sum(pixel_weight * values * values, axis=0))


def soft_sign(step_raw):
    clip_by = jnp.maximum(1.0, jnp.sqrt(jnp.mean(step_raw * step_raw)))
    return jnp.tanh(step_raw / clip_by)


def make_votes(grads, rows_old, cols_old, moment_old):
    decay_rate = 1.0 - STEP ** (-0.8)
    votes, rows_new, cols_new = ([], [], [])
    row_at, col_at = (0, 0)
    for matrix in grads[:4]:
        row_size, col_size = matrix.shape
        square = matrix * matrix + EPS_ROW
        row_part = decay_rate * rows_old[row_at : row_at + row_size] + (
            1.0 - decay_rate
        ) * jnp.mean(square, axis=1)
        col_part = decay_rate * cols_old[col_at : col_at + col_size] + (
            1.0 - decay_rate
        ) * jnp.mean(square, axis=0)
        second = row_part[:, None] * col_part[None, :] / jnp.mean(row_part)
        votes.append(soft_sign(matrix * lax.rsqrt(second)))
        rows_new.append(row_part)
        cols_new.append(col_part)
        row_at += row_size
        col_at += col_size
    flat_norm = grads[4].reshape(-1)
    moment_new = decay_rate * moment_old + (1.0 - decay_rate) * (flat_norm * flat_norm + EPS_ROW)
    votes.append(soft_sign(flat_norm * lax.rsqrt(moment_new)))
    return (votes, jnp.concatenate(rows_new), jnp.concatenate(cols_new), moment_new)


def norm_backward(grad_out, pre_value, norm_pair, gain_row):
    normed = (pre_value - norm_pair[0]) * norm_pair[1]
    grad_gain = jnp.sum(grad_out * normed, axis=0)
    grad_shift = jnp.sum(grad_out, axis=0)
    grad_pre = (grad_out * gain_row * norm_pair[1]).astype(jnp.bfloat16)
    return (grad_gain, grad_shift, grad_pre)


def place():
    me = lax.axis_index("dp")
    core = lax.rem(me, 2)
    x = lax.rem(lax.div(me, 2), 2)
    y = lax.rem(lax.div(me, 4), 2)
    z = lax.div(me, 8)
    return me, core, x, y, z


def greet(partners):
    barrier = pltpu.get_barrier_semaphore()
    for partner in partners:
        pl.semaphore_signal(barrier, inc=1, device_id=(partner,), device_id_type=MESH)
    pl.semaphore_wait(barrier, len(partners))


def send(src, dst, send_sem, recv_sem, partner):
    copy = pltpu.make_async_remote_copy(
        src_ref=src,
        dst_ref=dst,
        send_sem=send_sem,
        recv_sem=recv_sem,
        device_id=(partner,),
        device_id_type=MESH,
    )
    copy.start()
    return copy


def sum_kernel(x_ref, out_ref, plane, line, plane_send, plane_recv, line_send, line_recv):
    me = lax.axis_index("dp")
    z, spot = lax.div(me, 8), lax.rem(me, 8)
    near = [z * 8 + lax.rem(spot + k, 8) for k in range(1, 8)]
    far = [lax.rem(z + k, 4) * 8 + spot for k in range(1, 4)]
    greet(near + far)
    copies = [
        send(x_ref, plane.at[spot], plane_send.at[k], plane_recv.at[k], partner)
        for k, partner in enumerate(near)
    ]
    plane[spot] = x_ref[...]
    for copy in copies:
        copy.wait()
    line[z] = functools.reduce(lambda a, b: a + b, [plane[k] for k in range(8)])
    copies = [
        send(line.at[z], line.at[z], line_send.at[k], line_recv.at[k], partner)
        for k, partner in enumerate(far)
    ]
    for copy in copies:
        copy.wait()
    out_ref[...] = (line[0] + line[1]) + (line[2] + line[3])


def sum_all(x, collective_id):
    vmem = pl.BlockSpec(memory_space=pltpu.VMEM)
    return pl.pallas_call(
        sum_kernel,
        out_shape=jax.ShapeDtypeStruct(x.shape, x.dtype),
        in_specs=[vmem],
        out_specs=vmem,
        scratch_shapes=[
            pltpu.VMEM((8,) + x.shape, x.dtype),
            pltpu.VMEM((4,) + x.shape, x.dtype),
            pltpu.SemaphoreType.DMA((7,)),
            pltpu.SemaphoreType.DMA((7,)),
            pltpu.SemaphoreType.DMA((3,)),
            pltpu.SemaphoreType.DMA((3,)),
        ],
        compiler_params=pltpu.CompilerParams(collective_id=collective_id, has_side_effects=True),
        name="sum_all",
    )(x)


def scale_of(row, scales, edges):
    picked = scales[2]
    picked = jnp.where(row < edges[1], scales[1], picked)
    return jnp.where(row < edges[0], scales[0], picked)


def update_kernel(
    edges,
    root,
    scale_ref,
    votes,
    tail_sum,
    tail_weight,
    tail_scale,
    one_ref,
    two_ref,
    short_ref,
    new_ref,
    vote_ref,
    out_ref,
    core_in,
    ax_in,
    by_in,
    plane_in,
    line_in,
    halo_in,
    total,
    weight,
    vote_flat,
    new_flat,
    mine,
    tail_low,
    rs_send,
    rs_recv,
    line_send,
    line_recv,
    halo_sem,
    ag_send,
    ag_recv,
    local_sem,
):
    me, core, x, y, z = place()
    flip_core = me + 1 - 2 * core
    flip_x = me + 2 - 4 * x
    flip_y = me + 4 - 8 * y
    planes = [lax.rem(z + k, 4) for k in range(4)]
    sources = [lax.rem(z + 4 - k, 4) for k in range(4)]
    spot = lax.rem(me, 8)
    line_peers = [plane * 8 + spot for plane in planes]
    before, after = lax.rem(me + 31, 32), lax.rem(me + 1, 32)
    scales = [scale_ref[k] for k in range(3)]

    def fetch(row, count, place_at, sem):
        parts = (
            (one_ref, 0, edges[0]),
            (two_ref, edges[0], edges[1]),
            (short_ref, edges[1], edges[2]),
        )
        for ref, low, high in parts:

            @pl.when(jnp.logical_and(row >= low, row < high))
            def _():
                start = pl.multiple_of(row - low, count)
                pltpu.make_async_copy(
                    ref.at[pl.ds(start, count)], weight.at[pl.ds(place_at, count)], sem
                ).start()

    first_row = me * OWN
    for k in range(OWN // PIECE):
        fetch(first_row + k * PIECE, PIECE, k * PIECE, local_sem.at[0])
    fetch(first_row + OWN, TAIL, OWN, local_sem.at[1])

    greet([flip_core, flip_x, flip_y] + line_peers[1:] + [before, after])

    order = [0, 3, 1, 2]

    core_copies = [
        send(
            votes.at[t, :, :, 1 - core],
            core_in.at[t],
            rs_send.at[0, t],
            rs_recv.at[0, t],
            flip_core,
        )
        for t in order
    ]

    def first_steps(k, t):
        core_copies[k].wait()
        core_in[t] = core_in[t] + votes[t, :, :, core]
        return (
            send(
                core_in.at[t, :, 1 - x, pl.ds(0, HALF)],
                ax_in.at[t],
                rs_send.at[1, t],
                rs_recv.at[1, t],
                flip_x,
            ),
            send(
                core_in.at[t, 1 - y, :, pl.ds(HALF, HALF)],
                by_in.at[t],
                rs_send.at[2, t],
                rs_recv.at[2, t],
                flip_y,
            ),
        )

    def second_steps(t, copies):
        copies[0].wait()
        ax_in[t] = ax_in[t] + core_in[t, :, x, :HALF]
        first = send(
            ax_in.at[t, 1 - y],
            plane_in.at[t, pl.ds(0, HALF)],
            rs_send.at[3, t],
            rs_recv.at[3, t],
            flip_y,
        )
        copies[1].wait()
        by_in[t] = by_in[t] + core_in[t, y, :, HALF:]
        second = send(
            by_in.at[t, 1 - x],
            plane_in.at[t, pl.ds(HALF, HALF)],
            rs_send.at[4, t],
            rs_recv.at[4, t],
            flip_x,
        )
        return first, second

    def line_copy(t):
        return pltpu.make_async_remote_copy(
            src_ref=plane_in.at[t],
            dst_ref=line_in.at[z],
            send_sem=line_send.at[t],
            recv_sem=line_recv.at[z],
            device_id=(t * 8 + spot,),
            device_id_type=MESH,
        )

    def third_steps(t, copies):
        copies[0].wait()
        plane_in[t, :HALF] = plane_in[t, :HALF] + ax_in[t, y]
        copies[1].wait()
        plane_in[t, HALF:] = plane_in[t, HALF:] + by_in[t, x]

        @pl.when(z != t)
        def _():
            line_copy(t).start()

        @pl.when(z == t)
        def _():
            line_in[t] = plane_in[t]

    firsts, seconds = {}, {}
    for k in range(6):
        if k < 4:
            firsts[k] = first_steps(k, order[k])
        if 1 <= k < 5:
            seconds[k - 1] = second_steps(order[k - 1], firsts[k - 1])
        if k >= 2:
            third_steps(order[k - 2], seconds[k - 2])

    for t in range(4):

        @pl.when(z != t)
        def _():
            line_copy(t).wait_send()
            pltpu.make_async_remote_copy(
                src_ref=plane_in.at[t],
                dst_ref=line_in.at[t],
                send_sem=line_send.at[t],
                recv_sem=line_recv.at[t],
                device_id=(t * 8 + spot,),
                device_id_type=MESH,
            ).wait_recv()

    total[pl.ds(0, OWN), :] = functools.reduce(
        lambda a, b: a + b, [line_in[t].astype(jnp.float32) for t in range(4)]
    )
    halo = send(total.at[pl.ds(0, TAIL)], halo_in, halo_sem.at[0], halo_sem.at[1], before)

    pltpu.make_async_copy(
        weight.at[pl.ds(0, OWN)], weight.at[pl.ds(0, OWN)], local_sem.at[0]
    ).wait()

    def flat_rows(row, values, ref):
        for k in range(4):
            ref[pl.ds(row * 4 + k, 8, stride=4), :] = values[:, 128 * k : 128 * (k + 1)]

    def renew(row, scale_row):
        summed = total[pl.ds(row, 8), :]
        fresh = weight[pl.ds(row, 8), :] - scale_row * jnp.tanh(summed * root)
        flat_rows(row, summed, vote_flat)
        flat_rows(row, fresh, new_flat)

    @pl.loop(0, OWN // 8)
    def _(k):
        row = pl.multiple_of(k * 8, 8)
        renew(row, scale_of(first_row + row, scales, edges))

    mine[...] = new_flat[pl.ds(0, 4 * OWN), :].astype(jnp.bfloat16)

    span, part = 4 * OWN, 4 * HALF

    def rows_of(plane, yy, xx, cc, half):
        block = plane * 8 + yy * 4 + xx * 2 + cc
        return pl.ds(pl.multiple_of(block * span + half * part, 16), part)

    own_rows = pl.ds(pl.multiple_of(me * span, 16), span)
    keep = pltpu.make_async_copy(mine, out_ref.at[own_rows], local_sem.at[2])
    keep.start()
    spread = [
        send(mine, out_ref.at[own_rows], ag_send.at[0, k], ag_recv.at[0, k], line_peers[k])
        for k in range(1, 4)
    ]

    halo.wait()

    @pl.when(me < 31)
    def _():
        pltpu.make_async_copy(
            weight.at[pl.ds(OWN, TAIL)], weight.at[pl.ds(OWN, TAIL)], local_sem.at[1]
        ).wait()
        total[pl.ds(OWN, TAIL), :] = halo_in[...]
        for k in range(TAIL // 8):
            renew(OWN + 8 * k, scale_of(first_row + OWN + 8 * k, scales, edges))

    tail_new = tail_weight[...] - tail_scale[...] * jnp.tanh(tail_sum[...] * root)
    weight[pl.ds(OWN, TAIL), :] = tail_new

    @pl.when(me == 31)
    def _():
        for k in range(TAIL // 8):
            flat_rows(OWN + 8 * k, tail_sum[8 * k : 8 * k + 8, :], vote_flat)
            flat_rows(OWN + 8 * k, weight[OWN + 8 * k : OWN + 8 * k + 8, :], new_flat)

    shift = 2 * me
    count = vote_ref.shape[0]
    vote_ref[...] = vote_flat[pl.ds(shift, count), :]
    new_ref[...] = new_flat[pl.ds(shift, count), :]
    for k in range(TAIL // 8):
        flat_rows(OWN + 8 * k, weight[OWN + 8 * k : OWN + 8 * k + 8, :], new_flat)
    tail_low[...] = new_flat[pl.ds(4 * OWN, 4 * TAIL), :].astype(jnp.bfloat16)
    keep_tail = pltpu.make_async_copy(
        tail_low, out_ref.at[pl.ds(32 * span, 4 * TAIL)], local_sem.at[3]
    )
    keep_tail.start()

    keep.wait()

    def piece(plane, yy, xx, cc, half, kind, k, partner):
        rows = rows_of(plane, yy, xx, cc, half)
        return send(
            out_ref.at[rows], out_ref.at[rows], ag_send.at[kind, k], ag_recv.at[kind, k], partner
        )

    stage_one, stage_two, stage_three = [], [], []
    for k, plane in enumerate(sources):
        if k:
            spread[k - 1].wait()
        stage_one.append(
            (
                piece(plane, y, x, core, 0, 1, k, flip_y),
                piece(plane, y, x, core, 1, 2, k, flip_x),
            )
        )
    for k, plane in enumerate(sources):
        stage_one[k][0].wait()
        stage_one[k][1].wait()
        stage_two.append(
            [piece(plane, yy, x, core, 0, 3 + yy, k, flip_x) for yy in range(2)]
            + [piece(plane, y, xx, core, 1, 5 + xx, k, flip_y) for xx in range(2)]
        )
    for k, plane in enumerate(sources):
        for copy in stage_two[k]:
            copy.wait()
        for yy in range(2):
            for xx in range(2):
                rows = pl.ds(
                    pl.multiple_of((plane * 8 + yy * 4 + xx * 2 + core) * span, 16), span
                )
                kind = 7 + 2 * yy + xx
                stage_three.append(
                    send(
                        out_ref.at[rows],
                        out_ref.at[rows],
                        ag_send.at[kind, k],
                        ag_recv.at[kind, k],
                        flip_core,
                    )
                )
    for copy in stage_three:
        copy.wait()
    keep_tail.wait()


def update_weights(
    votes, tail_sum, tail_weight, tail_scale, scales, conv_one, conv_two, shortcut, workers
):
    edges = [conv_one.shape[0]]
    edges.append(edges[0] + conv_two.shape[0])
    edges.append(edges[1] + shortcut.shape[0])
    width = conv_one.shape[1]
    flat_rows = (edges[2] + TAIL) * width // 128
    share = flat_rows // workers
    vmem = pl.BlockSpec(memory_space=pltpu.VMEM)
    hbm = pl.BlockSpec(memory_space=pl.ANY)
    low = jnp.bfloat16
    dma = pltpu.SemaphoreType.DMA
    return pl.pallas_call(
        functools.partial(update_kernel, tuple(edges), 1.0 / math.sqrt(workers)),
        out_shape=(
            jax.ShapeDtypeStruct((share, 128), jnp.float32),
            jax.ShapeDtypeStruct((share, 128), jnp.float32),
            jax.ShapeDtypeStruct((flat_rows, 128), low),
        ),
        in_specs=[pl.BlockSpec(memory_space=pltpu.SMEM)] + [vmem] * 4 + [hbm] * 3,
        out_specs=(vmem, vmem, hbm),
        scratch_shapes=[
            pltpu.VMEM((4, 2, 2, OWN, width), low),
            pltpu.VMEM((4, 2, HALF, width), low),
            pltpu.VMEM((4, 2, HALF, width), low),
            pltpu.VMEM((4, OWN, width), low),
            pltpu.VMEM((4, OWN, width), low),
            pltpu.VMEM((TAIL, width), jnp.float32),
            pltpu.VMEM((OWN + TAIL, width), jnp.float32),
            pltpu.VMEM((OWN + TAIL, width), jnp.float32),
            pltpu.VMEM((4 * (OWN + TAIL), 128), jnp.float32),
            pltpu.VMEM((4 * (OWN + TAIL), 128), jnp.float32),
            pltpu.VMEM((4 * OWN, 128), low),
            pltpu.VMEM((4 * TAIL, 128), low),
            dma((5, 4)),
            dma((5, 4)),
            dma((4,)),
            dma((4,)),
            dma((2,)),
            dma((11, 4)),
            dma((11, 4)),
            dma((4,)),
        ],
        compiler_params=pltpu.CompilerParams(
            collective_id=5, has_side_effects=True, vmem_limit_bytes=48 * 1024 * 1024
        ),
        name="update",
    )(scales, votes, tail_sum, tail_weight, tail_scale, conv_one, conv_two, shortcut)


def scale_for(weight):
    return jnp.maximum(EPS_SCALE, jnp.sqrt(jnp.mean(weight * weight)))


def local(
    spread,
    images,
    valid_slot,
    labels,
    conv_one,
    conv_two,
    shortcut,
    classifier,
    norm_params,
    row_state,
    col_state,
    bn_moment,
):
    in_width = images.shape[3]
    width = conv_one.shape[1]
    kernel_one = conv_one.astype(jnp.bfloat16).reshape(3, 3, in_width, width)
    kernel_two = conv_two.astype(jnp.bfloat16).reshape(3, 3, width, width)
    kernel_short = shortcut.astype(jnp.bfloat16).reshape(1, 1, in_width, width)
    head_low = classifier.astype(jnp.bfloat16)
    slot_count = images.shape[0]
    out_side = images.shape[1] // 2
    pixel_count = out_side * out_side
    slot_weight = valid_slot.astype(jnp.float32)
    pixel_weight = jnp.broadcast_to(slot_weight[:, None], (slot_count, pixel_count)).reshape(-1, 1)
    main_pre, side_pre = first_section(images, kernel_one, kernel_short)
    main_sums = masked_moments(pixel_weight, main_pre)
    side_sums = masked_moments(pixel_weight, side_pre)
    count_row = jnp.broadcast_to(jnp.sum(slot_weight), (width,))
    none_row = jnp.zeros((width,), jnp.float32)
    if spread:
        first_sums = sum_all(
            jnp.stack([*main_sums, *side_sums, count_row, none_row, none_row, none_row]), 1
        )
    else:
        first_sums = lax.psum(jnp.stack([*main_sums, *side_sums, count_row]), "dp")
    valid_count = first_sums[4, 0]
    denominator = jnp.maximum(valid_count, 1.0)
    pixels = denominator * pixel_count
    norm_one = settle(first_sums[0], first_sums[1], pixels)
    norm_side = settle(first_sums[2], first_sums[3], pixels)
    hidden_one, active, main_two = second_section(
        main_pre, norm_one, norm_params, kernel_two, slot_count, out_side
    )
    two_sums = masked_moments(pixel_weight, main_two)
    if spread:
        second_sums = sum_all(jnp.stack([*two_sums] + [none_row] * 6), 2)
    else:
        second_sums = lax.psum(jnp.stack([*two_sums]), "dp")
    norm_two = settle(second_sums[0], second_sums[1], pixels)
    joined_pre = (
        (main_two - norm_two[0]) * norm_two[1] * norm_params[2]
        + norm_params[3]
        + (side_pre - norm_side[0]) * norm_side[1] * norm_params[4]
        + norm_params[5]
    )
    joined = jax.nn.silu(joined_pre).reshape(slot_count, pixel_count, -1)
    pooled = jnp.mean(joined, axis=1).astype(jnp.bfloat16)
    logits = jnp.dot(pooled, head_low, preferred_element_type=jnp.float32)
    largest = jnp.max(logits, axis=1, keepdims=True)
    exp_terms = jnp.exp(logits - largest)
    total_exp = jnp.sum(exp_terms, axis=1, keepdims=True)
    log_total = largest[:, 0] + jnp.log(total_exp[:, 0])
    onehot = (labels[:, None] == jnp.arange(logits.shape[1], dtype=jnp.int32)[None, :]).astype(
        jnp.float32
    )
    local_sum = jnp.sum(slot_weight * (log_total - jnp.sum(onehot * logits, axis=1)))
    grad_logits = ((exp_terms / total_exp - onehot) * (slot_weight / denominator)[:, None]).astype(
        jnp.bfloat16
    )
    grad_head = lax.dot_general(
        pooled, grad_logits, (((0,), (0,)), ((), ())), preferred_element_type=jnp.float32
    )
    grad_pooled = lax.dot_general(
        grad_logits, head_low, (((1,), (1,)), ((), ())), preferred_element_type=jnp.float32
    )
    spread_pooled = jnp.broadcast_to(
        (grad_pooled / pixel_count)[:, None, :], (slot_count, pixel_count, width)
    )
    grad_joined = spread_pooled.reshape(slot_count * pixel_count, width) * silu_slope(joined_pre)
    gain_two, shift_two, grad_two = norm_backward(grad_joined, main_two, norm_two, norm_params[2])
    gain_side, shift_side, grad_side = norm_backward(
        grad_joined, side_pre, norm_side, norm_params[4]
    )
    grad_two_maps = grad_two.reshape(slot_count, out_side, out_side, width)
    grad_side_maps = grad_side.reshape(slot_count, out_side, out_side, width)
    grad_conv_two = conv_weight_grad(active, grad_two_maps, 1, 1, 1)
    grad_short = conv_weight_grad(images, grad_side_maps, 2, 0, -1)
    kernel_turned = jnp.transpose(kernel_two[::-1, ::-1], (0, 1, 3, 2))
    grad_active = conv_apply(grad_two_maps, kernel_turned, 1, 1).reshape(
        slot_count * pixel_count, width
    )
    grad_hidden = grad_active * silu_slope(hidden_one)
    gain_one, shift_one, grad_one = norm_backward(grad_hidden, main_pre, norm_one, norm_params[0])
    grad_conv_one = conv_weight_grad(
        images, grad_one.reshape(slot_count, out_side, out_side, width), 2, 1, 0
    )
    grad_norms = jnp.stack([gain_one, shift_one, gain_two, shift_two, gain_side, shift_side])
    grads = (grad_conv_one, grad_conv_two, grad_short, grad_head, grad_norms)
    votes, rows_new, cols_new, moment_new = make_votes(
        grads, row_state[0], col_state[0], bn_moment[0]
    )
    workers = lax.axis_size("dp")
    weights = (conv_one, conv_two, shortcut, classifier, norm_params)
    scales = [scale_for(weight) for weight in weights]
    tail_vote = jnp.concatenate([votes[3].reshape(-1, width), votes[4].reshape(-1, width)])
    tail_weight = jnp.concatenate([classifier.reshape(-1, width), norm_params])
    if spread:
        loss_rows = jnp.broadcast_to(local_sum, (8, width))
        tail_sum = sum_all(jnp.concatenate([tail_vote, loss_rows]), 3)
        loss_sum = tail_sum[TAIL, 0]
        low_votes = jnp.concatenate([vote.astype(jnp.bfloat16) for vote in votes[:3]])
        head_rows = classifier.size // width
        tail_scale = jnp.concatenate(
            [
                jnp.broadcast_to(scales[3], (head_rows, width)),
                jnp.broadcast_to(scales[4], (TAIL - head_rows, width)),
            ]
        )
        new_mine, vote_mine, copies = update_weights(
            low_votes.reshape(4, 2, 2, 2, OWN, width),
            tail_sum[:TAIL],
            tail_weight,
            tail_scale,
            jnp.stack(scales[:3]),
            conv_one,
            conv_two,
            shortcut,
            workers,
        )
        new_mine, vote_mine, copies = [
            value.reshape(-1) for value in (new_mine, vote_mine, copies)
        ]
    else:
        loss_sum = lax.psum(local_sum, "dp")
        flat_vote = jnp.concatenate([vote.reshape(-1) for vote in votes])
        flat_old = jnp.concatenate([weight.reshape(-1) for weight in weights])
        flat_scale = jnp.concatenate(
            [
                jnp.broadcast_to(scale, (weight.size,))
                for scale, weight in zip(scales, weights)
            ]
        )
        vote_mine = lax.psum_scatter(flat_vote, "dp", tiled=True)
        share = vote_mine.shape[0]
        start = lax.axis_index("dp") * share
        new_mine = lax.dynamic_slice_in_dim(
            flat_old, start, share
        ) - lax.dynamic_slice_in_dim(flat_scale, start, share) * jnp.tanh(
            vote_mine / math.sqrt(workers)
        )
        copies = lax.all_gather(new_mine.astype(jnp.bfloat16), "dp", tiled=True)
    return (
        loss_sum,
        valid_count,
        new_mine,
        copies,
        vote_mine,
        rows_new[None, :],
        cols_new[None, :],
        moment_new[None, :],
    )


def solution(mesh):
    placed = (
        P("dp", None, None, None),
        P("dp"),
        P("dp"),
        P(),
        P(),
        P(),
        P(),
        P(),
        P("dp", None),
        P("dp", None),
        P("dp", None),
    )
    return jax.shard_map(
        functools.partial(local, mesh.shape["dp"] == 32),
        mesh=mesh,
        in_specs=placed,
        out_specs=(P(), P(), P("dp"), P(), P("dp"), P("dp", None), P("dp", None), P("dp", None)),
        check_vma=False,
    )
```

```python
import functools
import math

import jax
import jax.numpy as jnp
from jax import lax
from jax.experimental import pallas as pl
from jax.experimental.pallas import tpu as pltpu
from jax.sharding import PartitionSpec as P

STEP = 10
MESH = pl.DeviceIdType.MESH

EPS_NORM = 1e-05
EPS_ROW = 1e-30
EPS_SCALE = 0.001
FORWARD_DIMS = ("NHWC", "HWIO", "NHWC")
WEIGHT_DIMS = ("CHWN", "IHWO", "HWNC")
OWN = 224
HALF = 112
TAIL = 16
PIECE = 32


def conv_apply(maps, kernel, stride, margin):
    return lax.conv_general_dilated(
        maps,
        kernel,
        (stride, stride),
        ((margin, margin), (margin, margin)),
        dimension_numbers=FORWARD_DIMS,
        preferred_element_type=jnp.float32,
    )


def conv_weight_grad(maps, grad_out, stride, low_pad, high_pad):
    result = lax.conv_general_dilated(
        maps,
        grad_out,
        (1, 1),
        ((low_pad, high_pad), (low_pad, high_pad)),
        rhs_dilation=(stride, stride),
        dimension_numbers=WEIGHT_DIMS,
        preferred_element_type=jnp.float32,
    )
    return result.reshape(-1, result.shape[3])


def silu_slope(values):
    sigmoid_part = jax.nn.sigmoid(values)
    return sigmoid_part * (1.0 + values * (1.0 - sigmoid_part))


def settle(sum_plain, sum_square, pixels):
    mean_value = sum_plain / pixels
    return (mean_value, lax.rsqrt(sum_square / pixels - mean_value * mean_value + EPS_NORM))


def first_section(images, kernel_one, kernel_short):
    row_count = images.shape[0] * (images.shape[1] // 2) ** 2
    main_pre = conv_apply(images, kernel_one, 2, 1).reshape(row_count, -1)
    side_pre = conv_apply(images, kernel_short, 2, 0).reshape(row_count, -1)
    return (main_pre, side_pre)


def second_section(main_pre, norm_one, norm_params, kernel_two, slot_count, out_side):
    hidden_one = (main_pre - norm_one[0]) * norm_one[1] * norm_params[0] + norm_params[1]
    active = (
        jax.nn.silu(hidden_one).astype(jnp.bfloat16).reshape(slot_count, out_side, out_side, -1)
    )
    main_two = conv_apply(active, kernel_two, 1, 1).reshape(slot_count * out_side * out_side, -1)
    return (hidden_one, active, main_two)


def masked_moments(pixel_weight, values):
    return (jnp.sum(pixel_weight * values, axis=0), jnp.sum(pixel_weight * values * values, axis=0))


def soft_sign(step_raw):
    clip_by = jnp.maximum(1.0, jnp.sqrt(jnp.mean(step_raw * step_raw)))
    return jnp.tanh(step_raw / clip_by)


def make_votes(grads, rows_old, cols_old, moment_old):
    decay_rate = 1.0 - STEP ** (-0.8)
    votes, rows_new, cols_new = ([], [], [])
    row_at, col_at = (0, 0)
    for matrix in grads[:4]:
        row_size, col_size = matrix.shape
        square = matrix * matrix + EPS_ROW
        row_part = decay_rate * rows_old[row_at : row_at + row_size] + (
            1.0 - decay_rate
        ) * jnp.mean(square, axis=1)
        col_part = decay_rate * cols_old[col_at : col_at + col_size] + (
            1.0 - decay_rate
        ) * jnp.mean(square, axis=0)
        second = row_part[:, None] * col_part[None, :] / jnp.mean(row_part)
        votes.append(soft_sign(matrix * lax.rsqrt(second)))
        rows_new.append(row_part)
        cols_new.append(col_part)
        row_at += row_size
        col_at += col_size
    flat_norm = grads[4].reshape(-1)
    moment_new = decay_rate * moment_old + (1.0 - decay_rate) * (flat_norm * flat_norm + EPS_ROW)
    votes.append(soft_sign(flat_norm * lax.rsqrt(moment_new)))
    return (votes, jnp.concatenate(rows_new), jnp.concatenate(cols_new), moment_new)


def norm_backward(grad_out, pre_value, norm_pair, gain_row):
    normed = (pre_value - norm_pair[0]) * norm_pair[1]
    grad_gain = jnp.sum(grad_out * normed, axis=0)
    grad_shift = jnp.sum(grad_out, axis=0)
    grad_pre = (grad_out * gain_row * norm_pair[1]).astype(jnp.bfloat16)
    return (grad_gain, grad_shift, grad_pre)


def place():
    me = lax.axis_index("dp")
    core = lax.rem(me, 2)
    x = lax.rem(lax.div(me, 2), 2)
    y = lax.rem(lax.div(me, 4), 2)
    z = lax.div(me, 8)
    return me, core, x, y, z


def greet(partners):
    barrier = pltpu.get_barrier_semaphore()
    for partner in partners:
        pl.semaphore_signal(barrier, inc=1, device_id=(partner,), device_id_type=MESH)
    pl.semaphore_wait(barrier, len(partners))


def send(src, dst, send_sem, recv_sem, partner):
    copy = pltpu.make_async_remote_copy(
        src_ref=src,
        dst_ref=dst,
        send_sem=send_sem,
        recv_sem=recv_sem,
        device_id=(partner,),
        device_id_type=MESH,
    )
    copy.start()
    return copy


def sum_kernel(x_ref, out_ref, plane, line, plane_send, plane_recv, line_send, line_recv):
    me = lax.axis_index("dp")
    z, spot = lax.div(me, 8), lax.rem(me, 8)
    near = [z * 8 + lax.rem(spot + k, 8) for k in range(1, 8)]
    far = [lax.rem(z + k, 4) * 8 + spot for k in range(1, 4)]
    greet(near + far)
    copies = [
        send(x_ref, plane.at[spot], plane_send.at[k], plane_recv.at[k], partner)
        for k, partner in enumerate(near)
    ]
    plane[spot] = x_ref[...]
    for copy in copies:
        copy.wait()
    line[z] = functools.reduce(lambda a, b: a + b, [plane[k] for k in range(8)])
    copies = [
        send(line.at[z], line.at[z], line_send.at[k], line_recv.at[k], partner)
        for k, partner in enumerate(far)
    ]
    for copy in copies:
        copy.wait()
    out_ref[...] = (line[0] + line[1]) + (line[2] + line[3])


def sum_all(x, collective_id):
    vmem = pl.BlockSpec(memory_space=pltpu.VMEM)
    return pl.pallas_call(
        sum_kernel,
        out_shape=jax.ShapeDtypeStruct(x.shape, x.dtype),
        in_specs=[vmem],
        out_specs=vmem,
        scratch_shapes=[
            pltpu.VMEM((8,) + x.shape, x.dtype),
            pltpu.VMEM((4,) + x.shape, x.dtype),
            pltpu.SemaphoreType.DMA((7,)),
            pltpu.SemaphoreType.DMA((7,)),
            pltpu.SemaphoreType.DMA((3,)),
            pltpu.SemaphoreType.DMA((3,)),
        ],
        compiler_params=pltpu.CompilerParams(collective_id=collective_id, has_side_effects=True),
        name="sum_all",
    )(x)


def scale_of(row, scales, edges):
    picked = scales[2]
    picked = jnp.where(row < edges[1], scales[1], picked)
    return jnp.where(row < edges[0], scales[0], picked)


def update_kernel(
    edges,
    root,
    scale_ref,
    votes,
    tail_sum,
    tail_weight,
    tail_scale,
    one_ref,
    two_ref,
    short_ref,
    new_ref,
    vote_ref,
    out_ref,
    core_in,
    ax_in,
    by_in,
    plane_in,
    line_in,
    halo_in,
    total,
    weight,
    vote_flat,
    new_flat,
    mine,
    tail_low,
    rs_send,
    rs_recv,
    line_send,
    line_recv,
    halo_sem,
    ag_send,
    ag_recv,
    local_sem,
):
    me, core, x, y, z = place()
    flip_core = me + 1 - 2 * core
    flip_x = me + 2 - 4 * x
    flip_y = me + 4 - 8 * y
    planes = [lax.rem(z + k, 4) for k in range(4)]
    sources = [lax.rem(z + 4 - k, 4) for k in range(4)]
    spot = lax.rem(me, 8)
    line_peers = [plane * 8 + spot for plane in planes]
    before, after = lax.rem(me + 31, 32), lax.rem(me + 1, 32)
    scales = [scale_ref[k] for k in range(3)]

    def fetch(row, count, place_at, sem):
        parts = (
            (one_ref, 0, edges[0]),
            (two_ref, edges[0], edges[1]),
            (short_ref, edges[1], edges[2]),
        )
        for ref, low, high in parts:

            @pl.when(jnp.logical_and(row >= low, row < high))
            def _():
                start = pl.multiple_of(row - low, count)
                pltpu.make_async_copy(
                    ref.at[pl.ds(start, count)], weight.at[pl.ds(place_at, count)], sem
                ).start()

    first_row = me * OWN
    for k in range(OWN // PIECE):
        fetch(first_row + k * PIECE, PIECE, k * PIECE, local_sem.at[0])
    fetch(first_row + OWN, TAIL, OWN, local_sem.at[1])

    greet([flip_core, flip_x, flip_y] + line_peers[1:] + [before, after])

    order = [0, 3, 1, 2]

    core_copies = [
        send(
            votes.at[t, :, :, 1 - core],
            core_in.at[t],
            rs_send.at[0, t],
            rs_recv.at[0, t],
            flip_core,
        )
        for t in order
    ]

    def first_steps(k, t):
        core_copies[k].wait()
        core_in[t] = core_in[t] + votes[t, :, :, core]
        return (
            send(
                core_in.at[t, :, 1 - x, pl.ds(0, HALF)],
                ax_in.at[t],
                rs_send.at[1, t],
                rs_recv.at[1, t],
                flip_x,
            ),
            send(
                core_in.at[t, 1 - y, :, pl.ds(HALF, HALF)],
                by_in.at[t],
                rs_send.at[2, t],
                rs_recv.at[2, t],
                flip_y,
            ),
        )

    def second_steps(t, copies):
        copies[0].wait()
        ax_in[t] = ax_in[t] + core_in[t, :, x, :HALF]
        first = send(
            ax_in.at[t, 1 - y],
            plane_in.at[t, pl.ds(0, HALF)],
            rs_send.at[3, t],
            rs_recv.at[3, t],
            flip_y,
        )
        copies[1].wait()
        by_in[t] = by_in[t] + core_in[t, y, :, HALF:]
        second = send(
            by_in.at[t, 1 - x],
            plane_in.at[t, pl.ds(HALF, HALF)],
            rs_send.at[4, t],
            rs_recv.at[4, t],
            flip_x,
        )
        return first, second

    def line_copy(t):
        return pltpu.make_async_remote_copy(
            src_ref=plane_in.at[t],
            dst_ref=line_in.at[z],
            send_sem=line_send.at[t],
            recv_sem=line_recv.at[z],
            device_id=(t * 8 + spot,),
            device_id_type=MESH,
        )

    def third_steps(t, copies):
        copies[0].wait()
        plane_in[t, :HALF] = plane_in[t, :HALF] + ax_in[t, y]
        copies[1].wait()
        plane_in[t, HALF:] = plane_in[t, HALF:] + by_in[t, x]

        @pl.when(z != t)
        def _():
            line_copy(t).start()

        @pl.when(z == t)
        def _():
            line_in[t] = plane_in[t]

    firsts, seconds = {}, {}
    for k in range(6):
        if k < 4:
            firsts[k] = first_steps(k, order[k])
        if 1 <= k < 5:
            seconds[k - 1] = second_steps(order[k - 1], firsts[k - 1])
        if k >= 2:
            third_steps(order[k - 2], seconds[k - 2])

    for t in range(4):

        @pl.when(z != t)
        def _():
            line_copy(t).wait_send()
            pltpu.make_async_remote_copy(
                src_ref=plane_in.at[t],
                dst_ref=line_in.at[t],
                send_sem=line_send.at[t],
                recv_sem=line_recv.at[t],
                device_id=(t * 8 + spot,),
                device_id_type=MESH,
            ).wait_recv()

    total[pl.ds(0, OWN), :] = functools.reduce(
        lambda a, b: a + b, [line_in[t].astype(jnp.float32) for t in range(4)]
    )
    halo = send(total.at[pl.ds(0, TAIL)], halo_in, halo_sem.at[0], halo_sem.at[1], before)

    pltpu.make_async_copy(
        weight.at[pl.ds(0, OWN)], weight.at[pl.ds(0, OWN)], local_sem.at[0]
    ).wait()

    def flat_rows(row, values, ref):
        for k in range(4):
            ref[pl.ds(row * 4 + k, 8, stride=4), :] = values[:, 128 * k : 128 * (k + 1)]

    def renew(row, scale_row):
        summed = total[pl.ds(row, 8), :]
        fresh = weight[pl.ds(row, 8), :] - scale_row * jnp.tanh(summed * root)
        flat_rows(row, summed, vote_flat)
        flat_rows(row, fresh, new_flat)

    @pl.loop(0, OWN // 8)
    def _(k):
        row = pl.multiple_of(k * 8, 8)
        renew(row, scale_of(first_row + row, scales, edges))

    mine[...] = new_flat[pl.ds(0, 4 * OWN), :].astype(jnp.bfloat16)

    span, part = 4 * OWN, 4 * HALF

    def rows_of(plane, yy, xx, cc, half):
        block = plane * 8 + yy * 4 + xx * 2 + cc
        return pl.ds(pl.multiple_of(block * span + half * part, 16), part)

    own_rows = pl.ds(pl.multiple_of(me * span, 16), span)
    keep = pltpu.make_async_copy(mine, out_ref.at[own_rows], local_sem.at[2])
    keep.start()
    spread = [
        send(mine, out_ref.at[own_rows], ag_send.at[0, k], ag_recv.at[0, k], line_peers[k])
        for k in range(1, 4)
    ]

    halo.wait()

    @pl.when(me < 31)
    def _():
        pltpu.make_async_copy(
            weight.at[pl.ds(OWN, TAIL)], weight.at[pl.ds(OWN, TAIL)], local_sem.at[1]
        ).wait()
        total[pl.ds(OWN, TAIL), :] = halo_in[...]
        for k in range(TAIL // 8):
            renew(OWN + 8 * k, scale_of(first_row + OWN + 8 * k, scales, edges))

    tail_new = tail_weight[...] - tail_scale[...] * jnp.tanh(tail_sum[...] * root)
    weight[pl.ds(OWN, TAIL), :] = tail_new

    @pl.when(me == 31)
    def _():
        for k in range(TAIL // 8):
            flat_rows(OWN + 8 * k, tail_sum[8 * k : 8 * k + 8, :], vote_flat)
            flat_rows(OWN + 8 * k, weight[OWN + 8 * k : OWN + 8 * k + 8, :], new_flat)

    shift = 2 * me
    count = vote_ref.shape[0]
    vote_ref[...] = vote_flat[pl.ds(shift, count), :]
    new_ref[...] = new_flat[pl.ds(shift, count), :]
    for k in range(TAIL // 8):
        flat_rows(OWN + 8 * k, weight[OWN + 8 * k : OWN + 8 * k + 8, :], new_flat)
    tail_low[...] = new_flat[pl.ds(4 * OWN, 4 * TAIL), :].astype(jnp.bfloat16)
    keep_tail = pltpu.make_async_copy(
        tail_low, out_ref.at[pl.ds(32 * span, 4 * TAIL)], local_sem.at[3]
    )
    keep_tail.start()

    keep.wait()

    def piece(plane, yy, xx, cc, half, kind, k, partner):
        rows = rows_of(plane, yy, xx, cc, half)
        return send(
            out_ref.at[rows], out_ref.at[rows], ag_send.at[kind, k], ag_recv.at[kind, k], partner
        )

    stage_one, stage_two, stage_three = [], [], []
    for k, plane in enumerate(sources):
        if k:
            spread[k - 1].wait()
        stage_one.append(
            (
                piece(plane, y, x, core, 0, 1, k, flip_y),
                piece(plane, y, x, core, 1, 2, k, flip_x),
            )
        )
    for k, plane in enumerate(sources):
        stage_one[k][0].wait()
        stage_one[k][1].wait()
        stage_two.append(
            [piece(plane, yy, x, core, 0, 3 + yy, k, flip_x) for yy in range(2)]
            + [piece(plane, y, xx, core, 1, 5 + xx, k, flip_y) for xx in range(2)]
        )
    for k, plane in enumerate(sources):
        for copy in stage_two[k]:
            copy.wait()
        for yy in range(2):
            for xx in range(2):
                rows = pl.ds(
                    pl.multiple_of((plane * 8 + yy * 4 + xx * 2 + core) * span, 16), span
                )
                kind = 7 + 2 * yy + xx
                stage_three.append(
                    send(
                        out_ref.at[rows],
                        out_ref.at[rows],
                        ag_send.at[kind, k],
                        ag_recv.at[kind, k],
                        flip_core,
                    )
                )
    for copy in stage_three:
        copy.wait()
    keep_tail.wait()


def update_weights(
    votes, tail_sum, tail_weight, tail_scale, scales, conv_one, conv_two, shortcut, workers
):
    edges = [conv_one.shape[0]]
    edges.append(edges[0] + conv_two.shape[0])
    edges.append(edges[1] + shortcut.shape[0])
    width = conv_one.shape[1]
    flat_rows = (edges[2] + TAIL) * width // 128
    share = flat_rows // workers
    vmem = pl.BlockSpec(memory_space=pltpu.VMEM)
    hbm = pl.BlockSpec(memory_space=pl.ANY)
    low = jnp.bfloat16
    dma = pltpu.SemaphoreType.DMA
    return pl.pallas_call(
        functools.partial(update_kernel, tuple(edges), 1.0 / math.sqrt(workers)),
        out_shape=(
            jax.ShapeDtypeStruct((share, 128), jnp.float32),
            jax.ShapeDtypeStruct((share, 128), jnp.float32),
            jax.ShapeDtypeStruct((flat_rows, 128), low),
        ),
        in_specs=[pl.BlockSpec(memory_space=pltpu.SMEM)] + [vmem] * 4 + [hbm] * 3,
        out_specs=(vmem, vmem, hbm),
        scratch_shapes=[
            pltpu.VMEM((4, 2, 2, OWN, width), low),
            pltpu.VMEM((4, 2, HALF, width), low),
            pltpu.VMEM((4, 2, HALF, width), low),
            pltpu.VMEM((4, OWN, width), low),
            pltpu.VMEM((4, OWN, width), low),
            pltpu.VMEM((TAIL, width), jnp.float32),
            pltpu.VMEM((OWN + TAIL, width), jnp.float32),
            pltpu.VMEM((OWN + TAIL, width), jnp.float32),
            pltpu.VMEM((4 * (OWN + TAIL), 128), jnp.float32),
            pltpu.VMEM((4 * (OWN + TAIL), 128), jnp.float32),
            pltpu.VMEM((4 * OWN, 128), low),
            pltpu.VMEM((4 * TAIL, 128), low),
            dma((5, 4)),
            dma((5, 4)),
            dma((4,)),
            dma((4,)),
            dma((2,)),
            dma((11, 4)),
            dma((11, 4)),
            dma((4,)),
        ],
        compiler_params=pltpu.CompilerParams(
            collective_id=5, has_side_effects=True, vmem_limit_bytes=48 * 1024 * 1024
        ),
        name="update",
    )(scales, votes, tail_sum, tail_weight, tail_scale, conv_one, conv_two, shortcut)


def settle_rows(sums, pixels, gain, shift):
    mean = sums[0] / pixels
    inv = lax.rsqrt(sums[1] / pixels - mean * mean + EPS_NORM)
    slope = gain * inv
    return mean, inv, slope, shift - mean * slope


def gate(values):
    return 0.5 * jnp.tanh(0.5 * values) + 0.5


def eye_mask(rows, columns, offset=0):
    down = lax.broadcasted_iota(jnp.int32, (rows, columns), 0) + offset
    return down == lax.broadcasted_iota(jnp.int32, (rows, columns), 1)


def column_of(row, size):
    spread = jnp.where(eye_mask(size, size), jnp.broadcast_to(row, (size, size)), 0)
    return jnp.sum(spread, axis=1, keepdims=True)


def total_of(values):
    return jnp.sum(jnp.sum(values, axis=0, keepdims=True), axis=1, keepdims=True)


def fold(values):
    return jnp.sum(values.reshape(values.shape[0] // 8, 8, values.shape[1]), axis=0)


def cast_weight(source, target, square_ref, taps, depth):
    step = 128
    square_ref[...] = jnp.zeros_like(square_ref)
    for tap in range(taps):
        new_tap = (tap % 3) * 3 + tap // 3

        @pl.loop(0, depth // step)
        def _(k):
            start = pl.multiple_of(k * step, step)
            values = source[pl.ds(tap * depth + start, step), :]
            target[new_tap, pl.ds(start, step), :] = values.astype(jnp.bfloat16)
            square_ref[...] += fold(values * values)


def factored_votes(
    grad, rows, row_block, rows_ref, rows_new, col_old, level, votes, vote_at
):
    width = grad.shape[1]
    keep = 1.0 - STEP ** (-0.8)
    step = 128
    quarters = width // 128

    def first(k, carry):
        col_sum, row_sum = carry
        start = pl.multiple_of(k * step, step)
        old = rows_ref[pl.ds(row_block + k, 1), :] * keep
        line = jnp.zeros((8, 128), jnp.float32)
        for m in range(step // 8):
            block = grad[pl.ds(start + 8 * m, 8), :]
            square = block * block
            col_sum = col_sum + square
            part = square[:, :128]
            for q in range(1, quarters):
                part = part + square[:, 128 * q : 128 * (q + 1)]
            part = part * ((1.0 - keep) / width)
            diagonal = eye_mask(8, 128, 8 * m)
            part = part + jnp.where(diagonal, jnp.broadcast_to(old, (8, 128)), 0.0)
            row = jnp.sum(part, axis=1, keepdims=True) + (1.0 - keep) * EPS_ROW
            row = jnp.broadcast_to(row, (8, 128))
            level[pl.ds(start + 8 * m, 8), :] = row
            row_sum = row_sum + row
            line = line + jnp.where(diagonal, row, 0.0)
        rows_new[pl.ds(row_block + k, 1), :] = jnp.sum(line, axis=0, keepdims=True)
        return col_sum, row_sum

    col_sum, row_sum = lax.fori_loop(
        0,
        rows // step,
        first,
        (jnp.zeros((8, width), jnp.float32), jnp.zeros((8, 128), jnp.float32)),
    )
    col_new = keep * col_old + (1.0 - keep) * (
        jnp.sum(col_sum, axis=0, keepdims=True) / rows + EPS_ROW
    )
    scale = lax.rsqrt(col_new)
    root_mean = jnp.sqrt(jnp.sum(row_sum, axis=0, keepdims=True) / rows)

    def second(k, carry):
        start = pl.multiple_of(k * step, step)
        for m in range(step // 8):
            here = pl.ds(start + 8 * m, 8)
            factor = lax.rsqrt(level[here, :]) * root_mean
            level[here, :] = factor
            raw = grad[here, :] * scale
            power = raw * raw
            part = power[:, :128]
            for q in range(1, quarters):
                part = part + power[:, 128 * q : 128 * (q + 1)]
            carry = carry + part * (factor * factor)
        return carry

    power = lax.fori_loop(0, rows // step, second, jnp.zeros((8, 128), jnp.float32))
    clip = jnp.maximum(1.0, jnp.sqrt(total_of(power) / (rows * width)))
    scale = scale / clip

    def third(k, _):
        start = pl.multiple_of(k * step, step)
        for m in range(step // 16):
            here = pl.ds(start + 16 * m, 16)
            factor = level[here, :]
            factor = jnp.concatenate([factor] * quarters, axis=1)
            vote = jnp.tanh(grad[here, :] * factor * scale)
            votes[pl.ds(vote_at + start + 16 * m, 16), :] = vote.astype(jnp.bfloat16)
        return 0

    lax.fori_loop(0, rows // step, third, 0)
    return col_new


def worker_kernel(
    xs,
    one_hbm,
    two_hbm,
    short_hbm,
    head_ref,
    norm_ref,
    valid_ref,
    label_ref,
    row_ref,
    col_ref,
    moment_ref,
    votes,
    tail_ref,
    scale_ref,
    count_ref,
    row_new,
    col_new,
    moment_new,
    grad_one,
    grad_two,
    grad_short,
    low_one,
    low_two,
    low_short,
    main_pre,
    side_pre,
    main_two,
    active,
    back_two,
    back_one,
    back_side,
    active_t,
    xs_t,
    head_pad,
    level,
    square,
    post,
    plane,
    line,
    fetch_sem,
    plane_send,
    plane_recv,
    line_send,
    line_recv,
):
    slots, in_width = xs.shape[4:]
    width = main_pre.shape[1]
    side = 4
    band = side * slots
    pixel_count = side * side
    classes = head_ref.shape[1]
    keep = 1.0 - STEP ** (-0.8)
    low = jnp.bfloat16
    f32 = jnp.float32

    me = lax.axis_index("dp")
    z, spot = lax.div(me, 8), lax.rem(me, 8)
    near = [z * 8 + lax.rem(spot + k, 8) for k in range(1, 8)]
    far = [lax.rem(z + k, 4) * 8 + spot for k in range(1, 4)]

    fetches = [
        pltpu.make_async_copy(source, target, fetch_sem.at[k])
        for k, (source, target) in enumerate(
            ((one_hbm, grad_one), (short_hbm, grad_short), (two_hbm, grad_two))
        )
    ]
    for fetch in fetches:
        fetch.start()
    barrier = pltpu.get_barrier_semaphore()
    for partner in near + far:
        pl.semaphore_signal(barrier, inc=1, device_id=(partner,), device_id_type=MESH)

    def scale_row(row, weight_square, size):
        mean = total_of(weight_square) / size
        value = jnp.maximum(EPS_SCALE, jnp.sqrt(mean))
        scale_ref[row : row + 1, :] = jnp.broadcast_to(value, (1, width))

    def exchange_start(which, values):
        post[which] = values
        plane[which, spot] = values
        return [
            send(
                post.at[which],
                plane.at[which, spot],
                plane_send.at[which, k],
                plane_recv.at[which, k],
                partner,
            )
            for k, partner in enumerate(near)
        ]

    def exchange_middle(which, copies):
        for copy in copies:
            copy.wait()
        line[which, z] = functools.reduce(lambda a, b: a + b, [plane[which, k] for k in range(8)])
        return [
            send(
                line.at[which, z],
                line.at[which, z],
                line_send.at[which, k],
                line_recv.at[which, k],
                partner,
            )
            for k, partner in enumerate(far)
        ]

    def exchange_end(which, copies):
        for copy in copies:
            copy.wait()
        return (line[which, 0] + line[which, 1]) + (line[which, 2] + line[which, 3])

    valid_column = column_of(valid_ref[...].astype(f32), slots)
    weight_slot = jnp.broadcast_to(valid_column, (slots, width))
    weight_band = jnp.concatenate([weight_slot] * side, axis=0)

    fetches[0].wait()
    cast_weight(grad_one, low_one, square, 9, in_width)
    scale_row(0, square[...], grad_one.size)
    fetches[1].wait()
    cast_weight(grad_short, low_short, square, 1, in_width)
    scale_row(2, square[...], grad_short.size)

    def image_taps(j):
        pieces = []
        for b in range(3):
            column = j if b else j - 1
            if column < 0:
                continue
            across = 0 if b == 1 else 1
            for a in range(3):
                if a == 1:
                    piece = xs[across, column, 0].reshape(band, in_width)
                elif a == 2:
                    piece = xs[across, column, 1].reshape(band, in_width)
                else:
                    piece = xs[across, column, 1, : side - 1].reshape(band - slots, in_width)
                    piece = jnp.concatenate([jnp.zeros((slots, in_width), low), piece], axis=0)
                pieces.append(piece)
        return jnp.concatenate(pieces, axis=1)

    def moments(values):
        weighted = values * weight_band
        return (
            jnp.sum(weighted, axis=0, keepdims=True),
            jnp.sum(weighted * values, axis=0, keepdims=True),
        )

    def add_up(old, new):
        return [a + b for a, b in zip(old, new)]

    none = jnp.zeros((1, width), f32)
    main_sums, side_sums = [none, none], [none, none]
    for j in range(side):
        here = pl.ds(j * band, band)
        low_rows = low_one[3 if j == 0 else 0 :].reshape(-1, width)
        value = jnp.dot(image_taps(j), low_rows, preferred_element_type=f32)
        main_pre[here, :] = value
        main_sums = add_up(main_sums, moments(value))
        value = jnp.dot(
            xs[0, j, 0].reshape(band, in_width), low_short[0], preferred_element_type=f32
        )
        side_pre[here, :] = value
        side_sums = add_up(side_sums, moments(value))

    count = jnp.broadcast_to(jnp.sum(valid_column, axis=0, keepdims=True), (1, width))
    pl.semaphore_wait(barrier, len(near) + len(far))
    copies = exchange_start(
        0, jnp.concatenate(main_sums + side_sums + [count, none, none, none], axis=0)
    )
    fetches[2].wait()
    cast_weight(grad_two, low_two, square, 9, width)
    scale_row(1, square[...], grad_two.size)
    copies = exchange_middle(0, copies)
    for across in range(2):
        for down in range(2):
            for j in range(side):
                block = xs[across, j, down].reshape(band, in_width)
                xs_t[across, down, :, j * band : (j + 1) * band] = block.T
    border = jnp.zeros((side, 1, slots, width), low)
    active[:, 0:1] = border
    active[:, side + 1 :] = border
    back_two[:, 0:1] = border
    back_two[:, side + 1 :] = border
    back_one[:, side:] = border
    head_pad[...] = jnp.zeros_like(head_pad)
    head_pad[:, :classes] = head_ref[...]
    head = head_pad[...]
    scale_row(3, fold(head * head)[:, :128], head_ref.size)
    params = norm_ref[...]
    scale_row(4, params * params, norm_ref.size)
    sums = exchange_end(0, copies)

    valid_count = sums[4:5]
    count_ref[...] = valid_count
    denominator = jnp.maximum(valid_count, 1.0)
    pixels = denominator * pixel_count
    gains = [norm_ref[k : k + 1, :] for k in range(6)]
    mean_one, inv_one, slope_one, base_one = settle_rows(
        (sums[0:1], sums[1:2]), pixels, gains[0], gains[1]
    )
    mean_side, inv_side, slope_side, base_side = settle_rows(
        (sums[2:3], sums[3:4]), pixels, gains[4], gains[5]
    )

    for j in range(side):
        hidden = main_pre[pl.ds(j * band, band), :] * slope_one + base_one
        active[j, 1 : side + 1] = (
            (hidden * gate(hidden)).astype(low).reshape(side, slots, width)
        )
    two_sums = [none, none]
    for j in range(side):
        taps = [b for b in range(3) if 0 <= j + b - 1 < side]
        pieces = [
            active[j + b - 1, a : a + side].reshape(band, width) for b in taps for a in range(3)
        ]
        low_rows = low_two[3 * taps[0] : 3 * taps[-1] + 3].reshape(-1, width)
        value = jnp.dot(jnp.concatenate(pieces, axis=1), low_rows, preferred_element_type=f32)
        main_two[pl.ds(j * band, band), :] = value
        two_sums = add_up(two_sums, moments(value))
    copies = exchange_start(1, jnp.concatenate(two_sums + [none] * 6, axis=0))
    for j in range(side):
        block = active[j, 1 : side + 1].reshape(band, width)
        active_t[:, j * band : (j + 1) * band] = block.T
    copies = exchange_middle(1, copies)
    sums = exchange_end(1, copies)
    mean_two, inv_two, slope_two, base_two = settle_rows(
        (sums[0:1], sums[1:2]), pixels, gains[2], gains[3]
    )

    base_joined = base_two + base_side

    def joined_of(here):
        return main_two[here, :] * slope_two + side_pre[here, :] * slope_side + base_joined

    pooled = jnp.zeros((slots, width), f32)
    for p in range(pixel_count):
        joined = joined_of(pl.ds(p * slots, slots))
        pooled = pooled + joined * gate(joined)
    pooled = (pooled / pixel_count).astype(low)
    head_low = head_pad[...].astype(low)
    logits = jnp.dot(pooled, head_low, preferred_element_type=f32)
    lane = lax.broadcasted_iota(jnp.int32, logits.shape, 1)
    real = lane < classes
    largest = jnp.max(jnp.where(real, logits, -jnp.inf), axis=1, keepdims=True)
    powers = jnp.where(real, jnp.exp(jnp.where(real, logits - largest, 0.0)), 0.0)
    total_power = jnp.sum(powers, axis=1, keepdims=True)
    label_column = column_of(label_ref[...].astype(f32), slots).astype(jnp.int32)
    onehot = jnp.where(lane == label_column, 1.0, 0.0)
    entropy = largest + jnp.log(total_power) - jnp.sum(onehot * logits, axis=1, keepdims=True)
    loss = jnp.sum(entropy * valid_column, axis=0, keepdims=True)
    grad_logits = (
        (powers / total_power - onehot) * (valid_column / denominator[:, :1])
    ).astype(low)
    grad_head = lax.dot_general(
        grad_logits, pooled, (((0,), (0,)), ((), ())), preferred_element_type=f32
    )[:16]
    grad_pooled = lax.dot_general(
        grad_logits, head_low, (((1,), (1,)), ((), ())), preferred_element_type=f32
    )
    grad_pooled = grad_pooled / pixel_count

    gain_two, gain_side, shift_two = none, none, none
    for p in range(pixel_count):
        here = pl.ds(p * slots, slots)
        joined = joined_of(here)
        opened = gate(joined)
        grad = grad_pooled * (opened * (1.0 + joined * (1.0 - opened)))
        shift_two = shift_two + jnp.sum(grad, axis=0, keepdims=True)
        gain_two = gain_two + jnp.sum(
            grad * ((main_two[here, :] - mean_two) * inv_two), axis=0, keepdims=True
        )
        gain_side = gain_side + jnp.sum(
            grad * ((side_pre[here, :] - mean_side) * inv_side), axis=0, keepdims=True
        )
        back_two[p // side, 1 + p % side] = (grad * slope_two).astype(low)
        back_side[here, :] = (grad * slope_side).astype(low)

    grad_short[...] = jnp.dot(xs_t[0, 0], back_side[...], preferred_element_type=f32)
    for b in range(3):
        first, last = max(0, b - 1), min(side, side + b - 1)
        left = active_t[:, first * band : last * band]
        for a in range(3):
            right = back_two[first - b + 1 : last - b + 1, 2 - a : 2 - a + side]
            grad_two[pl.ds((a * 3 + b) * width, width), :] = jnp.dot(
                left, right.reshape(-1, width), preferred_element_type=f32
            )

    gain_one, shift_one = none, none
    for j in range(side):
        taps = [b for b in range(3) if 0 <= j - b + 1 < side]
        pieces = [
            back_two[j - b + 1, 2 - a : 2 - a + side].reshape(band, width)
            for b in taps
            for a in range(3)
        ]
        weights = jnp.concatenate([low_two[b * 3 + a] for b in taps for a in range(3)], axis=1)
        grad = lax.dot_general(
            jnp.concatenate(pieces, axis=1),
            weights,
            (((1,), (1,)), ((), ())),
            preferred_element_type=f32,
        )
        before = main_pre[pl.ds(j * band, band), :]
        hidden = before * slope_one + base_one
        opened = gate(hidden)
        grad = grad * (opened * (1.0 + hidden * (1.0 - opened)))
        shift_one = shift_one + jnp.sum(grad, axis=0, keepdims=True)
        gain_one = gain_one + jnp.sum(
            grad * ((before - mean_one) * inv_one), axis=0, keepdims=True
        )
        back_one[j, :side] = (grad * slope_one).astype(low).reshape(side, slots, width)

    for b in range(3):
        first, last = (0, side - 1) if b == 0 else (0, side)
        shift = 1 if b == 0 else 0
        for a in range(3):
            left = xs_t[0 if b == 1 else 1, 0 if a == 1 else 1, :, first * band : last * band]
            start = 1 if a == 0 else 0
            right = back_one[first + shift : last + shift, start : start + side]
            grad_one[pl.ds((a * 3 + b) * in_width, in_width), :] = jnp.dot(
                left, right.reshape(-1, width), preferred_element_type=f32
            )

    row_at, vote_at = 0, 0
    for k, grad in enumerate((grad_one, grad_two, grad_short)):
        here = pl.ds(k * width, width)
        col_new[:, here] = factored_votes(
            grad,
            grad.shape[0],
            row_at,
            row_ref,
            row_new,
            col_ref[:, here],
            level,
            votes,
            vote_at,
        )
        row_at += grad.shape[0] // 128
        vote_at += grad.shape[0]

    square_head = grad_head * grad_head + EPS_ROW
    real = lax.broadcasted_iota(jnp.int32, square_head.shape, 0) < classes
    square_head = jnp.where(real, square_head, 0.0)
    old = jnp.concatenate([row_ref[row_at + k : row_at + k + 1, :] for k in range(4)], axis=1)
    row = keep * old + (1.0 - keep) * jnp.sum(square_head, axis=0, keepdims=True) / classes
    for k in range(4):
        row_new[row_at + k : row_at + k + 1, :] = row[:, 128 * k : 128 * (k + 1)]
    diagonal = eye_mask(16, classes)
    old = jnp.broadcast_to(col_ref[:, 3 * width :], (16, classes))
    old = jnp.sum(jnp.where(diagonal, old, 0.0), axis=1, keepdims=True)
    column = keep * old + (1.0 - keep) * jnp.sum(square_head, axis=1, keepdims=True) / width
    col_new[:, 3 * width :] = jnp.sum(
        jnp.where(diagonal, jnp.broadcast_to(column, (16, classes)), 0.0), axis=0, keepdims=True
    )
    real_column = lax.broadcasted_iota(jnp.int32, column.shape, 0) < classes
    column = jnp.where(real_column, column, 1.0)
    mean = jnp.sum(row, axis=1, keepdims=True) / width
    raw = grad_head * (lax.rsqrt(row) * jnp.sqrt(mean)) * lax.rsqrt(column)
    clip = jnp.maximum(1.0, jnp.sqrt(total_of(raw * raw) / (classes * width)))
    tail_ref[:16, :] = jnp.tanh(raw / clip)

    raws = []
    for k, grad in enumerate((gain_one, shift_one, gain_two, shift_two, gain_side, shift_two)):
        here = pl.ds(k * width, width)
        moment = keep * moment_ref[:, here] + (1.0 - keep) * (grad * grad + EPS_ROW)
        moment_new[:, here] = moment
        raws.append(grad * lax.rsqrt(moment))
    raw = jnp.concatenate(raws, axis=0)
    clip = jnp.maximum(1.0, jnp.sqrt(total_of(raw * raw) / raw.size))
    tail_ref[classes : classes + 6, :] = jnp.tanh(raw / clip)
    tail_ref[16:, :] = jnp.broadcast_to(loss, (8, width))


def run_worker(xs, conv_one, conv_two, shortcut, classifier, norm_params, valid, labels, rows, cols, moment):
    vmem = pl.BlockSpec(memory_space=pltpu.VMEM)
    hbm = pl.BlockSpec(memory_space=pl.ANY)
    low, f32 = jnp.bfloat16, jnp.float32
    dma = pltpu.SemaphoreType.DMA
    slots, in_width = xs.shape[4:]
    width = conv_one.shape[1]
    pixels = 16 * slots
    shape = jax.ShapeDtypeStruct
    matrix_rows = conv_one.shape[0] + conv_two.shape[0] + shortcut.shape[0]
    return pl.pallas_call(
        worker_kernel,
        out_shape=(
            shape((matrix_rows, width), low),
            shape((TAIL + 8, width), f32),
            shape((8, width), f32),
            shape((1, width), f32),
            shape(rows.shape, f32),
            shape(cols.shape, f32),
            shape(moment.shape, f32),
        ),
        in_specs=[vmem] + [hbm] * 3 + [vmem] * 7,
        out_specs=(vmem,) * 7,
        scratch_shapes=[
            pltpu.VMEM(conv_one.shape, f32),
            pltpu.VMEM(conv_two.shape, f32),
            pltpu.VMEM(shortcut.shape, f32),
            pltpu.VMEM((9, in_width, width), low),
            pltpu.VMEM((9, width, width), low),
            pltpu.VMEM((1, in_width, width), low),
            pltpu.VMEM((pixels, width), f32),
            pltpu.VMEM((pixels, width), f32),
            pltpu.VMEM((pixels, width), f32),
            pltpu.VMEM((4, 6, slots, width), low),
            pltpu.VMEM((4, 6, slots, width), low),
            pltpu.VMEM((4, 5, slots, width), low),
            pltpu.VMEM((pixels, width), low),
            pltpu.VMEM((width, pixels), low),
            pltpu.VMEM((2, 2, in_width, pixels), low),
            pltpu.VMEM((width, 128), f32),
            pltpu.VMEM((conv_two.shape[0], 128), f32),
            pltpu.VMEM((8, width), f32),
            pltpu.VMEM((2, 8, width), f32),
            pltpu.VMEM((2, 8, 8, width), f32),
            pltpu.VMEM((2, 4, 8, width), f32),
            dma((3,)),
            dma((2, 7)),
            dma((2, 7)),
            dma((2, 3)),
            dma((2, 3)),
        ],
        compiler_params=pltpu.CompilerParams(
            collective_id=1, has_side_effects=True, vmem_limit_bytes=60 * 1024 * 1024
        ),
        name="worker",
    )(xs, conv_one, conv_two, shortcut, classifier, norm_params, valid, labels, rows, cols, moment)


def scale_for(weight):
    return jnp.maximum(EPS_SCALE, jnp.sqrt(jnp.mean(weight * weight)))


def local_general(
    images,
    valid_slot,
    labels,
    conv_one,
    conv_two,
    shortcut,
    classifier,
    norm_params,
    row_state,
    col_state,
    bn_moment,
):
    in_width = images.shape[3]
    width = conv_one.shape[1]
    kernel_one = conv_one.astype(jnp.bfloat16).reshape(3, 3, in_width, width)
    kernel_two = conv_two.astype(jnp.bfloat16).reshape(3, 3, width, width)
    kernel_short = shortcut.astype(jnp.bfloat16).reshape(1, 1, in_width, width)
    head_low = classifier.astype(jnp.bfloat16)
    slot_count = images.shape[0]
    out_side = images.shape[1] // 2
    pixel_count = out_side * out_side
    slot_weight = valid_slot.astype(jnp.float32)
    pixel_weight = jnp.broadcast_to(slot_weight[:, None], (slot_count, pixel_count)).reshape(-1, 1)
    main_pre, side_pre = first_section(images, kernel_one, kernel_short)
    main_sums = masked_moments(pixel_weight, main_pre)
    side_sums = masked_moments(pixel_weight, side_pre)
    count_row = jnp.broadcast_to(jnp.sum(slot_weight), (width,))
    first_sums = lax.psum(jnp.stack([*main_sums, *side_sums, count_row]), "dp")
    valid_count = first_sums[4, 0]
    denominator = jnp.maximum(valid_count, 1.0)
    pixels = denominator * pixel_count
    norm_one = settle(first_sums[0], first_sums[1], pixels)
    norm_side = settle(first_sums[2], first_sums[3], pixels)
    hidden_one, active, main_two = second_section(
        main_pre, norm_one, norm_params, kernel_two, slot_count, out_side
    )
    two_sums = masked_moments(pixel_weight, main_two)
    second_sums = lax.psum(jnp.stack([*two_sums]), "dp")
    norm_two = settle(second_sums[0], second_sums[1], pixels)
    joined_pre = (
        (main_two - norm_two[0]) * norm_two[1] * norm_params[2]
        + norm_params[3]
        + (side_pre - norm_side[0]) * norm_side[1] * norm_params[4]
        + norm_params[5]
    )
    joined = jax.nn.silu(joined_pre).reshape(slot_count, pixel_count, -1)
    pooled = jnp.mean(joined, axis=1).astype(jnp.bfloat16)
    logits = jnp.dot(pooled, head_low, preferred_element_type=jnp.float32)
    largest = jnp.max(logits, axis=1, keepdims=True)
    exp_terms = jnp.exp(logits - largest)
    total_exp = jnp.sum(exp_terms, axis=1, keepdims=True)
    log_total = largest[:, 0] + jnp.log(total_exp[:, 0])
    onehot = (labels[:, None] == jnp.arange(logits.shape[1], dtype=jnp.int32)[None, :]).astype(
        jnp.float32
    )
    local_sum = jnp.sum(slot_weight * (log_total - jnp.sum(onehot * logits, axis=1)))
    grad_logits = ((exp_terms / total_exp - onehot) * (slot_weight / denominator)[:, None]).astype(
        jnp.bfloat16
    )
    grad_head = lax.dot_general(
        pooled, grad_logits, (((0,), (0,)), ((), ())), preferred_element_type=jnp.float32
    )
    grad_pooled = lax.dot_general(
        grad_logits, head_low, (((1,), (1,)), ((), ())), preferred_element_type=jnp.float32
    )
    spread_pooled = jnp.broadcast_to(
        (grad_pooled / pixel_count)[:, None, :], (slot_count, pixel_count, width)
    )
    grad_joined = spread_pooled.reshape(slot_count * pixel_count, width) * silu_slope(joined_pre)
    gain_two, shift_two, grad_two = norm_backward(grad_joined, main_two, norm_two, norm_params[2])
    gain_side, shift_side, grad_side = norm_backward(
        grad_joined, side_pre, norm_side, norm_params[4]
    )
    grad_two_maps = grad_two.reshape(slot_count, out_side, out_side, width)
    grad_side_maps = grad_side.reshape(slot_count, out_side, out_side, width)
    grad_conv_two = conv_weight_grad(active, grad_two_maps, 1, 1, 1)
    grad_short = conv_weight_grad(images, grad_side_maps, 2, 0, -1)
    kernel_turned = jnp.transpose(kernel_two[::-1, ::-1], (0, 1, 3, 2))
    grad_active = conv_apply(grad_two_maps, kernel_turned, 1, 1).reshape(
        slot_count * pixel_count, width
    )
    grad_hidden = grad_active * silu_slope(hidden_one)
    gain_one, shift_one, grad_one = norm_backward(grad_hidden, main_pre, norm_one, norm_params[0])
    grad_conv_one = conv_weight_grad(
        images, grad_one.reshape(slot_count, out_side, out_side, width), 2, 1, 0
    )
    grad_norms = jnp.stack([gain_one, shift_one, gain_two, shift_two, gain_side, shift_side])
    grads = (grad_conv_one, grad_conv_two, grad_short, grad_head, grad_norms)
    votes, rows_new, cols_new, moment_new = make_votes(
        grads, row_state[0], col_state[0], bn_moment[0]
    )
    workers = lax.axis_size("dp")
    weights = (conv_one, conv_two, shortcut, classifier, norm_params)
    scales = [scale_for(weight) for weight in weights]
    loss_sum = lax.psum(local_sum, "dp")
    flat_vote = jnp.concatenate([vote.reshape(-1) for vote in votes])
    flat_old = jnp.concatenate([weight.reshape(-1) for weight in weights])
    flat_scale = jnp.concatenate(
        [
            jnp.broadcast_to(scale, (weight.size,))
            for scale, weight in zip(scales, weights)
        ]
    )
    vote_mine = lax.psum_scatter(flat_vote, "dp", tiled=True)
    share = vote_mine.shape[0]
    start = lax.axis_index("dp") * share
    new_mine = lax.dynamic_slice_in_dim(
        flat_old, start, share
    ) - lax.dynamic_slice_in_dim(flat_scale, start, share) * jnp.tanh(
        vote_mine / math.sqrt(workers)
    )
    copies = lax.all_gather(new_mine.astype(jnp.bfloat16), "dp", tiled=True)
    return (
        loss_sum,
        valid_count,
        new_mine,
        copies,
        vote_mine,
        rows_new[None, :],
        cols_new[None, :],
        moment_new[None, :],
    )


def local(
    images,
    valid_slot,
    labels,
    conv_one,
    conv_two,
    shortcut,
    classifier,
    norm_params,
    row_state,
    col_state,
    bn_moment,
):
    slots, height, _, in_width = images.shape
    width = conv_one.shape[1]
    side = height // 2
    xs = images.reshape(slots, side, 2, side, 2, in_width).transpose(4, 3, 2, 1, 0, 5)
    votes, tail_vote, scales, valid_count, rows_new, cols_new, moment_new = run_worker(
        xs,
        conv_one,
        conv_two,
        shortcut,
        classifier,
        norm_params,
        valid_slot.reshape(1, -1),
        labels.reshape(1, -1),
        row_state.reshape(-1, 128),
        col_state,
        bn_moment,
    )
    tail_sum = sum_all(tail_vote, 3)
    classes = classifier.shape[1]
    head_sum = tail_sum[:classes].T.reshape(classes, width)
    flat_sum = jnp.concatenate([head_sum, tail_sum[classes:TAIL]])
    tail_weight = jnp.concatenate([classifier.reshape(classes, width), norm_params])
    tail_scale = jnp.concatenate(
        [
            jnp.broadcast_to(scales[3], (classes, width)),
            jnp.broadcast_to(scales[4], (TAIL - classes, width)),
        ]
    )
    new_mine, vote_mine, copies = update_weights(
        votes.reshape(4, 2, 2, 2, OWN, width),
        flat_sum,
        tail_weight,
        tail_scale,
        scales[:3, 0],
        conv_one,
        conv_two,
        shortcut,
        lax.axis_size("dp"),
    )
    return (
        tail_sum[TAIL, 0],
        valid_count[0, 0],
        new_mine.reshape(-1),
        copies.reshape(-1),
        vote_mine.reshape(-1),
        rows_new.reshape(1, -1),
        cols_new,
        moment_new,
    )


def solution(mesh):
    placed = (
        P("dp", None, None, None),
        P("dp"),
        P("dp"),
        P(),
        P(),
        P(),
        P(),
        P(),
        P("dp", None),
        P("dp", None),
        P("dp", None),
    )
    return jax.shard_map(
        local if mesh.shape["dp"] == 32 else local_general,
        mesh=mesh,
        in_specs=placed,
        out_specs=(P(), P(), P("dp"), P(), P("dp"), P("dp", None), P("dp", None), P("dp", None)),
        check_vma=False,
    )
```

```python
import functools
import math

import jax
import jax.numpy as jnp
from jax import lax
from jax.experimental import pallas as pl
from jax.experimental.pallas import tpu as pltpu
from jax.sharding import PartitionSpec as P

STEP = 10
MESH = pl.DeviceIdType.MESH

EPS_NORM = 1e-05
EPS_ROW = 1e-30
EPS_SCALE = 0.001
FORWARD_DIMS = ("NHWC", "HWIO", "NHWC")
WEIGHT_DIMS = ("CHWN", "IHWO", "HWNC")
OWN = 224
HALF = 112
TAIL = 16
PIECE = 32


def conv_apply(maps, kernel, stride, margin):
    return lax.conv_general_dilated(
        maps,
        kernel,
        (stride, stride),
        ((margin, margin), (margin, margin)),
        dimension_numbers=FORWARD_DIMS,
        preferred_element_type=jnp.float32,
    )


def conv_weight_grad(maps, grad_out, stride, low_pad, high_pad):
    result = lax.conv_general_dilated(
        maps,
        grad_out,
        (1, 1),
        ((low_pad, high_pad), (low_pad, high_pad)),
        rhs_dilation=(stride, stride),
        dimension_numbers=WEIGHT_DIMS,
        preferred_element_type=jnp.float32,
    )
    return result.reshape(-1, result.shape[3])


def silu_slope(values):
    sigmoid_part = jax.nn.sigmoid(values)
    return sigmoid_part * (1.0 + values * (1.0 - sigmoid_part))


def settle(sum_plain, sum_square, pixels):
    mean_value = sum_plain / pixels
    return (mean_value, lax.rsqrt(sum_square / pixels - mean_value * mean_value + EPS_NORM))


def first_section(images, kernel_one, kernel_short):
    row_count = images.shape[0] * (images.shape[1] // 2) ** 2
    main_pre = conv_apply(images, kernel_one, 2, 1).reshape(row_count, -1)
    side_pre = conv_apply(images, kernel_short, 2, 0).reshape(row_count, -1)
    return (main_pre, side_pre)


def second_section(main_pre, norm_one, norm_params, kernel_two, slot_count, out_side):
    hidden_one = (main_pre - norm_one[0]) * norm_one[1] * norm_params[0] + norm_params[1]
    active = (
        jax.nn.silu(hidden_one).astype(jnp.bfloat16).reshape(slot_count, out_side, out_side, -1)
    )
    main_two = conv_apply(active, kernel_two, 1, 1).reshape(slot_count * out_side * out_side, -1)
    return (hidden_one, active, main_two)


def masked_moments(pixel_weight, values):
    return (jnp.sum(pixel_weight * values, axis=0), jnp.sum(pixel_weight * values * values, axis=0))


def soft_sign(step_raw):
    clip_by = jnp.maximum(1.0, jnp.sqrt(jnp.mean(step_raw * step_raw)))
    return jnp.tanh(step_raw / clip_by)


def make_votes(grads, rows_old, cols_old, moment_old):
    decay_rate = 1.0 - STEP ** (-0.8)
    votes, rows_new, cols_new = ([], [], [])
    row_at, col_at = (0, 0)
    for matrix in grads[:4]:
        row_size, col_size = matrix.shape
        square = matrix * matrix + EPS_ROW
        row_part = decay_rate * rows_old[row_at : row_at + row_size] + (
            1.0 - decay_rate
        ) * jnp.mean(square, axis=1)
        col_part = decay_rate * cols_old[col_at : col_at + col_size] + (
            1.0 - decay_rate
        ) * jnp.mean(square, axis=0)
        second = row_part[:, None] * col_part[None, :] / jnp.mean(row_part)
        votes.append(soft_sign(matrix * lax.rsqrt(second)))
        rows_new.append(row_part)
        cols_new.append(col_part)
        row_at += row_size
        col_at += col_size
    flat_norm = grads[4].reshape(-1)
    moment_new = decay_rate * moment_old + (1.0 - decay_rate) * (flat_norm * flat_norm + EPS_ROW)
    votes.append(soft_sign(flat_norm * lax.rsqrt(moment_new)))
    return (votes, jnp.concatenate(rows_new), jnp.concatenate(cols_new), moment_new)


def norm_backward(grad_out, pre_value, norm_pair, gain_row):
    normed = (pre_value - norm_pair[0]) * norm_pair[1]
    grad_gain = jnp.sum(grad_out * normed, axis=0)
    grad_shift = jnp.sum(grad_out, axis=0)
    grad_pre = (grad_out * gain_row * norm_pair[1]).astype(jnp.bfloat16)
    return (grad_gain, grad_shift, grad_pre)


def place():
    me = lax.axis_index("dp")
    core = lax.rem(me, 2)
    x = lax.rem(lax.div(me, 2), 2)
    y = lax.rem(lax.div(me, 4), 2)
    z = lax.div(me, 8)
    return me, core, x, y, z


def send(src, dst, send_sem, recv_sem, partner):
    copy = pltpu.make_async_remote_copy(
        src_ref=src,
        dst_ref=dst,
        send_sem=send_sem,
        recv_sem=recv_sem,
        device_id=(partner,),
        device_id_type=MESH,
    )
    copy.start()
    return copy


def scale_of(row, scales, edges):
    picked = scales[2]
    picked = jnp.where(row < edges[1], scales[1], picked)
    return jnp.where(row < edges[0], scales[0], picked)


def settle_rows(sums, pixels, gain, shift):
    mean = sums[0] / pixels
    inv = lax.rsqrt(sums[1] / pixels - mean * mean + EPS_NORM)
    slope = gain * inv
    return mean, inv, slope, shift - mean * slope


def gate(values):
    return 0.5 * jnp.tanh(0.5 * values) + 0.5


def eye_mask(rows, columns, offset=0):
    down = lax.broadcasted_iota(jnp.int32, (rows, columns), 0) + offset
    return down == lax.broadcasted_iota(jnp.int32, (rows, columns), 1)


def column_of(row, size):
    spread = jnp.where(eye_mask(size, size), jnp.broadcast_to(row, (size, size)), 0)
    return jnp.sum(spread, axis=1, keepdims=True)


def total_of(values):
    return jnp.sum(jnp.sum(values, axis=0, keepdims=True), axis=1, keepdims=True)


def fold(values):
    return jnp.sum(values.reshape(values.shape[0] // 8, 8, values.shape[1]), axis=0)


def cast_weight(source, target, square_ref, taps, depth):
    step = 128
    square_ref[...] = jnp.zeros_like(square_ref)
    for tap in range(taps):
        new_tap = (tap % 3) * 3 + tap // 3

        @pl.loop(0, depth // step)
        def _(k):
            start = pl.multiple_of(k * step, step)
            values = source[pl.ds(tap * depth + start, step), :]
            target[new_tap, pl.ds(start, step), :] = values.astype(jnp.bfloat16)
            square_ref[...] += fold(values * values)


def factored_votes(grad, rows, row_at, rows_old, rows_new, col_old, level, votes, vote_at, between):
    width = grad.shape[1]
    keep = 1.0 - STEP ** (-0.8)
    step = 128
    quarters = width // 128

    def first(k, carry):
        col_sum, row_sum = carry
        start = pl.multiple_of(k * step, step)
        lanes = pl.ds(pl.multiple_of(row_at + start, step), step)
        old = rows_old[:, lanes] * keep
        line = jnp.zeros((8, 128), jnp.float32)
        for m in range(step // 8):
            block = grad[pl.ds(start + 8 * m, 8), :]
            square = block * block
            col_sum = col_sum + square
            part = square[:, :128]
            for q in range(1, quarters):
                part = part + square[:, 128 * q : 128 * (q + 1)]
            part = part * ((1.0 - keep) / width)
            diagonal = eye_mask(8, 128, 8 * m)
            part = part + jnp.where(diagonal, jnp.broadcast_to(old, (8, 128)), 0.0)
            row = jnp.sum(part, axis=1, keepdims=True) + (1.0 - keep) * EPS_ROW
            row = jnp.broadcast_to(row, (8, 128))
            level[pl.ds(start + 8 * m, 8), :] = row
            row_sum = row_sum + row
            line = line + jnp.where(diagonal, row, 0.0)
        rows_new[:, lanes] = jnp.sum(line, axis=0, keepdims=True)
        return col_sum, row_sum

    col_sum, row_sum = lax.fori_loop(
        0,
        rows // step,
        first,
        (jnp.zeros((8, width), jnp.float32), jnp.zeros((8, 128), jnp.float32)),
    )
    col_new = keep * col_old + (1.0 - keep) * (
        jnp.sum(col_sum, axis=0, keepdims=True) / rows + EPS_ROW
    )
    scale = lax.rsqrt(col_new)
    root_mean = jnp.sqrt(jnp.sum(row_sum, axis=0, keepdims=True) / rows)

    def second(k, carry):
        start = pl.multiple_of(k * step, step)
        for m in range(step // 8):
            here = pl.ds(start + 8 * m, 8)
            factor = lax.rsqrt(level[here, :]) * root_mean
            level[here, :] = factor
            raw = grad[here, :] * scale
            power = raw * raw
            part = power[:, :128]
            for q in range(1, quarters):
                part = part + power[:, 128 * q : 128 * (q + 1)]
            carry = carry + part * (factor * factor)
        return carry

    between[0]()
    power = lax.fori_loop(0, rows // step, second, jnp.zeros((8, 128), jnp.float32))
    between[1]()
    clip = jnp.maximum(1.0, jnp.sqrt(total_of(power) / (rows * width)))
    scale = scale / clip

    def third(k, _):
        start = pl.multiple_of(k * step, step)
        for m in range(step // 16):
            here = pl.ds(start + 16 * m, 16)
            factor = level[here, :]
            factor = jnp.concatenate([factor] * quarters, axis=1)
            vote = jnp.tanh(grad[here, :] * factor * scale)
            votes[pl.ds(vote_at + start + 16 * m, 16), :] = vote.astype(jnp.bfloat16)
        return 0

    lax.fori_loop(0, rows // step, third, 0)
    return col_new


def step_kernel(
    edges,
    root,
    xs,
    one_hbm,
    two_hbm,
    short_hbm,
    head_ref,
    norm_ref,
    valid_ref,
    label_ref,
    row_ref,
    col_ref,
    moment_ref,
    new_ref,
    vote_ref,
    out_ref,
    row_new,
    col_new,
    moment_new,
    loss_ref,
    count_ref,
    grad_one,
    grad_two,
    grad_short,
    low_one,
    low_two,
    low_short,
    main_pre,
    side_pre,
    main_two,
    active,
    back_two,
    back_one,
    back_side,
    active_t,
    xs_t,
    head_pad,
    level,
    square,
    post,
    plane,
    line,
    tail_post,
    tail_plane,
    tail_line,
    votes,
    core_in,
    ax_in,
    by_in,
    plane_in,
    line_in,
    halo_in,
    total,
    weight,
    vote_flat,
    new_flat,
    mine,
    tail_low,
    fetch_sem,
    small_send,
    small_recv,
    core_send,
    core_recv,
    rs_send,
    rs_recv,
    line_send,
    line_recv,
    halo_sem,
    ag_send,
    ag_recv,
    keep_sem,
):
    slots, in_width = xs.shape[4:]
    width = main_pre.shape[1]
    side = 4
    band = side * slots
    pixel_count = side * side
    classes = head_ref.shape[0]
    keep = 1.0 - STEP ** (-0.8)
    low = jnp.bfloat16
    f32 = jnp.float32

    me, core, x, y, z = place()
    flip_core = me + 1 - 2 * core
    flip_x = me + 2 - 4 * x
    flip_y = me + 4 - 8 * y
    spot = lax.rem(me, 8)
    near = [z * 8 + lax.rem(spot + k, 8) for k in range(1, 8)]
    far = [lax.rem(z + k, 4) * 8 + spot for k in range(1, 4)]
    ahead, behind = lax.rem(me + 31, 32), lax.rem(me + 1, 32)
    partners = near + far + [ahead, behind]

    fetches = [
        pltpu.make_async_copy(source, target, fetch_sem.at[k])
        for k, (source, target) in enumerate(
            ((one_hbm, grad_one), (short_hbm, grad_short), (two_hbm, grad_two))
        )
    ]
    for fetch in fetches:
        fetch.start()
    barrier = pltpu.get_barrier_semaphore()
    for partner in partners:
        pl.semaphore_signal(barrier, inc=1, device_id=(partner,), device_id_type=MESH)

    def fetch_rows(row, count, place_at, sem):
        parts = (
            (one_hbm, 0, edges[0]),
            (two_hbm, edges[0], edges[1]),
            (short_hbm, edges[1], edges[2]),
        )
        for ref, first, last in parts:

            @pl.when(jnp.logical_and(row >= first, row < last))
            def _():
                start = pl.multiple_of(row - first, count)
                pltpu.make_async_copy(
                    ref.at[pl.ds(start, count)], weight.at[pl.ds(place_at, count)], sem
                ).start()

    first_row = me * OWN
    for k in range(OWN // PIECE):
        fetch_rows(first_row + k * PIECE, PIECE, k * PIECE, fetch_sem.at[3])
    fetch_rows(first_row + OWN, TAIL, OWN, fetch_sem.at[4])

    scales = {}

    def scale_from(weight_square, size):
        return jnp.maximum(EPS_SCALE, jnp.sqrt(total_of(weight_square) / size))

    exchanges = (
        (post.at[0], plane.at[0], line.at[0]),
        (post.at[1], plane.at[1], line.at[1]),
        (tail_post, tail_plane, tail_line),
    )

    def exchange_start(which, values):
        mine_ref, plane_ref, _ = exchanges[which]
        mine_ref[...] = values
        plane_ref[spot] = values
        return [
            send(
                mine_ref,
                plane_ref.at[spot],
                small_send.at[which, k],
                small_recv.at[which, k],
                partner,
            )
            for k, partner in enumerate(near)
        ]

    def exchange_middle(which, copies):
        _, plane_ref, line_ref = exchanges[which]
        for copy in copies:
            copy.wait()
        line_ref[z] = functools.reduce(lambda a, b: a + b, [plane_ref[k] for k in range(8)])
        return [
            send(
                line_ref.at[z],
                line_ref.at[z],
                small_send.at[which, 7 + k],
                small_recv.at[which, 7 + k],
                partner,
            )
            for k, partner in enumerate(far)
        ]

    def exchange_end(which, copies):
        line_ref = exchanges[which][2]
        for copy in copies:
            copy.wait()
        return (line_ref[0] + line_ref[1]) + (line_ref[2] + line_ref[3])

    def block_rows(t, yy, xx, cc):
        block = t * 8 + yy * 4 + xx * 2 + cc
        return pl.ds(pl.multiple_of(block * OWN, 16), OWN)

    def scatter_start(t):
        return [
            send(
                votes.at[block_rows(t, yy, xx, 1 - core)],
                core_in.at[t, yy, xx],
                core_send.at[t, 2 * yy + xx],
                core_recv.at[t, 2 * yy + xx],
                flip_core,
            )
            for yy in range(2)
            for xx in range(2)
        ]

    def scatter_one(t, copies):
        for copy in copies:
            copy.wait()
        for yy in range(2):
            for xx in range(2):
                core_in[t, yy, xx] = core_in[t, yy, xx] + votes[block_rows(t, yy, xx, core), :]
        return (
            send(
                core_in.at[t, :, 1 - x, pl.ds(0, HALF)],
                ax_in.at[t],
                rs_send.at[0, t],
                rs_recv.at[0, t],
                flip_x,
            ),
            send(
                core_in.at[t, 1 - y, :, pl.ds(HALF, HALF)],
                by_in.at[t],
                rs_send.at[1, t],
                rs_recv.at[1, t],
                flip_y,
            ),
        )

    def scatter_two(t, copies):
        copies[0].wait()
        ax_in[t] = ax_in[t] + core_in[t, :, x, :HALF]
        first = send(
            ax_in.at[t, 1 - y],
            plane_in.at[t, pl.ds(0, HALF)],
            rs_send.at[2, t],
            rs_recv.at[2, t],
            flip_y,
        )
        copies[1].wait()
        by_in[t] = by_in[t] + core_in[t, y, :, HALF:]
        second = send(
            by_in.at[t, 1 - x],
            plane_in.at[t, pl.ds(HALF, HALF)],
            rs_send.at[3, t],
            rs_recv.at[3, t],
            flip_x,
        )
        return first, second

    def line_copy(t, slot):
        return pltpu.make_async_remote_copy(
            src_ref=plane_in.at[t],
            dst_ref=line_in.at[slot],
            send_sem=line_send.at[t],
            recv_sem=line_recv.at[slot],
            device_id=(t * 8 + spot,),
            device_id_type=MESH,
        )

    def scatter_three(t, copies):
        copies[0].wait()
        plane_in[t, :HALF] = plane_in[t, :HALF] + ax_in[t, y]
        copies[1].wait()
        plane_in[t, HALF:] = plane_in[t, HALF:] + by_in[t, x]

        @pl.when(z != t)
        def _():
            line_copy(t, z).start()

        @pl.when(z == t)
        def _():
            line_in[t] = plane_in[t]

    span, part = 4 * OWN, 4 * HALF
    own_rows = pl.ds(pl.multiple_of(me * span, 16), span)

    def flat_rows(row, values, ref):
        for k in range(4):
            ref[pl.ds(row * 4 + k, 8, stride=4), :] = values[:, 128 * k : 128 * (k + 1)]

    def renew(row, at_row):
        scale = scale_of(at_row, [scales[k] for k in range(3)], edges)
        summed = total[pl.ds(row, 8), :]
        fresh = weight[pl.ds(row, 8), :] - scale * jnp.tanh(summed * root)
        flat_rows(row, summed, vote_flat)
        flat_rows(row, fresh, new_flat)

    def halo_copy():
        return pltpu.make_async_remote_copy(
            src_ref=total.at[pl.ds(0, TAIL)],
            dst_ref=halo_in,
            send_sem=halo_sem.at[0],
            recv_sem=halo_sem.at[1],
            device_id=(ahead,),
            device_id_type=MESH,
        )

    def keep_copy():
        return pltpu.make_async_copy(mine, out_ref.at[own_rows], keep_sem.at[0])

    def spread_copy(k):
        return pltpu.make_async_remote_copy(
            src_ref=mine,
            dst_ref=out_ref.at[own_rows],
            send_sem=ag_send.at[0, k],
            recv_sem=ag_recv.at[0, z],
            device_id=(far[k],),
            device_id_type=MESH,
        )

    def own_block():
        for k in range(1, 4):
            line_copy(0, lax.rem(z + k, 4)).wait_recv()
        total[pl.ds(0, OWN), :] = functools.reduce(
            lambda a, b: a + b, [line_in[t].astype(f32) for t in range(4)]
        )
        halo_copy().start()
        pltpu.make_async_copy(
            weight.at[pl.ds(0, OWN)], weight.at[pl.ds(0, OWN)], fetch_sem.at[3]
        ).wait()

        @pl.loop(0, OWN // 8)
        def _(k):
            row = pl.multiple_of(k * 8, 8)
            renew(row, first_row + row)

        mine[...] = new_flat[pl.ds(0, span), :].astype(low)
        keep_copy().start()
        for k in range(3):
            spread_copy(k).start()

    def piece(rows, kind, t, partner):
        return send(
            out_ref.at[rows], out_ref.at[rows], ag_send.at[kind, t], ag_recv.at[kind, t], partner
        )

    def half_rows(t, yy, xx, half):
        block = t * 8 + yy * 4 + xx * 2 + core
        return pl.ds(pl.multiple_of(block * span + half * part, 16), part)

    def gather_one(t):
        @pl.when(z == t)
        def _():
            keep_copy().wait()

        @pl.when(z != t)
        def _():
            pltpu.make_async_remote_copy(
                src_ref=mine,
                dst_ref=out_ref.at[own_rows],
                send_sem=ag_send.at[0, 0],
                recv_sem=ag_recv.at[0, t],
                device_id=(far[0],),
                device_id_type=MESH,
            ).wait_recv()

        return (
            piece(half_rows(t, y, x, 0), 1, t, flip_y),
            piece(half_rows(t, y, x, 1), 2, t, flip_x),
        )

    def gather_two(t, copies):
        copies[0].wait()
        sent = [piece(half_rows(t, yy, x, 0), 3 + yy, t, flip_x) for yy in range(2)]
        copies[1].wait()
        return sent + [piece(half_rows(t, y, xx, 1), 5 + xx, t, flip_y) for xx in range(2)]

    def gather_three(t, copies):
        for copy in copies:
            copy.wait()
        sent = []
        for yy in range(2):
            for xx in range(2):
                block = t * 8 + yy * 4 + xx * 2 + core
                rows = pl.ds(pl.multiple_of(block * span, 16), span)
                sent.append(piece(rows, 7 + 2 * yy + xx, t, flip_core))
        return sent

    valid_column = column_of(valid_ref[...].astype(f32), slots)
    weight_slot = jnp.broadcast_to(valid_column, (slots, width))
    weight_band = jnp.concatenate([weight_slot] * side, axis=0)

    fetches[0].wait()
    cast_weight(grad_one, low_one, square, 9, in_width)
    scales[0] = scale_from(square[...], grad_one.size)
    fetches[1].wait()
    cast_weight(grad_short, low_short, square, 1, in_width)
    scales[2] = scale_from(square[...], grad_short.size)

    def image_taps(j):
        pieces = []
        for b in range(3):
            column = j if b else j - 1
            if column < 0:
                continue
            across = 0 if b == 1 else 1
            for a in range(3):
                if a == 1:
                    piece = xs[across, column, 0].reshape(band, in_width)
                elif a == 2:
                    piece = xs[across, column, 1].reshape(band, in_width)
                else:
                    piece = xs[across, column, 1, : side - 1].reshape(band - slots, in_width)
                    piece = jnp.concatenate([jnp.zeros((slots, in_width), low), piece], axis=0)
                pieces.append(piece)
        return jnp.concatenate(pieces, axis=1)

    def moments(values):
        weighted = values * weight_band
        return (
            jnp.sum(weighted, axis=0, keepdims=True),
            jnp.sum(weighted * values, axis=0, keepdims=True),
        )

    def add_up(old, new):
        return [a + b for a, b in zip(old, new)]

    none = jnp.zeros((1, width), f32)
    main_sums, side_sums = [none, none], [none, none]
    for j in range(side):
        here = pl.ds(j * band, band)
        low_rows = low_one[3 if j == 0 else 0 :].reshape(-1, width)
        value = jnp.dot(image_taps(j), low_rows, preferred_element_type=f32)
        main_pre[here, :] = value
        main_sums = add_up(main_sums, moments(value))
        value = jnp.dot(
            xs[0, j, 0].reshape(band, in_width), low_short[0], preferred_element_type=f32
        )
        side_pre[here, :] = value
        side_sums = add_up(side_sums, moments(value))

    count = jnp.broadcast_to(jnp.sum(valid_column, axis=0, keepdims=True), (1, width))
    pl.semaphore_wait(barrier, len(partners))
    copies = exchange_start(
        0, jnp.concatenate(main_sums + side_sums + [count, none, none, none], axis=0)
    )
    fetches[2].wait()
    cast_weight(grad_two, low_two, square, 9, width)
    scales[1] = scale_from(square[...], grad_two.size)
    copies = exchange_middle(0, copies)
    for across in range(2):
        for down in range(2):
            for j in range(side):
                block = xs[across, j, down].reshape(band, in_width)
                xs_t[across, down, :, j * band : (j + 1) * band] = block.T
    border = jnp.zeros((side, 1, slots, width), low)
    active[:, 0:1] = border
    active[:, side + 1 :] = border
    back_two[:, 0:1] = border
    back_two[:, side + 1 :] = border
    back_one[:, side:] = border
    head_pad[...] = jnp.zeros_like(head_pad)
    head_pad[:classes, :] = head_ref[...]
    head = head_pad[:16, :]
    scales[3] = scale_from(head * head, head_ref.size)
    params = norm_ref[...]
    scales[4] = scale_from(params * params, norm_ref.size)
    sums = exchange_end(0, copies)

    valid_count = sums[4:5]
    count_ref[...] = valid_count[:, :1]
    denominator = jnp.maximum(valid_count, 1.0)
    pixels = denominator * pixel_count
    gains = [norm_ref[k : k + 1, :] for k in range(6)]
    mean_one, inv_one, slope_one, base_one = settle_rows(
        (sums[0:1], sums[1:2]), pixels, gains[0], gains[1]
    )
    mean_side, inv_side, slope_side, base_side = settle_rows(
        (sums[2:3], sums[3:4]), pixels, gains[4], gains[5]
    )

    for j in range(side):
        hidden = main_pre[pl.ds(j * band, band), :] * slope_one + base_one
        active[j, 1 : side + 1] = (
            (hidden * gate(hidden)).astype(low).reshape(side, slots, width)
        )
    two_sums = [none, none]
    for j in range(side):
        taps = [b for b in range(3) if 0 <= j + b - 1 < side]
        pieces = [
            active[j + b - 1, a : a + side].reshape(band, width) for b in taps for a in range(3)
        ]
        low_rows = low_two[3 * taps[0] : 3 * taps[-1] + 3].reshape(-1, width)
        value = jnp.dot(jnp.concatenate(pieces, axis=1), low_rows, preferred_element_type=f32)
        main_two[pl.ds(j * band, band), :] = value
        two_sums = add_up(two_sums, moments(value))
    copies = exchange_start(1, jnp.concatenate(two_sums + [none] * 6, axis=0))
    for j in range(side):
        block = active[j, 1 : side + 1].reshape(band, width)
        active_t[:, j * band : (j + 1) * band] = block.T
    copies = exchange_middle(1, copies)
    sums = exchange_end(1, copies)
    mean_two, inv_two, slope_two, base_two = settle_rows(
        (sums[0:1], sums[1:2]), pixels, gains[2], gains[3]
    )

    base_joined = base_two + base_side

    def joined_of(here):
        return main_two[here, :] * slope_two + side_pre[here, :] * slope_side + base_joined

    pooled = jnp.zeros((slots, width), f32)
    for p in range(pixel_count):
        joined = joined_of(pl.ds(p * slots, slots))
        pooled = pooled + joined * gate(joined)
    pooled = (pooled / pixel_count).astype(low)
    head_low = head_pad[...].astype(low)
    logits = lax.dot_general(
        pooled, head_low, (((1,), (1,)), ((), ())), preferred_element_type=f32
    )
    lane = lax.broadcasted_iota(jnp.int32, logits.shape, 1)
    real = lane < classes
    largest = jnp.max(jnp.where(real, logits, -jnp.inf), axis=1, keepdims=True)
    powers = jnp.where(real, jnp.exp(jnp.where(real, logits - largest, 0.0)), 0.0)
    total_power = jnp.sum(powers, axis=1, keepdims=True)
    label_column = column_of(label_ref[...].astype(f32), slots).astype(jnp.int32)
    onehot = jnp.where(lane == label_column, 1.0, 0.0)
    entropy = largest + jnp.log(total_power) - jnp.sum(onehot * logits, axis=1, keepdims=True)
    loss = jnp.sum(entropy * valid_column, axis=0, keepdims=True)
    grad_logits = (
        (powers / total_power - onehot) * (valid_column / denominator[:, :1])
    ).astype(low)
    grad_head = lax.dot_general(
        grad_logits, pooled, (((0,), (0,)), ((), ())), preferred_element_type=f32
    )[:16]
    grad_pooled = jnp.dot(grad_logits, head_low, preferred_element_type=f32) / pixel_count

    gain_two, gain_side, shift_two = none, none, none
    for p in range(pixel_count):
        here = pl.ds(p * slots, slots)
        joined = joined_of(here)
        opened = gate(joined)
        grad = grad_pooled * (opened * (1.0 + joined * (1.0 - opened)))
        shift_two = shift_two + jnp.sum(grad, axis=0, keepdims=True)
        gain_two = gain_two + jnp.sum(
            grad * ((main_two[here, :] - mean_two) * inv_two), axis=0, keepdims=True
        )
        gain_side = gain_side + jnp.sum(
            grad * ((side_pre[here, :] - mean_side) * inv_side), axis=0, keepdims=True
        )
        back_two[p // side, 1 + p % side] = (grad * slope_two).astype(low)
        back_side[here, :] = (grad * slope_side).astype(low)

    grad_short[...] = jnp.dot(xs_t[0, 0], back_side[...], preferred_element_type=f32)
    for b in range(3):
        first, last = max(0, b - 1), min(side, side + b - 1)
        left = active_t[:, first * band : last * band]
        for a in range(3):
            right = back_two[first - b + 1 : last - b + 1, 2 - a : 2 - a + side]
            grad_two[pl.ds((a * 3 + b) * width, width), :] = jnp.dot(
                left, right.reshape(-1, width), preferred_element_type=f32
            )


    def nothing():
        pass

    def matrix_votes(k, grad, between):
        here = pl.ds(k * width, width)
        start = edges[k - 1] if k else 0
        col_new[:, here] = factored_votes(
            grad, grad.shape[0], start, row_ref, row_new, col_ref[:, here], level, votes, start, between
        )

    matrix_votes(2, grad_short, (nothing, nothing))
    matrix_votes(1, grad_two, (nothing, nothing))
    stage = {t: scatter_start(t) for t in (2, 3)}

    gain_one, shift_one = none, none
    for j in range(side):
        taps = [b for b in range(3) if 0 <= j - b + 1 < side]
        pieces = [
            back_two[j - b + 1, 2 - a : 2 - a + side].reshape(band, width)
            for b in taps
            for a in range(3)
        ]
        weights = jnp.concatenate([low_two[b * 3 + a] for b in taps for a in range(3)], axis=1)
        grad = lax.dot_general(
            jnp.concatenate(pieces, axis=1),
            weights,
            (((1,), (1,)), ((), ())),
            preferred_element_type=f32,
        )
        before = main_pre[pl.ds(j * band, band), :]
        hidden = before * slope_one + base_one
        opened = gate(hidden)
        grad = grad * (opened * (1.0 + hidden * (1.0 - opened)))
        shift_one = shift_one + jnp.sum(grad, axis=0, keepdims=True)
        gain_one = gain_one + jnp.sum(
            grad * ((before - mean_one) * inv_one), axis=0, keepdims=True
        )
        back_one[j, :side] = (grad * slope_one).astype(low).reshape(side, slots, width)
        if j == 1:
            stage[2] = scatter_one(2, stage[2])
        if j == 2:
            stage[3] = scatter_one(3, stage[3])

    square_head = grad_head * grad_head + EPS_ROW
    real = lax.broadcasted_iota(jnp.int32, square_head.shape, 0) < classes
    square_head = jnp.where(real, square_head, 0.0)
    head_lanes = pl.ds(edges[2], width)
    old = row_ref[:, head_lanes]
    row = keep * old + (1.0 - keep) * jnp.sum(square_head, axis=0, keepdims=True) / classes
    row_new[:, head_lanes] = row
    diagonal = eye_mask(16, classes)
    old = jnp.broadcast_to(col_ref[:, 3 * width :], (16, classes))
    old = jnp.sum(jnp.where(diagonal, old, 0.0), axis=1, keepdims=True)
    column = keep * old + (1.0 - keep) * jnp.sum(square_head, axis=1, keepdims=True) / width
    col_new[:, 3 * width :] = jnp.sum(
        jnp.where(diagonal, jnp.broadcast_to(column, (16, classes)), 0.0), axis=0, keepdims=True
    )
    real_column = lax.broadcasted_iota(jnp.int32, column.shape, 0) < classes
    column = jnp.where(real_column, column, 1.0)
    mean = jnp.sum(row, axis=1, keepdims=True) / width
    raw = grad_head * (lax.rsqrt(row) * jnp.sqrt(mean)) * lax.rsqrt(column)
    clip = jnp.maximum(1.0, jnp.sqrt(total_of(raw * raw) / (classes * width)))
    head_votes = jnp.tanh(raw / clip)[:classes]

    raws = []
    for k, grad in enumerate((gain_one, shift_one, gain_two, shift_two, gain_side, shift_two)):
        here = pl.ds(k * width, width)
        moment = keep * moment_ref[:, here] + (1.0 - keep) * (grad * grad + EPS_ROW)
        moment_new[:, here] = moment
        raws.append(grad * lax.rsqrt(moment))
    raw = jnp.concatenate(raws, axis=0)
    clip = jnp.maximum(1.0, jnp.sqrt(total_of(raw * raw) / raw.size))
    norm_votes = jnp.tanh(raw / clip)
    copies = exchange_start(
        2,
        jnp.concatenate([head_votes, norm_votes, jnp.broadcast_to(loss, (8, width))], axis=0),
    )


    for b in range(3):
        first, last = (0, side - 1) if b == 0 else (0, side)
        shift = 1 if b == 0 else 0
        for a in range(3):
            left = xs_t[0 if b == 1 else 1, 0 if a == 1 else 1, :, first * band : last * band]
            start = 1 if a == 0 else 0
            right = back_one[first + shift : last + shift, start : start + side]
            grad_one[pl.ds((a * 3 + b) * in_width, in_width), :] = jnp.dot(
                left, right.reshape(-1, width), preferred_element_type=f32
            )
        if b == 0:
            stage[2] = scatter_two(2, stage[2])
        if b == 1:
            copies = exchange_middle(2, copies)
        if b == 2:
            stage[3] = scatter_two(3, stage[3])

    matrix_votes(
        0,
        grad_one,
        (lambda: scatter_three(2, stage[2]), lambda: scatter_three(3, stage[3])),
    )
    stage = {t: scatter_start(t) for t in (1, 0)}

    @pl.when(z >= 2)
    def _():
        own_block()

    gathered = {}
    for t in (1, 0):
        stage[t] = scatter_one(t, stage[t])
    for t in (2, 3):
        gathered[t] = gather_one(t)
    for t in (1, 0):
        stage[t] = scatter_two(t, stage[t])
    for t in (2, 3):
        gathered[t] = gather_two(t, gathered[t])
    for t in (1, 0):
        scatter_three(t, stage[t])
    for t in (2, 3):
        gathered[t] = gather_three(t, gathered[t])

    @pl.when(z < 2)
    def _():
        own_block()

    sums = exchange_end(2, copies)
    loss_ref[...] = sums[TAIL:, :1][:1]
    old = jnp.concatenate([head_ref[...], norm_ref[...]], axis=0)
    is_head = lax.broadcasted_iota(jnp.int32, (TAIL, width), 0) < classes
    scale = jnp.where(is_head, scales[3], scales[4])
    sums = sums[:TAIL]
    fresh = old - scale * jnp.tanh(sums * root)
    both = jnp.concatenate([sums, fresh], axis=0)
    high = both.astype(low)
    rest = both - high.astype(f32)
    middle = rest.astype(low)
    parts = jnp.concatenate([high, middle, (rest - middle.astype(f32)).astype(low)], axis=0)

    for t in (1, 0):
        gathered[t] = gather_one(t)

    flat_sums, flat_new = [], []
    window = 256
    for q in range(classes):
        start = min(q * width // classes // 128 * 128, width - window)
        down = lax.broadcasted_iota(jnp.int32, (window, width), 0)
        across = lax.broadcasted_iota(jnp.int32, (window, width), 1)
        gap = across - classes * down + (q * width - classes * start)
        chosen = jnp.where(jnp.logical_and(gap >= 0, gap < classes), 1.0, 0.0).astype(low)
        moved = jnp.dot(parts[:, start : start + window], chosen, preferred_element_type=f32)
        moved = moved[: 2 * TAIL] + moved[2 * TAIL : 4 * TAIL] + moved[4 * TAIL :]
        spot_of = lax.broadcasted_iota(jnp.int32, (TAIL, width), 1).astype(f32) + q * width
        class_of = spot_of - classes * jnp.floor((spot_of + 0.5) / classes)
        here = lax.broadcasted_iota(jnp.int32, (TAIL, width), 0).astype(f32) == class_of
        flat_sums.append(jnp.sum(jnp.where(here, moved[:TAIL], 0.0), axis=0, keepdims=True))
        flat_new.append(jnp.sum(jnp.where(here, moved[TAIL:], 0.0), axis=0, keepdims=True))
    flat_sums = jnp.concatenate(flat_sums + [sums[classes:]], axis=0)
    flat_new = jnp.concatenate(flat_new + [fresh[classes:]], axis=0)

    for t in (1, 0):
        gathered[t] = gather_two(t, gathered[t])

    halo_copy().wait()

    @pl.when(me < 31)
    def _():
        pltpu.make_async_copy(
            weight.at[pl.ds(OWN, TAIL)], weight.at[pl.ds(OWN, TAIL)], fetch_sem.at[4]
        ).wait()
        total[pl.ds(OWN, TAIL), :] = halo_in[...]
        for k in range(TAIL // 8):
            renew(OWN + 8 * k, first_row + OWN + 8 * k)

    @pl.when(me == 31)
    def _():
        for k in range(TAIL // 8):
            flat_rows(OWN + 8 * k, flat_sums[8 * k : 8 * k + 8], vote_flat)
            flat_rows(OWN + 8 * k, flat_new[8 * k : 8 * k + 8], new_flat)

    shift = 2 * me
    share = vote_ref.shape[0]
    vote_ref[...] = vote_flat[pl.ds(shift, share), :]
    new_ref[...] = new_flat[pl.ds(shift, share), :]
    for k in range(TAIL // 8):
        flat_rows(OWN + 8 * k, flat_new[8 * k : 8 * k + 8], new_flat)
    tail_low[...] = new_flat[pl.ds(span, 4 * TAIL), :].astype(low)
    keep_tail = pltpu.make_async_copy(
        tail_low, out_ref.at[pl.ds(32 * span, 4 * TAIL)], keep_sem.at[1]
    )
    keep_tail.start()

    for t in (1, 0):
        gathered[t] = gather_three(t, gathered[t])
    for t in range(4):
        for copy in gathered[t]:
            copy.wait()

        @pl.when(z != t)
        def _():
            line_copy(t, z).wait_send()

    for k in range(3):
        spread_copy(k).wait_send()
    keep_tail.wait()


def finish_kernel(count, chunks, *refs):
    sources, targets, sem = refs[:count], refs[count : 2 * count], refs[2 * count]
    copies = []
    rows = sources[0].shape[0]
    step = -(-rows // chunks // 16) * 16
    for k in range(chunks):
        here = pl.ds(k * step, min(step, rows - k * step))
        copies.append(
            pltpu.make_async_copy(sources[0].at[here], targets[0].at[here], sem.at[k])
        )
    for k in (1, 2):
        copies.append(pltpu.make_async_copy(sources[k], targets[k], sem.at[chunks + k]))
    for copy in copies:
        copy.start()
    for k in range(3, count):
        targets[k][...] = sources[k][...]
    for copy in copies:
        copy.wait()


def finish(values):
    vmem = pl.BlockSpec(memory_space=pltpu.VMEM)
    hbm = pl.BlockSpec(memory_space=pl.ANY)
    count, chunks = len(values), 8
    specs = [hbm] * 3 + [vmem] * (count - 3)
    return pl.pallas_call(
        functools.partial(finish_kernel, count, chunks),
        out_shape=[jax.ShapeDtypeStruct(value.shape, value.dtype) for value in values],
        in_specs=specs,
        out_specs=specs,
        scratch_shapes=[pltpu.SemaphoreType.DMA((chunks + 3,))],
        name="finish",
    )(*values)


def run_step(xs, conv_one, conv_two, shortcut, head, norm_params, valid, labels, rows, cols, moment):
    vmem = pl.BlockSpec(memory_space=pltpu.VMEM)
    hbm = pl.BlockSpec(memory_space=pl.ANY)
    low, f32 = jnp.bfloat16, jnp.float32
    dma = pltpu.SemaphoreType.DMA
    workers = lax.axis_size("dp")
    slots, in_width = xs.shape[4:]
    width = conv_one.shape[1]
    pixels = 16 * slots
    shape = jax.ShapeDtypeStruct
    edges = [conv_one.shape[0]]
    edges.append(edges[0] + conv_two.shape[0])
    edges.append(edges[1] + shortcut.shape[0])
    flat = (edges[2] + TAIL) * width // 128
    share = flat // workers
    return pl.pallas_call(
        functools.partial(step_kernel, tuple(edges), 1.0 / math.sqrt(workers)),
        out_shape=(
            shape((share, 128), f32),
            shape((share, 128), f32),
            shape((flat, 128), low),
            shape(rows.shape, f32),
            shape(cols.shape, f32),
            shape(moment.shape, f32),
            shape((1, 1), f32),
            shape((1, 1), f32),
        ),
        in_specs=[vmem] + [hbm] * 3 + [vmem] * 7,
        out_specs=(vmem, vmem, hbm) + (vmem,) * 5,
        scratch_shapes=[
            pltpu.VMEM(conv_one.shape, f32),
            pltpu.VMEM(conv_two.shape, f32),
            pltpu.VMEM(shortcut.shape, f32),
            pltpu.VMEM((9, in_width, width), low),
            pltpu.VMEM((9, width, width), low),
            pltpu.VMEM((1, in_width, width), low),
            pltpu.VMEM((pixels, width), f32),
            pltpu.VMEM((pixels, width), f32),
            pltpu.VMEM((pixels, width), f32),
            pltpu.VMEM((4, 6, slots, width), low),
            pltpu.VMEM((4, 6, slots, width), low),
            pltpu.VMEM((4, 5, slots, width), low),
            pltpu.VMEM((pixels, width), low),
            pltpu.VMEM((width, pixels), low),
            pltpu.VMEM((2, 2, in_width, pixels), low),
            pltpu.VMEM((128, width), f32),
            pltpu.VMEM((conv_two.shape[0], 128), f32),
            pltpu.VMEM((8, width), f32),
            pltpu.VMEM((2, 8, width), f32),
            pltpu.VMEM((2, 8, 8, width), f32),
            pltpu.VMEM((2, 4, 8, width), f32),
            pltpu.VMEM((TAIL + 8, width), f32),
            pltpu.VMEM((8, TAIL + 8, width), f32),
            pltpu.VMEM((4, TAIL + 8, width), f32),
            pltpu.VMEM((edges[2], width), low),
            pltpu.VMEM((4, 2, 2, OWN, width), low),
            pltpu.VMEM((4, 2, HALF, width), low),
            pltpu.VMEM((4, 2, HALF, width), low),
            pltpu.VMEM((4, OWN, width), low),
            pltpu.VMEM((4, OWN, width), low),
            pltpu.VMEM((TAIL, width), f32),
            pltpu.VMEM((OWN + TAIL, width), f32),
            pltpu.VMEM((OWN + TAIL, width), f32),
            pltpu.VMEM((4 * (OWN + TAIL), 128), f32),
            pltpu.VMEM((4 * (OWN + TAIL), 128), f32),
            pltpu.VMEM((4 * OWN, 128), low),
            pltpu.VMEM((4 * TAIL, 128), low),
            dma((5,)),
            dma((3, 10)),
            dma((3, 10)),
            dma((4, 4)),
            dma((4, 4)),
            dma((4, 4)),
            dma((4, 4)),
            dma((4,)),
            dma((4,)),
            dma((2,)),
            dma((11, 4)),
            dma((11, 4)),
            dma((2,)),
        ],
        compiler_params=pltpu.CompilerParams(
            collective_id=1, has_side_effects=True, vmem_limit_bytes=63 * 1024 * 1024
        ),
        name="step",
    )(xs, conv_one, conv_two, shortcut, head, norm_params, valid, labels, rows, cols, moment)


def scale_for(weight):
    return jnp.maximum(EPS_SCALE, jnp.sqrt(jnp.mean(weight * weight)))


def local_general(
    images,
    valid_slot,
    labels,
    conv_one,
    conv_two,
    shortcut,
    classifier,
    norm_params,
    row_state,
    col_state,
    bn_moment,
):
    in_width = images.shape[3]
    width = conv_one.shape[1]
    kernel_one = conv_one.astype(jnp.bfloat16).reshape(3, 3, in_width, width)
    kernel_two = conv_two.astype(jnp.bfloat16).reshape(3, 3, width, width)
    kernel_short = shortcut.astype(jnp.bfloat16).reshape(1, 1, in_width, width)
    head_low = classifier.astype(jnp.bfloat16)
    slot_count = images.shape[0]
    out_side = images.shape[1] // 2
    pixel_count = out_side * out_side
    slot_weight = valid_slot.astype(jnp.float32)
    pixel_weight = jnp.broadcast_to(slot_weight[:, None], (slot_count, pixel_count)).reshape(-1, 1)
    main_pre, side_pre = first_section(images, kernel_one, kernel_short)
    main_sums = masked_moments(pixel_weight, main_pre)
    side_sums = masked_moments(pixel_weight, side_pre)
    count_row = jnp.broadcast_to(jnp.sum(slot_weight), (width,))
    first_sums = lax.psum(jnp.stack([*main_sums, *side_sums, count_row]), "dp")
    valid_count = first_sums[4, 0]
    denominator = jnp.maximum(valid_count, 1.0)
    pixels = denominator * pixel_count
    norm_one = settle(first_sums[0], first_sums[1], pixels)
    norm_side = settle(first_sums[2], first_sums[3], pixels)
    hidden_one, active, main_two = second_section(
        main_pre, norm_one, norm_params, kernel_two, slot_count, out_side
    )
    two_sums = masked_moments(pixel_weight, main_two)
    second_sums = lax.psum(jnp.stack([*two_sums]), "dp")
    norm_two = settle(second_sums[0], second_sums[1], pixels)
    joined_pre = (
        (main_two - norm_two[0]) * norm_two[1] * norm_params[2]
        + norm_params[3]
        + (side_pre - norm_side[0]) * norm_side[1] * norm_params[4]
        + norm_params[5]
    )
    joined = jax.nn.silu(joined_pre).reshape(slot_count, pixel_count, -1)
    pooled = jnp.mean(joined, axis=1).astype(jnp.bfloat16)
    logits = jnp.dot(pooled, head_low, preferred_element_type=jnp.float32)
    largest = jnp.max(logits, axis=1, keepdims=True)
    exp_terms = jnp.exp(logits - largest)
    total_exp = jnp.sum(exp_terms, axis=1, keepdims=True)
    log_total = largest[:, 0] + jnp.log(total_exp[:, 0])
    onehot = (labels[:, None] == jnp.arange(logits.shape[1], dtype=jnp.int32)[None, :]).astype(
        jnp.float32
    )
    local_sum = jnp.sum(slot_weight * (log_total - jnp.sum(onehot * logits, axis=1)))
    grad_logits = ((exp_terms / total_exp - onehot) * (slot_weight / denominator)[:, None]).astype(
        jnp.bfloat16
    )
    grad_head = lax.dot_general(
        pooled, grad_logits, (((0,), (0,)), ((), ())), preferred_element_type=jnp.float32
    )
    grad_pooled = lax.dot_general(
        grad_logits, head_low, (((1,), (1,)), ((), ())), preferred_element_type=jnp.float32
    )
    spread_pooled = jnp.broadcast_to(
        (grad_pooled / pixel_count)[:, None, :], (slot_count, pixel_count, width)
    )
    grad_joined = spread_pooled.reshape(slot_count * pixel_count, width) * silu_slope(joined_pre)
    gain_two, shift_two, grad_two = norm_backward(grad_joined, main_two, norm_two, norm_params[2])
    gain_side, shift_side, grad_side = norm_backward(
        grad_joined, side_pre, norm_side, norm_params[4]
    )
    grad_two_maps = grad_two.reshape(slot_count, out_side, out_side, width)
    grad_side_maps = grad_side.reshape(slot_count, out_side, out_side, width)
    grad_conv_two = conv_weight_grad(active, grad_two_maps, 1, 1, 1)
    grad_short = conv_weight_grad(images, grad_side_maps, 2, 0, -1)
    kernel_turned = jnp.transpose(kernel_two[::-1, ::-1], (0, 1, 3, 2))
    grad_active = conv_apply(grad_two_maps, kernel_turned, 1, 1).reshape(
        slot_count * pixel_count, width
    )
    grad_hidden = grad_active * silu_slope(hidden_one)
    gain_one, shift_one, grad_one = norm_backward(grad_hidden, main_pre, norm_one, norm_params[0])
    grad_conv_one = conv_weight_grad(
        images, grad_one.reshape(slot_count, out_side, out_side, width), 2, 1, 0
    )
    grad_norms = jnp.stack([gain_one, shift_one, gain_two, shift_two, gain_side, shift_side])
    grads = (grad_conv_one, grad_conv_two, grad_short, grad_head, grad_norms)
    votes, rows_new, cols_new, moment_new = make_votes(
        grads, row_state[0], col_state[0], bn_moment[0]
    )
    workers = lax.axis_size("dp")
    weights = (conv_one, conv_two, shortcut, classifier, norm_params)
    scales = [scale_for(weight) for weight in weights]
    loss_sum = lax.psum(local_sum, "dp")
    flat_vote = jnp.concatenate([vote.reshape(-1) for vote in votes])
    flat_old = jnp.concatenate([weight.reshape(-1) for weight in weights])
    flat_scale = jnp.concatenate(
        [
            jnp.broadcast_to(scale, (weight.size,))
            for scale, weight in zip(scales, weights)
        ]
    )
    vote_mine = lax.psum_scatter(flat_vote, "dp", tiled=True)
    share = vote_mine.shape[0]
    start = lax.axis_index("dp") * share
    new_mine = lax.dynamic_slice_in_dim(
        flat_old, start, share
    ) - lax.dynamic_slice_in_dim(flat_scale, start, share) * jnp.tanh(
        vote_mine / math.sqrt(workers)
    )
    copies = lax.all_gather(new_mine.astype(jnp.bfloat16), "dp", tiled=True)
    return (
        loss_sum,
        valid_count,
        new_mine,
        copies,
        vote_mine,
        rows_new[None, :],
        cols_new[None, :],
        moment_new[None, :],
    )


def local(
    images,
    valid_slot,
    labels,
    conv_one,
    conv_two,
    shortcut,
    classifier,
    norm_params,
    row_state,
    col_state,
    bn_moment,
):
    slots, height, _, in_width = images.shape
    side = height // 2
    xs = images.reshape(slots, side, 2, side, 2, in_width).transpose(4, 3, 2, 1, 0, 5)
    new_mine, vote_mine, copies, rows_new, cols_new, moment_new, loss_sum, valid_count = run_step(
        xs,
        conv_one,
        conv_two,
        shortcut,
        classifier.T,
        norm_params,
        valid_slot.reshape(1, -1),
        labels.reshape(1, -1),
        row_state,
        col_state,
        bn_moment,
    )
    copies, new_mine, vote_mine, rows_new, cols_new, moment_new, loss_sum, valid_count = finish(
        (copies, new_mine, vote_mine, rows_new, cols_new, moment_new, loss_sum, valid_count)
    )
    return (
        loss_sum.reshape(()),
        valid_count.reshape(()),
        new_mine.reshape(-1),
        copies.reshape(-1),
        vote_mine.reshape(-1),
        rows_new,
        cols_new,
        moment_new,
    )


def solution(mesh):
    placed = (
        P("dp", None, None, None),
        P("dp"),
        P("dp"),
        P(),
        P(),
        P(),
        P(),
        P(),
        P("dp", None),
        P("dp", None),
        P("dp", None),
    )
    return jax.shard_map(
        local if mesh.shape["dp"] == 32 else local_general,
        mesh=mesh,
        in_specs=placed,
        out_specs=(P(), P(), P("dp"), P(), P("dp"), P("dp", None), P("dp", None), P("dp", None)),
        check_vma=False,
    )
```

```python
import functools
import math

import jax
import jax.numpy as jnp
from jax import lax
from jax.experimental import pallas as pl
from jax.experimental.pallas import tpu as pltpu
from jax.sharding import PartitionSpec as P

STEP = 10
MESH = pl.DeviceIdType.MESH

EPS_NORM = 1e-05
EPS_ROW = 1e-30
EPS_SCALE = 0.001
FORWARD_DIMS = ("NHWC", "HWIO", "NHWC")
WEIGHT_DIMS = ("CHWN", "IHWO", "HWNC")
OWN = 224
TAIL = 16
PIECE = 32
SPAN = 4 * OWN
HALF = SPAN // 2
GROUP = 64


def conv_apply(maps, kernel, stride, margin):
    return lax.conv_general_dilated(
        maps,
        kernel,
        (stride, stride),
        ((margin, margin), (margin, margin)),
        dimension_numbers=FORWARD_DIMS,
        preferred_element_type=jnp.float32,
    )


def conv_weight_grad(maps, grad_out, stride, low_pad, high_pad):
    result = lax.conv_general_dilated(
        maps,
        grad_out,
        (1, 1),
        ((low_pad, high_pad), (low_pad, high_pad)),
        rhs_dilation=(stride, stride),
        dimension_numbers=WEIGHT_DIMS,
        preferred_element_type=jnp.float32,
    )
    return result.reshape(-1, result.shape[3])


def silu_slope(values):
    sigmoid_part = jax.nn.sigmoid(values)
    return sigmoid_part * (1.0 + values * (1.0 - sigmoid_part))


def settle(sum_plain, sum_square, pixels):
    mean_value = sum_plain / pixels
    return (mean_value, lax.rsqrt(sum_square / pixels - mean_value * mean_value + EPS_NORM))


def first_section(images, kernel_one, kernel_short):
    row_count = images.shape[0] * (images.shape[1] // 2) ** 2
    main_pre = conv_apply(images, kernel_one, 2, 1).reshape(row_count, -1)
    side_pre = conv_apply(images, kernel_short, 2, 0).reshape(row_count, -1)
    return (main_pre, side_pre)


def second_section(main_pre, norm_one, norm_params, kernel_two, slot_count, out_side):
    hidden_one = (main_pre - norm_one[0]) * norm_one[1] * norm_params[0] + norm_params[1]
    active = (
        jax.nn.silu(hidden_one).astype(jnp.bfloat16).reshape(slot_count, out_side, out_side, -1)
    )
    main_two = conv_apply(active, kernel_two, 1, 1).reshape(slot_count * out_side * out_side, -1)
    return (hidden_one, active, main_two)


def masked_moments(pixel_weight, values):
    return (jnp.sum(pixel_weight * values, axis=0), jnp.sum(pixel_weight * values * values, axis=0))


def soft_sign(step_raw):
    clip_by = jnp.maximum(1.0, jnp.sqrt(jnp.mean(step_raw * step_raw)))
    return jnp.tanh(step_raw / clip_by)


def make_votes(grads, rows_old, cols_old, moment_old):
    decay_rate = 1.0 - STEP ** (-0.8)
    votes, rows_new, cols_new = ([], [], [])
    row_at, col_at = (0, 0)
    for matrix in grads[:4]:
        row_size, col_size = matrix.shape
        square = matrix * matrix + EPS_ROW
        row_part = decay_rate * rows_old[row_at : row_at + row_size] + (
            1.0 - decay_rate
        ) * jnp.mean(square, axis=1)
        col_part = decay_rate * cols_old[col_at : col_at + col_size] + (
            1.0 - decay_rate
        ) * jnp.mean(square, axis=0)
        second = row_part[:, None] * col_part[None, :] / jnp.mean(row_part)
        votes.append(soft_sign(matrix * lax.rsqrt(second)))
        rows_new.append(row_part)
        cols_new.append(col_part)
        row_at += row_size
        col_at += col_size
    flat_norm = grads[4].reshape(-1)
    moment_new = decay_rate * moment_old + (1.0 - decay_rate) * (flat_norm * flat_norm + EPS_ROW)
    votes.append(soft_sign(flat_norm * lax.rsqrt(moment_new)))
    return (votes, jnp.concatenate(rows_new), jnp.concatenate(cols_new), moment_new)


def norm_backward(grad_out, pre_value, norm_pair, gain_row):
    normed = (pre_value - norm_pair[0]) * norm_pair[1]
    grad_gain = jnp.sum(grad_out * normed, axis=0)
    grad_shift = jnp.sum(grad_out, axis=0)
    grad_pre = (grad_out * gain_row * norm_pair[1]).astype(jnp.bfloat16)
    return (grad_gain, grad_shift, grad_pre)


def place():
    me = lax.axis_index("dp")
    core = lax.rem(me, 2)
    x = lax.rem(lax.div(me, 2), 2)
    y = lax.rem(lax.div(me, 4), 2)
    z = lax.div(me, 8)
    return me, core, x, y, z


def send(src, dst, send_sem, recv_sem, partner):
    copy = pltpu.make_async_remote_copy(
        src_ref=src,
        dst_ref=dst,
        send_sem=send_sem,
        recv_sem=recv_sem,
        device_id=(partner,),
        device_id_type=MESH,
    )
    copy.start()
    return copy


def scale_of(row, scales, edges):
    picked = scales[2]
    picked = jnp.where(row < edges[1], scales[1], picked)
    return jnp.where(row < edges[0], scales[0], picked)


def settle_rows(sums, pixels, gain, shift):
    mean = sums[0] / pixels
    inv = lax.rsqrt(sums[1] / pixels - mean * mean + EPS_NORM)
    slope = gain * inv
    return mean, inv, slope, shift - mean * slope


def gate(values):
    return 0.5 * jnp.tanh(0.5 * values) + 0.5


def eye_mask(rows, columns, offset=0):
    down = lax.broadcasted_iota(jnp.int32, (rows, columns), 0) + offset
    return down == lax.broadcasted_iota(jnp.int32, (rows, columns), 1)


def column_of(row, size):
    spread = jnp.where(eye_mask(size, size), jnp.broadcast_to(row, (size, size)), 0)
    return jnp.sum(spread, axis=1, keepdims=True)


def total_of(values):
    return jnp.sum(jnp.sum(values, axis=0, keepdims=True), axis=1, keepdims=True)


def fold(values):
    return jnp.sum(values.reshape(values.shape[0] // 8, 8, values.shape[1]), axis=0)


def cast_weight(source, target, square_ref, taps, depth):
    step = 128
    square_ref[...] = jnp.zeros_like(square_ref)
    for tap in range(taps):
        new_tap = (tap % 3) * 3 + tap // 3

        @pl.loop(0, depth // step)
        def _(k):
            start = pl.multiple_of(k * step, step)
            values = source[pl.ds(tap * depth + start, step), :]
            target[new_tap, pl.ds(start, step), :] = values.astype(jnp.bfloat16)
            square_ref[...] += fold(values * values)


def factored_votes(grad, rows, row_at, rows_old, rows_new, col_old, level, votes, vote_at, between):
    width = grad.shape[1]
    keep = 1.0 - STEP ** (-0.8)
    step = 128
    quarters = width // 128

    def first(k, carry):
        col_sum, row_sum = carry
        start = pl.multiple_of(k * step, step)
        lanes = pl.ds(pl.multiple_of(row_at + start, step), step)
        old = rows_old[:, lanes] * keep
        line = jnp.zeros((8, 128), jnp.float32)
        for m in range(step // 8):
            block = grad[pl.ds(start + 8 * m, 8), :]
            square = block * block
            col_sum = col_sum + square
            part = square[:, :128]
            for q in range(1, quarters):
                part = part + square[:, 128 * q : 128 * (q + 1)]
            part = part * ((1.0 - keep) / width)
            diagonal = eye_mask(8, 128, 8 * m)
            part = part + jnp.where(diagonal, jnp.broadcast_to(old, (8, 128)), 0.0)
            row = jnp.sum(part, axis=1, keepdims=True) + (1.0 - keep) * EPS_ROW
            row = jnp.broadcast_to(row, (8, 128))
            level[pl.ds(start + 8 * m, 8), :] = row
            row_sum = row_sum + row
            line = line + jnp.where(diagonal, row, 0.0)
        rows_new[:, lanes] = jnp.sum(line, axis=0, keepdims=True)
        return col_sum, row_sum

    col_sum, row_sum = lax.fori_loop(
        0,
        rows // step,
        first,
        (jnp.zeros((8, width), jnp.float32), jnp.zeros((8, 128), jnp.float32)),
    )
    col_new = keep * col_old + (1.0 - keep) * (
        jnp.sum(col_sum, axis=0, keepdims=True) / rows + EPS_ROW
    )
    scale = lax.rsqrt(col_new)
    root_mean = jnp.sqrt(jnp.sum(row_sum, axis=0, keepdims=True) / rows)

    def second(k, carry):
        start = pl.multiple_of(k * step, step)
        for m in range(step // 8):
            here = pl.ds(start + 8 * m, 8)
            factor = lax.rsqrt(level[here, :]) * root_mean
            level[here, :] = factor
            raw = grad[here, :] * scale
            power = raw * raw
            part = power[:, :128]
            for q in range(1, quarters):
                part = part + power[:, 128 * q : 128 * (q + 1)]
            carry = carry + part * (factor * factor)
        return carry

    between[0]()
    power = lax.fori_loop(0, rows // step, second, jnp.zeros((8, 128), jnp.float32))
    between[1]()
    clip = jnp.maximum(1.0, jnp.sqrt(total_of(power) / (rows * width)))
    scale = scale / clip

    def third(k, _):
        start = pl.multiple_of(k * step, step)
        for m in range(step // 16):
            here = pl.ds(start + 16 * m, 16)
            factor = level[here, :]
            factor = jnp.concatenate([factor] * quarters, axis=1)
            vote = jnp.tanh(grad[here, :] * factor * scale)
            vote = vote.astype(jnp.bfloat16)
            at = pl.multiple_of((vote_at + start) * 4 + GROUP * m, GROUP)
            for q in range(quarters):
                votes[pl.ds(at + 16 * q, 16), :] = vote[:, 128 * q : 128 * (q + 1)]
        return 0

    lax.fori_loop(0, rows // step, third, 0)
    return col_new


def step_kernel(
    edges,
    root,
    images,
    one_hbm,
    two_hbm,
    short_hbm,
    head_ref,
    norm_ref,
    valid_ref,
    label_ref,
    row_ref,
    col_ref,
    moment_ref,
    new_ref,
    vote_ref,
    out_ref,
    row_new,
    col_new,
    moment_new,
    loss_ref,
    count_ref,
    xs,
    grad_one,
    grad_two,
    grad_short,
    low_one,
    low_two,
    low_short,
    main_pre,
    side_pre,
    main_two,
    active,
    back_two,
    back_one,
    back_side,
    active_t,
    xs_t,
    head_pad,
    level,
    square,
    post,
    plane,
    line,
    tail_post,
    tail_plane,
    tail_line,
    core_in,
    ax_in,
    by_in,
    plane_in,
    line_in,
    halo_in,
    total,
    weight,
    vote_flat,
    new_flat,
    fetch_sem,
    small_send,
    small_recv,
    core_send,
    core_recv,
    rs_send,
    rs_recv,
    line_send,
    line_recv,
    halo_sem,
    ag_send,
    ag_recv,
    free_sem,
):
    slots, in_width = xs.shape[4:]
    width = main_pre.shape[1]
    side = 4
    band = side * slots
    pixel_count = side * side
    classes = head_ref.shape[0]
    keep = 1.0 - STEP ** (-0.8)
    low = jnp.bfloat16
    f32 = jnp.float32

    me, core, x, y, z = place()
    flip_core = me + 1 - 2 * core
    flip_x = me + 2 - 4 * x
    flip_y = me + 4 - 8 * y
    spot = lax.rem(me, 8)
    near = [z * 8 + lax.rem(spot + k, 8) for k in range(1, 8)]
    far = [lax.rem(z + k, 4) * 8 + spot for k in range(1, 4)]
    ahead, behind = lax.rem(me + 31, 32), lax.rem(me + 1, 32)
    partners = near + far + [ahead, behind]

    fetches = [
        pltpu.make_async_copy(source, target, fetch_sem.at[k])
        for k, (source, target) in enumerate(
            ((one_hbm, grad_one), (short_hbm, grad_short), (two_hbm, grad_two))
        )
    ]
    for fetch in fetches:
        fetch.start()
    barrier = pltpu.get_barrier_semaphore()
    for partner in partners:
        pl.semaphore_signal(barrier, inc=1, device_id=(partner,), device_id_type=MESH)

    def fetch_rows(row, count, place_at, sem):
        parts = (
            (one_hbm, 0, edges[0]),
            (two_hbm, edges[0], edges[1]),
            (short_hbm, edges[1], edges[2]),
        )
        for ref, first, last in parts:

            @pl.when(jnp.logical_and(row >= first, row < last))
            def _():
                start = pl.multiple_of(row - first, count)
                pltpu.make_async_copy(
                    ref.at[pl.ds(start, count)], weight.at[pl.ds(place_at, count)], sem
                ).start()

    first_row = me * OWN
    for k in range(OWN // PIECE):
        fetch_rows(first_row + k * PIECE, PIECE, k * PIECE, fetch_sem.at[3])
    fetch_rows(first_row + OWN, TAIL, OWN, fetch_sem.at[4])

    lines = images.shape[0]
    for half in range(2):
        lanes = slice(128 * half, 128 * (half + 1))
        level[:lines, :] = images[:, lanes].astype(f32)
        for h in range(2 * side):
            for w in range(2 * side):
                rows = level[pl.ds(2 * side * h + w, slots, stride=4 * pixel_count), :]
                xs[w % 2, w // 2, h % 2, h // 2, :, lanes] = rows.astype(low)

    scales = {}

    def scale_from(weight_square, size):
        return jnp.maximum(EPS_SCALE, jnp.sqrt(total_of(weight_square) / size))

    exchanges = (
        (post.at[0], plane.at[0], line.at[0]),
        (post.at[1], plane.at[1], line.at[1]),
        (tail_post, tail_plane, tail_line),
    )

    def exchange_start(which, values):
        mine_ref, plane_ref, _ = exchanges[which]
        mine_ref[...] = values
        plane_ref[spot] = values
        return [
            send(
                mine_ref,
                plane_ref.at[spot],
                small_send.at[which, k],
                small_recv.at[which, k],
                partner,
            )
            for k, partner in enumerate(near)
        ]

    def exchange_middle(which, copies):
        _, plane_ref, line_ref = exchanges[which]
        for copy in copies:
            copy.wait()
        line_ref[z] = functools.reduce(lambda a, b: a + b, [plane_ref[k] for k in range(8)])
        return [
            send(
                line_ref.at[z],
                line_ref.at[z],
                small_send.at[which, 7 + k],
                small_recv.at[which, 7 + k],
                partner,
            )
            for k, partner in enumerate(far)
        ]

    def exchange_end(which, copies):
        line_ref = exchanges[which][2]
        for copy in copies:
            copy.wait()
        return (line_ref[0] + line_ref[1]) + (line_ref[2] + line_ref[3])

    def block_rows(t, yy, xx, cc):
        block = t * 8 + yy * 4 + xx * 2 + cc
        return pl.ds(pl.multiple_of(block * SPAN, 16), SPAN)

    def scatter_start(t):
        return [
            send(
                out_ref.at[block_rows(t, yy, xx, 1 - core)],
                core_in.at[t, yy, xx],
                core_send.at[t, 2 * yy + xx],
                core_recv.at[t, 2 * yy + xx],
                flip_core,
            )
            for yy in range(2)
            for xx in range(2)
        ]

    def scatter_one(t, copies):
        for copy in copies:
            copy.wait()
        for yy in range(2):
            for xx in range(2):
                core_in[t, yy, xx] = core_in[t, yy, xx] + out_ref[block_rows(t, yy, xx, core), :]
        pl.semaphore_signal(
            free_sem.at[t], inc=1, device_id=(flip_core,), device_id_type=MESH
        )
        return (
            send(
                core_in.at[t, :, 1 - x, pl.ds(0, HALF)],
                ax_in.at[t],
                rs_send.at[0, t],
                rs_recv.at[0, t],
                flip_x,
            ),
            send(
                core_in.at[t, 1 - y, :, pl.ds(HALF, HALF)],
                by_in.at[t],
                rs_send.at[1, t],
                rs_recv.at[1, t],
                flip_y,
            ),
        )

    def scatter_two(t, copies):
        copies[0].wait()
        ax_in[t] = ax_in[t] + core_in[t, :, x, :HALF]
        first = send(
            ax_in.at[t, 1 - y],
            plane_in.at[t, pl.ds(0, HALF)],
            rs_send.at[2, t],
            rs_recv.at[2, t],
            flip_y,
        )
        copies[1].wait()
        by_in[t] = by_in[t] + core_in[t, y, :, HALF:]
        second = send(
            by_in.at[t, 1 - x],
            plane_in.at[t, pl.ds(HALF, HALF)],
            rs_send.at[3, t],
            rs_recv.at[3, t],
            flip_x,
        )
        return first, second

    def line_copy(t, slot):
        return pltpu.make_async_remote_copy(
            src_ref=plane_in.at[t],
            dst_ref=line_in.at[slot],
            send_sem=line_send.at[t],
            recv_sem=line_recv.at[slot],
            device_id=(t * 8 + spot,),
            device_id_type=MESH,
        )

    def scatter_three(t, copies):
        copies[0].wait()
        plane_in[t, :HALF] = plane_in[t, :HALF] + ax_in[t, y]
        copies[1].wait()
        plane_in[t, HALF:] = plane_in[t, HALF:] + by_in[t, x]

        @pl.when(z != t)
        def _():
            line_copy(t, z).start()

        @pl.when(z == t)
        def _():
            line_in[t] = plane_in[t]

    own_rows = pl.ds(pl.multiple_of(me * SPAN, 16), SPAN)

    def flat_rows(row, q, values, ref):
        ref[pl.ds(row * 4 + q, 8, stride=4), :] = values

    def renew(row, at_row):
        scale = scale_of(at_row, [scales[k] for k in range(3)], edges)
        for u in (0, 8):
            for q in range(4):
                summed = total[pl.ds(row * 4 + 16 * q + u, 8), :]
                old = weight[pl.ds(row + u, 8), 128 * q : 128 * (q + 1)]
                fresh = old - scale * jnp.tanh(summed * root)
                flat_rows(row + u, q, summed, vote_flat)
                flat_rows(row + u, q, fresh, new_flat)

    def halo_copy():
        return pltpu.make_async_remote_copy(
            src_ref=total.at[pl.ds(0, GROUP)],
            dst_ref=halo_in,
            send_sem=halo_sem.at[0],
            recv_sem=halo_sem.at[1],
            device_id=(ahead,),
            device_id_type=MESH,
        )

    def spread_copy(k):
        return pltpu.make_async_remote_copy(
            src_ref=out_ref.at[own_rows],
            dst_ref=out_ref.at[own_rows],
            send_sem=ag_send.at[0, k],
            recv_sem=ag_recv.at[0, z],
            device_id=(far[k],),
            device_id_type=MESH,
        )

    def own_block():
        for k in range(1, 4):
            line_copy(0, lax.rem(z + k, 4)).wait_recv()
        total[pl.ds(0, SPAN), :] = functools.reduce(
            lambda a, b: a + b, [line_in[t].astype(f32) for t in range(4)]
        )
        halo_copy().start()
        pltpu.make_async_copy(
            weight.at[pl.ds(0, OWN)], weight.at[pl.ds(0, OWN)], fetch_sem.at[3]
        ).wait()

        @pl.loop(0, OWN // 16)
        def _(k):
            row = pl.multiple_of(k * 16, 16)
            renew(row, first_row + row)

        out_ref[own_rows, :] = new_flat[pl.ds(0, SPAN), :].astype(low)
        for k in range(3):
            spread_copy(k).start()

    def piece(rows, kind, t, partner):
        return send(
            out_ref.at[rows], out_ref.at[rows], ag_send.at[kind, t], ag_recv.at[kind, t], partner
        )

    def half_rows(t, yy, xx, half):
        block = t * 8 + yy * 4 + xx * 2 + core
        return pl.ds(pl.multiple_of(block * SPAN + half * HALF, 16), HALF)

    def gather_one(t):
        @pl.when(z != t)
        def _():
            pltpu.make_async_remote_copy(
                src_ref=out_ref.at[own_rows],
                dst_ref=out_ref.at[own_rows],
                send_sem=ag_send.at[0, 0],
                recv_sem=ag_recv.at[0, t],
                device_id=(far[0],),
                device_id_type=MESH,
            ).wait_recv()

        return (
            piece(half_rows(t, y, x, 0), 1, t, flip_y),
            piece(half_rows(t, y, x, 1), 2, t, flip_x),
        )

    def gather_two(t, copies):
        copies[0].wait()
        sent = [piece(half_rows(t, yy, x, 0), 3 + yy, t, flip_x) for yy in range(2)]
        copies[1].wait()
        return sent + [piece(half_rows(t, y, xx, 1), 5 + xx, t, flip_y) for xx in range(2)]

    def gather_three(t, copies):
        for copy in copies:
            copy.wait()
        pl.semaphore_wait(free_sem.at[t], 1)
        sent = []
        for yy in range(2):
            for xx in range(2):
                block = t * 8 + yy * 4 + xx * 2 + core
                rows = pl.ds(pl.multiple_of(block * SPAN, 16), SPAN)
                sent.append(piece(rows, 7 + 2 * yy + xx, t, flip_core))
        return sent

    valid_column = column_of(valid_ref[...].astype(f32), slots)
    weight_slot = jnp.broadcast_to(valid_column, (slots, width))
    weight_band = jnp.concatenate([weight_slot] * side, axis=0)

    fetches[0].wait()
    cast_weight(grad_one, low_one, square, 9, in_width)
    scales[0] = scale_from(square[...], grad_one.size)
    fetches[1].wait()
    cast_weight(grad_short, low_short, square, 1, in_width)
    scales[2] = scale_from(square[...], grad_short.size)

    def image_taps(j):
        pieces = []
        for b in range(3):
            column = j if b else j - 1
            if column < 0:
                continue
            across = 0 if b == 1 else 1
            for a in range(3):
                if a == 1:
                    piece = xs[across, column, 0].reshape(band, in_width)
                elif a == 2:
                    piece = xs[across, column, 1].reshape(band, in_width)
                else:
                    piece = xs[across, column, 1, : side - 1].reshape(band - slots, in_width)
                    piece = jnp.concatenate([jnp.zeros((slots, in_width), low), piece], axis=0)
                pieces.append(piece)
        return jnp.concatenate(pieces, axis=1)

    def moments(values):
        weighted = values * weight_band
        return (
            jnp.sum(weighted, axis=0, keepdims=True),
            jnp.sum(weighted * values, axis=0, keepdims=True),
        )

    def add_up(old, new):
        return [a + b for a, b in zip(old, new)]

    none = jnp.zeros((1, width), f32)
    main_sums, side_sums = [none, none], [none, none]
    for j in range(side):
        here = pl.ds(j * band, band)
        low_rows = low_one[3 if j == 0 else 0 :].reshape(-1, width)
        value = jnp.dot(image_taps(j), low_rows, preferred_element_type=f32)
        main_pre[here, :] = value
        main_sums = add_up(main_sums, moments(value))
        value = jnp.dot(
            xs[0, j, 0].reshape(band, in_width), low_short[0], preferred_element_type=f32
        )
        side_pre[here, :] = value
        side_sums = add_up(side_sums, moments(value))

    count = jnp.broadcast_to(jnp.sum(valid_column, axis=0, keepdims=True), (1, width))
    pl.semaphore_wait(barrier, len(partners))
    copies = exchange_start(
        0, jnp.concatenate(main_sums + side_sums + [count, none, none, none], axis=0)
    )
    fetches[2].wait()
    cast_weight(grad_two, low_two, square, 9, width)
    scales[1] = scale_from(square[...], grad_two.size)
    copies = exchange_middle(0, copies)
    for across in range(2):
        for down in range(2):
            for j in range(side):
                block = xs[across, j, down].reshape(band, in_width)
                xs_t[across, down, :, j * band : (j + 1) * band] = block.T
    border = jnp.zeros((side, 1, slots, width), low)
    active[:, 0:1] = border
    active[:, side + 1 :] = border
    back_two[:, 0:1] = border
    back_two[:, side + 1 :] = border
    back_one[:, side:] = border
    head_pad[...] = jnp.zeros_like(head_pad)
    head_pad[:classes, :] = head_ref[...]
    head = head_pad[:16, :]
    scales[3] = scale_from(head * head, head_ref.size)
    params = norm_ref[...]
    scales[4] = scale_from(params * params, norm_ref.size)
    sums = exchange_end(0, copies)

    valid_count = sums[4:5]
    count_ref[...] = valid_count[:, :1]
    denominator = jnp.maximum(valid_count, 1.0)
    pixels = denominator * pixel_count
    gains = [norm_ref[k : k + 1, :] for k in range(6)]
    mean_one, inv_one, slope_one, base_one = settle_rows(
        (sums[0:1], sums[1:2]), pixels, gains[0], gains[1]
    )
    mean_side, inv_side, slope_side, base_side = settle_rows(
        (sums[2:3], sums[3:4]), pixels, gains[4], gains[5]
    )

    for j in range(side):
        hidden = main_pre[pl.ds(j * band, band), :] * slope_one + base_one
        active[j, 1 : side + 1] = (
            (hidden * gate(hidden)).astype(low).reshape(side, slots, width)
        )
    two_sums = [none, none]
    for j in range(side):
        taps = [b for b in range(3) if 0 <= j + b - 1 < side]
        pieces = [
            active[j + b - 1, a : a + side].reshape(band, width) for b in taps for a in range(3)
        ]
        low_rows = low_two[3 * taps[0] : 3 * taps[-1] + 3].reshape(-1, width)
        value = jnp.dot(jnp.concatenate(pieces, axis=1), low_rows, preferred_element_type=f32)
        main_two[pl.ds(j * band, band), :] = value
        two_sums = add_up(two_sums, moments(value))
    copies = exchange_start(1, jnp.concatenate(two_sums + [none] * 6, axis=0))
    for j in range(side):
        block = active[j, 1 : side + 1].reshape(band, width)
        active_t[:, j * band : (j + 1) * band] = block.T
    copies = exchange_middle(1, copies)
    sums = exchange_end(1, copies)
    mean_two, inv_two, slope_two, base_two = settle_rows(
        (sums[0:1], sums[1:2]), pixels, gains[2], gains[3]
    )

    base_joined = base_two + base_side

    def joined_of(here):
        return main_two[here, :] * slope_two + side_pre[here, :] * slope_side + base_joined

    pooled = jnp.zeros((slots, width), f32)
    for p in range(pixel_count):
        joined = joined_of(pl.ds(p * slots, slots))
        pooled = pooled + joined * gate(joined)
    pooled = (pooled / pixel_count).astype(low)
    head_low = head_pad[...].astype(low)
    logits = lax.dot_general(
        pooled, head_low, (((1,), (1,)), ((), ())), preferred_element_type=f32
    )
    lane = lax.broadcasted_iota(jnp.int32, logits.shape, 1)
    real = lane < classes
    largest = jnp.max(jnp.where(real, logits, -jnp.inf), axis=1, keepdims=True)
    powers = jnp.where(real, jnp.exp(jnp.where(real, logits - largest, 0.0)), 0.0)
    total_power = jnp.sum(powers, axis=1, keepdims=True)
    label_column = column_of(label_ref[...].astype(f32), slots).astype(jnp.int32)
    onehot = jnp.where(lane == label_column, 1.0, 0.0)
    entropy = largest + jnp.log(total_power) - jnp.sum(onehot * logits, axis=1, keepdims=True)
    loss = jnp.sum(entropy * valid_column, axis=0, keepdims=True)
    grad_logits = (
        (powers / total_power - onehot) * (valid_column / denominator[:, :1])
    ).astype(low)
    grad_head = lax.dot_general(
        grad_logits, pooled, (((0,), (0,)), ((), ())), preferred_element_type=f32
    )[:16]
    grad_pooled = jnp.dot(grad_logits, head_low, preferred_element_type=f32) / pixel_count

    gain_two, gain_side, shift_two = none, none, none
    for p in range(pixel_count):
        here = pl.ds(p * slots, slots)
        joined = joined_of(here)
        opened = gate(joined)
        grad = grad_pooled * (opened * (1.0 + joined * (1.0 - opened)))
        shift_two = shift_two + jnp.sum(grad, axis=0, keepdims=True)
        gain_two = gain_two + jnp.sum(
            grad * ((main_two[here, :] - mean_two) * inv_two), axis=0, keepdims=True
        )
        gain_side = gain_side + jnp.sum(
            grad * ((side_pre[here, :] - mean_side) * inv_side), axis=0, keepdims=True
        )
        back_two[p // side, 1 + p % side] = (grad * slope_two).astype(low)
        back_side[here, :] = (grad * slope_side).astype(low)

    grad_short[...] = jnp.dot(xs_t[0, 0], back_side[...], preferred_element_type=f32)
    for b in range(3):
        first, last = max(0, b - 1), min(side, side + b - 1)
        left = active_t[:, first * band : last * band]
        for a in range(3):
            right = back_two[first - b + 1 : last - b + 1, 2 - a : 2 - a + side]
            grad_two[pl.ds((a * 3 + b) * width, width), :] = jnp.dot(
                left, right.reshape(-1, width), preferred_element_type=f32
            )


    def nothing():
        pass

    def matrix_votes(k, grad, between):
        here = pl.ds(k * width, width)
        start = edges[k - 1] if k else 0
        col_new[:, here] = factored_votes(
            grad, grad.shape[0], start, row_ref, row_new, col_ref[:, here], level, out_ref, start, between
        )

    matrix_votes(2, grad_short, (nothing, nothing))
    matrix_votes(1, grad_two, (nothing, nothing))
    stage = {t: scatter_start(t) for t in (2, 3)}

    gain_one, shift_one = none, none
    for j in range(side):
        taps = [b for b in range(3) if 0 <= j - b + 1 < side]
        pieces = [
            back_two[j - b + 1, 2 - a : 2 - a + side].reshape(band, width)
            for b in taps
            for a in range(3)
        ]
        weights = jnp.concatenate([low_two[b * 3 + a] for b in taps for a in range(3)], axis=1)
        grad = lax.dot_general(
            jnp.concatenate(pieces, axis=1),
            weights,
            (((1,), (1,)), ((), ())),
            preferred_element_type=f32,
        )
        before = main_pre[pl.ds(j * band, band), :]
        hidden = before * slope_one + base_one
        opened = gate(hidden)
        grad = grad * (opened * (1.0 + hidden * (1.0 - opened)))
        shift_one = shift_one + jnp.sum(grad, axis=0, keepdims=True)
        gain_one = gain_one + jnp.sum(
            grad * ((before - mean_one) * inv_one), axis=0, keepdims=True
        )
        back_one[j, :side] = (grad * slope_one).astype(low).reshape(side, slots, width)
        if j == 1:
            stage[2] = scatter_one(2, stage[2])
        if j == 2:
            stage[3] = scatter_one(3, stage[3])

    square_head = grad_head * grad_head + EPS_ROW
    real = lax.broadcasted_iota(jnp.int32, square_head.shape, 0) < classes
    square_head = jnp.where(real, square_head, 0.0)
    head_lanes = pl.ds(edges[2], width)
    old = row_ref[:, head_lanes]
    row = keep * old + (1.0 - keep) * jnp.sum(square_head, axis=0, keepdims=True) / classes
    row_new[:, head_lanes] = row
    diagonal = eye_mask(16, classes)
    old = jnp.broadcast_to(col_ref[:, 3 * width :], (16, classes))
    old = jnp.sum(jnp.where(diagonal, old, 0.0), axis=1, keepdims=True)
    column = keep * old + (1.0 - keep) * jnp.sum(square_head, axis=1, keepdims=True) / width
    col_new[:, 3 * width :] = jnp.sum(
        jnp.where(diagonal, jnp.broadcast_to(column, (16, classes)), 0.0), axis=0, keepdims=True
    )
    real_column = lax.broadcasted_iota(jnp.int32, column.shape, 0) < classes
    column = jnp.where(real_column, column, 1.0)
    mean = jnp.sum(row, axis=1, keepdims=True) / width
    raw = grad_head * (lax.rsqrt(row) * jnp.sqrt(mean)) * lax.rsqrt(column)
    clip = jnp.maximum(1.0, jnp.sqrt(total_of(raw * raw) / (classes * width)))
    head_votes = jnp.tanh(raw / clip)[:classes]

    raws = []
    for k, grad in enumerate((gain_one, shift_one, gain_two, shift_two, gain_side, shift_two)):
        here = pl.ds(k * width, width)
        moment = keep * moment_ref[:, here] + (1.0 - keep) * (grad * grad + EPS_ROW)
        moment_new[:, here] = moment
        raws.append(grad * lax.rsqrt(moment))
    raw = jnp.concatenate(raws, axis=0)
    clip = jnp.maximum(1.0, jnp.sqrt(total_of(raw * raw) / raw.size))
    norm_votes = jnp.tanh(raw / clip)
    copies = exchange_start(
        2,
        jnp.concatenate([head_votes, norm_votes, jnp.broadcast_to(loss, (8, width))], axis=0),
    )


    for b in range(3):
        first, last = (0, side - 1) if b == 0 else (0, side)
        shift = 1 if b == 0 else 0
        for a in range(3):
            left = xs_t[0 if b == 1 else 1, 0 if a == 1 else 1, :, first * band : last * band]
            start = 1 if a == 0 else 0
            right = back_one[first + shift : last + shift, start : start + side]
            grad_one[pl.ds((a * 3 + b) * in_width, in_width), :] = jnp.dot(
                left, right.reshape(-1, width), preferred_element_type=f32
            )
        if b == 0:
            stage[2] = scatter_two(2, stage[2])
        if b == 1:
            copies = exchange_middle(2, copies)
        if b == 2:
            stage[3] = scatter_two(3, stage[3])

    matrix_votes(
        0,
        grad_one,
        (lambda: scatter_three(2, stage[2]), lambda: scatter_three(3, stage[3])),
    )
    stage = {t: scatter_start(t) for t in (1, 0)}

    @pl.when(z >= 2)
    def _():
        own_block()

    gathered = {}
    for t in (1, 0):
        stage[t] = scatter_one(t, stage[t])
    for t in (2, 3):
        gathered[t] = gather_one(t)
    for t in (1, 0):
        stage[t] = scatter_two(t, stage[t])
    for t in (2, 3):
        gathered[t] = gather_two(t, gathered[t])
    for t in (1, 0):
        scatter_three(t, stage[t])
    for t in (2, 3):
        gathered[t] = gather_three(t, gathered[t])

    @pl.when(z < 2)
    def _():
        own_block()

    sums = exchange_end(2, copies)
    loss_ref[...] = sums[TAIL:, :1][:1]
    old = jnp.concatenate([head_ref[...], norm_ref[...]], axis=0)
    is_head = lax.broadcasted_iota(jnp.int32, (TAIL, width), 0) < classes
    scale = jnp.where(is_head, scales[3], scales[4])
    sums = sums[:TAIL]
    fresh = old - scale * jnp.tanh(sums * root)
    both = jnp.concatenate([sums, fresh], axis=0)
    high = both.astype(low)
    rest = both - high.astype(f32)
    middle = rest.astype(low)
    parts = jnp.concatenate([high, middle, (rest - middle.astype(f32)).astype(low)], axis=0)

    for t in (1, 0):
        gathered[t] = gather_one(t)

    flat_sums, flat_new = [], []
    window = 256
    for q in range(classes):
        start = min(q * width // classes // 128 * 128, width - window)
        down = lax.broadcasted_iota(jnp.int32, (window, width), 0)
        across = lax.broadcasted_iota(jnp.int32, (window, width), 1)
        gap = across - classes * down + (q * width - classes * start)
        chosen = jnp.where(jnp.logical_and(gap >= 0, gap < classes), 1.0, 0.0).astype(low)
        moved = jnp.dot(parts[:, start : start + window], chosen, preferred_element_type=f32)
        moved = moved[: 2 * TAIL] + moved[2 * TAIL : 4 * TAIL] + moved[4 * TAIL :]
        spot_of = lax.broadcasted_iota(jnp.int32, (TAIL, width), 1).astype(f32) + q * width
        class_of = spot_of - classes * jnp.floor((spot_of + 0.5) / classes)
        here = lax.broadcasted_iota(jnp.int32, (TAIL, width), 0).astype(f32) == class_of
        flat_sums.append(jnp.sum(jnp.where(here, moved[:TAIL], 0.0), axis=0, keepdims=True))
        flat_new.append(jnp.sum(jnp.where(here, moved[TAIL:], 0.0), axis=0, keepdims=True))
    flat_sums = jnp.concatenate(flat_sums + [sums[classes:]], axis=0)
    flat_new = jnp.concatenate(flat_new + [fresh[classes:]], axis=0)

    for t in (1, 0):
        gathered[t] = gather_two(t, gathered[t])

    halo_copy().wait()

    @pl.when(me < 31)
    def _():
        pltpu.make_async_copy(
            weight.at[pl.ds(OWN, TAIL)], weight.at[pl.ds(OWN, TAIL)], fetch_sem.at[4]
        ).wait()
        total[pl.ds(SPAN, GROUP), :] = halo_in[...]
        renew(OWN, first_row + OWN)

    def tail_rows(values, ref):
        for u in (0, 8):
            for q in range(4):
                flat_rows(OWN + u, q, values[u : u + 8, 128 * q : 128 * (q + 1)], ref)

    @pl.when(me == 31)
    def _():
        tail_rows(flat_sums, vote_flat)
        tail_rows(flat_new, new_flat)

    shift = 2 * me
    share = vote_ref.shape[0]
    vote_ref[...] = vote_flat[pl.ds(shift, share), :]
    new_ref[...] = new_flat[pl.ds(shift, share), :]
    tail_rows(flat_new, new_flat)
    out_ref[pl.ds(32 * SPAN, GROUP), :] = new_flat[pl.ds(SPAN, GROUP), :].astype(low)

    for t in (1, 0):
        gathered[t] = gather_three(t, gathered[t])
    for t in range(4):
        for copy in gathered[t]:
            copy.wait()

        @pl.when(z != t)
        def _():
            line_copy(t, z).wait_send()

    for k in range(3):
        spread_copy(k).wait_send()


def finish_kernel(count, *refs):
    copies = [
        pltpu.make_async_copy(refs[k], refs[count + k], refs[2 * count].at[k])
        for k in range(count)
    ]
    for copy in copies:
        copy.start()
    for copy in copies:
        copy.wait()


def finish(values):
    count = len(values)
    specs = [pl.BlockSpec(memory_space=pl.ANY)] * count
    return pl.pallas_call(
        functools.partial(finish_kernel, count),
        out_shape=[jax.ShapeDtypeStruct(value.shape, value.dtype) for value in values],
        in_specs=specs,
        out_specs=specs,
        scratch_shapes=[pltpu.SemaphoreType.DMA((count,))],
        name="finish",
    )(*values)


def run_step(images, conv_one, conv_two, shortcut, head, norm_params, valid, labels, rows, cols, moment):
    vmem = pl.BlockSpec(memory_space=pltpu.VMEM)
    hbm = pl.BlockSpec(memory_space=pl.ANY)
    low, f32 = jnp.bfloat16, jnp.float32
    dma = pltpu.SemaphoreType.DMA
    workers = lax.axis_size("dp")
    slots, in_width = valid.shape[1], images.shape[1]
    width = conv_one.shape[1]
    pixels = images.shape[0] // 4
    shape = pltpu.VMEM
    edges = [conv_one.shape[0]]
    edges.append(edges[0] + conv_two.shape[0])
    edges.append(edges[1] + shortcut.shape[0])
    flat = (edges[2] + TAIL) * width // 128
    share = flat // workers
    return pl.pallas_call(
        functools.partial(step_kernel, tuple(edges), 1.0 / math.sqrt(workers)),
        out_shape=(
            shape((share, 128), f32),
            shape((share, 128), f32),
            shape((flat, 128), low),
            shape(rows.shape, f32),
            shape(cols.shape, f32),
            shape(moment.shape, f32),
            shape((1, 1), f32),
            shape((1, 1), f32),
        ),
        in_specs=[vmem] + [hbm] * 3 + [vmem] * 7,
        out_specs=(vmem,) * 8,
        scratch_shapes=[
            pltpu.VMEM((2, 4, 2, 4, slots, in_width), low),
            pltpu.VMEM(conv_one.shape, f32),
            pltpu.VMEM(conv_two.shape, f32),
            pltpu.VMEM(shortcut.shape, f32),
            pltpu.VMEM((9, in_width, width), low),
            pltpu.VMEM((9, width, width), low),
            pltpu.VMEM((1, in_width, width), low),
            pltpu.VMEM((pixels, width), f32),
            pltpu.VMEM((pixels, width), f32),
            pltpu.VMEM((pixels, width), f32),
            pltpu.VMEM((4, 6, slots, width), low),
            pltpu.VMEM((4, 6, slots, width), low),
            pltpu.VMEM((4, 5, slots, width), low),
            pltpu.VMEM((pixels, width), low),
            pltpu.VMEM((width, pixels), low),
            pltpu.VMEM((2, 2, in_width, pixels), low),
            pltpu.VMEM((128, width), f32),
            pltpu.VMEM((conv_two.shape[0], 128), f32),
            pltpu.VMEM((8, width), f32),
            pltpu.VMEM((2, 8, width), f32),
            pltpu.VMEM((2, 8, 8, width), f32),
            pltpu.VMEM((2, 4, 8, width), f32),
            pltpu.VMEM((TAIL + 8, width), f32),
            pltpu.VMEM((8, TAIL + 8, width), f32),
            pltpu.VMEM((4, TAIL + 8, width), f32),
            pltpu.VMEM((4, 2, 2, SPAN, 128), low),
            pltpu.VMEM((4, 2, HALF, 128), low),
            pltpu.VMEM((4, 2, HALF, 128), low),
            pltpu.VMEM((4, SPAN, 128), low),
            pltpu.VMEM((4, SPAN, 128), low),
            pltpu.VMEM((GROUP, 128), f32),
            pltpu.VMEM((SPAN + GROUP, 128), f32),
            pltpu.VMEM((OWN + TAIL, width), f32),
            pltpu.VMEM((SPAN + GROUP, 128), f32),
            pltpu.VMEM((SPAN + GROUP, 128), f32),
            dma((5,)),
            dma((3, 10)),
            dma((3, 10)),
            dma((4, 4)),
            dma((4, 4)),
            dma((4, 4)),
            dma((4, 4)),
            dma((4,)),
            dma((4,)),
            dma((2,)),
            dma((11, 4)),
            dma((11, 4)),
            pltpu.SemaphoreType.REGULAR((4,)),
        ],
        compiler_params=pltpu.CompilerParams(
            collective_id=1, has_side_effects=True, vmem_limit_bytes=54 * 1024 * 1024
        ),
        name="step",
    )(images, conv_one, conv_two, shortcut, head, norm_params, valid, labels, rows, cols, moment)


def scale_for(weight):
    return jnp.maximum(EPS_SCALE, jnp.sqrt(jnp.mean(weight * weight)))


def local_general(
    images,
    valid_slot,
    labels,
    conv_one,
    conv_two,
    shortcut,
    classifier,
    norm_params,
    row_state,
    col_state,
    bn_moment,
):
    in_width = images.shape[3]
    width = conv_one.shape[1]
    kernel_one = conv_one.astype(jnp.bfloat16).reshape(3, 3, in_width, width)
    kernel_two = conv_two.astype(jnp.bfloat16).reshape(3, 3, width, width)
    kernel_short = shortcut.astype(jnp.bfloat16).reshape(1, 1, in_width, width)
    head_low = classifier.astype(jnp.bfloat16)
    slot_count = images.shape[0]
    out_side = images.shape[1] // 2
    pixel_count = out_side * out_side
    slot_weight = valid_slot.astype(jnp.float32)
    pixel_weight = jnp.broadcast_to(slot_weight[:, None], (slot_count, pixel_count)).reshape(-1, 1)
    main_pre, side_pre = first_section(images, kernel_one, kernel_short)
    main_sums = masked_moments(pixel_weight, main_pre)
    side_sums = masked_moments(pixel_weight, side_pre)
    count_row = jnp.broadcast_to(jnp.sum(slot_weight), (width,))
    first_sums = lax.psum(jnp.stack([*main_sums, *side_sums, count_row]), "dp")
    valid_count = first_sums[4, 0]
    denominator = jnp.maximum(valid_count, 1.0)
    pixels = denominator * pixel_count
    norm_one = settle(first_sums[0], first_sums[1], pixels)
    norm_side = settle(first_sums[2], first_sums[3], pixels)
    hidden_one, active, main_two = second_section(
        main_pre, norm_one, norm_params, kernel_two, slot_count, out_side
    )
    two_sums = masked_moments(pixel_weight, main_two)
    second_sums = lax.psum(jnp.stack([*two_sums]), "dp")
    norm_two = settle(second_sums[0], second_sums[1], pixels)
    joined_pre = (
        (main_two - norm_two[0]) * norm_two[1] * norm_params[2]
        + norm_params[3]
        + (side_pre - norm_side[0]) * norm_side[1] * norm_params[4]
        + norm_params[5]
    )
    joined = jax.nn.silu(joined_pre).reshape(slot_count, pixel_count, -1)
    pooled = jnp.mean(joined, axis=1).astype(jnp.bfloat16)
    logits = jnp.dot(pooled, head_low, preferred_element_type=jnp.float32)
    largest = jnp.max(logits, axis=1, keepdims=True)
    exp_terms = jnp.exp(logits - largest)
    total_exp = jnp.sum(exp_terms, axis=1, keepdims=True)
    log_total = largest[:, 0] + jnp.log(total_exp[:, 0])
    onehot = (labels[:, None] == jnp.arange(logits.shape[1], dtype=jnp.int32)[None, :]).astype(
        jnp.float32
    )
    local_sum = jnp.sum(slot_weight * (log_total - jnp.sum(onehot * logits, axis=1)))
    grad_logits = ((exp_terms / total_exp - onehot) * (slot_weight / denominator)[:, None]).astype(
        jnp.bfloat16
    )
    grad_head = lax.dot_general(
        pooled, grad_logits, (((0,), (0,)), ((), ())), preferred_element_type=jnp.float32
    )
    grad_pooled = lax.dot_general(
        grad_logits, head_low, (((1,), (1,)), ((), ())), preferred_element_type=jnp.float32
    )
    spread_pooled = jnp.broadcast_to(
        (grad_pooled / pixel_count)[:, None, :], (slot_count, pixel_count, width)
    )
    grad_joined = spread_pooled.reshape(slot_count * pixel_count, width) * silu_slope(joined_pre)
    gain_two, shift_two, grad_two = norm_backward(grad_joined, main_two, norm_two, norm_params[2])
    gain_side, shift_side, grad_side = norm_backward(
        grad_joined, side_pre, norm_side, norm_params[4]
    )
    grad_two_maps = grad_two.reshape(slot_count, out_side, out_side, width)
    grad_side_maps = grad_side.reshape(slot_count, out_side, out_side, width)
    grad_conv_two = conv_weight_grad(active, grad_two_maps, 1, 1, 1)
    grad_short = conv_weight_grad(images, grad_side_maps, 2, 0, -1)
    kernel_turned = jnp.transpose(kernel_two[::-1, ::-1], (0, 1, 3, 2))
    grad_active = conv_apply(grad_two_maps, kernel_turned, 1, 1).reshape(
        slot_count * pixel_count, width
    )
    grad_hidden = grad_active * silu_slope(hidden_one)
    gain_one, shift_one, grad_one = norm_backward(grad_hidden, main_pre, norm_one, norm_params[0])
    grad_conv_one = conv_weight_grad(
        images, grad_one.reshape(slot_count, out_side, out_side, width), 2, 1, 0
    )
    grad_norms = jnp.stack([gain_one, shift_one, gain_two, shift_two, gain_side, shift_side])
    grads = (grad_conv_one, grad_conv_two, grad_short, grad_head, grad_norms)
    votes, rows_new, cols_new, moment_new = make_votes(
        grads, row_state[0], col_state[0], bn_moment[0]
    )
    workers = lax.axis_size("dp")
    weights = (conv_one, conv_two, shortcut, classifier, norm_params)
    scales = [scale_for(weight) for weight in weights]
    loss_sum = lax.psum(local_sum, "dp")
    flat_vote = jnp.concatenate([vote.reshape(-1) for vote in votes])
    flat_old = jnp.concatenate([weight.reshape(-1) for weight in weights])
    flat_scale = jnp.concatenate(
        [
            jnp.broadcast_to(scale, (weight.size,))
            for scale, weight in zip(scales, weights)
        ]
    )
    vote_mine = lax.psum_scatter(flat_vote, "dp", tiled=True)
    share = vote_mine.shape[0]
    start = lax.axis_index("dp") * share
    new_mine = lax.dynamic_slice_in_dim(
        flat_old, start, share
    ) - lax.dynamic_slice_in_dim(flat_scale, start, share) * jnp.tanh(
        vote_mine / math.sqrt(workers)
    )
    copies = lax.all_gather(new_mine.astype(jnp.bfloat16), "dp", tiled=True)
    return (
        loss_sum,
        valid_count,
        new_mine,
        copies,
        vote_mine,
        rows_new[None, :],
        cols_new[None, :],
        moment_new[None, :],
    )


def local(
    images,
    valid_slot,
    labels,
    conv_one,
    conv_two,
    shortcut,
    classifier,
    norm_params,
    row_state,
    col_state,
    bn_moment,
):
    new_mine, vote_mine, copies, rows_new, cols_new, moment_new, loss_sum, valid_count = run_step(
        images.reshape(-1, images.shape[-1]),
        conv_one,
        conv_two,
        shortcut,
        classifier.T,
        norm_params,
        valid_slot.reshape(1, -1),
        labels.reshape(1, -1),
        row_state,
        col_state,
        bn_moment,
    )
    copies, new_mine, vote_mine, rows_new, cols_new, moment_new, loss_sum, valid_count = finish(
        (copies, new_mine, vote_mine, rows_new, cols_new, moment_new, loss_sum, valid_count)
    )
    return (
        loss_sum.reshape(()),
        valid_count.reshape(()),
        new_mine.reshape(-1),
        copies.reshape(-1),
        vote_mine.reshape(-1),
        rows_new,
        cols_new,
        moment_new,
    )


def solution(mesh):
    placed = (
        P("dp", None, None, None),
        P("dp"),
        P("dp"),
        P(),
        P(),
        P(),
        P(),
        P(),
        P("dp", None),
        P("dp", None),
        P("dp", None),
    )
    return jax.shard_map(
        local if mesh.shape["dp"] == 32 else local_general,
        mesh=mesh,
        in_specs=placed,
        out_specs=(P(), P(), P("dp"), P(), P("dp"), P("dp", None), P("dp", None), P("dp", None)),
        check_vma=False,
    )
```

```python
import functools
import math

import jax
import jax.numpy as jnp
from jax import lax
from jax.experimental import pallas as pl
from jax.experimental.pallas import tpu as pltpu
from jax.sharding import PartitionSpec as P

STEP = 10
MESH = pl.DeviceIdType.MESH

EPS_NORM = 1e-05
EPS_ROW = 1e-30
EPS_SCALE = 0.001
FORWARD_DIMS = ("NHWC", "HWIO", "NHWC")
WEIGHT_DIMS = ("CHWN", "IHWO", "HWNC")
OWN = 224
TAIL = 16
PIECE = 32
SPAN = 4 * OWN
HALF = SPAN // 2
GROUP = 64


def conv_apply(maps, kernel, stride, margin):
    return lax.conv_general_dilated(
        maps,
        kernel,
        (stride, stride),
        ((margin, margin), (margin, margin)),
        dimension_numbers=FORWARD_DIMS,
        preferred_element_type=jnp.float32,
    )


def conv_weight_grad(maps, grad_out, stride, low_pad, high_pad):
    result = lax.conv_general_dilated(
        maps,
        grad_out,
        (1, 1),
        ((low_pad, high_pad), (low_pad, high_pad)),
        rhs_dilation=(stride, stride),
        dimension_numbers=WEIGHT_DIMS,
        preferred_element_type=jnp.float32,
    )
    return result.reshape(-1, result.shape[3])


def silu_slope(values):
    sigmoid_part = jax.nn.sigmoid(values)
    return sigmoid_part * (1.0 + values * (1.0 - sigmoid_part))


def settle(sum_plain, sum_square, pixels):
    mean_value = sum_plain / pixels
    return (mean_value, lax.rsqrt(sum_square / pixels - mean_value * mean_value + EPS_NORM))


def first_section(images, kernel_one, kernel_short):
    row_count = images.shape[0] * (images.shape[1] // 2) ** 2
    main_pre = conv_apply(images, kernel_one, 2, 1).reshape(row_count, -1)
    side_pre = conv_apply(images, kernel_short, 2, 0).reshape(row_count, -1)
    return (main_pre, side_pre)


def second_section(main_pre, norm_one, norm_params, kernel_two, slot_count, out_side):
    hidden_one = (main_pre - norm_one[0]) * norm_one[1] * norm_params[0] + norm_params[1]
    active = (
        jax.nn.silu(hidden_one).astype(jnp.bfloat16).reshape(slot_count, out_side, out_side, -1)
    )
    main_two = conv_apply(active, kernel_two, 1, 1).reshape(slot_count * out_side * out_side, -1)
    return (hidden_one, active, main_two)


def masked_moments(pixel_weight, values):
    return (jnp.sum(pixel_weight * values, axis=0), jnp.sum(pixel_weight * values * values, axis=0))


def soft_sign(step_raw):
    clip_by = jnp.maximum(1.0, jnp.sqrt(jnp.mean(step_raw * step_raw)))
    return jnp.tanh(step_raw / clip_by)


def make_votes(grads, rows_old, cols_old, moment_old):
    decay_rate = 1.0 - STEP ** (-0.8)
    votes, rows_new, cols_new = ([], [], [])
    row_at, col_at = (0, 0)
    for matrix in grads[:4]:
        row_size, col_size = matrix.shape
        square = matrix * matrix + EPS_ROW
        row_part = decay_rate * rows_old[row_at : row_at + row_size] + (
            1.0 - decay_rate
        ) * jnp.mean(square, axis=1)
        col_part = decay_rate * cols_old[col_at : col_at + col_size] + (
            1.0 - decay_rate
        ) * jnp.mean(square, axis=0)
        second = row_part[:, None] * col_part[None, :] / jnp.mean(row_part)
        votes.append(soft_sign(matrix * lax.rsqrt(second)))
        rows_new.append(row_part)
        cols_new.append(col_part)
        row_at += row_size
        col_at += col_size
    flat_norm = grads[4].reshape(-1)
    moment_new = decay_rate * moment_old + (1.0 - decay_rate) * (flat_norm * flat_norm + EPS_ROW)
    votes.append(soft_sign(flat_norm * lax.rsqrt(moment_new)))
    return (votes, jnp.concatenate(rows_new), jnp.concatenate(cols_new), moment_new)


def norm_backward(grad_out, pre_value, norm_pair, gain_row):
    normed = (pre_value - norm_pair[0]) * norm_pair[1]
    grad_gain = jnp.sum(grad_out * normed, axis=0)
    grad_shift = jnp.sum(grad_out, axis=0)
    grad_pre = (grad_out * gain_row * norm_pair[1]).astype(jnp.bfloat16)
    return (grad_gain, grad_shift, grad_pre)


def place():
    me = lax.axis_index("dp")
    core = lax.rem(me, 2)
    x = lax.rem(lax.div(me, 2), 2)
    y = lax.rem(lax.div(me, 4), 2)
    z = lax.div(me, 8)
    return me, core, x, y, z


def send(src, dst, send_sem, recv_sem, partner):
    copy = pltpu.make_async_remote_copy(
        src_ref=src,
        dst_ref=dst,
        send_sem=send_sem,
        recv_sem=recv_sem,
        device_id=(partner,),
        device_id_type=MESH,
    )
    copy.start()
    return copy


def scale_of(row, scales, edges):
    picked = scales[2]
    picked = jnp.where(row < edges[1], scales[1], picked)
    return jnp.where(row < edges[0], scales[0], picked)


def make_units(edges):
    one, two, short = edges[0] // 16, edges[1] // 16, edges[2] // 16
    units = []
    at = one
    for size, x_first in ((2, True), (2, False), (2, True), (3, False)):
        units.append((at, size, x_first, 16 * size, (1, 1)))
        at += 32 * size
    assert at == two
    at = 0
    for size, x_first in ((2, True), (2, False)):
        units.append((at, size, x_first, 16 * size, (0, 0)))
        at += 32 * size
    assert one - at == 16 and short - two == 16
    units.append((at, 1, True, two - at, (0, 2)))
    return units


def settle_rows(sums, pixels, gain, shift):
    mean = sums[0] / pixels
    inv = lax.rsqrt(sums[1] / pixels - mean * mean + EPS_NORM)
    slope = gain * inv
    return mean, inv, slope, shift - mean * slope


def gate(values):
    return 0.5 * jnp.tanh(0.5 * values) + 0.5


def eye_mask(rows, columns, offset=0):
    down = lax.broadcasted_iota(jnp.int32, (rows, columns), 0) + offset
    return down == lax.broadcasted_iota(jnp.int32, (rows, columns), 1)


def column_of(row, size):
    spread = jnp.where(eye_mask(size, size), jnp.broadcast_to(row, (size, size)), 0)
    return jnp.sum(spread, axis=1, keepdims=True)


def total_of(values):
    return jnp.sum(jnp.sum(values, axis=0, keepdims=True), axis=1, keepdims=True)


def fold(values):
    return jnp.sum(values.reshape(values.shape[0] // 8, 8, values.shape[1]), axis=0)


def cast_weight(source, target, square_ref, taps, depth):
    step = 128
    square_ref[...] = jnp.zeros_like(square_ref)
    for tap in range(taps):
        new_tap = (tap % 3) * 3 + tap // 3

        @pl.loop(0, depth // step)
        def _(k):
            start = pl.multiple_of(k * step, step)
            values = source[pl.ds(tap * depth + start, step), :]
            target[new_tap, pl.ds(start, step), :] = values.astype(jnp.bfloat16)
            square_ref[...] += fold(values * values)


def factored_votes(grad, rows, row_at, rows_old, rows_new, col_old, level, votes, vote_at, between):
    width = grad.shape[1]
    keep = 1.0 - STEP ** (-0.8)
    step = 128
    quarters = width // 128

    def first(k, carry):
        col_sum, row_sum = carry
        start = pl.multiple_of(k * step, step)
        lanes = pl.ds(pl.multiple_of(row_at + start, step), step)
        old = rows_old[:, lanes] * keep
        line = jnp.zeros((8, 128), jnp.float32)
        for m in range(step // 8):
            block = grad[pl.ds(start + 8 * m, 8), :]
            square = block * block
            col_sum = col_sum + square
            part = square[:, :128]
            for q in range(1, quarters):
                part = part + square[:, 128 * q : 128 * (q + 1)]
            part = part * ((1.0 - keep) / width)
            diagonal = eye_mask(8, 128, 8 * m)
            part = part + jnp.where(diagonal, jnp.broadcast_to(old, (8, 128)), 0.0)
            row = jnp.sum(part, axis=1, keepdims=True) + (1.0 - keep) * EPS_ROW
            row = jnp.broadcast_to(row, (8, 128))
            level[pl.ds(start + 8 * m, 8), :] = row
            row_sum = row_sum + row
            line = line + jnp.where(diagonal, row, 0.0)
        rows_new[:, lanes] = jnp.sum(line, axis=0, keepdims=True)
        return col_sum, row_sum

    col_sum, row_sum = lax.fori_loop(
        0,
        rows // step,
        first,
        (jnp.zeros((8, width), jnp.float32), jnp.zeros((8, 128), jnp.float32)),
    )
    col_new = keep * col_old + (1.0 - keep) * (
        jnp.sum(col_sum, axis=0, keepdims=True) / rows + EPS_ROW
    )
    scale = lax.rsqrt(col_new)
    root_mean = jnp.sqrt(jnp.sum(row_sum, axis=0, keepdims=True) / rows)

    def second(k, carry):
        start = pl.multiple_of(k * step, step)
        for m in range(step // 8):
            here = pl.ds(start + 8 * m, 8)
            factor = lax.rsqrt(level[here, :]) * root_mean
            level[here, :] = factor
            raw = grad[here, :] * scale
            power = raw * raw
            part = power[:, :128]
            for q in range(1, quarters):
                part = part + power[:, 128 * q : 128 * (q + 1)]
            carry = carry + part * (factor * factor)
        return carry

    between[0]()
    power = lax.fori_loop(0, rows // step, second, jnp.zeros((8, 128), jnp.float32))
    between[1]()
    clip = jnp.maximum(1.0, jnp.sqrt(total_of(power) / (rows * width)))
    scale = scale / clip

    def third(k, _):
        start = pl.multiple_of(k * step, step)
        for m in range(step // 16):
            here = pl.ds(start + 16 * m, 16)
            factor = level[here, :]
            factor = jnp.concatenate([factor] * quarters, axis=1)
            vote = jnp.tanh(grad[here, :] * factor * scale)
            vote = vote.astype(jnp.bfloat16)
            at = pl.multiple_of((vote_at + start) * 4 + GROUP * m, GROUP)
            for q in range(quarters):
                votes[pl.ds(at + 16 * q, 16), :] = vote[:, 128 * q : 128 * (q + 1)]
        return 0

    lax.fori_loop(0, rows // step, third, 0)
    return col_new


def step_kernel(
    edges,
    units,
    root,
    images,
    one_hbm,
    two_hbm,
    short_hbm,
    head_ref,
    norm_ref,
    valid_ref,
    label_ref,
    row_ref,
    col_ref,
    moment_ref,
    new_ref,
    vote_ref,
    out_ref,
    row_new,
    col_new,
    moment_new,
    loss_ref,
    count_ref,
    xs,
    grad_one,
    grad_two,
    grad_short,
    low_one,
    low_two,
    low_short,
    main_pre,
    side_pre,
    main_two,
    active,
    back_two,
    back_one,
    back_side,
    active_t,
    xs_t,
    head_pad,
    level,
    square,
    post,
    plane,
    line,
    tail_post,
    tail_plane,
    tail_line,
    core_in,
    wide_in,
    deep_in,
    line_in,
    sum_low,
    landed,
    total,
    own_weight,
    weight,
    vote_flat,
    new_flat,
    fetch_sem,
    small_send,
    small_recv,
    rs_send,
    rs_recv,
    line_send,
    line_recv,
    pass_send,
    land_recv,
    spread_send,
    spread_recv,
    ag_send,
    ag_recv,
    free_sem,
    load_sem,
):
    slots, in_width = xs.shape[4:]
    width = main_pre.shape[1]
    side = 4
    band = side * slots
    pixel_count = side * side
    classes = head_ref.shape[0]
    keep = 1.0 - STEP ** (-0.8)
    low = jnp.bfloat16
    f32 = jnp.float32

    me, core, x, y, z = place()
    flip_core = me + 1 - 2 * core
    flip_x = me + 2 - 4 * x
    flip_y = me + 4 - 8 * y
    spot = lax.rem(me, 8)
    near = [z * 8 + lax.rem(spot + k, 8) for k in range(1, 8)]
    far = [lax.rem(z + k, 4) * 8 + spot for k in range(1, 4)]
    others = [lax.rem(me + k, 32) for k in range(1, 32)]

    count = images.shape[0]
    loads = []
    for half in range(2):
        lanes = slice(128 * half, 128 * (half + 1))
        loads.append(
            pltpu.make_async_copy(
                images.at[:, lanes], core_in.at[pl.ds(half * count, count)], load_sem.at[half]
            )
        )
        loads[half].start()

    fetches = [
        pltpu.make_async_copy(source, target, fetch_sem.at[k])
        for k, (source, target) in enumerate(
            ((one_hbm, grad_one), (short_hbm, grad_short), (two_hbm, grad_two))
        )
    ]
    for fetch in fetches:
        fetch.start()
    barrier = pltpu.get_barrier_semaphore()
    for partner in others:
        pl.semaphore_signal(barrier, inc=1, device_id=(partner,), device_id_type=MESH)

    def fetch_rows(row, count, place_at, sem):
        parts = (
            (one_hbm, 0, edges[0]),
            (two_hbm, edges[0], edges[1]),
            (short_hbm, edges[1], edges[2]),
        )
        for ref, first, last in parts:

            @pl.when(jnp.logical_and(row >= first, row < last))
            def _():
                start = pl.multiple_of(row - first, count)
                pltpu.make_async_copy(
                    ref.at[pl.ds(start, count)], weight.at[pl.ds(place_at, count)], sem
                ).start()

    first_row = me * OWN
    for k in range(OWN // PIECE):
        fetch_rows(first_row + k * PIECE, PIECE, k * PIECE, fetch_sem.at[3])
    fetch_rows(first_row + OWN, TAIL, OWN, fetch_sem.at[4])

    for half in range(2):
        lanes = slice(128 * half, 128 * (half + 1))
        loads[half].wait()
        level[:count, :] = core_in[pl.ds(half * count, count), :].astype(f32)
        for h in range(2 * side):
            for w in range(2 * side):
                rows = level[pl.ds(2 * side * h + w, slots, stride=4 * pixel_count), :]
                xs[w % 2, w // 2, h % 2, h // 2, :, lanes] = rows.astype(low)

    scales = {}

    def scale_from(weight_square, size):
        return jnp.maximum(EPS_SCALE, jnp.sqrt(total_of(weight_square) / size))

    exchanges = (
        (post.at[0], plane.at[0], line.at[0]),
        (post.at[1], plane.at[1], line.at[1]),
        (tail_post, tail_plane, tail_line),
    )

    def exchange_start(which, values):
        mine_ref, plane_ref, _ = exchanges[which]
        mine_ref[...] = values
        plane_ref[spot] = values
        return [
            send(
                mine_ref,
                plane_ref.at[spot],
                small_send.at[which, k],
                small_recv.at[which, k],
                partner,
            )
            for k, partner in enumerate(near)
        ]

    def exchange_middle(which, copies):
        _, plane_ref, line_ref = exchanges[which]
        for copy in copies:
            copy.wait()
        line_ref[z] = functools.reduce(lambda a, b: a + b, [plane_ref[k] for k in range(8)])
        return [
            send(
                line_ref.at[z],
                line_ref.at[z],
                small_send.at[which, 7 + k],
                small_recv.at[which, 7 + k],
                partner,
            )
            for k, partner in enumerate(far)
        ]

    def exchange_end(which, copies):
        line_ref = exchanges[which][2]
        for copy in copies:
            copy.wait()
        return (line_ref[0] + line_ref[1]) + (line_ref[2] + line_ref[3])

    def lines(start, count):
        return pl.ds(pl.multiple_of(start, 16), count)

    sizes = [GROUP * unit[1] for unit in units]
    starts = [sum(sizes[:k]) for k in range(len(units) + 1)]

    def part_of(ref, u, share, start, count):
        return ref.at[lines(share * starts[u] + start, count)]

    def places(u):
        if units[u][2]:
            return x, y, flip_x, flip_y
        return y, x, flip_y, flip_x

    def unit_start(u, cc):
        return GROUP * units[u][0] + cc * (GROUP * units[u][3])

    def own_group(u):
        first, second, _, _ = places(u)
        return units[u][0] + core * units[u][3] + (first * 8 + second * 4 + z) * units[u][1]

    def halve(source, target, u, stage, partner):
        return send(source, target, rs_send.at[u, stage], rs_recv.at[u, stage], partner)

    def scatter_start(u):
        size = 16 * sizes[u]
        return halve(
            out_ref.at[lines(unit_start(u, 1 - core), size)],
            part_of(core_in, u, 16, 0, size),
            u,
            0,
            flip_core,
        )

    def add_to(ref, u, share, source_ref, source_start):
        size = share * sizes[u]
        here = lines(share * starts[u], size)
        ref[here, :] = ref[here, :] + source_ref[lines(source_start, size), :]

    def scatter_one(u, copy):
        copy.wait()
        add_to(core_in, u, 16, out_ref, unit_start(u, core))
        pl.semaphore_signal(
            free_sem.at[u], inc=1, device_id=(flip_core,), device_id_type=MESH
        )
        first, _, flip_first, _ = places(u)
        size = 8 * sizes[u]
        return halve(
            part_of(core_in, u, 16, (1 - first) * size, size),
            part_of(wide_in, u, 8, 0, size),
            u,
            1,
            flip_first,
        )

    def scatter_two(u, copy):
        copy.wait()
        first, second, _, flip_second = places(u)
        add_to(wide_in, u, 8, core_in, 16 * starts[u] + first * 8 * sizes[u])
        size = 4 * sizes[u]
        return halve(
            part_of(wide_in, u, 8, (1 - second) * size, size),
            part_of(deep_in, u, 4, 0, size),
            u,
            2,
            flip_second,
        )

    def line_copy(u, k):
        plane_to = lax.rem(z + k, 4)
        return pltpu.make_async_remote_copy(
            src_ref=part_of(deep_in, u, 4, plane_to * sizes[u], sizes[u]),
            dst_ref=part_of(line_in, u, 4, z * sizes[u], sizes[u]),
            send_sem=line_send.at[u, k],
            recv_sem=line_recv.at[u, k],
            device_id=(plane_to * 8 + spot,),
            device_id_type=MESH,
        )

    def scatter_three(u, copy):
        copy.wait()
        _, second, _, _ = places(u)
        add_to(deep_in, u, 4, wide_in, 8 * starts[u] + second * 4 * sizes[u])
        for k in (3, 2, 1):
            line_copy(u, k).start()
        here = lines(4 * starts[u] + z * sizes[u], sizes[u])
        line_in[here, :] = deep_in[here, :]

    groups = (edges[2] + TAIL) // 16
    spare = (groups - 1) // 32
    passes = []

    def land(local, group, to, slot, index):
        source = sum_low.at[lines(local * GROUP, GROUP)]
        target = landed.at[lines(slot * GROUP, GROUP)]
        copy = pltpu.make_async_remote_copy(
            src_ref=source,
            dst_ref=target,
            send_sem=pass_send.at[index],
            recv_sem=land_recv.at[slot],
            device_id=(to,),
            device_id_type=MESH,
        )
        return copy, source, target

    def pass_on(u):
        for m in range(units[u][1]):
            local = starts[u] // GROUP + m
            group = own_group(u) + m
            to, slot = lax.div(group, spare), lax.rem(group, spare)
            for halo in range(2):
                index = 2 * local + halo
                if halo:
                    receiver, at = lax.rem(to + 31, 32), spare
                    wanted = jnp.logical_and(slot == 0, group > 0)
                else:
                    receiver, at, wanted = to, slot, group >= 0
                away = jnp.logical_and(wanted, receiver != me)
                here = jnp.logical_and(wanted, receiver == me)
                copy, source, target = land(local, group, receiver, at, index)

                @pl.when(away)
                def _():
                    copy.start()

                @pl.when(here)
                def _():
                    target[...] = source[...]

                passes.append((away, copy))

    def flat_rows(row, q, values, ref):
        ref[pl.ds(row * 4 + q, 8, stride=4), :] = values

    def old_rows(u, cc):
        matrix = units[u][4][cc]
        base = edges[matrix - 1] if matrix else 0
        return (one_hbm, two_hbm, short_hbm)[matrix], 16 * own_group(u) - base, 16 * units[u][1]

    def own_fetch(u):
        target = own_weight.at[pl.ds(starts[u] // 4, 16 * units[u][1])]
        matrices = units[u][4]
        for cc in range(2):
            if cc and matrices[0] == matrices[1]:
                continue

            @pl.when((core == cc) if matrices[0] != matrices[1] else (core >= 0))
            def _():
                ref, row, count = old_rows(u, cc)
                pltpu.make_async_copy(
                    ref.at[pl.ds(pl.multiple_of(row, 16), count)], target, fetch_sem.at[5 + u]
                ).start()

    for u in range(len(units)):
        own_fetch(u)

    def spread_copy(u, k):
        own = out_ref.at[lines(own_group(u) * GROUP, sizes[u])]
        return pltpu.make_async_remote_copy(
            src_ref=own,
            dst_ref=own,
            send_sem=spread_send.at[u, k],
            recv_sem=spread_recv.at[u, k],
            device_id=(far[k - 1],),
            device_id_type=MESH,
        )

    def own_block(u):
        size = sizes[u]
        for k in range(1, 4):
            line_copy(u, k).wait_recv()
        here = pl.ds(starts[u], size)
        low_sum = functools.reduce(
            lambda a, b: a + b,
            [line_in[pl.ds(4 * starts[u] + t * size, size), :].astype(f32) for t in range(4)],
        ).astype(low)
        sum_low[here, :] = low_sum
        total[here, :] = low_sum.astype(f32)
        target = own_weight.at[pl.ds(starts[u] // 4, 16 * units[u][1])]
        pltpu.make_async_copy(target, target, fetch_sem.at[5 + u]).wait()
        matrices = units[u][4]
        scale = jnp.where(core == 0, scales[matrices[0]], scales[matrices[1]])
        for m in range(units[u][1]):
            row = starts[u] // 4 + 16 * m
            for part in (0, 8):
                for q in range(4):
                    summed = total[pl.ds(row * 4 + 16 * q + part, 8), :]
                    old = own_weight[pl.ds(row + part, 8), 128 * q : 128 * (q + 1)]
                    fresh = old - scale * jnp.tanh(summed * root)
                    flat_rows(row + part, q, fresh, new_flat)
        out_ref[lines(own_group(u) * GROUP, size), :] = new_flat[here, :].astype(low)
        for k in (3, 2, 1):
            spread_copy(u, k).start()
        pass_on(u)

    def piece(rows, u, stage, partner):
        return send(
            out_ref.at[rows], out_ref.at[rows], ag_send.at[u, stage], ag_recv.at[u, stage], partner
        )

    def gather_one(u):
        for k in range(1, 4):
            spread_copy(u, k).wait_recv()
        first, second, _, flip_second = places(u)
        size = 4 * sizes[u]
        start = unit_start(u, core) + (2 * first + second) * size
        return piece(lines(start, size), u, 0, flip_second)

    def gather_two(u, copy):
        copy.wait()
        first, _, flip_first, _ = places(u)
        size = 8 * sizes[u]
        return piece(lines(unit_start(u, core) + first * size, size), u, 1, flip_first)

    def gather_three(u, copy):
        copy.wait()
        pl.semaphore_wait(free_sem.at[u], 1)
        return piece(lines(unit_start(u, core), 16 * sizes[u]), u, 2, flip_core)

    def renew(row, at_row):
        scale = scale_of(at_row, [scales[k] for k in range(3)], edges)
        for part in (0, 8):
            for q in range(4):
                summed = total[pl.ds(row * 4 + 16 * q + part, 8), :]
                old = weight[pl.ds(row + part, 8), 128 * q : 128 * (q + 1)]
                fresh = old - scale * jnp.tanh(summed * root)
                flat_rows(row + part, q, summed, vote_flat)
                flat_rows(row + part, q, fresh, new_flat)

    valid_column = column_of(valid_ref[...].astype(f32), slots)
    weight_slot = jnp.broadcast_to(valid_column, (slots, width))
    weight_band = jnp.concatenate([weight_slot] * side, axis=0)

    fetches[0].wait()
    cast_weight(grad_one, low_one, square, 9, in_width)
    scales[0] = scale_from(square[...], grad_one.size)
    fetches[1].wait()
    cast_weight(grad_short, low_short, square, 1, in_width)
    scales[2] = scale_from(square[...], grad_short.size)

    def image_taps(j):
        pieces = []
        for b in range(3):
            column = j if b else j - 1
            if column < 0:
                continue
            across = 0 if b == 1 else 1
            for a in range(3):
                if a == 1:
                    piece = xs[across, column, 0].reshape(band, in_width)
                elif a == 2:
                    piece = xs[across, column, 1].reshape(band, in_width)
                else:
                    piece = xs[across, column, 1, : side - 1].reshape(band - slots, in_width)
                    piece = jnp.concatenate([jnp.zeros((slots, in_width), low), piece], axis=0)
                pieces.append(piece)
        return jnp.concatenate(pieces, axis=1)

    def moments(values):
        weighted = values * weight_band
        return (
            jnp.sum(weighted, axis=0, keepdims=True),
            jnp.sum(weighted * values, axis=0, keepdims=True),
        )

    def add_up(old, new):
        return [a + b for a, b in zip(old, new)]

    none = jnp.zeros((1, width), f32)
    main_sums, side_sums = [none, none], [none, none]
    for j in range(side):
        here = pl.ds(j * band, band)
        low_rows = low_one[3 if j == 0 else 0 :].reshape(-1, width)
        value = jnp.dot(image_taps(j), low_rows, preferred_element_type=f32)
        main_pre[here, :] = value
        main_sums = add_up(main_sums, moments(value))
        value = jnp.dot(
            xs[0, j, 0].reshape(band, in_width), low_short[0], preferred_element_type=f32
        )
        side_pre[here, :] = value
        side_sums = add_up(side_sums, moments(value))

    count = jnp.broadcast_to(jnp.sum(valid_column, axis=0, keepdims=True), (1, width))
    pl.semaphore_wait(barrier, len(others))
    copies = exchange_start(
        0, jnp.concatenate(main_sums + side_sums + [count, none, none, none], axis=0)
    )
    fetches[2].wait()
    cast_weight(grad_two, low_two, square, 9, width)
    scales[1] = scale_from(square[...], grad_two.size)
    copies = exchange_middle(0, copies)
    for across in range(2):
        for down in range(2):
            for j in range(side):
                block = xs[across, j, down].reshape(band, in_width)
                xs_t[across, down, :, j * band : (j + 1) * band] = block.T
    border = jnp.zeros((side, 1, slots, width), low)
    active[:, 0:1] = border
    active[:, side + 1 :] = border
    back_two[:, 0:1] = border
    back_two[:, side + 1 :] = border
    back_one[:, side:] = border
    head_pad[...] = jnp.zeros_like(head_pad)
    head_pad[:classes, :] = head_ref[...]
    head = head_pad[:16, :]
    scales[3] = scale_from(head * head, head_ref.size)
    params = norm_ref[...]
    scales[4] = scale_from(params * params, norm_ref.size)
    sums = exchange_end(0, copies)

    valid_count = sums[4:5]
    count_ref[...] = valid_count[:, :1]
    denominator = jnp.maximum(valid_count, 1.0)
    pixels = denominator * pixel_count
    gains = [norm_ref[k : k + 1, :] for k in range(6)]
    mean_one, inv_one, slope_one, base_one = settle_rows(
        (sums[0:1], sums[1:2]), pixels, gains[0], gains[1]
    )
    mean_side, inv_side, slope_side, base_side = settle_rows(
        (sums[2:3], sums[3:4]), pixels, gains[4], gains[5]
    )

    for j in range(side):
        hidden = main_pre[pl.ds(j * band, band), :] * slope_one + base_one
        active[j, 1 : side + 1] = (
            (hidden * gate(hidden)).astype(low).reshape(side, slots, width)
        )
    two_sums = [none, none]
    for j in range(side):
        taps = [b for b in range(3) if 0 <= j + b - 1 < side]
        pieces = [
            active[j + b - 1, a : a + side].reshape(band, width) for b in taps for a in range(3)
        ]
        low_rows = low_two[3 * taps[0] : 3 * taps[-1] + 3].reshape(-1, width)
        value = jnp.dot(jnp.concatenate(pieces, axis=1), low_rows, preferred_element_type=f32)
        main_two[pl.ds(j * band, band), :] = value
        two_sums = add_up(two_sums, moments(value))
    copies = exchange_start(1, jnp.concatenate(two_sums + [none] * 6, axis=0))
    for j in range(side):
        block = active[j, 1 : side + 1].reshape(band, width)
        active_t[:, j * band : (j + 1) * band] = block.T
    copies = exchange_middle(1, copies)
    sums = exchange_end(1, copies)
    mean_two, inv_two, slope_two, base_two = settle_rows(
        (sums[0:1], sums[1:2]), pixels, gains[2], gains[3]
    )

    base_joined = base_two + base_side

    def joined_of(here):
        return main_two[here, :] * slope_two + side_pre[here, :] * slope_side + base_joined

    pooled = jnp.zeros((slots, width), f32)
    for p in range(pixel_count):
        joined = joined_of(pl.ds(p * slots, slots))
        pooled = pooled + joined * gate(joined)
    pooled = (pooled / pixel_count).astype(low)
    head_low = head_pad[...].astype(low)
    logits = lax.dot_general(
        pooled, head_low, (((1,), (1,)), ((), ())), preferred_element_type=f32
    )
    lane = lax.broadcasted_iota(jnp.int32, logits.shape, 1)
    real = lane < classes
    largest = jnp.max(jnp.where(real, logits, -jnp.inf), axis=1, keepdims=True)
    powers = jnp.where(real, jnp.exp(jnp.where(real, logits - largest, 0.0)), 0.0)
    total_power = jnp.sum(powers, axis=1, keepdims=True)
    label_column = column_of(label_ref[...].astype(f32), slots).astype(jnp.int32)
    onehot = jnp.where(lane == label_column, 1.0, 0.0)
    entropy = largest + jnp.log(total_power) - jnp.sum(onehot * logits, axis=1, keepdims=True)
    loss = jnp.sum(entropy * valid_column, axis=0, keepdims=True)
    grad_logits = (
        (powers / total_power - onehot) * (valid_column / denominator[:, :1])
    ).astype(low)
    grad_head = lax.dot_general(
        grad_logits, pooled, (((0,), (0,)), ((), ())), preferred_element_type=f32
    )[:16]
    grad_pooled = jnp.dot(grad_logits, head_low, preferred_element_type=f32) / pixel_count

    gain_two, gain_side, shift_two = none, none, none
    for p in range(pixel_count):
        here = pl.ds(p * slots, slots)
        joined = joined_of(here)
        opened = gate(joined)
        grad = grad_pooled * (opened * (1.0 + joined * (1.0 - opened)))
        shift_two = shift_two + jnp.sum(grad, axis=0, keepdims=True)
        gain_two = gain_two + jnp.sum(
            grad * ((main_two[here, :] - mean_two) * inv_two), axis=0, keepdims=True
        )
        gain_side = gain_side + jnp.sum(
            grad * ((side_pre[here, :] - mean_side) * inv_side), axis=0, keepdims=True
        )
        back_two[p // side, 1 + p % side] = (grad * slope_two).astype(low)
        back_side[here, :] = (grad * slope_side).astype(low)

    grad_short[...] = jnp.dot(xs_t[0, 0], back_side[...], preferred_element_type=f32)
    for b in range(3):
        first, last = max(0, b - 1), min(side, side + b - 1)
        left = active_t[:, first * band : last * band]
        for a in range(3):
            right = back_two[first - b + 1 : last - b + 1, 2 - a : 2 - a + side]
            grad_two[pl.ds((a * 3 + b) * width, width), :] = jnp.dot(
                left, right.reshape(-1, width), preferred_element_type=f32
            )


    def nothing():
        pass

    def matrix_votes(k, grad, between):
        here = pl.ds(k * width, width)
        start = edges[k - 1] if k else 0
        col_new[:, here] = factored_votes(
            grad, grad.shape[0], start, row_ref, row_new, col_ref[:, here], level, out_ref, start, between
        )

    matrix_votes(2, grad_short, (nothing, nothing))
    matrix_votes(1, grad_two, (nothing, nothing))
    stage = {u: scatter_start(u) for u in range(4)}

    gain_one, shift_one = none, none
    for j in range(side):
        taps = [b for b in range(3) if 0 <= j - b + 1 < side]
        pieces = [
            back_two[j - b + 1, 2 - a : 2 - a + side].reshape(band, width)
            for b in taps
            for a in range(3)
        ]
        weights = jnp.concatenate([low_two[b * 3 + a] for b in taps for a in range(3)], axis=1)
        grad = lax.dot_general(
            jnp.concatenate(pieces, axis=1),
            weights,
            (((1,), (1,)), ((), ())),
            preferred_element_type=f32,
        )
        before = main_pre[pl.ds(j * band, band), :]
        hidden = before * slope_one + base_one
        opened = gate(hidden)
        grad = grad * (opened * (1.0 + hidden * (1.0 - opened)))
        shift_one = shift_one + jnp.sum(grad, axis=0, keepdims=True)
        gain_one = gain_one + jnp.sum(
            grad * ((before - mean_one) * inv_one), axis=0, keepdims=True
        )
        back_one[j, :side] = (grad * slope_one).astype(low).reshape(side, slots, width)
        if j == 1:
            stage[0] = scatter_one(0, stage[0])
            stage[1] = scatter_one(1, stage[1])
        if j == 2:
            stage[2] = scatter_one(2, stage[2])
            stage[3] = scatter_one(3, stage[3])

    square_head = grad_head * grad_head + EPS_ROW
    real = lax.broadcasted_iota(jnp.int32, square_head.shape, 0) < classes
    square_head = jnp.where(real, square_head, 0.0)
    head_lanes = pl.ds(edges[2], width)
    old = row_ref[:, head_lanes]
    row = keep * old + (1.0 - keep) * jnp.sum(square_head, axis=0, keepdims=True) / classes
    row_new[:, head_lanes] = row
    diagonal = eye_mask(16, classes)
    old = jnp.broadcast_to(col_ref[:, 3 * width :], (16, classes))
    old = jnp.sum(jnp.where(diagonal, old, 0.0), axis=1, keepdims=True)
    column = keep * old + (1.0 - keep) * jnp.sum(square_head, axis=1, keepdims=True) / width
    col_new[:, 3 * width :] = jnp.sum(
        jnp.where(diagonal, jnp.broadcast_to(column, (16, classes)), 0.0), axis=0, keepdims=True
    )
    real_column = lax.broadcasted_iota(jnp.int32, column.shape, 0) < classes
    column = jnp.where(real_column, column, 1.0)
    mean = jnp.sum(row, axis=1, keepdims=True) / width
    raw = grad_head * (lax.rsqrt(row) * jnp.sqrt(mean)) * lax.rsqrt(column)
    clip = jnp.maximum(1.0, jnp.sqrt(total_of(raw * raw) / (classes * width)))
    head_votes = jnp.tanh(raw / clip)[:classes]

    raws = []
    for k, grad in enumerate((gain_one, shift_one, gain_two, shift_two, gain_side, shift_two)):
        here = pl.ds(k * width, width)
        moment = keep * moment_ref[:, here] + (1.0 - keep) * (grad * grad + EPS_ROW)
        moment_new[:, here] = moment
        raws.append(grad * lax.rsqrt(moment))
    raw = jnp.concatenate(raws, axis=0)
    clip = jnp.maximum(1.0, jnp.sqrt(total_of(raw * raw) / raw.size))
    norm_votes = jnp.tanh(raw / clip)
    copies = exchange_start(
        2,
        jnp.concatenate([head_votes, norm_votes, jnp.broadcast_to(loss, (8, width))], axis=0),
    )


    for b in range(3):
        first, last = (0, side - 1) if b == 0 else (0, side)
        shift = 1 if b == 0 else 0
        for a in range(3):
            left = xs_t[0 if b == 1 else 1, 0 if a == 1 else 1, :, first * band : last * band]
            start = 1 if a == 0 else 0
            right = back_one[first + shift : last + shift, start : start + side]
            grad_one[pl.ds((a * 3 + b) * in_width, in_width), :] = jnp.dot(
                left, right.reshape(-1, width), preferred_element_type=f32
            )
        if b == 0:
            stage[0] = scatter_two(0, stage[0])
            stage[1] = scatter_two(1, stage[1])
        if b == 1:
            copies = exchange_middle(2, copies)
        if b == 2:
            stage[2] = scatter_two(2, stage[2])
            stage[3] = scatter_two(3, stage[3])

    def first_line():
        scatter_three(0, stage[0])
        scatter_three(1, stage[1])

    def second_line():
        scatter_three(2, stage[2])
        scatter_three(3, stage[3])

    matrix_votes(0, grad_one, (first_line, second_line))
    last = (4, 5, 6)
    stage = {u: scatter_start(u) for u in last}
    gathered = {}
    own_block(0)
    own_block(1)
    for u in last:
        stage[u] = scatter_one(u, stage[u])
    own_block(2)
    own_block(3)
    for u in (0, 1):
        gathered[u] = gather_one(u)
    for u in last:
        stage[u] = scatter_two(u, stage[u])
    for u in (2, 3):
        gathered[u] = gather_one(u)
    for u in (0, 1):
        gathered[u] = gather_two(u, gathered[u])
    for u in last:
        scatter_three(u, stage[u])
    for u in (2, 3):
        gathered[u] = gather_two(u, gathered[u])
    for u in (0, 1):
        gathered[u] = gather_three(u, gathered[u])
    for u in last:
        own_block(u)
    for u in (2, 3):
        gathered[u] = gather_three(u, gathered[u])

    sums = exchange_end(2, copies)
    loss_ref[...] = sums[TAIL:, :1][:1]
    old = jnp.concatenate([head_ref[...], norm_ref[...]], axis=0)
    is_head = lax.broadcasted_iota(jnp.int32, (TAIL, width), 0) < classes
    scale = jnp.where(is_head, scales[3], scales[4])
    sums = sums[:TAIL]
    fresh = old - scale * jnp.tanh(sums * root)
    both = jnp.concatenate([sums, fresh], axis=0)
    high = both.astype(low)
    rest = both - high.astype(f32)
    middle = rest.astype(low)
    parts = jnp.concatenate([high, middle, (rest - middle.astype(f32)).astype(low)], axis=0)

    for u in last:
        gathered[u] = gather_one(u)

    flat_sums, flat_new = [], []
    window = 256
    for q in range(classes):
        start = min(q * width // classes // 128 * 128, width - window)
        down = lax.broadcasted_iota(jnp.int32, (window, width), 0)
        across = lax.broadcasted_iota(jnp.int32, (window, width), 1)
        gap = across - classes * down + (q * width - classes * start)
        chosen = jnp.where(jnp.logical_and(gap >= 0, gap < classes), 1.0, 0.0).astype(low)
        moved = jnp.dot(parts[:, start : start + window], chosen, preferred_element_type=f32)
        moved = moved[: 2 * TAIL] + moved[2 * TAIL : 4 * TAIL] + moved[4 * TAIL :]
        spot_of = lax.broadcasted_iota(jnp.int32, (TAIL, width), 1).astype(f32) + q * width
        class_of = spot_of - classes * jnp.floor((spot_of + 0.5) / classes)
        here = lax.broadcasted_iota(jnp.int32, (TAIL, width), 0).astype(f32) == class_of
        flat_sums.append(jnp.sum(jnp.where(here, moved[:TAIL], 0.0), axis=0, keepdims=True))
        flat_new.append(jnp.sum(jnp.where(here, moved[TAIL:], 0.0), axis=0, keepdims=True))
    flat_sums = jnp.concatenate(flat_sums + [sums[classes:]], axis=0)
    flat_new = jnp.concatenate(flat_new + [fresh[classes:]], axis=0)

    for u in last:
        gathered[u] = gather_two(u, gathered[u])

    mine = [own_group(u) for u in range(len(units))]
    for slot in range(spare + 1):
        group = me * spare + slot
        own = group < 0
        for u, unit in enumerate(units):
            inside = jnp.logical_and(group >= mine[u], group < mine[u] + unit[1])
            own = jnp.logical_or(own, inside)

        @pl.when(jnp.logical_and(jnp.logical_not(own), group < groups - 1))
        def _():
            land(0, group, me, slot, 0)[0].wait_recv()

    pltpu.make_async_copy(
        weight.at[pl.ds(0, OWN)], weight.at[pl.ds(0, OWN)], fetch_sem.at[3]
    ).wait()
    total[pl.ds(0, SPAN), :] = landed[pl.ds(0, SPAN), :].astype(f32)

    @pl.loop(0, OWN // 16)
    def _(k):
        row = pl.multiple_of(k * 16, 16)
        renew(row, first_row + row)

    @pl.when(me < 31)
    def _():
        pltpu.make_async_copy(
            weight.at[pl.ds(OWN, TAIL)], weight.at[pl.ds(OWN, TAIL)], fetch_sem.at[4]
        ).wait()
        total[pl.ds(SPAN, GROUP), :] = landed[pl.ds(SPAN, GROUP), :].astype(f32)
        renew(OWN, first_row + OWN)

    def tail_rows(values, ref):
        for u in (0, 8):
            for q in range(4):
                flat_rows(OWN + u, q, values[u : u + 8, 128 * q : 128 * (q + 1)], ref)

    @pl.when(me == 31)
    def _():
        tail_rows(flat_sums, vote_flat)
        tail_rows(flat_new, new_flat)

    shift = 2 * me
    share = vote_ref.shape[0]
    vote_ref[...] = vote_flat[pl.ds(shift, share), :]
    new_ref[...] = new_flat[pl.ds(shift, share), :]
    tail_rows(flat_new, new_flat)
    out_ref[pl.ds(32 * SPAN, GROUP), :] = new_flat[pl.ds(SPAN, GROUP), :].astype(low)

    for u in last:
        gathered[u] = gather_three(u, gathered[u])
    for u in range(len(units)):
        gathered[u].wait()
        for k in range(1, 4):
            line_copy(u, k).wait_send()
            spread_copy(u, k).wait_send()
    for away, copy in passes:

        @pl.when(away)
        def _():
            copy.wait_send()


def finish_kernel(count, *refs):
    sources, targets, sem = refs[:count], refs[count : 2 * count], refs[2 * count]
    copies = [
        pltpu.make_async_copy(sources[k], targets[k], sem.at[k]) for k in range(count - 2)
    ]
    for copy in copies:
        copy.start()
    for k in (count - 2, count - 1):
        targets[k][...] = sources[k][...]
    for copy in copies:
        copy.wait()


def finish(values):
    vmem = pl.BlockSpec(memory_space=pltpu.VMEM)
    hbm = pl.BlockSpec(memory_space=pl.ANY)
    count = len(values)
    held = [pltpu.with_memory_space_constraint(value, pltpu.VMEM) for value in values[:-2]]
    return pl.pallas_call(
        functools.partial(finish_kernel, count),
        out_shape=[jax.ShapeDtypeStruct(value.shape, value.dtype) for value in values],
        in_specs=[vmem] * count,
        out_specs=[hbm] * (count - 2) + [vmem] * 2,
        scratch_shapes=[pltpu.SemaphoreType.DMA((count,))],
        compiler_params=pltpu.CompilerParams(vmem_limit_bytes=1024 * 1024),
        name="finish",
    )(*held, *values[-2:])


def run_step(images, conv_one, conv_two, shortcut, head, norm_params, valid, labels, rows, cols, moment):
    vmem = pl.BlockSpec(memory_space=pltpu.VMEM)
    hbm = pl.BlockSpec(memory_space=pl.ANY)
    low, f32 = jnp.bfloat16, jnp.float32
    dma = pltpu.SemaphoreType.DMA
    workers = lax.axis_size("dp")
    slots, in_width = valid.shape[1], images.shape[1]
    width = conv_one.shape[1]
    pixels = images.shape[0] // 4
    shape = pltpu.VMEM
    edges = [conv_one.shape[0]]
    edges.append(edges[0] + conv_two.shape[0])
    edges.append(edges[1] + shortcut.shape[0])
    units = make_units(edges)
    flat = (edges[2] + TAIL) * width // 128
    share = flat // workers
    return pl.pallas_call(
        functools.partial(step_kernel, tuple(edges), tuple(units), 1.0 / math.sqrt(workers)),
        out_shape=(
            shape((share, 128), f32),
            shape((share, 128), f32),
            shape((flat, 128), low),
            shape(rows.shape, f32),
            shape(cols.shape, f32),
            shape(moment.shape, f32),
            jax.ShapeDtypeStruct((1, 1), f32),
            jax.ShapeDtypeStruct((1, 1), f32),
        ),
        in_specs=[hbm] * 4 + [vmem] * 7,
        out_specs=(vmem,) * 8,
        scratch_shapes=[
            pltpu.VMEM((2, 4, 2, 4, slots, in_width), low),
            pltpu.VMEM(conv_one.shape, f32),
            pltpu.VMEM(conv_two.shape, f32),
            pltpu.VMEM(shortcut.shape, f32),
            pltpu.VMEM((9, in_width, width), low),
            pltpu.VMEM((9, width, width), low),
            pltpu.VMEM((1, in_width, width), low),
            pltpu.VMEM((pixels, width), f32),
            pltpu.VMEM((pixels, width), f32),
            pltpu.VMEM((pixels, width), f32),
            pltpu.VMEM((4, 6, slots, width), low),
            pltpu.VMEM((4, 6, slots, width), low),
            pltpu.VMEM((4, 5, slots, width), low),
            pltpu.VMEM((pixels, width), low),
            pltpu.VMEM((width, pixels), low),
            pltpu.VMEM((2, 2, in_width, pixels), low),
            pltpu.VMEM((128, width), f32),
            pltpu.VMEM((conv_two.shape[0], 128), f32),
            pltpu.VMEM((8, width), f32),
            pltpu.VMEM((2, 8, width), f32),
            pltpu.VMEM((2, 8, 8, width), f32),
            pltpu.VMEM((2, 4, 8, width), f32),
            pltpu.VMEM((TAIL + 8, width), f32),
            pltpu.VMEM((8, TAIL + 8, width), f32),
            pltpu.VMEM((4, TAIL + 8, width), f32),
            pltpu.VMEM((16 * SPAN, 128), low),
            pltpu.VMEM((8 * SPAN, 128), low),
            pltpu.VMEM((4 * SPAN, 128), low),
            pltpu.VMEM((4 * SPAN, 128), low),
            pltpu.VMEM((SPAN, 128), low),
            pltpu.VMEM((SPAN + GROUP, 128), low),
            pltpu.VMEM((SPAN + GROUP, 128), f32),
            pltpu.VMEM((OWN, width), f32),
            pltpu.VMEM((OWN + TAIL, width), f32),
            pltpu.VMEM((SPAN + GROUP, 128), f32),
            pltpu.VMEM((SPAN + GROUP, 128), f32),
            dma((5 + len(units),)),
            dma((3, 10)),
            dma((3, 10)),
            dma((len(units), 3)),
            dma((len(units), 3)),
            dma((len(units), 4)),
            dma((len(units), 4)),
            dma((2 * OWN // 16,)),
            dma((OWN // 16 + 1,)),
            dma((len(units), 4)),
            dma((len(units), 4)),
            dma((len(units), 3)),
            dma((len(units), 3)),
            pltpu.SemaphoreType.REGULAR((len(units),)),
            dma((2,)),
        ],
        compiler_params=pltpu.CompilerParams(
            collective_id=1, has_side_effects=True, vmem_limit_bytes=52 * 1024 * 1024
        ),
        name="step",
    )(images, conv_one, conv_two, shortcut, head, norm_params, valid, labels, rows, cols, moment)


def scale_for(weight):
    return jnp.maximum(EPS_SCALE, jnp.sqrt(jnp.mean(weight * weight)))


def local_general(
    images,
    valid_slot,
    labels,
    conv_one,
    conv_two,
    shortcut,
    classifier,
    norm_params,
    row_state,
    col_state,
    bn_moment,
):
    in_width = images.shape[3]
    width = conv_one.shape[1]
    kernel_one = conv_one.astype(jnp.bfloat16).reshape(3, 3, in_width, width)
    kernel_two = conv_two.astype(jnp.bfloat16).reshape(3, 3, width, width)
    kernel_short = shortcut.astype(jnp.bfloat16).reshape(1, 1, in_width, width)
    head_low = classifier.astype(jnp.bfloat16)
    slot_count = images.shape[0]
    out_side = images.shape[1] // 2
    pixel_count = out_side * out_side
    slot_weight = valid_slot.astype(jnp.float32)
    pixel_weight = jnp.broadcast_to(slot_weight[:, None], (slot_count, pixel_count)).reshape(-1, 1)
    main_pre, side_pre = first_section(images, kernel_one, kernel_short)
    main_sums = masked_moments(pixel_weight, main_pre)
    side_sums = masked_moments(pixel_weight, side_pre)
    count_row = jnp.broadcast_to(jnp.sum(slot_weight), (width,))
    first_sums = lax.psum(jnp.stack([*main_sums, *side_sums, count_row]), "dp")
    valid_count = first_sums[4, 0]
    denominator = jnp.maximum(valid_count, 1.0)
    pixels = denominator * pixel_count
    norm_one = settle(first_sums[0], first_sums[1], pixels)
    norm_side = settle(first_sums[2], first_sums[3], pixels)
    hidden_one, active, main_two = second_section(
        main_pre, norm_one, norm_params, kernel_two, slot_count, out_side
    )
    two_sums = masked_moments(pixel_weight, main_two)
    second_sums = lax.psum(jnp.stack([*two_sums]), "dp")
    norm_two = settle(second_sums[0], second_sums[1], pixels)
    joined_pre = (
        (main_two - norm_two[0]) * norm_two[1] * norm_params[2]
        + norm_params[3]
        + (side_pre - norm_side[0]) * norm_side[1] * norm_params[4]
        + norm_params[5]
    )
    joined = jax.nn.silu(joined_pre).reshape(slot_count, pixel_count, -1)
    pooled = jnp.mean(joined, axis=1).astype(jnp.bfloat16)
    logits = jnp.dot(pooled, head_low, preferred_element_type=jnp.float32)
    largest = jnp.max(logits, axis=1, keepdims=True)
    exp_terms = jnp.exp(logits - largest)
    total_exp = jnp.sum(exp_terms, axis=1, keepdims=True)
    log_total = largest[:, 0] + jnp.log(total_exp[:, 0])
    onehot = (labels[:, None] == jnp.arange(logits.shape[1], dtype=jnp.int32)[None, :]).astype(
        jnp.float32
    )
    local_sum = jnp.sum(slot_weight * (log_total - jnp.sum(onehot * logits, axis=1)))
    grad_logits = ((exp_terms / total_exp - onehot) * (slot_weight / denominator)[:, None]).astype(
        jnp.bfloat16
    )
    grad_head = lax.dot_general(
        pooled, grad_logits, (((0,), (0,)), ((), ())), preferred_element_type=jnp.float32
    )
    grad_pooled = lax.dot_general(
        grad_logits, head_low, (((1,), (1,)), ((), ())), preferred_element_type=jnp.float32
    )
    spread_pooled = jnp.broadcast_to(
        (grad_pooled / pixel_count)[:, None, :], (slot_count, pixel_count, width)
    )
    grad_joined = spread_pooled.reshape(slot_count * pixel_count, width) * silu_slope(joined_pre)
    gain_two, shift_two, grad_two = norm_backward(grad_joined, main_two, norm_two, norm_params[2])
    gain_side, shift_side, grad_side = norm_backward(
        grad_joined, side_pre, norm_side, norm_params[4]
    )
    grad_two_maps = grad_two.reshape(slot_count, out_side, out_side, width)
    grad_side_maps = grad_side.reshape(slot_count, out_side, out_side, width)
    grad_conv_two = conv_weight_grad(active, grad_two_maps, 1, 1, 1)
    grad_short = conv_weight_grad(images, grad_side_maps, 2, 0, -1)
    kernel_turned = jnp.transpose(kernel_two[::-1, ::-1], (0, 1, 3, 2))
    grad_active = conv_apply(grad_two_maps, kernel_turned, 1, 1).reshape(
        slot_count * pixel_count, width
    )
    grad_hidden = grad_active * silu_slope(hidden_one)
    gain_one, shift_one, grad_one = norm_backward(grad_hidden, main_pre, norm_one, norm_params[0])
    grad_conv_one = conv_weight_grad(
        images, grad_one.reshape(slot_count, out_side, out_side, width), 2, 1, 0
    )
    grad_norms = jnp.stack([gain_one, shift_one, gain_two, shift_two, gain_side, shift_side])
    grads = (grad_conv_one, grad_conv_two, grad_short, grad_head, grad_norms)
    votes, rows_new, cols_new, moment_new = make_votes(
        grads, row_state[0], col_state[0], bn_moment[0]
    )
    workers = lax.axis_size("dp")
    weights = (conv_one, conv_two, shortcut, classifier, norm_params)
    scales = [scale_for(weight) for weight in weights]
    loss_sum = lax.psum(local_sum, "dp")
    flat_vote = jnp.concatenate([vote.reshape(-1) for vote in votes])
    flat_old = jnp.concatenate([weight.reshape(-1) for weight in weights])
    flat_scale = jnp.concatenate(
        [
            jnp.broadcast_to(scale, (weight.size,))
            for scale, weight in zip(scales, weights)
        ]
    )
    vote_mine = lax.psum_scatter(flat_vote, "dp", tiled=True)
    share = vote_mine.shape[0]
    start = lax.axis_index("dp") * share
    new_mine = lax.dynamic_slice_in_dim(
        flat_old, start, share
    ) - lax.dynamic_slice_in_dim(flat_scale, start, share) * jnp.tanh(
        vote_mine / math.sqrt(workers)
    )
    copies = lax.all_gather(new_mine.astype(jnp.bfloat16), "dp", tiled=True)
    return (
        loss_sum,
        valid_count,
        new_mine,
        copies,
        vote_mine,
        rows_new[None, :],
        cols_new[None, :],
        moment_new[None, :],
    )


def local(
    images,
    valid_slot,
    labels,
    conv_one,
    conv_two,
    shortcut,
    classifier,
    norm_params,
    row_state,
    col_state,
    bn_moment,
):
    new_mine, vote_mine, copies, rows_new, cols_new, moment_new, loss_sum, valid_count = run_step(
        images.reshape(-1, images.shape[-1]),
        conv_one,
        conv_two,
        shortcut,
        classifier.T,
        norm_params,
        valid_slot.reshape(1, -1),
        labels.reshape(1, -1),
        row_state,
        col_state,
        bn_moment,
    )
    copies, new_mine, vote_mine, rows_new, cols_new, moment_new, loss_sum, valid_count = finish(
        (copies, new_mine, vote_mine, rows_new, cols_new, moment_new, loss_sum, valid_count)
    )
    return (
        loss_sum.reshape(()),
        valid_count.reshape(()),
        new_mine.reshape(-1),
        copies.reshape(-1),
        vote_mine.reshape(-1),
        rows_new,
        cols_new,
        moment_new,
    )


def solution(mesh):
    placed = (
        P("dp", None, None, None),
        P("dp"),
        P("dp"),
        P(),
        P(),
        P(),
        P(),
        P(),
        P("dp", None),
        P("dp", None),
        P("dp", None),
    )
    return jax.shard_map(
        local if mesh.shape["dp"] == 32 else local_general,
        mesh=mesh,
        in_specs=placed,
        out_specs=(P(), P(), P("dp"), P(), P("dp"), P("dp", None), P("dp", None), P("dp", None)),
        check_vma=False,
    )
```

```python
import functools
import math

import jax
import jax.numpy as jnp
from jax import lax
from jax.experimental import pallas as pl
from jax.experimental.pallas import tpu as pltpu
from jax.sharding import PartitionSpec as P

STEP = 10
MESH = pl.DeviceIdType.MESH

EPS_NORM = 1e-05
EPS_ROW = 1e-30
EPS_SCALE = 0.001
FORWARD_DIMS = ("NHWC", "HWIO", "NHWC")
WEIGHT_DIMS = ("CHWN", "IHWO", "HWNC")
OWN = 224
TAIL = 16
PIECE = 32
SPAN = 4 * OWN
HALF = SPAN // 2
GROUP = 64


def conv_apply(maps, kernel, stride, margin):
    return lax.conv_general_dilated(
        maps,
        kernel,
        (stride, stride),
        ((margin, margin), (margin, margin)),
        dimension_numbers=FORWARD_DIMS,
        preferred_element_type=jnp.float32,
    )


def conv_weight_grad(maps, grad_out, stride, low_pad, high_pad):
    result = lax.conv_general_dilated(
        maps,
        grad_out,
        (1, 1),
        ((low_pad, high_pad), (low_pad, high_pad)),
        rhs_dilation=(stride, stride),
        dimension_numbers=WEIGHT_DIMS,
        preferred_element_type=jnp.float32,
    )
    return result.reshape(-1, result.shape[3])


def silu_slope(values):
    sigmoid_part = jax.nn.sigmoid(values)
    return sigmoid_part * (1.0 + values * (1.0 - sigmoid_part))


def settle(sum_plain, sum_square, pixels):
    mean_value = sum_plain / pixels
    return (mean_value, lax.rsqrt(sum_square / pixels - mean_value * mean_value + EPS_NORM))


def first_section(images, kernel_one, kernel_short):
    row_count = images.shape[0] * (images.shape[1] // 2) ** 2
    main_pre = conv_apply(images, kernel_one, 2, 1).reshape(row_count, -1)
    side_pre = conv_apply(images, kernel_short, 2, 0).reshape(row_count, -1)
    return (main_pre, side_pre)


def second_section(main_pre, norm_one, norm_params, kernel_two, slot_count, out_side):
    hidden_one = (main_pre - norm_one[0]) * norm_one[1] * norm_params[0] + norm_params[1]
    active = (
        jax.nn.silu(hidden_one).astype(jnp.bfloat16).reshape(slot_count, out_side, out_side, -1)
    )
    main_two = conv_apply(active, kernel_two, 1, 1).reshape(slot_count * out_side * out_side, -1)
    return (hidden_one, active, main_two)


def masked_moments(pixel_weight, values):
    return (jnp.sum(pixel_weight * values, axis=0), jnp.sum(pixel_weight * values * values, axis=0))


def soft_sign(step_raw):
    clip_by = jnp.maximum(1.0, jnp.sqrt(jnp.mean(step_raw * step_raw)))
    return jnp.tanh(step_raw / clip_by)


def make_votes(grads, rows_old, cols_old, moment_old):
    decay_rate = 1.0 - STEP ** (-0.8)
    votes, rows_new, cols_new = ([], [], [])
    row_at, col_at = (0, 0)
    for matrix in grads[:4]:
        row_size, col_size = matrix.shape
        square = matrix * matrix + EPS_ROW
        row_part = decay_rate * rows_old[row_at : row_at + row_size] + (
            1.0 - decay_rate
        ) * jnp.mean(square, axis=1)
        col_part = decay_rate * cols_old[col_at : col_at + col_size] + (
            1.0 - decay_rate
        ) * jnp.mean(square, axis=0)
        second = row_part[:, None] * col_part[None, :] / jnp.mean(row_part)
        votes.append(soft_sign(matrix * lax.rsqrt(second)))
        rows_new.append(row_part)
        cols_new.append(col_part)
        row_at += row_size
        col_at += col_size
    flat_norm = grads[4].reshape(-1)
    moment_new = decay_rate * moment_old + (1.0 - decay_rate) * (flat_norm * flat_norm + EPS_ROW)
    votes.append(soft_sign(flat_norm * lax.rsqrt(moment_new)))
    return (votes, jnp.concatenate(rows_new), jnp.concatenate(cols_new), moment_new)


def norm_backward(grad_out, pre_value, norm_pair, gain_row):
    normed = (pre_value - norm_pair[0]) * norm_pair[1]
    grad_gain = jnp.sum(grad_out * normed, axis=0)
    grad_shift = jnp.sum(grad_out, axis=0)
    grad_pre = (grad_out * gain_row * norm_pair[1]).astype(jnp.bfloat16)
    return (grad_gain, grad_shift, grad_pre)


SCHEDULE = (
    (),
    (),
    (),
    (
        (1, 0), (1, 1), (1, 3), (1, 4), (1, 5), (1, 7), (1, 2),
    ),
    (),
    (),
    (),
    (),
    (),
    (),
    (
        (1, 6), (2, 1), (2, 3), (1, 8), (2, 0), (2, 7), (1, 9), (3, 0), (1, 10), (1, 12),
        (1, 11), (2, 2), (2, 4), (4, 0), (3, 1), (5, 0), (3, 3), (3, 2), (2, 5), (2, 6), (4, 1),
        (1, 13), (4, 3), (3, 4), (3, 7), (3, 5), (2, 8), (5, 1), (2, 10), (2, 9), (2, 12),
        (4, 2), (6, 0), (3, 9), (2, 11), (4, 5), (6, 1), (2, 13), (4, 7), (3, 6), (4, 4),
        (3, 11), (3, 10), (3, 13), (5, 2), (3, 8), (5, 3), (6, 3), (6, 2), (5, 5), (4, 6),
        (7, 0), (5, 4), (4, 9), (6, 5), (7, 1), (4, 10), (4, 8), (5, 7), (7, 3), (6, 7), (6, 4),
        (7, 5), (4, 13), (7, 2), (5, 10), (3, 12), (4, 11), (5, 6), (5, 9), (6, 6), (4, 12),
        (5, 8), (6, 8), (6, 9), (5, 11), (7, 7), (7, 4), (7, 9), (6, 10), (5, 12), (5, 13),
        (6, 11), (7, 6), (7, 11), (6, 12), (7, 8), (6, 13), (7, 10), (7, 13), (7, 12),
    ),
)


def place():
    me = lax.axis_index("dp")
    core = lax.rem(me, 2)
    x = lax.rem(lax.div(me, 2), 2)
    y = lax.rem(lax.div(me, 4), 2)
    z = lax.div(me, 8)
    return me, core, x, y, z


def send(src, dst, send_sem, recv_sem, partner):
    copy = pltpu.make_async_remote_copy(
        src_ref=src,
        dst_ref=dst,
        send_sem=send_sem,
        recv_sem=recv_sem,
        device_id=(partner,),
        device_id_type=MESH,
    )
    copy.start()
    return copy


def scale_of(row, scales, edges):
    picked = scales[2]
    picked = jnp.where(row < edges[1], scales[1], picked)
    return jnp.where(row < edges[0], scales[0], picked)


def make_units(edges):
    one, two, short = edges[0] // 16, edges[1] // 16, edges[2] // 16
    units = []
    for k in range((two - one) // 32):
        units.append((one + 32 * k, 1, k % 2 == 0, 16, (1, 1)))
    for k in range(one // 32):
        units.append((32 * k, 1, k % 2 == 1, 16, (0, 0)))
    at = one // 32 * 32
    assert one - at == 16 and short - two == 16
    units.append((at, 1, False, two - at, (0, 2)))
    return units


def settle_rows(sums, pixels, gain, shift):
    mean = sums[0] / pixels
    inv = lax.rsqrt(sums[1] / pixels - mean * mean + EPS_NORM)
    slope = gain * inv
    return mean, inv, slope, shift - mean * slope


def gate(values):
    return 0.5 * jnp.tanh(0.5 * values) + 0.5


def eye_mask(rows, columns, offset=0):
    down = lax.broadcasted_iota(jnp.int32, (rows, columns), 0) + offset
    return down == lax.broadcasted_iota(jnp.int32, (rows, columns), 1)


def column_of(row, size):
    spread = jnp.where(eye_mask(size, size), jnp.broadcast_to(row, (size, size)), 0)
    return jnp.sum(spread, axis=1, keepdims=True)


def total_of(values):
    return jnp.sum(jnp.sum(values, axis=0, keepdims=True), axis=1, keepdims=True)


def fold(values):
    return jnp.sum(values.reshape(values.shape[0] // 8, 8, values.shape[1]), axis=0)


def cast_weight(source, target, square_ref, taps, depth, fetches):
    step = 128
    square_ref[...] = jnp.zeros_like(square_ref)
    for tap in range(taps):
        if tap % (taps // len(fetches)) == 0:
            fetches[tap * len(fetches) // taps].wait()
        new_tap = (tap % 3) * 3 + tap // 3

        @pl.loop(0, depth // step)
        def _(k):
            start = pl.multiple_of(k * step, step)
            values = source[pl.ds(tap * depth + start, step), :]
            target[new_tap, pl.ds(start, step), :] = values.astype(jnp.bfloat16)
            square_ref[...] += fold(values * values)


def factored_votes(grad, rows, row_at, rows_old, rows_new, col_old, level, votes, vote_at, between, after):
    width = grad.shape[1]
    keep = 1.0 - STEP ** (-0.8)
    step = 128
    quarters = width // 128

    def first(k, carry):
        col_sum, row_sum = carry
        start = pl.multiple_of(k * step, step)
        lanes = pl.ds(pl.multiple_of(row_at + start, step), step)
        old = rows_old[:, lanes] * keep
        line = jnp.zeros((8, 128), jnp.float32)
        for m in range(step // 8):
            block = grad[pl.ds(start + 8 * m, 8), :]
            square = block * block
            col_sum = col_sum + square
            part = square[:, :128]
            for q in range(1, quarters):
                part = part + square[:, 128 * q : 128 * (q + 1)]
            part = part * ((1.0 - keep) / width)
            diagonal = eye_mask(8, 128, 8 * m)
            part = part + jnp.where(diagonal, jnp.broadcast_to(old, (8, 128)), 0.0)
            row = jnp.sum(part, axis=1, keepdims=True) + (1.0 - keep) * EPS_ROW
            row = jnp.broadcast_to(row, (8, 128))
            level[pl.ds(start + 8 * m, 8), :] = row
            row_sum = row_sum + row
            line = line + jnp.where(diagonal, row, 0.0)
        rows_new[:, lanes] = jnp.sum(line, axis=0, keepdims=True)
        return col_sum, row_sum

    col_sum, row_sum = lax.fori_loop(
        0,
        rows // step,
        first,
        (jnp.zeros((8, width), jnp.float32), jnp.zeros((8, 128), jnp.float32)),
    )
    col_new = keep * col_old + (1.0 - keep) * (
        jnp.sum(col_sum, axis=0, keepdims=True) / rows + EPS_ROW
    )
    scale = lax.rsqrt(col_new)
    root_mean = jnp.sqrt(jnp.sum(row_sum, axis=0, keepdims=True) / rows)

    def second(k, carry):
        start = pl.multiple_of(k * step, step)
        for m in range(step // 8):
            here = pl.ds(start + 8 * m, 8)
            factor = lax.rsqrt(level[here, :]) * root_mean
            level[here, :] = factor
            raw = grad[here, :] * scale
            power = raw * raw
            part = power[:, :128]
            for q in range(1, quarters):
                part = part + power[:, 128 * q : 128 * (q + 1)]
            carry = carry + part * (factor * factor)
        return carry

    between[0]()
    power = lax.fori_loop(0, rows // step, second, jnp.zeros((8, 128), jnp.float32))
    between[1]()
    clip = jnp.maximum(1.0, jnp.sqrt(total_of(power) / (rows * width)))
    scale = scale / clip

    def third(k, _):
        start = pl.multiple_of(k * step, step)
        for m in range(step // 16):
            here = pl.ds(start + 16 * m, 16)
            factor = level[here, :]
            factor = jnp.concatenate([factor] * quarters, axis=1)
            vote = jnp.tanh(grad[here, :] * factor * scale).astype(jnp.bfloat16)
            at = pl.multiple_of((vote_at + start) * 4 + GROUP * m, GROUP)
            for q in range(quarters):
                votes[pl.ds(at + 16 * q, 16), :] = vote[:, 128 * q : 128 * (q + 1)]
        return 0

    part = 512 // step
    for k in range(0, rows // step, part):
        lax.fori_loop(k, min(k + part, rows // step), third, 0)
        after(k // part)
    return col_new


def step_kernel(
    edges,
    units,
    root,
    images,
    one_hbm,
    two_hbm,
    short_hbm,
    head_ref,
    norm_ref,
    valid_ref,
    label_ref,
    row_ref,
    col_ref,
    moment_ref,
    new_ref,
    vote_ref,
    out_ref,
    row_new,
    col_new,
    moment_new,
    loss_ref,
    count_ref,
    xs,
    grad_one,
    grad_two,
    grad_short,
    low_one,
    low_two,
    low_short,
    main_pre,
    side_pre,
    main_two,
    active,
    back_two,
    back_one,
    back_side,
    active_t,
    xs_t,
    head_pad,
    level,
    square,
    post_one,
    plane_one,
    line_one,
    post_two,
    plane_two,
    line_two,
    tail_post,
    tail_plane,
    tail_line,
    core_in,
    wide_in,
    deep_in,
    line_in,
    sum_low,
    landed,
    total,
    own_weight,
    weight,
    vote_flat,
    new_flat,
    fetch_sem,
    small_send,
    small_recv,
    rs_send,
    rs_recv,
    line_send,
    line_recv,
    pass_send,
    land_recv,
    spread_send,
    spread_recv,
    ag_send,
    ag_recv,
    free_sem,
    load_sem,
):
    slots, in_width = xs.shape[4:]
    width = main_pre.shape[1]
    side = 4
    band = side * slots
    pixel_count = side * side
    classes = head_ref.shape[0]
    keep = 1.0 - STEP ** (-0.8)
    low = jnp.bfloat16
    f32 = jnp.float32

    me, core, x, y, z = place()
    flip_core = me + 1 - 2 * core
    flip_x = me + 2 - 4 * x
    flip_y = me + 4 - 8 * y
    spot = lax.rem(me, 8)
    near = [z * 8 + lax.rem(spot + k, 8) for k in range(1, 8)]
    far = [lax.rem(z + k, 4) * 8 + spot for k in range(1, 4)]
    others = [lax.rem(me + k, 32) for k in range(1, 32)]

    count = images.shape[0]
    loads = []
    for half in range(2):
        lanes = slice(128 * half, 128 * (half + 1))
        loads.append(
            pltpu.make_async_copy(
                images.at[:, lanes], core_in.at[pl.ds(half * count, count)], load_sem.at[half]
            )
        )
        loads[half].start()

    def chunks_of(source, target, first, count):
        rows = source.shape[0] // count
        return [
            pltpu.make_async_copy(
                source.at[pl.ds(k * rows, rows)],
                target.at[pl.ds(k * rows, rows)],
                fetch_sem.at[first + k],
            )
            for k in range(count)
        ]

    fetch_one = chunks_of(one_hbm, grad_one, 0, 3)
    fetch_short = chunks_of(short_hbm, grad_short, 3, 1)
    fetch_two = chunks_of(two_hbm, grad_two, 4, 3)
    for fetch in fetch_one + fetch_short:
        fetch.start()
    barrier = pltpu.get_barrier_semaphore()
    for partner in others:
        pl.semaphore_signal(barrier, inc=1, device_id=(partner,), device_id_type=MESH)

    def fetch_rows(row, count, place_at, sem):
        parts = (
            (one_hbm, 0, edges[0]),
            (two_hbm, edges[0], edges[1]),
            (short_hbm, edges[1], edges[2]),
        )
        for ref, first, last in parts:

            @pl.when(jnp.logical_and(row >= first, row < last))
            def _():
                start = pl.multiple_of(row - first, count)
                pltpu.make_async_copy(
                    ref.at[pl.ds(start, count)], weight.at[pl.ds(place_at, count)], sem
                ).start()

    first_row = me * OWN

    for half in range(2):
        lanes = slice(128 * half, 128 * (half + 1))
        loads[half].wait()
        level[:count, :] = core_in[pl.ds(half * count, count), :].astype(f32)
        for h in range(2 * side):
            for w in range(2 * side):
                rows = level[pl.ds(2 * side * h + w, slots, stride=4 * pixel_count), :]
                xs[w % 2, w // 2, h % 2, h // 2, :, lanes] = rows.astype(low)

    scales = {}

    def scale_from(weight_square, size):
        return jnp.maximum(EPS_SCALE, jnp.sqrt(total_of(weight_square) / size))

    exchanges = (
        (post_one, plane_one, line_one),
        (post_two, plane_two, line_two),
        (tail_post, tail_plane, tail_line),
    )

    def exchange_start(which, values):
        mine_ref, plane_ref, _ = exchanges[which]
        mine_ref[...] = values
        plane_ref[spot] = values
        return [
            send(
                mine_ref,
                plane_ref.at[spot],
                small_send.at[which, k],
                small_recv.at[which, k],
                partner,
            )
            for k, partner in enumerate(near)
        ]

    def pack_rows(rows):
        pieces = [row[:, 128 * q : 128 * (q + 1)] for row in rows for q in range(4)]
        pad = -len(pieces) % 8
        if pad:
            pieces.append(jnp.zeros((pad, 128), f32))
        return jnp.concatenate(pieces, axis=0)

    def unpack_row(lines_in, k):
        return jnp.concatenate([lines_in[4 * k + q : 4 * k + q + 1] for q in range(4)], axis=1)

    def exchange_middle(which, copies):
        _, plane_ref, line_ref = exchanges[which]
        for copy in copies:
            copy.wait()
        line_ref[z] = functools.reduce(lambda a, b: a + b, [plane_ref[k] for k in range(8)])
        return [
            send(
                line_ref.at[z],
                line_ref.at[z],
                small_send.at[which, 7 + k],
                small_recv.at[which, 7 + k],
                partner,
            )
            for k, partner in enumerate(far)
        ]

    def exchange_end(which, copies):
        line_ref = exchanges[which][2]
        for copy in copies:
            copy.wait()
        return (line_ref[0] + line_ref[1]) + (line_ref[2] + line_ref[3])

    def lines(start, count):
        return pl.ds(pl.multiple_of(start, 16), count)

    sizes = [GROUP * unit[1] for unit in units]
    starts = [sum(sizes[:k]) for k in range(len(units) + 1)]

    def part_of(ref, u, share, start, count):
        return ref.at[lines(share * starts[u] + start, count)]

    def places(u):
        if units[u][2]:
            return x, y, flip_x, flip_y
        return y, x, flip_y, flip_x

    def unit_start(u, cc):
        return GROUP * units[u][0] + cc * (GROUP * units[u][3])

    def own_group(u):
        first, second, _, _ = places(u)
        return units[u][0] + core * units[u][3] + (first * 8 + second * 4 + z) * units[u][1]

    def halve(source, target, u, stage, partner):
        return send(source, target, rs_send.at[u, stage], rs_recv.at[u, stage], partner)

    def scatter_start(u):
        size = 16 * sizes[u]
        return halve(
            out_ref.at[lines(unit_start(u, 1 - core), size)],
            part_of(core_in, u, 16, 0, size),
            u,
            0,
            flip_core,
        )

    def add_to(ref, u, share, source_ref, source_start):
        size = share * sizes[u]
        here = lines(share * starts[u], size)
        ref[here, :] = ref[here, :] + source_ref[lines(source_start, size), :]

    def scatter_one(u, copy):
        copy.wait()
        add_to(core_in, u, 16, out_ref, unit_start(u, core))
        pl.semaphore_signal(
            free_sem.at[u], inc=1, device_id=(flip_core,), device_id_type=MESH
        )
        first, _, flip_first, _ = places(u)
        size = 8 * sizes[u]
        return halve(
            part_of(core_in, u, 16, (1 - first) * size, size),
            part_of(wide_in, u, 8, 0, size),
            u,
            1,
            flip_first,
        )

    def scatter_two(u, copy):
        copy.wait()
        first, second, _, flip_second = places(u)
        add_to(wide_in, u, 8, core_in, 16 * starts[u] + first * 8 * sizes[u])
        size = 4 * sizes[u]
        return halve(
            part_of(wide_in, u, 8, (1 - second) * size, size),
            part_of(deep_in, u, 4, 0, size),
            u,
            2,
            flip_second,
        )

    def line_copy(u, k):
        plane_to = lax.rem(z + k, 4)
        return pltpu.make_async_remote_copy(
            src_ref=part_of(deep_in, u, 4, plane_to * sizes[u], sizes[u]),
            dst_ref=part_of(line_in, u, 4, z * sizes[u], sizes[u]),
            send_sem=line_send.at[u, k],
            recv_sem=line_recv.at[u, k],
            device_id=(plane_to * 8 + spot,),
            device_id_type=MESH,
        )

    def scatter_three(u, copy):
        copy.wait()
        _, second, _, _ = places(u)
        add_to(deep_in, u, 4, wide_in, 8 * starts[u] + second * 4 * sizes[u])
        for k in (3, 2, 1):
            line_copy(u, k).start()
        here = lines(4 * starts[u] + z * sizes[u], sizes[u])
        line_in[here, :] = deep_in[here, :]

    groups = (edges[2] + TAIL) // 16
    spare = (groups - 1) // 32
    passes = []

    def land(local, group, to, slot, index):
        source = sum_low.at[lines(local * GROUP, GROUP)]
        target = landed.at[lines(slot * GROUP, GROUP)]
        copy = pltpu.make_async_remote_copy(
            src_ref=source,
            dst_ref=target,
            send_sem=pass_send.at[index],
            recv_sem=land_recv.at[slot],
            device_id=(to,),
            device_id_type=MESH,
        )
        return copy, source, target

    def pass_on(u):
        for m in range(units[u][1]):
            local = starts[u] // GROUP + m
            group = own_group(u) + m
            to, slot = lax.div(group, spare), lax.rem(group, spare)
            for halo in range(2):
                index = 2 * local + halo
                if halo:
                    receiver, at = lax.rem(to + 31, 32), spare
                    wanted = jnp.logical_and(slot == 0, group > 0)
                else:
                    receiver, at, wanted = to, slot, group >= 0
                away = jnp.logical_and(wanted, receiver != me)
                here = jnp.logical_and(wanted, receiver == me)
                copy, source, target = land(local, group, receiver, at, index)

                @pl.when(away)
                def _():
                    copy.start()

                @pl.when(here)
                def _():
                    target[...] = source[...]

                passes.append((away, copy))

    def flat_rows(row, q, values, ref):
        ref[pl.ds(row * 4 + q, 8, stride=4), :] = values

    def old_rows(u, cc):
        matrix = units[u][4][cc]
        base = edges[matrix - 1] if matrix else 0
        return (one_hbm, two_hbm, short_hbm)[matrix], 16 * own_group(u) - base, 16 * units[u][1]

    def own_fetch(u):
        target = own_weight.at[pl.ds(starts[u] // 4, 16 * units[u][1])]
        matrices = units[u][4]
        for cc in range(2):
            if cc and matrices[0] == matrices[1]:
                continue

            @pl.when((core == cc) if matrices[0] != matrices[1] else (core >= 0))
            def _():
                ref, row, count = old_rows(u, cc)
                pltpu.make_async_copy(
                    ref.at[pl.ds(pl.multiple_of(row, 16), count)], target, fetch_sem.at[9 + u]
                ).start()

    def spread_copy(u, k):
        own = out_ref.at[lines(own_group(u) * GROUP, sizes[u])]
        return pltpu.make_async_remote_copy(
            src_ref=own,
            dst_ref=own,
            send_sem=spread_send.at[u, k],
            recv_sem=spread_recv.at[u, k],
            device_id=(far[k - 1],),
            device_id_type=MESH,
        )

    def own_block(u):
        size = sizes[u]
        for k in range(1, 4):
            line_copy(u, k).wait_recv()
        here = pl.ds(starts[u], size)
        low_sum = functools.reduce(
            lambda a, b: a + b,
            [line_in[pl.ds(4 * starts[u] + t * size, size), :].astype(f32) for t in range(4)],
        ).astype(low)
        sum_low[here, :] = low_sum
        total[here, :] = low_sum.astype(f32)
        target = own_weight.at[pl.ds(starts[u] // 4, 16 * units[u][1])]
        pltpu.make_async_copy(target, target, fetch_sem.at[9 + u]).wait()
        matrices = units[u][4]
        scale = jnp.where(core == 0, scales[matrices[0]], scales[matrices[1]])
        for m in range(units[u][1]):
            row = starts[u] // 4 + 16 * m
            for part in (0, 8):
                for q in range(4):
                    summed = total[pl.ds(row * 4 + 16 * q + part, 8), :]
                    old = own_weight[pl.ds(row + part, 8), 128 * q : 128 * (q + 1)]
                    fresh = old - scale * jnp.tanh(summed * root)
                    flat_rows(row + part, q, fresh, new_flat)
        out_ref[lines(own_group(u) * GROUP, size), :] = new_flat[here, :].astype(low)
        for k in (3, 2, 1):
            spread_copy(u, k).start()
        pass_on(u)

    def piece(rows, u, stage, partner):
        return send(
            out_ref.at[rows], out_ref.at[rows], ag_send.at[u, stage], ag_recv.at[u, stage], partner
        )

    def gather_one(u):
        for k in range(1, 4):
            spread_copy(u, k).wait_recv()
        first, second, _, flip_second = places(u)
        size = 4 * sizes[u]
        start = unit_start(u, core) + (2 * first + second) * size
        return piece(lines(start, size), u, 0, flip_second)

    def gather_two(u, copy):
        copy.wait()
        first, _, flip_first, _ = places(u)
        size = 8 * sizes[u]
        return piece(lines(unit_start(u, core) + first * size, size), u, 1, flip_first)

    def gather_three(u, copy):
        copy.wait()
        pl.semaphore_wait(free_sem.at[u], 1)
        return piece(lines(unit_start(u, core), 16 * sizes[u]), u, 2, flip_core)

    def renew(row, at_row):
        scale = scale_of(at_row, [scales[k] for k in range(3)], edges)
        for part in (0, 8):
            for q in range(4):
                summed = total[pl.ds(row * 4 + 16 * q + part, 8), :]
                old = weight[pl.ds(row + part, 8), 128 * q : 128 * (q + 1)]
                fresh = old - scale * jnp.tanh(summed * root)
                flat_rows(row + part, q, summed, vote_flat)
                flat_rows(row + part, q, fresh, new_flat)

    valid_column = column_of(valid_ref[...].astype(f32), slots)
    weight_slot = jnp.broadcast_to(valid_column, (slots, width))
    weight_band = jnp.concatenate([weight_slot] * side, axis=0)

    cast_weight(grad_one, low_one, square, 9, in_width, fetch_one)
    scales[0] = scale_from(square[...], grad_one.size)
    cast_weight(grad_short, low_short, square, 1, in_width, fetch_short)
    scales[2] = scale_from(square[...], grad_short.size)
    for fetch in fetch_two:
        fetch.start()
    for k in range(OWN // PIECE):
        fetch_rows(first_row + k * PIECE, PIECE, k * PIECE, fetch_sem.at[7])
    fetch_rows(first_row + OWN, TAIL, OWN, fetch_sem.at[8])
    for u in range(len(units)):
        own_fetch(u)

    def image_taps(j):
        pieces = []
        for b in range(3):
            column = j if b else j - 1
            if column < 0:
                continue
            across = 0 if b == 1 else 1
            for a in range(3):
                if a == 1:
                    piece = xs[across, column, 0].reshape(band, in_width)
                elif a == 2:
                    piece = xs[across, column, 1].reshape(band, in_width)
                else:
                    piece = xs[across, column, 1, : side - 1].reshape(band - slots, in_width)
                    piece = jnp.concatenate([jnp.zeros((slots, in_width), low), piece], axis=0)
                pieces.append(piece)
        return jnp.concatenate(pieces, axis=1)

    def moments(values):
        weighted = values * weight_band
        return (
            jnp.sum(weighted, axis=0, keepdims=True),
            jnp.sum(weighted * values, axis=0, keepdims=True),
        )

    def add_up(old, new):
        return [a + b for a, b in zip(old, new)]

    none = jnp.zeros((1, width), f32)
    main_sums, side_sums = [none, none], [none, none]
    for j in range(side):
        here = pl.ds(j * band, band)
        low_rows = low_one[3 if j == 0 else 0 :].reshape(-1, width)
        value = jnp.dot(image_taps(j), low_rows, preferred_element_type=f32)
        main_pre[here, :] = value
        main_sums = add_up(main_sums, moments(value))
        value = jnp.dot(
            xs[0, j, 0].reshape(band, in_width), low_short[0], preferred_element_type=f32
        )
        side_pre[here, :] = value
        side_sums = add_up(side_sums, moments(value))

    count = jnp.broadcast_to(jnp.sum(valid_column, axis=0, keepdims=True), (1, width))
    pl.semaphore_wait(barrier, len(others))
    copies = exchange_start(
        0, pack_rows(main_sums + side_sums + [count])
    )
    cast_weight(grad_two, low_two, square, 9, width, fetch_two)
    scales[1] = scale_from(square[...], grad_two.size)
    copies = exchange_middle(0, copies)
    for across in range(2):
        for down in range(2):
            for j in range(side):
                block = xs[across, j, down].reshape(band, in_width)
                xs_t[across, down, :, j * band : (j + 1) * band] = block.T
    border = jnp.zeros((side, 1, slots, width), low)
    active[:, 0:1] = border
    active[:, side + 1 :] = border
    back_two[:, 0:1] = border
    back_two[:, side + 1 :] = border
    back_one[:, side:] = border
    head_pad[...] = jnp.zeros_like(head_pad)
    head_pad[:classes, :] = head_ref[...]
    head = head_pad[:16, :]
    scales[3] = scale_from(head * head, head_ref.size)
    params = norm_ref[...]
    scales[4] = scale_from(params * params, norm_ref.size)
    sums = exchange_end(0, copies)
    sums = [unpack_row(sums, k) for k in range(5)]

    valid_count = sums[4]
    count_ref[...] = valid_count[:, :1]
    denominator = jnp.maximum(valid_count, 1.0)
    pixels = denominator * pixel_count
    gains = [norm_ref[k : k + 1, :] for k in range(6)]
    mean_one, inv_one, slope_one, base_one = settle_rows(
        (sums[0], sums[1]), pixels, gains[0], gains[1]
    )
    mean_side, inv_side, slope_side, base_side = settle_rows(
        (sums[2], sums[3]), pixels, gains[4], gains[5]
    )

    for j in range(side):
        hidden = main_pre[pl.ds(j * band, band), :] * slope_one + base_one
        active[j, 1 : side + 1] = (
            (hidden * gate(hidden)).astype(low).reshape(side, slots, width)
        )
    two_sums = [none, none]
    for j in range(side):
        taps = [b for b in range(3) if 0 <= j + b - 1 < side]
        pieces = [
            active[j + b - 1, a : a + side].reshape(band, width) for b in taps for a in range(3)
        ]
        low_rows = low_two[3 * taps[0] : 3 * taps[-1] + 3].reshape(-1, width)
        value = jnp.dot(jnp.concatenate(pieces, axis=1), low_rows, preferred_element_type=f32)
        main_two[pl.ds(j * band, band), :] = value
        two_sums = add_up(two_sums, moments(value))
    copies = exchange_start(1, pack_rows(two_sums))
    for j in range(side):
        block = active[j, 1 : side + 1].reshape(band, width)
        active_t[:, j * band : (j + 1) * band] = block.T
    copies = exchange_middle(1, copies)
    sums = exchange_end(1, copies)
    sums = [unpack_row(sums, k) for k in range(2)]
    mean_two, inv_two, slope_two, base_two = settle_rows(
        (sums[0], sums[1]), pixels, gains[2], gains[3]
    )

    base_joined = base_two + base_side

    def joined_of(here):
        return main_two[here, :] * slope_two + side_pre[here, :] * slope_side + base_joined

    pooled = jnp.zeros((slots, width), f32)
    for p in range(pixel_count):
        joined = joined_of(pl.ds(p * slots, slots))
        pooled = pooled + joined * gate(joined)
    pooled = (pooled / pixel_count).astype(low)
    head_low = head_pad[...].astype(low)
    logits = lax.dot_general(
        pooled, head_low, (((1,), (1,)), ((), ())), preferred_element_type=f32
    )
    lane = lax.broadcasted_iota(jnp.int32, logits.shape, 1)
    real = lane < classes
    largest = jnp.max(jnp.where(real, logits, -jnp.inf), axis=1, keepdims=True)
    powers = jnp.where(real, jnp.exp(jnp.where(real, logits - largest, 0.0)), 0.0)
    total_power = jnp.sum(powers, axis=1, keepdims=True)
    label_column = column_of(label_ref[...].astype(f32), slots).astype(jnp.int32)
    onehot = jnp.where(lane == label_column, 1.0, 0.0)
    entropy = largest + jnp.log(total_power) - jnp.sum(onehot * logits, axis=1, keepdims=True)
    loss = jnp.sum(entropy * valid_column, axis=0, keepdims=True)
    grad_logits = (
        (powers / total_power - onehot) * (valid_column / denominator[:, :1])
    ).astype(low)
    grad_head = lax.dot_general(
        grad_logits, pooled, (((0,), (0,)), ((), ())), preferred_element_type=f32
    )[:16]
    grad_pooled = jnp.dot(grad_logits, head_low, preferred_element_type=f32) / pixel_count

    gain_two, gain_side, shift_two = none, none, none
    for p in range(pixel_count):
        here = pl.ds(p * slots, slots)
        joined = joined_of(here)
        opened = gate(joined)
        grad = grad_pooled * (opened * (1.0 + joined * (1.0 - opened)))
        shift_two = shift_two + jnp.sum(grad, axis=0, keepdims=True)
        gain_two = gain_two + jnp.sum(
            grad * ((main_two[here, :] - mean_two) * inv_two), axis=0, keepdims=True
        )
        gain_side = gain_side + jnp.sum(
            grad * ((side_pre[here, :] - mean_side) * inv_side), axis=0, keepdims=True
        )
        back_two[p // side, 1 + p % side] = (grad * slope_two).astype(low)
        back_side[here, :] = (grad * slope_side).astype(low)

    for b in range(3):
        first, last = max(0, b - 1), min(side, side + b - 1)
        left = active_t[:, first * band : last * band]
        for a in range(3):
            right = back_two[first - b + 1 : last - b + 1, 2 - a : 2 - a + side]
            grad_two[pl.ds((a * 3 + b) * width, width), :] = jnp.dot(
                left, right.reshape(-1, width), preferred_element_type=f32
            )

    def nothing():
        pass

    def matrix_votes(k, grad, between, after):
        here = pl.ds(k * width, width)
        start = edges[k - 1] if k else 0
        col_new[:, here] = factored_votes(
            grad,
            grad.shape[0],
            start,
            row_ref,
            row_new,
            col_ref[:, here],
            level,
            out_ref,
            start,
            between,
            after,
        )

    in_flight = {}
    steps = (
        lambda u, copy: scatter_start(u),
        scatter_one,
        scatter_two,
        scatter_three,
        lambda u, copy: own_block(u),
        lambda u, copy: gather_one(u),
        gather_two,
        gather_three,
    )

    def go(number, u):
        in_flight[u] = steps[number](u, in_flight.get(u))

    def turn(number):
        for step_number, u in SCHEDULE[number]:
            go(step_number, u)

    early = edges[1] // 512 - edges[0] // 512
    matrix_votes(1, grad_two, (nothing, nothing), lambda k: go(0, k))
    turn(0)
    grad_short[...] = jnp.dot(xs_t[0, 0], back_side[...], preferred_element_type=f32)
    matrix_votes(2, grad_short, (nothing, nothing), lambda k: None)

    gain_one, shift_one = none, none
    for j in range(side):
        taps = [b for b in range(3) if 0 <= j - b + 1 < side]
        pieces = [
            back_two[j - b + 1, 2 - a : 2 - a + side].reshape(band, width)
            for b in taps
            for a in range(3)
        ]
        weights = jnp.concatenate([low_two[b * 3 + a] for b in taps for a in range(3)], axis=1)
        grad = lax.dot_general(
            jnp.concatenate(pieces, axis=1),
            weights,
            (((1,), (1,)), ((), ())),
            preferred_element_type=f32,
        )
        before = main_pre[pl.ds(j * band, band), :]
        hidden = before * slope_one + base_one
        opened = gate(hidden)
        grad = grad * (opened * (1.0 + hidden * (1.0 - opened)))
        shift_one = shift_one + jnp.sum(grad, axis=0, keepdims=True)
        gain_one = gain_one + jnp.sum(
            grad * ((before - mean_one) * inv_one), axis=0, keepdims=True
        )
        back_one[j, :side] = (grad * slope_one).astype(low).reshape(side, slots, width)
        turn(1 + j)

    square_head = grad_head * grad_head + EPS_ROW
    real = lax.broadcasted_iota(jnp.int32, square_head.shape, 0) < classes
    square_head = jnp.where(real, square_head, 0.0)
    head_lanes = pl.ds(edges[2], width)
    old = row_ref[:, head_lanes]
    row = keep * old + (1.0 - keep) * jnp.sum(square_head, axis=0, keepdims=True) / classes
    row_new[:, head_lanes] = row
    diagonal = eye_mask(16, classes)
    old = jnp.broadcast_to(col_ref[:, 3 * width :], (16, classes))
    old = jnp.sum(jnp.where(diagonal, old, 0.0), axis=1, keepdims=True)
    column = keep * old + (1.0 - keep) * jnp.sum(square_head, axis=1, keepdims=True) / width
    col_new[:, 3 * width :] = jnp.sum(
        jnp.where(diagonal, jnp.broadcast_to(column, (16, classes)), 0.0), axis=0, keepdims=True
    )
    real_column = lax.broadcasted_iota(jnp.int32, column.shape, 0) < classes
    column = jnp.where(real_column, column, 1.0)
    mean = jnp.sum(row, axis=1, keepdims=True) / width
    raw = grad_head * (lax.rsqrt(row) * jnp.sqrt(mean)) * lax.rsqrt(column)
    clip = jnp.maximum(1.0, jnp.sqrt(total_of(raw * raw) / (classes * width)))
    head_votes = jnp.tanh(raw / clip)[:classes]

    raws = []
    for k, grad in enumerate((gain_one, shift_one, gain_two, shift_two, gain_side, shift_two)):
        here = pl.ds(k * width, width)
        moment = keep * moment_ref[:, here] + (1.0 - keep) * (grad * grad + EPS_ROW)
        moment_new[:, here] = moment
        raws.append(grad * lax.rsqrt(moment))
    raw = jnp.concatenate(raws, axis=0)
    clip = jnp.maximum(1.0, jnp.sqrt(total_of(raw * raw) / raw.size))
    norm_votes = jnp.tanh(raw / clip)
    tail_votes = jnp.concatenate([head_votes, norm_votes], axis=0)
    copies = exchange_start(
        2,
        jnp.concatenate(
            [tail_votes[:, 128 * q : 128 * (q + 1)] for q in range(4)]
            + [jnp.broadcast_to(loss, (8, 128))],
            axis=0,
        ),
    )


    for b in range(3):
        first, last = (0, side - 1) if b == 0 else (0, side)
        shift = 1 if b == 0 else 0
        for a in range(3):
            left = xs_t[0 if b == 1 else 1, 0 if a == 1 else 1, :, first * band : last * band]
            start = 1 if a == 0 else 0
            right = back_one[first + shift : last + shift, start : start + side]
            grad_one[pl.ds((a * 3 + b) * in_width, in_width), :] = jnp.dot(
                left, right.reshape(-1, width), preferred_element_type=f32
            )
        if b == 1:
            copies = exchange_middle(2, copies)
        turn(5 + b)

    matrix_votes(
        0,
        grad_one,
        (lambda: turn(8), lambda: turn(9)),
        lambda k: go(0, early + k),
    )
    last_turn = SCHEDULE[10]
    cut = [k for k, (number, _) in enumerate(last_turn) if number == 4][-1] + 1
    ending = len(last_turn) - 3
    for number, u in last_turn[:cut]:
        go(number, u)

    sums = exchange_end(2, copies)
    loss_ref[...] = sums[4 * TAIL : 4 * TAIL + 1, :1]
    old = jnp.concatenate([head_ref[...], norm_ref[...]], axis=0)
    is_head = lax.broadcasted_iota(jnp.int32, (TAIL, width), 0) < classes
    scale = jnp.where(is_head, scales[3], scales[4])
    sums = jnp.concatenate([sums[TAIL * q : TAIL * (q + 1)] for q in range(4)], axis=1)
    fresh = old - scale * jnp.tanh(sums * root)
    both = jnp.concatenate([sums, fresh], axis=0)
    high = both.astype(low)
    rest = both - high.astype(f32)
    middle = rest.astype(low)
    parts = jnp.concatenate([high, middle, (rest - middle.astype(f32)).astype(low)], axis=0)

    flat_sums, flat_new = [], []
    window = 256
    for q in range(classes):
        start = min(q * width // classes // 128 * 128, width - window)
        down = lax.broadcasted_iota(jnp.int32, (window, width), 0)
        across = lax.broadcasted_iota(jnp.int32, (window, width), 1)
        gap = across - classes * down + (q * width - classes * start)
        chosen = jnp.where(jnp.logical_and(gap >= 0, gap < classes), 1.0, 0.0).astype(low)
        moved = jnp.dot(parts[:, start : start + window], chosen, preferred_element_type=f32)
        moved = moved[: 2 * TAIL] + moved[2 * TAIL : 4 * TAIL] + moved[4 * TAIL :]
        spot_of = lax.broadcasted_iota(jnp.int32, (TAIL, width), 1).astype(f32) + q * width
        class_of = spot_of - classes * jnp.floor((spot_of + 0.5) / classes)
        here = lax.broadcasted_iota(jnp.int32, (TAIL, width), 0).astype(f32) == class_of
        flat_sums.append(jnp.sum(jnp.where(here, moved[:TAIL], 0.0), axis=0, keepdims=True))
        flat_new.append(jnp.sum(jnp.where(here, moved[TAIL:], 0.0), axis=0, keepdims=True))
    flat_sums = jnp.concatenate(flat_sums + [sums[classes:]], axis=0)
    flat_new = jnp.concatenate(flat_new + [fresh[classes:]], axis=0)

    for number, u in last_turn[cut:ending]:
        go(number, u)

    mine = [own_group(u) for u in range(len(units))]
    for slot in range(spare + 1):
        group = me * spare + slot
        own = group < 0
        for u, unit in enumerate(units):
            inside = jnp.logical_and(group >= mine[u], group < mine[u] + unit[1])
            own = jnp.logical_or(own, inside)

        @pl.when(jnp.logical_and(jnp.logical_not(own), group < groups - 1))
        def _():
            land(0, group, me, slot, 0)[0].wait_recv()

    pltpu.make_async_copy(
        weight.at[pl.ds(0, OWN)], weight.at[pl.ds(0, OWN)], fetch_sem.at[7]
    ).wait()
    total[pl.ds(0, SPAN), :] = landed[pl.ds(0, SPAN), :].astype(f32)

    @pl.loop(0, OWN // 16)
    def _(k):
        row = pl.multiple_of(k * 16, 16)
        renew(row, first_row + row)

    @pl.when(me < 31)
    def _():
        pltpu.make_async_copy(
            weight.at[pl.ds(OWN, TAIL)], weight.at[pl.ds(OWN, TAIL)], fetch_sem.at[8]
        ).wait()
        total[pl.ds(SPAN, GROUP), :] = landed[pl.ds(SPAN, GROUP), :].astype(f32)
        renew(OWN, first_row + OWN)

    def tail_rows(values, ref):
        for u in (0, 8):
            for q in range(4):
                flat_rows(OWN + u, q, values[u : u + 8, 128 * q : 128 * (q + 1)], ref)

    @pl.when(me == 31)
    def _():
        tail_rows(flat_sums, vote_flat)
        tail_rows(flat_new, new_flat)

    shift = 2 * me
    share = vote_ref.shape[0]
    vote_ref[...] = vote_flat[pl.ds(shift, share), :]
    new_ref[...] = new_flat[pl.ds(shift, share), :]
    tail_rows(flat_new, new_flat)
    out_ref[pl.ds(32 * SPAN, GROUP), :] = new_flat[pl.ds(SPAN, GROUP), :].astype(low)

    for number, u in last_turn[ending:]:
        go(number, u)
    for u in range(len(units)):
        in_flight[u].wait()
        for k in range(1, 4):
            line_copy(u, k).wait_send()
            spread_copy(u, k).wait_send()
    for away, copy in passes:

        @pl.when(away)
        def _():
            copy.wait_send()


def finish_kernel(count, chunks, *refs):
    sources, targets, sem = refs[:count], refs[count : 2 * count], refs[2 * count]
    rows = sources[0].shape[0]
    step = -(-rows // chunks // 16) * 16
    copies = []
    for k in range(chunks):
        here = pl.ds(k * step, min(step, rows - k * step))
        copies.append(
            pltpu.make_async_copy(sources[0].at[here], targets[0].at[here], sem.at[k])
        )
    for k in range(1, count - 2):
        copies.append(pltpu.make_async_copy(sources[k], targets[k], sem.at[chunks + k]))
    for copy in copies:
        copy.start()
    for k in (count - 2, count - 1):
        targets[k][...] = sources[k][...]
    for copy in copies:
        copy.wait()


def finish(values):
    vmem = pl.BlockSpec(memory_space=pltpu.VMEM)
    hbm = pl.BlockSpec(memory_space=pl.ANY)
    count, chunks = len(values), 8
    held = [pltpu.with_memory_space_constraint(value, pltpu.VMEM) for value in values[:-2]]
    return pl.pallas_call(
        functools.partial(finish_kernel, count, chunks),
        out_shape=[jax.ShapeDtypeStruct(value.shape, value.dtype) for value in values],
        in_specs=[vmem] * count,
        out_specs=[hbm] * (count - 2) + [vmem] * 2,
        scratch_shapes=[pltpu.SemaphoreType.DMA((chunks + count,))],
        compiler_params=pltpu.CompilerParams(vmem_limit_bytes=1024 * 1024),
        name="finish",
    )(*held, *values[-2:])


def run_step(images, conv_one, conv_two, shortcut, head, norm_params, valid, labels, rows, cols, moment):
    vmem = pl.BlockSpec(memory_space=pltpu.VMEM)
    hbm = pl.BlockSpec(memory_space=pl.ANY)
    low, f32 = jnp.bfloat16, jnp.float32
    dma = pltpu.SemaphoreType.DMA
    workers = lax.axis_size("dp")
    slots, in_width = valid.shape[1], images.shape[1]
    width = conv_one.shape[1]
    pixels = images.shape[0] // 4
    shape = pltpu.VMEM
    edges = [conv_one.shape[0]]
    edges.append(edges[0] + conv_two.shape[0])
    edges.append(edges[1] + shortcut.shape[0])
    units = make_units(edges)
    flat = (edges[2] + TAIL) * width // 128
    share = flat // workers
    return pl.pallas_call(
        functools.partial(step_kernel, tuple(edges), tuple(units), 1.0 / math.sqrt(workers)),
        out_shape=(
            shape((share, 128), f32),
            shape((share, 128), f32),
            shape((flat, 128), low),
            shape(rows.shape, f32),
            shape(cols.shape, f32),
            shape(moment.shape, f32),
            jax.ShapeDtypeStruct((1, 1), f32),
            jax.ShapeDtypeStruct((1, 1), f32),
        ),
        in_specs=[hbm] * 4 + [vmem] * 7,
        out_specs=(vmem,) * 8,
        scratch_shapes=[
            pltpu.VMEM((2, 4, 2, 4, slots, in_width), low),
            pltpu.VMEM(conv_one.shape, f32),
            pltpu.VMEM(conv_two.shape, f32),
            pltpu.VMEM(shortcut.shape, f32),
            pltpu.VMEM((9, in_width, width), low),
            pltpu.VMEM((9, width, width), low),
            pltpu.VMEM((1, in_width, width), low),
            pltpu.VMEM((pixels, width), f32),
            pltpu.VMEM((pixels, width), f32),
            pltpu.VMEM((pixels, width), f32),
            pltpu.VMEM((4, 6, slots, width), low),
            pltpu.VMEM((4, 6, slots, width), low),
            pltpu.VMEM((4, 5, slots, width), low),
            pltpu.VMEM((pixels, width), low),
            pltpu.VMEM((width, pixels), low),
            pltpu.VMEM((2, 2, in_width, pixels), low),
            pltpu.VMEM((128, width), f32),
            pltpu.VMEM((conv_two.shape[0], 128), f32),
            pltpu.VMEM((8, width), f32),
            pltpu.VMEM((24, 128), f32),
            pltpu.VMEM((8, 24, 128), f32),
            pltpu.VMEM((4, 24, 128), f32),
            pltpu.VMEM((8, 128), f32),
            pltpu.VMEM((8, 8, 128), f32),
            pltpu.VMEM((4, 8, 128), f32),
            pltpu.VMEM((GROUP + 8, 128), f32),
            pltpu.VMEM((8, GROUP + 8, 128), f32),
            pltpu.VMEM((4, GROUP + 8, 128), f32),
            pltpu.VMEM((16 * SPAN, 128), low),
            pltpu.VMEM((8 * SPAN, 128), low),
            pltpu.VMEM((4 * SPAN, 128), low),
            pltpu.VMEM((4 * SPAN, 128), low),
            pltpu.VMEM((SPAN, 128), low),
            pltpu.VMEM((SPAN + GROUP, 128), low),
            pltpu.VMEM((SPAN + GROUP, 128), f32),
            pltpu.VMEM((OWN, width), f32),
            pltpu.VMEM((OWN + TAIL, width), f32),
            pltpu.VMEM((SPAN + GROUP, 128), f32),
            pltpu.VMEM((SPAN + GROUP, 128), f32),
            dma((9 + len(units),)),
            dma((3, 10)),
            dma((3, 10)),
            dma((len(units), 3)),
            dma((len(units), 3)),
            dma((len(units), 4)),
            dma((len(units), 4)),
            dma((2 * OWN // 16,)),
            dma((OWN // 16 + 1,)),
            dma((len(units), 4)),
            dma((len(units), 4)),
            dma((len(units), 3)),
            dma((len(units), 3)),
            pltpu.SemaphoreType.REGULAR((len(units),)),
            dma((2,)),
        ],
        compiler_params=pltpu.CompilerParams(
            collective_id=1, has_side_effects=True, vmem_limit_bytes=54 * 1024 * 1024
        ),
        name="step",
    )(images, conv_one, conv_two, shortcut, head, norm_params, valid, labels, rows, cols, moment)


def scale_for(weight):
    return jnp.maximum(EPS_SCALE, jnp.sqrt(jnp.mean(weight * weight)))


def local_general(
    images,
    valid_slot,
    labels,
    conv_one,
    conv_two,
    shortcut,
    classifier,
    norm_params,
    row_state,
    col_state,
    bn_moment,
):
    in_width = images.shape[3]
    width = conv_one.shape[1]
    kernel_one = conv_one.astype(jnp.bfloat16).reshape(3, 3, in_width, width)
    kernel_two = conv_two.astype(jnp.bfloat16).reshape(3, 3, width, width)
    kernel_short = shortcut.astype(jnp.bfloat16).reshape(1, 1, in_width, width)
    head_low = classifier.astype(jnp.bfloat16)
    slot_count = images.shape[0]
    out_side = images.shape[1] // 2
    pixel_count = out_side * out_side
    slot_weight = valid_slot.astype(jnp.float32)
    pixel_weight = jnp.broadcast_to(slot_weight[:, None], (slot_count, pixel_count)).reshape(-1, 1)
    main_pre, side_pre = first_section(images, kernel_one, kernel_short)
    main_sums = masked_moments(pixel_weight, main_pre)
    side_sums = masked_moments(pixel_weight, side_pre)
    count_row = jnp.broadcast_to(jnp.sum(slot_weight), (width,))
    first_sums = lax.psum(jnp.stack([*main_sums, *side_sums, count_row]), "dp")
    valid_count = first_sums[4, 0]
    denominator = jnp.maximum(valid_count, 1.0)
    pixels = denominator * pixel_count
    norm_one = settle(first_sums[0], first_sums[1], pixels)
    norm_side = settle(first_sums[2], first_sums[3], pixels)
    hidden_one, active, main_two = second_section(
        main_pre, norm_one, norm_params, kernel_two, slot_count, out_side
    )
    two_sums = masked_moments(pixel_weight, main_two)
    second_sums = lax.psum(jnp.stack([*two_sums]), "dp")
    norm_two = settle(second_sums[0], second_sums[1], pixels)
    joined_pre = (
        (main_two - norm_two[0]) * norm_two[1] * norm_params[2]
        + norm_params[3]
        + (side_pre - norm_side[0]) * norm_side[1] * norm_params[4]
        + norm_params[5]
    )
    joined = jax.nn.silu(joined_pre).reshape(slot_count, pixel_count, -1)
    pooled = jnp.mean(joined, axis=1).astype(jnp.bfloat16)
    logits = jnp.dot(pooled, head_low, preferred_element_type=jnp.float32)
    largest = jnp.max(logits, axis=1, keepdims=True)
    exp_terms = jnp.exp(logits - largest)
    total_exp = jnp.sum(exp_terms, axis=1, keepdims=True)
    log_total = largest[:, 0] + jnp.log(total_exp[:, 0])
    onehot = (labels[:, None] == jnp.arange(logits.shape[1], dtype=jnp.int32)[None, :]).astype(
        jnp.float32
    )
    local_sum = jnp.sum(slot_weight * (log_total - jnp.sum(onehot * logits, axis=1)))
    grad_logits = ((exp_terms / total_exp - onehot) * (slot_weight / denominator)[:, None]).astype(
        jnp.bfloat16
    )
    grad_head = lax.dot_general(
        pooled, grad_logits, (((0,), (0,)), ((), ())), preferred_element_type=jnp.float32
    )
    grad_pooled = lax.dot_general(
        grad_logits, head_low, (((1,), (1,)), ((), ())), preferred_element_type=jnp.float32
    )
    spread_pooled = jnp.broadcast_to(
        (grad_pooled / pixel_count)[:, None, :], (slot_count, pixel_count, width)
    )
    grad_joined = spread_pooled.reshape(slot_count * pixel_count, width) * silu_slope(joined_pre)
    gain_two, shift_two, grad_two = norm_backward(grad_joined, main_two, norm_two, norm_params[2])
    gain_side, shift_side, grad_side = norm_backward(
        grad_joined, side_pre, norm_side, norm_params[4]
    )
    grad_two_maps = grad_two.reshape(slot_count, out_side, out_side, width)
    grad_side_maps = grad_side.reshape(slot_count, out_side, out_side, width)
    grad_conv_two = conv_weight_grad(active, grad_two_maps, 1, 1, 1)
    grad_short = conv_weight_grad(images, grad_side_maps, 2, 0, -1)
    kernel_turned = jnp.transpose(kernel_two[::-1, ::-1], (0, 1, 3, 2))
    grad_active = conv_apply(grad_two_maps, kernel_turned, 1, 1).reshape(
        slot_count * pixel_count, width
    )
    grad_hidden = grad_active * silu_slope(hidden_one)
    gain_one, shift_one, grad_one = norm_backward(grad_hidden, main_pre, norm_one, norm_params[0])
    grad_conv_one = conv_weight_grad(
        images, grad_one.reshape(slot_count, out_side, out_side, width), 2, 1, 0
    )
    grad_norms = jnp.stack([gain_one, shift_one, gain_two, shift_two, gain_side, shift_side])
    grads = (grad_conv_one, grad_conv_two, grad_short, grad_head, grad_norms)
    votes, rows_new, cols_new, moment_new = make_votes(
        grads, row_state[0], col_state[0], bn_moment[0]
    )
    workers = lax.axis_size("dp")
    weights = (conv_one, conv_two, shortcut, classifier, norm_params)
    scales = [scale_for(weight) for weight in weights]
    loss_sum = lax.psum(local_sum, "dp")
    flat_vote = jnp.concatenate([vote.reshape(-1) for vote in votes])
    flat_old = jnp.concatenate([weight.reshape(-1) for weight in weights])
    flat_scale = jnp.concatenate(
        [
            jnp.broadcast_to(scale, (weight.size,))
            for scale, weight in zip(scales, weights)
        ]
    )
    vote_mine = lax.psum_scatter(flat_vote, "dp", tiled=True)
    share = vote_mine.shape[0]
    start = lax.axis_index("dp") * share
    new_mine = lax.dynamic_slice_in_dim(
        flat_old, start, share
    ) - lax.dynamic_slice_in_dim(flat_scale, start, share) * jnp.tanh(
        vote_mine / math.sqrt(workers)
    )
    copies = lax.all_gather(new_mine.astype(jnp.bfloat16), "dp", tiled=True)
    return (
        loss_sum,
        valid_count,
        new_mine,
        copies,
        vote_mine,
        rows_new[None, :],
        cols_new[None, :],
        moment_new[None, :],
    )


def local(
    images,
    valid_slot,
    labels,
    conv_one,
    conv_two,
    shortcut,
    classifier,
    norm_params,
    row_state,
    col_state,
    bn_moment,
):
    new_mine, vote_mine, copies, rows_new, cols_new, moment_new, loss_sum, valid_count = run_step(
        images.reshape(-1, images.shape[-1]),
        conv_one,
        conv_two,
        shortcut,
        classifier.T,
        norm_params,
        valid_slot.reshape(1, -1),
        labels.reshape(1, -1),
        row_state,
        col_state,
        bn_moment,
    )
    copies, new_mine, vote_mine, rows_new, cols_new, moment_new, loss_sum, valid_count = finish(
        (copies, new_mine, vote_mine, rows_new, cols_new, moment_new, loss_sum, valid_count)
    )
    return (
        loss_sum.reshape(()),
        valid_count.reshape(()),
        new_mine.reshape(-1),
        copies.reshape(-1),
        vote_mine.reshape(-1),
        rows_new,
        cols_new,
        moment_new,
    )


def solution(mesh):
    placed = (
        P("dp", None, None, None),
        P("dp"),
        P("dp"),
        P(),
        P(),
        P(),
        P(),
        P(),
        P("dp", None),
        P("dp", None),
        P("dp", None),
    )
    return jax.shard_map(
        local if mesh.shape["dp"] == 32 else local_general,
        mesh=mesh,
        in_specs=placed,
        out_specs=(P(), P(), P("dp"), P(), P("dp"), P("dp", None), P("dp", None), P("dp", None)),
        check_vma=False,
    )
```

```python
import functools
import math

import jax
import jax.numpy as jnp
from jax import lax
from jax.experimental import pallas as pl
from jax.experimental.pallas import tpu as pltpu
from jax.sharding import PartitionSpec as P

STEP = 10
MESH = pl.DeviceIdType.MESH

EPS_NORM = 1e-05
EPS_ROW = 1e-30
EPS_SCALE = 0.001
FORWARD_DIMS = ("NHWC", "HWIO", "NHWC")
WEIGHT_DIMS = ("CHWN", "IHWO", "HWNC")
OWN = 224
TAIL = 16
PIECE = 32
SPAN = 4 * OWN
HALF = SPAN // 2
GROUP = 64


def conv_apply(maps, kernel, stride, margin):
    return lax.conv_general_dilated(
        maps,
        kernel,
        (stride, stride),
        ((margin, margin), (margin, margin)),
        dimension_numbers=FORWARD_DIMS,
        preferred_element_type=jnp.float32,
    )


def conv_weight_grad(maps, grad_out, stride, low_pad, high_pad):
    result = lax.conv_general_dilated(
        maps,
        grad_out,
        (1, 1),
        ((low_pad, high_pad), (low_pad, high_pad)),
        rhs_dilation=(stride, stride),
        dimension_numbers=WEIGHT_DIMS,
        preferred_element_type=jnp.float32,
    )
    return result.reshape(-1, result.shape[3])


def silu_slope(values):
    sigmoid_part = jax.nn.sigmoid(values)
    return sigmoid_part * (1.0 + values * (1.0 - sigmoid_part))


def settle(sum_plain, sum_square, pixels):
    mean_value = sum_plain / pixels
    return (mean_value, lax.rsqrt(sum_square / pixels - mean_value * mean_value + EPS_NORM))


def first_section(images, kernel_one, kernel_short):
    row_count = images.shape[0] * (images.shape[1] // 2) ** 2
    main_pre = conv_apply(images, kernel_one, 2, 1).reshape(row_count, -1)
    side_pre = conv_apply(images, kernel_short, 2, 0).reshape(row_count, -1)
    return (main_pre, side_pre)


def second_section(main_pre, norm_one, norm_params, kernel_two, slot_count, out_side):
    hidden_one = (main_pre - norm_one[0]) * norm_one[1] * norm_params[0] + norm_params[1]
    active = (
        jax.nn.silu(hidden_one).astype(jnp.bfloat16).reshape(slot_count, out_side, out_side, -1)
    )
    main_two = conv_apply(active, kernel_two, 1, 1).reshape(slot_count * out_side * out_side, -1)
    return (hidden_one, active, main_two)


def masked_moments(pixel_weight, values):
    return (jnp.sum(pixel_weight * values, axis=0), jnp.sum(pixel_weight * values * values, axis=0))


def soft_sign(step_raw):
    clip_by = jnp.maximum(1.0, jnp.sqrt(jnp.mean(step_raw * step_raw)))
    return jnp.tanh(step_raw / clip_by)


def make_votes(grads, rows_old, cols_old, moment_old):
    decay_rate = 1.0 - STEP ** (-0.8)
    votes, rows_new, cols_new = ([], [], [])
    row_at, col_at = (0, 0)
    for matrix in grads[:4]:
        row_size, col_size = matrix.shape
        square = matrix * matrix + EPS_ROW
        row_part = decay_rate * rows_old[row_at : row_at + row_size] + (
            1.0 - decay_rate
        ) * jnp.mean(square, axis=1)
        col_part = decay_rate * cols_old[col_at : col_at + col_size] + (
            1.0 - decay_rate
        ) * jnp.mean(square, axis=0)
        second = row_part[:, None] * col_part[None, :] / jnp.mean(row_part)
        votes.append(soft_sign(matrix * lax.rsqrt(second)))
        rows_new.append(row_part)
        cols_new.append(col_part)
        row_at += row_size
        col_at += col_size
    flat_norm = grads[4].reshape(-1)
    moment_new = decay_rate * moment_old + (1.0 - decay_rate) * (flat_norm * flat_norm + EPS_ROW)
    votes.append(soft_sign(flat_norm * lax.rsqrt(moment_new)))
    return (votes, jnp.concatenate(rows_new), jnp.concatenate(cols_new), moment_new)


def norm_backward(grad_out, pre_value, norm_pair, gain_row):
    normed = (pre_value - norm_pair[0]) * norm_pair[1]
    grad_gain = jnp.sum(grad_out * normed, axis=0)
    grad_shift = jnp.sum(grad_out, axis=0)
    grad_pre = (grad_out * gain_row * norm_pair[1]).astype(jnp.bfloat16)
    return (grad_gain, grad_shift, grad_pre)


SCHEDULE = (
        (0, 10), (0, 1), (0, 8), (0, 2), (0, 0), (0, 5), (1, 0), (0, 4), (0, 11), (1, 5),
        (0, 13), (0, 7), (1, 2), (1, 8), (1, 1), (0, 3), (1, 4), (0, 6), (0, 9), (0, 12), (1, 3),
        (1, 9), (2, 1), (1, 7), (1, 11), (1, 12), (1, 6), (2, 0), (2, 2), (2, 4), (1, 13),
        (2, 5), (3, 2), (2, 3), (3, 0), (2, 8), (2, 6), (2, 12), (3, 1), (1, 10), (2, 9), (4, 0),
        (3, 3), (4, 1), (3, 5), (3, 9), (2, 7), (4, 3), (5, 0), (2, 11), (3, 4), (4, 5), (5, 1),
        (3, 7), (2, 13), (3, 11), (5, 3), (2, 10), (6, 1), (3, 6), (4, 2), (3, 13), (3, 10),
        (3, 12), (6, 0), (3, 8), (7, 1), (7, 0), (4, 7), (4, 11), (5, 5), (4, 4), (6, 3), (4, 9),
        (7, 3), (6, 5), (4, 13), (4, 10), (5, 2), (5, 7), (5, 9), (7, 5), (5, 4), (6, 2), (6, 4),
        (6, 7), (4, 6), (4, 8), (5, 6), (4, 12), (5, 13), (6, 9), (7, 2), (5, 11), (5, 8),
        (7, 4), (6, 6), (6, 11), (5, 10), (7, 7), (6, 8), (6, 13), (7, 8), (6, 10), (7, 9),
        (7, 6), (5, 12), (7, 13), (7, 11), (7, 10), (6, 12), (7, 12),

)


def place():
    me = lax.axis_index("dp")
    core = lax.rem(me, 2)
    x = lax.rem(lax.div(me, 2), 2)
    y = lax.rem(lax.div(me, 4), 2)
    z = lax.div(me, 8)
    return me, core, x, y, z


def send(src, dst, send_sem, recv_sem, partner):
    copy = pltpu.make_async_remote_copy(
        src_ref=src,
        dst_ref=dst,
        send_sem=send_sem,
        recv_sem=recv_sem,
        device_id=(partner,),
        device_id_type=MESH,
    )
    copy.start()
    return copy


def scale_of(row, scales, edges):
    picked = scales[2]
    picked = jnp.where(row < edges[1], scales[1], picked)
    return jnp.where(row < edges[0], scales[0], picked)


def make_units(edges):
    one, two, short = edges[0] // 16, edges[1] // 16, edges[2] // 16
    units = []
    for k in range((two - one) // 32):
        units.append((one + 32 * k, 1, k % 2 == 0, 16, (1, 1)))
    for k in range(one // 32):
        units.append((32 * k, 1, k % 2 == 1, 16, (0, 0)))
    at = one // 32 * 32
    assert one - at == 16 and short - two == 16
    units.append((at, 1, False, two - at, (0, 2)))
    return units


def settle_rows(sums, pixels, gain, shift):
    mean = sums[0] / pixels
    inv = lax.rsqrt(sums[1] / pixels - mean * mean + EPS_NORM)
    slope = gain * inv
    return mean, inv, slope, shift - mean * slope


def gate(values):
    return 0.5 * jnp.tanh(0.5 * values) + 0.5


def eye_mask(rows, columns, offset=0):
    down = lax.broadcasted_iota(jnp.int32, (rows, columns), 0) + offset
    return down == lax.broadcasted_iota(jnp.int32, (rows, columns), 1)


def column_of(row, size):
    spread = jnp.where(eye_mask(size, size), jnp.broadcast_to(row, (size, size)), 0)
    return jnp.sum(spread, axis=1, keepdims=True)


def total_of(values):
    return jnp.sum(jnp.sum(values, axis=0, keepdims=True), axis=1, keepdims=True)


def fold(values):
    return jnp.sum(values.reshape(values.shape[0] // 8, 8, values.shape[1]), axis=0)


def cast_weight(source, target, square_ref, taps, depth, fetches):
    step = 128
    square_ref[...] = jnp.zeros_like(square_ref)
    for tap in range(taps):
        if tap % (taps // len(fetches)) == 0:
            fetches[tap * len(fetches) // taps].wait()
        new_tap = (tap % 3) * 3 + tap // 3

        @pl.loop(0, depth // step)
        def _(k):
            start = pl.multiple_of(k * step, step)
            values = source[pl.ds(tap * depth + start, step), :]
            target[new_tap, pl.ds(start, step), :] = values.astype(jnp.bfloat16)
            square_ref[...] += fold(values * values)


def factored_votes(grad, rows, row_at, rows_old, rows_new, col_old, level, votes, vote_at):
    width = grad.shape[1]
    keep = 1.0 - STEP ** (-0.8)
    step = 128
    quarters = width // 128

    def first(k, carry):
        col_sum, row_sum = carry
        start = pl.multiple_of(k * step, step)
        lanes = pl.ds(pl.multiple_of(row_at + start, step), step)
        old = rows_old[:, lanes] * keep
        line = jnp.zeros((8, 128), jnp.float32)
        for m in range(step // 8):
            block = grad[pl.ds(start + 8 * m, 8), :]
            square = block * block
            col_sum = col_sum + square
            part = square[:, :128]
            for q in range(1, quarters):
                part = part + square[:, 128 * q : 128 * (q + 1)]
            part = part * ((1.0 - keep) / width)
            diagonal = eye_mask(8, 128, 8 * m)
            part = part + jnp.where(diagonal, jnp.broadcast_to(old, (8, 128)), 0.0)
            row = jnp.sum(part, axis=1, keepdims=True) + (1.0 - keep) * EPS_ROW
            row = jnp.broadcast_to(row, (8, 128))
            level[pl.ds(start + 8 * m, 8), :] = row
            row_sum = row_sum + row
            line = line + jnp.where(diagonal, row, 0.0)
        rows_new[:, lanes] = jnp.sum(line, axis=0, keepdims=True)
        return col_sum, row_sum

    col_sum, row_sum = lax.fori_loop(
        0,
        rows // step,
        first,
        (jnp.zeros((8, width), jnp.float32), jnp.zeros((8, 128), jnp.float32)),
    )
    col_new = keep * col_old + (1.0 - keep) * (
        jnp.sum(col_sum, axis=0, keepdims=True) / rows + EPS_ROW
    )
    scale = lax.rsqrt(col_new)
    root_mean = jnp.sqrt(jnp.sum(row_sum, axis=0, keepdims=True) / rows)

    def second(k, carry):
        start = pl.multiple_of(k * step, step)
        for m in range(step // 8):
            here = pl.ds(start + 8 * m, 8)
            factor = lax.rsqrt(level[here, :]) * root_mean
            level[here, :] = factor
            raw = grad[here, :] * scale
            power = raw * raw
            part = power[:, :128]
            for q in range(1, quarters):
                part = part + power[:, 128 * q : 128 * (q + 1)]
            carry = carry + part * (factor * factor)
        return carry

    power = lax.fori_loop(0, rows // step, second, jnp.zeros((8, 128), jnp.float32))
    clip = jnp.maximum(1.0, jnp.sqrt(total_of(power) / (rows * width)))
    scale = scale / clip

    def third(k, _):
        start = pl.multiple_of(k * step, step)
        for m in range(step // 16):
            here = pl.ds(start + 16 * m, 16)
            factor = level[here, :]
            factor = jnp.concatenate([factor] * quarters, axis=1)
            vote = jnp.tanh(grad[here, :] * factor * scale).astype(jnp.bfloat16)
            at = pl.multiple_of((vote_at + start) * 4 + GROUP * m, GROUP)
            for q in range(quarters):
                votes[pl.ds(at + 16 * q, 16), :] = vote[:, 128 * q : 128 * (q + 1)]
        return 0

    lax.fori_loop(0, rows // step, third, 0)
    return col_new


def worker_kernel(
    edges,
    images,
    one_hbm,
    two_hbm,
    short_hbm,
    head_ref,
    norm_ref,
    valid_ref,
    label_ref,
    row_ref,
    col_ref,
    moment_ref,
    votes_ref,
    tail_ref,
    scale_ref,
    row_new,
    col_new,
    moment_new,
    count_ref,
    xs,
    grad_one,
    grad_two,
    grad_short,
    low_one,
    low_two,
    low_short,
    main_pre,
    side_pre,
    main_two,
    active,
    back_two,
    back_one,
    back_side,
    active_t,
    xs_t,
    head_pad,
    level,
    square,
    image_in,
    post_one,
    plane_one,
    line_one,
    post_two,
    plane_two,
    line_two,
    tail_post,
    tail_plane,
    tail_line,
    fetch_sem,
    small_send,
    small_recv,
    load_sem,
):
    slots, in_width = xs.shape[4:]
    width = main_pre.shape[1]
    side = 4
    band = side * slots
    pixel_count = side * side
    classes = head_ref.shape[0]
    keep = 1.0 - STEP ** (-0.8)
    low = jnp.bfloat16
    f32 = jnp.float32

    me = lax.axis_index("dp")
    z = lax.div(me, 8)
    spot = lax.rem(me, 8)
    near = [z * 8 + lax.rem(spot + k, 8) for k in range(1, 8)]
    far = [lax.rem(z + k, 4) * 8 + spot for k in range(1, 4)]

    count = images.shape[0]
    loads = []
    for half in range(2):
        lanes = slice(128 * half, 128 * (half + 1))
        loads.append(
            pltpu.make_async_copy(
                images.at[:, lanes], image_in.at[pl.ds(half * count, count)], load_sem.at[half]
            )
        )
        loads[half].start()

    def chunks_of(source, target, first, count):
        rows = source.shape[0] // count
        return [
            pltpu.make_async_copy(
                source.at[pl.ds(k * rows, rows)],
                target.at[pl.ds(k * rows, rows)],
                fetch_sem.at[first + k],
            )
            for k in range(count)
        ]

    fetch_one = chunks_of(one_hbm, grad_one, 0, 3)
    fetch_short = chunks_of(short_hbm, grad_short, 3, 1)
    fetch_two = chunks_of(two_hbm, grad_two, 4, 3)
    for fetch in fetch_one + fetch_short:
        fetch.start()
    barrier = pltpu.get_barrier_semaphore()
    for partner in near + far:
        pl.semaphore_signal(barrier, inc=1, device_id=(partner,), device_id_type=MESH)

    for half in range(2):
        lanes = slice(128 * half, 128 * (half + 1))
        loads[half].wait()
        level[:count, :] = image_in[pl.ds(half * count, count), :].astype(f32)
        for h in range(2 * side):
            for w in range(2 * side):
                rows = level[pl.ds(2 * side * h + w, slots, stride=4 * pixel_count), :]
                xs[w % 2, w // 2, h % 2, h // 2, :, lanes] = rows.astype(low)

    scales = {}

    def scale_from(weight_square, size):
        return jnp.maximum(EPS_SCALE, jnp.sqrt(total_of(weight_square) / size))

    exchanges = (
        (post_one, plane_one, line_one),
        (post_two, plane_two, line_two),
        (tail_post, tail_plane, tail_line),
    )

    def exchange_start(which, values):
        mine_ref, plane_ref, _ = exchanges[which]
        mine_ref[...] = values
        plane_ref[spot] = values
        return [
            send(
                mine_ref,
                plane_ref.at[spot],
                small_send.at[which, k],
                small_recv.at[which, k],
                partner,
            )
            for k, partner in enumerate(near)
        ]

    def pack_rows(rows):
        pieces = [row[:, 128 * q : 128 * (q + 1)] for row in rows for q in range(4)]
        pad = -len(pieces) % 8
        if pad:
            pieces.append(jnp.zeros((pad, 128), f32))
        return jnp.concatenate(pieces, axis=0)

    def unpack_row(lines_in, k):
        return jnp.concatenate([lines_in[4 * k + q : 4 * k + q + 1] for q in range(4)], axis=1)

    def exchange_middle(which, copies):
        _, plane_ref, line_ref = exchanges[which]
        for copy in copies:
            copy.wait()
        line_ref[z] = functools.reduce(lambda a, b: a + b, [plane_ref[k] for k in range(8)])
        return [
            send(
                line_ref.at[z],
                line_ref.at[z],
                small_send.at[which, 7 + k],
                small_recv.at[which, 7 + k],
                partner,
            )
            for k, partner in enumerate(far)
        ]

    def exchange_end(which, copies):
        line_ref = exchanges[which][2]
        for copy in copies:
            copy.wait()
        return (line_ref[0] + line_ref[1]) + (line_ref[2] + line_ref[3])

    valid_column = column_of(valid_ref[...].astype(f32), slots)
    weight_slot = jnp.broadcast_to(valid_column, (slots, width))
    weight_band = jnp.concatenate([weight_slot] * side, axis=0)

    cast_weight(grad_one, low_one, square, 9, in_width, fetch_one)
    scales[0] = scale_from(square[...], grad_one.size)
    cast_weight(grad_short, low_short, square, 1, in_width, fetch_short)
    scales[2] = scale_from(square[...], grad_short.size)
    for fetch in fetch_two:
        fetch.start()

    def image_taps(j):
        pieces = []
        for b in range(3):
            column = j if b else j - 1
            if column < 0:
                continue
            across = 0 if b == 1 else 1
            for a in range(3):
                if a == 1:
                    piece = xs[across, column, 0].reshape(band, in_width)
                elif a == 2:
                    piece = xs[across, column, 1].reshape(band, in_width)
                else:
                    piece = xs[across, column, 1, : side - 1].reshape(band - slots, in_width)
                    piece = jnp.concatenate([jnp.zeros((slots, in_width), low), piece], axis=0)
                pieces.append(piece)
        return jnp.concatenate(pieces, axis=1)

    def moments(values):
        weighted = values * weight_band
        return (
            jnp.sum(weighted, axis=0, keepdims=True),
            jnp.sum(weighted * values, axis=0, keepdims=True),
        )

    def add_up(old, new):
        return [a + b for a, b in zip(old, new)]

    none = jnp.zeros((1, width), f32)
    main_sums, side_sums = [none, none], [none, none]
    for j in range(side):
        here = pl.ds(j * band, band)
        low_rows = low_one[3 if j == 0 else 0 :].reshape(-1, width)
        value = jnp.dot(image_taps(j), low_rows, preferred_element_type=f32)
        main_pre[here, :] = value
        main_sums = add_up(main_sums, moments(value))
        value = jnp.dot(
            xs[0, j, 0].reshape(band, in_width), low_short[0], preferred_element_type=f32
        )
        side_pre[here, :] = value
        side_sums = add_up(side_sums, moments(value))

    count = jnp.broadcast_to(jnp.sum(valid_column, axis=0, keepdims=True), (1, width))
    pl.semaphore_wait(barrier, len(near) + len(far))
    copies = exchange_start(
        0, pack_rows(main_sums + side_sums + [count])
    )
    cast_weight(grad_two, low_two, square, 9, width, fetch_two)
    scales[1] = scale_from(square[...], grad_two.size)
    copies = exchange_middle(0, copies)
    for across in range(2):
        for down in range(2):
            for j in range(side):
                block = xs[across, j, down].reshape(band, in_width)
                xs_t[across, down, :, j * band : (j + 1) * band] = block.T
    border = jnp.zeros((side, 1, slots, width), low)
    active[:, 0:1] = border
    active[:, side + 1 :] = border
    back_two[:, 0:1] = border
    back_two[:, side + 1 :] = border
    back_one[:, side:] = border
    head_pad[...] = jnp.zeros_like(head_pad)
    head_pad[:classes, :] = head_ref[...]
    head = head_pad[:16, :]
    scales[3] = scale_from(head * head, head_ref.size)
    params = norm_ref[...]
    scales[4] = scale_from(params * params, norm_ref.size)
    sums = exchange_end(0, copies)
    sums = [unpack_row(sums, k) for k in range(5)]

    valid_count = sums[4]
    count_ref[...] = valid_count[:, :1]
    denominator = jnp.maximum(valid_count, 1.0)
    pixels = denominator * pixel_count
    gains = [norm_ref[k : k + 1, :] for k in range(6)]
    mean_one, inv_one, slope_one, base_one = settle_rows(
        (sums[0], sums[1]), pixels, gains[0], gains[1]
    )
    mean_side, inv_side, slope_side, base_side = settle_rows(
        (sums[2], sums[3]), pixels, gains[4], gains[5]
    )

    for j in range(side):
        hidden = main_pre[pl.ds(j * band, band), :] * slope_one + base_one
        active[j, 1 : side + 1] = (
            (hidden * gate(hidden)).astype(low).reshape(side, slots, width)
        )
    two_sums = [none, none]
    for j in range(side):
        taps = [b for b in range(3) if 0 <= j + b - 1 < side]
        pieces = [
            active[j + b - 1, a : a + side].reshape(band, width) for b in taps for a in range(3)
        ]
        low_rows = low_two[3 * taps[0] : 3 * taps[-1] + 3].reshape(-1, width)
        value = jnp.dot(jnp.concatenate(pieces, axis=1), low_rows, preferred_element_type=f32)
        main_two[pl.ds(j * band, band), :] = value
        two_sums = add_up(two_sums, moments(value))
    copies = exchange_start(1, pack_rows(two_sums))
    for j in range(side):
        block = active[j, 1 : side + 1].reshape(band, width)
        active_t[:, j * band : (j + 1) * band] = block.T
    copies = exchange_middle(1, copies)
    sums = exchange_end(1, copies)
    sums = [unpack_row(sums, k) for k in range(2)]
    mean_two, inv_two, slope_two, base_two = settle_rows(
        (sums[0], sums[1]), pixels, gains[2], gains[3]
    )

    base_joined = base_two + base_side

    def joined_of(here):
        return main_two[here, :] * slope_two + side_pre[here, :] * slope_side + base_joined

    pooled = jnp.zeros((slots, width), f32)
    for p in range(pixel_count):
        joined = joined_of(pl.ds(p * slots, slots))
        pooled = pooled + joined * gate(joined)
    pooled = (pooled / pixel_count).astype(low)
    head_low = head_pad[...].astype(low)
    logits = lax.dot_general(
        pooled, head_low, (((1,), (1,)), ((), ())), preferred_element_type=f32
    )
    lane = lax.broadcasted_iota(jnp.int32, logits.shape, 1)
    real = lane < classes
    largest = jnp.max(jnp.where(real, logits, -jnp.inf), axis=1, keepdims=True)
    powers = jnp.where(real, jnp.exp(jnp.where(real, logits - largest, 0.0)), 0.0)
    total_power = jnp.sum(powers, axis=1, keepdims=True)
    label_column = column_of(label_ref[...].astype(f32), slots).astype(jnp.int32)
    onehot = jnp.where(lane == label_column, 1.0, 0.0)
    entropy = largest + jnp.log(total_power) - jnp.sum(onehot * logits, axis=1, keepdims=True)
    loss = jnp.sum(entropy * valid_column, axis=0, keepdims=True)
    grad_logits = (
        (powers / total_power - onehot) * (valid_column / denominator[:, :1])
    ).astype(low)
    grad_head = lax.dot_general(
        grad_logits, pooled, (((0,), (0,)), ((), ())), preferred_element_type=f32
    )[:16]
    grad_pooled = jnp.dot(grad_logits, head_low, preferred_element_type=f32) / pixel_count

    gain_two, gain_side, shift_two = none, none, none
    for p in range(pixel_count):
        here = pl.ds(p * slots, slots)
        joined = joined_of(here)
        opened = gate(joined)
        grad = grad_pooled * (opened * (1.0 + joined * (1.0 - opened)))
        shift_two = shift_two + jnp.sum(grad, axis=0, keepdims=True)
        gain_two = gain_two + jnp.sum(
            grad * ((main_two[here, :] - mean_two) * inv_two), axis=0, keepdims=True
        )
        gain_side = gain_side + jnp.sum(
            grad * ((side_pre[here, :] - mean_side) * inv_side), axis=0, keepdims=True
        )
        back_two[p // side, 1 + p % side] = (grad * slope_two).astype(low)
        back_side[here, :] = (grad * slope_side).astype(low)

    for b in range(3):
        first, last = max(0, b - 1), min(side, side + b - 1)
        left = active_t[:, first * band : last * band]
        for a in range(3):
            right = back_two[first - b + 1 : last - b + 1, 2 - a : 2 - a + side]
            grad_two[pl.ds((a * 3 + b) * width, width), :] = jnp.dot(
                left, right.reshape(-1, width), preferred_element_type=f32
            )

    def matrix_votes(k, grad):
        here = pl.ds(k * width, width)
        start = edges[k - 1] if k else 0
        col_new[:, here] = factored_votes(
            grad,
            grad.shape[0],
            start,
            row_ref,
            row_new,
            col_ref[:, here],
            level,
            votes_ref,
            start,
        )

    grad_short[...] = jnp.dot(xs_t[0, 0], back_side[...], preferred_element_type=f32)
    matrix_votes(2, grad_short)
    matrix_votes(1, grad_two)

    gain_one, shift_one = none, none
    for j in range(side):
        taps = [b for b in range(3) if 0 <= j - b + 1 < side]
        pieces = [
            back_two[j - b + 1, 2 - a : 2 - a + side].reshape(band, width)
            for b in taps
            for a in range(3)
        ]
        weights = jnp.concatenate([low_two[b * 3 + a] for b in taps for a in range(3)], axis=1)
        grad = lax.dot_general(
            jnp.concatenate(pieces, axis=1),
            weights,
            (((1,), (1,)), ((), ())),
            preferred_element_type=f32,
        )
        before = main_pre[pl.ds(j * band, band), :]
        hidden = before * slope_one + base_one
        opened = gate(hidden)
        grad = grad * (opened * (1.0 + hidden * (1.0 - opened)))
        shift_one = shift_one + jnp.sum(grad, axis=0, keepdims=True)
        gain_one = gain_one + jnp.sum(
            grad * ((before - mean_one) * inv_one), axis=0, keepdims=True
        )
        back_one[j, :side] = (grad * slope_one).astype(low).reshape(side, slots, width)

    square_head = grad_head * grad_head + EPS_ROW
    real = lax.broadcasted_iota(jnp.int32, square_head.shape, 0) < classes
    square_head = jnp.where(real, square_head, 0.0)
    head_lanes = pl.ds(edges[2], width)
    old = row_ref[:, head_lanes]
    row = keep * old + (1.0 - keep) * jnp.sum(square_head, axis=0, keepdims=True) / classes
    row_new[:, head_lanes] = row
    diagonal = eye_mask(16, classes)
    old = jnp.broadcast_to(col_ref[:, 3 * width :], (16, classes))
    old = jnp.sum(jnp.where(diagonal, old, 0.0), axis=1, keepdims=True)
    column = keep * old + (1.0 - keep) * jnp.sum(square_head, axis=1, keepdims=True) / width
    col_new[:, 3 * width :] = jnp.sum(
        jnp.where(diagonal, jnp.broadcast_to(column, (16, classes)), 0.0), axis=0, keepdims=True
    )
    real_column = lax.broadcasted_iota(jnp.int32, column.shape, 0) < classes
    column = jnp.where(real_column, column, 1.0)
    mean = jnp.sum(row, axis=1, keepdims=True) / width
    raw = grad_head * (lax.rsqrt(row) * jnp.sqrt(mean)) * lax.rsqrt(column)
    clip = jnp.maximum(1.0, jnp.sqrt(total_of(raw * raw) / (classes * width)))
    head_votes = jnp.tanh(raw / clip)[:classes]

    raws = []
    for k, grad in enumerate((gain_one, shift_one, gain_two, shift_two, gain_side, shift_two)):
        here = pl.ds(k * width, width)
        moment = keep * moment_ref[:, here] + (1.0 - keep) * (grad * grad + EPS_ROW)
        moment_new[:, here] = moment
        raws.append(grad * lax.rsqrt(moment))
    raw = jnp.concatenate(raws, axis=0)
    clip = jnp.maximum(1.0, jnp.sqrt(total_of(raw * raw) / raw.size))
    norm_votes = jnp.tanh(raw / clip)
    tail_votes = jnp.concatenate([head_votes, norm_votes], axis=0)
    copies = exchange_start(
        2,
        jnp.concatenate(
            [tail_votes[:, 128 * q : 128 * (q + 1)] for q in range(4)]
            + [jnp.broadcast_to(loss, (8, 128))],
            axis=0,
        ),
    )


    for b in range(3):
        first, last = (0, side - 1) if b == 0 else (0, side)
        shift = 1 if b == 0 else 0
        for a in range(3):
            left = xs_t[0 if b == 1 else 1, 0 if a == 1 else 1, :, first * band : last * band]
            start = 1 if a == 0 else 0
            right = back_one[first + shift : last + shift, start : start + side]
            grad_one[pl.ds((a * 3 + b) * in_width, in_width), :] = jnp.dot(
                left, right.reshape(-1, width), preferred_element_type=f32
            )
        if b == 1:
            copies = exchange_middle(2, copies)

    matrix_votes(0, grad_one)
    tail_ref[...] = exchange_end(2, copies)
    scale_ref[...] = jnp.concatenate(
        [jnp.broadcast_to(scales[k], (1, 128)) for k in range(5)]
        + [jnp.zeros((3, 128), f32)],
        axis=0,
    )


def share_kernel(
    edges,
    units,
    root,
    votes_ref,
    tail_ref,
    scale_ref,
    one_hbm,
    two_hbm,
    short_hbm,
    head_ref,
    norm_ref,
    new_ref,
    vote_ref,
    out_ref,
    loss_ref,
    core_in,
    wide_in,
    deep_in,
    line_in,
    sum_low,
    landed,
    total,
    own_weight,
    weight,
    vote_flat,
    new_flat,
    fetch_sem,
    rs_send,
    rs_recv,
    line_send,
    line_recv,
    pass_send,
    land_recv,
    spread_send,
    spread_recv,
    ag_send,
    ag_recv,
):
    width = norm_ref.shape[1]
    classes = head_ref.shape[0]
    low = jnp.bfloat16
    f32 = jnp.float32

    me, core, x, y, z = place()
    flip_core = me + 1 - 2 * core
    flip_x = me + 2 - 4 * x
    flip_y = me + 4 - 8 * y
    spot = lax.rem(me, 8)
    far = [lax.rem(z + k, 4) * 8 + spot for k in range(1, 4)]
    others = [lax.rem(me + k, 32) for k in range(1, 32)]
    barrier = pltpu.get_barrier_semaphore()
    for partner in others:
        pl.semaphore_signal(barrier, inc=1, device_id=(partner,), device_id_type=MESH)
    scales = [scale_ref[k : k + 1, :1] for k in range(5)]

    def fetch_rows(row, count, place_at, sem):
        parts = (
            (one_hbm, 0, edges[0]),
            (two_hbm, edges[0], edges[1]),
            (short_hbm, edges[1], edges[2]),
        )
        for ref, first, last in parts:

            @pl.when(jnp.logical_and(row >= first, row < last))
            def _():
                start = pl.multiple_of(row - first, count)
                pltpu.make_async_copy(
                    ref.at[pl.ds(start, count)], weight.at[pl.ds(place_at, count)], sem
                ).start()

    first_row = me * OWN

    def lines(start, count):
        return pl.ds(pl.multiple_of(start, 16), count)

    sizes = [GROUP * unit[1] for unit in units]
    starts = [sum(sizes[:k]) for k in range(len(units) + 1)]

    def part_of(ref, u, share, start, count):
        return ref.at[lines(share * starts[u] + start, count)]

    def places(u):
        if units[u][2]:
            return x, y, flip_x, flip_y
        return y, x, flip_y, flip_x

    def unit_start(u, cc):
        return GROUP * units[u][0] + cc * (GROUP * units[u][3])

    def own_group(u):
        first, second, _, _ = places(u)
        return units[u][0] + core * units[u][3] + (first * 8 + second * 4 + z) * units[u][1]

    def halve(source, target, u, stage, partner):
        return send(source, target, rs_send.at[u, stage], rs_recv.at[u, stage], partner)

    def scatter_start(u):
        size = 16 * sizes[u]
        return halve(
            votes_ref.at[lines(unit_start(u, 1 - core), size)],
            part_of(core_in, u, 16, 0, size),
            u,
            0,
            flip_core,
        )

    def add_to(ref, u, share, source_ref, source_start):
        size = share * sizes[u]
        here = lines(share * starts[u], size)
        ref[here, :] = ref[here, :] + source_ref[lines(source_start, size), :]

    def scatter_one(u, copy):
        copy.wait()
        add_to(core_in, u, 16, votes_ref, unit_start(u, core))
        first, _, flip_first, _ = places(u)
        size = 8 * sizes[u]
        return halve(
            part_of(core_in, u, 16, (1 - first) * size, size),
            part_of(wide_in, u, 8, 0, size),
            u,
            1,
            flip_first,
        )

    def scatter_two(u, copy):
        copy.wait()
        first, second, _, flip_second = places(u)
        add_to(wide_in, u, 8, core_in, 16 * starts[u] + first * 8 * sizes[u])
        size = 4 * sizes[u]
        return halve(
            part_of(wide_in, u, 8, (1 - second) * size, size),
            part_of(deep_in, u, 4, 0, size),
            u,
            2,
            flip_second,
        )

    def line_copy(u, k):
        plane_to = lax.rem(z + k, 4)
        return pltpu.make_async_remote_copy(
            src_ref=part_of(deep_in, u, 4, plane_to * sizes[u], sizes[u]),
            dst_ref=part_of(line_in, u, 4, z * sizes[u], sizes[u]),
            send_sem=line_send.at[u, k],
            recv_sem=line_recv.at[u, k],
            device_id=(plane_to * 8 + spot,),
            device_id_type=MESH,
        )

    def scatter_three(u, copy):
        copy.wait()
        _, second, _, _ = places(u)
        add_to(deep_in, u, 4, wide_in, 8 * starts[u] + second * 4 * sizes[u])
        for k in (3, 2, 1):
            line_copy(u, k).start()
        here = lines(4 * starts[u] + z * sizes[u], sizes[u])
        line_in[here, :] = deep_in[here, :]

    groups = (edges[2] + TAIL) // 16
    spare = (groups - 1) // 32
    passes = []

    def land(local, group, to, slot, index):
        source = sum_low.at[lines(local * GROUP, GROUP)]
        target = landed.at[lines(slot * GROUP, GROUP)]
        copy = pltpu.make_async_remote_copy(
            src_ref=source,
            dst_ref=target,
            send_sem=pass_send.at[index],
            recv_sem=land_recv.at[slot],
            device_id=(to,),
            device_id_type=MESH,
        )
        return copy, source, target

    def pass_on(u):
        for m in range(units[u][1]):
            local = starts[u] // GROUP + m
            group = own_group(u) + m
            to, slot = lax.div(group, spare), lax.rem(group, spare)
            for halo in range(2):
                index = 2 * local + halo
                if halo:
                    receiver, at = lax.rem(to + 31, 32), spare
                    wanted = jnp.logical_and(slot == 0, group > 0)
                else:
                    receiver, at, wanted = to, slot, group >= 0
                away = jnp.logical_and(wanted, receiver != me)
                here = jnp.logical_and(wanted, receiver == me)
                copy, source, target = land(local, group, receiver, at, index)

                @pl.when(away)
                def _():
                    copy.start()

                @pl.when(here)
                def _():
                    target[...] = source[...]

                passes.append((away, copy))

    def flat_rows(row, q, values, ref):
        ref[pl.ds(row * 4 + q, 8, stride=4), :] = values

    def old_rows(u, cc):
        matrix = units[u][4][cc]
        base = edges[matrix - 1] if matrix else 0
        return (one_hbm, two_hbm, short_hbm)[matrix], 16 * own_group(u) - base, 16 * units[u][1]

    def own_fetch(u):
        target = own_weight.at[pl.ds(starts[u] // 4, 16 * units[u][1])]
        matrices = units[u][4]
        for cc in range(2):
            if cc and matrices[0] == matrices[1]:
                continue

            @pl.when((core == cc) if matrices[0] != matrices[1] else (core >= 0))
            def _():
                ref, row, count = old_rows(u, cc)
                pltpu.make_async_copy(
                    ref.at[pl.ds(pl.multiple_of(row, 16), count)], target, fetch_sem.at[2 + u]
                ).start()

    def spread_copy(u, k):
        own = out_ref.at[lines(own_group(u) * GROUP, sizes[u])]
        return pltpu.make_async_remote_copy(
            src_ref=own,
            dst_ref=own,
            send_sem=spread_send.at[u, k],
            recv_sem=spread_recv.at[u, k],
            device_id=(far[k - 1],),
            device_id_type=MESH,
        )

    def own_block(u):
        size = sizes[u]
        for k in range(1, 4):
            line_copy(u, k).wait_recv()
        here = pl.ds(starts[u], size)
        low_sum = functools.reduce(
            lambda a, b: a + b,
            [line_in[pl.ds(4 * starts[u] + t * size, size), :].astype(f32) for t in range(4)],
        ).astype(low)
        sum_low[here, :] = low_sum
        total[here, :] = low_sum.astype(f32)
        target = own_weight.at[pl.ds(starts[u] // 4, 16 * units[u][1])]
        pltpu.make_async_copy(target, target, fetch_sem.at[2 + u]).wait()
        matrices = units[u][4]
        scale = jnp.where(core == 0, scales[matrices[0]], scales[matrices[1]])
        for m in range(units[u][1]):
            row = starts[u] // 4 + 16 * m
            for part in (0, 8):
                for q in range(4):
                    summed = total[pl.ds(row * 4 + 16 * q + part, 8), :]
                    old = own_weight[pl.ds(row + part, 8), 128 * q : 128 * (q + 1)]
                    fresh = old - scale * jnp.tanh(summed * root)
                    flat_rows(row + part, q, fresh, new_flat)
        out_ref[lines(own_group(u) * GROUP, size), :] = new_flat[here, :].astype(low)
        for k in (3, 2, 1):
            spread_copy(u, k).start()
        pass_on(u)

    def piece(rows, u, stage, partner):
        return send(
            out_ref.at[rows], out_ref.at[rows], ag_send.at[u, stage], ag_recv.at[u, stage], partner
        )

    def gather_one(u):
        for k in range(1, 4):
            spread_copy(u, k).wait_recv()
        first, second, _, flip_second = places(u)
        size = 4 * sizes[u]
        start = unit_start(u, core) + (2 * first + second) * size
        return piece(lines(start, size), u, 0, flip_second)

    def gather_two(u, copy):
        copy.wait()
        first, _, flip_first, _ = places(u)
        size = 8 * sizes[u]
        return piece(lines(unit_start(u, core) + first * size, size), u, 1, flip_first)

    def gather_three(u, copy):
        copy.wait()
        return piece(lines(unit_start(u, core), 16 * sizes[u]), u, 2, flip_core)

    def renew(row, at_row):
        scale = scale_of(at_row, [scales[k] for k in range(3)], edges)
        for part in (0, 8):
            for q in range(4):
                summed = total[pl.ds(row * 4 + 16 * q + part, 8), :]
                old = weight[pl.ds(row + part, 8), 128 * q : 128 * (q + 1)]
                fresh = old - scale * jnp.tanh(summed * root)
                flat_rows(row + part, q, summed, vote_flat)
                flat_rows(row + part, q, fresh, new_flat)

    in_flight = {}
    steps = (
        lambda u, copy: scatter_start(u),
        scatter_one,
        scatter_two,
        scatter_three,
        lambda u, copy: own_block(u),
        lambda u, copy: gather_one(u),
        gather_two,
        gather_three,
    )

    def go(number, u):
        in_flight[u] = steps[number](u, in_flight.get(u))

    for k in range(OWN // PIECE):
        fetch_rows(first_row + k * PIECE, PIECE, k * PIECE, fetch_sem.at[0])
    fetch_rows(first_row + OWN, TAIL, OWN, fetch_sem.at[1])
    for u in range(len(units)):
        own_fetch(u)
    pl.semaphore_wait(barrier, len(others))

    last_turn = SCHEDULE
    cut = [k for k, (number, _) in enumerate(last_turn) if number == 4][-1] + 1
    ending = len(last_turn) - 3
    for number, u in last_turn[:cut]:
        go(number, u)

    sums = tail_ref[...]
    loss_ref[...] = sums[4 * TAIL : 4 * TAIL + 1, :1]
    old = jnp.concatenate([head_ref[...], norm_ref[...]], axis=0)
    is_head = lax.broadcasted_iota(jnp.int32, (TAIL, width), 0) < classes
    scale = jnp.where(is_head, scales[3], scales[4])
    sums = jnp.concatenate([sums[TAIL * q : TAIL * (q + 1)] for q in range(4)], axis=1)
    fresh = old - scale * jnp.tanh(sums * root)
    both = jnp.concatenate([sums, fresh], axis=0)
    high = both.astype(low)
    rest = both - high.astype(f32)
    middle = rest.astype(low)
    parts = jnp.concatenate([high, middle, (rest - middle.astype(f32)).astype(low)], axis=0)

    flat_sums, flat_new = [], []
    window = 256
    for q in range(classes):
        start = min(q * width // classes // 128 * 128, width - window)
        down = lax.broadcasted_iota(jnp.int32, (window, width), 0)
        across = lax.broadcasted_iota(jnp.int32, (window, width), 1)
        gap = across - classes * down + (q * width - classes * start)
        chosen = jnp.where(jnp.logical_and(gap >= 0, gap < classes), 1.0, 0.0).astype(low)
        moved = jnp.dot(parts[:, start : start + window], chosen, preferred_element_type=f32)
        moved = moved[: 2 * TAIL] + moved[2 * TAIL : 4 * TAIL] + moved[4 * TAIL :]
        spot_of = lax.broadcasted_iota(jnp.int32, (TAIL, width), 1).astype(f32) + q * width
        class_of = spot_of - classes * jnp.floor((spot_of + 0.5) / classes)
        here = lax.broadcasted_iota(jnp.int32, (TAIL, width), 0).astype(f32) == class_of
        flat_sums.append(jnp.sum(jnp.where(here, moved[:TAIL], 0.0), axis=0, keepdims=True))
        flat_new.append(jnp.sum(jnp.where(here, moved[TAIL:], 0.0), axis=0, keepdims=True))
    flat_sums = jnp.concatenate(flat_sums + [sums[classes:]], axis=0)
    flat_new = jnp.concatenate(flat_new + [fresh[classes:]], axis=0)

    for number, u in last_turn[cut:ending]:
        go(number, u)

    mine = [own_group(u) for u in range(len(units))]
    for slot in range(spare + 1):
        group = me * spare + slot
        own = group < 0
        for u, unit in enumerate(units):
            inside = jnp.logical_and(group >= mine[u], group < mine[u] + unit[1])
            own = jnp.logical_or(own, inside)

        @pl.when(jnp.logical_and(jnp.logical_not(own), group < groups - 1))
        def _():
            land(0, group, me, slot, 0)[0].wait_recv()

    pltpu.make_async_copy(
        weight.at[pl.ds(0, OWN)], weight.at[pl.ds(0, OWN)], fetch_sem.at[0]
    ).wait()
    total[pl.ds(0, SPAN), :] = landed[pl.ds(0, SPAN), :].astype(f32)

    @pl.loop(0, OWN // 16)
    def _(k):
        row = pl.multiple_of(k * 16, 16)
        renew(row, first_row + row)

    @pl.when(me < 31)
    def _():
        pltpu.make_async_copy(
            weight.at[pl.ds(OWN, TAIL)], weight.at[pl.ds(OWN, TAIL)], fetch_sem.at[1]
        ).wait()
        total[pl.ds(SPAN, GROUP), :] = landed[pl.ds(SPAN, GROUP), :].astype(f32)
        renew(OWN, first_row + OWN)

    def tail_rows(values, ref):
        for u in (0, 8):
            for q in range(4):
                flat_rows(OWN + u, q, values[u : u + 8, 128 * q : 128 * (q + 1)], ref)

    @pl.when(me == 31)
    def _():
        tail_rows(flat_sums, vote_flat)
        tail_rows(flat_new, new_flat)

    shift = 2 * me
    share = vote_ref.shape[0]
    vote_ref[...] = vote_flat[pl.ds(shift, share), :]
    new_ref[...] = new_flat[pl.ds(shift, share), :]
    tail_rows(flat_new, new_flat)
    out_ref[pl.ds(32 * SPAN, GROUP), :] = new_flat[pl.ds(SPAN, GROUP), :].astype(low)

    for number, u in last_turn[ending:]:
        go(number, u)
    for u in range(len(units)):
        in_flight[u].wait()
        for k in range(1, 4):
            line_copy(u, k).wait_send()
            spread_copy(u, k).wait_send()
    for away, copy in passes:

        @pl.when(away)
        def _():
            copy.wait_send()


def finish_kernel(count, chunks, *refs):
    sources, targets, sem = refs[:count], refs[count : 2 * count], refs[2 * count]
    rows = sources[0].shape[0]
    step = -(-rows // chunks // 16) * 16
    copies = []
    for k in range(chunks):
        here = pl.ds(k * step, min(step, rows - k * step))
        copies.append(
            pltpu.make_async_copy(sources[0].at[here], targets[0].at[here], sem.at[k])
        )
    for k in range(1, count - 2):
        copies.append(pltpu.make_async_copy(sources[k], targets[k], sem.at[chunks + k]))
    for copy in copies:
        copy.start()
    for k in (count - 2, count - 1):
        targets[k][...] = sources[k][...]
    for copy in copies:
        copy.wait()


def finish(values):
    vmem = pl.BlockSpec(memory_space=pltpu.VMEM)
    hbm = pl.BlockSpec(memory_space=pl.ANY)
    count, chunks = len(values), 8
    held = [pltpu.with_memory_space_constraint(value, pltpu.VMEM) for value in values[:-2]]
    return pl.pallas_call(
        functools.partial(finish_kernel, count, chunks),
        out_shape=[jax.ShapeDtypeStruct(value.shape, value.dtype) for value in values],
        in_specs=[vmem] * count,
        out_specs=[hbm] * (count - 2) + [vmem] * 2,
        scratch_shapes=[pltpu.SemaphoreType.DMA((chunks + count,))],
        compiler_params=pltpu.CompilerParams(vmem_limit_bytes=1024 * 1024),
        name="finish",
    )(*held, *values[-2:])


def run_worker(images, conv_one, conv_two, shortcut, head, norm_params, valid, labels, rows, cols, moment):
    vmem = pl.BlockSpec(memory_space=pltpu.VMEM)
    hbm = pl.BlockSpec(memory_space=pl.ANY)
    low, f32 = jnp.bfloat16, jnp.float32
    dma = pltpu.SemaphoreType.DMA
    slots, in_width = valid.shape[1], images.shape[1]
    width = conv_one.shape[1]
    pixels = images.shape[0] // 4
    shape = pltpu.VMEM
    edges = edges_of(conv_one, conv_two, shortcut)
    return pl.pallas_call(
        functools.partial(worker_kernel, edges),
        out_shape=(
            shape((edges[2] * 4, 128), low),
            shape((GROUP + 8, 128), f32),
            shape((8, 128), f32),
            shape(rows.shape, f32),
            shape(cols.shape, f32),
            shape(moment.shape, f32),
            jax.ShapeDtypeStruct((1, 1), f32),
        ),
        in_specs=[hbm] * 4 + [vmem] * 7,
        out_specs=(vmem,) * 7,
        scratch_shapes=[
            pltpu.VMEM((2, 4, 2, 4, slots, in_width), low),
            pltpu.VMEM(conv_one.shape, f32),
            pltpu.VMEM(conv_two.shape, f32),
            pltpu.VMEM(shortcut.shape, f32),
            pltpu.VMEM((9, in_width, width), low),
            pltpu.VMEM((9, width, width), low),
            pltpu.VMEM((1, in_width, width), low),
            pltpu.VMEM((pixels, width), f32),
            pltpu.VMEM((pixels, width), f32),
            pltpu.VMEM((pixels, width), f32),
            pltpu.VMEM((4, 6, slots, width), low),
            pltpu.VMEM((4, 6, slots, width), low),
            pltpu.VMEM((4, 5, slots, width), low),
            pltpu.VMEM((pixels, width), low),
            pltpu.VMEM((width, pixels), low),
            pltpu.VMEM((2, 2, in_width, pixels), low),
            pltpu.VMEM((128, width), f32),
            pltpu.VMEM((conv_two.shape[0], 128), f32),
            pltpu.VMEM((8, width), f32),
            pltpu.VMEM((2 * images.shape[0], 128), low),
            pltpu.VMEM((24, 128), f32),
            pltpu.VMEM((8, 24, 128), f32),
            pltpu.VMEM((4, 24, 128), f32),
            pltpu.VMEM((8, 128), f32),
            pltpu.VMEM((8, 8, 128), f32),
            pltpu.VMEM((4, 8, 128), f32),
            pltpu.VMEM((GROUP + 8, 128), f32),
            pltpu.VMEM((8, GROUP + 8, 128), f32),
            pltpu.VMEM((4, GROUP + 8, 128), f32),
            dma((7,)),
            dma((3, 10)),
            dma((3, 10)),
            dma((2,)),
        ],
        compiler_params=pltpu.CompilerParams(
            collective_id=1, has_side_effects=True, vmem_limit_bytes=50 * 1024 * 1024
        ),
        name="worker",
    )(images, conv_one, conv_two, shortcut, head, norm_params, valid, labels, rows, cols, moment)


def run_share(votes, tail, scales, conv_one, conv_two, shortcut, head, norm_params):
    vmem = pl.BlockSpec(memory_space=pltpu.VMEM)
    hbm = pl.BlockSpec(memory_space=pl.ANY)
    low, f32 = jnp.bfloat16, jnp.float32
    dma = pltpu.SemaphoreType.DMA
    workers = lax.axis_size("dp")
    width = conv_one.shape[1]
    shape = pltpu.VMEM
    edges = edges_of(conv_one, conv_two, shortcut)
    units = tuple(make_units(edges))
    flat = (edges[2] + TAIL) * width // 128
    share = flat // workers
    held = [pltpu.with_memory_space_constraint(value, pltpu.VMEM) for value in (votes, tail, scales)]
    return pl.pallas_call(
        functools.partial(share_kernel, edges, units, 1.0 / math.sqrt(workers)),
        out_shape=(
            shape((share, 128), f32),
            shape((share, 128), f32),
            shape((flat, 128), low),
            jax.ShapeDtypeStruct((1, 1), f32),
        ),
        in_specs=[vmem] * 3 + [hbm] * 3 + [vmem] * 2,
        out_specs=(vmem,) * 4,
        scratch_shapes=[
            pltpu.VMEM((16 * SPAN, 128), low),
            pltpu.VMEM((8 * SPAN, 128), low),
            pltpu.VMEM((4 * SPAN, 128), low),
            pltpu.VMEM((4 * SPAN, 128), low),
            pltpu.VMEM((SPAN, 128), low),
            pltpu.VMEM((SPAN + GROUP, 128), low),
            pltpu.VMEM((SPAN + GROUP, 128), f32),
            pltpu.VMEM((OWN, width), f32),
            pltpu.VMEM((OWN + TAIL, width), f32),
            pltpu.VMEM((SPAN + GROUP, 128), f32),
            pltpu.VMEM((SPAN + GROUP, 128), f32),
            dma((2 + len(units),)),
            dma((len(units), 3)),
            dma((len(units), 3)),
            dma((len(units), 4)),
            dma((len(units), 4)),
            dma((2 * OWN // 16,)),
            dma((OWN // 16 + 1,)),
            dma((len(units), 4)),
            dma((len(units), 4)),
            dma((len(units), 3)),
            dma((len(units), 3)),
        ],
        compiler_params=pltpu.CompilerParams(
            collective_id=2, has_side_effects=True, vmem_limit_bytes=20 * 1024 * 1024
        ),
        name="share",
    )(*held, conv_one, conv_two, shortcut, head, norm_params)


def edges_of(*weights):
    return tuple(sum(weight.shape[0] for weight in weights[: k + 1]) for k in range(3))


def scale_for(weight):
    return jnp.maximum(EPS_SCALE, jnp.sqrt(jnp.mean(weight * weight)))


def local_general(
    images,
    valid_slot,
    labels,
    conv_one,
    conv_two,
    shortcut,
    classifier,
    norm_params,
    row_state,
    col_state,
    bn_moment,
):
    in_width = images.shape[3]
    width = conv_one.shape[1]
    kernel_one = conv_one.astype(jnp.bfloat16).reshape(3, 3, in_width, width)
    kernel_two = conv_two.astype(jnp.bfloat16).reshape(3, 3, width, width)
    kernel_short = shortcut.astype(jnp.bfloat16).reshape(1, 1, in_width, width)
    head_low = classifier.astype(jnp.bfloat16)
    slot_count = images.shape[0]
    out_side = images.shape[1] // 2
    pixel_count = out_side * out_side
    slot_weight = valid_slot.astype(jnp.float32)
    pixel_weight = jnp.broadcast_to(slot_weight[:, None], (slot_count, pixel_count)).reshape(-1, 1)
    main_pre, side_pre = first_section(images, kernel_one, kernel_short)
    main_sums = masked_moments(pixel_weight, main_pre)
    side_sums = masked_moments(pixel_weight, side_pre)
    count_row = jnp.broadcast_to(jnp.sum(slot_weight), (width,))
    first_sums = lax.psum(jnp.stack([*main_sums, *side_sums, count_row]), "dp")
    valid_count = first_sums[4, 0]
    denominator = jnp.maximum(valid_count, 1.0)
    pixels = denominator * pixel_count
    norm_one = settle(first_sums[0], first_sums[1], pixels)
    norm_side = settle(first_sums[2], first_sums[3], pixels)
    hidden_one, active, main_two = second_section(
        main_pre, norm_one, norm_params, kernel_two, slot_count, out_side
    )
    two_sums = masked_moments(pixel_weight, main_two)
    second_sums = lax.psum(jnp.stack([*two_sums]), "dp")
    norm_two = settle(second_sums[0], second_sums[1], pixels)
    joined_pre = (
        (main_two - norm_two[0]) * norm_two[1] * norm_params[2]
        + norm_params[3]
        + (side_pre - norm_side[0]) * norm_side[1] * norm_params[4]
        + norm_params[5]
    )
    joined = jax.nn.silu(joined_pre).reshape(slot_count, pixel_count, -1)
    pooled = jnp.mean(joined, axis=1).astype(jnp.bfloat16)
    logits = jnp.dot(pooled, head_low, preferred_element_type=jnp.float32)
    largest = jnp.max(logits, axis=1, keepdims=True)
    exp_terms = jnp.exp(logits - largest)
    total_exp = jnp.sum(exp_terms, axis=1, keepdims=True)
    log_total = largest[:, 0] + jnp.log(total_exp[:, 0])
    onehot = (labels[:, None] == jnp.arange(logits.shape[1], dtype=jnp.int32)[None, :]).astype(
        jnp.float32
    )
    local_sum = jnp.sum(slot_weight * (log_total - jnp.sum(onehot * logits, axis=1)))
    grad_logits = ((exp_terms / total_exp - onehot) * (slot_weight / denominator)[:, None]).astype(
        jnp.bfloat16
    )
    grad_head = lax.dot_general(
        pooled, grad_logits, (((0,), (0,)), ((), ())), preferred_element_type=jnp.float32
    )
    grad_pooled = lax.dot_general(
        grad_logits, head_low, (((1,), (1,)), ((), ())), preferred_element_type=jnp.float32
    )
    spread_pooled = jnp.broadcast_to(
        (grad_pooled / pixel_count)[:, None, :], (slot_count, pixel_count, width)
    )
    grad_joined = spread_pooled.reshape(slot_count * pixel_count, width) * silu_slope(joined_pre)
    gain_two, shift_two, grad_two = norm_backward(grad_joined, main_two, norm_two, norm_params[2])
    gain_side, shift_side, grad_side = norm_backward(
        grad_joined, side_pre, norm_side, norm_params[4]
    )
    grad_two_maps = grad_two.reshape(slot_count, out_side, out_side, width)
    grad_side_maps = grad_side.reshape(slot_count, out_side, out_side, width)
    grad_conv_two = conv_weight_grad(active, grad_two_maps, 1, 1, 1)
    grad_short = conv_weight_grad(images, grad_side_maps, 2, 0, -1)
    kernel_turned = jnp.transpose(kernel_two[::-1, ::-1], (0, 1, 3, 2))
    grad_active = conv_apply(grad_two_maps, kernel_turned, 1, 1).reshape(
        slot_count * pixel_count, width
    )
    grad_hidden = grad_active * silu_slope(hidden_one)
    gain_one, shift_one, grad_one = norm_backward(grad_hidden, main_pre, norm_one, norm_params[0])
    grad_conv_one = conv_weight_grad(
        images, grad_one.reshape(slot_count, out_side, out_side, width), 2, 1, 0
    )
    grad_norms = jnp.stack([gain_one, shift_one, gain_two, shift_two, gain_side, shift_side])
    grads = (grad_conv_one, grad_conv_two, grad_short, grad_head, grad_norms)
    votes, rows_new, cols_new, moment_new = make_votes(
        grads, row_state[0], col_state[0], bn_moment[0]
    )
    workers = lax.axis_size("dp")
    weights = (conv_one, conv_two, shortcut, classifier, norm_params)
    scales = [scale_for(weight) for weight in weights]
    loss_sum = lax.psum(local_sum, "dp")
    flat_vote = jnp.concatenate([vote.reshape(-1) for vote in votes])
    flat_old = jnp.concatenate([weight.reshape(-1) for weight in weights])
    flat_scale = jnp.concatenate(
        [
            jnp.broadcast_to(scale, (weight.size,))
            for scale, weight in zip(scales, weights)
        ]
    )
    vote_mine = lax.psum_scatter(flat_vote, "dp", tiled=True)
    share = vote_mine.shape[0]
    start = lax.axis_index("dp") * share
    new_mine = lax.dynamic_slice_in_dim(
        flat_old, start, share
    ) - lax.dynamic_slice_in_dim(flat_scale, start, share) * jnp.tanh(
        vote_mine / math.sqrt(workers)
    )
    copies = lax.all_gather(new_mine.astype(jnp.bfloat16), "dp", tiled=True)
    return (
        loss_sum,
        valid_count,
        new_mine,
        copies,
        vote_mine,
        rows_new[None, :],
        cols_new[None, :],
        moment_new[None, :],
    )


def local(
    images,
    valid_slot,
    labels,
    conv_one,
    conv_two,
    shortcut,
    classifier,
    norm_params,
    row_state,
    col_state,
    bn_moment,
):
    head = classifier.T
    votes, tail, scales, rows_new, cols_new, moment_new, valid_count = run_worker(
        images.reshape(-1, images.shape[-1]),
        conv_one,
        conv_two,
        shortcut,
        head,
        norm_params,
        valid_slot.reshape(1, -1),
        labels.reshape(1, -1),
        row_state,
        col_state,
        bn_moment,
    )
    new_mine, vote_mine, copies, loss_sum = run_share(
        votes, tail, scales, conv_one, conv_two, shortcut, head, norm_params
    )
    copies, new_mine, vote_mine, rows_new, cols_new, moment_new, loss_sum, valid_count = finish(
        (copies, new_mine, vote_mine, rows_new, cols_new, moment_new, loss_sum, valid_count)
    )
    return (
        loss_sum.reshape(()),
        valid_count.reshape(()),
        new_mine.reshape(-1),
        copies.reshape(-1),
        vote_mine.reshape(-1),
        rows_new,
        cols_new,
        moment_new,
    )


def solution(mesh):
    placed = (
        P("dp", None, None, None),
        P("dp"),
        P("dp"),
        P(),
        P(),
        P(),
        P(),
        P(),
        P("dp", None),
        P("dp", None),
        P("dp", None),
    )
    return jax.shard_map(
        local if mesh.shape["dp"] == 32 else local_general,
        mesh=mesh,
        in_specs=placed,
        out_specs=(P(), P(), P("dp"), P(), P("dp"), P("dp", None), P("dp", None), P("dp", None)),
        check_vma=False,
    )
```

```python
import functools
import math

import jax
import jax.numpy as jnp
from jax import lax
from jax.experimental import pallas as pl
from jax.experimental.pallas import tpu as pltpu
from jax.sharding import PartitionSpec as P

STEP = 10
MESH = pl.DeviceIdType.MESH

EPS_NORM = 1e-05
EPS_ROW = 1e-30
EPS_SCALE = 0.001
FORWARD_DIMS = ("NHWC", "HWIO", "NHWC")
WEIGHT_DIMS = ("CHWN", "IHWO", "HWNC")
OWN = 224
TAIL = 16
PIECE = 32
SPAN = 4 * OWN
HALF = SPAN // 2
GROUP = 64


def conv_apply(maps, kernel, stride, margin):
    return lax.conv_general_dilated(
        maps,
        kernel,
        (stride, stride),
        ((margin, margin), (margin, margin)),
        dimension_numbers=FORWARD_DIMS,
        preferred_element_type=jnp.float32,
    )


def conv_weight_grad(maps, grad_out, stride, low_pad, high_pad):
    result = lax.conv_general_dilated(
        maps,
        grad_out,
        (1, 1),
        ((low_pad, high_pad), (low_pad, high_pad)),
        rhs_dilation=(stride, stride),
        dimension_numbers=WEIGHT_DIMS,
        preferred_element_type=jnp.float32,
    )
    return result.reshape(-1, result.shape[3])


def silu_slope(values):
    sigmoid_part = jax.nn.sigmoid(values)
    return sigmoid_part * (1.0 + values * (1.0 - sigmoid_part))


def settle(sum_plain, sum_square, pixels):
    mean_value = sum_plain / pixels
    return (mean_value, lax.rsqrt(sum_square / pixels - mean_value * mean_value + EPS_NORM))


def first_section(images, kernel_one, kernel_short):
    row_count = images.shape[0] * (images.shape[1] // 2) ** 2
    main_pre = conv_apply(images, kernel_one, 2, 1).reshape(row_count, -1)
    side_pre = conv_apply(images, kernel_short, 2, 0).reshape(row_count, -1)
    return (main_pre, side_pre)


def second_section(main_pre, norm_one, norm_params, kernel_two, slot_count, out_side):
    hidden_one = (main_pre - norm_one[0]) * norm_one[1] * norm_params[0] + norm_params[1]
    active = (
        jax.nn.silu(hidden_one).astype(jnp.bfloat16).reshape(slot_count, out_side, out_side, -1)
    )
    main_two = conv_apply(active, kernel_two, 1, 1).reshape(slot_count * out_side * out_side, -1)
    return (hidden_one, active, main_two)


def masked_moments(pixel_weight, values):
    return (jnp.sum(pixel_weight * values, axis=0), jnp.sum(pixel_weight * values * values, axis=0))


def soft_sign(step_raw):
    clip_by = jnp.maximum(1.0, jnp.sqrt(jnp.mean(step_raw * step_raw)))
    return jnp.tanh(step_raw / clip_by)


def make_votes(grads, rows_old, cols_old, moment_old):
    decay_rate = 1.0 - STEP ** (-0.8)
    votes, rows_new, cols_new = ([], [], [])
    row_at, col_at = (0, 0)
    for matrix in grads[:4]:
        row_size, col_size = matrix.shape
        square = matrix * matrix + EPS_ROW
        row_part = decay_rate * rows_old[row_at : row_at + row_size] + (
            1.0 - decay_rate
        ) * jnp.mean(square, axis=1)
        col_part = decay_rate * cols_old[col_at : col_at + col_size] + (
            1.0 - decay_rate
        ) * jnp.mean(square, axis=0)
        second = row_part[:, None] * col_part[None, :] / jnp.mean(row_part)
        votes.append(soft_sign(matrix * lax.rsqrt(second)))
        rows_new.append(row_part)
        cols_new.append(col_part)
        row_at += row_size
        col_at += col_size
    flat_norm = grads[4].reshape(-1)
    moment_new = decay_rate * moment_old + (1.0 - decay_rate) * (flat_norm * flat_norm + EPS_ROW)
    votes.append(soft_sign(flat_norm * lax.rsqrt(moment_new)))
    return (votes, jnp.concatenate(rows_new), jnp.concatenate(cols_new), moment_new)


def norm_backward(grad_out, pre_value, norm_pair, gain_row):
    normed = (pre_value - norm_pair[0]) * norm_pair[1]
    grad_gain = jnp.sum(grad_out * normed, axis=0)
    grad_shift = jnp.sum(grad_out, axis=0)
    grad_pre = (grad_out * gain_row * norm_pair[1]).astype(jnp.bfloat16)
    return (grad_gain, grad_shift, grad_pre)


SCHEDULE = (
    (),
    (
        (1, 0),
    ),
    (
        (0, 2), (1, 1),
    ),
    (
        (0, 3), (1, 2), (2, 0), (0, 4), (1, 3), (2, 1),
    ),
    (
        (0, 5), (1, 4), (2, 2), (3, 0),
    ),
    (
        (0, 6), (1, 5), (2, 3), (3, 1),
    ),
    (
        (0, 7), (1, 6), (2, 4), (3, 2), (4, 0),
    ),
    (),
    (
        (0, 8), (1, 7), (2, 5), (3, 3), (4, 1),
    ),
    (),
    (
        (1, 8), (2, 6), (3, 4), (4, 2), (1, 9), (2, 7), (3, 5), (4, 3), (5, 0), (0, 11), (1, 10),
        (2, 8), (3, 6), (4, 4), (5, 1), (0, 12), (1, 11), (2, 9), (3, 7), (4, 5), (5, 2), (6, 0),
        (0, 13), (1, 12), (2, 10), (3, 8), (4, 6), (5, 3), (6, 1), (1, 13), (2, 11), (3, 9),
        (4, 7), (8, 0), (5, 4), (6, 2), (2, 12), (3, 10), (4, 8), (5, 5), (6, 3), (7, 0),
        (2, 13), (3, 11), (4, 9), (5, 6), (6, 4), (7, 1), (3, 12), (4, 10), (5, 7), (6, 5),
        (7, 2), (3, 13), (4, 11), (5, 8), (6, 6), (7, 3), (4, 12), (5, 9), (6, 7), (7, 4),
        (4, 13), (5, 10), (6, 8), (7, 5), (5, 11), (6, 9), (7, 6), (5, 12), (6, 10), (7, 7),
        (5, 13), (6, 11), (7, 8), (6, 12), (7, 9), (6, 13), (9, 0), (7, 10), (7, 11), (7, 12),
        (7, 13),
    ),
)


def place():
    me = lax.axis_index("dp")
    core = lax.rem(me, 2)
    x = lax.rem(lax.div(me, 2), 2)
    y = lax.rem(lax.div(me, 4), 2)
    z = lax.div(me, 8)
    return me, core, x, y, z


def send(src, dst, send_sem, recv_sem, partner):
    copy = pltpu.make_async_remote_copy(
        src_ref=src,
        dst_ref=dst,
        send_sem=send_sem,
        recv_sem=recv_sem,
        device_id=(partner,),
        device_id_type=MESH,
    )
    copy.start()
    return copy


def scale_of(row, scales, edges):
    picked = scales[2]
    picked = jnp.where(row < edges[1], scales[1], picked)
    return jnp.where(row < edges[0], scales[0], picked)


def make_units(edges):
    one, two, short = edges[0] // 16, edges[1] // 16, edges[2] // 16
    units = []
    for k in range((two - one) // 32):
        units.append((one + 32 * k, 1, k % 2 == 0, 16, (1, 1)))
    for k in range(one // 32):
        units.append((32 * k, 1, k % 2 == 1, 16, (0, 0)))
    at = one // 32 * 32
    assert one - at == 16 and short - two == 16
    units.append((at, 1, False, two - at, (0, 2)))
    return units


def settle_rows(sums, pixels, gain, shift):
    mean = sums[0] / pixels
    inv = lax.rsqrt(sums[1] / pixels - mean * mean + EPS_NORM)
    slope = gain * inv
    return mean, inv, slope, shift - mean * slope


def gate(values):
    return 0.5 * jnp.tanh(0.5 * values) + 0.5


def eye_mask(rows, columns, offset=0):
    down = lax.broadcasted_iota(jnp.int32, (rows, columns), 0) + offset
    return down == lax.broadcasted_iota(jnp.int32, (rows, columns), 1)


def column_of(row, size):
    spread = jnp.where(eye_mask(size, size), jnp.broadcast_to(row, (size, size)), 0)
    return jnp.sum(spread, axis=1, keepdims=True)


def total_of(values):
    return jnp.sum(jnp.sum(values, axis=0, keepdims=True), axis=1, keepdims=True)


def fold(values):
    return jnp.sum(values.reshape(values.shape[0] // 8, 8, values.shape[1]), axis=0)


def cast_weight(source, target, square_ref, taps, depth, fetches):
    step = 128
    square_ref[...] = jnp.zeros_like(square_ref)
    for tap in range(taps):
        if tap % (taps // len(fetches)) == 0:
            fetches[tap * len(fetches) // taps].wait()
        new_tap = (tap % 3) * 3 + tap // 3

        @pl.loop(0, depth // step)
        def _(k):
            start = pl.multiple_of(k * step, step)
            values = source[pl.ds(tap * depth + start, step), :]
            target[new_tap, pl.ds(start, step), :] = values.astype(jnp.bfloat16)
            square_ref[...] += fold(values * values)


def factored_votes(grad, rows, row_at, rows_old, rows_new, col_old, level, votes, vote_at, between, after):
    width = grad.shape[1]
    keep = 1.0 - STEP ** (-0.8)
    step = 128
    quarters = width // 128

    def first(k, carry):
        col_sum, row_sum = carry
        start = pl.multiple_of(k * step, step)
        lanes = pl.ds(pl.multiple_of(row_at + start, step), step)
        old = rows_old[:, lanes] * keep
        line = jnp.zeros((8, 128), jnp.float32)
        for m in range(step // 8):
            block = grad[pl.ds(start + 8 * m, 8), :]
            square = block * block
            col_sum = col_sum + square
            part = square[:, :128]
            for q in range(1, quarters):
                part = part + square[:, 128 * q : 128 * (q + 1)]
            part = part * ((1.0 - keep) / width)
            diagonal = eye_mask(8, 128, 8 * m)
            part = part + jnp.where(diagonal, jnp.broadcast_to(old, (8, 128)), 0.0)
            row = jnp.sum(part, axis=1, keepdims=True) + (1.0 - keep) * EPS_ROW
            row = jnp.broadcast_to(row, (8, 128))
            level[pl.ds(start + 8 * m, 8), :] = row
            row_sum = row_sum + row
            line = line + jnp.where(diagonal, row, 0.0)
        rows_new[:, lanes] = jnp.sum(line, axis=0, keepdims=True)
        return col_sum, row_sum

    col_sum, row_sum = lax.fori_loop(
        0,
        rows // step,
        first,
        (jnp.zeros((8, width), jnp.float32), jnp.zeros((8, 128), jnp.float32)),
    )
    col_new = keep * col_old + (1.0 - keep) * (
        jnp.sum(col_sum, axis=0, keepdims=True) / rows + EPS_ROW
    )
    scale = lax.rsqrt(col_new)
    root_mean = jnp.sqrt(jnp.sum(row_sum, axis=0, keepdims=True) / rows)

    def second(k, carry):
        start = pl.multiple_of(k * step, step)
        for m in range(step // 8):
            here = pl.ds(start + 8 * m, 8)
            factor = lax.rsqrt(level[here, :]) * root_mean
            level[here, :] = factor
            raw = grad[here, :] * scale
            power = raw * raw
            part = power[:, :128]
            for q in range(1, quarters):
                part = part + power[:, 128 * q : 128 * (q + 1)]
            carry = carry + part * (factor * factor)
        return carry

    between[0]()
    power = lax.fori_loop(0, rows // step, second, jnp.zeros((8, 128), jnp.float32))
    between[1]()
    clip = jnp.maximum(1.0, jnp.sqrt(total_of(power) / (rows * width)))
    scale = scale / clip

    def third(k, _):
        start = pl.multiple_of(k * step, step)
        for m in range(step // 16):
            here = pl.ds(start + 16 * m, 16)
            factor = level[here, :]
            factor = jnp.concatenate([factor] * quarters, axis=1)
            vote = jnp.tanh(grad[here, :] * factor * scale).astype(jnp.bfloat16)
            at = pl.multiple_of((vote_at + start) * 4 + GROUP * m, GROUP)
            for q in range(quarters):
                votes[pl.ds(at + 16 * q, 16), :] = vote[:, 128 * q : 128 * (q + 1)]
        return 0

    part = 512 // step
    for k in range(0, rows // step, part):
        lax.fori_loop(k, min(k + part, rows // step), third, 0)
        after(k // part)
    return col_new


def step_kernel(
    edges,
    units,
    root,
    images,
    one_hbm,
    two_hbm,
    short_hbm,
    head_ref,
    norm_ref,
    valid_ref,
    label_ref,
    row_ref,
    col_ref,
    moment_ref,
    new_ref,
    vote_ref,
    out_ref,
    row_new,
    col_new,
    moment_new,
    loss_ref,
    count_ref,
    xs,
    grad_one,
    grad_two,
    grad_short,
    low_one,
    low_two,
    low_short,
    main_pre,
    side_pre,
    main_two,
    active,
    back_two,
    back_one,
    back_side,
    active_t,
    xs_t,
    head_pad,
    level,
    square,
    post_one,
    plane_one,
    line_one,
    post_two,
    plane_two,
    line_two,
    tail_post,
    tail_plane,
    tail_line,
    core_in,
    wide_in,
    deep_in,
    line_in,
    sum_low,
    landed,
    total,
    own_weight,
    weight,
    vote_flat,
    new_flat,
    fetch_sem,
    small_send,
    small_recv,
    rs_send,
    rs_recv,
    line_send,
    line_recv,
    pass_send,
    land_recv,
    spread_send,
    spread_recv,
    ag_send,
    ag_recv,
    free_sem,
    load_sem,
):
    slots, in_width = xs.shape[4:]
    width = main_pre.shape[1]
    side = 4
    band = side * slots
    pixel_count = side * side
    classes = head_ref.shape[0]
    keep = 1.0 - STEP ** (-0.8)
    low = jnp.bfloat16
    f32 = jnp.float32

    me, core, x, y, z = place()
    flip_core = me + 1 - 2 * core
    flip_x = me + 2 - 4 * x
    flip_y = me + 4 - 8 * y
    spot = lax.rem(me, 8)
    near = [z * 8 + lax.rem(spot + k, 8) for k in range(1, 8)]
    far = [lax.rem(z + k, 4) * 8 + spot for k in range(1, 4)]
    others = [lax.rem(me + k, 32) for k in range(1, 32)]

    count = images.shape[0]
    loads = []
    for half in range(2):
        lanes = slice(128 * half, 128 * (half + 1))
        loads.append(
            pltpu.make_async_copy(
                images.at[:, lanes], core_in.at[pl.ds(half * count, count)], load_sem.at[half]
            )
        )
        loads[half].start()

    def chunks_of(source, target, first, count):
        rows = source.shape[0] // count
        return [
            pltpu.make_async_copy(
                source.at[pl.ds(k * rows, rows)],
                target.at[pl.ds(k * rows, rows)],
                fetch_sem.at[first + k],
            )
            for k in range(count)
        ]

    fetch_one = chunks_of(one_hbm, grad_one, 0, 3)
    fetch_short = chunks_of(short_hbm, grad_short, 3, 1)
    fetch_two = chunks_of(two_hbm, grad_two, 4, 3)
    for fetch in fetch_one + fetch_short:
        fetch.start()
    barrier = pltpu.get_barrier_semaphore()
    for partner in others:
        pl.semaphore_signal(barrier, inc=1, device_id=(partner,), device_id_type=MESH)

    def fetch_rows(row, count, place_at, sem):
        parts = (
            (one_hbm, 0, edges[0]),
            (two_hbm, edges[0], edges[1]),
            (short_hbm, edges[1], edges[2]),
        )
        for ref, first, last in parts:

            @pl.when(jnp.logical_and(row >= first, row < last))
            def _():
                start = pl.multiple_of(row - first, count)
                pltpu.make_async_copy(
                    ref.at[pl.ds(start, count)], weight.at[pl.ds(place_at, count)], sem
                ).start()

    first_row = me * OWN

    for half in range(2):
        lanes = slice(128 * half, 128 * (half + 1))
        loads[half].wait()
        level[:count, :] = core_in[pl.ds(half * count, count), :].astype(f32)
        for h in range(2 * side):
            for w in range(2 * side):
                rows = level[pl.ds(2 * side * h + w, slots, stride=4 * pixel_count), :]
                xs[w % 2, w // 2, h % 2, h // 2, :, lanes] = rows.astype(low)

    scales = {}

    def scale_from(weight_square, size):
        return jnp.maximum(EPS_SCALE, jnp.sqrt(total_of(weight_square) / size))

    exchanges = (
        (post_one, plane_one, line_one),
        (post_two, plane_two, line_two),
        (tail_post, tail_plane, tail_line),
    )

    def exchange_start(which, values):
        mine_ref, plane_ref, _ = exchanges[which]
        mine_ref[...] = values
        plane_ref[spot] = values
        return [
            send(
                mine_ref,
                plane_ref.at[spot],
                small_send.at[which, k],
                small_recv.at[which, k],
                partner,
            )
            for k, partner in enumerate(near)
        ]

    def pack_rows(rows):
        pieces = [row[:, 128 * q : 128 * (q + 1)] for row in rows for q in range(4)]
        pad = -len(pieces) % 8
        if pad:
            pieces.append(jnp.zeros((pad, 128), f32))
        return jnp.concatenate(pieces, axis=0)

    def unpack_row(lines_in, k):
        return jnp.concatenate([lines_in[4 * k + q : 4 * k + q + 1] for q in range(4)], axis=1)

    def exchange_middle(which, copies):
        _, plane_ref, line_ref = exchanges[which]
        for copy in copies:
            copy.wait()
        line_ref[z] = functools.reduce(lambda a, b: a + b, [plane_ref[k] for k in range(8)])
        return [
            send(
                line_ref.at[z],
                line_ref.at[z],
                small_send.at[which, 7 + k],
                small_recv.at[which, 7 + k],
                partner,
            )
            for k, partner in enumerate(far)
        ]

    def exchange_end(which, copies):
        line_ref = exchanges[which][2]
        for copy in copies:
            copy.wait()
        return (line_ref[0] + line_ref[1]) + (line_ref[2] + line_ref[3])

    def lines(start, count):
        return pl.ds(pl.multiple_of(start, 16), count)

    sizes = [GROUP * unit[1] for unit in units]
    starts = [sum(sizes[:k]) for k in range(len(units) + 1)]

    def part_of(ref, u, share, start, count):
        return ref.at[lines(share * starts[u] + start, count)]

    def places(u):
        if units[u][2]:
            return x, y, flip_x, flip_y
        return y, x, flip_y, flip_x

    def unit_start(u, cc):
        return GROUP * units[u][0] + cc * (GROUP * units[u][3])

    def own_group(u):
        first, second, _, _ = places(u)
        return units[u][0] + core * units[u][3] + (first * 8 + second * 4 + z) * units[u][1]

    def halve(source, target, u, stage, partner):
        return send(source, target, rs_send.at[u, stage], rs_recv.at[u, stage], partner)

    def scatter_start(u):
        size = 16 * sizes[u]
        return halve(
            out_ref.at[lines(unit_start(u, 1 - core), size)],
            part_of(core_in, u, 16, 0, size),
            u,
            0,
            flip_core,
        )

    def add_to(ref, u, share, source_ref, source_start):
        size = share * sizes[u]
        here = lines(share * starts[u], size)
        ref[here, :] = ref[here, :] + source_ref[lines(source_start, size), :]

    def scatter_one(u, copy):
        copy.wait()
        add_to(core_in, u, 16, out_ref, unit_start(u, core))
        pl.semaphore_signal(
            free_sem.at[u], inc=1, device_id=(flip_core,), device_id_type=MESH
        )
        first, _, flip_first, _ = places(u)
        size = 8 * sizes[u]
        return halve(
            part_of(core_in, u, 16, (1 - first) * size, size),
            part_of(wide_in, u, 8, 0, size),
            u,
            1,
            flip_first,
        )

    def scatter_two(u, copy):
        copy.wait()
        first, second, _, flip_second = places(u)
        add_to(wide_in, u, 8, core_in, 16 * starts[u] + first * 8 * sizes[u])
        size = 4 * sizes[u]
        return halve(
            part_of(wide_in, u, 8, (1 - second) * size, size),
            part_of(deep_in, u, 4, 0, size),
            u,
            2,
            flip_second,
        )

    def line_copy(u, k):
        plane_to = lax.rem(z + k, 4)
        return pltpu.make_async_remote_copy(
            src_ref=part_of(deep_in, u, 4, plane_to * sizes[u], sizes[u]),
            dst_ref=part_of(line_in, u, 4, z * sizes[u], sizes[u]),
            send_sem=line_send.at[u, k],
            recv_sem=line_recv.at[u, k],
            device_id=(plane_to * 8 + spot,),
            device_id_type=MESH,
        )

    def scatter_three(u, copy):
        copy.wait()
        _, second, _, _ = places(u)
        add_to(deep_in, u, 4, wide_in, 8 * starts[u] + second * 4 * sizes[u])
        for k in (3, 2, 1):
            line_copy(u, k).start()
        here = lines(4 * starts[u] + z * sizes[u], sizes[u])
        line_in[here, :] = deep_in[here, :]

    groups = (edges[2] + TAIL) // 16
    spare = (groups - 1) // 32
    passes = []

    def land(local, group, to, slot, index):
        source = sum_low.at[lines(local * GROUP, GROUP)]
        target = landed.at[lines(slot * GROUP, GROUP)]
        copy = pltpu.make_async_remote_copy(
            src_ref=source,
            dst_ref=target,
            send_sem=pass_send.at[index],
            recv_sem=land_recv.at[slot],
            device_id=(to,),
            device_id_type=MESH,
        )
        return copy, source, target

    def pass_on(u):
        for m in range(units[u][1]):
            local = starts[u] // GROUP + m
            group = own_group(u) + m
            to, slot = lax.div(group, spare), lax.rem(group, spare)
            for halo in range(2):
                index = 2 * local + halo
                if halo:
                    receiver, at = lax.rem(to + 31, 32), spare
                    wanted = jnp.logical_and(slot == 0, group > 0)
                else:
                    receiver, at, wanted = to, slot, group >= 0
                away = jnp.logical_and(wanted, receiver != me)
                here = jnp.logical_and(wanted, receiver == me)
                copy, source, target = land(local, group, receiver, at, index)

                @pl.when(away)
                def _():
                    copy.start()

                @pl.when(here)
                def _():
                    target[...] = source[...]

                passes.append((away, copy))

    def flat_rows(row, q, values, ref):
        ref[pl.ds(row * 4 + q, 8, stride=4), :] = values

    def old_rows(u, cc):
        matrix = units[u][4][cc]
        base = edges[matrix - 1] if matrix else 0
        return (one_hbm, two_hbm, short_hbm)[matrix], 16 * own_group(u) - base, 16 * units[u][1]

    def own_fetch(u):
        target = own_weight.at[pl.ds(starts[u] // 4, 16 * units[u][1])]
        matrices = units[u][4]
        for cc in range(2):
            if cc and matrices[0] == matrices[1]:
                continue

            @pl.when((core == cc) if matrices[0] != matrices[1] else (core >= 0))
            def _():
                ref, row, count = old_rows(u, cc)
                pltpu.make_async_copy(
                    ref.at[pl.ds(pl.multiple_of(row, 16), count)], target, fetch_sem.at[9 + u]
                ).start()

    def spread_copy(u, k):
        own = out_ref.at[lines(own_group(u) * GROUP, sizes[u])]
        return pltpu.make_async_remote_copy(
            src_ref=own,
            dst_ref=own,
            send_sem=spread_send.at[u, k],
            recv_sem=spread_recv.at[u, k],
            device_id=(far[k - 1],),
            device_id_type=MESH,
        )

    def own_block(u):
        size = sizes[u]
        for k in range(1, 4):
            line_copy(u, k).wait_recv()
        here = pl.ds(starts[u], size)
        low_sum = functools.reduce(
            lambda a, b: a + b,
            [line_in[pl.ds(4 * starts[u] + t * size, size), :].astype(f32) for t in range(4)],
        ).astype(low)
        sum_low[here, :] = low_sum
        total[here, :] = low_sum.astype(f32)
        target = own_weight.at[pl.ds(starts[u] // 4, 16 * units[u][1])]
        pltpu.make_async_copy(target, target, fetch_sem.at[9 + u]).wait()
        matrices = units[u][4]
        scale = jnp.where(core == 0, scales[matrices[0]], scales[matrices[1]])
        for m in range(units[u][1]):
            row = starts[u] // 4 + 16 * m
            for part in (0, 8):
                for q in range(4):
                    summed = total[pl.ds(row * 4 + 16 * q + part, 8), :]
                    old = own_weight[pl.ds(row + part, 8), 128 * q : 128 * (q + 1)]
                    fresh = old - scale * jnp.tanh(summed * root)
                    flat_rows(row + part, q, fresh, new_flat)
        out_ref[lines(own_group(u) * GROUP, size), :] = new_flat[here, :].astype(low)
        for k in (3, 2, 1):
            spread_copy(u, k).start()
        pass_on(u)

    def piece(rows, u, stage, partner):
        return send(
            out_ref.at[rows], out_ref.at[rows], ag_send.at[u, stage], ag_recv.at[u, stage], partner
        )

    def gather_one(u):
        for k in range(1, 4):
            spread_copy(u, k).wait_recv()
        first, second, _, flip_second = places(u)
        size = 4 * sizes[u]
        start = unit_start(u, core) + (2 * first + second) * size
        return piece(lines(start, size), u, 0, flip_second)

    def gather_two(u, copy):
        copy.wait()
        first, _, flip_first, _ = places(u)
        size = 8 * sizes[u]
        return piece(lines(unit_start(u, core) + first * size, size), u, 1, flip_first)

    def gather_three(u, copy):
        copy.wait()
        pl.semaphore_wait(free_sem.at[u], 1)
        return piece(lines(unit_start(u, core), 16 * sizes[u]), u, 2, flip_core)

    def renew(row, at_row):
        scale = scale_of(at_row, [scales[k] for k in range(3)], edges)
        for part in (0, 8):
            for q in range(4):
                summed = total[pl.ds(row * 4 + 16 * q + part, 8), :]
                old = weight[pl.ds(row + part, 8), 128 * q : 128 * (q + 1)]
                fresh = old - scale * jnp.tanh(summed * root)
                flat_rows(row + part, q, summed, vote_flat)
                flat_rows(row + part, q, fresh, new_flat)

    valid_column = column_of(valid_ref[...].astype(f32), slots)
    weight_slot = jnp.broadcast_to(valid_column, (slots, width))
    weight_band = jnp.concatenate([weight_slot] * side, axis=0)

    cast_weight(grad_one, low_one, square, 9, in_width, fetch_one)
    scales[0] = scale_from(square[...], grad_one.size)
    cast_weight(grad_short, low_short, square, 1, in_width, fetch_short)
    scales[2] = scale_from(square[...], grad_short.size)
    for fetch in fetch_two:
        fetch.start()
    for k in range(OWN // PIECE):
        fetch_rows(first_row + k * PIECE, PIECE, k * PIECE, fetch_sem.at[7])
    fetch_rows(first_row + OWN, TAIL, OWN, fetch_sem.at[8])
    for u in range(len(units)):
        own_fetch(u)

    def image_taps(j):
        pieces = []
        for b in range(3):
            column = j if b else j - 1
            if column < 0:
                continue
            across = 0 if b == 1 else 1
            for a in range(3):
                if a == 1:
                    piece = xs[across, column, 0].reshape(band, in_width)
                elif a == 2:
                    piece = xs[across, column, 1].reshape(band, in_width)
                else:
                    piece = xs[across, column, 1, : side - 1].reshape(band - slots, in_width)
                    piece = jnp.concatenate([jnp.zeros((slots, in_width), low), piece], axis=0)
                pieces.append(piece)
        return jnp.concatenate(pieces, axis=1)

    def moments(values):
        weighted = values * weight_band
        return (
            jnp.sum(weighted, axis=0, keepdims=True),
            jnp.sum(weighted * values, axis=0, keepdims=True),
        )

    def add_up(old, new):
        return [a + b for a, b in zip(old, new)]

    none = jnp.zeros((1, width), f32)
    main_sums, side_sums = [none, none], [none, none]
    for j in range(side):
        here = pl.ds(j * band, band)
        low_rows = low_one[3 if j == 0 else 0 :].reshape(-1, width)
        value = jnp.dot(image_taps(j), low_rows, preferred_element_type=f32)
        main_pre[here, :] = value
        main_sums = add_up(main_sums, moments(value))
        value = jnp.dot(
            xs[0, j, 0].reshape(band, in_width), low_short[0], preferred_element_type=f32
        )
        side_pre[here, :] = value
        side_sums = add_up(side_sums, moments(value))

    count = jnp.broadcast_to(jnp.sum(valid_column, axis=0, keepdims=True), (1, width))
    pl.semaphore_wait(barrier, len(others))
    copies = exchange_start(
        0, pack_rows(main_sums + side_sums + [count])
    )
    cast_weight(grad_two, low_two, square, 9, width, fetch_two)
    scales[1] = scale_from(square[...], grad_two.size)
    copies = exchange_middle(0, copies)
    for across in range(2):
        for down in range(2):
            for j in range(side):
                block = xs[across, j, down].reshape(band, in_width)
                xs_t[across, down, :, j * band : (j + 1) * band] = block.T
    border = jnp.zeros((side, 1, slots, width), low)
    active[:, 0:1] = border
    active[:, side + 1 :] = border
    back_two[:, 0:1] = border
    back_two[:, side + 1 :] = border
    back_one[:, side:] = border
    head_pad[...] = jnp.zeros_like(head_pad)
    head_pad[:classes, :] = head_ref[...]
    head = head_pad[:16, :]
    scales[3] = scale_from(head * head, head_ref.size)
    params = norm_ref[...]
    scales[4] = scale_from(params * params, norm_ref.size)
    sums = exchange_end(0, copies)
    sums = [unpack_row(sums, k) for k in range(5)]

    valid_count = sums[4]
    count_ref[...] = valid_count[:, :1]
    denominator = jnp.maximum(valid_count, 1.0)
    pixels = denominator * pixel_count
    gains = [norm_ref[k : k + 1, :] for k in range(6)]
    mean_one, inv_one, slope_one, base_one = settle_rows(
        (sums[0], sums[1]), pixels, gains[0], gains[1]
    )
    mean_side, inv_side, slope_side, base_side = settle_rows(
        (sums[2], sums[3]), pixels, gains[4], gains[5]
    )

    for j in range(side):
        hidden = main_pre[pl.ds(j * band, band), :] * slope_one + base_one
        active[j, 1 : side + 1] = (
            (hidden * gate(hidden)).astype(low).reshape(side, slots, width)
        )
    two_sums = [none, none]
    for j in range(side):
        taps = [b for b in range(3) if 0 <= j + b - 1 < side]
        pieces = [
            active[j + b - 1, a : a + side].reshape(band, width) for b in taps for a in range(3)
        ]
        low_rows = low_two[3 * taps[0] : 3 * taps[-1] + 3].reshape(-1, width)
        value = jnp.dot(jnp.concatenate(pieces, axis=1), low_rows, preferred_element_type=f32)
        main_two[pl.ds(j * band, band), :] = value
        two_sums = add_up(two_sums, moments(value))
    copies = exchange_start(1, pack_rows(two_sums))
    for j in range(side):
        block = active[j, 1 : side + 1].reshape(band, width)
        active_t[:, j * band : (j + 1) * band] = block.T
    copies = exchange_middle(1, copies)
    sums = exchange_end(1, copies)
    sums = [unpack_row(sums, k) for k in range(2)]
    mean_two, inv_two, slope_two, base_two = settle_rows(
        (sums[0], sums[1]), pixels, gains[2], gains[3]
    )

    base_joined = base_two + base_side

    def joined_of(here):
        return main_two[here, :] * slope_two + side_pre[here, :] * slope_side + base_joined

    pooled = jnp.zeros((slots, width), f32)
    for p in range(pixel_count):
        joined = joined_of(pl.ds(p * slots, slots))
        pooled = pooled + joined * gate(joined)
    pooled = (pooled / pixel_count).astype(low)
    head_low = head_pad[...].astype(low)
    logits = lax.dot_general(
        pooled, head_low, (((1,), (1,)), ((), ())), preferred_element_type=f32
    )
    lane = lax.broadcasted_iota(jnp.int32, logits.shape, 1)
    real = lane < classes
    largest = jnp.max(jnp.where(real, logits, -jnp.inf), axis=1, keepdims=True)
    powers = jnp.where(real, jnp.exp(jnp.where(real, logits - largest, 0.0)), 0.0)
    total_power = jnp.sum(powers, axis=1, keepdims=True)
    label_column = column_of(label_ref[...].astype(f32), slots).astype(jnp.int32)
    onehot = jnp.where(lane == label_column, 1.0, 0.0)
    entropy = largest + jnp.log(total_power) - jnp.sum(onehot * logits, axis=1, keepdims=True)
    loss = jnp.sum(entropy * valid_column, axis=0, keepdims=True)
    grad_logits = (
        (powers / total_power - onehot) * (valid_column / denominator[:, :1])
    ).astype(low)
    grad_head = lax.dot_general(
        grad_logits, pooled, (((0,), (0,)), ((), ())), preferred_element_type=f32
    )[:16]
    grad_pooled = jnp.dot(grad_logits, head_low, preferred_element_type=f32) / pixel_count

    gain_two, gain_side, shift_two = none, none, none
    for p in range(pixel_count):
        here = pl.ds(p * slots, slots)
        joined = joined_of(here)
        opened = gate(joined)
        grad = grad_pooled * (opened * (1.0 + joined * (1.0 - opened)))
        shift_two = shift_two + jnp.sum(grad, axis=0, keepdims=True)
        gain_two = gain_two + jnp.sum(
            grad * ((main_two[here, :] - mean_two) * inv_two), axis=0, keepdims=True
        )
        gain_side = gain_side + jnp.sum(
            grad * ((side_pre[here, :] - mean_side) * inv_side), axis=0, keepdims=True
        )
        back_two[p // side, 1 + p % side] = (grad * slope_two).astype(low)
        back_side[here, :] = (grad * slope_side).astype(low)

    for b in range(3):
        first, last = max(0, b - 1), min(side, side + b - 1)
        left = active_t[:, first * band : last * band]
        for a in range(3):
            right = back_two[first - b + 1 : last - b + 1, 2 - a : 2 - a + side]
            grad_two[pl.ds((a * 3 + b) * width, width), :] = jnp.dot(
                left, right.reshape(-1, width), preferred_element_type=f32
            )

    def nothing():
        pass

    def matrix_votes(k, grad, between, after):
        here = pl.ds(k * width, width)
        start = edges[k - 1] if k else 0
        col_new[:, here] = factored_votes(
            grad,
            grad.shape[0],
            start,
            row_ref,
            row_new,
            col_ref[:, here],
            level,
            out_ref,
            start,
            between,
            after,
        )

    kept = {}

    def tail_step():
        sums = exchange_end(2, kept["tail"])
        loss_ref[...] = sums[4 * TAIL : 4 * TAIL + 1, :1]
        old = jnp.concatenate([head_ref[...], norm_ref[...]], axis=0)
        is_head = lax.broadcasted_iota(jnp.int32, (TAIL, width), 0) < classes
        scale = jnp.where(is_head, scales[3], scales[4])
        sums = jnp.concatenate([sums[TAIL * q : TAIL * (q + 1)] for q in range(4)], axis=1)
        fresh = old - scale * jnp.tanh(sums * root)
        both = jnp.concatenate([sums, fresh], axis=0)
        high = both.astype(low)
        rest = both - high.astype(f32)
        middle = rest.astype(low)
        parts = jnp.concatenate([high, middle, (rest - middle.astype(f32)).astype(low)], axis=0)

        flat_sums, flat_new = [], []
        window = 256
        for q in range(classes):
            start = min(q * width // classes // 128 * 128, width - window)
            down = lax.broadcasted_iota(jnp.int32, (window, width), 0)
            across = lax.broadcasted_iota(jnp.int32, (window, width), 1)
            gap = across - classes * down + (q * width - classes * start)
            chosen = jnp.where(jnp.logical_and(gap >= 0, gap < classes), 1.0, 0.0).astype(low)
            moved = jnp.dot(parts[:, start : start + window], chosen, preferred_element_type=f32)
            moved = moved[: 2 * TAIL] + moved[2 * TAIL : 4 * TAIL] + moved[4 * TAIL :]
            spot_of = lax.broadcasted_iota(jnp.int32, (TAIL, width), 1).astype(f32) + q * width
            class_of = spot_of - classes * jnp.floor((spot_of + 0.5) / classes)
            here = lax.broadcasted_iota(jnp.int32, (TAIL, width), 0).astype(f32) == class_of
            flat_sums.append(jnp.sum(jnp.where(here, moved[:TAIL], 0.0), axis=0, keepdims=True))
            flat_new.append(jnp.sum(jnp.where(here, moved[TAIL:], 0.0), axis=0, keepdims=True))
        kept["sums"] = jnp.concatenate(flat_sums + [sums[classes:]], axis=0)
        kept["new"] = jnp.concatenate(flat_new + [fresh[classes:]], axis=0)

    def return_step():
        mine = [own_group(u) for u in range(len(units))]
        for slot in range(spare + 1):
            group = me * spare + slot
            own = group < 0
            for u, unit in enumerate(units):
                inside = jnp.logical_and(group >= mine[u], group < mine[u] + unit[1])
                own = jnp.logical_or(own, inside)

            @pl.when(jnp.logical_and(jnp.logical_not(own), group < groups - 1))
            def _():
                land(0, group, me, slot, 0)[0].wait_recv()

        pltpu.make_async_copy(
            weight.at[pl.ds(0, OWN)], weight.at[pl.ds(0, OWN)], fetch_sem.at[7]
        ).wait()
        total[pl.ds(0, SPAN), :] = landed[pl.ds(0, SPAN), :].astype(f32)

        @pl.loop(0, OWN // 16)
        def _(k):
            row = pl.multiple_of(k * 16, 16)
            renew(row, first_row + row)

        @pl.when(me < 31)
        def _():
            pltpu.make_async_copy(
                weight.at[pl.ds(OWN, TAIL)], weight.at[pl.ds(OWN, TAIL)], fetch_sem.at[8]
            ).wait()
            total[pl.ds(SPAN, GROUP), :] = landed[pl.ds(SPAN, GROUP), :].astype(f32)
            renew(OWN, first_row + OWN)

        def tail_rows(values, ref):
            for u in (0, 8):
                for q in range(4):
                    flat_rows(OWN + u, q, values[u : u + 8, 128 * q : 128 * (q + 1)], ref)

        @pl.when(me == 31)
        def _():
            tail_rows(kept["sums"], vote_flat)
            tail_rows(kept["new"], new_flat)

        shift = 2 * me
        share = vote_ref.shape[0]
        vote_ref[...] = vote_flat[pl.ds(shift, share), :]
        new_ref[...] = new_flat[pl.ds(shift, share), :]
        tail_rows(kept["new"], new_flat)
        out_ref[pl.ds(32 * SPAN, GROUP), :] = new_flat[pl.ds(SPAN, GROUP), :].astype(low)

    in_flight = {}
    steps = (
        lambda u, copy: scatter_start(u),
        scatter_one,
        scatter_two,
        scatter_three,
        lambda u, copy: own_block(u),
        lambda u, copy: gather_one(u),
        gather_two,
        gather_three,
        lambda u, copy: tail_step(),
        lambda u, copy: return_step(),
    )

    def go(number, u):
        got = steps[number](u, in_flight.get(u))
        if number < 8:
            in_flight[u] = got

    def turn(number):
        for step_number, u in SCHEDULE[number]:
            go(step_number, u)

    early = edges[1] // 512 - edges[0] // 512
    matrix_votes(1, grad_two, (nothing, nothing), lambda k: go(0, k) if k < 2 else None)
    turn(0)
    grad_short[...] = jnp.dot(xs_t[0, 0], back_side[...], preferred_element_type=f32)
    matrix_votes(2, grad_short, (nothing, nothing), lambda k: None)

    gain_one, shift_one = none, none
    for j in range(side):
        taps = [b for b in range(3) if 0 <= j - b + 1 < side]
        pieces = [
            back_two[j - b + 1, 2 - a : 2 - a + side].reshape(band, width)
            for b in taps
            for a in range(3)
        ]
        weights = jnp.concatenate([low_two[b * 3 + a] for b in taps for a in range(3)], axis=1)
        grad = lax.dot_general(
            jnp.concatenate(pieces, axis=1),
            weights,
            (((1,), (1,)), ((), ())),
            preferred_element_type=f32,
        )
        before = main_pre[pl.ds(j * band, band), :]
        hidden = before * slope_one + base_one
        opened = gate(hidden)
        grad = grad * (opened * (1.0 + hidden * (1.0 - opened)))
        shift_one = shift_one + jnp.sum(grad, axis=0, keepdims=True)
        gain_one = gain_one + jnp.sum(
            grad * ((before - mean_one) * inv_one), axis=0, keepdims=True
        )
        back_one[j, :side] = (grad * slope_one).astype(low).reshape(side, slots, width)
        turn(1 + j)

    square_head = grad_head * grad_head + EPS_ROW
    real = lax.broadcasted_iota(jnp.int32, square_head.shape, 0) < classes
    square_head = jnp.where(real, square_head, 0.0)
    head_lanes = pl.ds(edges[2], width)
    old = row_ref[:, head_lanes]
    row = keep * old + (1.0 - keep) * jnp.sum(square_head, axis=0, keepdims=True) / classes
    row_new[:, head_lanes] = row
    diagonal = eye_mask(16, classes)
    old = jnp.broadcast_to(col_ref[:, 3 * width :], (16, classes))
    old = jnp.sum(jnp.where(diagonal, old, 0.0), axis=1, keepdims=True)
    column = keep * old + (1.0 - keep) * jnp.sum(square_head, axis=1, keepdims=True) / width
    col_new[:, 3 * width :] = jnp.sum(
        jnp.where(diagonal, jnp.broadcast_to(column, (16, classes)), 0.0), axis=0, keepdims=True
    )
    real_column = lax.broadcasted_iota(jnp.int32, column.shape, 0) < classes
    column = jnp.where(real_column, column, 1.0)
    mean = jnp.sum(row, axis=1, keepdims=True) / width
    raw = grad_head * (lax.rsqrt(row) * jnp.sqrt(mean)) * lax.rsqrt(column)
    clip = jnp.maximum(1.0, jnp.sqrt(total_of(raw * raw) / (classes * width)))
    head_votes = jnp.tanh(raw / clip)[:classes]

    raws = []
    for k, grad in enumerate((gain_one, shift_one, gain_two, shift_two, gain_side, shift_two)):
        here = pl.ds(k * width, width)
        moment = keep * moment_ref[:, here] + (1.0 - keep) * (grad * grad + EPS_ROW)
        moment_new[:, here] = moment
        raws.append(grad * lax.rsqrt(moment))
    raw = jnp.concatenate(raws, axis=0)
    clip = jnp.maximum(1.0, jnp.sqrt(total_of(raw * raw) / raw.size))
    norm_votes = jnp.tanh(raw / clip)
    tail_votes = jnp.concatenate([head_votes, norm_votes], axis=0)
    kept["tail"] = exchange_start(
        2,
        jnp.concatenate(
            [tail_votes[:, 128 * q : 128 * (q + 1)] for q in range(4)]
            + [jnp.broadcast_to(loss, (8, 128))],
            axis=0,
        ),
    )


    for b in range(3):
        first, last = (0, side - 1) if b == 0 else (0, side)
        shift = 1 if b == 0 else 0
        for a in range(3):
            left = xs_t[0 if b == 1 else 1, 0 if a == 1 else 1, :, first * band : last * band]
            start = 1 if a == 0 else 0
            right = back_one[first + shift : last + shift, start : start + side]
            grad_one[pl.ds((a * 3 + b) * in_width, in_width), :] = jnp.dot(
                left, right.reshape(-1, width), preferred_element_type=f32
            )
        if b == 1:
            kept["tail"] = exchange_middle(2, kept["tail"])
        turn(5 + b)

    matrix_votes(
        0,
        grad_one,
        (lambda: turn(8), lambda: turn(9)),
        lambda k: go(0, early + k) if k < 2 else None,
    )
    turn(10)
    for u in range(len(units)):
        in_flight[u].wait()
        for k in range(1, 4):
            line_copy(u, k).wait_send()
            spread_copy(u, k).wait_send()
    for away, copy in passes:

        @pl.when(away)
        def _():
            copy.wait_send()


def finish_kernel(count, chunks, *refs):
    sources, targets, sem = refs[:count], refs[count : 2 * count], refs[2 * count]
    rows = sources[0].shape[0]
    step = -(-rows // chunks // 16) * 16
    copies = []
    for k in range(chunks):
        here = pl.ds(k * step, min(step, rows - k * step))
        copies.append(
            pltpu.make_async_copy(sources[0].at[here], targets[0].at[here], sem.at[k])
        )
    for k in range(1, count - 2):
        copies.append(pltpu.make_async_copy(sources[k], targets[k], sem.at[chunks + k]))
    for copy in copies:
        copy.start()
    for k in (count - 2, count - 1):
        targets[k][...] = sources[k][...]
    for copy in copies:
        copy.wait()


def finish(values):
    vmem = pl.BlockSpec(memory_space=pltpu.VMEM)
    hbm = pl.BlockSpec(memory_space=pl.ANY)
    count, chunks = len(values), 8
    held = [pltpu.with_memory_space_constraint(value, pltpu.VMEM) for value in values[:-2]]
    return pl.pallas_call(
        functools.partial(finish_kernel, count, chunks),
        out_shape=[jax.ShapeDtypeStruct(value.shape, value.dtype) for value in values],
        in_specs=[vmem] * count,
        out_specs=[hbm] * (count - 2) + [vmem] * 2,
        scratch_shapes=[pltpu.SemaphoreType.DMA((chunks + count,))],
        compiler_params=pltpu.CompilerParams(vmem_limit_bytes=1024 * 1024),
        name="finish",
    )(*held, *values[-2:])


def run_step(images, conv_one, conv_two, shortcut, head, norm_params, valid, labels, rows, cols, moment):
    vmem = pl.BlockSpec(memory_space=pltpu.VMEM)
    hbm = pl.BlockSpec(memory_space=pl.ANY)
    low, f32 = jnp.bfloat16, jnp.float32
    dma = pltpu.SemaphoreType.DMA
    workers = lax.axis_size("dp")
    slots, in_width = valid.shape[1], images.shape[1]
    width = conv_one.shape[1]
    pixels = images.shape[0] // 4
    shape = pltpu.VMEM
    edges = [conv_one.shape[0]]
    edges.append(edges[0] + conv_two.shape[0])
    edges.append(edges[1] + shortcut.shape[0])
    units = make_units(edges)
    flat = (edges[2] + TAIL) * width // 128
    share = flat // workers
    return pl.pallas_call(
        functools.partial(step_kernel, tuple(edges), tuple(units), 1.0 / math.sqrt(workers)),
        out_shape=(
            shape((share, 128), f32),
            shape((share, 128), f32),
            shape((flat, 128), low),
            shape(rows.shape, f32),
            shape(cols.shape, f32),
            shape(moment.shape, f32),
            jax.ShapeDtypeStruct((1, 1), f32),
            jax.ShapeDtypeStruct((1, 1), f32),
        ),
        in_specs=[hbm] * 4 + [vmem] * 7,
        out_specs=(vmem,) * 8,
        scratch_shapes=[
            pltpu.VMEM((2, 4, 2, 4, slots, in_width), low),
            pltpu.VMEM(conv_one.shape, f32),
            pltpu.VMEM(conv_two.shape, f32),
            pltpu.VMEM(shortcut.shape, f32),
            pltpu.VMEM((9, in_width, width), low),
            pltpu.VMEM((9, width, width), low),
            pltpu.VMEM((1, in_width, width), low),
            pltpu.VMEM((pixels, width), f32),
            pltpu.VMEM((pixels, width), f32),
            pltpu.VMEM((pixels, width), f32),
            pltpu.VMEM((4, 6, slots, width), low),
            pltpu.VMEM((4, 6, slots, width), low),
            pltpu.VMEM((4, 5, slots, width), low),
            pltpu.VMEM((pixels, width), low),
            pltpu.VMEM((width, pixels), low),
            pltpu.VMEM((2, 2, in_width, pixels), low),
            pltpu.VMEM((128, width), f32),
            pltpu.VMEM((conv_two.shape[0], 128), f32),
            pltpu.VMEM((8, width), f32),
            pltpu.VMEM((24, 128), f32),
            pltpu.VMEM((8, 24, 128), f32),
            pltpu.VMEM((4, 24, 128), f32),
            pltpu.VMEM((8, 128), f32),
            pltpu.VMEM((8, 8, 128), f32),
            pltpu.VMEM((4, 8, 128), f32),
            pltpu.VMEM((GROUP + 8, 128), f32),
            pltpu.VMEM((8, GROUP + 8, 128), f32),
            pltpu.VMEM((4, GROUP + 8, 128), f32),
            pltpu.VMEM((16 * SPAN, 128), low),
            pltpu.VMEM((8 * SPAN, 128), low),
            pltpu.VMEM((4 * SPAN, 128), low),
            pltpu.VMEM((4 * SPAN, 128), low),
            pltpu.VMEM((SPAN, 128), low),
            pltpu.VMEM((SPAN + GROUP, 128), low),
            pltpu.VMEM((SPAN + GROUP, 128), f32),
            pltpu.VMEM((OWN, width), f32),
            pltpu.VMEM((OWN + TAIL, width), f32),
            pltpu.VMEM((SPAN + GROUP, 128), f32),
            pltpu.VMEM((SPAN + GROUP, 128), f32),
            dma((9 + len(units),)),
            dma((3, 10)),
            dma((3, 10)),
            dma((len(units), 3)),
            dma((len(units), 3)),
            dma((len(units), 4)),
            dma((len(units), 4)),
            dma((2 * OWN // 16,)),
            dma((OWN // 16 + 1,)),
            dma((len(units), 4)),
            dma((len(units), 4)),
            dma((len(units), 3)),
            dma((len(units), 3)),
            pltpu.SemaphoreType.REGULAR((len(units),)),
            dma((2,)),
        ],
        compiler_params=pltpu.CompilerParams(
            collective_id=1, has_side_effects=True, vmem_limit_bytes=54 * 1024 * 1024
        ),
        name="step",
    )(images, conv_one, conv_two, shortcut, head, norm_params, valid, labels, rows, cols, moment)


def scale_for(weight):
    return jnp.maximum(EPS_SCALE, jnp.sqrt(jnp.mean(weight * weight)))


def local_general(
    images,
    valid_slot,
    labels,
    conv_one,
    conv_two,
    shortcut,
    classifier,
    norm_params,
    row_state,
    col_state,
    bn_moment,
):
    in_width = images.shape[3]
    width = conv_one.shape[1]
    kernel_one = conv_one.astype(jnp.bfloat16).reshape(3, 3, in_width, width)
    kernel_two = conv_two.astype(jnp.bfloat16).reshape(3, 3, width, width)
    kernel_short = shortcut.astype(jnp.bfloat16).reshape(1, 1, in_width, width)
    head_low = classifier.astype(jnp.bfloat16)
    slot_count = images.shape[0]
    out_side = images.shape[1] // 2
    pixel_count = out_side * out_side
    slot_weight = valid_slot.astype(jnp.float32)
    pixel_weight = jnp.broadcast_to(slot_weight[:, None], (slot_count, pixel_count)).reshape(-1, 1)
    main_pre, side_pre = first_section(images, kernel_one, kernel_short)
    main_sums = masked_moments(pixel_weight, main_pre)
    side_sums = masked_moments(pixel_weight, side_pre)
    count_row = jnp.broadcast_to(jnp.sum(slot_weight), (width,))
    first_sums = lax.psum(jnp.stack([*main_sums, *side_sums, count_row]), "dp")
    valid_count = first_sums[4, 0]
    denominator = jnp.maximum(valid_count, 1.0)
    pixels = denominator * pixel_count
    norm_one = settle(first_sums[0], first_sums[1], pixels)
    norm_side = settle(first_sums[2], first_sums[3], pixels)
    hidden_one, active, main_two = second_section(
        main_pre, norm_one, norm_params, kernel_two, slot_count, out_side
    )
    two_sums = masked_moments(pixel_weight, main_two)
    second_sums = lax.psum(jnp.stack([*two_sums]), "dp")
    norm_two = settle(second_sums[0], second_sums[1], pixels)
    joined_pre = (
        (main_two - norm_two[0]) * norm_two[1] * norm_params[2]
        + norm_params[3]
        + (side_pre - norm_side[0]) * norm_side[1] * norm_params[4]
        + norm_params[5]
    )
    joined = jax.nn.silu(joined_pre).reshape(slot_count, pixel_count, -1)
    pooled = jnp.mean(joined, axis=1).astype(jnp.bfloat16)
    logits = jnp.dot(pooled, head_low, preferred_element_type=jnp.float32)
    largest = jnp.max(logits, axis=1, keepdims=True)
    exp_terms = jnp.exp(logits - largest)
    total_exp = jnp.sum(exp_terms, axis=1, keepdims=True)
    log_total = largest[:, 0] + jnp.log(total_exp[:, 0])
    onehot = (labels[:, None] == jnp.arange(logits.shape[1], dtype=jnp.int32)[None, :]).astype(
        jnp.float32
    )
    local_sum = jnp.sum(slot_weight * (log_total - jnp.sum(onehot * logits, axis=1)))
    grad_logits = ((exp_terms / total_exp - onehot) * (slot_weight / denominator)[:, None]).astype(
        jnp.bfloat16
    )
    grad_head = lax.dot_general(
        pooled, grad_logits, (((0,), (0,)), ((), ())), preferred_element_type=jnp.float32
    )
    grad_pooled = lax.dot_general(
        grad_logits, head_low, (((1,), (1,)), ((), ())), preferred_element_type=jnp.float32
    )
    spread_pooled = jnp.broadcast_to(
        (grad_pooled / pixel_count)[:, None, :], (slot_count, pixel_count, width)
    )
    grad_joined = spread_pooled.reshape(slot_count * pixel_count, width) * silu_slope(joined_pre)
    gain_two, shift_two, grad_two = norm_backward(grad_joined, main_two, norm_two, norm_params[2])
    gain_side, shift_side, grad_side = norm_backward(
        grad_joined, side_pre, norm_side, norm_params[4]
    )
    grad_two_maps = grad_two.reshape(slot_count, out_side, out_side, width)
    grad_side_maps = grad_side.reshape(slot_count, out_side, out_side, width)
    grad_conv_two = conv_weight_grad(active, grad_two_maps, 1, 1, 1)
    grad_short = conv_weight_grad(images, grad_side_maps, 2, 0, -1)
    kernel_turned = jnp.transpose(kernel_two[::-1, ::-1], (0, 1, 3, 2))
    grad_active = conv_apply(grad_two_maps, kernel_turned, 1, 1).reshape(
        slot_count * pixel_count, width
    )
    grad_hidden = grad_active * silu_slope(hidden_one)
    gain_one, shift_one, grad_one = norm_backward(grad_hidden, main_pre, norm_one, norm_params[0])
    grad_conv_one = conv_weight_grad(
        images, grad_one.reshape(slot_count, out_side, out_side, width), 2, 1, 0
    )
    grad_norms = jnp.stack([gain_one, shift_one, gain_two, shift_two, gain_side, shift_side])
    grads = (grad_conv_one, grad_conv_two, grad_short, grad_head, grad_norms)
    votes, rows_new, cols_new, moment_new = make_votes(
        grads, row_state[0], col_state[0], bn_moment[0]
    )
    workers = lax.axis_size("dp")
    weights = (conv_one, conv_two, shortcut, classifier, norm_params)
    scales = [scale_for(weight) for weight in weights]
    loss_sum = lax.psum(local_sum, "dp")
    flat_vote = jnp.concatenate([vote.reshape(-1) for vote in votes])
    flat_old = jnp.concatenate([weight.reshape(-1) for weight in weights])
    flat_scale = jnp.concatenate(
        [
            jnp.broadcast_to(scale, (weight.size,))
            for scale, weight in zip(scales, weights)
        ]
    )
    vote_mine = lax.psum_scatter(flat_vote, "dp", tiled=True)
    share = vote_mine.shape[0]
    start = lax.axis_index("dp") * share
    new_mine = lax.dynamic_slice_in_dim(
        flat_old, start, share
    ) - lax.dynamic_slice_in_dim(flat_scale, start, share) * jnp.tanh(
        vote_mine / math.sqrt(workers)
    )
    copies = lax.all_gather(new_mine.astype(jnp.bfloat16), "dp", tiled=True)
    return (
        loss_sum,
        valid_count,
        new_mine,
        copies,
        vote_mine,
        rows_new[None, :],
        cols_new[None, :],
        moment_new[None, :],
    )


def local(
    images,
    valid_slot,
    labels,
    conv_one,
    conv_two,
    shortcut,
    classifier,
    norm_params,
    row_state,
    col_state,
    bn_moment,
):
    new_mine, vote_mine, copies, rows_new, cols_new, moment_new, loss_sum, valid_count = run_step(
        images.reshape(-1, images.shape[-1]),
        conv_one,
        conv_two,
        shortcut,
        classifier.T,
        norm_params,
        valid_slot.reshape(1, -1),
        labels.reshape(1, -1),
        row_state,
        col_state,
        bn_moment,
    )
    copies, new_mine, vote_mine, rows_new, cols_new, moment_new, loss_sum, valid_count = finish(
        (copies, new_mine, vote_mine, rows_new, cols_new, moment_new, loss_sum, valid_count)
    )
    return (
        loss_sum.reshape(()),
        valid_count.reshape(()),
        new_mine.reshape(-1),
        copies.reshape(-1),
        vote_mine.reshape(-1),
        rows_new,
        cols_new,
        moment_new,
    )


def solution(mesh):
    placed = (
        P("dp", None, None, None),
        P("dp"),
        P("dp"),
        P(),
        P(),
        P(),
        P(),
        P(),
        P("dp", None),
        P("dp", None),
        P("dp", None),
    )
    return jax.shard_map(
        local if mesh.shape["dp"] == 32 else local_general,
        mesh=mesh,
        in_specs=placed,
        out_specs=(P(), P(), P("dp"), P(), P("dp"), P("dp", None), P("dp", None), P("dp", None)),
        check_vma=False,
    )
```

```python
import functools
import math

import jax
import jax.numpy as jnp
from jax import lax
from jax.experimental import pallas as pl
from jax.experimental.pallas import tpu as pltpu
from jax.sharding import PartitionSpec as P

STEP = 10
MESH = pl.DeviceIdType.MESH

EPS_NORM = 1e-05
EPS_ROW = 1e-30
EPS_SCALE = 0.001
FORWARD_DIMS = ("NHWC", "HWIO", "NHWC")
WEIGHT_DIMS = ("CHWN", "IHWO", "HWNC")
OWN = 224
TAIL = 16
PIECE = 32
SPAN = 4 * OWN
HALF = SPAN // 2
GROUP = 64


def conv_apply(maps, kernel, stride, margin):
    return lax.conv_general_dilated(
        maps,
        kernel,
        (stride, stride),
        ((margin, margin), (margin, margin)),
        dimension_numbers=FORWARD_DIMS,
        preferred_element_type=jnp.float32,
    )


def conv_weight_grad(maps, grad_out, stride, low_pad, high_pad):
    result = lax.conv_general_dilated(
        maps,
        grad_out,
        (1, 1),
        ((low_pad, high_pad), (low_pad, high_pad)),
        rhs_dilation=(stride, stride),
        dimension_numbers=WEIGHT_DIMS,
        preferred_element_type=jnp.float32,
    )
    return result.reshape(-1, result.shape[3])


def silu_slope(values):
    sigmoid_part = jax.nn.sigmoid(values)
    return sigmoid_part * (1.0 + values * (1.0 - sigmoid_part))


def settle(sum_plain, sum_square, pixels):
    mean_value = sum_plain / pixels
    return (mean_value, lax.rsqrt(sum_square / pixels - mean_value * mean_value + EPS_NORM))


def first_section(images, kernel_one, kernel_short):
    row_count = images.shape[0] * (images.shape[1] // 2) ** 2
    main_pre = conv_apply(images, kernel_one, 2, 1).reshape(row_count, -1)
    side_pre = conv_apply(images, kernel_short, 2, 0).reshape(row_count, -1)
    return (main_pre, side_pre)


def second_section(main_pre, norm_one, norm_params, kernel_two, slot_count, out_side):
    hidden_one = (main_pre - norm_one[0]) * norm_one[1] * norm_params[0] + norm_params[1]
    active = (
        jax.nn.silu(hidden_one).astype(jnp.bfloat16).reshape(slot_count, out_side, out_side, -1)
    )
    main_two = conv_apply(active, kernel_two, 1, 1).reshape(slot_count * out_side * out_side, -1)
    return (hidden_one, active, main_two)


def masked_moments(pixel_weight, values):
    return (jnp.sum(pixel_weight * values, axis=0), jnp.sum(pixel_weight * values * values, axis=0))


def soft_sign(step_raw):
    clip_by = jnp.maximum(1.0, jnp.sqrt(jnp.mean(step_raw * step_raw)))
    return jnp.tanh(step_raw / clip_by)


def make_votes(grads, rows_old, cols_old, moment_old):
    decay_rate = 1.0 - STEP ** (-0.8)
    votes, rows_new, cols_new = ([], [], [])
    row_at, col_at = (0, 0)
    for matrix in grads[:4]:
        row_size, col_size = matrix.shape
        square = matrix * matrix + EPS_ROW
        row_part = decay_rate * rows_old[row_at : row_at + row_size] + (
            1.0 - decay_rate
        ) * jnp.mean(square, axis=1)
        col_part = decay_rate * cols_old[col_at : col_at + col_size] + (
            1.0 - decay_rate
        ) * jnp.mean(square, axis=0)
        second = row_part[:, None] * col_part[None, :] / jnp.mean(row_part)
        votes.append(soft_sign(matrix * lax.rsqrt(second)))
        rows_new.append(row_part)
        cols_new.append(col_part)
        row_at += row_size
        col_at += col_size
    flat_norm = grads[4].reshape(-1)
    moment_new = decay_rate * moment_old + (1.0 - decay_rate) * (flat_norm * flat_norm + EPS_ROW)
    votes.append(soft_sign(flat_norm * lax.rsqrt(moment_new)))
    return (votes, jnp.concatenate(rows_new), jnp.concatenate(cols_new), moment_new)


def norm_backward(grad_out, pre_value, norm_pair, gain_row):
    normed = (pre_value - norm_pair[0]) * norm_pair[1]
    grad_gain = jnp.sum(grad_out * normed, axis=0)
    grad_shift = jnp.sum(grad_out, axis=0)
    grad_pre = (grad_out * gain_row * norm_pair[1]).astype(jnp.bfloat16)
    return (grad_gain, grad_shift, grad_pre)


SCHEDULE = (
    (),
    (
        (1, 0),
    ),
    (
        (0, 2), (1, 1),
    ),
    (
        (0, 3), (1, 2), (2, 0), (0, 4), (1, 3), (2, 1),
    ),
    (
        (0, 5), (1, 4), (2, 2), (3, 0),
    ),
    (
        (0, 6), (1, 5), (2, 3), (3, 1),
    ),
    (
        (0, 7), (1, 6), (2, 4), (3, 2), (4, 0),
    ),
    (),
    (
        (0, 8), (1, 7), (2, 5), (3, 3), (4, 1),
    ),
    (),
    (
        (1, 8), (2, 6), (3, 4), (4, 2), (1, 9), (2, 7), (3, 5), (4, 3), (5, 0), (0, 11), (1, 10),
        (2, 8), (3, 6), (4, 4), (5, 1), (0, 12), (1, 11), (2, 9), (3, 7), (4, 5), (5, 2), (6, 0),
        (0, 13), (1, 12), (2, 10), (3, 8), (4, 6), (5, 3), (6, 1), (1, 13), (2, 11), (3, 9),
        (4, 7), (8, 0), (5, 4), (6, 2), (2, 12), (3, 10), (4, 8), (5, 5), (6, 3), (7, 0),
        (2, 13), (3, 11), (4, 9), (5, 6), (6, 4), (7, 1), (3, 12), (4, 10), (5, 7), (6, 5),
        (7, 2), (3, 13), (4, 11), (5, 8), (6, 6), (7, 3), (4, 12), (5, 9), (6, 7), (7, 4),
        (4, 13), (5, 10), (6, 8), (7, 5), (5, 11), (6, 9), (7, 6), (5, 12), (6, 10), (7, 7),
        (5, 13), (6, 11), (7, 8), (6, 12), (7, 9), (6, 13), (9, 0), (7, 10), (7, 11), (7, 12),
        (7, 13),
    ),
)


def place():
    me = lax.axis_index("dp")
    core = lax.rem(me, 2)
    x = lax.rem(lax.div(me, 2), 2)
    y = lax.rem(lax.div(me, 4), 2)
    z = lax.div(me, 8)
    return me, core, x, y, z


def send(src, dst, send_sem, recv_sem, partner):
    copy = pltpu.make_async_remote_copy(
        src_ref=src,
        dst_ref=dst,
        send_sem=send_sem,
        recv_sem=recv_sem,
        device_id=(partner,),
        device_id_type=MESH,
    )
    copy.start()
    return copy


def scale_of(row, scales, edges):
    picked = scales[2]
    picked = jnp.where(row < edges[1], scales[1], picked)
    return jnp.where(row < edges[0], scales[0], picked)


def make_units(edges):
    one, two, short = edges[0] // 16, edges[1] // 16, edges[2] // 16
    units = []
    for k in range((two - one) // 32):
        units.append((one + 32 * k, 1, k % 2 == 0, 16, (1, 1)))
    for k in range(one // 32):
        units.append((32 * k, 1, k % 2 == 1, 16, (0, 0)))
    at = one // 32 * 32
    assert one - at == 16 and short - two == 16
    units.append((at, 1, False, two - at, (0, 2)))
    return units


def settle_rows(sums, pixels, gain, shift):
    mean = sums[0] / pixels
    inv = lax.rsqrt(sums[1] / pixels - mean * mean + EPS_NORM)
    slope = gain * inv
    return mean, inv, slope, shift - mean * slope


def gate(values):
    return 0.5 * jnp.tanh(0.5 * values) + 0.5


def eye_mask(rows, columns, offset=0):
    down = lax.broadcasted_iota(jnp.int32, (rows, columns), 0) + offset
    return down == lax.broadcasted_iota(jnp.int32, (rows, columns), 1)


def column_of(row, size):
    spread = jnp.where(eye_mask(size, size), jnp.broadcast_to(row, (size, size)), 0)
    return jnp.sum(spread, axis=1, keepdims=True)


def total_of(values):
    return jnp.sum(jnp.sum(values, axis=0, keepdims=True), axis=1, keepdims=True)


def fold(values):
    return jnp.sum(values.reshape(values.shape[0] // 8, 8, values.shape[1]), axis=0)


def cast_weight(source, target, square_ref, taps, depth, fetches):
    step = 128
    square_ref[...] = jnp.zeros_like(square_ref)
    for tap in range(taps):
        if tap % (taps // len(fetches)) == 0:
            fetches[tap * len(fetches) // taps].wait()
        new_tap = (tap % 3) * 3 + tap // 3

        @pl.loop(0, depth // step)
        def _(k):
            start = pl.multiple_of(k * step, step)
            values = source[pl.ds(tap * depth + start, step), :]
            target[pl.ds(new_tap * depth + start, step), :] = values.astype(jnp.bfloat16)
            square_ref[...] += fold(values * values)


def factored_votes(grad, rows, row_at, rows_old, rows_new, col_old, level, votes, vote_at, between, after):
    width = grad.shape[1]
    keep = 1.0 - STEP ** (-0.8)
    step = 128
    quarters = width // 128

    def first(k, carry):
        col_sum, row_sum = carry
        start = pl.multiple_of(k * step, step)
        lanes = pl.ds(pl.multiple_of(row_at + start, step), step)
        old = rows_old[:, lanes] * keep
        line = jnp.zeros((8, 128), jnp.float32)
        for m in range(step // 8):
            block = grad[pl.ds(start + 8 * m, 8), :]
            square = block * block
            col_sum = col_sum + square
            part = square[:, :128]
            for q in range(1, quarters):
                part = part + square[:, 128 * q : 128 * (q + 1)]
            part = part * ((1.0 - keep) / width)
            diagonal = eye_mask(8, 128, 8 * m)
            part = part + jnp.where(diagonal, jnp.broadcast_to(old, (8, 128)), 0.0)
            row = jnp.sum(part, axis=1, keepdims=True) + (1.0 - keep) * EPS_ROW
            row = jnp.broadcast_to(row, (8, 128))
            level[pl.ds(start + 8 * m, 8), :] = row
            row_sum = row_sum + row
            line = line + jnp.where(diagonal, row, 0.0)
        rows_new[:, lanes] = jnp.sum(line, axis=0, keepdims=True)
        return col_sum, row_sum

    col_sum, row_sum = lax.fori_loop(
        0,
        rows // step,
        first,
        (jnp.zeros((8, width), jnp.float32), jnp.zeros((8, 128), jnp.float32)),
    )
    col_new = keep * col_old + (1.0 - keep) * (
        jnp.sum(col_sum, axis=0, keepdims=True) / rows + EPS_ROW
    )
    scale = lax.rsqrt(col_new)
    root_mean = jnp.sqrt(jnp.sum(row_sum, axis=0, keepdims=True) / rows)

    def second(k, carry):
        start = pl.multiple_of(k * step, step)
        for m in range(step // 8):
            here = pl.ds(start + 8 * m, 8)
            factor = lax.rsqrt(level[here, :]) * root_mean
            level[here, :] = factor
            raw = grad[here, :] * scale
            power = raw * raw
            part = power[:, :128]
            for q in range(1, quarters):
                part = part + power[:, 128 * q : 128 * (q + 1)]
            carry = carry + part * (factor * factor)
        return carry

    between[0]()
    power = lax.fori_loop(0, rows // step, second, jnp.zeros((8, 128), jnp.float32))
    between[1]()
    clip = jnp.maximum(1.0, jnp.sqrt(total_of(power) / (rows * width)))
    scale = scale / clip

    def third(k, _):
        start = pl.multiple_of(k * step, step)
        for m in range(step // 16):
            here = pl.ds(start + 16 * m, 16)
            factor = level[here, :]
            factor = jnp.concatenate([factor] * quarters, axis=1)
            vote = jnp.tanh(grad[here, :] * factor * scale).astype(jnp.bfloat16)
            at = pl.multiple_of((vote_at + start) * 4 + GROUP * m, GROUP)
            for q in range(quarters):
                votes[pl.ds(at + 16 * q, 16), :] = vote[:, 128 * q : 128 * (q + 1)]
        return 0

    part = 512 // step
    for k in range(0, rows // step, part):
        lax.fori_loop(k, min(k + part, rows // step), third, 0)
        after(k // part)
    return col_new


def step_kernel(
    edges,
    units,
    root,
    images,
    one_hbm,
    two_hbm,
    short_hbm,
    head_ref,
    norm_ref,
    valid_ref,
    label_ref,
    row_ref,
    col_ref,
    moment_ref,
    new_ref,
    vote_ref,
    out_ref,
    row_new,
    col_new,
    moment_new,
    loss_ref,
    count_ref,
    xs,
    grad_one,
    grad_two,
    grad_short,
    low_one,
    low_two,
    low_short,
    main_pre,
    side_pre,
    main_two,
    active,
    back_side,
    active_t,
    xs_t,
    head_pad,
    level,
    square,
    post_one,
    plane_one,
    line_one,
    post_two,
    plane_two,
    line_two,
    tail_post,
    tail_plane,
    tail_line,
    core_in,
    wide_in,
    deep_in,
    line_in,
    sum_low,
    landed,
    total,
    own_weight,
    weight,
    vote_flat,
    new_flat,
    fetch_sem,
    small_send,
    small_recv,
    rs_send,
    rs_recv,
    line_send,
    line_recv,
    pass_send,
    land_recv,
    spread_send,
    spread_recv,
    ag_send,
    ag_recv,
    free_sem,
    load_sem,
):
    slots, in_width = xs.shape[4:]
    width = main_pre.shape[1]
    side = 4
    band = side * slots
    pixel_count = side * side
    classes = head_ref.shape[0]
    keep = 1.0 - STEP ** (-0.8)
    low = jnp.bfloat16
    f32 = jnp.float32

    me, core, x, y, z = place()
    flip_core = me + 1 - 2 * core
    flip_x = me + 2 - 4 * x
    flip_y = me + 4 - 8 * y
    spot = lax.rem(me, 8)
    near = [z * 8 + lax.rem(spot + k, 8) for k in range(1, 8)]
    far = [lax.rem(z + k, 4) * 8 + spot for k in range(1, 4)]
    others = [lax.rem(me + k, 32) for k in range(1, 32)]

    count = images.shape[0]
    loads = []
    for half in range(2):
        lanes = slice(128 * half, 128 * (half + 1))
        loads.append(
            pltpu.make_async_copy(
                images.at[:, lanes], core_in.at[pl.ds(half * count, count)], load_sem.at[half]
            )
        )
        loads[half].start()

    def chunks_of(source, target, first, count):
        rows = source.shape[0] // count
        return [
            pltpu.make_async_copy(
                source.at[pl.ds(k * rows, rows)],
                target.at[pl.ds(k * rows, rows)],
                fetch_sem.at[first + k],
            )
            for k in range(count)
        ]

    fetch_one = chunks_of(one_hbm, grad_one, 0, 3)
    fetch_short = chunks_of(short_hbm, grad_short, 3, 1)
    fetch_two = chunks_of(two_hbm, grad_two, 4, 3)
    for fetch in fetch_one + fetch_short:
        fetch.start()
    barrier = pltpu.get_barrier_semaphore()
    for partner in others:
        pl.semaphore_signal(barrier, inc=1, device_id=(partner,), device_id_type=MESH)

    def fetch_rows(row, count, place_at, sem):
        parts = (
            (one_hbm, 0, edges[0]),
            (two_hbm, edges[0], edges[1]),
            (short_hbm, edges[1], edges[2]),
        )
        for ref, first, last in parts:

            @pl.when(jnp.logical_and(row >= first, row < last))
            def _():
                start = pl.multiple_of(row - first, count)
                pltpu.make_async_copy(
                    ref.at[pl.ds(start, count)], weight.at[pl.ds(place_at, count)], sem
                ).start()

    first_row = me * OWN

    for half in range(2):
        lanes = slice(128 * half, 128 * (half + 1))
        loads[half].wait()
        level[:count, :] = core_in[pl.ds(half * count, count), :].astype(f32)
        for h in range(2 * side):
            for w in range(2 * side):
                rows = level[pl.ds(2 * side * h + w, slots, stride=4 * pixel_count), :]
                xs[w % 2, w // 2, h % 2, h // 2, :, lanes] = rows.astype(low)

    scales = {}

    def scale_from(weight_square, size):
        return jnp.maximum(EPS_SCALE, jnp.sqrt(total_of(weight_square) / size))

    exchanges = (
        (post_one, plane_one, line_one),
        (post_two, plane_two, line_two),
        (tail_post, tail_plane, tail_line),
    )

    def exchange_start(which, values):
        mine_ref, plane_ref, _ = exchanges[which]
        mine_ref[...] = values
        plane_ref[spot] = values
        return [
            send(
                mine_ref,
                plane_ref.at[spot],
                small_send.at[which, k],
                small_recv.at[which, k],
                partner,
            )
            for k, partner in enumerate(near)
        ]

    def pack_rows(rows):
        pieces = [row[:, 128 * q : 128 * (q + 1)] for row in rows for q in range(4)]
        pad = -len(pieces) % 8
        if pad:
            pieces.append(jnp.zeros((pad, 128), f32))
        return jnp.concatenate(pieces, axis=0)

    def unpack_row(lines_in, k):
        return jnp.concatenate([lines_in[4 * k + q : 4 * k + q + 1] for q in range(4)], axis=1)

    def exchange_middle(which, copies):
        _, plane_ref, line_ref = exchanges[which]
        for copy in copies:
            copy.wait()
        line_ref[z] = functools.reduce(lambda a, b: a + b, [plane_ref[k] for k in range(8)])
        return [
            send(
                line_ref.at[z],
                line_ref.at[z],
                small_send.at[which, 7 + k],
                small_recv.at[which, 7 + k],
                partner,
            )
            for k, partner in enumerate(far)
        ]

    def exchange_end(which, copies):
        line_ref = exchanges[which][2]
        for copy in copies:
            copy.wait()
        return (line_ref[0] + line_ref[1]) + (line_ref[2] + line_ref[3])

    def lines(start, count):
        return pl.ds(pl.multiple_of(start, 16), count)

    sizes = [GROUP * unit[1] for unit in units]
    starts = [sum(sizes[:k]) for k in range(len(units) + 1)]

    def part_of(ref, u, share, start, count):
        return ref.at[lines(share * starts[u] + start, count)]

    def places(u):
        if units[u][2]:
            return x, y, flip_x, flip_y
        return y, x, flip_y, flip_x

    def unit_start(u, cc):
        return GROUP * units[u][0] + cc * (GROUP * units[u][3])

    def own_group(u):
        first, second, _, _ = places(u)
        return units[u][0] + core * units[u][3] + (first * 8 + second * 4 + z) * units[u][1]

    def halve(source, target, u, stage, partner):
        return send(source, target, rs_send.at[u, stage], rs_recv.at[u, stage], partner)

    def scatter_start(u):
        size = 16 * sizes[u]
        return halve(
            out_ref.at[lines(unit_start(u, 1 - core), size)],
            part_of(core_in, u, 16, 0, size),
            u,
            0,
            flip_core,
        )

    def add_to(ref, u, share, source_ref, source_start):
        size = share * sizes[u]
        here = lines(share * starts[u], size)
        ref[here, :] = ref[here, :] + source_ref[lines(source_start, size), :]

    def scatter_one(u, copy):
        copy.wait()
        add_to(core_in, u, 16, out_ref, unit_start(u, core))
        pl.semaphore_signal(
            free_sem.at[u], inc=1, device_id=(flip_core,), device_id_type=MESH
        )
        first, _, flip_first, _ = places(u)
        size = 8 * sizes[u]
        return halve(
            part_of(core_in, u, 16, (1 - first) * size, size),
            part_of(wide_in, u, 8, 0, size),
            u,
            1,
            flip_first,
        )

    def scatter_two(u, copy):
        copy.wait()
        first, second, _, flip_second = places(u)
        add_to(wide_in, u, 8, core_in, 16 * starts[u] + first * 8 * sizes[u])
        size = 4 * sizes[u]
        return halve(
            part_of(wide_in, u, 8, (1 - second) * size, size),
            part_of(deep_in, u, 4, 0, size),
            u,
            2,
            flip_second,
        )

    def line_copy(u, k):
        plane_to = lax.rem(z + k, 4)
        return pltpu.make_async_remote_copy(
            src_ref=part_of(deep_in, u, 4, plane_to * sizes[u], sizes[u]),
            dst_ref=part_of(line_in, u, 4, z * sizes[u], sizes[u]),
            send_sem=line_send.at[u, k],
            recv_sem=line_recv.at[u, k],
            device_id=(plane_to * 8 + spot,),
            device_id_type=MESH,
        )

    def scatter_three(u, copy):
        copy.wait()
        _, second, _, _ = places(u)
        add_to(deep_in, u, 4, wide_in, 8 * starts[u] + second * 4 * sizes[u])
        for k in (3, 2, 1):
            line_copy(u, k).start()
        here = lines(4 * starts[u] + z * sizes[u], sizes[u])
        line_in[here, :] = deep_in[here, :]

    groups = (edges[2] + TAIL) // 16
    spare = (groups - 1) // 32
    passes = []

    def land(local, group, to, slot, index):
        source = sum_low.at[lines(local * GROUP, GROUP)]
        target = landed.at[lines(slot * GROUP, GROUP)]
        copy = pltpu.make_async_remote_copy(
            src_ref=source,
            dst_ref=target,
            send_sem=pass_send.at[index],
            recv_sem=land_recv.at[slot],
            device_id=(to,),
            device_id_type=MESH,
        )
        return copy, source, target

    def pass_on(u):
        for m in range(units[u][1]):
            local = starts[u] // GROUP + m
            group = own_group(u) + m
            to, slot = lax.div(group, spare), lax.rem(group, spare)
            for halo in range(2):
                index = 2 * local + halo
                if halo:
                    receiver, at = lax.rem(to + 31, 32), spare
                    wanted = jnp.logical_and(slot == 0, group > 0)
                else:
                    receiver, at, wanted = to, slot, group >= 0
                away = jnp.logical_and(wanted, receiver != me)
                here = jnp.logical_and(wanted, receiver == me)
                copy, source, target = land(local, group, receiver, at, index)

                @pl.when(away)
                def _():
                    copy.start()

                @pl.when(here)
                def _():
                    target[...] = source[...]

                passes.append((away, copy))

    def flat_rows(row, q, values, ref):
        ref[pl.ds(row * 4 + q, 8, stride=4), :] = values

    def old_rows(u, cc):
        matrix = units[u][4][cc]
        base = edges[matrix - 1] if matrix else 0
        return (one_hbm, two_hbm, short_hbm)[matrix], 16 * own_group(u) - base, 16 * units[u][1]

    def own_fetch(u):
        target = own_weight.at[pl.ds(starts[u] // 4, 16 * units[u][1])]
        matrices = units[u][4]
        for cc in range(2):
            if cc and matrices[0] == matrices[1]:
                continue

            @pl.when((core == cc) if matrices[0] != matrices[1] else (core >= 0))
            def _():
                ref, row, count = old_rows(u, cc)
                pltpu.make_async_copy(
                    ref.at[pl.ds(pl.multiple_of(row, 16), count)], target, fetch_sem.at[9 + u]
                ).start()

    def spread_copy(u, k):
        own = out_ref.at[lines(own_group(u) * GROUP, sizes[u])]
        return pltpu.make_async_remote_copy(
            src_ref=own,
            dst_ref=own,
            send_sem=spread_send.at[u, k],
            recv_sem=spread_recv.at[u, k],
            device_id=(far[k - 1],),
            device_id_type=MESH,
        )

    def own_block(u):
        size = sizes[u]
        for k in range(1, 4):
            line_copy(u, k).wait_recv()
        here = pl.ds(starts[u], size)
        low_sum = functools.reduce(
            lambda a, b: a + b,
            [line_in[pl.ds(4 * starts[u] + t * size, size), :].astype(f32) for t in range(4)],
        ).astype(low)
        sum_low[here, :] = low_sum
        total[here, :] = low_sum.astype(f32)
        target = own_weight.at[pl.ds(starts[u] // 4, 16 * units[u][1])]
        pltpu.make_async_copy(target, target, fetch_sem.at[9 + u]).wait()
        matrices = units[u][4]
        scale = jnp.where(core == 0, scales[matrices[0]], scales[matrices[1]])
        for m in range(units[u][1]):
            row = starts[u] // 4 + 16 * m
            for part in (0, 8):
                for q in range(4):
                    summed = total[pl.ds(row * 4 + 16 * q + part, 8), :]
                    old = own_weight[pl.ds(row + part, 8), 128 * q : 128 * (q + 1)]
                    fresh = old - scale * jnp.tanh(summed * root)
                    flat_rows(row + part, q, fresh, new_flat)
        out_ref[lines(own_group(u) * GROUP, size), :] = new_flat[here, :].astype(low)
        for k in (3, 2, 1):
            spread_copy(u, k).start()
        pass_on(u)

    def piece(rows, u, stage, partner):
        return send(
            out_ref.at[rows], out_ref.at[rows], ag_send.at[u, stage], ag_recv.at[u, stage], partner
        )

    def gather_one(u):
        for k in range(1, 4):
            spread_copy(u, k).wait_recv()
        first, second, _, flip_second = places(u)
        size = 4 * sizes[u]
        start = unit_start(u, core) + (2 * first + second) * size
        return piece(lines(start, size), u, 0, flip_second)

    def gather_two(u, copy):
        copy.wait()
        first, _, flip_first, _ = places(u)
        size = 8 * sizes[u]
        return piece(lines(unit_start(u, core) + first * size, size), u, 1, flip_first)

    def gather_three(u, copy):
        copy.wait()
        pl.semaphore_wait(free_sem.at[u], 1)
        return piece(lines(unit_start(u, core), 16 * sizes[u]), u, 2, flip_core)

    def renew(row, at_row):
        scale = scale_of(at_row, [scales[k] for k in range(3)], edges)
        for part in (0, 8):
            for q in range(4):
                summed = total[pl.ds(row * 4 + 16 * q + part, 8), :]
                old = weight[pl.ds(row + part, 8), 128 * q : 128 * (q + 1)]
                fresh = old - scale * jnp.tanh(summed * root)
                flat_rows(row + part, q, summed, vote_flat)
                flat_rows(row + part, q, fresh, new_flat)

    valid_column = column_of(valid_ref[...].astype(f32), slots)
    weight_slot = jnp.broadcast_to(valid_column, (slots, width))

    cast_weight(grad_one, low_one, square, 9, in_width, fetch_one)
    scales[0] = scale_from(square[...], grad_one.size)
    cast_weight(grad_short, low_short, square, 1, in_width, fetch_short)
    scales[2] = scale_from(square[...], grad_short.size)
    for fetch in fetch_two:
        fetch.start()
    for k in range(OWN // PIECE):
        fetch_rows(first_row + k * PIECE, PIECE, k * PIECE, fetch_sem.at[7])
    fetch_rows(first_row + OWN, TAIL, OWN, fetch_sem.at[8])
    for u in range(len(units)):
        own_fetch(u)

    def image_taps(b):
        across, last = (0, side) if b == 1 else (1, side - 1 if b == 0 else side)
        even = xs[across, :last, 0].reshape(-1, in_width)
        odd = xs[across, :last, 1].reshape(-1, in_width)
        above = []
        for j in range(last):
            above.append(jnp.zeros((slots, in_width), low))
            above.append(xs[across, j, 1, : side - 1].reshape(band - slots, in_width))
        return jnp.concatenate([jnp.concatenate(above, axis=0), even, odd], axis=1)

    def moments(values):
        count, columns = values.shape
        values = values.reshape(count // slots, slots, columns)
        weighted = values * weight_slot[:, :columns]
        return [
            jnp.sum(jnp.sum(each, axis=0), axis=0, keepdims=True)
            for each in (weighted, weighted * values)
        ]

    def side_by_side(pairs):
        return [jnp.concatenate(each, axis=1) for each in zip(*pairs)]

    half = width // 2
    halves = [slice(0, half), slice(half, width)]
    none = jnp.zeros((1, width), f32)

    def product(left, right):
        return jnp.dot(left, right, preferred_element_type=f32)

    main_sums, side_sums = [], []
    deep = 3 * in_width
    for cols in halves:
        main_pre[:band, cols] = jnp.zeros((band, half), f32)
        main_pre[band:, cols] = product(image_taps(0), low_one[:deep, cols])
        main_pre[:, cols] += product(image_taps(1), low_one[deep : 2 * deep, cols])
        value = main_pre[:, cols] + product(image_taps(2), low_one[2 * deep :, cols])
        main_pre[:, cols] = value
        main_sums.append(moments(value))
        value = product(xs[0, :, 0].reshape(-1, in_width), low_short[:, cols])
        side_pre[:, cols] = value
        side_sums.append(moments(value))
    main_sums, side_sums = side_by_side(main_sums), side_by_side(side_sums)

    count = jnp.broadcast_to(jnp.sum(valid_column, axis=0, keepdims=True), (1, width))
    pl.semaphore_wait(barrier, len(others))
    copies = exchange_start(
        0, pack_rows(list(main_sums) + list(side_sums) + [count])
    )
    cast_weight(grad_two, low_two, square, 9, width, fetch_two)
    scales[1] = scale_from(square[...], grad_two.size)
    copies = exchange_middle(0, copies)
    for across in range(2):
        for down in range(2):
            for j in range(side):
                block = xs[across, j, down].reshape(band, in_width)
                xs_t[across, down, :, j * band : (j + 1) * band] = block.T
    border = jnp.zeros((side, 1, slots, width), low)
    active[:, 0:1] = border
    active[:, side + 1 :] = border
    no_rows = jnp.zeros((slots, width), low)
    for j in range(side):
        for i in (0, side + 1):
            low_one[pl.ds(((side + 2) * j + i) * slots, slots), :] = no_rows
    head_pad[...] = jnp.zeros_like(head_pad)
    head_pad[:classes, :] = head_ref[...]
    head = head_pad[:16, :]
    scales[3] = scale_from(head * head, head_ref.size)
    params = norm_ref[...]
    scales[4] = scale_from(params * params, norm_ref.size)
    sums = exchange_end(0, copies)
    sums = [unpack_row(sums, k) for k in range(5)]

    valid_count = sums[4]
    count_ref[...] = valid_count[:, :1]
    denominator = jnp.maximum(valid_count, 1.0)
    pixels = denominator * pixel_count
    gains = [norm_ref[k : k + 1, :] for k in range(6)]
    mean_one, inv_one, slope_one, base_one = settle_rows(
        (sums[0], sums[1]), pixels, gains[0], gains[1]
    )
    mean_side, inv_side, slope_side, base_side = settle_rows(
        (sums[2], sums[3]), pixels, gains[4], gains[5]
    )

    for j in range(side):
        hidden = main_pre[pl.ds(j * band, band), :] * slope_one + base_one
        active[j, 1 : side + 1] = (
            (hidden * gate(hidden)).astype(low).reshape(side, slots, width)
        )

    def active_taps(first, last):
        pieces = [active[first:last, a : a + side].reshape(-1, width) for a in range(3)]
        return jnp.concatenate(pieces, axis=1)

    two_sums = []
    deep = 3 * width
    for cols in halves:
        main_two[:band, cols] = jnp.zeros((band, half), f32)
        main_two[band:, cols] = product(active_taps(0, side - 1), low_two[:deep, cols])
        main_two[: 3 * band, cols] += product(active_taps(1, side), low_two[2 * deep :, cols])
        value = main_two[:, cols] + product(active_taps(0, side), low_two[deep : 2 * deep, cols])
        main_two[:, cols] = value
        two_sums.append(moments(value))
    two_sums = side_by_side(two_sums)
    copies = exchange_start(1, pack_rows(two_sums))
    for j in range(side):
        block = active[j, 1 : side + 1].reshape(band, width)
        active_t[:, j * band : (j + 1) * band] = block.T
    copies = exchange_middle(1, copies)
    sums = exchange_end(1, copies)
    sums = [unpack_row(sums, k) for k in range(2)]
    mean_two, inv_two, slope_two, base_two = settle_rows(
        (sums[0], sums[1]), pixels, gains[2], gains[3]
    )

    base_joined = base_two + base_side

    quarters = [slice(128 * q, 128 * (q + 1)) for q in range(width // 128)]

    def joined_of(here, lanes):
        return (
            main_two[here, lanes] * slope_two[:, lanes]
            + side_pre[here, lanes] * slope_side[:, lanes]
            + base_joined[:, lanes]
        )

    pooled = []
    for lanes in quarters:
        total_joined = jnp.zeros((slots, 128), f32)
        for p in range(pixel_count):
            joined = joined_of(pl.ds(p * slots, slots), lanes)
            total_joined = total_joined + joined * gate(joined)
        pooled.append(total_joined)
    pooled = jnp.concatenate(pooled, axis=1)
    pooled = (pooled / pixel_count).astype(low)
    head_low = head_pad[...].astype(low)
    logits = lax.dot_general(
        pooled, head_low, (((1,), (1,)), ((), ())), preferred_element_type=f32
    )
    lane = lax.broadcasted_iota(jnp.int32, logits.shape, 1)
    real = lane < classes
    largest = jnp.max(jnp.where(real, logits, -jnp.inf), axis=1, keepdims=True)
    powers = jnp.where(real, jnp.exp(jnp.where(real, logits - largest, 0.0)), 0.0)
    total_power = jnp.sum(powers, axis=1, keepdims=True)
    label_column = column_of(label_ref[...].astype(f32), slots).astype(jnp.int32)
    onehot = jnp.where(lane == label_column, 1.0, 0.0)
    entropy = largest + jnp.log(total_power) - jnp.sum(onehot * logits, axis=1, keepdims=True)
    loss = jnp.sum(entropy * valid_column, axis=0, keepdims=True)
    grad_logits = (
        (powers / total_power - onehot) * (valid_column / denominator[:, :1])
    ).astype(low)
    grad_head = lax.dot_general(
        grad_logits, pooled, (((0,), (0,)), ((), ())), preferred_element_type=f32
    )[:16]
    grad_pooled = jnp.dot(grad_logits, head_low, preferred_element_type=f32) / pixel_count

    def back_rows(j, i, count):
        return low_one[pl.ds(((side + 2) * j + i) * slots, count * slots), :]

    join_sums = []
    for lanes in quarters:
        three = [jnp.zeros((8, 128), f32)] * 3
        for p in range(pixel_count):
            here = pl.ds(p * slots, slots)
            joined = joined_of(here, lanes)
            opened = gate(joined)
            grad = grad_pooled[:, lanes] * (opened * (1.0 + joined * (1.0 - opened)))
            normed_two = (main_two[here, lanes] - mean_two[:, lanes]) * inv_two[:, lanes]
            normed_side = (side_pre[here, lanes] - mean_side[:, lanes]) * inv_side[:, lanes]
            three = [
                old + fold(new) for old, new in zip(three, (grad * normed_two, grad * normed_side, grad))
            ]
            at = ((side + 2) * (p // side) + 1 + p % side) * slots
            low_one[pl.ds(at, slots), lanes] = (grad * slope_two[:, lanes]).astype(low)
            back_side[here, lanes] = (grad * slope_side[:, lanes]).astype(low)
        join_sums.append([jnp.sum(each, axis=0, keepdims=True) for each in three])
    gain_two, gain_side, shift_two = side_by_side(join_sums)

    for b in range(3):
        first, last = max(0, b - 1), min(side, side + b - 1)
        left = active_t[:, first * band : last * band]
        for a in range(3):
            right = [back_rows(j, 2 - a, side) for j in range(first - b + 1, last - b + 1)]
            grad_two[pl.ds((a * 3 + b) * width, width), :] = product(
                left, jnp.concatenate(right, axis=0)
            )

    def nothing():
        pass

    def matrix_votes(k, grad, between, after):
        here = pl.ds(k * width, width)
        start = edges[k - 1] if k else 0
        col_new[:, here] = factored_votes(
            grad,
            grad.shape[0],
            start,
            row_ref,
            row_new,
            col_ref[:, here],
            level,
            out_ref,
            start,
            between,
            after,
        )

    kept = {}

    def tail_step():
        sums = exchange_end(2, kept["tail"])
        loss_ref[...] = sums[4 * TAIL : 4 * TAIL + 1, :1]
        old = jnp.concatenate([head_ref[...], norm_ref[...]], axis=0)
        is_head = lax.broadcasted_iota(jnp.int32, (TAIL, width), 0) < classes
        scale = jnp.where(is_head, scales[3], scales[4])
        sums = jnp.concatenate([sums[TAIL * q : TAIL * (q + 1)] for q in range(4)], axis=1)
        fresh = old - scale * jnp.tanh(sums * root)
        both = jnp.concatenate([sums, fresh], axis=0)
        high = both.astype(low)
        rest = both - high.astype(f32)
        middle = rest.astype(low)
        parts = jnp.concatenate([high, middle, (rest - middle.astype(f32)).astype(low)], axis=0)

        flat_sums, flat_new = [], []
        window = 256
        for q in range(classes):
            start = min(q * width // classes // 128 * 128, width - window)
            down = lax.broadcasted_iota(jnp.int32, (window, width), 0)
            across = lax.broadcasted_iota(jnp.int32, (window, width), 1)
            gap = across - classes * down + (q * width - classes * start)
            chosen = jnp.where(jnp.logical_and(gap >= 0, gap < classes), 1.0, 0.0).astype(low)
            moved = jnp.dot(parts[:, start : start + window], chosen, preferred_element_type=f32)
            moved = moved[: 2 * TAIL] + moved[2 * TAIL : 4 * TAIL] + moved[4 * TAIL :]
            spot_of = lax.broadcasted_iota(jnp.int32, (TAIL, width), 1).astype(f32) + q * width
            class_of = spot_of - classes * jnp.floor((spot_of + 0.5) / classes)
            here = lax.broadcasted_iota(jnp.int32, (TAIL, width), 0).astype(f32) == class_of
            flat_sums.append(jnp.sum(jnp.where(here, moved[:TAIL], 0.0), axis=0, keepdims=True))
            flat_new.append(jnp.sum(jnp.where(here, moved[TAIL:], 0.0), axis=0, keepdims=True))
        kept["sums"] = jnp.concatenate(flat_sums + [sums[classes:]], axis=0)
        kept["new"] = jnp.concatenate(flat_new + [fresh[classes:]], axis=0)

    def return_step():
        mine = [own_group(u) for u in range(len(units))]
        for slot in range(spare + 1):
            group = me * spare + slot
            own = group < 0
            for u, unit in enumerate(units):
                inside = jnp.logical_and(group >= mine[u], group < mine[u] + unit[1])
                own = jnp.logical_or(own, inside)

            @pl.when(jnp.logical_and(jnp.logical_not(own), group < groups - 1))
            def _():
                land(0, group, me, slot, 0)[0].wait_recv()

        pltpu.make_async_copy(
            weight.at[pl.ds(0, OWN)], weight.at[pl.ds(0, OWN)], fetch_sem.at[7]
        ).wait()
        total[pl.ds(0, SPAN), :] = landed[pl.ds(0, SPAN), :].astype(f32)

        @pl.loop(0, OWN // 16)
        def _(k):
            row = pl.multiple_of(k * 16, 16)
            renew(row, first_row + row)

        @pl.when(me < 31)
        def _():
            pltpu.make_async_copy(
                weight.at[pl.ds(OWN, TAIL)], weight.at[pl.ds(OWN, TAIL)], fetch_sem.at[8]
            ).wait()
            total[pl.ds(SPAN, GROUP), :] = landed[pl.ds(SPAN, GROUP), :].astype(f32)
            renew(OWN, first_row + OWN)

        def tail_rows(values, ref):
            for u in (0, 8):
                for q in range(4):
                    flat_rows(OWN + u, q, values[u : u + 8, 128 * q : 128 * (q + 1)], ref)

        @pl.when(me == 31)
        def _():
            tail_rows(kept["sums"], vote_flat)
            tail_rows(kept["new"], new_flat)

        shift = 2 * me
        share = vote_ref.shape[0]
        vote_ref[...] = vote_flat[pl.ds(shift, share), :]
        new_ref[...] = new_flat[pl.ds(shift, share), :]
        tail_rows(kept["new"], new_flat)
        out_ref[pl.ds(32 * SPAN, GROUP), :] = new_flat[pl.ds(SPAN, GROUP), :].astype(low)

    in_flight = {}
    steps = (
        lambda u, copy: scatter_start(u),
        scatter_one,
        scatter_two,
        scatter_three,
        lambda u, copy: own_block(u),
        lambda u, copy: gather_one(u),
        gather_two,
        gather_three,
        lambda u, copy: tail_step(),
        lambda u, copy: return_step(),
    )

    def go(number, u):
        got = steps[number](u, in_flight.get(u))
        if number < 8:
            in_flight[u] = got

    def turn(number):
        for step_number, u in SCHEDULE[number]:
            go(step_number, u)

    early = edges[1] // 512 - edges[0] // 512
    matrix_votes(1, grad_two, (nothing, nothing), lambda k: go(0, k) if k < 2 else None)
    turn(0)
    grad_short[...] = jnp.dot(xs_t[0, 0], back_side[...], preferred_element_type=f32)
    matrix_votes(2, grad_short, (nothing, nothing), lambda k: None)

    def back_taps(first, last):
        pieces = [
            jnp.concatenate([back_rows(j, 2 - a, side) for j in range(first, last)], axis=0)
            for a in range(3)
        ]
        return jnp.concatenate(pieces, axis=1)

    def back_weights(b, cols):
        pieces = [
            low_two[pl.ds((3 * b + a) * width + cols.start, half), :] for a in range(3)
        ]
        return jnp.concatenate(pieces, axis=1)

    def product_turned(left, right):
        return lax.dot_general(left, right, (((1,), (1,)), ((), ())), preferred_element_type=f32)

    for k, cols in enumerate(halves):
        main_two[: 3 * band, cols] = product_turned(back_taps(1, side), back_weights(0, cols))
        main_two[3 * band :, cols] = jnp.zeros((band, half), f32)
        main_two[band:, cols] += product_turned(back_taps(0, side - 1), back_weights(2, cols))
        main_two[:, cols] += product_turned(back_taps(0, side), back_weights(1, cols))
        turn(1 + k)

    active[:, side : side + 1] = border
    first_sums = [[], []]
    for j in range(side):
        for lanes in quarters:
            here = pl.ds(j * band, band)
            before = main_pre[here, lanes]
            hidden = before * slope_one[:, lanes] + base_one[:, lanes]
            opened = gate(hidden)
            grad = main_two[here, lanes] * (opened * (1.0 + hidden * (1.0 - opened)))
            normed = (before - mean_one[:, lanes]) * inv_one[:, lanes]
            first_sums[0].append(fold(grad * normed))
            first_sums[1].append(fold(grad))
            active[j, :side, :, lanes] = (
                (grad * slope_one[:, lanes]).astype(low).reshape(side, slots, 128)
            )
        if j % 2:
            turn(3 + j // 2)
    gain_one, shift_one = [
        jnp.concatenate(
            [
                jnp.sum(functools.reduce(lambda a, b: a + b, sums[q::4]), axis=0, keepdims=True)
                for q in range(4)
            ],
            axis=1,
        )
        for sums in first_sums
    ]

    square_head = grad_head * grad_head + EPS_ROW
    real = lax.broadcasted_iota(jnp.int32, square_head.shape, 0) < classes
    square_head = jnp.where(real, square_head, 0.0)
    head_lanes = pl.ds(edges[2], width)
    old = row_ref[:, head_lanes]
    row = keep * old + (1.0 - keep) * jnp.sum(square_head, axis=0, keepdims=True) / classes
    row_new[:, head_lanes] = row
    diagonal = eye_mask(16, classes)
    old = jnp.broadcast_to(col_ref[:, 3 * width :], (16, classes))
    old = jnp.sum(jnp.where(diagonal, old, 0.0), axis=1, keepdims=True)
    column = keep * old + (1.0 - keep) * jnp.sum(square_head, axis=1, keepdims=True) / width
    col_new[:, 3 * width :] = jnp.sum(
        jnp.where(diagonal, jnp.broadcast_to(column, (16, classes)), 0.0), axis=0, keepdims=True
    )
    real_column = lax.broadcasted_iota(jnp.int32, column.shape, 0) < classes
    column = jnp.where(real_column, column, 1.0)
    mean = jnp.sum(row, axis=1, keepdims=True) / width
    raw = grad_head * (lax.rsqrt(row) * jnp.sqrt(mean)) * lax.rsqrt(column)
    clip = jnp.maximum(1.0, jnp.sqrt(total_of(raw * raw) / (classes * width)))
    head_votes = jnp.tanh(raw / clip)[:classes]

    raws = []
    for k, grad in enumerate((gain_one, shift_one, gain_two, shift_two, gain_side, shift_two)):
        here = pl.ds(k * width, width)
        moment = keep * moment_ref[:, here] + (1.0 - keep) * (grad * grad + EPS_ROW)
        moment_new[:, here] = moment
        raws.append(grad * lax.rsqrt(moment))
    raw = jnp.concatenate(raws, axis=0)
    clip = jnp.maximum(1.0, jnp.sqrt(total_of(raw * raw) / raw.size))
    norm_votes = jnp.tanh(raw / clip)
    tail_votes = jnp.concatenate([head_votes, norm_votes], axis=0)
    kept["tail"] = exchange_start(
        2,
        jnp.concatenate(
            [tail_votes[:, 128 * q : 128 * (q + 1)] for q in range(4)]
            + [jnp.broadcast_to(loss, (8, 128))],
            axis=0,
        ),
    )


    for b in range(3):
        first, last = (0, side - 1) if b == 0 else (0, side)
        shift = 1 if b == 0 else 0
        for a in range(3):
            left = xs_t[0 if b == 1 else 1, 0 if a == 1 else 1, :, first * band : last * band]
            start = 1 if a == 0 else 0
            right = active[first + shift : last + shift, start : start + side]
            grad_one[pl.ds((a * 3 + b) * in_width, in_width), :] = jnp.dot(
                left, right.reshape(-1, width), preferred_element_type=f32
            )
        if b == 1:
            kept["tail"] = exchange_middle(2, kept["tail"])
        turn(5 + b)

    matrix_votes(
        0,
        grad_one,
        (lambda: turn(8), lambda: turn(9)),
        lambda k: go(0, early + k) if k < 2 else None,
    )
    turn(10)
    for u in range(len(units)):
        in_flight[u].wait()
        for k in range(1, 4):
            line_copy(u, k).wait_send()
            spread_copy(u, k).wait_send()
    for away, copy in passes:

        @pl.when(away)
        def _():
            copy.wait_send()


def finish_kernel(count, chunks, *refs):
    sources, targets, sem = refs[:count], refs[count : 2 * count], refs[2 * count]
    rows = sources[0].shape[0]
    step = -(-rows // chunks // 16) * 16
    copies = []
    for k in range(chunks):
        here = pl.ds(k * step, min(step, rows - k * step))
        copies.append(
            pltpu.make_async_copy(sources[0].at[here], targets[0].at[here], sem.at[k])
        )
    for k in range(1, count):
        copies.append(pltpu.make_async_copy(sources[k], targets[k], sem.at[chunks + k]))
    for copy in copies:
        copy.start()
    for copy in copies:
        copy.wait()


def finish(values):
    count, chunks = len(values), 4
    held = [pltpu.with_memory_space_constraint(value, pltpu.VMEM) for value in values]
    return pl.pallas_call(
        functools.partial(finish_kernel, count, chunks),
        out_shape=[jax.ShapeDtypeStruct(value.shape, value.dtype) for value in values],
        in_specs=[pl.BlockSpec(memory_space=pltpu.VMEM)] * count,
        out_specs=[pl.BlockSpec(memory_space=pl.ANY)] * count,
        scratch_shapes=[pltpu.SemaphoreType.DMA((chunks + count,))],
        compiler_params=pltpu.CompilerParams(vmem_limit_bytes=1024 * 1024),
        name="finish",
    )(*held)


def run_step(images, conv_one, conv_two, shortcut, head, norm_params, valid, labels, rows, cols, moment):
    vmem = pl.BlockSpec(memory_space=pltpu.VMEM)
    hbm = pl.BlockSpec(memory_space=pl.ANY)
    low, f32 = jnp.bfloat16, jnp.float32
    dma = pltpu.SemaphoreType.DMA
    workers = lax.axis_size("dp")
    slots, in_width = valid.shape[1], images.shape[1]
    width = conv_one.shape[1]
    pixels = images.shape[0] // 4
    shape = pltpu.VMEM
    edges = [conv_one.shape[0]]
    edges.append(edges[0] + conv_two.shape[0])
    edges.append(edges[1] + shortcut.shape[0])
    units = make_units(edges)
    flat = (edges[2] + TAIL) * width // 128
    share = flat // workers
    return pl.pallas_call(
        functools.partial(step_kernel, tuple(edges), tuple(units), 1.0 / math.sqrt(workers)),
        out_shape=(
            shape((share, 128), f32),
            shape((share, 128), f32),
            shape((flat, 128), low),
            shape(rows.shape, f32),
            shape(cols.shape, f32),
            shape(moment.shape, f32),
            shape((1, 1), f32),
            shape((1, 1), f32),
        ),
        in_specs=[hbm] * 4 + [vmem] * 7,
        out_specs=(vmem,) * 8,
        scratch_shapes=[
            pltpu.VMEM((2, 4, 2, 4, slots, in_width), low),
            pltpu.VMEM(conv_one.shape, f32),
            pltpu.VMEM(conv_two.shape, f32),
            pltpu.VMEM(shortcut.shape, f32),
            pltpu.VMEM(conv_one.shape, low),
            pltpu.VMEM(conv_two.shape, low),
            pltpu.VMEM(shortcut.shape, low),
            pltpu.VMEM((pixels, width), f32),
            pltpu.VMEM((pixels, width), f32),
            pltpu.VMEM((pixels, width), f32),
            pltpu.VMEM((4, 6, slots, width), low),
            pltpu.VMEM((pixels, width), low),
            pltpu.VMEM((width, pixels), low),
            pltpu.VMEM((2, 2, in_width, pixels), low),
            pltpu.VMEM((128, width), f32),
            pltpu.VMEM((conv_two.shape[0], 128), f32),
            pltpu.VMEM((8, width), f32),
            pltpu.VMEM((24, 128), f32),
            pltpu.VMEM((8, 24, 128), f32),
            pltpu.VMEM((4, 24, 128), f32),
            pltpu.VMEM((8, 128), f32),
            pltpu.VMEM((8, 8, 128), f32),
            pltpu.VMEM((4, 8, 128), f32),
            pltpu.VMEM((GROUP + 8, 128), f32),
            pltpu.VMEM((8, GROUP + 8, 128), f32),
            pltpu.VMEM((4, GROUP + 8, 128), f32),
            pltpu.VMEM((16 * SPAN, 128), low),
            pltpu.VMEM((8 * SPAN, 128), low),
            pltpu.VMEM((4 * SPAN, 128), low),
            pltpu.VMEM((4 * SPAN, 128), low),
            pltpu.VMEM((SPAN, 128), low),
            pltpu.VMEM((SPAN + GROUP, 128), low),
            pltpu.VMEM((SPAN + GROUP, 128), f32),
            pltpu.VMEM((OWN, width), f32),
            pltpu.VMEM((OWN + TAIL, width), f32),
            pltpu.VMEM((SPAN + GROUP, 128), f32),
            pltpu.VMEM((SPAN + GROUP, 128), f32),
            dma((9 + len(units),)),
            dma((3, 10)),
            dma((3, 10)),
            dma((len(units), 3)),
            dma((len(units), 3)),
            dma((len(units), 4)),
            dma((len(units), 4)),
            dma((2 * OWN // 16,)),
            dma((OWN // 16 + 1,)),
            dma((len(units), 4)),
            dma((len(units), 4)),
            dma((len(units), 3)),
            dma((len(units), 3)),
            pltpu.SemaphoreType.REGULAR((len(units),)),
            dma((2,)),
        ],
        compiler_params=pltpu.CompilerParams(
            collective_id=1, has_side_effects=True, vmem_limit_bytes=54 * 1024 * 1024
        ),
        name="step",
    )(images, conv_one, conv_two, shortcut, head, norm_params, valid, labels, rows, cols, moment)


def scale_for(weight):
    return jnp.maximum(EPS_SCALE, jnp.sqrt(jnp.mean(weight * weight)))


def local_general(
    images,
    valid_slot,
    labels,
    conv_one,
    conv_two,
    shortcut,
    classifier,
    norm_params,
    row_state,
    col_state,
    bn_moment,
):
    in_width = images.shape[3]
    width = conv_one.shape[1]
    kernel_one = conv_one.astype(jnp.bfloat16).reshape(3, 3, in_width, width)
    kernel_two = conv_two.astype(jnp.bfloat16).reshape(3, 3, width, width)
    kernel_short = shortcut.astype(jnp.bfloat16).reshape(1, 1, in_width, width)
    head_low = classifier.astype(jnp.bfloat16)
    slot_count = images.shape[0]
    out_side = images.shape[1] // 2
    pixel_count = out_side * out_side
    slot_weight = valid_slot.astype(jnp.float32)
    pixel_weight = jnp.broadcast_to(slot_weight[:, None], (slot_count, pixel_count)).reshape(-1, 1)
    main_pre, side_pre = first_section(images, kernel_one, kernel_short)
    main_sums = masked_moments(pixel_weight, main_pre)
    side_sums = masked_moments(pixel_weight, side_pre)
    count_row = jnp.broadcast_to(jnp.sum(slot_weight), (width,))
    first_sums = lax.psum(jnp.stack([*main_sums, *side_sums, count_row]), "dp")
    valid_count = first_sums[4, 0]
    denominator = jnp.maximum(valid_count, 1.0)
    pixels = denominator * pixel_count
    norm_one = settle(first_sums[0], first_sums[1], pixels)
    norm_side = settle(first_sums[2], first_sums[3], pixels)
    hidden_one, active, main_two = second_section(
        main_pre, norm_one, norm_params, kernel_two, slot_count, out_side
    )
    two_sums = masked_moments(pixel_weight, main_two)
    second_sums = lax.psum(jnp.stack([*two_sums]), "dp")
    norm_two = settle(second_sums[0], second_sums[1], pixels)
    joined_pre = (
        (main_two - norm_two[0]) * norm_two[1] * norm_params[2]
        + norm_params[3]
        + (side_pre - norm_side[0]) * norm_side[1] * norm_params[4]
        + norm_params[5]
    )
    joined = jax.nn.silu(joined_pre).reshape(slot_count, pixel_count, -1)
    pooled = jnp.mean(joined, axis=1).astype(jnp.bfloat16)
    logits = jnp.dot(pooled, head_low, preferred_element_type=jnp.float32)
    largest = jnp.max(logits, axis=1, keepdims=True)
    exp_terms = jnp.exp(logits - largest)
    total_exp = jnp.sum(exp_terms, axis=1, keepdims=True)
    log_total = largest[:, 0] + jnp.log(total_exp[:, 0])
    onehot = (labels[:, None] == jnp.arange(logits.shape[1], dtype=jnp.int32)[None, :]).astype(
        jnp.float32
    )
    local_sum = jnp.sum(slot_weight * (log_total - jnp.sum(onehot * logits, axis=1)))
    grad_logits = ((exp_terms / total_exp - onehot) * (slot_weight / denominator)[:, None]).astype(
        jnp.bfloat16
    )
    grad_head = lax.dot_general(
        pooled, grad_logits, (((0,), (0,)), ((), ())), preferred_element_type=jnp.float32
    )
    grad_pooled = lax.dot_general(
        grad_logits, head_low, (((1,), (1,)), ((), ())), preferred_element_type=jnp.float32
    )
    spread_pooled = jnp.broadcast_to(
        (grad_pooled / pixel_count)[:, None, :], (slot_count, pixel_count, width)
    )
    grad_joined = spread_pooled.reshape(slot_count * pixel_count, width) * silu_slope(joined_pre)
    gain_two, shift_two, grad_two = norm_backward(grad_joined, main_two, norm_two, norm_params[2])
    gain_side, shift_side, grad_side = norm_backward(
        grad_joined, side_pre, norm_side, norm_params[4]
    )
    grad_two_maps = grad_two.reshape(slot_count, out_side, out_side, width)
    grad_side_maps = grad_side.reshape(slot_count, out_side, out_side, width)
    grad_conv_two = conv_weight_grad(active, grad_two_maps, 1, 1, 1)
    grad_short = conv_weight_grad(images, grad_side_maps, 2, 0, -1)
    kernel_turned = jnp.transpose(kernel_two[::-1, ::-1], (0, 1, 3, 2))
    grad_active = conv_apply(grad_two_maps, kernel_turned, 1, 1).reshape(
        slot_count * pixel_count, width
    )
    grad_hidden = grad_active * silu_slope(hidden_one)
    gain_one, shift_one, grad_one = norm_backward(grad_hidden, main_pre, norm_one, norm_params[0])
    grad_conv_one = conv_weight_grad(
        images, grad_one.reshape(slot_count, out_side, out_side, width), 2, 1, 0
    )
    grad_norms = jnp.stack([gain_one, shift_one, gain_two, shift_two, gain_side, shift_side])
    grads = (grad_conv_one, grad_conv_two, grad_short, grad_head, grad_norms)
    votes, rows_new, cols_new, moment_new = make_votes(
        grads, row_state[0], col_state[0], bn_moment[0]
    )
    workers = lax.axis_size("dp")
    weights = (conv_one, conv_two, shortcut, classifier, norm_params)
    scales = [scale_for(weight) for weight in weights]
    loss_sum = lax.psum(local_sum, "dp")
    flat_vote = jnp.concatenate([vote.reshape(-1) for vote in votes])
    flat_old = jnp.concatenate([weight.reshape(-1) for weight in weights])
    flat_scale = jnp.concatenate(
        [
            jnp.broadcast_to(scale, (weight.size,))
            for scale, weight in zip(scales, weights)
        ]
    )
    vote_mine = lax.psum_scatter(flat_vote, "dp", tiled=True)
    share = vote_mine.shape[0]
    start = lax.axis_index("dp") * share
    new_mine = lax.dynamic_slice_in_dim(
        flat_old, start, share
    ) - lax.dynamic_slice_in_dim(flat_scale, start, share) * jnp.tanh(
        vote_mine / math.sqrt(workers)
    )
    copies = lax.all_gather(new_mine.astype(jnp.bfloat16), "dp", tiled=True)
    return (
        loss_sum,
        valid_count,
        new_mine,
        copies,
        vote_mine,
        rows_new[None, :],
        cols_new[None, :],
        moment_new[None, :],
    )


def local(
    images,
    valid_slot,
    labels,
    conv_one,
    conv_two,
    shortcut,
    classifier,
    norm_params,
    row_state,
    col_state,
    bn_moment,
):
    new_mine, vote_mine, copies, rows_new, cols_new, moment_new, loss_sum, valid_count = run_step(
        images.reshape(-1, images.shape[-1]),
        conv_one,
        conv_two,
        shortcut,
        classifier.T,
        norm_params,
        valid_slot.reshape(1, -1),
        labels.reshape(1, -1),
        row_state,
        col_state,
        bn_moment,
    )
    copies, new_mine, vote_mine, rows_new, cols_new, moment_new, loss_sum, valid_count = finish(
        (copies, new_mine, vote_mine, rows_new, cols_new, moment_new, loss_sum, valid_count)
    )
    return (
        loss_sum.reshape(()),
        valid_count.reshape(()),
        new_mine.reshape(-1),
        copies.reshape(-1),
        vote_mine.reshape(-1),
        rows_new,
        cols_new,
        moment_new,
    )


def solution(mesh):
    placed = (
        P("dp", None, None, None),
        P("dp"),
        P("dp"),
        P(),
        P(),
        P(),
        P(),
        P(),
        P("dp", None),
        P("dp", None),
        P("dp", None),
    )
    return jax.shard_map(
        local if mesh.shape["dp"] == 32 else local_general,
        mesh=mesh,
        in_specs=placed,
        out_specs=(P(), P(), P("dp"), P(), P("dp"), P("dp", None), P("dp", None), P("dp", None)),
        check_vma=False,
    )
```

```python
import functools
import math

import jax
import jax.numpy as jnp
from jax import lax
from jax.experimental import pallas as pl
from jax.experimental.pallas import tpu as pltpu
from jax.sharding import PartitionSpec as P

STEP = 10
MESH = pl.DeviceIdType.MESH

EPS_NORM = 1e-05
EPS_ROW = 1e-30
EPS_SCALE = 0.001
FORWARD_DIMS = ("NHWC", "HWIO", "NHWC")
WEIGHT_DIMS = ("CHWN", "IHWO", "HWNC")
OWN = 224
TAIL = 16
PIECE = 32
SPAN = 4 * OWN
HALF = SPAN // 2
GROUP = 64


def conv_apply(maps, kernel, stride, margin):
    return lax.conv_general_dilated(
        maps,
        kernel,
        (stride, stride),
        ((margin, margin), (margin, margin)),
        dimension_numbers=FORWARD_DIMS,
        preferred_element_type=jnp.float32,
    )


def conv_weight_grad(maps, grad_out, stride, low_pad, high_pad):
    result = lax.conv_general_dilated(
        maps,
        grad_out,
        (1, 1),
        ((low_pad, high_pad), (low_pad, high_pad)),
        rhs_dilation=(stride, stride),
        dimension_numbers=WEIGHT_DIMS,
        preferred_element_type=jnp.float32,
    )
    return result.reshape(-1, result.shape[3])


def silu_slope(values):
    sigmoid_part = jax.nn.sigmoid(values)
    return sigmoid_part * (1.0 + values * (1.0 - sigmoid_part))


def settle(sum_plain, sum_square, pixels):
    mean_value = sum_plain / pixels
    return (mean_value, lax.rsqrt(sum_square / pixels - mean_value * mean_value + EPS_NORM))


def first_section(images, kernel_one, kernel_short):
    row_count = images.shape[0] * (images.shape[1] // 2) ** 2
    main_pre = conv_apply(images, kernel_one, 2, 1).reshape(row_count, -1)
    side_pre = conv_apply(images, kernel_short, 2, 0).reshape(row_count, -1)
    return (main_pre, side_pre)


def second_section(main_pre, norm_one, norm_params, kernel_two, slot_count, out_side):
    hidden_one = (main_pre - norm_one[0]) * norm_one[1] * norm_params[0] + norm_params[1]
    active = (
        jax.nn.silu(hidden_one).astype(jnp.bfloat16).reshape(slot_count, out_side, out_side, -1)
    )
    main_two = conv_apply(active, kernel_two, 1, 1).reshape(slot_count * out_side * out_side, -1)
    return (hidden_one, active, main_two)


def masked_moments(pixel_weight, values):
    return (jnp.sum(pixel_weight * values, axis=0), jnp.sum(pixel_weight * values * values, axis=0))


def soft_sign(step_raw):
    clip_by = jnp.maximum(1.0, jnp.sqrt(jnp.mean(step_raw * step_raw)))
    return jnp.tanh(step_raw / clip_by)


def make_votes(grads, rows_old, cols_old, moment_old):
    decay_rate = 1.0 - STEP ** (-0.8)
    votes, rows_new, cols_new = ([], [], [])
    row_at, col_at = (0, 0)
    for matrix in grads[:4]:
        row_size, col_size = matrix.shape
        square = matrix * matrix + EPS_ROW
        row_part = decay_rate * rows_old[row_at : row_at + row_size] + (
            1.0 - decay_rate
        ) * jnp.mean(square, axis=1)
        col_part = decay_rate * cols_old[col_at : col_at + col_size] + (
            1.0 - decay_rate
        ) * jnp.mean(square, axis=0)
        second = row_part[:, None] * col_part[None, :] / jnp.mean(row_part)
        votes.append(soft_sign(matrix * lax.rsqrt(second)))
        rows_new.append(row_part)
        cols_new.append(col_part)
        row_at += row_size
        col_at += col_size
    flat_norm = grads[4].reshape(-1)
    moment_new = decay_rate * moment_old + (1.0 - decay_rate) * (flat_norm * flat_norm + EPS_ROW)
    votes.append(soft_sign(flat_norm * lax.rsqrt(moment_new)))
    return (votes, jnp.concatenate(rows_new), jnp.concatenate(cols_new), moment_new)


def norm_backward(grad_out, pre_value, norm_pair, gain_row):
    normed = (pre_value - norm_pair[0]) * norm_pair[1]
    grad_gain = jnp.sum(grad_out * normed, axis=0)
    grad_shift = jnp.sum(grad_out, axis=0)
    grad_pre = (grad_out * gain_row * norm_pair[1]).astype(jnp.bfloat16)
    return (grad_gain, grad_shift, grad_pre)


SCHEDULE = (
    (),
    (
        (1, 0),
    ),
    (
        (0, 2), (1, 1),
    ),
    (
        (0, 3), (1, 2), (2, 0), (0, 4), (1, 3), (2, 1),
    ),
    (
        (0, 5), (1, 4), (2, 2), (3, 0),
    ),
    (
        (0, 6), (1, 5), (2, 3), (3, 1),
    ),
    (
        (0, 7), (1, 6), (2, 4), (3, 2), (4, 0),
    ),
    (),
    (
        (0, 8), (1, 7), (2, 5), (3, 3), (4, 1),
    ),
    (),
    (
        (1, 8), (2, 6), (3, 4), (4, 2), (1, 9), (2, 7), (3, 5), (4, 3), (5, 0), (0, 11), (1, 10),
        (2, 8), (3, 6), (4, 4), (5, 1), (0, 12), (1, 11), (2, 9), (3, 7), (4, 5), (5, 2), (6, 0),
        (0, 13), (1, 12), (2, 10), (3, 8), (4, 6), (5, 3), (6, 1), (1, 13), (2, 11), (3, 9),
        (4, 7), (8, 0), (5, 4), (6, 2), (2, 12), (3, 10), (4, 8), (5, 5), (6, 3), (7, 0),
        (2, 13), (3, 11), (4, 9), (5, 6), (6, 4), (7, 1), (3, 12), (4, 10), (5, 7), (6, 5),
        (7, 2), (3, 13), (4, 11), (5, 8), (6, 6), (7, 3), (4, 12), (5, 9), (6, 7), (7, 4),
        (4, 13), (5, 10), (6, 8), (7, 5), (5, 11), (6, 9), (7, 6), (5, 12), (6, 10), (7, 7),
        (5, 13), (6, 11), (7, 8), (6, 12), (7, 9), (6, 13), (9, 0), (7, 10), (7, 11), (7, 12),
        (7, 13),
    ),
)


def place():
    me = lax.axis_index("dp")
    core = lax.rem(me, 2)
    x = lax.rem(lax.div(me, 2), 2)
    y = lax.rem(lax.div(me, 4), 2)
    z = lax.div(me, 8)
    return me, core, x, y, z


def send(src, dst, send_sem, recv_sem, partner):
    copy = pltpu.make_async_remote_copy(
        src_ref=src,
        dst_ref=dst,
        send_sem=send_sem,
        recv_sem=recv_sem,
        device_id=(partner,),
        device_id_type=MESH,
    )
    copy.start()
    return copy


def scale_of(row, scales, edges):
    picked = scales[2]
    picked = jnp.where(row < edges[1], scales[1], picked)
    return jnp.where(row < edges[0], scales[0], picked)


def make_units(edges):
    one, two, short = edges[0] // 16, edges[1] // 16, edges[2] // 16
    units = []
    for k in range((two - one) // 32):
        units.append((one + 32 * k, 1, k % 2 == 0, 16, (1, 1)))
    for k in range(one // 32):
        units.append((32 * k, 1, k % 2 == 1, 16, (0, 0)))
    at = one // 32 * 32
    assert one - at == 16 and short - two == 16
    units.append((at, 1, False, two - at, (0, 2)))
    return units


def settle_rows(sums, pixels, gain, shift):
    mean = sums[0] / pixels
    inv = lax.rsqrt(sums[1] / pixels - mean * mean + EPS_NORM)
    slope = gain * inv
    return mean, inv, slope, shift - mean * slope


def gate(values):
    return 0.5 * jnp.tanh(0.5 * values) + 0.5


def eye_mask(rows, columns, offset=0):
    down = lax.broadcasted_iota(jnp.int32, (rows, columns), 0) + offset
    return down == lax.broadcasted_iota(jnp.int32, (rows, columns), 1)


def column_of(row, size):
    spread = jnp.where(eye_mask(size, size), jnp.broadcast_to(row, (size, size)), 0)
    return jnp.sum(spread, axis=1, keepdims=True)


def total_of(values):
    return jnp.sum(jnp.sum(values, axis=0, keepdims=True), axis=1, keepdims=True)


def fold(values):
    return jnp.sum(values.reshape(values.shape[0] // 8, 8, values.shape[1]), axis=0)


def cast_weight(source, target, square_ref, taps, depth, fetches):
    step = 128
    for tap in taps:
        chunk = source.shape[0] // depth // len(fetches)
        if tap % chunk == 0:
            fetches[tap // chunk].wait()
        new_tap = (tap % 3) * 3 + tap // 3

        @pl.loop(0, depth // step)
        def _(k):
            start = pl.multiple_of(k * step, step)
            values = source[pl.ds(tap * depth + start, step), :]
            target[new_tap, pl.ds(start, step), :] = values.astype(jnp.bfloat16)
            square_ref[...] += fold(values * values)


def factored_votes(grad, rows, row_at, rows_old, rows_new, col_old, level, votes, vote_at, between, after):
    width = grad.shape[1]
    keep = 1.0 - STEP ** (-0.8)
    step = 128
    quarters = width // 128

    def first(k, carry):
        col_sum, row_sum = carry
        start = pl.multiple_of(k * step, step)
        lanes = pl.ds(pl.multiple_of(row_at + start, step), step)
        old = rows_old[:, lanes] * keep
        line = jnp.zeros((8, 128), jnp.float32)
        for m in range(step // 8):
            block = grad[pl.ds(start + 8 * m, 8), :]
            square = block * block
            col_sum = col_sum + square
            part = square[:, :128]
            for q in range(1, quarters):
                part = part + square[:, 128 * q : 128 * (q + 1)]
            part = part * ((1.0 - keep) / width)
            diagonal = eye_mask(8, 128, 8 * m)
            part = part + jnp.where(diagonal, jnp.broadcast_to(old, (8, 128)), 0.0)
            row = jnp.sum(part, axis=1, keepdims=True) + (1.0 - keep) * EPS_ROW
            row = jnp.broadcast_to(row, (8, 128))
            level[pl.ds(start + 8 * m, 8), :] = row
            row_sum = row_sum + row
            line = line + jnp.where(diagonal, row, 0.0)
        rows_new[:, lanes] = jnp.sum(line, axis=0, keepdims=True)
        return col_sum, row_sum

    col_sum, row_sum = lax.fori_loop(
        0,
        rows // step,
        first,
        (jnp.zeros((8, width), jnp.float32), jnp.zeros((8, 128), jnp.float32)),
    )
    col_new = keep * col_old + (1.0 - keep) * (
        jnp.sum(col_sum, axis=0, keepdims=True) / rows + EPS_ROW
    )
    scale = lax.rsqrt(col_new)
    root_mean = jnp.sqrt(jnp.sum(row_sum, axis=0, keepdims=True) / rows)

    def second(k, carry):
        start = pl.multiple_of(k * step, step)
        for m in range(step // 8):
            here = pl.ds(start + 8 * m, 8)
            factor = lax.rsqrt(level[here, :]) * root_mean
            level[here, :] = factor
            raw = grad[here, :] * scale
            power = raw * raw
            part = power[:, :128]
            for q in range(1, quarters):
                part = part + power[:, 128 * q : 128 * (q + 1)]
            carry = carry + part * (factor * factor)
        return carry

    between[0]()
    power = lax.fori_loop(0, rows // step, second, jnp.zeros((8, 128), jnp.float32))
    between[1]()
    clip = jnp.maximum(1.0, jnp.sqrt(total_of(power) / (rows * width)))
    scale = scale / clip

    def third(k, _):
        start = pl.multiple_of(k * step, step)
        for m in range(step // 16):
            here = pl.ds(start + 16 * m, 16)
            factor = level[here, :]
            factor = jnp.concatenate([factor] * quarters, axis=1)
            vote = jnp.tanh(grad[here, :] * factor * scale).astype(jnp.bfloat16)
            at = pl.multiple_of((vote_at + start) * 4 + GROUP * m, GROUP)
            for q in range(quarters):
                votes[pl.ds(at + 16 * q, 16), :] = vote[:, 128 * q : 128 * (q + 1)]
        return 0

    part = 512 // step
    for k in range(0, rows // step, part):
        lax.fori_loop(k, min(k + part, rows // step), third, 0)
        after(k // part)
    return col_new


def step_kernel(
    edges,
    units,
    root,
    images,
    one_hbm,
    two_hbm,
    short_hbm,
    head_ref,
    norm_ref,
    valid_ref,
    label_ref,
    row_ref,
    col_ref,
    moment_ref,
    new_ref,
    vote_ref,
    out_ref,
    row_new,
    col_new,
    moment_new,
    loss_ref,
    count_ref,
    xs,
    grad_one,
    grad_two,
    grad_short,
    low_one,
    low_two,
    low_short,
    main_pre,
    side_pre,
    main_two,
    active,
    back_two,
    back_one,
    back_side,
    active_t,
    xs_t,
    head_pad,
    level,
    square,
    post_one,
    plane_one,
    line_one,
    post_two,
    plane_two,
    line_two,
    tail_post,
    tail_plane,
    tail_line,
    core_in,
    wide_in,
    deep_in,
    line_in,
    sum_low,
    landed,
    total,
    own_weight,
    weight,
    vote_flat,
    new_flat,
    fetch_sem,
    small_send,
    small_recv,
    rs_send,
    rs_recv,
    line_send,
    line_recv,
    pass_send,
    land_recv,
    spread_send,
    spread_recv,
    ag_send,
    ag_recv,
    free_sem,
    load_sem,
):
    slots, in_width = xs.shape[4:]
    width = main_pre.shape[1]
    side = 4
    band = side * slots
    pixel_count = side * side
    classes = head_ref.shape[0]
    keep = 1.0 - STEP ** (-0.8)
    low = jnp.bfloat16
    f32 = jnp.float32

    me, core, x, y, z = place()
    flip_core = me + 1 - 2 * core
    flip_x = me + 2 - 4 * x
    flip_y = me + 4 - 8 * y
    spot = lax.rem(me, 8)
    near = [z * 8 + lax.rem(spot + k, 8) for k in range(1, 8)]
    far = [lax.rem(z + k, 4) * 8 + spot for k in range(1, 4)]
    others = [lax.rem(me + k, 32) for k in range(1, 32)]

    count = images.shape[0]
    loads = []
    for half in range(2):
        lanes = slice(128 * half, 128 * (half + 1))
        loads.append(
            pltpu.make_async_copy(
                images.at[:, lanes], core_in.at[pl.ds(half * count, count)], load_sem.at[half]
            )
        )
        loads[half].start()

    def chunks_of(source, target, first, count):
        rows = source.shape[0] // count
        return [
            pltpu.make_async_copy(
                source.at[pl.ds(k * rows, rows)],
                target.at[pl.ds(k * rows, rows)],
                fetch_sem.at[first + k],
            )
            for k in range(count)
        ]

    fetch_one = chunks_of(one_hbm, grad_one, 0, 3)
    fetch_short = chunks_of(short_hbm, grad_short, 3, 1)
    fetch_two = chunks_of(two_hbm, grad_two, 4, 3)
    for fetch in fetch_one + fetch_short:
        fetch.start()
    barrier = pltpu.get_barrier_semaphore()
    for partner in others:
        pl.semaphore_signal(barrier, inc=1, device_id=(partner,), device_id_type=MESH)

    def fetch_rows(row, count, place_at, sem):
        parts = (
            (one_hbm, 0, edges[0]),
            (two_hbm, edges[0], edges[1]),
            (short_hbm, edges[1], edges[2]),
        )
        for ref, first, last in parts:

            @pl.when(jnp.logical_and(row >= first, row < last))
            def _():
                start = pl.multiple_of(row - first, count)
                pltpu.make_async_copy(
                    ref.at[pl.ds(start, count)], weight.at[pl.ds(place_at, count)], sem
                ).start()

    first_row = me * OWN

    for half in range(2):
        lanes = slice(128 * half, 128 * (half + 1))
        loads[half].wait()
        level[:count, :] = core_in[pl.ds(half * count, count), :].astype(f32)
        for h in range(2 * side):
            for w in range(2 * side):
                rows = level[pl.ds(2 * side * h + w, slots, stride=4 * pixel_count), :]
                xs[w % 2, w // 2, h % 2, h // 2, :, lanes] = rows.astype(low)

    scales = {}

    def scale_from(weight_square, size):
        return jnp.maximum(EPS_SCALE, jnp.sqrt(total_of(weight_square) / size))

    exchanges = (
        (post_one, plane_one, line_one),
        (post_two, plane_two, line_two),
        (tail_post, tail_plane, tail_line),
    )

    def exchange_start(which, values):
        mine_ref, plane_ref, _ = exchanges[which]
        mine_ref[...] = values
        plane_ref[spot] = values
        return [
            send(
                mine_ref,
                plane_ref.at[spot],
                small_send.at[which, k],
                small_recv.at[which, k],
                partner,
            )
            for k, partner in enumerate(near)
        ]

    def pack_rows(rows):
        pieces = [row[:, 128 * q : 128 * (q + 1)] for row in rows for q in range(4)]
        pad = -len(pieces) % 8
        if pad:
            pieces.append(jnp.zeros((pad, 128), f32))
        return jnp.concatenate(pieces, axis=0)

    def unpack_row(lines_in, k):
        return jnp.concatenate([lines_in[4 * k + q : 4 * k + q + 1] for q in range(4)], axis=1)

    def exchange_middle(which, copies):
        _, plane_ref, line_ref = exchanges[which]
        for copy in copies:
            copy.wait()
        line_ref[z] = functools.reduce(lambda a, b: a + b, [plane_ref[k] for k in range(8)])
        return [
            send(
                line_ref.at[z],
                line_ref.at[z],
                small_send.at[which, 7 + k],
                small_recv.at[which, 7 + k],
                partner,
            )
            for k, partner in enumerate(far)
        ]

    def exchange_end(which, copies):
        line_ref = exchanges[which][2]
        for copy in copies:
            copy.wait()
        return (line_ref[0] + line_ref[1]) + (line_ref[2] + line_ref[3])

    def lines(start, count):
        return pl.ds(pl.multiple_of(start, 16), count)

    sizes = [GROUP * unit[1] for unit in units]
    starts = [sum(sizes[:k]) for k in range(len(units) + 1)]

    def part_of(ref, u, share, start, count):
        return ref.at[lines(share * starts[u] + start, count)]

    def places(u):
        if units[u][2]:
            return x, y, flip_x, flip_y
        return y, x, flip_y, flip_x

    def unit_start(u, cc):
        return GROUP * units[u][0] + cc * (GROUP * units[u][3])

    def own_group(u):
        first, second, _, _ = places(u)
        return units[u][0] + core * units[u][3] + (first * 8 + second * 4 + z) * units[u][1]

    def halve(source, target, u, stage, partner):
        return send(source, target, rs_send.at[u, stage], rs_recv.at[u, stage], partner)

    def scatter_start(u):
        size = 16 * sizes[u]
        return halve(
            out_ref.at[lines(unit_start(u, 1 - core), size)],
            part_of(core_in, u, 16, 0, size),
            u,
            0,
            flip_core,
        )

    def add_to(ref, u, share, source_ref, source_start):
        size = share * sizes[u]
        here = lines(share * starts[u], size)
        ref[here, :] = ref[here, :] + source_ref[lines(source_start, size), :]

    def scatter_one(u, copy):
        copy.wait()
        add_to(core_in, u, 16, out_ref, unit_start(u, core))
        pl.semaphore_signal(
            free_sem.at[u], inc=1, device_id=(flip_core,), device_id_type=MESH
        )
        first, _, flip_first, _ = places(u)
        size = 8 * sizes[u]
        return halve(
            part_of(core_in, u, 16, (1 - first) * size, size),
            part_of(wide_in, u, 8, 0, size),
            u,
            1,
            flip_first,
        )

    def scatter_two(u, copy):
        copy.wait()
        first, second, _, flip_second = places(u)
        add_to(wide_in, u, 8, core_in, 16 * starts[u] + first * 8 * sizes[u])
        size = 4 * sizes[u]
        return halve(
            part_of(wide_in, u, 8, (1 - second) * size, size),
            part_of(deep_in, u, 4, 0, size),
            u,
            2,
            flip_second,
        )

    def line_copy(u, k):
        plane_to = lax.rem(z + k, 4)
        return pltpu.make_async_remote_copy(
            src_ref=part_of(deep_in, u, 4, plane_to * sizes[u], sizes[u]),
            dst_ref=part_of(line_in, u, 4, z * sizes[u], sizes[u]),
            send_sem=line_send.at[u, k],
            recv_sem=line_recv.at[u, k],
            device_id=(plane_to * 8 + spot,),
            device_id_type=MESH,
        )

    def scatter_three(u, copy):
        copy.wait()
        _, second, _, _ = places(u)
        add_to(deep_in, u, 4, wide_in, 8 * starts[u] + second * 4 * sizes[u])
        for k in (3, 2, 1):
            line_copy(u, k).start()
        here = lines(4 * starts[u] + z * sizes[u], sizes[u])
        line_in[here, :] = deep_in[here, :]

    groups = (edges[2] + TAIL) // 16
    spare = (groups - 1) // 32
    passes = []

    def land(local, group, to, slot, index):
        source = sum_low.at[lines(local * GROUP, GROUP)]
        target = landed.at[lines(slot * GROUP, GROUP)]
        copy = pltpu.make_async_remote_copy(
            src_ref=source,
            dst_ref=target,
            send_sem=pass_send.at[index],
            recv_sem=land_recv.at[slot],
            device_id=(to,),
            device_id_type=MESH,
        )
        return copy, source, target

    def pass_on(u):
        for m in range(units[u][1]):
            local = starts[u] // GROUP + m
            group = own_group(u) + m
            to, slot = lax.div(group, spare), lax.rem(group, spare)
            for halo in range(2):
                index = 2 * local + halo
                if halo:
                    receiver, at = lax.rem(to + 31, 32), spare
                    wanted = jnp.logical_and(slot == 0, group > 0)
                else:
                    receiver, at, wanted = to, slot, group >= 0
                away = jnp.logical_and(wanted, receiver != me)
                here = jnp.logical_and(wanted, receiver == me)
                copy, source, target = land(local, group, receiver, at, index)

                @pl.when(away)
                def _():
                    copy.start()

                @pl.when(here)
                def _():
                    target[...] = source[...]

                passes.append((away, copy))

    def flat_rows(row, q, values, ref):
        ref[pl.ds(row * 4 + q, 8, stride=4), :] = values

    def old_rows(u, cc):
        matrix = units[u][4][cc]
        base = edges[matrix - 1] if matrix else 0
        return (one_hbm, two_hbm, short_hbm)[matrix], 16 * own_group(u) - base, 16 * units[u][1]

    def own_fetch(u):
        target = own_weight.at[pl.ds(starts[u] // 4, 16 * units[u][1])]
        matrices = units[u][4]
        for cc in range(2):
            if cc and matrices[0] == matrices[1]:
                continue

            @pl.when((core == cc) if matrices[0] != matrices[1] else (core >= 0))
            def _():
                ref, row, count = old_rows(u, cc)
                pltpu.make_async_copy(
                    ref.at[pl.ds(pl.multiple_of(row, 16), count)], target, fetch_sem.at[9 + u]
                ).start()

    def spread_copy(u, k):
        own = out_ref.at[lines(own_group(u) * GROUP, sizes[u])]
        return pltpu.make_async_remote_copy(
            src_ref=own,
            dst_ref=own,
            send_sem=spread_send.at[u, k],
            recv_sem=spread_recv.at[u, k],
            device_id=(far[k - 1],),
            device_id_type=MESH,
        )

    def own_block(u):
        size = sizes[u]
        for k in range(1, 4):
            line_copy(u, k).wait_recv()
        here = pl.ds(starts[u], size)
        low_sum = functools.reduce(
            lambda a, b: a + b,
            [line_in[pl.ds(4 * starts[u] + t * size, size), :].astype(f32) for t in range(4)],
        ).astype(low)
        sum_low[here, :] = low_sum
        total[here, :] = low_sum.astype(f32)
        target = own_weight.at[pl.ds(starts[u] // 4, 16 * units[u][1])]
        pltpu.make_async_copy(target, target, fetch_sem.at[9 + u]).wait()
        matrices = units[u][4]
        scale = jnp.where(core == 0, scales[matrices[0]], scales[matrices[1]])
        for m in range(units[u][1]):
            row = starts[u] // 4 + 16 * m
            for part in (0, 8):
                for q in range(4):
                    summed = total[pl.ds(row * 4 + 16 * q + part, 8), :]
                    old = own_weight[pl.ds(row + part, 8), 128 * q : 128 * (q + 1)]
                    fresh = old - scale * jnp.tanh(summed * root)
                    flat_rows(row + part, q, fresh, new_flat)
        out_ref[lines(own_group(u) * GROUP, size), :] = new_flat[here, :].astype(low)
        for k in (3, 2, 1):
            spread_copy(u, k).start()
        pass_on(u)

    def piece(rows, u, stage, partner):
        return send(
            out_ref.at[rows], out_ref.at[rows], ag_send.at[u, stage], ag_recv.at[u, stage], partner
        )

    def gather_one(u):
        for k in range(1, 4):
            spread_copy(u, k).wait_recv()
        first, second, _, flip_second = places(u)
        size = 4 * sizes[u]
        start = unit_start(u, core) + (2 * first + second) * size
        return piece(lines(start, size), u, 0, flip_second)

    def gather_two(u, copy):
        copy.wait()
        first, _, flip_first, _ = places(u)
        size = 8 * sizes[u]
        return piece(lines(unit_start(u, core) + first * size, size), u, 1, flip_first)

    def gather_three(u, copy):
        copy.wait()
        pl.semaphore_wait(free_sem.at[u], 1)
        return piece(lines(unit_start(u, core), 16 * sizes[u]), u, 2, flip_core)

    def renew(row, at_row):
        scale = scale_of(at_row, [scales[k] for k in range(3)], edges)
        for part in (0, 8):
            for q in range(4):
                summed = total[pl.ds(row * 4 + 16 * q + part, 8), :]
                old = weight[pl.ds(row + part, 8), 128 * q : 128 * (q + 1)]
                fresh = old - scale * jnp.tanh(summed * root)
                flat_rows(row + part, q, summed, vote_flat)
                flat_rows(row + part, q, fresh, new_flat)

    valid_column = column_of(valid_ref[...].astype(f32), slots)
    weight_slot = jnp.broadcast_to(valid_column, (slots, width))
    weight_band = jnp.concatenate([weight_slot] * side, axis=0)

    square[...] = jnp.zeros_like(square)
    cast_weight(grad_one, low_one, square, range(9), in_width, fetch_one)
    scales[0] = scale_from(square[...], grad_one.size)
    square[...] = jnp.zeros_like(square)
    cast_weight(grad_short, low_short, square, range(1), in_width, fetch_short)
    scales[2] = scale_from(square[...], grad_short.size)
    for fetch in fetch_two:
        fetch.start()
    for k in range(OWN // PIECE):
        fetch_rows(first_row + k * PIECE, PIECE, k * PIECE, fetch_sem.at[7])
    fetch_rows(first_row + OWN, TAIL, OWN, fetch_sem.at[8])
    for u in range(len(units)):
        own_fetch(u)

    def image_taps(j):
        pieces = []
        for b in range(3):
            column = j if b else j - 1
            if column < 0:
                continue
            across = 0 if b == 1 else 1
            for a in range(3):
                if a == 1:
                    piece = xs[across, column, 0].reshape(band, in_width)
                elif a == 2:
                    piece = xs[across, column, 1].reshape(band, in_width)
                else:
                    piece = xs[across, column, 1, : side - 1].reshape(band - slots, in_width)
                    piece = jnp.concatenate([jnp.zeros((slots, in_width), low), piece], axis=0)
                pieces.append(piece)
        return jnp.concatenate(pieces, axis=1)

    def moments(values):
        weighted = values * weight_band
        return (
            jnp.sum(weighted, axis=0, keepdims=True),
            jnp.sum(weighted * values, axis=0, keepdims=True),
        )

    def add_up(old, new):
        return [a + b for a, b in zip(old, new)]

    none = jnp.zeros((1, width), f32)
    main_sums, side_sums = [none, none], [none, none]
    for j in range(side):
        here = pl.ds(j * band, band)
        low_rows = low_one[3 if j == 0 else 0 :].reshape(-1, width)
        value = jnp.dot(image_taps(j), low_rows, preferred_element_type=f32)
        main_pre[here, :] = value
        main_sums = add_up(main_sums, moments(value))
        value = jnp.dot(
            xs[0, j, 0].reshape(band, in_width), low_short[0], preferred_element_type=f32
        )
        side_pre[here, :] = value
        side_sums = add_up(side_sums, moments(value))

    count = jnp.broadcast_to(jnp.sum(valid_column, axis=0, keepdims=True), (1, width))
    pl.semaphore_wait(barrier, len(others))
    copies = exchange_start(
        0, pack_rows(main_sums + side_sums + [count])
    )
    square[...] = jnp.zeros_like(square)
    cast_weight(grad_two, low_two, square, range(5), width, fetch_two)
    copies = exchange_middle(0, copies)
    cast_weight(grad_two, low_two, square, range(5, 9), width, fetch_two)
    scales[1] = scale_from(square[...], grad_two.size)
    border = jnp.zeros((side, 1, slots, width), low)
    active[:, 0:1] = border
    active[:, side + 1 :] = border
    back_two[:, 0:1] = border
    back_two[:, side + 1 :] = border
    back_one[:, side:] = border
    head_pad[...] = jnp.zeros_like(head_pad)
    head_pad[:classes, :] = head_ref[...]
    head = head_pad[:16, :]
    scales[3] = scale_from(head * head, head_ref.size)
    params = norm_ref[...]
    scales[4] = scale_from(params * params, norm_ref.size)
    sums = exchange_end(0, copies)
    sums = [unpack_row(sums, k) for k in range(5)]

    valid_count = sums[4]
    count_ref[...] = valid_count[:, :1]
    denominator = jnp.maximum(valid_count, 1.0)
    pixels = denominator * pixel_count
    gains = [norm_ref[k : k + 1, :] for k in range(6)]
    mean_one, inv_one, slope_one, base_one = settle_rows(
        (sums[0], sums[1]), pixels, gains[0], gains[1]
    )
    mean_side, inv_side, slope_side, base_side = settle_rows(
        (sums[2], sums[3]), pixels, gains[4], gains[5]
    )

    for j in range(side):
        hidden = main_pre[pl.ds(j * band, band), :] * slope_one + base_one
        active[j, 1 : side + 1] = (
            (hidden * gate(hidden)).astype(low).reshape(side, slots, width)
        )
    two_sums = [none, none]
    for j in range(side):
        taps = [b for b in range(3) if 0 <= j + b - 1 < side]
        pieces = [
            active[j + b - 1, a : a + side].reshape(band, width) for b in taps for a in range(3)
        ]
        low_rows = low_two[3 * taps[0] : 3 * taps[-1] + 3].reshape(-1, width)
        value = jnp.dot(jnp.concatenate(pieces, axis=1), low_rows, preferred_element_type=f32)
        main_two[pl.ds(j * band, band), :] = value
        two_sums = add_up(two_sums, moments(value))
    copies = exchange_start(1, pack_rows(two_sums))
    for j in range(side):
        block = active[j, 1 : side + 1].reshape(band, width)
        active_t[:, j * band : (j + 1) * band] = block.T
    label_column = column_of(label_ref[...].astype(f32), slots).astype(jnp.int32)
    head_low = head_pad[...].astype(low)
    copies = exchange_middle(1, copies)
    for across in range(2):
        for down in range(2):
            for j in range(side):
                block = xs[across, j, down].reshape(band, in_width)
                xs_t[across, down, :, j * band : (j + 1) * band] = block.T
    sums = exchange_end(1, copies)
    sums = [unpack_row(sums, k) for k in range(2)]
    mean_two, inv_two, slope_two, base_two = settle_rows(
        (sums[0], sums[1]), pixels, gains[2], gains[3]
    )

    base_joined = base_two + base_side

    quarters = [slice(128 * q, 128 * (q + 1)) for q in range(width // 128)]

    def joined_of(here, lanes):
        return (
            main_two[here, lanes] * slope_two[:, lanes]
            + side_pre[here, lanes] * slope_side[:, lanes]
            + base_joined[:, lanes]
        )

    pooled = []
    for lanes in quarters:
        total_joined = jnp.zeros((slots, 128), f32)
        for p in range(pixel_count):
            joined = joined_of(pl.ds(p * slots, slots), lanes)
            total_joined = total_joined + joined * gate(joined)
        pooled.append(total_joined)
    pooled = jnp.concatenate(pooled, axis=1)
    pooled = (pooled / pixel_count).astype(low)
    logits = lax.dot_general(
        pooled, head_low, (((1,), (1,)), ((), ())), preferred_element_type=f32
    )
    lane = lax.broadcasted_iota(jnp.int32, logits.shape, 1)
    real = lane < classes
    largest = jnp.max(jnp.where(real, logits, -jnp.inf), axis=1, keepdims=True)
    powers = jnp.where(real, jnp.exp(jnp.where(real, logits - largest, 0.0)), 0.0)
    total_power = jnp.sum(powers, axis=1, keepdims=True)
    onehot = jnp.where(lane == label_column, 1.0, 0.0)
    entropy = largest + jnp.log(total_power) - jnp.sum(onehot * logits, axis=1, keepdims=True)
    loss = jnp.sum(entropy * valid_column, axis=0, keepdims=True)
    grad_logits = (
        (powers / total_power - onehot) * (valid_column / denominator[:, :1])
    ).astype(low)
    grad_head = lax.dot_general(
        grad_logits, pooled, (((0,), (0,)), ((), ())), preferred_element_type=f32
    )[:16]
    grad_pooled = jnp.dot(grad_logits, head_low, preferred_element_type=f32) / pixel_count

    join_sums = []
    for lanes in quarters:
        three = [jnp.zeros((8, 128), f32)] * 3
        for p in range(pixel_count):
            here = pl.ds(p * slots, slots)
            joined = joined_of(here, lanes)
            opened = gate(joined)
            grad = grad_pooled[:, lanes] * (opened * (1.0 + joined * (1.0 - opened)))
            normed_two = (main_two[here, lanes] - mean_two[:, lanes]) * inv_two[:, lanes]
            normed_side = (side_pre[here, lanes] - mean_side[:, lanes]) * inv_side[:, lanes]
            new = (grad * normed_two, grad * normed_side, grad)
            three = [old + fold(each) for old, each in zip(three, new)]
            back_two[p // side, 1 + p % side, :, lanes] = (grad * slope_two[:, lanes]).astype(low)
            back_side[here, lanes] = (grad * slope_side[:, lanes]).astype(low)
        join_sums.append([jnp.sum(each, axis=0, keepdims=True) for each in three])
    gain_two, gain_side, shift_two = [jnp.concatenate(each, axis=1) for each in zip(*join_sums)]

    for b in range(3):
        first, last = max(0, b - 1), min(side, side + b - 1)
        left = active_t[:, first * band : last * band]
        for a in range(3):
            right = back_two[first - b + 1 : last - b + 1, 2 - a : 2 - a + side]
            grad_two[pl.ds((a * 3 + b) * width, width), :] = jnp.dot(
                left, right.reshape(-1, width), preferred_element_type=f32
            )

    def nothing():
        pass

    def matrix_votes(k, grad, between, after):
        here = pl.ds(k * width, width)
        start = edges[k - 1] if k else 0
        col_new[:, here] = factored_votes(
            grad,
            grad.shape[0],
            start,
            row_ref,
            row_new,
            col_ref[:, here],
            level,
            out_ref,
            start,
            between,
            after,
        )

    kept = {}

    def tail_step():
        sums = exchange_end(2, kept["tail"])
        loss_ref[...] = sums[4 * TAIL : 4 * TAIL + 1, :1]
        old = jnp.concatenate([head_ref[...], norm_ref[...]], axis=0)
        is_head = lax.broadcasted_iota(jnp.int32, (TAIL, width), 0) < classes
        scale = jnp.where(is_head, scales[3], scales[4])
        sums = jnp.concatenate([sums[TAIL * q : TAIL * (q + 1)] for q in range(4)], axis=1)
        fresh = old - scale * jnp.tanh(sums * root)
        both = jnp.concatenate([sums, fresh], axis=0)
        high = both.astype(low)
        rest = both - high.astype(f32)
        middle = rest.astype(low)
        parts = jnp.concatenate([high, middle, (rest - middle.astype(f32)).astype(low)], axis=0)

        flat_sums, flat_new = [], []
        window = 256
        for q in range(classes):
            start = min(q * width // classes // 128 * 128, width - window)
            down = lax.broadcasted_iota(jnp.int32, (window, width), 0)
            across = lax.broadcasted_iota(jnp.int32, (window, width), 1)
            gap = across - classes * down + (q * width - classes * start)
            chosen = jnp.where(jnp.logical_and(gap >= 0, gap < classes), 1.0, 0.0).astype(low)
            moved = jnp.dot(parts[:, start : start + window], chosen, preferred_element_type=f32)
            moved = moved[: 2 * TAIL] + moved[2 * TAIL : 4 * TAIL] + moved[4 * TAIL :]
            spot_of = lax.broadcasted_iota(jnp.int32, (TAIL, width), 1).astype(f32) + q * width
            class_of = spot_of - classes * jnp.floor((spot_of + 0.5) / classes)
            here = lax.broadcasted_iota(jnp.int32, (TAIL, width), 0).astype(f32) == class_of
            flat_sums.append(jnp.sum(jnp.where(here, moved[:TAIL], 0.0), axis=0, keepdims=True))
            flat_new.append(jnp.sum(jnp.where(here, moved[TAIL:], 0.0), axis=0, keepdims=True))
        kept["sums"] = jnp.concatenate(flat_sums + [sums[classes:]], axis=0)
        kept["new"] = jnp.concatenate(flat_new + [fresh[classes:]], axis=0)

    def return_step():
        mine = [own_group(u) for u in range(len(units))]
        for slot in range(spare + 1):
            group = me * spare + slot
            own = group < 0
            for u, unit in enumerate(units):
                inside = jnp.logical_and(group >= mine[u], group < mine[u] + unit[1])
                own = jnp.logical_or(own, inside)

            @pl.when(jnp.logical_and(jnp.logical_not(own), group < groups - 1))
            def _():
                land(0, group, me, slot, 0)[0].wait_recv()

        pltpu.make_async_copy(
            weight.at[pl.ds(0, OWN)], weight.at[pl.ds(0, OWN)], fetch_sem.at[7]
        ).wait()
        total[pl.ds(0, SPAN), :] = landed[pl.ds(0, SPAN), :].astype(f32)

        @pl.loop(0, OWN // 16)
        def _(k):
            row = pl.multiple_of(k * 16, 16)
            renew(row, first_row + row)

        @pl.when(me < 31)
        def _():
            pltpu.make_async_copy(
                weight.at[pl.ds(OWN, TAIL)], weight.at[pl.ds(OWN, TAIL)], fetch_sem.at[8]
            ).wait()
            total[pl.ds(SPAN, GROUP), :] = landed[pl.ds(SPAN, GROUP), :].astype(f32)
            renew(OWN, first_row + OWN)

        def tail_rows(values, ref):
            for u in (0, 8):
                for q in range(4):
                    flat_rows(OWN + u, q, values[u : u + 8, 128 * q : 128 * (q + 1)], ref)

        @pl.when(me == 31)
        def _():
            tail_rows(kept["sums"], vote_flat)
            tail_rows(kept["new"], new_flat)

        shift = 2 * me
        share = vote_ref.shape[0]
        vote_ref[...] = vote_flat[pl.ds(shift, share), :]
        new_ref[...] = new_flat[pl.ds(shift, share), :]
        tail_rows(kept["new"], new_flat)
        out_ref[pl.ds(32 * SPAN, GROUP), :] = new_flat[pl.ds(SPAN, GROUP), :].astype(low)

    in_flight = {}
    steps = (
        lambda u, copy: scatter_start(u),
        scatter_one,
        scatter_two,
        scatter_three,
        lambda u, copy: own_block(u),
        lambda u, copy: gather_one(u),
        gather_two,
        gather_three,
        lambda u, copy: tail_step(),
        lambda u, copy: return_step(),
    )

    def go(number, u):
        got = steps[number](u, in_flight.get(u))
        if number < 8:
            in_flight[u] = got

    def turn(number):
        for step_number, u in SCHEDULE[number]:
            go(step_number, u)

    early = edges[1] // 512 - edges[0] // 512
    matrix_votes(1, grad_two, (nothing, nothing), lambda k: go(0, k) if k < 2 else None)
    turn(0)
    grad_short[...] = jnp.dot(xs_t[0, 0], back_side[...], preferred_element_type=f32)
    matrix_votes(2, grad_short, (nothing, nothing), lambda k: None)

    gain_one, shift_one = none, none
    for j in range(side):
        taps = [b for b in range(3) if 0 <= j - b + 1 < side]
        pieces = [
            back_two[j - b + 1, 2 - a : 2 - a + side].reshape(band, width)
            for b in taps
            for a in range(3)
        ]
        weights = jnp.concatenate([low_two[b * 3 + a] for b in taps for a in range(3)], axis=1)
        grad = lax.dot_general(
            jnp.concatenate(pieces, axis=1),
            weights,
            (((1,), (1,)), ((), ())),
            preferred_element_type=f32,
        )
        before = main_pre[pl.ds(j * band, band), :]
        hidden = before * slope_one + base_one
        opened = gate(hidden)
        grad = grad * (opened * (1.0 + hidden * (1.0 - opened)))
        shift_one = shift_one + jnp.sum(grad, axis=0, keepdims=True)
        gain_one = gain_one + jnp.sum(
            grad * ((before - mean_one) * inv_one), axis=0, keepdims=True
        )
        back_one[j, :side] = (grad * slope_one).astype(low).reshape(side, slots, width)
        turn(1 + j)

    square_head = grad_head * grad_head + EPS_ROW
    real = lax.broadcasted_iota(jnp.int32, square_head.shape, 0) < classes
    square_head = jnp.where(real, square_head, 0.0)
    head_lanes = pl.ds(edges[2], width)
    old = row_ref[:, head_lanes]
    row = keep * old + (1.0 - keep) * jnp.sum(square_head, axis=0, keepdims=True) / classes
    row_new[:, head_lanes] = row
    diagonal = eye_mask(16, classes)
    old = jnp.broadcast_to(col_ref[:, 3 * width :], (16, classes))
    old = jnp.sum(jnp.where(diagonal, old, 0.0), axis=1, keepdims=True)
    column = keep * old + (1.0 - keep) * jnp.sum(square_head, axis=1, keepdims=True) / width
    col_new[:, 3 * width :] = jnp.sum(
        jnp.where(diagonal, jnp.broadcast_to(column, (16, classes)), 0.0), axis=0, keepdims=True
    )
    real_column = lax.broadcasted_iota(jnp.int32, column.shape, 0) < classes
    column = jnp.where(real_column, column, 1.0)
    mean = jnp.sum(row, axis=1, keepdims=True) / width
    raw = grad_head * (lax.rsqrt(row) * jnp.sqrt(mean)) * lax.rsqrt(column)
    clip = jnp.maximum(1.0, jnp.sqrt(total_of(raw * raw) / (classes * width)))
    head_votes = jnp.tanh(raw / clip)[:classes]

    raws = []
    for k, grad in enumerate((gain_one, shift_one, gain_two, shift_two, gain_side, shift_two)):
        here = pl.ds(k * width, width)
        moment = keep * moment_ref[:, here] + (1.0 - keep) * (grad * grad + EPS_ROW)
        moment_new[:, here] = moment
        raws.append(grad * lax.rsqrt(moment))
    raw = jnp.concatenate(raws, axis=0)
    clip = jnp.maximum(1.0, jnp.sqrt(total_of(raw * raw) / raw.size))
    norm_votes = jnp.tanh(raw / clip)
    tail_votes = jnp.concatenate([head_votes, norm_votes], axis=0)
    kept["tail"] = exchange_start(
        2,
        jnp.concatenate(
            [tail_votes[:, 128 * q : 128 * (q + 1)] for q in range(4)]
            + [jnp.broadcast_to(loss, (8, 128))],
            axis=0,
        ),
    )


    for b in range(3):
        first, last = (0, side - 1) if b == 0 else (0, side)
        shift = 1 if b == 0 else 0
        for a in range(3):
            left = xs_t[0 if b == 1 else 1, 0 if a == 1 else 1, :, first * band : last * band]
            start = 1 if a == 0 else 0
            right = back_one[first + shift : last + shift, start : start + side]
            grad_one[pl.ds((a * 3 + b) * in_width, in_width), :] = jnp.dot(
                left, right.reshape(-1, width), preferred_element_type=f32
            )
        if b == 1:
            kept["tail"] = exchange_middle(2, kept["tail"])
        turn(5 + b)

    matrix_votes(
        0,
        grad_one,
        (lambda: turn(8), lambda: turn(9)),
        lambda k: go(0, early + k) if k < 2 else None,
    )
    turn(10)
    for u in range(len(units)):
        in_flight[u].wait()
        for k in range(1, 4):
            line_copy(u, k).wait_send()
            spread_copy(u, k).wait_send()
    for away, copy in passes:

        @pl.when(away)
        def _():
            copy.wait_send()


def finish_kernel(count, chunks, *refs):
    sources, targets, sem = refs[:count], refs[count : 2 * count], refs[2 * count]
    rows = sources[0].shape[0]
    step = -(-rows // chunks // 16) * 16
    copies = []
    for k in range(chunks):
        here = pl.ds(k * step, min(step, rows - k * step))
        copies.append(
            pltpu.make_async_copy(sources[0].at[here], targets[0].at[here], sem.at[k])
        )
    for k in range(1, count):
        copies.append(pltpu.make_async_copy(sources[k], targets[k], sem.at[chunks + k]))
    for copy in copies:
        copy.start()
    for copy in copies:
        copy.wait()


def finish(values):
    count, chunks = len(values), 4
    held = [pltpu.with_memory_space_constraint(value, pltpu.VMEM) for value in values]
    return pl.pallas_call(
        functools.partial(finish_kernel, count, chunks),
        out_shape=[jax.ShapeDtypeStruct(value.shape, value.dtype) for value in values],
        in_specs=[pl.BlockSpec(memory_space=pltpu.VMEM)] * count,
        out_specs=[pl.BlockSpec(memory_space=pl.ANY)] * count,
        scratch_shapes=[pltpu.SemaphoreType.DMA((chunks + count,))],
        compiler_params=pltpu.CompilerParams(vmem_limit_bytes=1024 * 1024),
        name="finish",
    )(*held)


def run_step(images, conv_one, conv_two, shortcut, head, norm_params, valid, labels, rows, cols, moment):
    vmem = pl.BlockSpec(memory_space=pltpu.VMEM)
    hbm = pl.BlockSpec(memory_space=pl.ANY)
    low, f32 = jnp.bfloat16, jnp.float32
    dma = pltpu.SemaphoreType.DMA
    workers = lax.axis_size("dp")
    slots, in_width = valid.shape[1], images.shape[1]
    width = conv_one.shape[1]
    pixels = images.shape[0] // 4
    shape = pltpu.VMEM
    edges = [conv_one.shape[0]]
    edges.append(edges[0] + conv_two.shape[0])
    edges.append(edges[1] + shortcut.shape[0])
    units = make_units(edges)
    flat = (edges[2] + TAIL) * width // 128
    share = flat // workers
    return pl.pallas_call(
        functools.partial(step_kernel, tuple(edges), tuple(units), 1.0 / math.sqrt(workers)),
        out_shape=(
            shape((share, 128), f32),
            shape((share, 128), f32),
            shape((flat, 128), low),
            shape(rows.shape, f32),
            shape(cols.shape, f32),
            shape(moment.shape, f32),
            shape((1, 1), f32),
            shape((1, 1), f32),
        ),
        in_specs=[hbm] * 4 + [vmem] * 7,
        out_specs=(vmem,) * 8,
        scratch_shapes=[
            pltpu.VMEM((2, 4, 2, 4, slots, in_width), low),
            pltpu.VMEM(conv_one.shape, f32),
            pltpu.VMEM(conv_two.shape, f32),
            pltpu.VMEM(shortcut.shape, f32),
            pltpu.VMEM((9, in_width, width), low),
            pltpu.VMEM((9, width, width), low),
            pltpu.VMEM((1, in_width, width), low),
            pltpu.VMEM((pixels, width), f32),
            pltpu.VMEM((pixels, width), f32),
            pltpu.VMEM((pixels, width), f32),
            pltpu.VMEM((4, 6, slots, width), low),
            pltpu.VMEM((4, 6, slots, width), low),
            pltpu.VMEM((4, 5, slots, width), low),
            pltpu.VMEM((pixels, width), low),
            pltpu.VMEM((width, pixels), low),
            pltpu.VMEM((2, 2, in_width, pixels), low),
            pltpu.VMEM((128, width), f32),
            pltpu.VMEM((conv_two.shape[0], 128), f32),
            pltpu.VMEM((8, width), f32),
            pltpu.VMEM((24, 128), f32),
            pltpu.VMEM((8, 24, 128), f32),
            pltpu.VMEM((4, 24, 128), f32),
            pltpu.VMEM((8, 128), f32),
            pltpu.VMEM((8, 8, 128), f32),
            pltpu.VMEM((4, 8, 128), f32),
            pltpu.VMEM((GROUP + 8, 128), f32),
            pltpu.VMEM((8, GROUP + 8, 128), f32),
            pltpu.VMEM((4, GROUP + 8, 128), f32),
            pltpu.VMEM((16 * SPAN, 128), low),
            pltpu.VMEM((8 * SPAN, 128), low),
            pltpu.VMEM((4 * SPAN, 128), low),
            pltpu.VMEM((4 * SPAN, 128), low),
            pltpu.VMEM((SPAN, 128), low),
            pltpu.VMEM((SPAN + GROUP, 128), low),
            pltpu.VMEM((SPAN + GROUP, 128), f32),
            pltpu.VMEM((OWN, width), f32),
            pltpu.VMEM((OWN + TAIL, width), f32),
            pltpu.VMEM((SPAN + GROUP, 128), f32),
            pltpu.VMEM((SPAN + GROUP, 128), f32),
            dma((9 + len(units),)),
            dma((3, 10)),
            dma((3, 10)),
            dma((len(units), 3)),
            dma((len(units), 3)),
            dma((len(units), 4)),
            dma((len(units), 4)),
            dma((2 * OWN // 16,)),
            dma((OWN // 16 + 1,)),
            dma((len(units), 4)),
            dma((len(units), 4)),
            dma((len(units), 3)),
            dma((len(units), 3)),
            pltpu.SemaphoreType.REGULAR((len(units),)),
            dma((2,)),
        ],
        compiler_params=pltpu.CompilerParams(
            collective_id=1, has_side_effects=True, vmem_limit_bytes=54 * 1024 * 1024
        ),
        name="step",
    )(images, conv_one, conv_two, shortcut, head, norm_params, valid, labels, rows, cols, moment)


def scale_for(weight):
    return jnp.maximum(EPS_SCALE, jnp.sqrt(jnp.mean(weight * weight)))


def local_general(
    images,
    valid_slot,
    labels,
    conv_one,
    conv_two,
    shortcut,
    classifier,
    norm_params,
    row_state,
    col_state,
    bn_moment,
):
    in_width = images.shape[3]
    width = conv_one.shape[1]
    kernel_one = conv_one.astype(jnp.bfloat16).reshape(3, 3, in_width, width)
    kernel_two = conv_two.astype(jnp.bfloat16).reshape(3, 3, width, width)
    kernel_short = shortcut.astype(jnp.bfloat16).reshape(1, 1, in_width, width)
    head_low = classifier.astype(jnp.bfloat16)
    slot_count = images.shape[0]
    out_side = images.shape[1] // 2
    pixel_count = out_side * out_side
    slot_weight = valid_slot.astype(jnp.float32)
    pixel_weight = jnp.broadcast_to(slot_weight[:, None], (slot_count, pixel_count)).reshape(-1, 1)
    main_pre, side_pre = first_section(images, kernel_one, kernel_short)
    main_sums = masked_moments(pixel_weight, main_pre)
    side_sums = masked_moments(pixel_weight, side_pre)
    count_row = jnp.broadcast_to(jnp.sum(slot_weight), (width,))
    first_sums = lax.psum(jnp.stack([*main_sums, *side_sums, count_row]), "dp")
    valid_count = first_sums[4, 0]
    denominator = jnp.maximum(valid_count, 1.0)
    pixels = denominator * pixel_count
    norm_one = settle(first_sums[0], first_sums[1], pixels)
    norm_side = settle(first_sums[2], first_sums[3], pixels)
    hidden_one, active, main_two = second_section(
        main_pre, norm_one, norm_params, kernel_two, slot_count, out_side
    )
    two_sums = masked_moments(pixel_weight, main_two)
    second_sums = lax.psum(jnp.stack([*two_sums]), "dp")
    norm_two = settle(second_sums[0], second_sums[1], pixels)
    joined_pre = (
        (main_two - norm_two[0]) * norm_two[1] * norm_params[2]
        + norm_params[3]
        + (side_pre - norm_side[0]) * norm_side[1] * norm_params[4]
        + norm_params[5]
    )
    joined = jax.nn.silu(joined_pre).reshape(slot_count, pixel_count, -1)
    pooled = jnp.mean(joined, axis=1).astype(jnp.bfloat16)
    logits = jnp.dot(pooled, head_low, preferred_element_type=jnp.float32)
    largest = jnp.max(logits, axis=1, keepdims=True)
    exp_terms = jnp.exp(logits - largest)
    total_exp = jnp.sum(exp_terms, axis=1, keepdims=True)
    log_total = largest[:, 0] + jnp.log(total_exp[:, 0])
    onehot = (labels[:, None] == jnp.arange(logits.shape[1], dtype=jnp.int32)[None, :]).astype(
        jnp.float32
    )
    local_sum = jnp.sum(slot_weight * (log_total - jnp.sum(onehot * logits, axis=1)))
    grad_logits = ((exp_terms / total_exp - onehot) * (slot_weight / denominator)[:, None]).astype(
        jnp.bfloat16
    )
    grad_head = lax.dot_general(
        pooled, grad_logits, (((0,), (0,)), ((), ())), preferred_element_type=jnp.float32
    )
    grad_pooled = lax.dot_general(
        grad_logits, head_low, (((1,), (1,)), ((), ())), preferred_element_type=jnp.float32
    )
    spread_pooled = jnp.broadcast_to(
        (grad_pooled / pixel_count)[:, None, :], (slot_count, pixel_count, width)
    )
    grad_joined = spread_pooled.reshape(slot_count * pixel_count, width) * silu_slope(joined_pre)
    gain_two, shift_two, grad_two = norm_backward(grad_joined, main_two, norm_two, norm_params[2])
    gain_side, shift_side, grad_side = norm_backward(
        grad_joined, side_pre, norm_side, norm_params[4]
    )
    grad_two_maps = grad_two.reshape(slot_count, out_side, out_side, width)
    grad_side_maps = grad_side.reshape(slot_count, out_side, out_side, width)
    grad_conv_two = conv_weight_grad(active, grad_two_maps, 1, 1, 1)
    grad_short = conv_weight_grad(images, grad_side_maps, 2, 0, -1)
    kernel_turned = jnp.transpose(kernel_two[::-1, ::-1], (0, 1, 3, 2))
    grad_active = conv_apply(grad_two_maps, kernel_turned, 1, 1).reshape(
        slot_count * pixel_count, width
    )
    grad_hidden = grad_active * silu_slope(hidden_one)
    gain_one, shift_one, grad_one = norm_backward(grad_hidden, main_pre, norm_one, norm_params[0])
    grad_conv_one = conv_weight_grad(
        images, grad_one.reshape(slot_count, out_side, out_side, width), 2, 1, 0
    )
    grad_norms = jnp.stack([gain_one, shift_one, gain_two, shift_two, gain_side, shift_side])
    grads = (grad_conv_one, grad_conv_two, grad_short, grad_head, grad_norms)
    votes, rows_new, cols_new, moment_new = make_votes(
        grads, row_state[0], col_state[0], bn_moment[0]
    )
    workers = lax.axis_size("dp")
    weights = (conv_one, conv_two, shortcut, classifier, norm_params)
    scales = [scale_for(weight) for weight in weights]
    loss_sum = lax.psum(local_sum, "dp")
    flat_vote = jnp.concatenate([vote.reshape(-1) for vote in votes])
    flat_old = jnp.concatenate([weight.reshape(-1) for weight in weights])
    flat_scale = jnp.concatenate(
        [
            jnp.broadcast_to(scale, (weight.size,))
            for scale, weight in zip(scales, weights)
        ]
    )
    vote_mine = lax.psum_scatter(flat_vote, "dp", tiled=True)
    share = vote_mine.shape[0]
    start = lax.axis_index("dp") * share
    new_mine = lax.dynamic_slice_in_dim(
        flat_old, start, share
    ) - lax.dynamic_slice_in_dim(flat_scale, start, share) * jnp.tanh(
        vote_mine / math.sqrt(workers)
    )
    copies = lax.all_gather(new_mine.astype(jnp.bfloat16), "dp", tiled=True)
    return (
        loss_sum,
        valid_count,
        new_mine,
        copies,
        vote_mine,
        rows_new[None, :],
        cols_new[None, :],
        moment_new[None, :],
    )


def local(
    images,
    valid_slot,
    labels,
    conv_one,
    conv_two,
    shortcut,
    classifier,
    norm_params,
    row_state,
    col_state,
    bn_moment,
):
    new_mine, vote_mine, copies, rows_new, cols_new, moment_new, loss_sum, valid_count = run_step(
        images.reshape(-1, images.shape[-1]),
        conv_one,
        conv_two,
        shortcut,
        classifier.T,
        norm_params,
        valid_slot.reshape(1, -1),
        labels.reshape(1, -1),
        row_state,
        col_state,
        bn_moment,
    )
    copies, new_mine, vote_mine, rows_new, cols_new, moment_new, loss_sum, valid_count = finish(
        (copies, new_mine, vote_mine, rows_new, cols_new, moment_new, loss_sum, valid_count)
    )
    return (
        loss_sum.reshape(()),
        valid_count.reshape(()),
        new_mine.reshape(-1),
        copies.reshape(-1),
        vote_mine.reshape(-1),
        rows_new,
        cols_new,
        moment_new,
    )


def solution(mesh):
    placed = (
        P("dp", None, None, None),
        P("dp"),
        P("dp"),
        P(),
        P(),
        P(),
        P(),
        P(),
        P("dp", None),
        P("dp", None),
        P("dp", None),
    )
    return jax.shard_map(
        local if mesh.shape["dp"] == 32 else local_general,
        mesh=mesh,
        in_specs=placed,
        out_specs=(P(), P(), P("dp"), P(), P("dp"), P("dp", None), P("dp", None), P("dp", None)),
        check_vma=False,
    )
```

```python
import functools
import math

import jax
import jax.numpy as jnp
from jax import lax
from jax.experimental import pallas as pl
from jax.experimental.pallas import tpu as pltpu
from jax.sharding import PartitionSpec as P

STEP = 10
MESH = pl.DeviceIdType.MESH

EPS_NORM = 1e-05
EPS_ROW = 1e-30
EPS_SCALE = 0.001
FORWARD_DIMS = ("NHWC", "HWIO", "NHWC")
WEIGHT_DIMS = ("CHWN", "IHWO", "HWNC")
OWN = 224
TAIL = 16
PIECE = 32
SPAN = 4 * OWN
HALF = SPAN // 2
GROUP = 64


def conv_apply(maps, kernel, stride, margin):
    return lax.conv_general_dilated(
        maps,
        kernel,
        (stride, stride),
        ((margin, margin), (margin, margin)),
        dimension_numbers=FORWARD_DIMS,
        preferred_element_type=jnp.float32,
    )


def conv_weight_grad(maps, grad_out, stride, low_pad, high_pad):
    result = lax.conv_general_dilated(
        maps,
        grad_out,
        (1, 1),
        ((low_pad, high_pad), (low_pad, high_pad)),
        rhs_dilation=(stride, stride),
        dimension_numbers=WEIGHT_DIMS,
        preferred_element_type=jnp.float32,
    )
    return result.reshape(-1, result.shape[3])


def silu_slope(values):
    sigmoid_part = jax.nn.sigmoid(values)
    return sigmoid_part * (1.0 + values * (1.0 - sigmoid_part))


def settle(sum_plain, sum_square, pixels):
    mean_value = sum_plain / pixels
    return (mean_value, lax.rsqrt(sum_square / pixels - mean_value * mean_value + EPS_NORM))


def first_section(images, kernel_one, kernel_short):
    row_count = images.shape[0] * (images.shape[1] // 2) ** 2
    main_pre = conv_apply(images, kernel_one, 2, 1).reshape(row_count, -1)
    side_pre = conv_apply(images, kernel_short, 2, 0).reshape(row_count, -1)
    return (main_pre, side_pre)


def second_section(main_pre, norm_one, norm_params, kernel_two, slot_count, out_side):
    hidden_one = (main_pre - norm_one[0]) * norm_one[1] * norm_params[0] + norm_params[1]
    active = (
        jax.nn.silu(hidden_one).astype(jnp.bfloat16).reshape(slot_count, out_side, out_side, -1)
    )
    main_two = conv_apply(active, kernel_two, 1, 1).reshape(slot_count * out_side * out_side, -1)
    return (hidden_one, active, main_two)


def masked_moments(pixel_weight, values):
    return (jnp.sum(pixel_weight * values, axis=0), jnp.sum(pixel_weight * values * values, axis=0))


def soft_sign(step_raw):
    clip_by = jnp.maximum(1.0, jnp.sqrt(jnp.mean(step_raw * step_raw)))
    return jnp.tanh(step_raw / clip_by)


def make_votes(grads, rows_old, cols_old, moment_old):
    decay_rate = 1.0 - STEP ** (-0.8)
    votes, rows_new, cols_new = ([], [], [])
    row_at, col_at = (0, 0)
    for matrix in grads[:4]:
        row_size, col_size = matrix.shape
        square = matrix * matrix + EPS_ROW
        row_part = decay_rate * rows_old[row_at : row_at + row_size] + (
            1.0 - decay_rate
        ) * jnp.mean(square, axis=1)
        col_part = decay_rate * cols_old[col_at : col_at + col_size] + (
            1.0 - decay_rate
        ) * jnp.mean(square, axis=0)
        second = row_part[:, None] * col_part[None, :] / jnp.mean(row_part)
        votes.append(soft_sign(matrix * lax.rsqrt(second)))
        rows_new.append(row_part)
        cols_new.append(col_part)
        row_at += row_size
        col_at += col_size
    flat_norm = grads[4].reshape(-1)
    moment_new = decay_rate * moment_old + (1.0 - decay_rate) * (flat_norm * flat_norm + EPS_ROW)
    votes.append(soft_sign(flat_norm * lax.rsqrt(moment_new)))
    return (votes, jnp.concatenate(rows_new), jnp.concatenate(cols_new), moment_new)


def norm_backward(grad_out, pre_value, norm_pair, gain_row):
    normed = (pre_value - norm_pair[0]) * norm_pair[1]
    grad_gain = jnp.sum(grad_out * normed, axis=0)
    grad_shift = jnp.sum(grad_out, axis=0)
    grad_pre = (grad_out * gain_row * norm_pair[1]).astype(jnp.bfloat16)
    return (grad_gain, grad_shift, grad_pre)


SCHEDULE = (
    (),
    (
        (1, 0),
    ),
    (
        (0, 2), (1, 1),
    ),
    (
        (0, 3), (1, 2), (2, 0), (0, 4), (1, 3), (2, 1),
    ),
    (
        (0, 5), (1, 4), (2, 2), (3, 0),
    ),
    (
        (0, 6), (1, 5), (2, 3), (3, 1),
    ),
    (
        (0, 7), (1, 6), (2, 4), (3, 2), (4, 0),
    ),
    (),
    (
        (0, 8), (1, 7), (2, 5), (3, 3), (4, 1),
    ),
    (),
    (
        (1, 8), (2, 6), (3, 4), (4, 2), (1, 9), (2, 7), (3, 5), (4, 3), (5, 0), (0, 11), (1, 10),
        (2, 8), (3, 6), (4, 4), (5, 1), (0, 12), (1, 11), (2, 9), (3, 7), (4, 5), (5, 2), (6, 0),
        (0, 13), (1, 12), (2, 10), (3, 8), (4, 6), (5, 3), (6, 1), (1, 13), (2, 11), (3, 9),
        (4, 7), (8, 0), (5, 4), (6, 2), (2, 12), (3, 10), (4, 8), (5, 5), (6, 3), (7, 0),
        (2, 13), (3, 11), (4, 9), (5, 6), (6, 4), (7, 1), (3, 12), (4, 10), (5, 7), (6, 5),
        (7, 2), (3, 13), (4, 11), (5, 8), (6, 6), (7, 3), (4, 12), (5, 9), (6, 7), (7, 4),
        (4, 13), (5, 10), (6, 8), (7, 5), (5, 11), (6, 9), (7, 6), (5, 12), (6, 10), (7, 7),
        (5, 13), (6, 11), (7, 8), (6, 12), (7, 9), (6, 13), (9, 0), (7, 10), (7, 11), (7, 12),
        (7, 13),
    ),
)


def place():
    me = lax.axis_index("dp")
    core = lax.rem(me, 2)
    x = lax.rem(lax.div(me, 2), 2)
    y = lax.rem(lax.div(me, 4), 2)
    z = lax.div(me, 8)
    return me, core, x, y, z


def send(src, dst, send_sem, recv_sem, partner):
    copy = pltpu.make_async_remote_copy(
        src_ref=src,
        dst_ref=dst,
        send_sem=send_sem,
        recv_sem=recv_sem,
        device_id=(partner,),
        device_id_type=MESH,
    )
    copy.start()
    return copy


def scale_of(row, scales, edges):
    picked = scales[2]
    picked = jnp.where(row < edges[1], scales[1], picked)
    return jnp.where(row < edges[0], scales[0], picked)


def make_units(edges):
    one, two, short = edges[0] // 16, edges[1] // 16, edges[2] // 16
    units = []
    for k in range((two - one) // 32):
        units.append((one + 32 * k, 1, k % 2 == 0, 16, (1, 1)))
    for k in range(one // 32):
        units.append((32 * k, 1, k % 2 == 1, 16, (0, 0)))
    at = one // 32 * 32
    assert one - at == 16 and short - two == 16
    units.append((at, 1, False, two - at, (0, 2)))
    return units


def settle_rows(sums, pixels, gain, shift):
    mean = sums[0] / pixels
    inv = lax.rsqrt(sums[1] / pixels - mean * mean + EPS_NORM)
    slope = gain * inv
    return mean, inv, slope, shift - mean * slope


def gate(values):
    return 0.5 * jnp.tanh(0.5 * values) + 0.5


def eye_mask(rows, columns, offset=0):
    down = lax.broadcasted_iota(jnp.int32, (rows, columns), 0) + offset
    return down == lax.broadcasted_iota(jnp.int32, (rows, columns), 1)


def column_of(row, size):
    spread = jnp.where(eye_mask(size, size), jnp.broadcast_to(row, (size, size)), 0)
    return jnp.sum(spread, axis=1, keepdims=True)


def total_of(values):
    return jnp.sum(jnp.sum(values, axis=0, keepdims=True), axis=1, keepdims=True)


def fold(values):
    return jnp.sum(values.reshape(values.shape[0] // 8, 8, values.shape[1]), axis=0)


def cast_weight(source, target, square_ref, taps, depth, fetches):
    step = 128
    for tap in taps:
        chunk = source.shape[0] // depth // len(fetches)
        if tap % chunk == 0:
            fetches[tap // chunk].wait()
        new_tap = (tap % 3) * 3 + tap // 3

        @pl.loop(0, depth // step)
        def _(k):
            start = pl.multiple_of(k * step, step)
            values = source[pl.ds(tap * depth + start, step), :]
            target[new_tap, pl.ds(start, step), :] = values.astype(jnp.bfloat16)
            square_ref[...] += fold(values * values)


def factored_votes(grad, rows, row_at, rows_old, rows_new, col_old, level, votes, vote_at, between, after):
    width = grad.shape[1]
    keep = 1.0 - STEP ** (-0.8)
    step = 128
    quarters = width // 128

    def first(k, carry):
        col_sum, row_sum = carry
        start = pl.multiple_of(k * step, step)
        lanes = pl.ds(pl.multiple_of(row_at + start, step), step)
        old = rows_old[:, lanes] * keep
        line = jnp.zeros((8, 128), jnp.float32)
        for m in range(step // 8):
            block = grad[pl.ds(start + 8 * m, 8), :]
            square = block * block
            col_sum = col_sum + square
            part = square[:, :128]
            for q in range(1, quarters):
                part = part + square[:, 128 * q : 128 * (q + 1)]
            part = part * ((1.0 - keep) / width)
            diagonal = eye_mask(8, 128, 8 * m)
            part = part + jnp.where(diagonal, jnp.broadcast_to(old, (8, 128)), 0.0)
            row = jnp.sum(part, axis=1, keepdims=True) + (1.0 - keep) * EPS_ROW
            row = jnp.broadcast_to(row, (8, 128))
            level[pl.ds(start + 8 * m, 8), :] = row
            row_sum = row_sum + row
            line = line + jnp.where(diagonal, row, 0.0)
        rows_new[:, lanes] = jnp.sum(line, axis=0, keepdims=True)
        return col_sum, row_sum

    col_sum, row_sum = lax.fori_loop(
        0,
        rows // step,
        first,
        (jnp.zeros((8, width), jnp.float32), jnp.zeros((8, 128), jnp.float32)),
    )
    col_new = keep * col_old + (1.0 - keep) * (
        jnp.sum(col_sum, axis=0, keepdims=True) / rows + EPS_ROW
    )
    scale = lax.rsqrt(col_new)
    root_mean = jnp.sqrt(jnp.sum(row_sum, axis=0, keepdims=True) / rows)

    def second(k, carry):
        start = pl.multiple_of(k * step, step)
        for m in range(step // 8):
            here = pl.ds(start + 8 * m, 8)
            factor = lax.rsqrt(level[here, :]) * root_mean
            level[here, :] = factor
            raw = grad[here, :] * scale
            power = raw * raw
            part = power[:, :128]
            for q in range(1, quarters):
                part = part + power[:, 128 * q : 128 * (q + 1)]
            carry = carry + part * (factor * factor)
        return carry

    between[0]()
    power = lax.fori_loop(0, rows // step, second, jnp.zeros((8, 128), jnp.float32))
    between[1]()
    clip = jnp.maximum(1.0, jnp.sqrt(total_of(power) / (rows * width)))
    scale = scale / clip

    def third(k, _):
        start = pl.multiple_of(k * step, step)
        for m in range(step // 16):
            here = pl.ds(start + 16 * m, 16)
            factor = level[here, :]
            factor = jnp.concatenate([factor] * quarters, axis=1)
            vote = jnp.tanh(grad[here, :] * factor * scale).astype(jnp.bfloat16)
            at = pl.multiple_of((vote_at + start) * 4 + GROUP * m, GROUP)
            for q in range(quarters):
                votes[pl.ds(at + 16 * q, 16), :] = vote[:, 128 * q : 128 * (q + 1)]
        return 0

    part = 512 // step
    for k in range(0, rows // step, part):
        lax.fori_loop(k, min(k + part, rows // step), third, 0)
        after(k // part)
    return col_new


def step_kernel(
    edges,
    units,
    root,
    images,
    one_hbm,
    two_hbm,
    short_hbm,
    head_ref,
    norm_ref,
    valid_ref,
    label_ref,
    row_ref,
    col_ref,
    moment_ref,
    new_ref,
    vote_ref,
    out_ref,
    row_new,
    col_new,
    moment_new,
    loss_ref,
    count_ref,
    xs,
    grad_one,
    grad_two,
    grad_short,
    low_one,
    low_two,
    low_short,
    main_pre,
    side_pre,
    main_two,
    active,
    back_two,
    back_one,
    back_side,
    active_t,
    xs_t,
    head_pad,
    level,
    square,
    post_one,
    plane_one,
    line_one,
    post_two,
    plane_two,
    line_two,
    tail_post,
    tail_plane,
    tail_line,
    core_in,
    wide_in,
    deep_in,
    line_in,
    sum_low,
    landed,
    total,
    own_weight,
    weight,
    vote_flat,
    new_flat,
    fetch_sem,
    small_send,
    small_recv,
    rs_send,
    rs_recv,
    line_send,
    line_recv,
    pass_send,
    land_recv,
    spread_send,
    spread_recv,
    ag_send,
    ag_recv,
    free_sem,
    load_sem,
):
    slots, in_width = xs.shape[4:]
    width = main_pre.shape[1]
    side = 4
    band = side * slots
    pixel_count = side * side
    classes = head_ref.shape[0]
    keep = 1.0 - STEP ** (-0.8)
    low = jnp.bfloat16
    f32 = jnp.float32

    me, core, x, y, z = place()
    flip_core = me + 1 - 2 * core
    flip_x = me + 2 - 4 * x
    flip_y = me + 4 - 8 * y
    spot = lax.rem(me, 8)
    near = [z * 8 + lax.rem(spot + k, 8) for k in range(1, 8)]
    far = [lax.rem(z + k, 4) * 8 + spot for k in range(1, 4)]
    others = [lax.rem(me + k, 32) for k in range(1, 32)]

    count = images.shape[0]
    loads = []
    for half in range(2):
        lanes = slice(128 * half, 128 * (half + 1))
        loads.append(
            pltpu.make_async_copy(
                images.at[:, lanes], core_in.at[pl.ds(half * count, count)], load_sem.at[half]
            )
        )
        loads[half].start()

    def chunks_of(source, target, first, count):
        rows = source.shape[0] // count
        return [
            pltpu.make_async_copy(
                source.at[pl.ds(k * rows, rows)],
                target.at[pl.ds(k * rows, rows)],
                fetch_sem.at[first + k],
            )
            for k in range(count)
        ]

    fetch_one = chunks_of(one_hbm, grad_one, 0, 3)
    fetch_short = chunks_of(short_hbm, grad_short, 3, 1)
    fetch_two = chunks_of(two_hbm, grad_two, 4, 3)
    for fetch in fetch_one + fetch_short:
        fetch.start()
    barrier = pltpu.get_barrier_semaphore()
    for partner in others:
        pl.semaphore_signal(barrier, inc=1, device_id=(partner,), device_id_type=MESH)

    def fetch_rows(row, count, place_at, sem):
        parts = (
            (one_hbm, 0, edges[0]),
            (two_hbm, edges[0], edges[1]),
            (short_hbm, edges[1], edges[2]),
        )
        for ref, first, last in parts:

            @pl.when(jnp.logical_and(row >= first, row < last))
            def _():
                start = pl.multiple_of(row - first, count)
                pltpu.make_async_copy(
                    ref.at[pl.ds(start, count)], weight.at[pl.ds(place_at, count)], sem
                ).start()

    first_row = me * OWN

    for half in range(2):
        lanes = slice(128 * half, 128 * (half + 1))
        loads[half].wait()
        level[:count, :] = core_in[pl.ds(half * count, count), :].astype(f32)
        for h in range(2 * side):
            for w in range(2 * side):
                rows = level[pl.ds(2 * side * h + w, slots, stride=4 * pixel_count), :]
                xs[w % 2, w // 2, h % 2, h // 2, :, lanes] = rows.astype(low)

    scales = {}

    def scale_from(weight_square, size):
        return jnp.maximum(EPS_SCALE, jnp.sqrt(total_of(weight_square) / size))

    exchanges = (
        (post_one, plane_one, line_one),
        (post_two, plane_two, line_two),
        (tail_post, tail_plane, tail_line),
    )

    def exchange_start(which, values):
        mine_ref, plane_ref, _ = exchanges[which]
        mine_ref[...] = values
        plane_ref[spot] = values
        return [
            send(
                mine_ref,
                plane_ref.at[spot],
                small_send.at[which, k],
                small_recv.at[which, k],
                partner,
            )
            for k, partner in enumerate(near)
        ]

    def pack_rows(rows):
        pieces = [row[:, 128 * q : 128 * (q + 1)] for row in rows for q in range(4)]
        pad = -len(pieces) % 8
        if pad:
            pieces.append(jnp.zeros((pad, 128), f32))
        return jnp.concatenate(pieces, axis=0)

    def unpack_row(lines_in, k):
        return jnp.concatenate([lines_in[4 * k + q : 4 * k + q + 1] for q in range(4)], axis=1)

    def exchange_middle(which, copies):
        _, plane_ref, line_ref = exchanges[which]
        for copy in copies:
            copy.wait()
        line_ref[z] = functools.reduce(lambda a, b: a + b, [plane_ref[k] for k in range(8)])
        return [
            send(
                line_ref.at[z],
                line_ref.at[z],
                small_send.at[which, 7 + k],
                small_recv.at[which, 7 + k],
                partner,
            )
            for k, partner in enumerate(far)
        ]

    def exchange_end(which, copies):
        line_ref = exchanges[which][2]
        for copy in copies:
            copy.wait()
        return (line_ref[0] + line_ref[1]) + (line_ref[2] + line_ref[3])

    def lines(start, count):
        return pl.ds(pl.multiple_of(start, 16), count)

    sizes = [GROUP * unit[1] for unit in units]
    starts = [sum(sizes[:k]) for k in range(len(units) + 1)]

    def part_of(ref, u, share, start, count):
        return ref.at[lines(share * starts[u] + start, count)]

    def places(u):
        if units[u][2]:
            return x, y, flip_x, flip_y
        return y, x, flip_y, flip_x

    def unit_start(u, cc):
        return GROUP * units[u][0] + cc * (GROUP * units[u][3])

    def own_group(u):
        first, second, _, _ = places(u)
        return units[u][0] + core * units[u][3] + (first * 8 + second * 4 + z) * units[u][1]

    def halve(source, target, u, stage, partner):
        return send(source, target, rs_send.at[u, stage], rs_recv.at[u, stage], partner)

    def scatter_start(u):
        size = 16 * sizes[u]
        return halve(
            out_ref.at[lines(unit_start(u, 1 - core), size)],
            part_of(core_in, u, 16, 0, size),
            u,
            0,
            flip_core,
        )

    def add_to(ref, u, share, source_ref, source_start):
        size = share * sizes[u]
        here = lines(share * starts[u], size)
        ref[here, :] = ref[here, :] + source_ref[lines(source_start, size), :]

    def scatter_one(u, copy):
        copy.wait()
        add_to(core_in, u, 16, out_ref, unit_start(u, core))
        pl.semaphore_signal(
            free_sem.at[u], inc=1, device_id=(flip_core,), device_id_type=MESH
        )
        first, _, flip_first, _ = places(u)
        size = 8 * sizes[u]
        return halve(
            part_of(core_in, u, 16, (1 - first) * size, size),
            part_of(wide_in, u, 8, 0, size),
            u,
            1,
            flip_first,
        )

    def scatter_two(u, copy):
        copy.wait()
        first, second, _, flip_second = places(u)
        add_to(wide_in, u, 8, core_in, 16 * starts[u] + first * 8 * sizes[u])
        size = 4 * sizes[u]
        return halve(
            part_of(wide_in, u, 8, (1 - second) * size, size),
            part_of(deep_in, u, 4, 0, size),
            u,
            2,
            flip_second,
        )

    def line_copy(u, k):
        plane_to = lax.rem(z + k, 4)
        return pltpu.make_async_remote_copy(
            src_ref=part_of(deep_in, u, 4, plane_to * sizes[u], sizes[u]),
            dst_ref=part_of(line_in, u, 4, z * sizes[u], sizes[u]),
            send_sem=line_send.at[u, k],
            recv_sem=line_recv.at[u, k],
            device_id=(plane_to * 8 + spot,),
            device_id_type=MESH,
        )

    def scatter_three(u, copy):
        copy.wait()
        _, second, _, _ = places(u)
        add_to(deep_in, u, 4, wide_in, 8 * starts[u] + second * 4 * sizes[u])
        for k in (3, 2, 1):
            line_copy(u, k).start()
        here = lines(4 * starts[u] + z * sizes[u], sizes[u])
        line_in[here, :] = deep_in[here, :]

    groups = (edges[2] + TAIL) // 16
    spare = (groups - 1) // 32
    passes = []

    def land(local, group, to, slot, index):
        source = sum_low.at[lines(local * GROUP, GROUP)]
        target = landed.at[lines(slot * GROUP, GROUP)]
        copy = pltpu.make_async_remote_copy(
            src_ref=source,
            dst_ref=target,
            send_sem=pass_send.at[index],
            recv_sem=land_recv.at[slot],
            device_id=(to,),
            device_id_type=MESH,
        )
        return copy, source, target

    def pass_on(u):
        for m in range(units[u][1]):
            local = starts[u] // GROUP + m
            group = own_group(u) + m
            to, slot = lax.div(group, spare), lax.rem(group, spare)
            for halo in range(2):
                index = 2 * local + halo
                if halo:
                    receiver, at = lax.rem(to + 31, 32), spare
                    wanted = jnp.logical_and(slot == 0, group > 0)
                else:
                    receiver, at, wanted = to, slot, group >= 0
                away = jnp.logical_and(wanted, receiver != me)
                here = jnp.logical_and(wanted, receiver == me)
                copy, source, target = land(local, group, receiver, at, index)

                @pl.when(away)
                def _():
                    copy.start()

                @pl.when(here)
                def _():
                    target[...] = source[...]

                passes.append((away, copy))

    def flat_rows(row, q, values, ref):
        ref[pl.ds(row * 4 + q, 8, stride=4), :] = values

    def old_rows(u, cc):
        matrix = units[u][4][cc]
        base = edges[matrix - 1] if matrix else 0
        return (one_hbm, two_hbm, short_hbm)[matrix], 16 * own_group(u) - base, 16 * units[u][1]

    def own_fetch(u):
        target = own_weight.at[pl.ds(starts[u] // 4, 16 * units[u][1])]
        matrices = units[u][4]
        for cc in range(2):
            if cc and matrices[0] == matrices[1]:
                continue

            @pl.when((core == cc) if matrices[0] != matrices[1] else (core >= 0))
            def _():
                ref, row, count = old_rows(u, cc)
                pltpu.make_async_copy(
                    ref.at[pl.ds(pl.multiple_of(row, 16), count)], target, fetch_sem.at[9 + u]
                ).start()

    def spread_copy(u, k):
        own = out_ref.at[lines(own_group(u) * GROUP, sizes[u])]
        return pltpu.make_async_remote_copy(
            src_ref=own,
            dst_ref=own,
            send_sem=spread_send.at[u, k],
            recv_sem=spread_recv.at[u, k],
            device_id=(far[k - 1],),
            device_id_type=MESH,
        )

    def own_block(u):
        size = sizes[u]
        for k in range(1, 4):
            line_copy(u, k).wait_recv()
        here = pl.ds(starts[u], size)
        low_sum = functools.reduce(
            lambda a, b: a + b,
            [line_in[pl.ds(4 * starts[u] + t * size, size), :].astype(f32) for t in range(4)],
        ).astype(low)
        sum_low[here, :] = low_sum
        total[here, :] = low_sum.astype(f32)
        target = own_weight.at[pl.ds(starts[u] // 4, 16 * units[u][1])]
        pltpu.make_async_copy(target, target, fetch_sem.at[9 + u]).wait()
        matrices = units[u][4]
        scale = jnp.where(core == 0, scales[matrices[0]], scales[matrices[1]])
        for m in range(units[u][1]):
            row = starts[u] // 4 + 16 * m
            for part in (0, 8):
                for q in range(4):
                    summed = total[pl.ds(row * 4 + 16 * q + part, 8), :]
                    old = own_weight[pl.ds(row + part, 8), 128 * q : 128 * (q + 1)]
                    fresh = old - scale * jnp.tanh(summed * root)
                    flat_rows(row + part, q, fresh, new_flat)
        out_ref[lines(own_group(u) * GROUP, size), :] = new_flat[here, :].astype(low)
        for k in (3, 2, 1):
            spread_copy(u, k).start()
        pass_on(u)

    def piece(rows, u, stage, partner):
        return send(
            out_ref.at[rows], out_ref.at[rows], ag_send.at[u, stage], ag_recv.at[u, stage], partner
        )

    def gather_one(u):
        for k in range(1, 4):
            spread_copy(u, k).wait_recv()
        first, second, _, flip_second = places(u)
        size = 4 * sizes[u]
        start = unit_start(u, core) + (2 * first + second) * size
        return piece(lines(start, size), u, 0, flip_second)

    def gather_two(u, copy):
        copy.wait()
        first, _, flip_first, _ = places(u)
        size = 8 * sizes[u]
        return piece(lines(unit_start(u, core) + first * size, size), u, 1, flip_first)

    def gather_three(u, copy):
        copy.wait()
        pl.semaphore_wait(free_sem.at[u], 1)
        return piece(lines(unit_start(u, core), 16 * sizes[u]), u, 2, flip_core)

    def renew(row, at_row):
        scale = scale_of(at_row, [scales[k] for k in range(3)], edges)
        for part in (0, 8):
            for q in range(4):
                summed = total[pl.ds(row * 4 + 16 * q + part, 8), :]
                old = weight[pl.ds(row + part, 8), 128 * q : 128 * (q + 1)]
                fresh = old - scale * jnp.tanh(summed * root)
                flat_rows(row + part, q, summed, vote_flat)
                flat_rows(row + part, q, fresh, new_flat)

    valid_column = column_of(valid_ref[...].astype(f32), slots)
    weight_slot = jnp.broadcast_to(valid_column, (slots, width))
    weight_pair = jnp.concatenate([weight_slot] * 2, axis=0)

    square[...] = jnp.zeros_like(square)
    cast_weight(grad_one, low_one, square, range(9), in_width, fetch_one)
    scales[0] = scale_from(square[...], grad_one.size)
    square[...] = jnp.zeros_like(square)
    cast_weight(grad_short, low_short, square, range(1), in_width, fetch_short)
    scales[2] = scale_from(square[...], grad_short.size)
    for fetch in fetch_two:
        fetch.start()
    for k in range(OWN // PIECE):
        fetch_rows(first_row + k * PIECE, PIECE, k * PIECE, fetch_sem.at[7])
    fetch_rows(first_row + OWN, TAIL, OWN, fetch_sem.at[8])
    for u in range(len(units)):
        own_fetch(u)

    pair = 2 * slots

    def image_taps(j, i):
        pieces = []
        for b in range(3):
            column = j if b else j - 1
            if column < 0:
                continue
            across = 0 if b == 1 else 1
            for a in range(3):
                if a == 1:
                    piece = xs[across, column, 0, i : i + 2].reshape(pair, in_width)
                elif a == 2:
                    piece = xs[across, column, 1, i : i + 2].reshape(pair, in_width)
                elif i:
                    piece = xs[across, column, 1, i - 1 : i + 1].reshape(pair, in_width)
                else:
                    piece = jnp.concatenate(
                        [jnp.zeros((slots, in_width), low), xs[across, column, 1, 0]], axis=0
                    )
                pieces.append(piece)
        return jnp.concatenate(pieces, axis=1)

    def moments(values):
        weighted = values * weight_pair
        return (
            jnp.sum(weighted, axis=0, keepdims=True),
            jnp.sum(weighted * values, axis=0, keepdims=True),
        )

    def add_up(old, new):
        return [a + b for a, b in zip(old, new)]

    none = jnp.zeros((1, width), f32)
    main_sums, side_sums = [none, none], [none, none]
    for j in range(side):
        low_rows = low_one[3 if j == 0 else 0 :].reshape(-1, width)
        for i in range(0, side, 2):
            here = pl.ds(j * band + i * slots, pair)
            value = jnp.dot(image_taps(j, i), low_rows, preferred_element_type=f32)
            main_pre[here, :] = value
            main_sums = add_up(main_sums, moments(value))
            value = jnp.dot(
                xs[0, j, 0, i : i + 2].reshape(pair, in_width),
                low_short[0],
                preferred_element_type=f32,
            )
            side_pre[here, :] = value
            side_sums = add_up(side_sums, moments(value))

    count = jnp.broadcast_to(jnp.sum(valid_column, axis=0, keepdims=True), (1, width))
    pl.semaphore_wait(barrier, len(others))
    copies = exchange_start(
        0, pack_rows(main_sums + side_sums + [count])
    )
    square[...] = jnp.zeros_like(square)
    cast_weight(grad_two, low_two, square, range(5), width, fetch_two)
    copies = exchange_middle(0, copies)
    cast_weight(grad_two, low_two, square, range(5, 9), width, fetch_two)
    scales[1] = scale_from(square[...], grad_two.size)
    border = jnp.zeros((side, 1, slots, width), low)
    active[:, 0:1] = border
    active[:, side + 1 :] = border
    back_two[:, 0:1] = border
    back_two[:, side + 1 :] = border
    back_one[:, side:] = border
    head_pad[...] = jnp.zeros_like(head_pad)
    head_pad[:classes, :] = head_ref[...]
    head = head_pad[:16, :]
    scales[3] = scale_from(head * head, head_ref.size)
    params = norm_ref[...]
    scales[4] = scale_from(params * params, norm_ref.size)
    sums = exchange_end(0, copies)
    sums = [unpack_row(sums, k) for k in range(5)]

    valid_count = sums[4]
    count_ref[...] = valid_count[:, :1]
    denominator = jnp.maximum(valid_count, 1.0)
    pixels = denominator * pixel_count
    gains = [norm_ref[k : k + 1, :] for k in range(6)]
    mean_one, inv_one, slope_one, base_one = settle_rows(
        (sums[0], sums[1]), pixels, gains[0], gains[1]
    )
    mean_side, inv_side, slope_side, base_side = settle_rows(
        (sums[2], sums[3]), pixels, gains[4], gains[5]
    )

    for j in range(side):
        hidden = main_pre[pl.ds(j * band, band), :] * slope_one + base_one
        active[j, 1 : side + 1] = (
            (hidden * gate(hidden)).astype(low).reshape(side, slots, width)
        )
    two_sums = [none, none]
    for j in range(side):
        taps = [b for b in range(3) if 0 <= j + b - 1 < side]
        low_rows = low_two[3 * taps[0] : 3 * taps[-1] + 3].reshape(-1, width)
        for i in range(0, side, 2):
            pieces = [
                active[j + b - 1, a + i : a + i + 2].reshape(pair, width)
                for b in taps
                for a in range(3)
            ]
            value = jnp.dot(jnp.concatenate(pieces, axis=1), low_rows, preferred_element_type=f32)
            main_two[pl.ds(j * band + i * slots, pair), :] = value
            two_sums = add_up(two_sums, moments(value))
    copies = exchange_start(1, pack_rows(two_sums))
    for j in range(side):
        block = active[j, 1 : side + 1].reshape(band, width)
        active_t[:, j * band : (j + 1) * band] = block.T
    label_column = column_of(label_ref[...].astype(f32), slots).astype(jnp.int32)
    head_low = head_pad[...].astype(low)
    copies = exchange_middle(1, copies)
    for across in range(2):
        for down in range(2):
            for j in range(side):
                block = xs[across, j, down].reshape(band, in_width)
                xs_t[across, down, :, j * band : (j + 1) * band] = block.T
    sums = exchange_end(1, copies)
    sums = [unpack_row(sums, k) for k in range(2)]
    mean_two, inv_two, slope_two, base_two = settle_rows(
        (sums[0], sums[1]), pixels, gains[2], gains[3]
    )

    base_joined = base_two + base_side

    quarters = [slice(128 * q, 128 * (q + 1)) for q in range(width // 128)]

    def joined_of(here, lanes):
        return (
            main_two[here, lanes] * slope_two[:, lanes]
            + side_pre[here, lanes] * slope_side[:, lanes]
            + base_joined[:, lanes]
        )

    pooled = []
    for lanes in quarters:
        total_joined = jnp.zeros((slots, 128), f32)
        for p in range(pixel_count):
            joined = joined_of(pl.ds(p * slots, slots), lanes)
            total_joined = total_joined + joined * gate(joined)
        pooled.append(total_joined)
    pooled = jnp.concatenate(pooled, axis=1)
    pooled = (pooled / pixel_count).astype(low)
    logits = lax.dot_general(
        pooled, head_low, (((1,), (1,)), ((), ())), preferred_element_type=f32
    )
    lane = lax.broadcasted_iota(jnp.int32, logits.shape, 1)
    real = lane < classes
    largest = jnp.max(jnp.where(real, logits, -jnp.inf), axis=1, keepdims=True)
    powers = jnp.where(real, jnp.exp(jnp.where(real, logits - largest, 0.0)), 0.0)
    total_power = jnp.sum(powers, axis=1, keepdims=True)
    onehot = jnp.where(lane == label_column, 1.0, 0.0)
    entropy = largest + jnp.log(total_power) - jnp.sum(onehot * logits, axis=1, keepdims=True)
    loss = jnp.sum(entropy * valid_column, axis=0, keepdims=True)
    grad_logits = (
        (powers / total_power - onehot) * (valid_column / denominator[:, :1])
    ).astype(low)
    grad_head = lax.dot_general(
        grad_logits, pooled, (((0,), (0,)), ((), ())), preferred_element_type=f32
    )[:16]
    grad_pooled = jnp.dot(grad_logits, head_low, preferred_element_type=f32) / pixel_count

    join_sums = []
    for lanes in quarters:
        three = [jnp.zeros((8, 128), f32)] * 3
        for p in range(pixel_count):
            here = pl.ds(p * slots, slots)
            joined = joined_of(here, lanes)
            opened = gate(joined)
            grad = grad_pooled[:, lanes] * (opened * (1.0 + joined * (1.0 - opened)))
            normed_two = (main_two[here, lanes] - mean_two[:, lanes]) * inv_two[:, lanes]
            normed_side = (side_pre[here, lanes] - mean_side[:, lanes]) * inv_side[:, lanes]
            new = (grad * normed_two, grad * normed_side, grad)
            three = [old + fold(each) for old, each in zip(three, new)]
            back_two[p // side, 1 + p % side, :, lanes] = (grad * slope_two[:, lanes]).astype(low)
            back_side[here, lanes] = (grad * slope_side[:, lanes]).astype(low)
        join_sums.append([jnp.sum(each, axis=0, keepdims=True) for each in three])
    gain_two, gain_side, shift_two = [jnp.concatenate(each, axis=1) for each in zip(*join_sums)]

    def turned_product(left_ref, columns, right, target, at):
        for m in range(0, left_ref.shape[0], 128):
            target[pl.ds(at + m, 128), :] = jnp.dot(
                left_ref[m : m + 128, columns], right, preferred_element_type=f32
            )

    for b in range(3):
        first, last = max(0, b - 1), min(side, side + b - 1)
        for a in range(3):
            right = back_two[first - b + 1 : last - b + 1, 2 - a : 2 - a + side]
            turned_product(
                active_t,
                slice(first * band, last * band),
                right.reshape(-1, width),
                grad_two,
                (a * 3 + b) * width,
            )

    def nothing():
        pass

    def matrix_votes(k, grad, between, after):
        here = pl.ds(k * width, width)
        start = edges[k - 1] if k else 0
        col_new[:, here] = factored_votes(
            grad,
            grad.shape[0],
            start,
            row_ref,
            row_new,
            col_ref[:, here],
            level,
            out_ref,
            start,
            between,
            after,
        )

    kept = {}

    def tail_step():
        sums = exchange_end(2, kept["tail"])
        loss_ref[...] = sums[4 * TAIL : 4 * TAIL + 1, :1]
        old = jnp.concatenate([head_ref[...], norm_ref[...]], axis=0)
        is_head = lax.broadcasted_iota(jnp.int32, (TAIL, width), 0) < classes
        scale = jnp.where(is_head, scales[3], scales[4])
        sums = jnp.concatenate([sums[TAIL * q : TAIL * (q + 1)] for q in range(4)], axis=1)
        fresh = old - scale * jnp.tanh(sums * root)
        both = jnp.concatenate([sums, fresh], axis=0)
        high = both.astype(low)
        rest = both - high.astype(f32)
        middle = rest.astype(low)
        parts = jnp.concatenate([high, middle, (rest - middle.astype(f32)).astype(low)], axis=0)

        flat_sums, flat_new = [], []
        window = 256
        for q in range(classes):
            start = min(q * width // classes // 128 * 128, width - window)
            down = lax.broadcasted_iota(jnp.int32, (window, width), 0)
            across = lax.broadcasted_iota(jnp.int32, (window, width), 1)
            gap = across - classes * down + (q * width - classes * start)
            chosen = jnp.where(jnp.logical_and(gap >= 0, gap < classes), 1.0, 0.0).astype(low)
            moved = jnp.dot(parts[:, start : start + window], chosen, preferred_element_type=f32)
            moved = moved[: 2 * TAIL] + moved[2 * TAIL : 4 * TAIL] + moved[4 * TAIL :]
            spot_of = lax.broadcasted_iota(jnp.int32, (TAIL, width), 1).astype(f32) + q * width
            class_of = spot_of - classes * jnp.floor((spot_of + 0.5) / classes)
            here = lax.broadcasted_iota(jnp.int32, (TAIL, width), 0).astype(f32) == class_of
            flat_sums.append(jnp.sum(jnp.where(here, moved[:TAIL], 0.0), axis=0, keepdims=True))
            flat_new.append(jnp.sum(jnp.where(here, moved[TAIL:], 0.0), axis=0, keepdims=True))
        kept["sums"] = jnp.concatenate(flat_sums + [sums[classes:]], axis=0)
        kept["new"] = jnp.concatenate(flat_new + [fresh[classes:]], axis=0)

    def return_step():
        mine = [own_group(u) for u in range(len(units))]
        for slot in range(spare + 1):
            group = me * spare + slot
            own = group < 0
            for u, unit in enumerate(units):
                inside = jnp.logical_and(group >= mine[u], group < mine[u] + unit[1])
                own = jnp.logical_or(own, inside)

            @pl.when(jnp.logical_and(jnp.logical_not(own), group < groups - 1))
            def _():
                land(0, group, me, slot, 0)[0].wait_recv()

        pltpu.make_async_copy(
            weight.at[pl.ds(0, OWN)], weight.at[pl.ds(0, OWN)], fetch_sem.at[7]
        ).wait()
        total[pl.ds(0, SPAN), :] = landed[pl.ds(0, SPAN), :].astype(f32)

        @pl.loop(0, OWN // 16)
        def _(k):
            row = pl.multiple_of(k * 16, 16)
            renew(row, first_row + row)

        @pl.when(me < 31)
        def _():
            pltpu.make_async_copy(
                weight.at[pl.ds(OWN, TAIL)], weight.at[pl.ds(OWN, TAIL)], fetch_sem.at[8]
            ).wait()
            total[pl.ds(SPAN, GROUP), :] = landed[pl.ds(SPAN, GROUP), :].astype(f32)
            renew(OWN, first_row + OWN)

        def tail_rows(values, ref):
            for u in (0, 8):
                for q in range(4):
                    flat_rows(OWN + u, q, values[u : u + 8, 128 * q : 128 * (q + 1)], ref)

        @pl.when(me == 31)
        def _():
            tail_rows(kept["sums"], vote_flat)
            tail_rows(kept["new"], new_flat)

        shift = 2 * me
        share = vote_ref.shape[0]
        vote_ref[...] = vote_flat[pl.ds(shift, share), :]
        new_ref[...] = new_flat[pl.ds(shift, share), :]
        tail_rows(kept["new"], new_flat)
        out_ref[pl.ds(32 * SPAN, GROUP), :] = new_flat[pl.ds(SPAN, GROUP), :].astype(low)

    in_flight = {}
    steps = (
        lambda u, copy: scatter_start(u),
        scatter_one,
        scatter_two,
        scatter_three,
        lambda u, copy: own_block(u),
        lambda u, copy: gather_one(u),
        gather_two,
        gather_three,
        lambda u, copy: tail_step(),
        lambda u, copy: return_step(),
    )

    def go(number, u):
        got = steps[number](u, in_flight.get(u))
        if number < 8:
            in_flight[u] = got

    def turn(number):
        for step_number, u in SCHEDULE[number]:
            go(step_number, u)

    early = edges[1] // 512 - edges[0] // 512
    matrix_votes(1, grad_two, (nothing, nothing), lambda k: go(0, k) if k < 2 else None)
    turn(0)
    grad_short[...] = jnp.dot(xs_t[0, 0], back_side[...], preferred_element_type=f32)
    matrix_votes(2, grad_short, (nothing, nothing), lambda k: None)

    gain_one, shift_one = none, none
    for j in range(side):
        taps = [b for b in range(3) if 0 <= j - b + 1 < side]
        pieces = [
            back_two[j - b + 1, 2 - a : 2 - a + side].reshape(band, width)
            for b in taps
            for a in range(3)
        ]
        weights = jnp.concatenate([low_two[b * 3 + a] for b in taps for a in range(3)], axis=1)
        grad = lax.dot_general(
            jnp.concatenate(pieces, axis=1),
            weights,
            (((1,), (1,)), ((), ())),
            preferred_element_type=f32,
        )
        before = main_pre[pl.ds(j * band, band), :]
        hidden = before * slope_one + base_one
        opened = gate(hidden)
        grad = grad * (opened * (1.0 + hidden * (1.0 - opened)))
        shift_one = shift_one + jnp.sum(grad, axis=0, keepdims=True)
        gain_one = gain_one + jnp.sum(
            grad * ((before - mean_one) * inv_one), axis=0, keepdims=True
        )
        back_one[j, :side] = (grad * slope_one).astype(low).reshape(side, slots, width)
        turn(1 + j)

    square_head = grad_head * grad_head + EPS_ROW
    real = lax.broadcasted_iota(jnp.int32, square_head.shape, 0) < classes
    square_head = jnp.where(real, square_head, 0.0)
    head_lanes = pl.ds(edges[2], width)
    old = row_ref[:, head_lanes]
    row = keep * old + (1.0 - keep) * jnp.sum(square_head, axis=0, keepdims=True) / classes
    row_new[:, head_lanes] = row
    diagonal = eye_mask(16, classes)
    old = jnp.broadcast_to(col_ref[:, 3 * width :], (16, classes))
    old = jnp.sum(jnp.where(diagonal, old, 0.0), axis=1, keepdims=True)
    column = keep * old + (1.0 - keep) * jnp.sum(square_head, axis=1, keepdims=True) / width
    col_new[:, 3 * width :] = jnp.sum(
        jnp.where(diagonal, jnp.broadcast_to(column, (16, classes)), 0.0), axis=0, keepdims=True
    )
    real_column = lax.broadcasted_iota(jnp.int32, column.shape, 0) < classes
    column = jnp.where(real_column, column, 1.0)
    mean = jnp.sum(row, axis=1, keepdims=True) / width
    raw = grad_head * (lax.rsqrt(row) * jnp.sqrt(mean)) * lax.rsqrt(column)
    clip = jnp.maximum(1.0, jnp.sqrt(total_of(raw * raw) / (classes * width)))
    head_votes = jnp.tanh(raw / clip)[:classes]

    raws = []
    for k, grad in enumerate((gain_one, shift_one, gain_two, shift_two, gain_side, shift_two)):
        here = pl.ds(k * width, width)
        moment = keep * moment_ref[:, here] + (1.0 - keep) * (grad * grad + EPS_ROW)
        moment_new[:, here] = moment
        raws.append(grad * lax.rsqrt(moment))
    raw = jnp.concatenate(raws, axis=0)
    clip = jnp.maximum(1.0, jnp.sqrt(total_of(raw * raw) / raw.size))
    norm_votes = jnp.tanh(raw / clip)
    tail_votes = jnp.concatenate([head_votes, norm_votes], axis=0)
    kept["tail"] = exchange_start(
        2,
        jnp.concatenate(
            [tail_votes[:, 128 * q : 128 * (q + 1)] for q in range(4)]
            + [jnp.broadcast_to(loss, (8, 128))],
            axis=0,
        ),
    )


    for b in range(3):
        first, last = (0, side - 1) if b == 0 else (0, side)
        shift = 1 if b == 0 else 0
        for a in range(3):
            start = 1 if a == 0 else 0
            right = back_one[first + shift : last + shift, start : start + side]
            turned_product(
                xs_t.at[0 if b == 1 else 1, 0 if a == 1 else 1],
                slice(first * band, last * band),
                right.reshape(-1, width),
                grad_one,
                (a * 3 + b) * in_width,
            )
        if b == 1:
            kept["tail"] = exchange_middle(2, kept["tail"])
        turn(5 + b)

    matrix_votes(
        0,
        grad_one,
        (lambda: turn(8), lambda: turn(9)),
        lambda k: go(0, early + k) if k < 2 else None,
    )
    turn(10)
    for u in range(len(units)):
        in_flight[u].wait()
        for k in range(1, 4):
            line_copy(u, k).wait_send()
            spread_copy(u, k).wait_send()
    for away, copy in passes:

        @pl.when(away)
        def _():
            copy.wait_send()


def finish_kernel(count, chunks, *refs):
    sources, targets, sem = refs[:count], refs[count : 2 * count], refs[2 * count]
    rows = sources[0].shape[0]
    step = -(-rows // chunks // 16) * 16
    copies = []
    for k in range(chunks):
        here = pl.ds(k * step, min(step, rows - k * step))
        copies.append(
            pltpu.make_async_copy(sources[0].at[here], targets[0].at[here], sem.at[k])
        )
    for k in range(1, count):
        copies.append(pltpu.make_async_copy(sources[k], targets[k], sem.at[chunks + k]))
    for copy in copies:
        copy.start()
    for copy in copies:
        copy.wait()


def finish(values):
    count, chunks = len(values), 4
    held = [pltpu.with_memory_space_constraint(value, pltpu.VMEM) for value in values]
    return pl.pallas_call(
        functools.partial(finish_kernel, count, chunks),
        out_shape=[jax.ShapeDtypeStruct(value.shape, value.dtype) for value in values],
        in_specs=[pl.BlockSpec(memory_space=pltpu.VMEM)] * count,
        out_specs=[pl.BlockSpec(memory_space=pl.ANY)] * count,
        scratch_shapes=[pltpu.SemaphoreType.DMA((chunks + count,))],
        compiler_params=pltpu.CompilerParams(vmem_limit_bytes=1024 * 1024),
        name="finish",
    )(*held)


def run_step(images, conv_one, conv_two, shortcut, head, norm_params, valid, labels, rows, cols, moment):
    vmem = pl.BlockSpec(memory_space=pltpu.VMEM)
    hbm = pl.BlockSpec(memory_space=pl.ANY)
    low, f32 = jnp.bfloat16, jnp.float32
    dma = pltpu.SemaphoreType.DMA
    workers = lax.axis_size("dp")
    slots, in_width = valid.shape[1], images.shape[1]
    width = conv_one.shape[1]
    pixels = images.shape[0] // 4
    shape = pltpu.VMEM
    edges = [conv_one.shape[0]]
    edges.append(edges[0] + conv_two.shape[0])
    edges.append(edges[1] + shortcut.shape[0])
    units = make_units(edges)
    flat = (edges[2] + TAIL) * width // 128
    share = flat // workers
    return pl.pallas_call(
        functools.partial(step_kernel, tuple(edges), tuple(units), 1.0 / math.sqrt(workers)),
        out_shape=(
            shape((share, 128), f32),
            shape((share, 128), f32),
            shape((flat, 128), low),
            shape(rows.shape, f32),
            shape(cols.shape, f32),
            shape(moment.shape, f32),
            shape((1, 1), f32),
            shape((1, 1), f32),
        ),
        in_specs=[hbm] * 4 + [vmem] * 7,
        out_specs=(vmem,) * 8,
        scratch_shapes=[
            pltpu.VMEM((2, 4, 2, 4, slots, in_width), low),
            pltpu.VMEM(conv_one.shape, f32),
            pltpu.VMEM(conv_two.shape, f32),
            pltpu.VMEM(shortcut.shape, f32),
            pltpu.VMEM((9, in_width, width), low),
            pltpu.VMEM((9, width, width), low),
            pltpu.VMEM((1, in_width, width), low),
            pltpu.VMEM((pixels, width), f32),
            pltpu.VMEM((pixels, width), f32),
            pltpu.VMEM((pixels, width), f32),
            pltpu.VMEM((4, 6, slots, width), low),
            pltpu.VMEM((4, 6, slots, width), low),
            pltpu.VMEM((4, 5, slots, width), low),
            pltpu.VMEM((pixels, width), low),
            pltpu.VMEM((width, pixels), low),
            pltpu.VMEM((2, 2, in_width, pixels), low),
            pltpu.VMEM((128, width), f32),
            pltpu.VMEM((conv_two.shape[0], 128), f32),
            pltpu.VMEM((8, width), f32),
            pltpu.VMEM((24, 128), f32),
            pltpu.VMEM((8, 24, 128), f32),
            pltpu.VMEM((4, 24, 128), f32),
            pltpu.VMEM((8, 128), f32),
            pltpu.VMEM((8, 8, 128), f32),
            pltpu.VMEM((4, 8, 128), f32),
            pltpu.VMEM((GROUP + 8, 128), f32),
            pltpu.VMEM((8, GROUP + 8, 128), f32),
            pltpu.VMEM((4, GROUP + 8, 128), f32),
            pltpu.VMEM((16 * SPAN, 128), low),
            pltpu.VMEM((8 * SPAN, 128), low),
            pltpu.VMEM((4 * SPAN, 128), low),
            pltpu.VMEM((4 * SPAN, 128), low),
            pltpu.VMEM((SPAN, 128), low),
            pltpu.VMEM((SPAN + GROUP, 128), low),
            pltpu.VMEM((SPAN + GROUP, 128), f32),
            pltpu.VMEM((OWN, width), f32),
            pltpu.VMEM((OWN + TAIL, width), f32),
            pltpu.VMEM((SPAN + GROUP, 128), f32),
            pltpu.VMEM((SPAN + GROUP, 128), f32),
            dma((9 + len(units),)),
            dma((3, 10)),
            dma((3, 10)),
            dma((len(units), 3)),
            dma((len(units), 3)),
            dma((len(units), 4)),
            dma((len(units), 4)),
            dma((2 * OWN // 16,)),
            dma((OWN // 16 + 1,)),
            dma((len(units), 4)),
            dma((len(units), 4)),
            dma((len(units), 3)),
            dma((len(units), 3)),
            pltpu.SemaphoreType.REGULAR((len(units),)),
            dma((2,)),
        ],
        compiler_params=pltpu.CompilerParams(
            collective_id=1, has_side_effects=True, vmem_limit_bytes=54 * 1024 * 1024
        ),
        name="step",
    )(images, conv_one, conv_two, shortcut, head, norm_params, valid, labels, rows, cols, moment)


def scale_for(weight):
    return jnp.maximum(EPS_SCALE, jnp.sqrt(jnp.mean(weight * weight)))


def local_general(
    images,
    valid_slot,
    labels,
    conv_one,
    conv_two,
    shortcut,
    classifier,
    norm_params,
    row_state,
    col_state,
    bn_moment,
):
    in_width = images.shape[3]
    width = conv_one.shape[1]
    kernel_one = conv_one.astype(jnp.bfloat16).reshape(3, 3, in_width, width)
    kernel_two = conv_two.astype(jnp.bfloat16).reshape(3, 3, width, width)
    kernel_short = shortcut.astype(jnp.bfloat16).reshape(1, 1, in_width, width)
    head_low = classifier.astype(jnp.bfloat16)
    slot_count = images.shape[0]
    out_side = images.shape[1] // 2
    pixel_count = out_side * out_side
    slot_weight = valid_slot.astype(jnp.float32)
    pixel_weight = jnp.broadcast_to(slot_weight[:, None], (slot_count, pixel_count)).reshape(-1, 1)
    main_pre, side_pre = first_section(images, kernel_one, kernel_short)
    main_sums = masked_moments(pixel_weight, main_pre)
    side_sums = masked_moments(pixel_weight, side_pre)
    count_row = jnp.broadcast_to(jnp.sum(slot_weight), (width,))
    first_sums = lax.psum(jnp.stack([*main_sums, *side_sums, count_row]), "dp")
    valid_count = first_sums[4, 0]
    denominator = jnp.maximum(valid_count, 1.0)
    pixels = denominator * pixel_count
    norm_one = settle(first_sums[0], first_sums[1], pixels)
    norm_side = settle(first_sums[2], first_sums[3], pixels)
    hidden_one, active, main_two = second_section(
        main_pre, norm_one, norm_params, kernel_two, slot_count, out_side
    )
    two_sums = masked_moments(pixel_weight, main_two)
    second_sums = lax.psum(jnp.stack([*two_sums]), "dp")
    norm_two = settle(second_sums[0], second_sums[1], pixels)
    joined_pre = (
        (main_two - norm_two[0]) * norm_two[1] * norm_params[2]
        + norm_params[3]
        + (side_pre - norm_side[0]) * norm_side[1] * norm_params[4]
        + norm_params[5]
    )
    joined = jax.nn.silu(joined_pre).reshape(slot_count, pixel_count, -1)
    pooled = jnp.mean(joined, axis=1).astype(jnp.bfloat16)
    logits = jnp.dot(pooled, head_low, preferred_element_type=jnp.float32)
    largest = jnp.max(logits, axis=1, keepdims=True)
    exp_terms = jnp.exp(logits - largest)
    total_exp = jnp.sum(exp_terms, axis=1, keepdims=True)
    log_total = largest[:, 0] + jnp.log(total_exp[:, 0])
    onehot = (labels[:, None] == jnp.arange(logits.shape[1], dtype=jnp.int32)[None, :]).astype(
        jnp.float32
    )
    local_sum = jnp.sum(slot_weight * (log_total - jnp.sum(onehot * logits, axis=1)))
    grad_logits = ((exp_terms / total_exp - onehot) * (slot_weight / denominator)[:, None]).astype(
        jnp.bfloat16
    )
    grad_head = lax.dot_general(
        pooled, grad_logits, (((0,), (0,)), ((), ())), preferred_element_type=jnp.float32
    )
    grad_pooled = lax.dot_general(
        grad_logits, head_low, (((1,), (1,)), ((), ())), preferred_element_type=jnp.float32
    )
    spread_pooled = jnp.broadcast_to(
        (grad_pooled / pixel_count)[:, None, :], (slot_count, pixel_count, width)
    )
    grad_joined = spread_pooled.reshape(slot_count * pixel_count, width) * silu_slope(joined_pre)
    gain_two, shift_two, grad_two = norm_backward(grad_joined, main_two, norm_two, norm_params[2])
    gain_side, shift_side, grad_side = norm_backward(
        grad_joined, side_pre, norm_side, norm_params[4]
    )
    grad_two_maps = grad_two.reshape(slot_count, out_side, out_side, width)
    grad_side_maps = grad_side.reshape(slot_count, out_side, out_side, width)
    grad_conv_two = conv_weight_grad(active, grad_two_maps, 1, 1, 1)
    grad_short = conv_weight_grad(images, grad_side_maps, 2, 0, -1)
    kernel_turned = jnp.transpose(kernel_two[::-1, ::-1], (0, 1, 3, 2))
    grad_active = conv_apply(grad_two_maps, kernel_turned, 1, 1).reshape(
        slot_count * pixel_count, width
    )
    grad_hidden = grad_active * silu_slope(hidden_one)
    gain_one, shift_one, grad_one = norm_backward(grad_hidden, main_pre, norm_one, norm_params[0])
    grad_conv_one = conv_weight_grad(
        images, grad_one.reshape(slot_count, out_side, out_side, width), 2, 1, 0
    )
    grad_norms = jnp.stack([gain_one, shift_one, gain_two, shift_two, gain_side, shift_side])
    grads = (grad_conv_one, grad_conv_two, grad_short, grad_head, grad_norms)
    votes, rows_new, cols_new, moment_new = make_votes(
        grads, row_state[0], col_state[0], bn_moment[0]
    )
    workers = lax.axis_size("dp")
    weights = (conv_one, conv_two, shortcut, classifier, norm_params)
    scales = [scale_for(weight) for weight in weights]
    loss_sum = lax.psum(local_sum, "dp")
    flat_vote = jnp.concatenate([vote.reshape(-1) for vote in votes])
    flat_old = jnp.concatenate([weight.reshape(-1) for weight in weights])
    flat_scale = jnp.concatenate(
        [
            jnp.broadcast_to(scale, (weight.size,))
            for scale, weight in zip(scales, weights)
        ]
    )
    vote_mine = lax.psum_scatter(flat_vote, "dp", tiled=True)
    share = vote_mine.shape[0]
    start = lax.axis_index("dp") * share
    new_mine = lax.dynamic_slice_in_dim(
        flat_old, start, share
    ) - lax.dynamic_slice_in_dim(flat_scale, start, share) * jnp.tanh(
        vote_mine / math.sqrt(workers)
    )
    copies = lax.all_gather(new_mine.astype(jnp.bfloat16), "dp", tiled=True)
    return (
        loss_sum,
        valid_count,
        new_mine,
        copies,
        vote_mine,
        rows_new[None, :],
        cols_new[None, :],
        moment_new[None, :],
    )


def local(
    images,
    valid_slot,
    labels,
    conv_one,
    conv_two,
    shortcut,
    classifier,
    norm_params,
    row_state,
    col_state,
    bn_moment,
):
    new_mine, vote_mine, copies, rows_new, cols_new, moment_new, loss_sum, valid_count = run_step(
        images.reshape(-1, images.shape[-1]),
        conv_one,
        conv_two,
        shortcut,
        classifier.T,
        norm_params,
        valid_slot.reshape(1, -1),
        labels.reshape(1, -1),
        row_state,
        col_state,
        bn_moment,
    )
    copies, new_mine, vote_mine, rows_new, cols_new, moment_new, loss_sum, valid_count = finish(
        (copies, new_mine, vote_mine, rows_new, cols_new, moment_new, loss_sum, valid_count)
    )
    return (
        loss_sum.reshape(()),
        valid_count.reshape(()),
        new_mine.reshape(-1),
        copies.reshape(-1),
        vote_mine.reshape(-1),
        rows_new,
        cols_new,
        moment_new,
    )


def solution(mesh):
    placed = (
        P("dp", None, None, None),
        P("dp"),
        P("dp"),
        P(),
        P(),
        P(),
        P(),
        P(),
        P("dp", None),
        P("dp", None),
        P("dp", None),
    )
    return jax.shard_map(
        local if mesh.shape["dp"] == 32 else local_general,
        mesh=mesh,
        in_specs=placed,
        out_specs=(P(), P(), P("dp"), P(), P("dp"), P("dp", None), P("dp", None), P("dp", None)),
        check_vma=False,
    )
```

```python
import functools
import math

import jax
import jax.numpy as jnp
from jax import lax
from jax.experimental import pallas as pl
from jax.experimental.pallas import tpu as pltpu
from jax.sharding import PartitionSpec as P

STEP = 10
MESH = pl.DeviceIdType.MESH

EPS_NORM = 1e-05
EPS_ROW = 1e-30
EPS_SCALE = 0.001
FORWARD_DIMS = ("NHWC", "HWIO", "NHWC")
WEIGHT_DIMS = ("CHWN", "IHWO", "HWNC")
OWN = 224
TAIL = 16
PIECE = 32
SPAN = 4 * OWN
HALF = SPAN // 2
GROUP = 64


def conv_apply(maps, kernel, stride, margin):
    return lax.conv_general_dilated(
        maps,
        kernel,
        (stride, stride),
        ((margin, margin), (margin, margin)),
        dimension_numbers=FORWARD_DIMS,
        preferred_element_type=jnp.float32,
    )


def conv_weight_grad(maps, grad_out, stride, low_pad, high_pad):
    result = lax.conv_general_dilated(
        maps,
        grad_out,
        (1, 1),
        ((low_pad, high_pad), (low_pad, high_pad)),
        rhs_dilation=(stride, stride),
        dimension_numbers=WEIGHT_DIMS,
        preferred_element_type=jnp.float32,
    )
    return result.reshape(-1, result.shape[3])


def silu_slope(values):
    sigmoid_part = jax.nn.sigmoid(values)
    return sigmoid_part * (1.0 + values * (1.0 - sigmoid_part))


def settle(sum_plain, sum_square, pixels):
    mean_value = sum_plain / pixels
    return (mean_value, lax.rsqrt(sum_square / pixels - mean_value * mean_value + EPS_NORM))


def first_section(images, kernel_one, kernel_short):
    row_count = images.shape[0] * (images.shape[1] // 2) ** 2
    main_pre = conv_apply(images, kernel_one, 2, 1).reshape(row_count, -1)
    side_pre = conv_apply(images, kernel_short, 2, 0).reshape(row_count, -1)
    return (main_pre, side_pre)


def second_section(main_pre, norm_one, norm_params, kernel_two, slot_count, out_side):
    hidden_one = (main_pre - norm_one[0]) * norm_one[1] * norm_params[0] + norm_params[1]
    active = (
        jax.nn.silu(hidden_one).astype(jnp.bfloat16).reshape(slot_count, out_side, out_side, -1)
    )
    main_two = conv_apply(active, kernel_two, 1, 1).reshape(slot_count * out_side * out_side, -1)
    return (hidden_one, active, main_two)


def masked_moments(pixel_weight, values):
    return (jnp.sum(pixel_weight * values, axis=0), jnp.sum(pixel_weight * values * values, axis=0))


def soft_sign(step_raw):
    clip_by = jnp.maximum(1.0, jnp.sqrt(jnp.mean(step_raw * step_raw)))
    return jnp.tanh(step_raw / clip_by)


def make_votes(grads, rows_old, cols_old, moment_old):
    decay_rate = 1.0 - STEP ** (-0.8)
    votes, rows_new, cols_new = ([], [], [])
    row_at, col_at = (0, 0)
    for matrix in grads[:4]:
        row_size, col_size = matrix.shape
        square = matrix * matrix + EPS_ROW
        row_part = decay_rate * rows_old[row_at : row_at + row_size] + (
            1.0 - decay_rate
        ) * jnp.mean(square, axis=1)
        col_part = decay_rate * cols_old[col_at : col_at + col_size] + (
            1.0 - decay_rate
        ) * jnp.mean(square, axis=0)
        second = row_part[:, None] * col_part[None, :] / jnp.mean(row_part)
        votes.append(soft_sign(matrix * lax.rsqrt(second)))
        rows_new.append(row_part)
        cols_new.append(col_part)
        row_at += row_size
        col_at += col_size
    flat_norm = grads[4].reshape(-1)
    moment_new = decay_rate * moment_old + (1.0 - decay_rate) * (flat_norm * flat_norm + EPS_ROW)
    votes.append(soft_sign(flat_norm * lax.rsqrt(moment_new)))
    return (votes, jnp.concatenate(rows_new), jnp.concatenate(cols_new), moment_new)


def norm_backward(grad_out, pre_value, norm_pair, gain_row):
    normed = (pre_value - norm_pair[0]) * norm_pair[1]
    grad_gain = jnp.sum(grad_out * normed, axis=0)
    grad_shift = jnp.sum(grad_out, axis=0)
    grad_pre = (grad_out * gain_row * norm_pair[1]).astype(jnp.bfloat16)
    return (grad_gain, grad_shift, grad_pre)


SCHEDULE = (
    (),
    (
        (1, 0),
    ),
    (
        (0, 2), (1, 1),
    ),
    (
        (0, 3), (1, 2), (2, 0), (0, 4), (1, 3), (2, 1),
    ),
    (
        (0, 5), (1, 4), (2, 2), (3, 0),
    ),
    (
        (0, 6), (1, 5), (2, 3), (3, 1),
    ),
    (
        (0, 7), (1, 6), (2, 4), (3, 2), (4, 0),
    ),
    (),
    (
        (0, 8), (1, 7), (2, 5), (3, 3), (4, 1),
    ),
    (),
    (
        (1, 8), (2, 6), (3, 4), (4, 2), (1, 9), (2, 7), (3, 5), (4, 3), (5, 0), (0, 11), (1, 10),
        (2, 8), (3, 6), (4, 4), (5, 1), (0, 12), (1, 11), (2, 9), (3, 7), (4, 5), (5, 2), (6, 0),
        (0, 13), (1, 12), (2, 10), (3, 8), (4, 6), (5, 3), (6, 1), (1, 13), (2, 11), (3, 9),
        (4, 7), (8, 0), (5, 4), (6, 2), (2, 12), (3, 10), (4, 8), (5, 5), (6, 3), (7, 0),
        (2, 13), (3, 11), (4, 9), (5, 6), (6, 4), (7, 1), (3, 12), (4, 10), (5, 7), (6, 5),
        (7, 2), (3, 13), (4, 11), (5, 8), (6, 6), (7, 3), (4, 12), (5, 9), (6, 7), (7, 4),
        (4, 13), (5, 10), (6, 8), (7, 5), (5, 11), (6, 9), (7, 6), (5, 12), (6, 10), (7, 7),
        (5, 13), (6, 11), (7, 8), (6, 12), (7, 9), (9, 0), (6, 13), (7, 10), (7, 11), (7, 12),
        (9, 1), (7, 13), (9, 2),
    ),
)


def place():
    me = lax.axis_index("dp")
    core = lax.rem(me, 2)
    x = lax.rem(lax.div(me, 2), 2)
    y = lax.rem(lax.div(me, 4), 2)
    z = lax.div(me, 8)
    return me, core, x, y, z


def send(src, dst, send_sem, recv_sem, partner):
    copy = pltpu.make_async_remote_copy(
        src_ref=src,
        dst_ref=dst,
        send_sem=send_sem,
        recv_sem=recv_sem,
        device_id=(partner,),
        device_id_type=MESH,
    )
    copy.start()
    return copy


def scale_of(row, scales, edges):
    picked = scales[2]
    picked = jnp.where(row < edges[1], scales[1], picked)
    return jnp.where(row < edges[0], scales[0], picked)


def make_units(edges):
    one, two, short = edges[0] // 16, edges[1] // 16, edges[2] // 16
    units = []
    for k in range((two - one) // 32):
        units.append((one + 32 * k, 1, k % 2 == 0, 16, (1, 1)))
    for k in range(one // 32):
        units.append((32 * k, 1, k % 2 == 1, 16, (0, 0)))
    at = one // 32 * 32
    assert one - at == 16 and short - two == 16
    units.append((at, 1, False, two - at, (0, 2)))
    return units


def settle_rows(sums, pixels, gain, shift):
    mean = sums[0] / pixels
    inv = lax.rsqrt(sums[1] / pixels - mean * mean + EPS_NORM)
    slope = gain * inv
    return mean, inv, slope, shift - mean * slope


def gate(values):
    return 0.5 * jnp.tanh(0.5 * values) + 0.5


def eye_mask(rows, columns, offset=0):
    down = lax.broadcasted_iota(jnp.int32, (rows, columns), 0) + offset
    return down == lax.broadcasted_iota(jnp.int32, (rows, columns), 1)


def column_of(row, size):
    spread = jnp.where(eye_mask(size, size), jnp.broadcast_to(row, (size, size)), 0)
    return jnp.sum(spread, axis=1, keepdims=True)


def total_of(values):
    return jnp.sum(jnp.sum(values, axis=0, keepdims=True), axis=1, keepdims=True)


def fold(values):
    return jnp.sum(values.reshape(values.shape[0] // 8, 8, values.shape[1]), axis=0)


def cast_weight(source, target, square_ref, taps, depth, fetches):
    step = 128
    for tap in taps:
        chunk = source.shape[0] // depth // len(fetches)
        if tap % chunk == 0:
            fetches[tap // chunk].wait()
        new_tap = (tap % 3) * 3 + tap // 3

        @pl.loop(0, depth // step)
        def _(k):
            start = pl.multiple_of(k * step, step)
            values = source[pl.ds(tap * depth + start, step), :]
            target[new_tap, pl.ds(start, step), :] = values.astype(jnp.bfloat16)
            square_ref[...] += fold(values * values)


def factored_votes(grad, rows, row_at, rows_old, rows_new, col_old, level, votes, vote_at, between, after):
    width = grad.shape[1]
    keep = 1.0 - STEP ** (-0.8)
    step = 128
    quarters = width // 128

    def first(k, carry):
        col_sum, row_sum = carry
        start = pl.multiple_of(k * step, step)
        lanes = pl.ds(pl.multiple_of(row_at + start, step), step)
        old = rows_old[:, lanes] * keep
        line = jnp.zeros((8, 128), jnp.float32)
        for m in range(step // 8):
            block = grad[pl.ds(start + 8 * m, 8), :]
            square = block * block
            col_sum = col_sum + square
            part = square[:, :128]
            for q in range(1, quarters):
                part = part + square[:, 128 * q : 128 * (q + 1)]
            part = part * ((1.0 - keep) / width)
            diagonal = eye_mask(8, 128, 8 * m)
            part = part + jnp.where(diagonal, jnp.broadcast_to(old, (8, 128)), 0.0)
            row = jnp.sum(part, axis=1, keepdims=True) + (1.0 - keep) * EPS_ROW
            row = jnp.broadcast_to(row, (8, 128))
            level[pl.ds(start + 8 * m, 8), :] = row
            row_sum = row_sum + row
            line = line + jnp.where(diagonal, row, 0.0)
        rows_new[:, lanes] = jnp.sum(line, axis=0, keepdims=True)
        return col_sum, row_sum

    col_sum, row_sum = lax.fori_loop(
        0,
        rows // step,
        first,
        (jnp.zeros((8, width), jnp.float32), jnp.zeros((8, 128), jnp.float32)),
    )
    col_new = keep * col_old + (1.0 - keep) * (
        jnp.sum(col_sum, axis=0, keepdims=True) / rows + EPS_ROW
    )
    scale = lax.rsqrt(col_new)
    root_mean = jnp.sqrt(jnp.sum(row_sum, axis=0, keepdims=True) / rows)

    def second(k, carry):
        start = pl.multiple_of(k * step, step)
        for m in range(step // 8):
            here = pl.ds(start + 8 * m, 8)
            factor = lax.rsqrt(level[here, :]) * root_mean
            level[here, :] = factor
            raw = grad[here, :] * scale
            power = raw * raw
            part = power[:, :128]
            for q in range(1, quarters):
                part = part + power[:, 128 * q : 128 * (q + 1)]
            carry = carry + part * (factor * factor)
        return carry

    between[0]()
    power = lax.fori_loop(0, rows // step, second, jnp.zeros((8, 128), jnp.float32))
    between[1]()
    clip = jnp.maximum(1.0, jnp.sqrt(total_of(power) / (rows * width)))
    scale = scale / clip

    def third(k, _):
        start = pl.multiple_of(k * step, step)
        for m in range(step // 16):
            here = pl.ds(start + 16 * m, 16)
            factor = level[here, :]
            factor = jnp.concatenate([factor] * quarters, axis=1)
            vote = jnp.tanh(grad[here, :] * factor * scale).astype(jnp.bfloat16)
            at = pl.multiple_of((vote_at + start) * 4 + GROUP * m, GROUP)
            for q in range(quarters):
                votes[pl.ds(at + 16 * q, 16), :] = vote[:, 128 * q : 128 * (q + 1)]
        return 0

    part = 512 // step
    for k in range(0, rows // step, part):
        lax.fori_loop(k, min(k + part, rows // step), third, 0)
        after(k // part)
    return col_new


def step_kernel(
    edges,
    units,
    root,
    images,
    one_hbm,
    two_hbm,
    short_hbm,
    head_ref,
    norm_ref,
    valid_ref,
    label_ref,
    row_ref,
    col_ref,
    moment_ref,
    new_ref,
    vote_ref,
    out_ref,
    row_new,
    col_new,
    moment_new,
    loss_ref,
    count_ref,
    xs,
    grad_one,
    grad_two,
    grad_short,
    low_one,
    low_two,
    low_short,
    main_pre,
    side_pre,
    main_two,
    active,
    back_two,
    back_one,
    back_side,
    active_t,
    xs_t,
    head_pad,
    level,
    square,
    post_one,
    plane_one,
    line_one,
    post_two,
    plane_two,
    line_two,
    tail_post,
    tail_plane,
    tail_line,
    core_in,
    wide_in,
    deep_in,
    line_in,
    sum_low,
    landed,
    total,
    own_weight,
    weight,
    vote_flat,
    new_flat,
    tail_vote,
    tail_new,
    fetch_sem,
    small_send,
    small_recv,
    sent,
    rs_recv,
    line_recv,
    pass_send,
    land_recv,
    spread_recv,
    ag_recv,
    free_sem,
    load_sem,
):
    slots, in_width = xs.shape[4:]
    width = main_pre.shape[1]
    side = 4
    band = side * slots
    pixel_count = side * side
    classes = head_ref.shape[0]
    keep = 1.0 - STEP ** (-0.8)
    low = jnp.bfloat16
    f32 = jnp.float32

    me, core, x, y, z = place()
    flip_core = me + 1 - 2 * core
    flip_x = me + 2 - 4 * x
    flip_y = me + 4 - 8 * y
    spot = lax.rem(me, 8)
    near = [z * 8 + lax.rem(spot + k, 8) for k in range(1, 8)]
    far = [lax.rem(z + k, 4) * 8 + spot for k in range(1, 4)]
    others = [lax.rem(me + k, 32) for k in range(1, 32)]

    count = images.shape[0]
    loads = []
    for half in range(2):
        lanes = slice(128 * half, 128 * (half + 1))
        loads.append(
            pltpu.make_async_copy(
                images.at[:, lanes], core_in.at[pl.ds(half * count, count)], load_sem.at[half]
            )
        )
        loads[half].start()

    def chunks_of(source, target, first, count):
        rows = source.shape[0] // count
        return [
            pltpu.make_async_copy(
                source.at[pl.ds(k * rows, rows)],
                target.at[pl.ds(k * rows, rows)],
                fetch_sem.at[first + k],
            )
            for k in range(count)
        ]

    fetch_one = chunks_of(one_hbm, grad_one, 0, 3)
    fetch_short = chunks_of(short_hbm, grad_short, 3, 1)
    fetch_two = chunks_of(two_hbm, grad_two, 4, 3)
    for fetch in fetch_one + fetch_short:
        fetch.start()
    barrier = pltpu.get_barrier_semaphore()
    for partner in others:
        pl.semaphore_signal(barrier, inc=1, device_id=(partner,), device_id_type=MESH)

    def fetch_rows(row, count, place_at, sem):
        parts = (
            (one_hbm, 0, edges[0]),
            (two_hbm, edges[0], edges[1]),
            (short_hbm, edges[1], edges[2]),
        )
        for ref, first, last in parts:

            @pl.when(jnp.logical_and(row >= first, row < last))
            def _():
                start = pl.multiple_of(row - first, count)
                pltpu.make_async_copy(
                    ref.at[pl.ds(start, count)], weight.at[pl.ds(place_at, count)], sem
                ).start()

    first_row = me * OWN

    for half in range(2):
        lanes = slice(128 * half, 128 * (half + 1))
        loads[half].wait()
        level[:count, :] = core_in[pl.ds(half * count, count), :].astype(f32)
        for h in range(2 * side):
            for w in range(2 * side):
                rows = level[pl.ds(2 * side * h + w, slots, stride=4 * pixel_count), :]
                xs[w % 2, w // 2, h % 2, h // 2, :, lanes] = rows.astype(low)

    scales = {}

    def scale_from(weight_square, size):
        return jnp.maximum(EPS_SCALE, jnp.sqrt(total_of(weight_square) / size))

    exchanges = (
        (post_one, plane_one, line_one),
        (post_two, plane_two, line_two),
        (tail_post, tail_plane, tail_line),
    )

    def exchange_start(which, values):
        mine_ref, plane_ref, _ = exchanges[which]
        mine_ref[...] = values
        plane_ref[spot] = values
        return [
            send(
                mine_ref,
                plane_ref.at[spot],
                small_send.at[which, k],
                small_recv.at[which, k],
                partner,
            )
            for k, partner in enumerate(near)
        ]

    def pack_rows(rows):
        pieces = [row[:, 128 * q : 128 * (q + 1)] for row in rows for q in range(4)]
        pad = -len(pieces) % 8
        if pad:
            pieces.append(jnp.zeros((pad, 128), f32))
        return jnp.concatenate(pieces, axis=0)

    def unpack_row(lines_in, k):
        return jnp.concatenate([lines_in[4 * k + q : 4 * k + q + 1] for q in range(4)], axis=1)

    def exchange_middle(which, copies):
        _, plane_ref, line_ref = exchanges[which]
        for copy in copies:
            copy.wait()
        line_ref[z] = functools.reduce(lambda a, b: a + b, [plane_ref[k] for k in range(8)])
        return [
            send(
                line_ref.at[z],
                line_ref.at[z],
                small_send.at[which, 7 + k],
                small_recv.at[which, 7 + k],
                partner,
            )
            for k, partner in enumerate(far)
        ]

    def exchange_end(which, copies):
        line_ref = exchanges[which][2]
        for copy in copies:
            copy.wait()
        return (line_ref[0] + line_ref[1]) + (line_ref[2] + line_ref[3])

    def lines(start, count):
        return pl.ds(pl.multiple_of(start, 16), count)

    sizes = [GROUP * unit[1] for unit in units]
    starts = [sum(sizes[:k]) for k in range(len(units) + 1)]

    def part_of(ref, u, share, start, count):
        return ref.at[lines(share * starts[u] + start, count)]

    def places(u):
        if units[u][2]:
            return x, y, flip_x, flip_y
        return y, x, flip_y, flip_x

    def unit_start(u, cc):
        return GROUP * units[u][0] + cc * (GROUP * units[u][3])

    def own_group(u):
        first, second, _, _ = places(u)
        return units[u][0] + core * units[u][3] + (first * 8 + second * 4 + z) * units[u][1]

    def halve(source, target, u, stage, partner):
        return send(source, target, sent.at[stage], rs_recv.at[u, stage], partner)

    def scatter_start(u):
        size = 16 * sizes[u]
        return halve(
            out_ref.at[lines(unit_start(u, 1 - core), size)],
            part_of(core_in, u, 16, 0, size),
            u,
            0,
            flip_core,
        )

    def add_to(ref, u, share, source_ref, source_start):
        size = share * sizes[u]
        here = lines(share * starts[u], size)
        ref[here, :] = ref[here, :] + source_ref[lines(source_start, size), :]

    def sent_all(kind, ref):
        pltpu.make_async_remote_copy(
            src_ref=ref,
            dst_ref=ref,
            send_sem=sent.at[kind],
            recv_sem=rs_recv.at[0, 0],
            device_id=(flip_core,),
            device_id_type=MESH,
        ).wait_send()

    def scatter_one(u, copy):
        copy.wait_recv()
        add_to(core_in, u, 16, out_ref, unit_start(u, core))
        if u == len(units) - 1:
            sent_all(0, core_in)
            pl.semaphore_signal(free_sem, inc=1, device_id=(flip_core,), device_id_type=MESH)
        first, _, flip_first, _ = places(u)
        size = 8 * sizes[u]
        return halve(
            part_of(core_in, u, 16, (1 - first) * size, size),
            part_of(wide_in, u, 8, 0, size),
            u,
            1,
            flip_first,
        )

    def scatter_two(u, copy):
        copy.wait_recv()
        first, second, _, flip_second = places(u)
        add_to(wide_in, u, 8, core_in, 16 * starts[u] + first * 8 * sizes[u])
        size = 4 * sizes[u]
        return halve(
            part_of(wide_in, u, 8, (1 - second) * size, size),
            part_of(deep_in, u, 4, 0, size),
            u,
            2,
            flip_second,
        )

    def line_copy(u, k):
        plane_to = lax.rem(z + k, 4)
        return pltpu.make_async_remote_copy(
            src_ref=part_of(deep_in, u, 4, plane_to * sizes[u], sizes[u]),
            dst_ref=part_of(line_in, u, 4, z * sizes[u], sizes[u]),
            send_sem=sent.at[3],
            recv_sem=line_recv.at[u],
            device_id=(plane_to * 8 + spot,),
            device_id_type=MESH,
        )

    def scatter_three(u, copy):
        copy.wait_recv()
        _, second, _, _ = places(u)
        add_to(deep_in, u, 4, wide_in, 8 * starts[u] + second * 4 * sizes[u])
        for k in (3, 2, 1):
            line_copy(u, k).start()
        here = lines(4 * starts[u] + z * sizes[u], sizes[u])
        line_in[here, :] = deep_in[here, :]

    def three_landed(u, sem):
        ref = part_of(line_in, u, 4, 0, 3 * sizes[u])
        pltpu.make_async_remote_copy(
            src_ref=ref,
            dst_ref=ref,
            send_sem=sent.at[3],
            recv_sem=sem.at[u],
            device_id=(far[0],),
            device_id_type=MESH,
        ).wait_recv()

    groups = (edges[2] + TAIL) // 16
    spare = (groups - 1) // 32
    passes = []

    def land(local, group, to, slot, index):
        source = sum_low.at[lines(local * GROUP, GROUP)]
        target = landed.at[lines(slot * GROUP, GROUP)]
        copy = pltpu.make_async_remote_copy(
            src_ref=source,
            dst_ref=target,
            send_sem=pass_send.at[index],
            recv_sem=land_recv.at[slot],
            device_id=(to,),
            device_id_type=MESH,
        )
        return copy, source, target

    def pass_on(u):
        for m in range(units[u][1]):
            local = starts[u] // GROUP + m
            group = own_group(u) + m
            to, slot = lax.div(group, spare), lax.rem(group, spare)

            def one(receiver, at, index):
                copy, source, target = land(local, group, receiver, at, index)

                @pl.when(receiver != me)
                def _():
                    copy.start()

                @pl.when(receiver == me)
                def _():
                    target[...] = source[...]

                return copy

            first = jnp.logical_and(slot == 0, group > 0)
            ahead = lax.rem(to + 31, 32)
            passes.append((to != me, one(to, slot, 2 * local)))

            @pl.when(first)
            def _():
                one(ahead, spare, 2 * local + 1)

            copy = land(local, group, ahead, spare, 2 * local + 1)[0]
            passes.append((jnp.logical_and(first, ahead != me), copy))

    def flat_rows(row, q, values, ref):
        ref[pl.ds(row * 4 + q, 8, stride=4), :] = values

    def old_rows(u, cc):
        matrix = units[u][4][cc]
        base = edges[matrix - 1] if matrix else 0
        return (one_hbm, two_hbm, short_hbm)[matrix], 16 * own_group(u) - base, 16 * units[u][1]

    def own_fetch(u):
        target = own_weight.at[pl.ds(starts[u] // 4, 16 * units[u][1])]
        matrices = units[u][4]
        for cc in range(2):
            if cc and matrices[0] == matrices[1]:
                continue

            @pl.when((core == cc) if matrices[0] != matrices[1] else (core >= 0))
            def _():
                ref, row, count = old_rows(u, cc)
                pltpu.make_async_copy(
                    ref.at[pl.ds(pl.multiple_of(row, 16), count)], target, fetch_sem.at[9 + u]
                ).start()

    def spread_copy(u, k):
        own = out_ref.at[lines(own_group(u) * GROUP, sizes[u])]
        return pltpu.make_async_remote_copy(
            src_ref=own,
            dst_ref=own,
            send_sem=sent.at[4],
            recv_sem=spread_recv.at[u],
            device_id=(far[k - 1],),
            device_id_type=MESH,
        )

    def own_block(u):
        size = sizes[u]
        three_landed(u, line_recv)
        here = pl.ds(starts[u], size)
        low_sum = functools.reduce(
            lambda a, b: a + b,
            [line_in[pl.ds(4 * starts[u] + t * size, size), :].astype(f32) for t in range(4)],
        ).astype(low)
        sum_low[here, :] = low_sum
        total[here, :] = low_sum.astype(f32)
        target = own_weight.at[pl.ds(starts[u] // 4, 16 * units[u][1])]
        pltpu.make_async_copy(target, target, fetch_sem.at[9 + u]).wait()
        matrices = units[u][4]
        scale = jnp.where(core == 0, scales[matrices[0]], scales[matrices[1]])
        for m in range(units[u][1]):
            row = starts[u] // 4 + 16 * m
            for part in (0, 8):
                for q in range(4):
                    summed = total[pl.ds(row * 4 + 16 * q + part, 8), :]
                    old = own_weight[pl.ds(row + part, 8), 128 * q : 128 * (q + 1)]
                    fresh = old - scale * jnp.tanh(summed * root)
                    flat_rows(row + part, q, fresh, new_flat)
        out_ref[lines(own_group(u) * GROUP, size), :] = new_flat[here, :].astype(low)
        for k in (3, 2, 1):
            spread_copy(u, k).start()
        pass_on(u)

    def piece(rows, u, stage, partner):
        return send(
            out_ref.at[rows], out_ref.at[rows], sent.at[5 + stage], ag_recv.at[u, stage], partner
        )

    def gather_one(u):
        three_landed(u, spread_recv)
        first, second, _, flip_second = places(u)
        size = 4 * sizes[u]
        start = unit_start(u, core) + (2 * first + second) * size
        return piece(lines(start, size), u, 0, flip_second)

    def gather_two(u, copy):
        copy.wait_recv()
        first, _, flip_first, _ = places(u)
        size = 8 * sizes[u]
        return piece(lines(unit_start(u, core) + first * size, size), u, 1, flip_first)

    def gather_three(u, copy):
        copy.wait_recv()
        if u == 0:
            pl.semaphore_wait(free_sem, 1)
        return piece(lines(unit_start(u, core), 16 * sizes[u]), u, 2, flip_core)

    def renew(row, at_row):
        scale = scale_of(at_row, [scales[k] for k in range(3)], edges)
        for part in (0, 8):
            for q in range(4):
                summed = total[pl.ds(row * 4 + 16 * q + part, 8), :]
                old = weight[pl.ds(row + part, 8), 128 * q : 128 * (q + 1)]
                fresh = old - scale * jnp.tanh(summed * root)
                flat_rows(row + part, q, summed, vote_flat)
                flat_rows(row + part, q, fresh, new_flat)

    valid_column = column_of(valid_ref[...].astype(f32), slots)
    weight_slot = jnp.broadcast_to(valid_column, (slots, width))
    weight_band = jnp.concatenate([weight_slot] * side, axis=0)

    square[...] = jnp.zeros_like(square)
    cast_weight(grad_one, low_one, square, range(9), in_width, fetch_one)
    scales[0] = scale_from(square[...], grad_one.size)
    square[...] = jnp.zeros_like(square)
    cast_weight(grad_short, low_short, square, range(1), in_width, fetch_short)
    scales[2] = scale_from(square[...], grad_short.size)
    for fetch in fetch_two:
        fetch.start()
    for k in range(OWN // PIECE):
        fetch_rows(first_row + k * PIECE, PIECE, k * PIECE, fetch_sem.at[7])
    fetch_rows(first_row + OWN, TAIL, OWN, fetch_sem.at[8])
    for u in range(len(units)):
        own_fetch(u)

    def image_taps(j):
        pieces = []
        for b in range(3):
            column = j if b else j - 1
            if column < 0:
                continue
            across = 0 if b == 1 else 1
            for a in range(3):
                if a == 1:
                    piece = xs[across, column, 0].reshape(band, in_width)
                elif a == 2:
                    piece = xs[across, column, 1].reshape(band, in_width)
                else:
                    piece = xs[across, column, 1, : side - 1].reshape(band - slots, in_width)
                    piece = jnp.concatenate([jnp.zeros((slots, in_width), low), piece], axis=0)
                pieces.append(piece)
        return jnp.concatenate(pieces, axis=1)

    def moments(values):
        weighted = values * weight_band
        return (
            jnp.sum(weighted, axis=0, keepdims=True),
            jnp.sum(weighted * values, axis=0, keepdims=True),
        )

    def add_up(old, new):
        return [a + b for a, b in zip(old, new)]

    none = jnp.zeros((1, width), f32)
    main_sums, side_sums = [none, none], [none, none]
    for j in range(side):
        here = pl.ds(j * band, band)
        low_rows = low_one[3 if j == 0 else 0 :].reshape(-1, width)
        value = jnp.dot(image_taps(j), low_rows, preferred_element_type=f32)
        main_pre[here, :] = value
        main_sums = add_up(main_sums, moments(value))
        value = jnp.dot(
            xs[0, j, 0].reshape(band, in_width), low_short[0], preferred_element_type=f32
        )
        side_pre[here, :] = value
        side_sums = add_up(side_sums, moments(value))

    count = jnp.broadcast_to(jnp.sum(valid_column, axis=0, keepdims=True), (1, width))
    pl.semaphore_wait(barrier, len(others))
    copies = exchange_start(
        0, pack_rows(main_sums + side_sums + [count])
    )
    square[...] = jnp.zeros_like(square)
    cast_weight(grad_two, low_two, square, range(5), width, fetch_two)
    copies = exchange_middle(0, copies)
    cast_weight(grad_two, low_two, square, range(5, 9), width, fetch_two)
    scales[1] = scale_from(square[...], grad_two.size)
    border = jnp.zeros((side, 1, slots, width), low)
    active[:, 0:1] = border
    active[:, side + 1 :] = border
    back_two[:, 0:1] = border
    back_two[:, side + 1 :] = border
    back_one[:, side:] = border
    head_pad[...] = jnp.zeros_like(head_pad)
    head_pad[:classes, :] = head_ref[...]
    head = head_pad[:16, :]
    scales[3] = scale_from(head * head, head_ref.size)
    params = norm_ref[...]
    scales[4] = scale_from(params * params, norm_ref.size)
    sums = exchange_end(0, copies)
    sums = [unpack_row(sums, k) for k in range(5)]

    valid_count = sums[4]
    count_ref[...] = valid_count[:, :1]
    denominator = jnp.maximum(valid_count, 1.0)
    pixels = denominator * pixel_count
    gains = [norm_ref[k : k + 1, :] for k in range(6)]
    mean_one, inv_one, slope_one, base_one = settle_rows(
        (sums[0], sums[1]), pixels, gains[0], gains[1]
    )
    mean_side, inv_side, slope_side, base_side = settle_rows(
        (sums[2], sums[3]), pixels, gains[4], gains[5]
    )

    for j in range(side):
        hidden = main_pre[pl.ds(j * band, band), :] * slope_one + base_one
        active[j, 1 : side + 1] = (
            (hidden * gate(hidden)).astype(low).reshape(side, slots, width)
        )
    two_sums = [none, none]
    for j in range(side):
        taps = [b for b in range(3) if 0 <= j + b - 1 < side]
        pieces = [
            active[j + b - 1, a : a + side].reshape(band, width) for b in taps for a in range(3)
        ]
        low_rows = low_two[3 * taps[0] : 3 * taps[-1] + 3].reshape(-1, width)
        value = jnp.dot(jnp.concatenate(pieces, axis=1), low_rows, preferred_element_type=f32)
        main_two[pl.ds(j * band, band), :] = value
        two_sums = add_up(two_sums, moments(value))
    copies = exchange_start(1, pack_rows(two_sums))
    for j in range(side):
        block = active[j, 1 : side + 1].reshape(band, width)
        active_t[:, j * band : (j + 1) * band] = block.T
    label_column = column_of(label_ref[...].astype(f32), slots).astype(jnp.int32)
    head_low = head_pad[...].astype(low)
    copies = exchange_middle(1, copies)
    for across in range(2):
        for down in range(2):
            for j in range(side):
                block = xs[across, j, down].reshape(band, in_width)
                xs_t[across, down, :, j * band : (j + 1) * band] = block.T
    sums = exchange_end(1, copies)
    sums = [unpack_row(sums, k) for k in range(2)]
    mean_two, inv_two, slope_two, base_two = settle_rows(
        (sums[0], sums[1]), pixels, gains[2], gains[3]
    )

    base_joined = base_two + base_side

    quarters = [slice(128 * q, 128 * (q + 1)) for q in range(width // 128)]

    def joined_of(here, lanes):
        return (
            main_two[here, lanes] * slope_two[:, lanes]
            + side_pre[here, lanes] * slope_side[:, lanes]
            + base_joined[:, lanes]
        )

    pooled = []
    for lanes in quarters:
        total_joined = jnp.zeros((slots, 128), f32)
        for p in range(pixel_count):
            joined = joined_of(pl.ds(p * slots, slots), lanes)
            total_joined = total_joined + joined * gate(joined)
        pooled.append(total_joined)
    pooled = jnp.concatenate(pooled, axis=1)
    pooled = (pooled / pixel_count).astype(low)
    logits = lax.dot_general(
        pooled, head_low, (((1,), (1,)), ((), ())), preferred_element_type=f32
    )
    lane = lax.broadcasted_iota(jnp.int32, logits.shape, 1)
    real = lane < classes
    largest = jnp.max(jnp.where(real, logits, -jnp.inf), axis=1, keepdims=True)
    powers = jnp.where(real, jnp.exp(jnp.where(real, logits - largest, 0.0)), 0.0)
    total_power = jnp.sum(powers, axis=1, keepdims=True)
    onehot = jnp.where(lane == label_column, 1.0, 0.0)
    entropy = largest + jnp.log(total_power) - jnp.sum(onehot * logits, axis=1, keepdims=True)
    loss = jnp.sum(entropy * valid_column, axis=0, keepdims=True)
    grad_logits = (
        (powers / total_power - onehot) * (valid_column / denominator[:, :1])
    ).astype(low)
    grad_head = lax.dot_general(
        grad_logits, pooled, (((0,), (0,)), ((), ())), preferred_element_type=f32
    )[:16]
    grad_pooled = jnp.dot(grad_logits, head_low, preferred_element_type=f32) / pixel_count

    join_sums = []
    for lanes in quarters:
        three = [jnp.zeros((8, 128), f32)] * 3
        for p in range(pixel_count):
            here = pl.ds(p * slots, slots)
            joined = joined_of(here, lanes)
            opened = gate(joined)
            grad = grad_pooled[:, lanes] * (opened * (1.0 + joined * (1.0 - opened)))
            normed_two = (main_two[here, lanes] - mean_two[:, lanes]) * inv_two[:, lanes]
            normed_side = (side_pre[here, lanes] - mean_side[:, lanes]) * inv_side[:, lanes]
            new = (grad * normed_two, grad * normed_side, grad)
            three = [old + fold(each) for old, each in zip(three, new)]
            back_two[p // side, 1 + p % side, :, lanes] = (grad * slope_two[:, lanes]).astype(low)
            back_side[here, lanes] = (grad * slope_side[:, lanes]).astype(low)
        join_sums.append([jnp.sum(each, axis=0, keepdims=True) for each in three])
    gain_two, gain_side, shift_two = [jnp.concatenate(each, axis=1) for each in zip(*join_sums)]

    for b in range(3):
        first, last = max(0, b - 1), min(side, side + b - 1)
        left = active_t[:, first * band : last * band]
        for a in range(3):
            right = back_two[first - b + 1 : last - b + 1, 2 - a : 2 - a + side]
            grad_two[pl.ds((a * 3 + b) * width, width), :] = jnp.dot(
                left, right.reshape(-1, width), preferred_element_type=f32
            )

    def nothing():
        pass

    def matrix_votes(k, grad, between, after):
        here = pl.ds(k * width, width)
        start = edges[k - 1] if k else 0
        col_new[:, here] = factored_votes(
            grad,
            grad.shape[0],
            start,
            row_ref,
            row_new,
            col_ref[:, here],
            level,
            out_ref,
            start,
            between,
            after,
        )

    kept = {}

    def tail_step():
        sums = exchange_end(2, kept["tail"])
        loss_ref[...] = sums[GROUP : GROUP + 1, :1]
        sums = sums[:GROUP]
        old = jnp.concatenate([head_ref[...], norm_ref[...]], axis=0)
        old = jnp.concatenate([old[:, 128 * q : 128 * (q + 1)] for q in range(4)], axis=0)
        down = lax.broadcasted_iota(jnp.int32, (GROUP, 128), 0)
        scale = jnp.where(lax.rem(down, TAIL) < classes, scales[3], scales[4])
        fresh = old - scale * jnp.tanh(sums * root)
        both = jnp.concatenate([sums, fresh], axis=0)
        high = both.astype(low)
        rest = both - high.astype(f32)
        middle = rest.astype(low)
        parts = jnp.concatenate([high, middle, (rest - middle.astype(f32)).astype(low)], axis=0)
        length = 128 * classes
        gap = lax.broadcasted_iota(jnp.int32, (128, length), 1) - classes * (
            lax.broadcasted_iota(jnp.int32, (128, length), 0)
        )
        chosen = jnp.where(jnp.logical_and(gap >= 0, gap < classes), 1.0, 0.0).astype(low)
        moved = jnp.dot(parts, chosen, preferred_element_type=f32)
        moved = moved[: 2 * GROUP] + moved[2 * GROUP : 4 * GROUP] + moved[4 * GROUP :]
        place_of = lax.broadcasted_iota(jnp.int32, (TAIL, length), 1).astype(f32)
        class_of = place_of - classes * jnp.floor((place_of + 0.5) / classes)
        here = lax.broadcasted_iota(jnp.int32, (TAIL, length), 0).astype(f32) == class_of
        for which, ref in enumerate((tail_vote, tail_new)):
            for q in range(4):
                block = moved[GROUP * which + TAIL * q : GROUP * which + TAIL * (q + 1)]
                line = jnp.sum(jnp.where(here, block, 0.0), axis=0, keepdims=True)
                for k in range(classes):
                    ref[classes * q + k : classes * q + k + 1, :] = line[:, 128 * k : 128 * (k + 1)]
                for k in range(TAIL - classes):
                    at = 4 * (classes + k) + q
                    row = TAIL * q + classes + k
                    ref[at : at + 1, :] = (sums, fresh)[which][row : row + 1]
        out_ref[pl.ds(32 * SPAN, GROUP), :] = tail_new[...].astype(low)

    def return_slots(slots_here):
        mine = [own_group(u) for u in range(len(units))]
        for slot in slots_here:
            group = me * spare + slot
            own = group < 0
            for u, unit in enumerate(units):
                inside = jnp.logical_and(group >= mine[u], group < mine[u] + unit[1])
                own = jnp.logical_or(own, inside)

            @pl.when(jnp.logical_and(jnp.logical_not(own), group < groups - 1))
            def _():
                land(0, group, me, slot, 0)[0].wait_recv()

        first, last = slots_here[0], min(slots_here[-1] + 1, spare)
        here = pl.ds(first * GROUP, (last - first) * GROUP)
        total[here, :] = landed[here, :].astype(f32)

        @pl.loop(first, last)
        def _(k):
            row = pl.multiple_of(k * 16, 16)
            renew(row, first_row + row)

    def return_step(part):
        if part == 0:
            pltpu.make_async_copy(
                weight.at[pl.ds(0, OWN)], weight.at[pl.ds(0, OWN)], fetch_sem.at[7]
            ).wait()
            return_slots(range(0, 7))
        elif part == 1:
            return_slots(range(7, spare + 1))
        else:

            @pl.when(me < 31)
            def _():
                pltpu.make_async_copy(
                    weight.at[pl.ds(OWN, TAIL)], weight.at[pl.ds(OWN, TAIL)], fetch_sem.at[8]
                ).wait()
                total[pl.ds(SPAN, GROUP), :] = landed[pl.ds(SPAN, GROUP), :].astype(f32)
                renew(OWN, first_row + OWN)

            @pl.when(me == 31)
            def _():
                vote_flat[pl.ds(SPAN, GROUP), :] = tail_vote[...]
                new_flat[pl.ds(SPAN, GROUP), :] = tail_new[...]

            shift = 2 * me
            share = vote_ref.shape[0]
            vote_ref[...] = vote_flat[pl.ds(shift, share), :]
            new_ref[...] = new_flat[pl.ds(shift, share), :]

    in_flight = {}
    steps = (
        lambda u, copy: scatter_start(u),
        scatter_one,
        scatter_two,
        scatter_three,
        lambda u, copy: own_block(u),
        lambda u, copy: gather_one(u),
        gather_two,
        gather_three,
        lambda u, copy: tail_step(),
        lambda u, copy: return_step(u),
    )

    def go(number, u):
        got = steps[number](u, in_flight.get(u))
        if number < 8:
            in_flight[u] = got

    def turn(number):
        for step_number, u in SCHEDULE[number]:
            go(step_number, u)

    early = edges[1] // 512 - edges[0] // 512
    matrix_votes(1, grad_two, (nothing, nothing), lambda k: go(0, k) if k < 2 else None)
    turn(0)
    grad_short[...] = jnp.dot(xs_t[0, 0], back_side[...], preferred_element_type=f32)
    matrix_votes(2, grad_short, (nothing, nothing), lambda k: None)

    gain_one, shift_one = none, none
    for j in range(side):
        taps = [b for b in range(3) if 0 <= j - b + 1 < side]
        pieces = [
            back_two[j - b + 1, 2 - a : 2 - a + side].reshape(band, width)
            for b in taps
            for a in range(3)
        ]
        weights = jnp.concatenate([low_two[b * 3 + a] for b in taps for a in range(3)], axis=1)
        grad = lax.dot_general(
            jnp.concatenate(pieces, axis=1),
            weights,
            (((1,), (1,)), ((), ())),
            preferred_element_type=f32,
        )
        before = main_pre[pl.ds(j * band, band), :]
        hidden = before * slope_one + base_one
        opened = gate(hidden)
        grad = grad * (opened * (1.0 + hidden * (1.0 - opened)))
        shift_one = shift_one + jnp.sum(grad, axis=0, keepdims=True)
        gain_one = gain_one + jnp.sum(
            grad * ((before - mean_one) * inv_one), axis=0, keepdims=True
        )
        back_one[j, :side] = (grad * slope_one).astype(low).reshape(side, slots, width)
        turn(1 + j)

    square_head = grad_head * grad_head + EPS_ROW
    real = lax.broadcasted_iota(jnp.int32, square_head.shape, 0) < classes
    square_head = jnp.where(real, square_head, 0.0)
    head_lanes = pl.ds(edges[2], width)
    old = row_ref[:, head_lanes]
    row = keep * old + (1.0 - keep) * jnp.sum(square_head, axis=0, keepdims=True) / classes
    row_new[:, head_lanes] = row
    diagonal = eye_mask(16, classes)
    old = jnp.broadcast_to(col_ref[:, 3 * width :], (16, classes))
    old = jnp.sum(jnp.where(diagonal, old, 0.0), axis=1, keepdims=True)
    column = keep * old + (1.0 - keep) * jnp.sum(square_head, axis=1, keepdims=True) / width
    col_new[:, 3 * width :] = jnp.sum(
        jnp.where(diagonal, jnp.broadcast_to(column, (16, classes)), 0.0), axis=0, keepdims=True
    )
    real_column = lax.broadcasted_iota(jnp.int32, column.shape, 0) < classes
    column = jnp.where(real_column, column, 1.0)
    mean = jnp.sum(row, axis=1, keepdims=True) / width
    raw = grad_head * (lax.rsqrt(row) * jnp.sqrt(mean)) * lax.rsqrt(column)
    clip = jnp.maximum(1.0, jnp.sqrt(total_of(raw * raw) / (classes * width)))
    head_votes = jnp.tanh(raw / clip)[:classes]

    raws = []
    for k, grad in enumerate((gain_one, shift_one, gain_two, shift_two, gain_side, shift_two)):
        here = pl.ds(k * width, width)
        moment = keep * moment_ref[:, here] + (1.0 - keep) * (grad * grad + EPS_ROW)
        moment_new[:, here] = moment
        raws.append(grad * lax.rsqrt(moment))
    raw = jnp.concatenate(raws, axis=0)
    clip = jnp.maximum(1.0, jnp.sqrt(total_of(raw * raw) / raw.size))
    norm_votes = jnp.tanh(raw / clip)
    tail_votes = jnp.concatenate([head_votes, norm_votes], axis=0)
    kept["tail"] = exchange_start(
        2,
        jnp.concatenate(
            [tail_votes[:, 128 * q : 128 * (q + 1)] for q in range(4)]
            + [jnp.broadcast_to(loss, (8, 128))],
            axis=0,
        ),
    )


    for b in range(3):
        first, last = (0, side - 1) if b == 0 else (0, side)
        shift = 1 if b == 0 else 0
        for a in range(3):
            left = xs_t[0 if b == 1 else 1, 0 if a == 1 else 1, :, first * band : last * band]
            start = 1 if a == 0 else 0
            right = back_one[first + shift : last + shift, start : start + side]
            grad_one[pl.ds((a * 3 + b) * in_width, in_width), :] = jnp.dot(
                left, right.reshape(-1, width), preferred_element_type=f32
            )
        if b == 1:
            kept["tail"] = exchange_middle(2, kept["tail"])
        turn(5 + b)

    matrix_votes(
        0,
        grad_one,
        (lambda: turn(8), lambda: turn(9)),
        lambda k: go(0, early + k) if k < 2 else None,
    )
    turn(10)
    for away, copy in passes:

        @pl.when(away)
        def _():
            copy.wait_send()

    three = deep_in.at[pl.ds(0, 3 * SPAN)]
    for kind, ref in enumerate((None, wide_in, deep_in, three, three, deep_in, wide_in, core_in)):
        if kind:
            sent_all(kind, ref)
    for u in range(len(units)):
        in_flight[u].wait_recv()


def finish_kernel(count, chunks, *refs):
    sources, targets, sem = refs[:count], refs[count : 2 * count], refs[2 * count]
    rows = sources[0].shape[0]
    step = -(-rows // chunks // 16) * 16
    copies = []
    for k in range(chunks):
        here = pl.ds(k * step, min(step, rows - k * step))
        copies.append(
            pltpu.make_async_copy(sources[0].at[here], targets[0].at[here], sem.at[k])
        )
    for k in range(1, count):
        copies.append(pltpu.make_async_copy(sources[k], targets[k], sem.at[chunks + k]))
    for copy in copies:
        copy.start()
    for copy in copies:
        copy.wait()


def finish(values):
    count, chunks = len(values), 4
    held = [pltpu.with_memory_space_constraint(value, pltpu.VMEM) for value in values]
    return pl.pallas_call(
        functools.partial(finish_kernel, count, chunks),
        out_shape=[jax.ShapeDtypeStruct(value.shape, value.dtype) for value in values],
        in_specs=[pl.BlockSpec(memory_space=pltpu.VMEM)] * count,
        out_specs=[pl.BlockSpec(memory_space=pl.ANY)] * count,
        scratch_shapes=[pltpu.SemaphoreType.DMA((chunks + count,))],
        compiler_params=pltpu.CompilerParams(vmem_limit_bytes=1024 * 1024),
        name="finish",
    )(*held)


def run_step(images, conv_one, conv_two, shortcut, head, norm_params, valid, labels, rows, cols, moment):
    vmem = pl.BlockSpec(memory_space=pltpu.VMEM)
    hbm = pl.BlockSpec(memory_space=pl.ANY)
    low, f32 = jnp.bfloat16, jnp.float32
    dma = pltpu.SemaphoreType.DMA
    workers = lax.axis_size("dp")
    slots, in_width = valid.shape[1], images.shape[1]
    width = conv_one.shape[1]
    pixels = images.shape[0] // 4
    shape = pltpu.VMEM
    edges = [conv_one.shape[0]]
    edges.append(edges[0] + conv_two.shape[0])
    edges.append(edges[1] + shortcut.shape[0])
    units = make_units(edges)
    flat = (edges[2] + TAIL) * width // 128
    share = flat // workers
    return pl.pallas_call(
        functools.partial(step_kernel, tuple(edges), tuple(units), 1.0 / math.sqrt(workers)),
        out_shape=(
            shape((share, 128), f32),
            shape((share, 128), f32),
            shape((flat, 128), low),
            shape(rows.shape, f32),
            shape(cols.shape, f32),
            shape(moment.shape, f32),
            shape((1, 1), f32),
            shape((1, 1), f32),
        ),
        in_specs=[hbm] * 4 + [vmem] * 7,
        out_specs=(vmem,) * 8,
        scratch_shapes=[
            pltpu.VMEM((2, 4, 2, 4, slots, in_width), low),
            pltpu.VMEM(conv_one.shape, f32),
            pltpu.VMEM(conv_two.shape, f32),
            pltpu.VMEM(shortcut.shape, f32),
            pltpu.VMEM((9, in_width, width), low),
            pltpu.VMEM((9, width, width), low),
            pltpu.VMEM((1, in_width, width), low),
            pltpu.VMEM((pixels, width), f32),
            pltpu.VMEM((pixels, width), f32),
            pltpu.VMEM((pixels, width), f32),
            pltpu.VMEM((4, 6, slots, width), low),
            pltpu.VMEM((4, 6, slots, width), low),
            pltpu.VMEM((4, 5, slots, width), low),
            pltpu.VMEM((pixels, width), low),
            pltpu.VMEM((width, pixels), low),
            pltpu.VMEM((2, 2, in_width, pixels), low),
            pltpu.VMEM((128, width), f32),
            pltpu.VMEM((conv_two.shape[0], 128), f32),
            pltpu.VMEM((8, width), f32),
            pltpu.VMEM((24, 128), f32),
            pltpu.VMEM((8, 24, 128), f32),
            pltpu.VMEM((4, 24, 128), f32),
            pltpu.VMEM((8, 128), f32),
            pltpu.VMEM((8, 8, 128), f32),
            pltpu.VMEM((4, 8, 128), f32),
            pltpu.VMEM((GROUP + 8, 128), f32),
            pltpu.VMEM((8, GROUP + 8, 128), f32),
            pltpu.VMEM((4, GROUP + 8, 128), f32),
            pltpu.VMEM((16 * SPAN, 128), low),
            pltpu.VMEM((8 * SPAN, 128), low),
            pltpu.VMEM((4 * SPAN, 128), low),
            pltpu.VMEM((4 * SPAN, 128), low),
            pltpu.VMEM((SPAN, 128), low),
            pltpu.VMEM((SPAN + GROUP, 128), low),
            pltpu.VMEM((SPAN + GROUP, 128), f32),
            pltpu.VMEM((OWN, width), f32),
            pltpu.VMEM((OWN + TAIL, width), f32),
            pltpu.VMEM((SPAN + GROUP, 128), f32),
            pltpu.VMEM((SPAN + GROUP, 128), f32),
            pltpu.VMEM((GROUP, 128), f32),
            pltpu.VMEM((GROUP, 128), f32),
            dma((9 + len(units),)),
            dma((3, 10)),
            dma((3, 10)),
            dma((8,)),
            dma((len(units), 3)),
            dma((len(units),)),
            dma((2 * OWN // 16,)),
            dma((OWN // 16 + 1,)),
            dma((len(units),)),
            dma((len(units), 3)),
            pltpu.SemaphoreType.REGULAR,
            dma((2,)),
        ],
        compiler_params=pltpu.CompilerParams(
            collective_id=1, has_side_effects=True, vmem_limit_bytes=54 * 1024 * 1024
        ),
        name="step",
    )(images, conv_one, conv_two, shortcut, head, norm_params, valid, labels, rows, cols, moment)


def scale_for(weight):
    return jnp.maximum(EPS_SCALE, jnp.sqrt(jnp.mean(weight * weight)))


def local_general(
    images,
    valid_slot,
    labels,
    conv_one,
    conv_two,
    shortcut,
    classifier,
    norm_params,
    row_state,
    col_state,
    bn_moment,
):
    in_width = images.shape[3]
    width = conv_one.shape[1]
    kernel_one = conv_one.astype(jnp.bfloat16).reshape(3, 3, in_width, width)
    kernel_two = conv_two.astype(jnp.bfloat16).reshape(3, 3, width, width)
    kernel_short = shortcut.astype(jnp.bfloat16).reshape(1, 1, in_width, width)
    head_low = classifier.astype(jnp.bfloat16)
    slot_count = images.shape[0]
    out_side = images.shape[1] // 2
    pixel_count = out_side * out_side
    slot_weight = valid_slot.astype(jnp.float32)
    pixel_weight = jnp.broadcast_to(slot_weight[:, None], (slot_count, pixel_count)).reshape(-1, 1)
    main_pre, side_pre = first_section(images, kernel_one, kernel_short)
    main_sums = masked_moments(pixel_weight, main_pre)
    side_sums = masked_moments(pixel_weight, side_pre)
    count_row = jnp.broadcast_to(jnp.sum(slot_weight), (width,))
    first_sums = lax.psum(jnp.stack([*main_sums, *side_sums, count_row]), "dp")
    valid_count = first_sums[4, 0]
    denominator = jnp.maximum(valid_count, 1.0)
    pixels = denominator * pixel_count
    norm_one = settle(first_sums[0], first_sums[1], pixels)
    norm_side = settle(first_sums[2], first_sums[3], pixels)
    hidden_one, active, main_two = second_section(
        main_pre, norm_one, norm_params, kernel_two, slot_count, out_side
    )
    two_sums = masked_moments(pixel_weight, main_two)
    second_sums = lax.psum(jnp.stack([*two_sums]), "dp")
    norm_two = settle(second_sums[0], second_sums[1], pixels)
    joined_pre = (
        (main_two - norm_two[0]) * norm_two[1] * norm_params[2]
        + norm_params[3]
        + (side_pre - norm_side[0]) * norm_side[1] * norm_params[4]
        + norm_params[5]
    )
    joined = jax.nn.silu(joined_pre).reshape(slot_count, pixel_count, -1)
    pooled = jnp.mean(joined, axis=1).astype(jnp.bfloat16)
    logits = jnp.dot(pooled, head_low, preferred_element_type=jnp.float32)
    largest = jnp.max(logits, axis=1, keepdims=True)
    exp_terms = jnp.exp(logits - largest)
    total_exp = jnp.sum(exp_terms, axis=1, keepdims=True)
    log_total = largest[:, 0] + jnp.log(total_exp[:, 0])
    onehot = (labels[:, None] == jnp.arange(logits.shape[1], dtype=jnp.int32)[None, :]).astype(
        jnp.float32
    )
    local_sum = jnp.sum(slot_weight * (log_total - jnp.sum(onehot * logits, axis=1)))
    grad_logits = ((exp_terms / total_exp - onehot) * (slot_weight / denominator)[:, None]).astype(
        jnp.bfloat16
    )
    grad_head = lax.dot_general(
        pooled, grad_logits, (((0,), (0,)), ((), ())), preferred_element_type=jnp.float32
    )
    grad_pooled = lax.dot_general(
        grad_logits, head_low, (((1,), (1,)), ((), ())), preferred_element_type=jnp.float32
    )
    spread_pooled = jnp.broadcast_to(
        (grad_pooled / pixel_count)[:, None, :], (slot_count, pixel_count, width)
    )
    grad_joined = spread_pooled.reshape(slot_count * pixel_count, width) * silu_slope(joined_pre)
    gain_two, shift_two, grad_two = norm_backward(grad_joined, main_two, norm_two, norm_params[2])
    gain_side, shift_side, grad_side = norm_backward(
        grad_joined, side_pre, norm_side, norm_params[4]
    )
    grad_two_maps = grad_two.reshape(slot_count, out_side, out_side, width)
    grad_side_maps = grad_side.reshape(slot_count, out_side, out_side, width)
    grad_conv_two = conv_weight_grad(active, grad_two_maps, 1, 1, 1)
    grad_short = conv_weight_grad(images, grad_side_maps, 2, 0, -1)
    kernel_turned = jnp.transpose(kernel_two[::-1, ::-1], (0, 1, 3, 2))
    grad_active = conv_apply(grad_two_maps, kernel_turned, 1, 1).reshape(
        slot_count * pixel_count, width
    )
    grad_hidden = grad_active * silu_slope(hidden_one)
    gain_one, shift_one, grad_one = norm_backward(grad_hidden, main_pre, norm_one, norm_params[0])
    grad_conv_one = conv_weight_grad(
        images, grad_one.reshape(slot_count, out_side, out_side, width), 2, 1, 0
    )
    grad_norms = jnp.stack([gain_one, shift_one, gain_two, shift_two, gain_side, shift_side])
    grads = (grad_conv_one, grad_conv_two, grad_short, grad_head, grad_norms)
    votes, rows_new, cols_new, moment_new = make_votes(
        grads, row_state[0], col_state[0], bn_moment[0]
    )
    workers = lax.axis_size("dp")
    weights = (conv_one, conv_two, shortcut, classifier, norm_params)
    scales = [scale_for(weight) for weight in weights]
    loss_sum = lax.psum(local_sum, "dp")
    flat_vote = jnp.concatenate([vote.reshape(-1) for vote in votes])
    flat_old = jnp.concatenate([weight.reshape(-1) for weight in weights])
    flat_scale = jnp.concatenate(
        [
            jnp.broadcast_to(scale, (weight.size,))
            for scale, weight in zip(scales, weights)
        ]
    )
    vote_mine = lax.psum_scatter(flat_vote, "dp", tiled=True)
    share = vote_mine.shape[0]
    start = lax.axis_index("dp") * share
    new_mine = lax.dynamic_slice_in_dim(
        flat_old, start, share
    ) - lax.dynamic_slice_in_dim(flat_scale, start, share) * jnp.tanh(
        vote_mine / math.sqrt(workers)
    )
    copies = lax.all_gather(new_mine.astype(jnp.bfloat16), "dp", tiled=True)
    return (
        loss_sum,
        valid_count,
        new_mine,
        copies,
        vote_mine,
        rows_new[None, :],
        cols_new[None, :],
        moment_new[None, :],
    )


def local(
    images,
    valid_slot,
    labels,
    conv_one,
    conv_two,
    shortcut,
    classifier,
    norm_params,
    row_state,
    col_state,
    bn_moment,
):
    new_mine, vote_mine, copies, rows_new, cols_new, moment_new, loss_sum, valid_count = run_step(
        images.reshape(-1, images.shape[-1]),
        conv_one,
        conv_two,
        shortcut,
        classifier.T,
        norm_params,
        valid_slot.reshape(1, -1),
        labels.reshape(1, -1),
        row_state,
        col_state,
        bn_moment,
    )
    copies, new_mine, vote_mine, rows_new, cols_new, moment_new, loss_sum, valid_count = finish(
        (copies, new_mine, vote_mine, rows_new, cols_new, moment_new, loss_sum, valid_count)
    )
    return (
        loss_sum.reshape(()),
        valid_count.reshape(()),
        new_mine.reshape(-1),
        copies.reshape(-1),
        vote_mine.reshape(-1),
        rows_new,
        cols_new,
        moment_new,
    )


def solution(mesh):
    placed = (
        P("dp", None, None, None),
        P("dp"),
        P("dp"),
        P(),
        P(),
        P(),
        P(),
        P(),
        P("dp", None),
        P("dp", None),
        P("dp", None),
    )
    return jax.shard_map(
        local if mesh.shape["dp"] == 32 else local_general,
        mesh=mesh,
        in_specs=placed,
        out_specs=(P(), P(), P("dp"), P(), P("dp"), P("dp", None), P("dp", None), P("dp", None)),
        check_vma=False,
    )
```

```python
import functools
import math

import jax
import jax.numpy as jnp
from jax import lax
from jax.experimental import pallas as pl
from jax.experimental.pallas import tpu as pltpu
from jax.sharding import PartitionSpec as P

STEP = 10
MESH = pl.DeviceIdType.MESH

EPS_NORM = 1e-05
EPS_ROW = 1e-30
EPS_SCALE = 0.001
FORWARD_DIMS = ("NHWC", "HWIO", "NHWC")
WEIGHT_DIMS = ("CHWN", "IHWO", "HWNC")
OWN = 224
TAIL = 16
PIECE = 32
SPAN = 4 * OWN
HALF = SPAN // 2
GROUP = 64


def conv_apply(maps, kernel, stride, margin):
    return lax.conv_general_dilated(
        maps,
        kernel,
        (stride, stride),
        ((margin, margin), (margin, margin)),
        dimension_numbers=FORWARD_DIMS,
        preferred_element_type=jnp.float32,
    )


def conv_weight_grad(maps, grad_out, stride, low_pad, high_pad):
    result = lax.conv_general_dilated(
        maps,
        grad_out,
        (1, 1),
        ((low_pad, high_pad), (low_pad, high_pad)),
        rhs_dilation=(stride, stride),
        dimension_numbers=WEIGHT_DIMS,
        preferred_element_type=jnp.float32,
    )
    return result.reshape(-1, result.shape[3])


def silu_slope(values):
    sigmoid_part = jax.nn.sigmoid(values)
    return sigmoid_part * (1.0 + values * (1.0 - sigmoid_part))


def settle(sum_plain, sum_square, pixels):
    mean_value = sum_plain / pixels
    return (mean_value, lax.rsqrt(sum_square / pixels - mean_value * mean_value + EPS_NORM))


def first_section(images, kernel_one, kernel_short):
    row_count = images.shape[0] * (images.shape[1] // 2) ** 2
    main_pre = conv_apply(images, kernel_one, 2, 1).reshape(row_count, -1)
    side_pre = conv_apply(images, kernel_short, 2, 0).reshape(row_count, -1)
    return (main_pre, side_pre)


def second_section(main_pre, norm_one, norm_params, kernel_two, slot_count, out_side):
    hidden_one = (main_pre - norm_one[0]) * norm_one[1] * norm_params[0] + norm_params[1]
    active = (
        jax.nn.silu(hidden_one).astype(jnp.bfloat16).reshape(slot_count, out_side, out_side, -1)
    )
    main_two = conv_apply(active, kernel_two, 1, 1).reshape(slot_count * out_side * out_side, -1)
    return (hidden_one, active, main_two)


def masked_moments(pixel_weight, values):
    return (jnp.sum(pixel_weight * values, axis=0), jnp.sum(pixel_weight * values * values, axis=0))


def soft_sign(step_raw):
    clip_by = jnp.maximum(1.0, jnp.sqrt(jnp.mean(step_raw * step_raw)))
    return jnp.tanh(step_raw / clip_by)


def make_votes(grads, rows_old, cols_old, moment_old):
    decay_rate = 1.0 - STEP ** (-0.8)
    votes, rows_new, cols_new = ([], [], [])
    row_at, col_at = (0, 0)
    for matrix in grads[:4]:
        row_size, col_size = matrix.shape
        square = matrix * matrix + EPS_ROW
        row_part = decay_rate * rows_old[row_at : row_at + row_size] + (
            1.0 - decay_rate
        ) * jnp.mean(square, axis=1)
        col_part = decay_rate * cols_old[col_at : col_at + col_size] + (
            1.0 - decay_rate
        ) * jnp.mean(square, axis=0)
        second = row_part[:, None] * col_part[None, :] / jnp.mean(row_part)
        votes.append(soft_sign(matrix * lax.rsqrt(second)))
        rows_new.append(row_part)
        cols_new.append(col_part)
        row_at += row_size
        col_at += col_size
    flat_norm = grads[4].reshape(-1)
    moment_new = decay_rate * moment_old + (1.0 - decay_rate) * (flat_norm * flat_norm + EPS_ROW)
    votes.append(soft_sign(flat_norm * lax.rsqrt(moment_new)))
    return (votes, jnp.concatenate(rows_new), jnp.concatenate(cols_new), moment_new)


def norm_backward(grad_out, pre_value, norm_pair, gain_row):
    normed = (pre_value - norm_pair[0]) * norm_pair[1]
    grad_gain = jnp.sum(grad_out * normed, axis=0)
    grad_shift = jnp.sum(grad_out, axis=0)
    grad_pre = (grad_out * gain_row * norm_pair[1]).astype(jnp.bfloat16)
    return (grad_gain, grad_shift, grad_pre)


SCHEDULE = (
    (),
    (),
    (
        (1, 0), (0, 2),
    ),
    (
        (1, 1), (0, 3),
    ),
    (
        (1, 2), (0, 4),
    ),
    (
        (2, 0), (1, 3), (0, 5),
    ),
    (),
    (
        (2, 1), (1, 4), (0, 6),
    ),
    (
        (3, 0), (2, 2), (1, 5), (0, 7),
    ),
    (),
    (
        (3, 1), (2, 3), (1, 6), (0, 8),
    ),
    (
        (3, 2), (2, 4), (1, 7), (4, 0), (3, 3), (2, 5), (1, 8), (4, 1), (3, 4), (2, 6), (1, 9),
        (0, 11), (4, 2), (3, 5), (2, 7), (1, 10), (0, 12), (5, 0), (4, 3), (3, 6), (2, 8),
        (1, 11), (0, 13), (5, 1), (4, 4), (3, 7), (2, 9), (1, 12), (6, 0), (5, 2), (4, 5),
        (3, 8), (2, 10), (1, 13), (6, 1), (5, 3), (4, 6), (3, 9), (2, 11), (6, 2), (5, 4),
        (4, 7), (8, 0), (3, 10), (2, 12), (7, 0), (6, 3), (5, 5), (4, 8), (3, 11), (2, 13),
        (7, 1), (6, 4), (5, 6), (4, 9), (3, 12), (7, 2), (6, 5), (5, 7), (4, 10), (3, 13),
        (7, 3), (6, 6), (5, 8), (4, 11), (7, 4), (6, 7), (5, 9), (4, 12), (7, 5), (6, 8),
        (5, 10), (4, 13), (7, 6), (6, 9), (5, 11), (7, 7), (6, 10), (5, 12), (7, 8), (6, 11),
        (5, 13), (7, 9), (9, 0), (6, 12), (7, 10), (6, 13), (7, 11), (7, 12), (9, 1), (7, 13),
        (9, 2),
    ),
)


def place():
    me = lax.axis_index("dp")
    core = lax.rem(me, 2)
    x = lax.rem(lax.div(me, 2), 2)
    y = lax.rem(lax.div(me, 4), 2)
    z = lax.div(me, 8)
    return me, core, x, y, z


def send(src, dst, send_sem, recv_sem, partner):
    copy = pltpu.make_async_remote_copy(
        src_ref=src,
        dst_ref=dst,
        send_sem=send_sem,
        recv_sem=recv_sem,
        device_id=(partner,),
        device_id_type=MESH,
    )
    copy.start()
    return copy


def scale_of(row, scales, edges):
    picked = scales[2]
    picked = jnp.where(row < edges[1], scales[1], picked)
    return jnp.where(row < edges[0], scales[0], picked)


def make_units(edges):
    one, two, short = edges[0] // 16, edges[1] // 16, edges[2] // 16
    units = []
    for k in range((two - one) // 32):
        units.append((one + 32 * k, 1, k % 2 == 0, 16, (1, 1)))
    for k in range(one // 32):
        units.append((32 * k, 1, k % 2 == 1, 16, (0, 0)))
    at = one // 32 * 32
    assert one - at == 16 and short - two == 16
    units.append((at, 1, False, two - at, (0, 2)))
    return units


def settle_rows(sums, pixels, gain, shift):
    mean = sums[0] / pixels
    inv = lax.rsqrt(sums[1] / pixels - mean * mean + EPS_NORM)
    slope = gain * inv
    return mean, inv, slope, shift - mean * slope


def gate(values):
    return 0.5 * jnp.tanh(0.5 * values) + 0.5


def eye_mask(rows, columns, offset=0):
    down = lax.broadcasted_iota(jnp.int32, (rows, columns), 0) + offset
    return down == lax.broadcasted_iota(jnp.int32, (rows, columns), 1)


def column_of(row, size):
    spread = jnp.where(eye_mask(size, size), jnp.broadcast_to(row, (size, size)), 0)
    return jnp.sum(spread, axis=1, keepdims=True)


def total_of(values):
    return jnp.sum(jnp.sum(values, axis=0, keepdims=True), axis=1, keepdims=True)


def fold(values):
    return jnp.sum(values.reshape(values.shape[0] // 8, 8, values.shape[1]), axis=0)


def cast_weight(source, target, square_ref, taps, depth, fetches):
    step = 128
    for tap in taps:
        chunk = source.shape[0] // depth // len(fetches)
        if tap % chunk == 0:
            fetches[tap // chunk].wait()
        new_tap = (tap % 3) * 3 + tap // 3

        @pl.loop(0, depth // step)
        def _(k):
            start = pl.multiple_of(k * step, step)
            values = source[pl.ds(tap * depth + start, step), :]
            target[new_tap, pl.ds(start, step), :] = values.astype(jnp.bfloat16)
            square_ref[...] += fold(values * values)


def factored_votes(grad, rows, row_at, rows_old, rows_new, col_old, level, votes, vote_at, between, after):
    width = grad.shape[1]
    keep = 1.0 - STEP ** (-0.8)
    step = 128
    quarters = width // 128

    def first(k, carry):
        col_sum, row_sum = carry
        start = pl.multiple_of(k * step, step)
        lanes = pl.ds(pl.multiple_of(row_at + start, step), step)
        old = rows_old[:, lanes] * keep
        line = jnp.zeros((8, 128), jnp.float32)
        for m in range(step // 8):
            block = grad[pl.ds(start + 8 * m, 8), :]
            square = block * block
            col_sum = col_sum + square
            part = square[:, :128]
            for q in range(1, quarters):
                part = part + square[:, 128 * q : 128 * (q + 1)]
            part = part * ((1.0 - keep) / width)
            diagonal = eye_mask(8, 128, 8 * m)
            part = part + jnp.where(diagonal, jnp.broadcast_to(old, (8, 128)), 0.0)
            row = jnp.sum(part, axis=1, keepdims=True) + (1.0 - keep) * EPS_ROW
            row = jnp.broadcast_to(row, (8, 128))
            level[pl.ds(start + 8 * m, 8), :] = row
            row_sum = row_sum + row
            line = line + jnp.where(diagonal, row, 0.0)
        rows_new[:, lanes] = jnp.sum(line, axis=0, keepdims=True)
        return col_sum, row_sum

    col_sum, row_sum = lax.fori_loop(
        0,
        rows // step,
        first,
        (jnp.zeros((8, width), jnp.float32), jnp.zeros((8, 128), jnp.float32)),
    )
    col_new = keep * col_old + (1.0 - keep) * (
        jnp.sum(col_sum, axis=0, keepdims=True) / rows + EPS_ROW
    )
    scale = lax.rsqrt(col_new)
    root_mean = jnp.sqrt(jnp.sum(row_sum, axis=0, keepdims=True) / rows)

    def second(k, carry):
        start = pl.multiple_of(k * step, step)
        for m in range(step // 8):
            here = pl.ds(start + 8 * m, 8)
            factor = lax.rsqrt(level[here, :]) * root_mean
            level[here, :] = factor
            raw = grad[here, :] * scale
            power = raw * raw
            part = power[:, :128]
            for q in range(1, quarters):
                part = part + power[:, 128 * q : 128 * (q + 1)]
            carry = carry + part * (factor * factor)
        return carry

    between[0]()
    power = lax.fori_loop(0, rows // step, second, jnp.zeros((8, 128), jnp.float32))
    between[1]()
    clip = jnp.maximum(1.0, jnp.sqrt(total_of(power) / (rows * width)))
    scale = scale / clip

    def third(k, _):
        start = pl.multiple_of(k * step, step)
        for m in range(step // 16):
            here = pl.ds(start + 16 * m, 16)
            factor = level[here, :]
            factor = jnp.concatenate([factor] * quarters, axis=1)
            vote = jnp.tanh(grad[here, :] * factor * scale).astype(jnp.bfloat16)
            at = pl.multiple_of((vote_at + start) * 4 + GROUP * m, GROUP)
            for q in range(quarters):
                votes[pl.ds(at + 16 * q, 16), :] = vote[:, 128 * q : 128 * (q + 1)]
        return 0

    part = 512 // step
    for k in range(0, rows // step, part):
        lax.fori_loop(k, min(k + part, rows // step), third, 0)
        after(k // part)
    return col_new


def step_kernel(
    edges,
    units,
    root,
    images,
    one_hbm,
    two_hbm,
    short_hbm,
    head_ref,
    norm_ref,
    valid_ref,
    label_ref,
    row_ref,
    col_ref,
    moment_ref,
    new_ref,
    vote_ref,
    out_ref,
    row_new,
    col_new,
    moment_new,
    loss_ref,
    count_ref,
    xs,
    grad_one,
    grad_two,
    grad_short,
    low_one,
    low_two,
    low_short,
    main_pre,
    side_pre,
    main_two,
    active,
    back_two,
    back_one,
    back_side,
    active_t,
    xs_t,
    head_pad,
    level,
    square,
    post_one,
    plane_one,
    line_one,
    post_two,
    plane_two,
    line_two,
    tail_post,
    tail_plane,
    tail_line,
    core_in,
    wide_in,
    deep_in,
    line_in,
    sum_low,
    landed,
    total,
    own_weight,
    weight,
    vote_flat,
    new_flat,
    tail_vote,
    tail_new,
    fetch_sem,
    small_send,
    small_recv,
    sent,
    rs_recv,
    line_recv,
    pass_send,
    land_recv,
    spread_recv,
    ag_recv,
    free_sem,
    load_sem,
):
    slots, in_width = xs.shape[4:]
    width = main_pre.shape[1]
    side = 4
    band = side * slots
    pixel_count = side * side
    side_pixels = 4 * pixel_count
    classes = head_ref.shape[0]
    keep = 1.0 - STEP ** (-0.8)
    low = jnp.bfloat16
    f32 = jnp.float32

    me, core, x, y, z = place()
    flip_core = me + 1 - 2 * core
    flip_x = me + 2 - 4 * x
    flip_y = me + 4 - 8 * y
    spot = lax.rem(me, 8)
    near = [z * 8 + lax.rem(spot + k, 8) for k in range(1, 8)]
    far = [lax.rem(z + k, 4) * 8 + spot for k in range(1, 4)]
    others = [lax.rem(me + k, 32) for k in range(1, 32)]

    count = images.shape[0]
    loads = []
    for half in range(2):
        lanes = slice(128 * half, 128 * (half + 1))
        loads.append(
            pltpu.make_async_copy(
                images.at[:, lanes], core_in.at[pl.ds(half * count, count)], load_sem.at[half]
            )
        )
        loads[half].start()

    def chunks_of(source, target, first, count):
        rows = source.shape[0] // count
        return [
            pltpu.make_async_copy(
                source.at[pl.ds(k * rows, rows)],
                target.at[pl.ds(k * rows, rows)],
                fetch_sem.at[first + k],
            )
            for k in range(count)
        ]

    fetch_one = chunks_of(one_hbm, grad_one, 0, 3)
    fetch_short = chunks_of(short_hbm, grad_short, 3, 1)
    fetch_two = chunks_of(two_hbm, grad_two, 4, 3)
    for fetch in fetch_one + fetch_short:
        fetch.start()
    barrier = pltpu.get_barrier_semaphore()
    for partner in others:
        pl.semaphore_signal(barrier, inc=1, device_id=(partner,), device_id_type=MESH)

    def fetch_rows(row, count, place_at, sem):
        parts = (
            (one_hbm, 0, edges[0]),
            (two_hbm, edges[0], edges[1]),
            (short_hbm, edges[1], edges[2]),
        )
        for ref, first, last in parts:

            @pl.when(jnp.logical_and(row >= first, row < last))
            def _():
                start = pl.multiple_of(row - first, count)
                pltpu.make_async_copy(
                    ref.at[pl.ds(start, count)], weight.at[pl.ds(place_at, count)], sem
                ).start()

    first_row = me * OWN

    for half in range(2):
        lanes = slice(128 * half, 128 * (half + 1))
        loads[half].wait()
        apart = side_pixels + 8

        @pl.loop(0, slots // 4)
        def _(k):
            for m in range(4):
                slot = k * 4 + m
                source = pl.multiple_of(half * count + slot * side_pixels, side_pixels)
                target = pl.multiple_of(slot * apart, 8)
                level[pl.ds(target, side_pixels), :] = core_in[
                    pl.ds(source, side_pixels), :
                ].astype(f32)

        for h in range(2 * side):
            for w in range(2 * side):
                rows = level[pl.ds(2 * side * h + w, slots, stride=apart), :]
                xs[w % 2, w // 2, h % 2, h // 2, :, lanes] = rows.astype(low)

    scales = {}

    def scale_from(weight_square, size):
        return jnp.maximum(EPS_SCALE, jnp.sqrt(total_of(weight_square) / size))

    exchanges = (
        (post_one, plane_one, line_one),
        (post_two, plane_two, line_two),
        (tail_post, tail_plane, tail_line),
    )

    def exchange_start(which, values):
        mine_ref, plane_ref, _ = exchanges[which]
        mine_ref[...] = values
        plane_ref[spot] = values
        return [
            send(
                mine_ref,
                plane_ref.at[spot],
                small_send.at[which, k],
                small_recv.at[which, k],
                partner,
            )
            for k, partner in enumerate(near)
        ]

    def pack_rows(rows):
        pieces = [row[:, 128 * q : 128 * (q + 1)] for row in rows for q in range(4)]
        pad = -len(pieces) % 8
        if pad:
            pieces.append(jnp.zeros((pad, 128), f32))
        return jnp.concatenate(pieces, axis=0)

    def unpack_row(lines_in, k):
        return jnp.concatenate([lines_in[4 * k + q : 4 * k + q + 1] for q in range(4)], axis=1)

    def exchange_middle(which, copies):
        _, plane_ref, line_ref = exchanges[which]
        for copy in copies:
            copy.wait()
        line_ref[z] = functools.reduce(lambda a, b: a + b, [plane_ref[k] for k in range(8)])
        return [
            send(
                line_ref.at[z],
                line_ref.at[z],
                small_send.at[which, 7 + k],
                small_recv.at[which, 7 + k],
                partner,
            )
            for k, partner in enumerate(far)
        ]

    def exchange_end(which, copies):
        line_ref = exchanges[which][2]
        for copy in copies:
            copy.wait()
        return (line_ref[0] + line_ref[1]) + (line_ref[2] + line_ref[3])

    def lines(start, count):
        return pl.ds(pl.multiple_of(start, 16), count)

    sizes = [GROUP * unit[1] for unit in units]
    starts = [sum(sizes[:k]) for k in range(len(units) + 1)]

    def part_of(ref, u, share, start, count):
        return ref.at[lines(share * starts[u] + start, count)]

    def places(u):
        if units[u][2]:
            return x, y, flip_x, flip_y
        return y, x, flip_y, flip_x

    def unit_start(u, cc):
        return GROUP * units[u][0] + cc * (GROUP * units[u][3])

    def own_group(u):
        first, second, _, _ = places(u)
        return units[u][0] + core * units[u][3] + (first * 8 + second * 4 + z) * units[u][1]

    def halve(source, target, u, stage, partner):
        return send(source, target, sent.at[stage], rs_recv.at[u, stage], partner)

    def scatter_start(u):
        size = 16 * sizes[u]
        return halve(
            out_ref.at[lines(unit_start(u, 1 - core), size)],
            part_of(core_in, u, 16, 0, size),
            u,
            0,
            flip_core,
        )

    def add_to(ref, u, share, source_ref, source_start):
        size = share * sizes[u]
        here = lines(share * starts[u], size)
        ref[here, :] = ref[here, :] + source_ref[lines(source_start, size), :]

    def sent_all(kind, ref):
        pltpu.make_async_remote_copy(
            src_ref=ref,
            dst_ref=ref,
            send_sem=sent.at[kind],
            recv_sem=rs_recv.at[0, 0],
            device_id=(flip_core,),
            device_id_type=MESH,
        ).wait_send()

    def scatter_one(u, copy):
        copy.wait_recv()
        add_to(core_in, u, 16, out_ref, unit_start(u, core))
        if u == len(units) - 1:
            sent_all(0, core_in)
            pl.semaphore_signal(free_sem, inc=1, device_id=(flip_core,), device_id_type=MESH)
        first, _, flip_first, _ = places(u)
        size = 8 * sizes[u]
        return halve(
            part_of(core_in, u, 16, (1 - first) * size, size),
            part_of(wide_in, u, 8, 0, size),
            u,
            1,
            flip_first,
        )

    def scatter_two(u, copy):
        copy.wait_recv()
        first, second, _, flip_second = places(u)
        add_to(wide_in, u, 8, core_in, 16 * starts[u] + first * 8 * sizes[u])
        size = 4 * sizes[u]
        return halve(
            part_of(wide_in, u, 8, (1 - second) * size, size),
            part_of(deep_in, u, 4, 0, size),
            u,
            2,
            flip_second,
        )

    def line_copy(u, k):
        plane_to = lax.rem(z + k, 4)
        return pltpu.make_async_remote_copy(
            src_ref=part_of(deep_in, u, 4, plane_to * sizes[u], sizes[u]),
            dst_ref=part_of(line_in, u, 4, z * sizes[u], sizes[u]),
            send_sem=sent.at[3],
            recv_sem=line_recv.at[u],
            device_id=(plane_to * 8 + spot,),
            device_id_type=MESH,
        )

    def scatter_three(u, copy):
        copy.wait_recv()
        _, second, _, _ = places(u)
        add_to(deep_in, u, 4, wide_in, 8 * starts[u] + second * 4 * sizes[u])
        for k in (3, 2, 1):
            line_copy(u, k).start()
        here = lines(4 * starts[u] + z * sizes[u], sizes[u])
        line_in[here, :] = deep_in[here, :]

    def three_landed(u, sem):
        ref = part_of(line_in, u, 4, 0, 3 * sizes[u])
        pltpu.make_async_remote_copy(
            src_ref=ref,
            dst_ref=ref,
            send_sem=sent.at[3],
            recv_sem=sem.at[u],
            device_id=(far[0],),
            device_id_type=MESH,
        ).wait_recv()

    groups = (edges[2] + TAIL) // 16
    spare = (groups - 1) // 32
    passes = []

    def land(local, group, to, slot, index):
        source = sum_low.at[lines(local * GROUP, GROUP)]
        target = landed.at[lines(slot * GROUP, GROUP)]
        copy = pltpu.make_async_remote_copy(
            src_ref=source,
            dst_ref=target,
            send_sem=pass_send.at[index],
            recv_sem=land_recv.at[slot],
            device_id=(to,),
            device_id_type=MESH,
        )
        return copy, source, target

    def pass_on(u):
        for m in range(units[u][1]):
            local = starts[u] // GROUP + m
            group = own_group(u) + m
            to, slot = lax.div(group, spare), lax.rem(group, spare)

            def one(receiver, at, index):
                copy, source, target = land(local, group, receiver, at, index)

                @pl.when(receiver != me)
                def _():
                    copy.start()

                @pl.when(receiver == me)
                def _():
                    target[...] = source[...]

                return copy

            first = jnp.logical_and(slot == 0, group > 0)
            ahead = lax.rem(to + 31, 32)
            passes.append((to != me, one(to, slot, 2 * local)))

            @pl.when(first)
            def _():
                one(ahead, spare, 2 * local + 1)

            copy = land(local, group, ahead, spare, 2 * local + 1)[0]
            passes.append((jnp.logical_and(first, ahead != me), copy))

    def flat_rows(row, q, values, ref):
        ref[pl.ds(row * 4 + q, 8, stride=4), :] = values

    def old_rows(u, cc):
        matrix = units[u][4][cc]
        base = edges[matrix - 1] if matrix else 0
        return (one_hbm, two_hbm, short_hbm)[matrix], 16 * own_group(u) - base, 16 * units[u][1]

    def own_fetch(u):
        target = own_weight.at[pl.ds(starts[u] // 4, 16 * units[u][1])]
        matrices = units[u][4]
        for cc in range(2):
            if cc and matrices[0] == matrices[1]:
                continue

            @pl.when((core == cc) if matrices[0] != matrices[1] else (core >= 0))
            def _():
                ref, row, count = old_rows(u, cc)
                pltpu.make_async_copy(
                    ref.at[pl.ds(pl.multiple_of(row, 16), count)], target, fetch_sem.at[9 + u]
                ).start()

    def spread_copy(u, k):
        own = out_ref.at[lines(own_group(u) * GROUP, sizes[u])]
        return pltpu.make_async_remote_copy(
            src_ref=own,
            dst_ref=own,
            send_sem=sent.at[4],
            recv_sem=spread_recv.at[u],
            device_id=(far[k - 1],),
            device_id_type=MESH,
        )

    def own_block(u):
        size = sizes[u]
        three_landed(u, line_recv)
        here = pl.ds(starts[u], size)
        low_sum = functools.reduce(
            lambda a, b: a + b,
            [line_in[pl.ds(4 * starts[u] + t * size, size), :].astype(f32) for t in range(4)],
        ).astype(low)
        sum_low[here, :] = low_sum
        summed = low_sum.astype(f32)
        target = own_weight.at[pl.ds(starts[u] // 4, 16 * units[u][1])]
        pltpu.make_async_copy(target, target, fetch_sem.at[9 + u]).wait()
        matrices = units[u][4]
        scale = scales[matrices[0]]
        if matrices[0] != matrices[1]:
            scale = jnp.where(core == 0, scale, scales[matrices[1]])
        turned = jnp.tanh(summed * root) * scale
        for m in range(units[u][1]):
            row = starts[u] // 4 + 16 * m
            for part in (0, 8):
                for q in range(4):
                    at = GROUP * m + 16 * q + part
                    old = own_weight[pl.ds(row + part, 8), 128 * q : 128 * (q + 1)]
                    flat_rows(row + part, q, old - turned[at : at + 8], new_flat)
        out_ref[lines(own_group(u) * GROUP, size), :] = new_flat[here, :].astype(low)
        for k in (3, 2, 1):
            spread_copy(u, k).start()
        pass_on(u)

    def piece(rows, u, stage, partner):
        return send(
            out_ref.at[rows], out_ref.at[rows], sent.at[5 + stage], ag_recv.at[u, stage], partner
        )

    def gather_one(u):
        three_landed(u, spread_recv)
        first, second, _, flip_second = places(u)
        size = 4 * sizes[u]
        start = unit_start(u, core) + (2 * first + second) * size
        return piece(lines(start, size), u, 0, flip_second)

    def gather_two(u, copy):
        copy.wait_recv()
        first, _, flip_first, _ = places(u)
        size = 8 * sizes[u]
        return piece(lines(unit_start(u, core) + first * size, size), u, 1, flip_first)

    def gather_three(u, copy):
        copy.wait_recv()
        if u == 0:
            pl.semaphore_wait(free_sem, 1)
        return piece(lines(unit_start(u, core), 16 * sizes[u]), u, 2, flip_core)

    def renew(row, at_row):
        scale = scale_of(at_row, [scales[k] for k in range(3)], edges)
        for part in (0, 8):
            for q in range(4):
                summed = total[pl.ds(row * 4 + 16 * q + part, 8), :]
                old = weight[pl.ds(row + part, 8), 128 * q : 128 * (q + 1)]
                fresh = old - scale * jnp.tanh(summed * root)
                flat_rows(row + part, q, summed, vote_flat)
                flat_rows(row + part, q, fresh, new_flat)

    valid_column = column_of(valid_ref[...].astype(f32), slots)
    weight_slot = jnp.broadcast_to(valid_column, (slots, width))
    weight_band = jnp.concatenate([weight_slot] * side, axis=0)

    square[...] = jnp.zeros_like(square)
    cast_weight(grad_one, low_one, square, range(9), in_width, fetch_one)
    scales[0] = scale_from(square[...], grad_one.size)
    square[...] = jnp.zeros_like(square)
    cast_weight(grad_short, low_short, square, range(1), in_width, fetch_short)
    scales[2] = scale_from(square[...], grad_short.size)
    for fetch in fetch_two:
        fetch.start()
    for k in range(OWN // PIECE):
        fetch_rows(first_row + k * PIECE, PIECE, k * PIECE, fetch_sem.at[7])
    fetch_rows(first_row + OWN, TAIL, OWN, fetch_sem.at[8])
    for u in range(len(units)):
        own_fetch(u)

    def image_taps(j):
        pieces = []
        for b in range(3):
            column = j if b else j - 1
            if column < 0:
                continue
            across = 0 if b == 1 else 1
            for a in range(3):
                if a == 1:
                    piece = xs[across, column, 0].reshape(band, in_width)
                elif a == 2:
                    piece = xs[across, column, 1].reshape(band, in_width)
                else:
                    piece = xs[across, column, 1, : side - 1].reshape(band - slots, in_width)
                    piece = jnp.concatenate([jnp.zeros((slots, in_width), low), piece], axis=0)
                pieces.append(piece)
        return jnp.concatenate(pieces, axis=1)

    def moments(values):
        weighted = values * weight_band
        return (
            jnp.sum(weighted, axis=0, keepdims=True),
            jnp.sum(weighted * values, axis=0, keepdims=True),
        )

    def add_up(old, new):
        return [a + b for a, b in zip(old, new)]

    none = jnp.zeros((1, width), f32)
    main_sums, side_sums = [none, none], [none, none]
    for j in range(side):
        here = pl.ds(j * band, band)
        low_rows = low_one[3 if j == 0 else 0 :].reshape(-1, width)
        value = jnp.dot(image_taps(j), low_rows, preferred_element_type=f32)
        main_pre[here, :] = value
        main_sums = add_up(main_sums, moments(value))
        value = jnp.dot(
            xs[0, j, 0].reshape(band, in_width), low_short[0], preferred_element_type=f32
        )
        side_pre[here, :] = value
        side_sums = add_up(side_sums, moments(value))

    count = jnp.broadcast_to(jnp.sum(valid_column, axis=0, keepdims=True), (1, width))
    pl.semaphore_wait(barrier, len(others))
    copies = exchange_start(
        0, pack_rows(main_sums + side_sums + [count])
    )
    square[...] = jnp.zeros_like(square)
    cast_weight(grad_two, low_two, square, range(5), width, fetch_two)
    copies = exchange_middle(0, copies)
    cast_weight(grad_two, low_two, square, range(5, 9), width, fetch_two)
    scales[1] = scale_from(square[...], grad_two.size)
    border = jnp.zeros((side, 1, slots, width), low)
    active[:, 0:1] = border
    active[:, side + 1 :] = border
    back_two[:, 0:1] = border
    back_two[:, side + 1 :] = border
    back_one[:, side:] = border
    head_pad[...] = jnp.zeros_like(head_pad)
    head_pad[:classes, :] = head_ref[...]
    head = head_pad[:16, :]
    scales[3] = scale_from(head * head, head_ref.size)
    params = norm_ref[...]
    scales[4] = scale_from(params * params, norm_ref.size)
    sums = exchange_end(0, copies)
    sums = [unpack_row(sums, k) for k in range(5)]

    valid_count = sums[4]
    count_ref[...] = valid_count[:, :1]
    denominator = jnp.maximum(valid_count, 1.0)
    pixels = denominator * pixel_count
    gains = [norm_ref[k : k + 1, :] for k in range(6)]
    mean_one, inv_one, slope_one, base_one = settle_rows(
        (sums[0], sums[1]), pixels, gains[0], gains[1]
    )
    mean_side, inv_side, slope_side, base_side = settle_rows(
        (sums[2], sums[3]), pixels, gains[4], gains[5]
    )

    for j in range(side):
        hidden = main_pre[pl.ds(j * band, band), :] * slope_one + base_one
        active[j, 1 : side + 1] = (
            (hidden * gate(hidden)).astype(low).reshape(side, slots, width)
        )
    two_sums = [none, none]
    for j in range(side):
        taps = [b for b in range(3) if 0 <= j + b - 1 < side]
        pieces = [
            active[j + b - 1, a : a + side].reshape(band, width) for b in taps for a in range(3)
        ]
        low_rows = low_two[3 * taps[0] : 3 * taps[-1] + 3].reshape(-1, width)
        value = jnp.dot(jnp.concatenate(pieces, axis=1), low_rows, preferred_element_type=f32)
        main_two[pl.ds(j * band, band), :] = value
        two_sums = add_up(two_sums, moments(value))
    copies = exchange_start(1, pack_rows(two_sums))
    for j in range(side):
        block = active[j, 1 : side + 1].reshape(band, width)
        active_t[:, j * band : (j + 1) * band] = block.T
    label_column = column_of(label_ref[...].astype(f32), slots).astype(jnp.int32)
    head_low = head_pad[...].astype(low)
    copies = exchange_middle(1, copies)
    for across in range(2):
        for down in range(2):
            for j in range(side):
                block = xs[across, j, down].reshape(band, in_width)
                xs_t[across, down, :, j * band : (j + 1) * band] = block.T
    sums = exchange_end(1, copies)
    sums = [unpack_row(sums, k) for k in range(2)]
    mean_two, inv_two, slope_two, base_two = settle_rows(
        (sums[0], sums[1]), pixels, gains[2], gains[3]
    )

    base_joined = base_two + base_side

    quarters = [slice(128 * q, 128 * (q + 1)) for q in range(width // 128)]

    def joined_of(here, lanes):
        return (
            main_two[here, lanes] * slope_two[:, lanes]
            + side_pre[here, lanes] * slope_side[:, lanes]
            + base_joined[:, lanes]
        )

    pooled = []
    for lanes in quarters:
        total_joined = jnp.zeros((slots, 128), f32)
        for p in range(pixel_count):
            joined = joined_of(pl.ds(p * slots, slots), lanes)
            total_joined = total_joined + joined * gate(joined)
        pooled.append(total_joined)
    pooled = jnp.concatenate(pooled, axis=1)
    pooled = (pooled / pixel_count).astype(low)
    logits = lax.dot_general(
        pooled, head_low, (((1,), (1,)), ((), ())), preferred_element_type=f32
    )
    lane = lax.broadcasted_iota(jnp.int32, logits.shape, 1)
    real = lane < classes
    largest = jnp.max(jnp.where(real, logits, -jnp.inf), axis=1, keepdims=True)
    powers = jnp.where(real, jnp.exp(jnp.where(real, logits - largest, 0.0)), 0.0)
    total_power = jnp.sum(powers, axis=1, keepdims=True)
    onehot = jnp.where(lane == label_column, 1.0, 0.0)
    entropy = largest + jnp.log(total_power) - jnp.sum(onehot * logits, axis=1, keepdims=True)
    loss = jnp.sum(entropy * valid_column, axis=0, keepdims=True)
    grad_logits = (
        (powers / total_power - onehot) * (valid_column / denominator[:, :1])
    ).astype(low)
    grad_head = lax.dot_general(
        grad_logits, pooled, (((0,), (0,)), ((), ())), preferred_element_type=f32
    )[:16]
    grad_pooled = jnp.dot(grad_logits, head_low, preferred_element_type=f32) / pixel_count

    join_sums = []
    for lanes in quarters:
        three = [jnp.zeros((8, 128), f32)] * 3
        for p in range(pixel_count):
            here = pl.ds(p * slots, slots)
            joined = joined_of(here, lanes)
            opened = gate(joined)
            grad = grad_pooled[:, lanes] * (opened * (1.0 + joined * (1.0 - opened)))
            normed_two = (main_two[here, lanes] - mean_two[:, lanes]) * inv_two[:, lanes]
            normed_side = (side_pre[here, lanes] - mean_side[:, lanes]) * inv_side[:, lanes]
            new = (grad * normed_two, grad * normed_side, grad)
            three = [old + fold(each) for old, each in zip(three, new)]
            back_two[p // side, 1 + p % side, :, lanes] = (grad * slope_two[:, lanes]).astype(low)
            back_side[here, lanes] = (grad * slope_side[:, lanes]).astype(low)
        join_sums.append([jnp.sum(each, axis=0, keepdims=True) for each in three])
    gain_two, gain_side, shift_two = [jnp.concatenate(each, axis=1) for each in zip(*join_sums)]

    for b in range(3):
        first, last = max(0, b - 1), min(side, side + b - 1)
        left = active_t[:, first * band : last * band]
        for a in range(3):
            right = back_two[first - b + 1 : last - b + 1, 2 - a : 2 - a + side]
            grad_two[pl.ds((a * 3 + b) * width, width), :] = jnp.dot(
                left, right.reshape(-1, width), preferred_element_type=f32
            )

    def nothing():
        pass

    def matrix_votes(k, grad, between, after):
        here = pl.ds(k * width, width)
        start = edges[k - 1] if k else 0
        col_new[:, here] = factored_votes(
            grad,
            grad.shape[0],
            start,
            row_ref,
            row_new,
            col_ref[:, here],
            level,
            out_ref,
            start,
            between,
            after,
        )

    kept = {}

    def tail_step():
        sums = exchange_end(2, kept["tail"])
        loss_ref[...] = sums[GROUP : GROUP + 1, :1]
        sums = sums[:GROUP]
        old = jnp.concatenate([head_ref[...], norm_ref[...]], axis=0)
        old = jnp.concatenate([old[:, 128 * q : 128 * (q + 1)] for q in range(4)], axis=0)
        down = lax.broadcasted_iota(jnp.int32, (GROUP, 128), 0)
        scale = jnp.where(lax.rem(down, TAIL) < classes, scales[3], scales[4])
        fresh = old - scale * jnp.tanh(sums * root)
        both = jnp.concatenate([sums, fresh], axis=0)
        high = both.astype(low)
        rest = both - high.astype(f32)
        middle = rest.astype(low)
        parts = jnp.concatenate([high, middle, (rest - middle.astype(f32)).astype(low)], axis=0)
        length = 128 * classes
        gap = lax.broadcasted_iota(jnp.int32, (128, length), 1) - classes * (
            lax.broadcasted_iota(jnp.int32, (128, length), 0)
        )
        chosen = jnp.where(jnp.logical_and(gap >= 0, gap < classes), 1.0, 0.0).astype(low)
        moved = jnp.dot(parts, chosen, preferred_element_type=f32)
        moved = moved[: 2 * GROUP] + moved[2 * GROUP : 4 * GROUP] + moved[4 * GROUP :]
        place_of = lax.broadcasted_iota(jnp.int32, (TAIL, length), 1).astype(f32)
        class_of = place_of - classes * jnp.floor((place_of + 0.5) / classes)
        here = lax.broadcasted_iota(jnp.int32, (TAIL, length), 0).astype(f32) == class_of
        for which, ref in enumerate((tail_vote, tail_new)):
            for q in range(4):
                block = moved[GROUP * which + TAIL * q : GROUP * which + TAIL * (q + 1)]
                line = jnp.sum(jnp.where(here, block, 0.0), axis=0, keepdims=True)
                for k in range(classes):
                    ref[classes * q + k : classes * q + k + 1, :] = line[:, 128 * k : 128 * (k + 1)]
                for k in range(TAIL - classes):
                    at = 4 * (classes + k) + q
                    row = TAIL * q + classes + k
                    ref[at : at + 1, :] = (sums, fresh)[which][row : row + 1]
        out_ref[pl.ds(32 * SPAN, GROUP), :] = tail_new[...].astype(low)

    def return_slots(slots_here):
        mine = [own_group(u) for u in range(len(units))]
        for slot in slots_here:
            group = me * spare + slot
            own = group < 0
            for u, unit in enumerate(units):
                inside = jnp.logical_and(group >= mine[u], group < mine[u] + unit[1])
                own = jnp.logical_or(own, inside)

            @pl.when(jnp.logical_and(jnp.logical_not(own), group < groups - 1))
            def _():
                land(0, group, me, slot, 0)[0].wait_recv()

        first, last = slots_here[0], min(slots_here[-1] + 1, spare)
        here = pl.ds(first * GROUP, (last - first) * GROUP)
        total[here, :] = landed[here, :].astype(f32)

        @pl.loop(first, last)
        def _(k):
            row = pl.multiple_of(k * 16, 16)
            renew(row, first_row + row)

    def return_step(part):
        if part == 0:
            pltpu.make_async_copy(
                weight.at[pl.ds(0, OWN)], weight.at[pl.ds(0, OWN)], fetch_sem.at[7]
            ).wait()
            return_slots(range(0, 7))
        elif part == 1:
            return_slots(range(7, spare + 1))
        else:

            @pl.when(me < 31)
            def _():
                pltpu.make_async_copy(
                    weight.at[pl.ds(OWN, TAIL)], weight.at[pl.ds(OWN, TAIL)], fetch_sem.at[8]
                ).wait()
                total[pl.ds(SPAN, GROUP), :] = landed[pl.ds(SPAN, GROUP), :].astype(f32)
                renew(OWN, first_row + OWN)

            @pl.when(me == 31)
            def _():
                vote_flat[pl.ds(SPAN, GROUP), :] = tail_vote[...]
                new_flat[pl.ds(SPAN, GROUP), :] = tail_new[...]

            shift = 2 * me
            share = vote_ref.shape[0]
            vote_ref[...] = vote_flat[pl.ds(shift, share), :]
            new_ref[...] = new_flat[pl.ds(shift, share), :]

    in_flight = {}
    steps = (
        lambda u, copy: scatter_start(u),
        scatter_one,
        scatter_two,
        scatter_three,
        lambda u, copy: own_block(u),
        lambda u, copy: gather_one(u),
        gather_two,
        gather_three,
        lambda u, copy: tail_step(),
        lambda u, copy: return_step(u),
    )

    def go(number, u):
        got = steps[number](u, in_flight.get(u))
        if number < 8:
            in_flight[u] = got

    def turn(number):
        for step_number, u in SCHEDULE[number]:
            go(step_number, u)

    early = edges[1] // 512 - edges[0] // 512
    matrix_votes(1, grad_two, (nothing, nothing), lambda k: go(0, k) if k < 2 else None)
    turn(0)

    gain_one, shift_one = none, none
    for j in range(side):
        taps = [b for b in range(3) if 0 <= j - b + 1 < side]
        pieces = [
            back_two[j - b + 1, 2 - a : 2 - a + side].reshape(band, width)
            for b in taps
            for a in range(3)
        ]
        weights = jnp.concatenate([low_two[b * 3 + a] for b in taps for a in range(3)], axis=1)
        grad = lax.dot_general(
            jnp.concatenate(pieces, axis=1),
            weights,
            (((1,), (1,)), ((), ())),
            preferred_element_type=f32,
        )
        before = main_pre[pl.ds(j * band, band), :]
        hidden = before * slope_one + base_one
        opened = gate(hidden)
        grad = grad * (opened * (1.0 + hidden * (1.0 - opened)))
        shift_one = shift_one + jnp.sum(grad, axis=0, keepdims=True)
        gain_one = gain_one + jnp.sum(
            grad * ((before - mean_one) * inv_one), axis=0, keepdims=True
        )
        back_one[j, :side] = (grad * slope_one).astype(low).reshape(side, slots, width)
        turn(1 + j)

    grad_short[...] = jnp.dot(xs_t[0, 0], back_side[...], preferred_element_type=f32)
    matrix_votes(2, grad_short, (nothing, nothing), lambda k: None)
    turn(5)

    square_head = grad_head * grad_head + EPS_ROW
    real = lax.broadcasted_iota(jnp.int32, square_head.shape, 0) < classes
    square_head = jnp.where(real, square_head, 0.0)
    head_lanes = pl.ds(edges[2], width)
    old = row_ref[:, head_lanes]
    row = keep * old + (1.0 - keep) * jnp.sum(square_head, axis=0, keepdims=True) / classes
    row_new[:, head_lanes] = row
    diagonal = eye_mask(16, classes)
    old = jnp.broadcast_to(col_ref[:, 3 * width :], (16, classes))
    old = jnp.sum(jnp.where(diagonal, old, 0.0), axis=1, keepdims=True)
    column = keep * old + (1.0 - keep) * jnp.sum(square_head, axis=1, keepdims=True) / width
    col_new[:, 3 * width :] = jnp.sum(
        jnp.where(diagonal, jnp.broadcast_to(column, (16, classes)), 0.0), axis=0, keepdims=True
    )
    real_column = lax.broadcasted_iota(jnp.int32, column.shape, 0) < classes
    column = jnp.where(real_column, column, 1.0)
    mean = jnp.sum(row, axis=1, keepdims=True) / width
    raw = grad_head * (lax.rsqrt(row) * jnp.sqrt(mean)) * lax.rsqrt(column)
    clip = jnp.maximum(1.0, jnp.sqrt(total_of(raw * raw) / (classes * width)))
    head_votes = jnp.tanh(raw / clip)[:classes]

    raws = []
    for k, grad in enumerate((gain_one, shift_one, gain_two, shift_two, gain_side, shift_two)):
        here = pl.ds(k * width, width)
        moment = keep * moment_ref[:, here] + (1.0 - keep) * (grad * grad + EPS_ROW)
        moment_new[:, here] = moment
        raws.append(grad * lax.rsqrt(moment))
    raw = jnp.concatenate(raws, axis=0)
    clip = jnp.maximum(1.0, jnp.sqrt(total_of(raw * raw) / raw.size))
    norm_votes = jnp.tanh(raw / clip)
    tail_votes = jnp.concatenate([head_votes, norm_votes], axis=0)
    kept["tail"] = exchange_start(
        2,
        jnp.concatenate(
            [tail_votes[:, 128 * q : 128 * (q + 1)] for q in range(4)]
            + [jnp.broadcast_to(loss, (8, 128))],
            axis=0,
        ),
    )


    for b in range(3):
        first, last = (0, side - 1) if b == 0 else (0, side)
        shift = 1 if b == 0 else 0
        for a in range(3):
            left = xs_t[0 if b == 1 else 1, 0 if a == 1 else 1, :, first * band : last * band]
            start = 1 if a == 0 else 0
            right = back_one[first + shift : last + shift, start : start + side]
            grad_one[pl.ds((a * 3 + b) * in_width, in_width), :] = jnp.dot(
                left, right.reshape(-1, width), preferred_element_type=f32
            )
        if b == 1:
            kept["tail"] = exchange_middle(2, kept["tail"])
        turn(6 + b)

    matrix_votes(
        0,
        grad_one,
        (lambda: turn(9), lambda: turn(10)),
        lambda k: go(0, early + k) if k < 2 else None,
    )
    turn(11)
    for away, copy in passes:

        @pl.when(away)
        def _():
            copy.wait_send()

    three = deep_in.at[pl.ds(0, 3 * SPAN)]
    for kind, ref in enumerate((None, wide_in, deep_in, three, three, deep_in, wide_in, core_in)):
        if kind:
            sent_all(kind, ref)
    for u in range(len(units)):
        in_flight[u].wait_recv()


def finish_kernel(count, chunks, *refs):
    sources, targets, sem = refs[:count], refs[count : 2 * count], refs[2 * count]
    rows = sources[0].shape[0]
    step = -(-rows // chunks // 16) * 16
    copies = []
    for k in range(chunks):
        here = pl.ds(k * step, min(step, rows - k * step))
        copies.append(
            pltpu.make_async_copy(sources[0].at[here], targets[0].at[here], sem.at[k])
        )
    for k in range(1, count):
        copies.append(pltpu.make_async_copy(sources[k], targets[k], sem.at[chunks + k]))
    for copy in copies:
        copy.start()
    for copy in copies:
        copy.wait()


def finish(values):
    count, chunks = len(values), 4
    held = [pltpu.with_memory_space_constraint(value, pltpu.VMEM) for value in values]
    return pl.pallas_call(
        functools.partial(finish_kernel, count, chunks),
        out_shape=[jax.ShapeDtypeStruct(value.shape, value.dtype) for value in values],
        in_specs=[pl.BlockSpec(memory_space=pltpu.VMEM)] * count,
        out_specs=[pl.BlockSpec(memory_space=pl.ANY)] * count,
        scratch_shapes=[pltpu.SemaphoreType.DMA((chunks + count,))],
        compiler_params=pltpu.CompilerParams(vmem_limit_bytes=1024 * 1024),
        name="finish",
    )(*held)


def run_step(images, conv_one, conv_two, shortcut, head, norm_params, valid, labels, rows, cols, moment):
    vmem = pl.BlockSpec(memory_space=pltpu.VMEM)
    hbm = pl.BlockSpec(memory_space=pl.ANY)
    low, f32 = jnp.bfloat16, jnp.float32
    dma = pltpu.SemaphoreType.DMA
    workers = lax.axis_size("dp")
    slots, in_width = valid.shape[1], images.shape[1]
    width = conv_one.shape[1]
    pixels = images.shape[0] // 4
    shape = pltpu.VMEM
    edges = [conv_one.shape[0]]
    edges.append(edges[0] + conv_two.shape[0])
    edges.append(edges[1] + shortcut.shape[0])
    units = make_units(edges)
    flat = (edges[2] + TAIL) * width // 128
    share = flat // workers
    return pl.pallas_call(
        functools.partial(step_kernel, tuple(edges), tuple(units), 1.0 / math.sqrt(workers)),
        out_shape=(
            shape((share, 128), f32),
            shape((share, 128), f32),
            shape((flat, 128), low),
            shape(rows.shape, f32),
            shape(cols.shape, f32),
            shape(moment.shape, f32),
            shape((1, 1), f32),
            shape((1, 1), f32),
        ),
        in_specs=[hbm] * 4 + [vmem] * 7,
        out_specs=(vmem,) * 8,
        scratch_shapes=[
            pltpu.VMEM((2, 4, 2, 4, slots, in_width), low),
            pltpu.VMEM(conv_one.shape, f32),
            pltpu.VMEM(conv_two.shape, f32),
            pltpu.VMEM(shortcut.shape, f32),
            pltpu.VMEM((9, in_width, width), low),
            pltpu.VMEM((9, width, width), low),
            pltpu.VMEM((1, in_width, width), low),
            pltpu.VMEM((pixels, width), f32),
            pltpu.VMEM((pixels, width), f32),
            pltpu.VMEM((pixels, width), f32),
            pltpu.VMEM((4, 6, slots, width), low),
            pltpu.VMEM((4, 6, slots, width), low),
            pltpu.VMEM((4, 5, slots, width), low),
            pltpu.VMEM((pixels, width), low),
            pltpu.VMEM((width, pixels), low),
            pltpu.VMEM((2, 2, in_width, pixels), low),
            pltpu.VMEM((128, width), f32),
            pltpu.VMEM((conv_two.shape[0], 128), f32),
            pltpu.VMEM((8, width), f32),
            pltpu.VMEM((24, 128), f32),
            pltpu.VMEM((8, 24, 128), f32),
            pltpu.VMEM((4, 24, 128), f32),
            pltpu.VMEM((8, 128), f32),
            pltpu.VMEM((8, 8, 128), f32),
            pltpu.VMEM((4, 8, 128), f32),
            pltpu.VMEM((GROUP + 8, 128), f32),
            pltpu.VMEM((8, GROUP + 8, 128), f32),
            pltpu.VMEM((4, GROUP + 8, 128), f32),
            pltpu.VMEM((16 * SPAN, 128), low),
            pltpu.VMEM((8 * SPAN, 128), low),
            pltpu.VMEM((4 * SPAN, 128), low),
            pltpu.VMEM((4 * SPAN, 128), low),
            pltpu.VMEM((SPAN, 128), low),
            pltpu.VMEM((SPAN + GROUP, 128), low),
            pltpu.VMEM((SPAN + GROUP, 128), f32),
            pltpu.VMEM((OWN, width), f32),
            pltpu.VMEM((OWN + TAIL, width), f32),
            pltpu.VMEM((SPAN + GROUP, 128), f32),
            pltpu.VMEM((SPAN + GROUP, 128), f32),
            pltpu.VMEM((GROUP, 128), f32),
            pltpu.VMEM((GROUP, 128), f32),
            dma((9 + len(units),)),
            dma((3, 10)),
            dma((3, 10)),
            dma((8,)),
            dma((len(units), 3)),
            dma((len(units),)),
            dma((2 * OWN // 16,)),
            dma((OWN // 16 + 1,)),
            dma((len(units),)),
            dma((len(units), 3)),
            pltpu.SemaphoreType.REGULAR,
            dma((2,)),
        ],
        compiler_params=pltpu.CompilerParams(
            collective_id=1, has_side_effects=True, vmem_limit_bytes=54 * 1024 * 1024
        ),
        name="step",
    )(images, conv_one, conv_two, shortcut, head, norm_params, valid, labels, rows, cols, moment)


def scale_for(weight):
    return jnp.maximum(EPS_SCALE, jnp.sqrt(jnp.mean(weight * weight)))


def local_general(
    images,
    valid_slot,
    labels,
    conv_one,
    conv_two,
    shortcut,
    classifier,
    norm_params,
    row_state,
    col_state,
    bn_moment,
):
    in_width = images.shape[3]
    width = conv_one.shape[1]
    kernel_one = conv_one.astype(jnp.bfloat16).reshape(3, 3, in_width, width)
    kernel_two = conv_two.astype(jnp.bfloat16).reshape(3, 3, width, width)
    kernel_short = shortcut.astype(jnp.bfloat16).reshape(1, 1, in_width, width)
    head_low = classifier.astype(jnp.bfloat16)
    slot_count = images.shape[0]
    out_side = images.shape[1] // 2
    pixel_count = out_side * out_side
    slot_weight = valid_slot.astype(jnp.float32)
    pixel_weight = jnp.broadcast_to(slot_weight[:, None], (slot_count, pixel_count)).reshape(-1, 1)
    main_pre, side_pre = first_section(images, kernel_one, kernel_short)
    main_sums = masked_moments(pixel_weight, main_pre)
    side_sums = masked_moments(pixel_weight, side_pre)
    count_row = jnp.broadcast_to(jnp.sum(slot_weight), (width,))
    first_sums = lax.psum(jnp.stack([*main_sums, *side_sums, count_row]), "dp")
    valid_count = first_sums[4, 0]
    denominator = jnp.maximum(valid_count, 1.0)
    pixels = denominator * pixel_count
    norm_one = settle(first_sums[0], first_sums[1], pixels)
    norm_side = settle(first_sums[2], first_sums[3], pixels)
    hidden_one, active, main_two = second_section(
        main_pre, norm_one, norm_params, kernel_two, slot_count, out_side
    )
    two_sums = masked_moments(pixel_weight, main_two)
    second_sums = lax.psum(jnp.stack([*two_sums]), "dp")
    norm_two = settle(second_sums[0], second_sums[1], pixels)
    joined_pre = (
        (main_two - norm_two[0]) * norm_two[1] * norm_params[2]
        + norm_params[3]
        + (side_pre - norm_side[0]) * norm_side[1] * norm_params[4]
        + norm_params[5]
    )
    joined = jax.nn.silu(joined_pre).reshape(slot_count, pixel_count, -1)
    pooled = jnp.mean(joined, axis=1).astype(jnp.bfloat16)
    logits = jnp.dot(pooled, head_low, preferred_element_type=jnp.float32)
    largest = jnp.max(logits, axis=1, keepdims=True)
    exp_terms = jnp.exp(logits - largest)
    total_exp = jnp.sum(exp_terms, axis=1, keepdims=True)
    log_total = largest[:, 0] + jnp.log(total_exp[:, 0])
    onehot = (labels[:, None] == jnp.arange(logits.shape[1], dtype=jnp.int32)[None, :]).astype(
        jnp.float32
    )
    local_sum = jnp.sum(slot_weight * (log_total - jnp.sum(onehot * logits, axis=1)))
    grad_logits = ((exp_terms / total_exp - onehot) * (slot_weight / denominator)[:, None]).astype(
        jnp.bfloat16
    )
    grad_head = lax.dot_general(
        pooled, grad_logits, (((0,), (0,)), ((), ())), preferred_element_type=jnp.float32
    )
    grad_pooled = lax.dot_general(
        grad_logits, head_low, (((1,), (1,)), ((), ())), preferred_element_type=jnp.float32
    )
    spread_pooled = jnp.broadcast_to(
        (grad_pooled / pixel_count)[:, None, :], (slot_count, pixel_count, width)
    )
    grad_joined = spread_pooled.reshape(slot_count * pixel_count, width) * silu_slope(joined_pre)
    gain_two, shift_two, grad_two = norm_backward(grad_joined, main_two, norm_two, norm_params[2])
    gain_side, shift_side, grad_side = norm_backward(
        grad_joined, side_pre, norm_side, norm_params[4]
    )
    grad_two_maps = grad_two.reshape(slot_count, out_side, out_side, width)
    grad_side_maps = grad_side.reshape(slot_count, out_side, out_side, width)
    grad_conv_two = conv_weight_grad(active, grad_two_maps, 1, 1, 1)
    grad_short = conv_weight_grad(images, grad_side_maps, 2, 0, -1)
    kernel_turned = jnp.transpose(kernel_two[::-1, ::-1], (0, 1, 3, 2))
    grad_active = conv_apply(grad_two_maps, kernel_turned, 1, 1).reshape(
        slot_count * pixel_count, width
    )
    grad_hidden = grad_active * silu_slope(hidden_one)
    gain_one, shift_one, grad_one = norm_backward(grad_hidden, main_pre, norm_one, norm_params[0])
    grad_conv_one = conv_weight_grad(
        images, grad_one.reshape(slot_count, out_side, out_side, width), 2, 1, 0
    )
    grad_norms = jnp.stack([gain_one, shift_one, gain_two, shift_two, gain_side, shift_side])
    grads = (grad_conv_one, grad_conv_two, grad_short, grad_head, grad_norms)
    votes, rows_new, cols_new, moment_new = make_votes(
        grads, row_state[0], col_state[0], bn_moment[0]
    )
    workers = lax.axis_size("dp")
    weights = (conv_one, conv_two, shortcut, classifier, norm_params)
    scales = [scale_for(weight) for weight in weights]
    loss_sum = lax.psum(local_sum, "dp")
    flat_vote = jnp.concatenate([vote.reshape(-1) for vote in votes])
    flat_old = jnp.concatenate([weight.reshape(-1) for weight in weights])
    flat_scale = jnp.concatenate(
        [
            jnp.broadcast_to(scale, (weight.size,))
            for scale, weight in zip(scales, weights)
        ]
    )
    vote_mine = lax.psum_scatter(flat_vote, "dp", tiled=True)
    share = vote_mine.shape[0]
    start = lax.axis_index("dp") * share
    new_mine = lax.dynamic_slice_in_dim(
        flat_old, start, share
    ) - lax.dynamic_slice_in_dim(flat_scale, start, share) * jnp.tanh(
        vote_mine / math.sqrt(workers)
    )
    copies = lax.all_gather(new_mine.astype(jnp.bfloat16), "dp", tiled=True)
    return (
        loss_sum,
        valid_count,
        new_mine,
        copies,
        vote_mine,
        rows_new[None, :],
        cols_new[None, :],
        moment_new[None, :],
    )


def local(
    images,
    valid_slot,
    labels,
    conv_one,
    conv_two,
    shortcut,
    classifier,
    norm_params,
    row_state,
    col_state,
    bn_moment,
):
    new_mine, vote_mine, copies, rows_new, cols_new, moment_new, loss_sum, valid_count = run_step(
        images.reshape(-1, images.shape[-1]),
        conv_one,
        conv_two,
        shortcut,
        classifier.T,
        norm_params,
        valid_slot.reshape(1, -1),
        labels.reshape(1, -1),
        row_state,
        col_state,
        bn_moment,
    )
    copies, new_mine, vote_mine, rows_new, cols_new, moment_new, loss_sum, valid_count = finish(
        (copies, new_mine, vote_mine, rows_new, cols_new, moment_new, loss_sum, valid_count)
    )
    return (
        loss_sum.reshape(()),
        valid_count.reshape(()),
        new_mine.reshape(-1),
        copies.reshape(-1),
        vote_mine.reshape(-1),
        rows_new,
        cols_new,
        moment_new,
    )


def solution(mesh):
    placed = (
        P("dp", None, None, None),
        P("dp"),
        P("dp"),
        P(),
        P(),
        P(),
        P(),
        P(),
        P("dp", None),
        P("dp", None),
        P("dp", None),
    )
    return jax.shard_map(
        local if mesh.shape["dp"] == 32 else local_general,
        mesh=mesh,
        in_specs=placed,
        out_specs=(P(), P(), P("dp"), P(), P("dp"), P("dp", None), P("dp", None), P("dp", None)),
        check_vma=False,
    )
```

```python
import functools
import math

import jax
import jax.numpy as jnp
from jax import lax
from jax.experimental import pallas as pl
from jax.experimental.pallas import tpu as pltpu
from jax.sharding import PartitionSpec as P

STEP = 10
MESH = pl.DeviceIdType.MESH

EPS_NORM = 1e-05
EPS_ROW = 1e-30
EPS_SCALE = 0.001
FORWARD_DIMS = ("NHWC", "HWIO", "NHWC")
WEIGHT_DIMS = ("CHWN", "IHWO", "HWNC")
OWN = 224
TAIL = 16
PIECE = 32
SPAN = 4 * OWN
HALF = SPAN // 2
GROUP = 64


def conv_apply(maps, kernel, stride, margin):
    return lax.conv_general_dilated(
        maps,
        kernel,
        (stride, stride),
        ((margin, margin), (margin, margin)),
        dimension_numbers=FORWARD_DIMS,
        preferred_element_type=jnp.float32,
    )


def conv_weight_grad(maps, grad_out, stride, low_pad, high_pad):
    result = lax.conv_general_dilated(
        maps,
        grad_out,
        (1, 1),
        ((low_pad, high_pad), (low_pad, high_pad)),
        rhs_dilation=(stride, stride),
        dimension_numbers=WEIGHT_DIMS,
        preferred_element_type=jnp.float32,
    )
    return result.reshape(-1, result.shape[3])


def silu_slope(values):
    sigmoid_part = jax.nn.sigmoid(values)
    return sigmoid_part * (1.0 + values * (1.0 - sigmoid_part))


def settle(sum_plain, sum_square, pixels):
    mean_value = sum_plain / pixels
    return (mean_value, lax.rsqrt(sum_square / pixels - mean_value * mean_value + EPS_NORM))


def first_section(images, kernel_one, kernel_short):
    row_count = images.shape[0] * (images.shape[1] // 2) ** 2
    main_pre = conv_apply(images, kernel_one, 2, 1).reshape(row_count, -1)
    side_pre = conv_apply(images, kernel_short, 2, 0).reshape(row_count, -1)
    return (main_pre, side_pre)


def second_section(main_pre, norm_one, norm_params, kernel_two, slot_count, out_side):
    hidden_one = (main_pre - norm_one[0]) * norm_one[1] * norm_params[0] + norm_params[1]
    active = (
        jax.nn.silu(hidden_one).astype(jnp.bfloat16).reshape(slot_count, out_side, out_side, -1)
    )
    main_two = conv_apply(active, kernel_two, 1, 1).reshape(slot_count * out_side * out_side, -1)
    return (hidden_one, active, main_two)


def masked_moments(pixel_weight, values):
    return (jnp.sum(pixel_weight * values, axis=0), jnp.sum(pixel_weight * values * values, axis=0))


def soft_sign(step_raw):
    clip_by = jnp.maximum(1.0, jnp.sqrt(jnp.mean(step_raw * step_raw)))
    return jnp.tanh(step_raw / clip_by)


def make_votes(grads, rows_old, cols_old, moment_old):
    decay_rate = 1.0 - STEP ** (-0.8)
    votes, rows_new, cols_new = ([], [], [])
    row_at, col_at = (0, 0)
    for matrix in grads[:4]:
        row_size, col_size = matrix.shape
        square = matrix * matrix + EPS_ROW
        row_part = decay_rate * rows_old[row_at : row_at + row_size] + (
            1.0 - decay_rate
        ) * jnp.mean(square, axis=1)
        col_part = decay_rate * cols_old[col_at : col_at + col_size] + (
            1.0 - decay_rate
        ) * jnp.mean(square, axis=0)
        second = row_part[:, None] * col_part[None, :] / jnp.mean(row_part)
        votes.append(soft_sign(matrix * lax.rsqrt(second)))
        rows_new.append(row_part)
        cols_new.append(col_part)
        row_at += row_size
        col_at += col_size
    flat_norm = grads[4].reshape(-1)
    moment_new = decay_rate * moment_old + (1.0 - decay_rate) * (flat_norm * flat_norm + EPS_ROW)
    votes.append(soft_sign(flat_norm * lax.rsqrt(moment_new)))
    return (votes, jnp.concatenate(rows_new), jnp.concatenate(cols_new), moment_new)


def norm_backward(grad_out, pre_value, norm_pair, gain_row):
    normed = (pre_value - norm_pair[0]) * norm_pair[1]
    grad_gain = jnp.sum(grad_out * normed, axis=0)
    grad_shift = jnp.sum(grad_out, axis=0)
    grad_pre = (grad_out * gain_row * norm_pair[1]).astype(jnp.bfloat16)
    return (grad_gain, grad_shift, grad_pre)


SCHEDULE = (
    (),
    (),
    (
        (1, 0), (0, 2),
    ),
    (
        (1, 1), (0, 3),
    ),
    (
        (1, 2), (0, 4),
    ),
    (
        (2, 0), (1, 3), (0, 5),
    ),
    (),
    (
        (2, 1), (1, 4), (0, 6),
    ),
    (
        (3, 0), (2, 2), (1, 5), (0, 7),
    ),
    (),
    (
        (3, 1), (2, 3), (1, 6), (0, 8),
    ),
    (
        (3, 2), (2, 4), (1, 7), (4, 0), (3, 3), (2, 5), (1, 8), (4, 1), (3, 4), (2, 6), (1, 9),
        (0, 11), (4, 2), (3, 5), (2, 7), (1, 10), (0, 12), (5, 0), (4, 3), (3, 6), (2, 8),
        (1, 11), (0, 13), (5, 1), (4, 4), (3, 7), (2, 9), (1, 12), (6, 0), (5, 2), (4, 5),
        (3, 8), (2, 10), (1, 13), (6, 1), (5, 3), (4, 6), (3, 9), (2, 11), (6, 2), (5, 4),
        (4, 7), (8, 0), (3, 10), (2, 12), (7, 0), (6, 3), (5, 5), (4, 8), (3, 11), (2, 13),
        (7, 1), (6, 4), (5, 6), (4, 9), (3, 12), (7, 2), (6, 5), (5, 7), (4, 10), (3, 13),
        (7, 3), (6, 6), (5, 8), (4, 11), (7, 4), (6, 7), (5, 9), (4, 12), (7, 5), (6, 8),
        (5, 10), (4, 13), (7, 6), (6, 9), (5, 11), (7, 7), (6, 10), (5, 12), (7, 8), (6, 11),
        (5, 13), (7, 9), (9, 0), (6, 12), (7, 10), (6, 13), (7, 11), (7, 12), (9, 1), (7, 13),
        (9, 2),
    ),
)


def place():
    me = lax.axis_index("dp")
    core = lax.rem(me, 2)
    x = lax.rem(lax.div(me, 2), 2)
    y = lax.rem(lax.div(me, 4), 2)
    z = lax.div(me, 8)
    return me, core, x, y, z


def send(src, dst, send_sem, recv_sem, partner):
    copy = pltpu.make_async_remote_copy(
        src_ref=src,
        dst_ref=dst,
        send_sem=send_sem,
        recv_sem=recv_sem,
        device_id=(partner,),
        device_id_type=MESH,
    )
    copy.start()
    return copy


def scale_of(row, scales, edges):
    picked = scales[2]
    picked = jnp.where(row < edges[1], scales[1], picked)
    return jnp.where(row < edges[0], scales[0], picked)


def make_units(edges):
    one, two, short = edges[0] // 16, edges[1] // 16, edges[2] // 16
    units = []
    for k in range((two - one) // 32):
        units.append((one + 32 * k, 1, k % 2 == 0, 16, (1, 1)))
    for k in range(one // 32):
        units.append((32 * k, 1, k % 2 == 1, 16, (0, 0)))
    at = one // 32 * 32
    assert one - at == 16 and short - two == 16
    units.append((at, 1, False, two - at, (0, 2)))
    return units


def settle_rows(sums, pixels, gain, shift):
    mean = sums[0] / pixels
    inv = lax.rsqrt(sums[1] / pixels - mean * mean + EPS_NORM)
    slope = gain * inv
    return mean, inv, slope, shift - mean * slope


def gate(values):
    return 0.5 * jnp.tanh(0.5 * values) + 0.5


def eye_mask(rows, columns, offset=0):
    down = lax.broadcasted_iota(jnp.int32, (rows, columns), 0) + offset
    return down == lax.broadcasted_iota(jnp.int32, (rows, columns), 1)


def column_of(row, size):
    spread = jnp.where(eye_mask(size, size), jnp.broadcast_to(row, (size, size)), 0)
    return jnp.sum(spread, axis=1, keepdims=True)


def total_of(values):
    return jnp.sum(jnp.sum(values, axis=0, keepdims=True), axis=1, keepdims=True)


def fold(values):
    return jnp.sum(values.reshape(values.shape[0] // 8, 8, values.shape[1]), axis=0)


def cast_weight(source, target, square_ref, taps, depth, fetches):
    step = 128
    for tap in taps:
        chunk = source.shape[0] // depth // len(fetches)
        if tap % chunk == 0:
            fetches[tap // chunk].wait()
        new_tap = (tap % 3) * 3 + tap // 3

        @pl.loop(0, depth // step)
        def _(k):
            start = pl.multiple_of(k * step, step)
            values = source[pl.ds(tap * depth + start, step), :]
            target[new_tap, pl.ds(start, step), :] = values.astype(jnp.bfloat16)
            square_ref[...] += fold(values * values)


def row_block(grad, row_at, rows_old, rows_new, level, k, carry):
    width = grad.shape[1]
    keep = 1.0 - STEP ** (-0.8)
    step = 128
    quarters = width // 128
    col_sum, row_sum = carry
    start = k * step
    lanes = pl.ds(row_at + start, step)
    if not isinstance(k, int):
        start = pl.multiple_of(start, step)
        lanes = pl.ds(pl.multiple_of(row_at + start, step), step)
    old = rows_old[:, lanes] * keep
    line = jnp.zeros((8, 128), jnp.float32)
    for m in range(step // 8):
        block = grad[pl.ds(start + 8 * m, 8), :]
        square = block * block
        col_sum = col_sum + square
        part = square[:, :128]
        for q in range(1, quarters):
            part = part + square[:, 128 * q : 128 * (q + 1)]
        part = part * ((1.0 - keep) / width)
        diagonal = eye_mask(8, 128, 8 * m)
        part = part + jnp.where(diagonal, jnp.broadcast_to(old, (8, 128)), 0.0)
        row = jnp.sum(part, axis=1, keepdims=True) + (1.0 - keep) * EPS_ROW
        row = jnp.broadcast_to(row, (8, 128))
        level[pl.ds(start + 8 * m, 8), :] = row
        row_sum = row_sum + row
        line = line + jnp.where(diagonal, row, 0.0)
    rows_new[:, lanes] = jnp.sum(line, axis=0, keepdims=True)
    return col_sum, row_sum


def no_sums(width):
    return jnp.zeros((8, width), jnp.float32), jnp.zeros((8, 128), jnp.float32)


def factored_votes(
    grad, rows, row_at, rows_old, rows_new, col_old, level, votes, vote_at, between, after, sums
):
    width = grad.shape[1]
    keep = 1.0 - STEP ** (-0.8)
    step = 128
    quarters = width // 128
    if sums is None:
        sums = lax.fori_loop(
            0,
            rows // step,
            functools.partial(row_block, grad, row_at, rows_old, rows_new, level),
            no_sums(width),
        )
    col_sum, row_sum = sums

    col_new = keep * col_old + (1.0 - keep) * (
        jnp.sum(col_sum, axis=0, keepdims=True) / rows + EPS_ROW
    )
    scale = lax.rsqrt(col_new)
    root_mean = jnp.sqrt(jnp.sum(row_sum, axis=0, keepdims=True) / rows)

    def second(k, carry):
        start = pl.multiple_of(k * step, step)
        for m in range(step // 8):
            here = pl.ds(start + 8 * m, 8)
            factor = lax.rsqrt(level[here, :]) * root_mean
            level[here, :] = factor
            raw = grad[here, :] * jnp.concatenate([factor] * quarters, axis=1) * scale
            power = raw * raw
            part = power[:, :128]
            for q in range(1, quarters):
                part = part + power[:, 128 * q : 128 * (q + 1)]
            carry = carry + part
        return carry

    between[0]()
    power = lax.fori_loop(0, rows // step, second, jnp.zeros((8, 128), jnp.float32))
    between[1]()
    clip = jnp.maximum(1.0, jnp.sqrt(total_of(power) / (rows * width)))
    scale = scale / clip

    def third(k, _):
        start = pl.multiple_of(k * step, step)
        for m in range(step // 16):
            here = pl.ds(start + 16 * m, 16)
            factor = level[here, :]
            factor = jnp.concatenate([factor] * quarters, axis=1)
            vote = jnp.tanh(grad[here, :] * factor * scale).astype(jnp.bfloat16)
            at = pl.multiple_of((vote_at + start) * 4 + GROUP * m, GROUP)
            for q in range(quarters):
                votes[pl.ds(at + 16 * q, 16), :] = vote[:, 128 * q : 128 * (q + 1)]
        return 0

    part = 512 // step
    for k in range(0, rows // step, part):
        lax.fori_loop(k, min(k + part, rows // step), third, 0)
        after(k // part)
    return col_new


def step_kernel(
    edges,
    units,
    root,
    images,
    one_hbm,
    two_hbm,
    short_hbm,
    head_ref,
    norm_ref,
    valid_ref,
    label_ref,
    row_ref,
    col_ref,
    moment_ref,
    new_ref,
    vote_ref,
    out_ref,
    row_new,
    col_new,
    moment_new,
    loss_ref,
    count_ref,
    xs,
    grad_one,
    grad_two,
    grad_short,
    low_one,
    low_two,
    low_short,
    main_pre,
    side_pre,
    main_two,
    active,
    back_two,
    back_one,
    back_side,
    active_t,
    xs_t,
    head_pad,
    level,
    square,
    post_one,
    plane_one,
    line_one,
    post_two,
    plane_two,
    line_two,
    tail_post,
    tail_plane,
    tail_line,
    core_in,
    wide_in,
    deep_in,
    line_in,
    sum_low,
    landed,
    total,
    own_weight,
    weight,
    vote_flat,
    new_flat,
    tail_vote,
    tail_new,
    fetch_sem,
    small_send,
    small_recv,
    sent,
    rs_recv,
    line_recv,
    pass_send,
    land_recv,
    spread_recv,
    ag_recv,
    free_sem,
    load_sem,
):
    slots, in_width = xs.shape[4:]
    width = main_pre.shape[1]
    side = 4
    band = side * slots
    pixel_count = side * side
    side_pixels = 4 * pixel_count
    classes = head_ref.shape[0]
    keep = 1.0 - STEP ** (-0.8)
    low = jnp.bfloat16
    f32 = jnp.float32

    me, core, x, y, z = place()
    flip_core = me + 1 - 2 * core
    flip_x = me + 2 - 4 * x
    flip_y = me + 4 - 8 * y
    spot = lax.rem(me, 8)
    near = [z * 8 + lax.rem(spot + k, 8) for k in range(1, 8)]
    far = [lax.rem(z + k, 4) * 8 + spot for k in range(1, 4)]
    others = [lax.rem(me + k, 32) for k in range(1, 32)]

    count = images.shape[0]
    loads = []
    for half in range(2):
        lanes = slice(128 * half, 128 * (half + 1))
        loads.append(
            pltpu.make_async_copy(
                images.at[:, lanes], core_in.at[pl.ds(half * count, count)], load_sem.at[half]
            )
        )
        loads[half].start()

    def chunks_of(source, target, first, count):
        rows = source.shape[0] // count
        return [
            pltpu.make_async_copy(
                source.at[pl.ds(k * rows, rows)],
                target.at[pl.ds(k * rows, rows)],
                fetch_sem.at[first + k],
            )
            for k in range(count)
        ]

    fetch_one = chunks_of(one_hbm, grad_one, 0, 3)
    fetch_short = chunks_of(short_hbm, grad_short, 3, 1)
    fetch_two = chunks_of(two_hbm, grad_two, 4, 3)
    for fetch in fetch_one + fetch_short:
        fetch.start()
    barrier = pltpu.get_barrier_semaphore()
    for partner in others:
        pl.semaphore_signal(barrier, inc=1, device_id=(partner,), device_id_type=MESH)

    def fetch_rows(row, count, place_at, sem):
        parts = (
            (one_hbm, 0, edges[0]),
            (two_hbm, edges[0], edges[1]),
            (short_hbm, edges[1], edges[2]),
        )
        for ref, first, last in parts:

            @pl.when(jnp.logical_and(row >= first, row < last))
            def _():
                start = pl.multiple_of(row - first, count)
                pltpu.make_async_copy(
                    ref.at[pl.ds(start, count)], weight.at[pl.ds(place_at, count)], sem
                ).start()

    first_row = me * OWN

    for half in range(2):
        lanes = slice(128 * half, 128 * (half + 1))
        loads[half].wait()
        apart = side_pixels + 8

        @pl.loop(0, slots // 4)
        def _(k):
            for m in range(4):
                slot = k * 4 + m
                source = pl.multiple_of(half * count + slot * side_pixels, side_pixels)
                target = pl.multiple_of(slot * apart, 8)
                level[pl.ds(target, side_pixels), :] = core_in[
                    pl.ds(source, side_pixels), :
                ].astype(f32)

        for h in range(2 * side):
            for w in range(2 * side):
                rows = level[pl.ds(2 * side * h + w, slots, stride=apart), :]
                xs[w % 2, w // 2, h % 2, h // 2, :, lanes] = rows.astype(low)

    scales = {}

    def scale_from(weight_square, size):
        return jnp.maximum(EPS_SCALE, jnp.sqrt(total_of(weight_square) / size))

    exchanges = (
        (post_one, plane_one, line_one),
        (post_two, plane_two, line_two),
        (tail_post, tail_plane, tail_line),
    )

    def exchange_start(which, values):
        mine_ref, plane_ref, _ = exchanges[which]
        mine_ref[...] = values
        plane_ref[spot] = values
        return [
            send(
                mine_ref,
                plane_ref.at[spot],
                small_send.at[which, k],
                small_recv.at[which, k],
                partner,
            )
            for k, partner in enumerate(near)
        ]

    def pack_rows(rows):
        pieces = [row[:, 128 * q : 128 * (q + 1)] for row in rows for q in range(4)]
        pad = -len(pieces) % 8
        if pad:
            pieces.append(jnp.zeros((pad, 128), f32))
        return jnp.concatenate(pieces, axis=0)

    def unpack_row(lines_in, k):
        return jnp.concatenate([lines_in[4 * k + q : 4 * k + q + 1] for q in range(4)], axis=1)

    def exchange_middle(which, copies):
        _, plane_ref, line_ref = exchanges[which]
        for copy in copies:
            copy.wait()
        line_ref[z] = functools.reduce(lambda a, b: a + b, [plane_ref[k] for k in range(8)])
        return [
            send(
                line_ref.at[z],
                line_ref.at[z],
                small_send.at[which, 7 + k],
                small_recv.at[which, 7 + k],
                partner,
            )
            for k, partner in enumerate(far)
        ]

    def exchange_end(which, copies):
        line_ref = exchanges[which][2]
        for copy in copies:
            copy.wait()
        return (line_ref[0] + line_ref[1]) + (line_ref[2] + line_ref[3])

    def lines(start, count):
        return pl.ds(pl.multiple_of(start, 16), count)

    sizes = [GROUP * unit[1] for unit in units]
    starts = [sum(sizes[:k]) for k in range(len(units) + 1)]

    def part_of(ref, u, share, start, count):
        return ref.at[lines(share * starts[u] + start, count)]

    def places(u):
        if units[u][2]:
            return x, y, flip_x, flip_y
        return y, x, flip_y, flip_x

    def unit_start(u, cc):
        return GROUP * units[u][0] + cc * (GROUP * units[u][3])

    def own_group(u):
        first, second, _, _ = places(u)
        return units[u][0] + core * units[u][3] + (first * 8 + second * 4 + z) * units[u][1]

    def halve(source, target, u, stage, partner):
        return send(source, target, sent.at[stage], rs_recv.at[u, stage], partner)

    def scatter_start(u):
        size = 16 * sizes[u]
        return halve(
            out_ref.at[lines(unit_start(u, 1 - core), size)],
            part_of(core_in, u, 16, 0, size),
            u,
            0,
            flip_core,
        )

    def add_to(ref, u, share, source_ref, source_start):
        size = share * sizes[u]
        here = lines(share * starts[u], size)
        ref[here, :] = ref[here, :] + source_ref[lines(source_start, size), :]

    def sent_all(kind, ref):
        pltpu.make_async_remote_copy(
            src_ref=ref,
            dst_ref=ref,
            send_sem=sent.at[kind],
            recv_sem=rs_recv.at[0, 0],
            device_id=(flip_core,),
            device_id_type=MESH,
        ).wait_send()

    def scatter_one(u, copy):
        copy.wait_recv()
        add_to(core_in, u, 16, out_ref, unit_start(u, core))
        if u == len(units) - 1:
            sent_all(0, core_in)
            pl.semaphore_signal(free_sem, inc=1, device_id=(flip_core,), device_id_type=MESH)
        first, _, flip_first, _ = places(u)
        size = 8 * sizes[u]
        return halve(
            part_of(core_in, u, 16, (1 - first) * size, size),
            part_of(wide_in, u, 8, 0, size),
            u,
            1,
            flip_first,
        )

    def scatter_two(u, copy):
        copy.wait_recv()
        first, second, _, flip_second = places(u)
        add_to(wide_in, u, 8, core_in, 16 * starts[u] + first * 8 * sizes[u])
        size = 4 * sizes[u]
        return halve(
            part_of(wide_in, u, 8, (1 - second) * size, size),
            part_of(deep_in, u, 4, 0, size),
            u,
            2,
            flip_second,
        )

    def line_copy(u, k):
        plane_to = lax.rem(z + k, 4)
        return pltpu.make_async_remote_copy(
            src_ref=part_of(deep_in, u, 4, plane_to * sizes[u], sizes[u]),
            dst_ref=part_of(line_in, u, 4, z * sizes[u], sizes[u]),
            send_sem=sent.at[3],
            recv_sem=line_recv.at[u],
            device_id=(plane_to * 8 + spot,),
            device_id_type=MESH,
        )

    def scatter_three(u, copy):
        copy.wait_recv()
        _, second, _, _ = places(u)
        add_to(deep_in, u, 4, wide_in, 8 * starts[u] + second * 4 * sizes[u])
        for k in (3, 2, 1):
            line_copy(u, k).start()
        here = lines(4 * starts[u] + z * sizes[u], sizes[u])
        line_in[here, :] = deep_in[here, :]

    def three_landed(u, sem):
        ref = part_of(line_in, u, 4, 0, 3 * sizes[u])
        pltpu.make_async_remote_copy(
            src_ref=ref,
            dst_ref=ref,
            send_sem=sent.at[3],
            recv_sem=sem.at[u],
            device_id=(far[0],),
            device_id_type=MESH,
        ).wait_recv()

    groups = (edges[2] + TAIL) // 16
    spare = (groups - 1) // 32
    passes = []

    def land(local, group, to, slot, index):
        source = sum_low.at[lines(local * GROUP, GROUP)]
        target = landed.at[lines(slot * GROUP, GROUP)]
        copy = pltpu.make_async_remote_copy(
            src_ref=source,
            dst_ref=target,
            send_sem=pass_send.at[index],
            recv_sem=land_recv.at[slot],
            device_id=(to,),
            device_id_type=MESH,
        )
        return copy, source, target

    def pass_on(u):
        for m in range(units[u][1]):
            local = starts[u] // GROUP + m
            group = own_group(u) + m
            to, slot = lax.div(group, spare), lax.rem(group, spare)

            def one(receiver, at, index):
                copy, source, target = land(local, group, receiver, at, index)

                @pl.when(receiver != me)
                def _():
                    copy.start()

                @pl.when(receiver == me)
                def _():
                    target[...] = source[...]

                return copy

            first = jnp.logical_and(slot == 0, group > 0)
            ahead = lax.rem(to + 31, 32)
            passes.append((to != me, one(to, slot, 2 * local)))

            @pl.when(first)
            def _():
                one(ahead, spare, 2 * local + 1)

            copy = land(local, group, ahead, spare, 2 * local + 1)[0]
            passes.append((jnp.logical_and(first, ahead != me), copy))

    def flat_rows(row, q, values, ref):
        ref[pl.ds(row * 4 + q, 8, stride=4), :] = values

    def old_rows(u, cc):
        matrix = units[u][4][cc]
        base = edges[matrix - 1] if matrix else 0
        return (one_hbm, two_hbm, short_hbm)[matrix], 16 * own_group(u) - base, 16 * units[u][1]

    def own_fetch(u):
        target = own_weight.at[pl.ds(starts[u] // 4, 16 * units[u][1])]
        matrices = units[u][4]
        for cc in range(2):
            if cc and matrices[0] == matrices[1]:
                continue

            @pl.when((core == cc) if matrices[0] != matrices[1] else (core >= 0))
            def _():
                ref, row, count = old_rows(u, cc)
                pltpu.make_async_copy(
                    ref.at[pl.ds(pl.multiple_of(row, 16), count)], target, fetch_sem.at[9 + u]
                ).start()

    def spread_copy(u, k):
        own = out_ref.at[lines(own_group(u) * GROUP, sizes[u])]
        return pltpu.make_async_remote_copy(
            src_ref=own,
            dst_ref=own,
            send_sem=sent.at[4],
            recv_sem=spread_recv.at[u],
            device_id=(far[k - 1],),
            device_id_type=MESH,
        )

    def own_block(u):
        size = sizes[u]
        three_landed(u, line_recv)
        here = pl.ds(starts[u], size)
        low_sum = functools.reduce(
            lambda a, b: a + b,
            [line_in[pl.ds(4 * starts[u] + t * size, size), :].astype(f32) for t in range(4)],
        ).astype(low)
        sum_low[here, :] = low_sum
        summed = low_sum.astype(f32)
        target = own_weight.at[pl.ds(starts[u] // 4, 16 * units[u][1])]
        pltpu.make_async_copy(target, target, fetch_sem.at[9 + u]).wait()
        matrices = units[u][4]
        scale = scales[matrices[0]]
        if matrices[0] != matrices[1]:
            scale = jnp.where(core == 0, scale, scales[matrices[1]])
        turned = jnp.tanh(summed * root) * scale
        for m in range(units[u][1]):
            row = starts[u] // 4 + 16 * m
            for part in (0, 8):
                for q in range(4):
                    at = GROUP * m + 16 * q + part
                    old = own_weight[pl.ds(row + part, 8), 128 * q : 128 * (q + 1)]
                    flat_rows(row + part, q, old - turned[at : at + 8], new_flat)
        out_ref[lines(own_group(u) * GROUP, size), :] = new_flat[here, :].astype(low)
        for k in (3, 2, 1):
            spread_copy(u, k).start()
        pass_on(u)

    def piece(rows, u, stage, partner):
        return send(
            out_ref.at[rows], out_ref.at[rows], sent.at[5 + stage], ag_recv.at[u, stage], partner
        )

    def gather_one(u):
        three_landed(u, spread_recv)
        first, second, _, flip_second = places(u)
        size = 4 * sizes[u]
        start = unit_start(u, core) + (2 * first + second) * size
        return piece(lines(start, size), u, 0, flip_second)

    def gather_two(u, copy):
        copy.wait_recv()
        first, _, flip_first, _ = places(u)
        size = 8 * sizes[u]
        return piece(lines(unit_start(u, core) + first * size, size), u, 1, flip_first)

    def gather_three(u, copy):
        copy.wait_recv()
        if u == 0:
            pl.semaphore_wait(free_sem, 1)
        return piece(lines(unit_start(u, core), 16 * sizes[u]), u, 2, flip_core)

    def renew(row, at_row):
        scale = scale_of(at_row, [scales[k] for k in range(3)], edges)
        for part in (0, 8):
            for q in range(4):
                summed = total[pl.ds(row * 4 + 16 * q + part, 8), :]
                old = weight[pl.ds(row + part, 8), 128 * q : 128 * (q + 1)]
                fresh = old - scale * jnp.tanh(summed * root)
                flat_rows(row + part, q, summed, vote_flat)
                flat_rows(row + part, q, fresh, new_flat)

    valid_column = column_of(valid_ref[...].astype(f32), slots)
    weight_slot = jnp.broadcast_to(valid_column, (slots, width))
    weight_band = jnp.concatenate([weight_slot] * side, axis=0)

    square[...] = jnp.zeros_like(square)
    cast_weight(grad_one, low_one, square, range(9), in_width, fetch_one)
    scales[0] = scale_from(square[...], grad_one.size)
    square[...] = jnp.zeros_like(square)
    cast_weight(grad_short, low_short, square, range(1), in_width, fetch_short)
    scales[2] = scale_from(square[...], grad_short.size)
    for fetch in fetch_two:
        fetch.start()

    def image_taps(j):
        pieces = []
        for b in range(3):
            column = j if b else j - 1
            if column < 0:
                continue
            across = 0 if b == 1 else 1
            for a in range(3):
                if a == 1:
                    piece = xs[across, column, 0].reshape(band, in_width)
                elif a == 2:
                    piece = xs[across, column, 1].reshape(band, in_width)
                else:
                    piece = xs[across, column, 1, : side - 1].reshape(band - slots, in_width)
                    piece = jnp.concatenate([jnp.zeros((slots, in_width), low), piece], axis=0)
                pieces.append(piece)
        return jnp.concatenate(pieces, axis=1)

    def moments(values):
        weighted = values * weight_band
        return (
            jnp.sum(weighted, axis=0, keepdims=True),
            jnp.sum(weighted * values, axis=0, keepdims=True),
        )

    def add_up(old, new):
        return [a + b for a, b in zip(old, new)]

    none = jnp.zeros((1, width), f32)
    main_sums, side_sums = [none, none], [none, none]
    for j in range(side):
        here = pl.ds(j * band, band)
        low_rows = low_one[3 if j == 0 else 0 :].reshape(-1, width)
        value = jnp.dot(image_taps(j), low_rows, preferred_element_type=f32)
        main_pre[here, :] = value
        main_sums = add_up(main_sums, moments(value))
        value = jnp.dot(
            xs[0, j, 0].reshape(band, in_width), low_short[0], preferred_element_type=f32
        )
        side_pre[here, :] = value
        side_sums = add_up(side_sums, moments(value))

    count = jnp.broadcast_to(jnp.sum(valid_column, axis=0, keepdims=True), (1, width))
    pl.semaphore_wait(barrier, len(others))
    copies = exchange_start(
        0, pack_rows(main_sums + side_sums + [count])
    )
    square[...] = jnp.zeros_like(square)
    cast_weight(grad_two, low_two, square, range(5), width, fetch_two)
    copies = exchange_middle(0, copies)
    cast_weight(grad_two, low_two, square, range(5, 9), width, fetch_two)
    scales[1] = scale_from(square[...], grad_two.size)
    border = jnp.zeros((side, 1, slots, width), low)
    active[:, 0:1] = border
    active[:, side + 1 :] = border
    back_two[:, 0:1] = border
    back_two[:, side + 1 :] = border
    back_one[:, side:] = border
    head_pad[...] = jnp.zeros_like(head_pad)
    head_pad[:classes, :] = head_ref[...]
    head = head_pad[:16, :]
    scales[3] = scale_from(head * head, head_ref.size)
    params = norm_ref[...]
    scales[4] = scale_from(params * params, norm_ref.size)
    sums = exchange_end(0, copies)
    sums = [unpack_row(sums, k) for k in range(5)]

    valid_count = sums[4]
    count_ref[...] = valid_count[:, :1]
    denominator = jnp.maximum(valid_count, 1.0)
    pixels = denominator * pixel_count
    gains = [norm_ref[k : k + 1, :] for k in range(6)]
    mean_one, inv_one, slope_one, base_one = settle_rows(
        (sums[0], sums[1]), pixels, gains[0], gains[1]
    )
    mean_side, inv_side, slope_side, base_side = settle_rows(
        (sums[2], sums[3]), pixels, gains[4], gains[5]
    )

    for j in range(side):
        hidden = main_pre[pl.ds(j * band, band), :] * slope_one + base_one
        active[j, 1 : side + 1] = (
            (hidden * gate(hidden)).astype(low).reshape(side, slots, width)
        )
    two_sums = [none, none]
    for j in range(side):
        taps = [b for b in range(3) if 0 <= j + b - 1 < side]
        pieces = [
            active[j + b - 1, a : a + side].reshape(band, width) for b in taps for a in range(3)
        ]
        low_rows = low_two[3 * taps[0] : 3 * taps[-1] + 3].reshape(-1, width)
        value = jnp.dot(jnp.concatenate(pieces, axis=1), low_rows, preferred_element_type=f32)
        main_two[pl.ds(j * band, band), :] = value
        two_sums = add_up(two_sums, moments(value))
    copies = exchange_start(1, pack_rows(two_sums))
    for k in range(OWN // PIECE):
        fetch_rows(first_row + k * PIECE, PIECE, k * PIECE, fetch_sem.at[7])
    fetch_rows(first_row + OWN, TAIL, OWN, fetch_sem.at[8])
    for u in range(len(units)):
        own_fetch(u)
    for j in range(side):
        block = active[j, 1 : side + 1].reshape(band, width)
        active_t[:, j * band : (j + 1) * band] = block.T
    label_column = column_of(label_ref[...].astype(f32), slots).astype(jnp.int32)
    head_low = head_pad[...].astype(low)
    copies = exchange_middle(1, copies)
    for across in range(2):
        for down in range(2):
            for j in range(side):
                block = xs[across, j, down].reshape(band, in_width)
                xs_t[across, down, :, j * band : (j + 1) * band] = block.T
    sums = exchange_end(1, copies)
    sums = [unpack_row(sums, k) for k in range(2)]
    mean_two, inv_two, slope_two, base_two = settle_rows(
        (sums[0], sums[1]), pixels, gains[2], gains[3]
    )

    base_joined = base_two + base_side

    quarters = [slice(128 * q, 128 * (q + 1)) for q in range(width // 128)]

    def joined_of(here, lanes):
        return (
            main_two[here, lanes] * slope_two[:, lanes]
            + side_pre[here, lanes] * slope_side[:, lanes]
            + base_joined[:, lanes]
        )

    pooled = []
    for lanes in quarters:
        total_joined = jnp.zeros((slots, 128), f32)
        for p in range(pixel_count):
            joined = joined_of(pl.ds(p * slots, slots), lanes)
            total_joined = total_joined + joined * gate(joined)
        pooled.append(total_joined)
    pooled = jnp.concatenate(pooled, axis=1)
    pooled = (pooled / pixel_count).astype(low)
    logits = lax.dot_general(
        pooled, head_low, (((1,), (1,)), ((), ())), preferred_element_type=f32
    )
    lane = lax.broadcasted_iota(jnp.int32, logits.shape, 1)
    real = lane < classes
    largest = jnp.max(jnp.where(real, logits, -jnp.inf), axis=1, keepdims=True)
    powers = jnp.where(real, jnp.exp(jnp.where(real, logits - largest, 0.0)), 0.0)
    total_power = jnp.sum(powers, axis=1, keepdims=True)
    onehot = jnp.where(lane == label_column, 1.0, 0.0)
    entropy = largest + jnp.log(total_power) - jnp.sum(onehot * logits, axis=1, keepdims=True)
    loss = jnp.sum(entropy * valid_column, axis=0, keepdims=True)
    grad_logits = (
        (powers / total_power - onehot) * (valid_column / denominator[:, :1])
    ).astype(low)
    grad_head = lax.dot_general(
        grad_logits, pooled, (((0,), (0,)), ((), ())), preferred_element_type=f32
    )[:16]
    grad_pooled = jnp.dot(grad_logits, head_low, preferred_element_type=f32) / pixel_count

    join_sums = []
    for lanes in quarters:
        three = [jnp.zeros((8, 128), f32)] * 3
        for p in range(pixel_count):
            here = pl.ds(p * slots, slots)
            joined = joined_of(here, lanes)
            opened = gate(joined)
            grad = grad_pooled[:, lanes] * (opened * (1.0 + joined * (1.0 - opened)))
            normed_two = (main_two[here, lanes] - mean_two[:, lanes]) * inv_two[:, lanes]
            normed_side = (side_pre[here, lanes] - mean_side[:, lanes]) * inv_side[:, lanes]
            new = (grad * normed_two, grad * normed_side, grad)
            three = [old + fold(each) for old, each in zip(three, new)]
            back_two[p // side, 1 + p % side, :, lanes] = (grad * slope_two[:, lanes]).astype(low)
            back_side[here, lanes] = (grad * slope_side[:, lanes]).astype(low)
        join_sums.append([jnp.sum(each, axis=0, keepdims=True) for each in three])
    gain_two, gain_side, shift_two = [jnp.concatenate(each, axis=1) for each in zip(*join_sums)]

    two_passed = no_sums(width)
    for b in range(3):
        first, last = max(0, b - 1), min(side, side + b - 1)
        left = active_t[:, first * band : last * band]
        for a in range(3):
            right = back_two[first - b + 1 : last - b + 1, 2 - a : 2 - a + side]
            tap = a * 3 + b
            grad_two[pl.ds(tap * width, width), :] = jnp.dot(
                left, right.reshape(-1, width), preferred_element_type=f32
            )
            for k in range(tap * width // 128, (tap + 1) * width // 128):
                two_passed = row_block(
                    grad_two, edges[0], row_ref, row_new, level, k, two_passed
                )

    def nothing():
        pass

    def matrix_votes(k, grad, between, after, sums=None):
        here = pl.ds(k * width, width)
        start = edges[k - 1] if k else 0
        col_new[:, here] = factored_votes(
            grad,
            grad.shape[0],
            start,
            row_ref,
            row_new,
            col_ref[:, here],
            level,
            out_ref,
            start,
            between,
            after,
            sums,
        )

    kept = {}

    def tail_step():
        sums = exchange_end(2, kept["tail"])
        loss_ref[...] = sums[GROUP : GROUP + 1, :1]
        sums = sums[:GROUP]
        old = jnp.concatenate([head_ref[...], norm_ref[...]], axis=0)
        old = jnp.concatenate([old[:, 128 * q : 128 * (q + 1)] for q in range(4)], axis=0)
        down = lax.broadcasted_iota(jnp.int32, (GROUP, 128), 0)
        scale = jnp.where(lax.rem(down, TAIL) < classes, scales[3], scales[4])
        fresh = old - scale * jnp.tanh(sums * root)
        both = jnp.concatenate([sums, fresh], axis=0)
        high = both.astype(low)
        rest = both - high.astype(f32)
        middle = rest.astype(low)
        parts = jnp.concatenate([high, middle, (rest - middle.astype(f32)).astype(low)], axis=0)
        length = 128 * classes
        gap = lax.broadcasted_iota(jnp.int32, (128, length), 1) - classes * (
            lax.broadcasted_iota(jnp.int32, (128, length), 0)
        )
        chosen = jnp.where(jnp.logical_and(gap >= 0, gap < classes), 1.0, 0.0).astype(low)
        moved = jnp.dot(parts, chosen, preferred_element_type=f32)
        moved = moved[: 2 * GROUP] + moved[2 * GROUP : 4 * GROUP] + moved[4 * GROUP :]
        place_of = lax.broadcasted_iota(jnp.int32, (TAIL, length), 1).astype(f32)
        class_of = place_of - classes * jnp.floor((place_of + 0.5) / classes)
        here = lax.broadcasted_iota(jnp.int32, (TAIL, length), 0).astype(f32) == class_of
        for which, ref in enumerate((tail_vote, tail_new)):
            for q in range(4):
                block = moved[GROUP * which + TAIL * q : GROUP * which + TAIL * (q + 1)]
                line = jnp.sum(jnp.where(here, block, 0.0), axis=0, keepdims=True)
                for k in range(classes):
                    ref[classes * q + k : classes * q + k + 1, :] = line[:, 128 * k : 128 * (k + 1)]
                for k in range(TAIL - classes):
                    at = 4 * (classes + k) + q
                    row = TAIL * q + classes + k
                    ref[at : at + 1, :] = (sums, fresh)[which][row : row + 1]
        out_ref[pl.ds(32 * SPAN, GROUP), :] = tail_new[...].astype(low)

    def return_slots(slots_here):
        mine = [own_group(u) for u in range(len(units))]
        for slot in slots_here:
            group = me * spare + slot
            own = group < 0
            for u, unit in enumerate(units):
                inside = jnp.logical_and(group >= mine[u], group < mine[u] + unit[1])
                own = jnp.logical_or(own, inside)

            @pl.when(jnp.logical_and(jnp.logical_not(own), group < groups - 1))
            def _():
                land(0, group, me, slot, 0)[0].wait_recv()

        first, last = slots_here[0], min(slots_here[-1] + 1, spare)
        here = pl.ds(first * GROUP, (last - first) * GROUP)
        total[here, :] = landed[here, :].astype(f32)

        @pl.loop(first, last)
        def _(k):
            row = pl.multiple_of(k * 16, 16)
            renew(row, first_row + row)

    def return_step(part):
        if part == 0:
            pltpu.make_async_copy(
                weight.at[pl.ds(0, OWN)], weight.at[pl.ds(0, OWN)], fetch_sem.at[7]
            ).wait()
            return_slots(range(0, 7))
        elif part == 1:
            return_slots(range(7, spare + 1))
        else:

            @pl.when(me < 31)
            def _():
                pltpu.make_async_copy(
                    weight.at[pl.ds(OWN, TAIL)], weight.at[pl.ds(OWN, TAIL)], fetch_sem.at[8]
                ).wait()
                total[pl.ds(SPAN, GROUP), :] = landed[pl.ds(SPAN, GROUP), :].astype(f32)
                renew(OWN, first_row + OWN)

            @pl.when(me == 31)
            def _():
                vote_flat[pl.ds(SPAN, GROUP), :] = tail_vote[...]
                new_flat[pl.ds(SPAN, GROUP), :] = tail_new[...]

            shift = 2 * me
            share = vote_ref.shape[0]
            vote_ref[...] = vote_flat[pl.ds(shift, share), :]
            new_ref[...] = new_flat[pl.ds(shift, share), :]

    in_flight = {}
    steps = (
        lambda u, copy: scatter_start(u),
        scatter_one,
        scatter_two,
        scatter_three,
        lambda u, copy: own_block(u),
        lambda u, copy: gather_one(u),
        gather_two,
        gather_three,
        lambda u, copy: tail_step(),
        lambda u, copy: return_step(u),
    )

    def go(number, u):
        got = steps[number](u, in_flight.get(u))
        if number < 8:
            in_flight[u] = got

    def turn(number):
        for step_number, u in SCHEDULE[number]:
            go(step_number, u)

    early = edges[1] // 512 - edges[0] // 512
    matrix_votes(1, grad_two, (nothing, nothing), lambda k: go(0, k) if k < 2 else None, two_passed)
    turn(0)

    gain_one, shift_one = none, none
    for j in range(side):
        taps = [b for b in range(3) if 0 <= j - b + 1 < side]
        pieces = [
            back_two[j - b + 1, 2 - a : 2 - a + side].reshape(band, width)
            for b in taps
            for a in range(3)
        ]
        weights = jnp.concatenate([low_two[b * 3 + a] for b in taps for a in range(3)], axis=1)
        grad = lax.dot_general(
            jnp.concatenate(pieces, axis=1),
            weights,
            (((1,), (1,)), ((), ())),
            preferred_element_type=f32,
        )
        before = main_pre[pl.ds(j * band, band), :]
        hidden = before * slope_one + base_one
        opened = gate(hidden)
        grad = grad * (opened * (1.0 + hidden * (1.0 - opened)))
        shift_one = shift_one + jnp.sum(grad, axis=0, keepdims=True)
        gain_one = gain_one + jnp.sum(
            grad * ((before - mean_one) * inv_one), axis=0, keepdims=True
        )
        back_one[j, :side] = (grad * slope_one).astype(low).reshape(side, slots, width)
        turn(1 + j)

    grad_short[...] = jnp.dot(xs_t[0, 0], back_side[...], preferred_element_type=f32)
    matrix_votes(2, grad_short, (nothing, nothing), lambda k: None)
    turn(5)

    square_head = grad_head * grad_head + EPS_ROW
    real = lax.broadcasted_iota(jnp.int32, square_head.shape, 0) < classes
    square_head = jnp.where(real, square_head, 0.0)
    head_lanes = pl.ds(edges[2], width)
    old = row_ref[:, head_lanes]
    row = keep * old + (1.0 - keep) * jnp.sum(square_head, axis=0, keepdims=True) / classes
    row_new[:, head_lanes] = row
    diagonal = eye_mask(16, classes)
    old = jnp.broadcast_to(col_ref[:, 3 * width :], (16, classes))
    old = jnp.sum(jnp.where(diagonal, old, 0.0), axis=1, keepdims=True)
    column = keep * old + (1.0 - keep) * jnp.sum(square_head, axis=1, keepdims=True) / width
    col_new[:, 3 * width :] = jnp.sum(
        jnp.where(diagonal, jnp.broadcast_to(column, (16, classes)), 0.0), axis=0, keepdims=True
    )
    real_column = lax.broadcasted_iota(jnp.int32, column.shape, 0) < classes
    column = jnp.where(real_column, column, 1.0)
    mean = jnp.sum(row, axis=1, keepdims=True) / width
    raw = grad_head * (lax.rsqrt(row) * jnp.sqrt(mean)) * lax.rsqrt(column)
    clip = jnp.maximum(1.0, jnp.sqrt(total_of(raw * raw) / (classes * width)))
    head_votes = jnp.tanh(raw / clip)[:classes]

    raws = []
    for k, grad in enumerate((gain_one, shift_one, gain_two, shift_two, gain_side, shift_two)):
        here = pl.ds(k * width, width)
        moment = keep * moment_ref[:, here] + (1.0 - keep) * (grad * grad + EPS_ROW)
        moment_new[:, here] = moment
        raws.append(grad * lax.rsqrt(moment))
    raw = jnp.concatenate(raws, axis=0)
    clip = jnp.maximum(1.0, jnp.sqrt(total_of(raw * raw) / raw.size))
    norm_votes = jnp.tanh(raw / clip)
    tail_votes = jnp.concatenate([head_votes, norm_votes], axis=0)
    kept["tail"] = exchange_start(
        2,
        jnp.concatenate(
            [tail_votes[:, 128 * q : 128 * (q + 1)] for q in range(4)]
            + [jnp.broadcast_to(loss, (8, 128))],
            axis=0,
        ),
    )


    for b in range(3):
        first, last = (0, side - 1) if b == 0 else (0, side)
        shift = 1 if b == 0 else 0
        for a in range(3):
            left = xs_t[0 if b == 1 else 1, 0 if a == 1 else 1, :, first * band : last * band]
            start = 1 if a == 0 else 0
            right = back_one[first + shift : last + shift, start : start + side]
            grad_one[pl.ds((a * 3 + b) * in_width, in_width), :] = jnp.dot(
                left, right.reshape(-1, width), preferred_element_type=f32
            )
        if b == 1:
            kept["tail"] = exchange_middle(2, kept["tail"])
        turn(6 + b)

    matrix_votes(
        0,
        grad_one,
        (lambda: turn(9), lambda: turn(10)),
        lambda k: go(0, early + k) if k < 2 else None,
    )
    turn(11)
    for away, copy in passes:

        @pl.when(away)
        def _():
            copy.wait_send()

    three = deep_in.at[pl.ds(0, 3 * SPAN)]
    for kind, ref in enumerate((None, wide_in, deep_in, three, three, deep_in, wide_in, core_in)):
        if kind:
            sent_all(kind, ref)
    for u in range(len(units)):
        in_flight[u].wait_recv()


def finish_kernel(count, chunks, *refs):
    sources, targets, sem = refs[:count], refs[count : 2 * count], refs[2 * count]
    rows = sources[0].shape[0]
    step = -(-rows // chunks // 16) * 16
    copies = []
    for k in range(chunks):
        here = pl.ds(k * step, min(step, rows - k * step))
        copies.append(
            pltpu.make_async_copy(sources[0].at[here], targets[0].at[here], sem.at[k])
        )
    for k in range(1, count):
        copies.append(pltpu.make_async_copy(sources[k], targets[k], sem.at[chunks + k]))
    for copy in copies:
        copy.start()
    for copy in copies:
        copy.wait()


def finish(values):
    count, chunks = len(values), 4
    held = [pltpu.with_memory_space_constraint(value, pltpu.VMEM) for value in values]
    return pl.pallas_call(
        functools.partial(finish_kernel, count, chunks),
        out_shape=[jax.ShapeDtypeStruct(value.shape, value.dtype) for value in values],
        in_specs=[pl.BlockSpec(memory_space=pltpu.VMEM)] * count,
        out_specs=[pl.BlockSpec(memory_space=pl.ANY)] * count,
        scratch_shapes=[pltpu.SemaphoreType.DMA((chunks + count,))],
        compiler_params=pltpu.CompilerParams(vmem_limit_bytes=1024 * 1024),
        name="finish",
    )(*held)


def run_step(images, conv_one, conv_two, shortcut, head, norm_params, valid, labels, rows, cols, moment):
    vmem = pl.BlockSpec(memory_space=pltpu.VMEM)
    hbm = pl.BlockSpec(memory_space=pl.ANY)
    low, f32 = jnp.bfloat16, jnp.float32
    dma = pltpu.SemaphoreType.DMA
    workers = lax.axis_size("dp")
    slots, in_width = valid.shape[1], images.shape[1]
    width = conv_one.shape[1]
    pixels = images.shape[0] // 4
    shape = pltpu.VMEM
    edges = [conv_one.shape[0]]
    edges.append(edges[0] + conv_two.shape[0])
    edges.append(edges[1] + shortcut.shape[0])
    units = make_units(edges)
    flat = (edges[2] + TAIL) * width // 128
    share = flat // workers
    return pl.pallas_call(
        functools.partial(step_kernel, tuple(edges), tuple(units), 1.0 / math.sqrt(workers)),
        out_shape=(
            shape((share, 128), f32),
            shape((share, 128), f32),
            shape((flat, 128), low),
            shape(rows.shape, f32),
            shape(cols.shape, f32),
            shape(moment.shape, f32),
            shape((1, 1), f32),
            shape((1, 1), f32),
        ),
        in_specs=[hbm] * 4 + [vmem] * 7,
        out_specs=(vmem,) * 8,
        scratch_shapes=[
            pltpu.VMEM((2, 4, 2, 4, slots, in_width), low),
            pltpu.VMEM(conv_one.shape, f32),
            pltpu.VMEM(conv_two.shape, f32),
            pltpu.VMEM(shortcut.shape, f32),
            pltpu.VMEM((9, in_width, width), low),
            pltpu.VMEM((9, width, width), low),
            pltpu.VMEM((1, in_width, width), low),
            pltpu.VMEM((pixels, width), f32),
            pltpu.VMEM((pixels, width), f32),
            pltpu.VMEM((pixels, width), f32),
            pltpu.VMEM((4, 6, slots, width), low),
            pltpu.VMEM((4, 6, slots, width), low),
            pltpu.VMEM((4, 5, slots, width), low),
            pltpu.VMEM((pixels, width), low),
            pltpu.VMEM((width, pixels), low),
            pltpu.VMEM((2, 2, in_width, pixels), low),
            pltpu.VMEM((128, width), f32),
            pltpu.VMEM((conv_two.shape[0], 128), f32),
            pltpu.VMEM((8, width), f32),
            pltpu.VMEM((24, 128), f32),
            pltpu.VMEM((8, 24, 128), f32),
            pltpu.VMEM((4, 24, 128), f32),
            pltpu.VMEM((8, 128), f32),
            pltpu.VMEM((8, 8, 128), f32),
            pltpu.VMEM((4, 8, 128), f32),
            pltpu.VMEM((GROUP + 8, 128), f32),
            pltpu.VMEM((8, GROUP + 8, 128), f32),
            pltpu.VMEM((4, GROUP + 8, 128), f32),
            pltpu.VMEM((16 * SPAN, 128), low),
            pltpu.VMEM((8 * SPAN, 128), low),
            pltpu.VMEM((4 * SPAN, 128), low),
            pltpu.VMEM((4 * SPAN, 128), low),
            pltpu.VMEM((SPAN, 128), low),
            pltpu.VMEM((SPAN + GROUP, 128), low),
            pltpu.VMEM((SPAN + GROUP, 128), f32),
            pltpu.VMEM((OWN, width), f32),
            pltpu.VMEM((OWN + TAIL, width), f32),
            pltpu.VMEM((SPAN + GROUP, 128), f32),
            pltpu.VMEM((SPAN + GROUP, 128), f32),
            pltpu.VMEM((GROUP, 128), f32),
            pltpu.VMEM((GROUP, 128), f32),
            dma((9 + len(units),)),
            dma((3, 10)),
            dma((3, 10)),
            dma((8,)),
            dma((len(units), 3)),
            dma((len(units),)),
            dma((2 * OWN // 16,)),
            dma((OWN // 16 + 1,)),
            dma((len(units),)),
            dma((len(units), 3)),
            pltpu.SemaphoreType.REGULAR,
            dma((2,)),
        ],
        compiler_params=pltpu.CompilerParams(
            collective_id=1, has_side_effects=True, vmem_limit_bytes=54 * 1024 * 1024
        ),
        name="step",
    )(images, conv_one, conv_two, shortcut, head, norm_params, valid, labels, rows, cols, moment)


def scale_for(weight):
    return jnp.maximum(EPS_SCALE, jnp.sqrt(jnp.mean(weight * weight)))


def local_general(
    images,
    valid_slot,
    labels,
    conv_one,
    conv_two,
    shortcut,
    classifier,
    norm_params,
    row_state,
    col_state,
    bn_moment,
):
    in_width = images.shape[3]
    width = conv_one.shape[1]
    kernel_one = conv_one.astype(jnp.bfloat16).reshape(3, 3, in_width, width)
    kernel_two = conv_two.astype(jnp.bfloat16).reshape(3, 3, width, width)
    kernel_short = shortcut.astype(jnp.bfloat16).reshape(1, 1, in_width, width)
    head_low = classifier.astype(jnp.bfloat16)
    slot_count = images.shape[0]
    out_side = images.shape[1] // 2
    pixel_count = out_side * out_side
    slot_weight = valid_slot.astype(jnp.float32)
    pixel_weight = jnp.broadcast_to(slot_weight[:, None], (slot_count, pixel_count)).reshape(-1, 1)
    main_pre, side_pre = first_section(images, kernel_one, kernel_short)
    main_sums = masked_moments(pixel_weight, main_pre)
    side_sums = masked_moments(pixel_weight, side_pre)
    count_row = jnp.broadcast_to(jnp.sum(slot_weight), (width,))
    first_sums = lax.psum(jnp.stack([*main_sums, *side_sums, count_row]), "dp")
    valid_count = first_sums[4, 0]
    denominator = jnp.maximum(valid_count, 1.0)
    pixels = denominator * pixel_count
    norm_one = settle(first_sums[0], first_sums[1], pixels)
    norm_side = settle(first_sums[2], first_sums[3], pixels)
    hidden_one, active, main_two = second_section(
        main_pre, norm_one, norm_params, kernel_two, slot_count, out_side
    )
    two_sums = masked_moments(pixel_weight, main_two)
    second_sums = lax.psum(jnp.stack([*two_sums]), "dp")
    norm_two = settle(second_sums[0], second_sums[1], pixels)
    joined_pre = (
        (main_two - norm_two[0]) * norm_two[1] * norm_params[2]
        + norm_params[3]
        + (side_pre - norm_side[0]) * norm_side[1] * norm_params[4]
        + norm_params[5]
    )
    joined = jax.nn.silu(joined_pre).reshape(slot_count, pixel_count, -1)
    pooled = jnp.mean(joined, axis=1).astype(jnp.bfloat16)
    logits = jnp.dot(pooled, head_low, preferred_element_type=jnp.float32)
    largest = jnp.max(logits, axis=1, keepdims=True)
    exp_terms = jnp.exp(logits - largest)
    total_exp = jnp.sum(exp_terms, axis=1, keepdims=True)
    log_total = largest[:, 0] + jnp.log(total_exp[:, 0])
    onehot = (labels[:, None] == jnp.arange(logits.shape[1], dtype=jnp.int32)[None, :]).astype(
        jnp.float32
    )
    local_sum = jnp.sum(slot_weight * (log_total - jnp.sum(onehot * logits, axis=1)))
    grad_logits = ((exp_terms / total_exp - onehot) * (slot_weight / denominator)[:, None]).astype(
        jnp.bfloat16
    )
    grad_head = lax.dot_general(
        pooled, grad_logits, (((0,), (0,)), ((), ())), preferred_element_type=jnp.float32
    )
    grad_pooled = lax.dot_general(
        grad_logits, head_low, (((1,), (1,)), ((), ())), preferred_element_type=jnp.float32
    )
    spread_pooled = jnp.broadcast_to(
        (grad_pooled / pixel_count)[:, None, :], (slot_count, pixel_count, width)
    )
    grad_joined = spread_pooled.reshape(slot_count * pixel_count, width) * silu_slope(joined_pre)
    gain_two, shift_two, grad_two = norm_backward(grad_joined, main_two, norm_two, norm_params[2])
    gain_side, shift_side, grad_side = norm_backward(
        grad_joined, side_pre, norm_side, norm_params[4]
    )
    grad_two_maps = grad_two.reshape(slot_count, out_side, out_side, width)
    grad_side_maps = grad_side.reshape(slot_count, out_side, out_side, width)
    grad_conv_two = conv_weight_grad(active, grad_two_maps, 1, 1, 1)
    grad_short = conv_weight_grad(images, grad_side_maps, 2, 0, -1)
    kernel_turned = jnp.transpose(kernel_two[::-1, ::-1], (0, 1, 3, 2))
    grad_active = conv_apply(grad_two_maps, kernel_turned, 1, 1).reshape(
        slot_count * pixel_count, width
    )
    grad_hidden = grad_active * silu_slope(hidden_one)
    gain_one, shift_one, grad_one = norm_backward(grad_hidden, main_pre, norm_one, norm_params[0])
    grad_conv_one = conv_weight_grad(
        images, grad_one.reshape(slot_count, out_side, out_side, width), 2, 1, 0
    )
    grad_norms = jnp.stack([gain_one, shift_one, gain_two, shift_two, gain_side, shift_side])
    grads = (grad_conv_one, grad_conv_two, grad_short, grad_head, grad_norms)
    votes, rows_new, cols_new, moment_new = make_votes(
        grads, row_state[0], col_state[0], bn_moment[0]
    )
    workers = lax.axis_size("dp")
    weights = (conv_one, conv_two, shortcut, classifier, norm_params)
    scales = [scale_for(weight) for weight in weights]
    loss_sum = lax.psum(local_sum, "dp")
    flat_vote = jnp.concatenate([vote.reshape(-1) for vote in votes])
    flat_old = jnp.concatenate([weight.reshape(-1) for weight in weights])
    flat_scale = jnp.concatenate(
        [
            jnp.broadcast_to(scale, (weight.size,))
            for scale, weight in zip(scales, weights)
        ]
    )
    vote_mine = lax.psum_scatter(flat_vote, "dp", tiled=True)
    share = vote_mine.shape[0]
    start = lax.axis_index("dp") * share
    new_mine = lax.dynamic_slice_in_dim(
        flat_old, start, share
    ) - lax.dynamic_slice_in_dim(flat_scale, start, share) * jnp.tanh(
        vote_mine / math.sqrt(workers)
    )
    copies = lax.all_gather(new_mine.astype(jnp.bfloat16), "dp", tiled=True)
    return (
        loss_sum,
        valid_count,
        new_mine,
        copies,
        vote_mine,
        rows_new[None, :],
        cols_new[None, :],
        moment_new[None, :],
    )


def local(
    images,
    valid_slot,
    labels,
    conv_one,
    conv_two,
    shortcut,
    classifier,
    norm_params,
    row_state,
    col_state,
    bn_moment,
):
    new_mine, vote_mine, copies, rows_new, cols_new, moment_new, loss_sum, valid_count = run_step(
        images.reshape(-1, images.shape[-1]),
        conv_one,
        conv_two,
        shortcut,
        classifier.T,
        norm_params,
        valid_slot.reshape(1, -1),
        labels.reshape(1, -1),
        row_state,
        col_state,
        bn_moment,
    )
    copies, new_mine, vote_mine, rows_new, cols_new, moment_new, loss_sum, valid_count = finish(
        (copies, new_mine, vote_mine, rows_new, cols_new, moment_new, loss_sum, valid_count)
    )
    return (
        loss_sum.reshape(()),
        valid_count.reshape(()),
        new_mine.reshape(-1),
        copies.reshape(-1),
        vote_mine.reshape(-1),
        rows_new,
        cols_new,
        moment_new,
    )


def solution(mesh):
    placed = (
        P("dp", None, None, None),
        P("dp"),
        P("dp"),
        P(),
        P(),
        P(),
        P(),
        P(),
        P("dp", None),
        P("dp", None),
        P("dp", None),
    )
    return jax.shard_map(
        local if mesh.shape["dp"] == 32 else local_general,
        mesh=mesh,
        in_specs=placed,
        out_specs=(P(), P(), P("dp"), P(), P("dp"), P("dp", None), P("dp", None), P("dp", None)),
        check_vma=False,
    )
```

```python
import functools
import math

import jax
import jax.numpy as jnp
from jax import lax
from jax.experimental import pallas as pl
from jax.experimental.pallas import tpu as pltpu
from jax.sharding import PartitionSpec as P

STEP = 10
MESH = pl.DeviceIdType.MESH

EPS_NORM = 1e-05
EPS_ROW = 1e-30
EPS_SCALE = 0.001
FORWARD_DIMS = ("NHWC", "HWIO", "NHWC")
WEIGHT_DIMS = ("CHWN", "IHWO", "HWNC")
OWN = 224
TAIL = 16
PIECE = 32
SPAN = 4 * OWN
HALF = SPAN // 2
GROUP = 64


def conv_apply(maps, kernel, stride, margin):
    return lax.conv_general_dilated(
        maps,
        kernel,
        (stride, stride),
        ((margin, margin), (margin, margin)),
        dimension_numbers=FORWARD_DIMS,
        preferred_element_type=jnp.float32,
    )


def conv_weight_grad(maps, grad_out, stride, low_pad, high_pad):
    result = lax.conv_general_dilated(
        maps,
        grad_out,
        (1, 1),
        ((low_pad, high_pad), (low_pad, high_pad)),
        rhs_dilation=(stride, stride),
        dimension_numbers=WEIGHT_DIMS,
        preferred_element_type=jnp.float32,
    )
    return result.reshape(-1, result.shape[3])


def silu_slope(values):
    sigmoid_part = jax.nn.sigmoid(values)
    return sigmoid_part * (1.0 + values * (1.0 - sigmoid_part))


def settle(sum_plain, sum_square, pixels):
    mean_value = sum_plain / pixels
    return (mean_value, lax.rsqrt(sum_square / pixels - mean_value * mean_value + EPS_NORM))


def first_section(images, kernel_one, kernel_short):
    row_count = images.shape[0] * (images.shape[1] // 2) ** 2
    main_pre = conv_apply(images, kernel_one, 2, 1).reshape(row_count, -1)
    side_pre = conv_apply(images, kernel_short, 2, 0).reshape(row_count, -1)
    return (main_pre, side_pre)


def second_section(main_pre, norm_one, norm_params, kernel_two, slot_count, out_side):
    hidden_one = (main_pre - norm_one[0]) * norm_one[1] * norm_params[0] + norm_params[1]
    active = (
        jax.nn.silu(hidden_one).astype(jnp.bfloat16).reshape(slot_count, out_side, out_side, -1)
    )
    main_two = conv_apply(active, kernel_two, 1, 1).reshape(slot_count * out_side * out_side, -1)
    return (hidden_one, active, main_two)


def masked_moments(pixel_weight, values):
    return (jnp.sum(pixel_weight * values, axis=0), jnp.sum(pixel_weight * values * values, axis=0))


def soft_sign(step_raw):
    clip_by = jnp.maximum(1.0, jnp.sqrt(jnp.mean(step_raw * step_raw)))
    return jnp.tanh(step_raw / clip_by)


def make_votes(grads, rows_old, cols_old, moment_old):
    decay_rate = 1.0 - STEP ** (-0.8)
    votes, rows_new, cols_new = ([], [], [])
    row_at, col_at = (0, 0)
    for matrix in grads[:4]:
        row_size, col_size = matrix.shape
        square = matrix * matrix + EPS_ROW
        row_part = decay_rate * rows_old[row_at : row_at + row_size] + (
            1.0 - decay_rate
        ) * jnp.mean(square, axis=1)
        col_part = decay_rate * cols_old[col_at : col_at + col_size] + (
            1.0 - decay_rate
        ) * jnp.mean(square, axis=0)
        second = row_part[:, None] * col_part[None, :] / jnp.mean(row_part)
        votes.append(soft_sign(matrix * lax.rsqrt(second)))
        rows_new.append(row_part)
        cols_new.append(col_part)
        row_at += row_size
        col_at += col_size
    flat_norm = grads[4].reshape(-1)
    moment_new = decay_rate * moment_old + (1.0 - decay_rate) * (flat_norm * flat_norm + EPS_ROW)
    votes.append(soft_sign(flat_norm * lax.rsqrt(moment_new)))
    return (votes, jnp.concatenate(rows_new), jnp.concatenate(cols_new), moment_new)


def norm_backward(grad_out, pre_value, norm_pair, gain_row):
    normed = (pre_value - norm_pair[0]) * norm_pair[1]
    grad_gain = jnp.sum(grad_out * normed, axis=0)
    grad_shift = jnp.sum(grad_out, axis=0)
    grad_pre = (grad_out * gain_row * norm_pair[1]).astype(jnp.bfloat16)
    return (grad_gain, grad_shift, grad_pre)


SCHEDULE = (
    (),
    (),
    (
        (1, 0), (0, 2),
    ),
    (
        (1, 1), (0, 3),
    ),
    (
        (1, 2), (0, 4),
    ),
    (
        (2, 0), (1, 3), (0, 5),
    ),
    (),
    (
        (2, 1), (1, 4), (0, 6),
    ),
    (
        (3, 0), (2, 2), (1, 5), (0, 7),
    ),
    (),
    (
        (3, 1), (2, 3), (1, 6), (0, 8),
    ),
    (
        (3, 2), (2, 4), (1, 7), (4, 0), (3, 3), (2, 5), (1, 8), (4, 1), (3, 4), (2, 6), (1, 9),
        (0, 11), (4, 2), (3, 5), (2, 7), (1, 10), (0, 12), (5, 0), (4, 3), (3, 6), (2, 8),
        (1, 11), (0, 13), (5, 1), (4, 4), (3, 7), (2, 9), (1, 12), (6, 0), (5, 2), (4, 5),
        (3, 8), (2, 10), (1, 13), (6, 1), (5, 3), (4, 6), (3, 9), (2, 11), (6, 2), (5, 4),
        (4, 7), (8, 0), (3, 10), (2, 12), (7, 0), (6, 3), (5, 5), (4, 8), (3, 11), (2, 13),
        (7, 1), (6, 4), (5, 6), (4, 9), (3, 12), (7, 2), (6, 5), (5, 7), (4, 10), (3, 13),
        (7, 3), (6, 6), (5, 8), (4, 11), (7, 4), (6, 7), (5, 9), (4, 12), (7, 5), (6, 8),
        (5, 10), (4, 13), (7, 6), (6, 9), (5, 11), (7, 7), (6, 10), (5, 12), (7, 8), (6, 11),
        (5, 13), (7, 9), (9, 0), (6, 12), (7, 10), (6, 13), (7, 11), (7, 12), (9, 1), (7, 13),
        (9, 2),
    ),
)


def place():
    me = lax.axis_index("dp")
    core = lax.rem(me, 2)
    x = lax.rem(lax.div(me, 2), 2)
    y = lax.rem(lax.div(me, 4), 2)
    z = lax.div(me, 8)
    return me, core, x, y, z


def send(src, dst, send_sem, recv_sem, partner):
    copy = pltpu.make_async_remote_copy(
        src_ref=src,
        dst_ref=dst,
        send_sem=send_sem,
        recv_sem=recv_sem,
        device_id=(partner,),
        device_id_type=MESH,
    )
    copy.start()
    return copy


def scale_of(row, scales, edges):
    picked = scales[2]
    picked = jnp.where(row < edges[1], scales[1], picked)
    return jnp.where(row < edges[0], scales[0], picked)


def make_units(edges):
    one, two, short = edges[0] // 16, edges[1] // 16, edges[2] // 16
    units = []
    for k in range((two - one) // 32):
        units.append((one + 32 * k, 1, k % 2 == 0, 16, (1, 1)))
    for k in range(one // 32):
        units.append((32 * k, 1, k % 2 == 1, 16, (0, 0)))
    at = one // 32 * 32
    assert one - at == 16 and short - two == 16
    units.append((at, 1, False, two - at, (0, 2)))
    return units


def settle_rows(sums, pixels, gain, shift):
    mean = sums[0] / pixels
    inv = lax.rsqrt(sums[1] / pixels - mean * mean + EPS_NORM)
    slope = gain * inv
    return mean, inv, slope, shift - mean * slope


def gate(values):
    return 0.5 * jnp.tanh(0.5 * values) + 0.5


def eye_mask(rows, columns, offset=0):
    down = lax.broadcasted_iota(jnp.int32, (rows, columns), 0) + offset
    return down == lax.broadcasted_iota(jnp.int32, (rows, columns), 1)


def column_of(row, size):
    spread = jnp.where(eye_mask(size, size), jnp.broadcast_to(row, (size, size)), 0)
    return jnp.sum(spread, axis=1, keepdims=True)


def total_of(values):
    return jnp.sum(jnp.sum(values, axis=0, keepdims=True), axis=1, keepdims=True)


def fold(values):
    return jnp.sum(values.reshape(values.shape[0] // 8, 8, values.shape[1]), axis=0)


def cast_weight(source, target, square_ref, taps, depth, fetches):
    step = 256
    for tap in taps:
        chunk = source.shape[0] // depth // len(fetches)
        if tap % chunk == 0:
            fetches[tap // chunk].wait()
        new_tap = (tap % 3) * 3 + tap // 3

        for start in range(0, depth, step):
            values = source[pl.ds(tap * depth + start, step), :]
            target[new_tap, pl.ds(start, step), :] = values.astype(jnp.bfloat16)
            square_ref[...] += fold(values * values)


def row_block(grad, row_at, rows_old, rows_new, level, k, carry):
    width = grad.shape[1]
    keep = 1.0 - STEP ** (-0.8)
    step = 128
    quarters = width // 128
    col_sum, row_sum = carry
    start = k * step
    lanes = pl.ds(row_at + start, step)
    if not isinstance(k, int):
        start = pl.multiple_of(start, step)
        lanes = pl.ds(pl.multiple_of(row_at + start, step), step)
    old = rows_old[:, lanes] * keep
    line = jnp.zeros((8, 128), jnp.float32)
    for m in range(step // 8):
        block = grad[pl.ds(start + 8 * m, 8), :]
        square = block * block
        col_sum = col_sum + square
        part = square[:, :128]
        for q in range(1, quarters):
            part = part + square[:, 128 * q : 128 * (q + 1)]
        part = part * ((1.0 - keep) / width)
        diagonal = eye_mask(8, 128, 8 * m)
        part = part + jnp.where(diagonal, jnp.broadcast_to(old, (8, 128)), 0.0)
        row = jnp.sum(part, axis=1, keepdims=True) + (1.0 - keep) * EPS_ROW
        row = jnp.broadcast_to(row, (8, 128))
        level[pl.ds(start + 8 * m, 8), :] = row
        row_sum = row_sum + row
        line = line + jnp.where(diagonal, row, 0.0)
    rows_new[:, lanes] = jnp.sum(line, axis=0, keepdims=True)
    return col_sum, row_sum


def no_sums(width):
    return jnp.zeros((8, width), jnp.float32), jnp.zeros((8, 128), jnp.float32)


def factored_votes(
    grad, rows, row_at, rows_old, rows_new, col_old, level, votes, vote_at, between, after, sums
):
    width = grad.shape[1]
    keep = 1.0 - STEP ** (-0.8)
    step = 128
    quarters = width // 128
    if sums is None:
        sums = lax.fori_loop(
            0,
            rows // step,
            functools.partial(row_block, grad, row_at, rows_old, rows_new, level),
            no_sums(width),
        )
    col_sum, row_sum = sums

    col_new = keep * col_old + (1.0 - keep) * (
        jnp.sum(col_sum, axis=0, keepdims=True) / rows + EPS_ROW
    )
    scale = lax.rsqrt(col_new)
    root_mean = jnp.sqrt(jnp.sum(row_sum, axis=0, keepdims=True) / rows)

    run = 2 * step

    def second(k, carry):
        start = pl.multiple_of(k * run, run)
        for m in range(run // 8):
            here = pl.ds(start + 8 * m, 8)
            factor = lax.rsqrt(level[here, :]) * root_mean
            level[here, :] = factor
            raw = grad[here, :] * jnp.concatenate([factor] * quarters, axis=1) * scale
            power = raw * raw
            part = power[:, :128]
            for q in range(1, quarters):
                part = part + power[:, 128 * q : 128 * (q + 1)]
            carry = carry + part
        return carry

    between[0]()
    power = lax.fori_loop(0, rows // run, second, jnp.zeros((8, 128), jnp.float32))
    between[1]()
    clip = jnp.maximum(1.0, jnp.sqrt(total_of(power) / (rows * width)))
    scale = scale / clip

    def third(start, count):
        for m in range(count // 16):
            here = pl.ds(start + 16 * m, 16)
            factor = level[here, :]
            factor = jnp.concatenate([factor] * quarters, axis=1)
            vote = jnp.tanh(grad[here, :] * factor * scale).astype(jnp.bfloat16)
            at = (vote_at + start) * 4 + GROUP * m
            for q in range(quarters):
                votes[pl.ds(at + 16 * q, 16), :] = vote[:, 128 * q : 128 * (q + 1)]

    for k, start in enumerate(range(0, rows, 512)):
        third(start, min(512, rows - start))
        after(k)
    return col_new


def step_kernel(
    edges,
    units,
    root,
    images,
    one_hbm,
    two_hbm,
    short_hbm,
    head_ref,
    norm_ref,
    valid_ref,
    label_ref,
    row_ref,
    col_ref,
    moment_ref,
    new_ref,
    vote_ref,
    out_ref,
    row_new,
    col_new,
    moment_new,
    loss_ref,
    count_ref,
    xs,
    grad_one,
    grad_two,
    grad_short,
    low_one,
    low_two,
    low_short,
    main_pre,
    side_pre,
    main_two,
    active,
    back_two,
    back_one,
    back_side,
    active_t,
    xs_t,
    head_pad,
    level,
    square,
    post_one,
    plane_one,
    line_one,
    post_two,
    plane_two,
    line_two,
    tail_post,
    tail_plane,
    tail_line,
    core_in,
    wide_in,
    deep_in,
    line_in,
    sum_low,
    landed,
    total,
    own_weight,
    weight,
    vote_flat,
    new_flat,
    tail_vote,
    tail_new,
    fetch_sem,
    small_send,
    small_recv,
    sent,
    rs_recv,
    line_recv,
    pass_send,
    land_recv,
    spread_recv,
    ag_recv,
    free_sem,
    load_sem,
):
    slots, in_width = xs.shape[4:]
    width = main_pre.shape[1]
    side = 4
    band = side * slots
    pixel_count = side * side
    side_pixels = 4 * pixel_count
    classes = head_ref.shape[0]
    keep = 1.0 - STEP ** (-0.8)
    low = jnp.bfloat16
    f32 = jnp.float32

    me, core, x, y, z = place()
    flip_core = me + 1 - 2 * core
    flip_x = me + 2 - 4 * x
    flip_y = me + 4 - 8 * y
    spot = lax.rem(me, 8)
    near = [z * 8 + lax.rem(spot + k, 8) for k in range(1, 8)]
    far = [lax.rem(z + k, 4) * 8 + spot for k in range(1, 4)]
    others = [lax.rem(me + k, 32) for k in range(1, 32)]

    count = images.shape[0]
    loads = []
    for half in range(2):
        lanes = slice(128 * half, 128 * (half + 1))
        loads.append(
            pltpu.make_async_copy(
                images.at[:, lanes], core_in.at[pl.ds(half * count, count)], load_sem.at[half]
            )
        )
        loads[half].start()

    def chunks_of(source, target, first, count):
        rows = source.shape[0] // count
        return [
            pltpu.make_async_copy(
                source.at[pl.ds(k * rows, rows)],
                target.at[pl.ds(k * rows, rows)],
                fetch_sem.at[first + k],
            )
            for k in range(count)
        ]

    fetch_one = chunks_of(one_hbm, grad_one, 0, 3)
    fetch_short = chunks_of(short_hbm, grad_short, 3, 1)
    fetch_two = chunks_of(two_hbm, grad_two, 4, 3)
    for fetch in fetch_one + fetch_short:
        fetch.start()
    barrier = pltpu.get_barrier_semaphore()
    for partner in others:
        pl.semaphore_signal(barrier, inc=1, device_id=(partner,), device_id_type=MESH)

    def fetch_rows(row, count, place_at, sem):
        parts = (
            (one_hbm, 0, edges[0]),
            (two_hbm, edges[0], edges[1]),
            (short_hbm, edges[1], edges[2]),
        )
        for ref, first, last in parts:

            @pl.when(jnp.logical_and(row >= first, row < last))
            def _():
                start = pl.multiple_of(row - first, count)
                pltpu.make_async_copy(
                    ref.at[pl.ds(start, count)], weight.at[pl.ds(place_at, count)], sem
                ).start()

    first_row = me * OWN

    for half in range(2):
        lanes = slice(128 * half, 128 * (half + 1))
        loads[half].wait()
        apart = side_pixels + 8

        @pl.loop(0, slots // 4)
        def _(k):
            for m in range(4):
                slot = k * 4 + m
                source = pl.multiple_of(half * count + slot * side_pixels, side_pixels)
                target = pl.multiple_of(slot * apart, 8)
                level[pl.ds(target, side_pixels), :] = core_in[
                    pl.ds(source, side_pixels), :
                ].astype(f32)

        for h in range(2 * side):
            for w in range(2 * side):
                rows = level[pl.ds(2 * side * h + w, slots, stride=apart), :]
                xs[w % 2, w // 2, h % 2, h // 2, :, lanes] = rows.astype(low)

    scales = {}

    def scale_from(weight_square, size):
        return jnp.maximum(EPS_SCALE, jnp.sqrt(total_of(weight_square) / size))

    exchanges = (
        (post_one, plane_one, line_one),
        (post_two, plane_two, line_two),
        (tail_post, tail_plane, tail_line),
    )

    def exchange_start(which, values):
        mine_ref, plane_ref, _ = exchanges[which]
        mine_ref[...] = values
        plane_ref[spot] = values
        return [
            send(
                mine_ref,
                plane_ref.at[spot],
                small_send.at[which, k],
                small_recv.at[which, k],
                partner,
            )
            for k, partner in enumerate(near)
        ]

    def pack_rows(rows):
        pieces = [row[:, 128 * q : 128 * (q + 1)] for row in rows for q in range(4)]
        pad = -len(pieces) % 8
        if pad:
            pieces.append(jnp.zeros((pad, 128), f32))
        return jnp.concatenate(pieces, axis=0)

    def unpack_row(lines_in, k):
        return jnp.concatenate([lines_in[4 * k + q : 4 * k + q + 1] for q in range(4)], axis=1)

    def exchange_middle(which, copies):
        _, plane_ref, line_ref = exchanges[which]
        for copy in copies:
            copy.wait()
        line_ref[z] = functools.reduce(lambda a, b: a + b, [plane_ref[k] for k in range(8)])
        return [
            send(
                line_ref.at[z],
                line_ref.at[z],
                small_send.at[which, 7 + k],
                small_recv.at[which, 7 + k],
                partner,
            )
            for k, partner in enumerate(far)
        ]

    def exchange_end(which, copies):
        line_ref = exchanges[which][2]
        for copy in copies:
            copy.wait()
        return (line_ref[0] + line_ref[1]) + (line_ref[2] + line_ref[3])

    def lines(start, count):
        return pl.ds(pl.multiple_of(start, 16), count)

    sizes = [GROUP * unit[1] for unit in units]
    starts = [sum(sizes[:k]) for k in range(len(units) + 1)]

    def part_of(ref, u, share, start, count):
        return ref.at[lines(share * starts[u] + start, count)]

    def places(u):
        if units[u][2]:
            return x, y, flip_x, flip_y
        return y, x, flip_y, flip_x

    def unit_start(u, cc):
        return GROUP * units[u][0] + cc * (GROUP * units[u][3])

    def own_group(u):
        first, second, _, _ = places(u)
        return units[u][0] + core * units[u][3] + (first * 8 + second * 4 + z) * units[u][1]

    def halve(source, target, u, stage, partner):
        return send(source, target, sent.at[stage], rs_recv.at[u, stage], partner)

    def scatter_start(u):
        size = 16 * sizes[u]
        return halve(
            out_ref.at[lines(unit_start(u, 1 - core), size)],
            part_of(core_in, u, 16, 0, size),
            u,
            0,
            flip_core,
        )

    def add_to(ref, u, share, source_ref, source_start):
        size = share * sizes[u]
        here = lines(share * starts[u], size)
        ref[here, :] = ref[here, :] + source_ref[lines(source_start, size), :]

    def sent_all(kind, ref):
        pltpu.make_async_remote_copy(
            src_ref=ref,
            dst_ref=ref,
            send_sem=sent.at[kind],
            recv_sem=rs_recv.at[0, 0],
            device_id=(flip_core,),
            device_id_type=MESH,
        ).wait_send()

    def scatter_one(u, copy):
        copy.wait_recv()
        add_to(core_in, u, 16, out_ref, unit_start(u, core))
        if u == len(units) - 1:
            sent_all(0, core_in)
            pl.semaphore_signal(free_sem, inc=1, device_id=(flip_core,), device_id_type=MESH)
        first, _, flip_first, _ = places(u)
        size = 8 * sizes[u]
        return halve(
            part_of(core_in, u, 16, (1 - first) * size, size),
            part_of(wide_in, u, 8, 0, size),
            u,
            1,
            flip_first,
        )

    def scatter_two(u, copy):
        copy.wait_recv()
        first, second, _, flip_second = places(u)
        add_to(wide_in, u, 8, core_in, 16 * starts[u] + first * 8 * sizes[u])
        size = 4 * sizes[u]
        return halve(
            part_of(wide_in, u, 8, (1 - second) * size, size),
            part_of(deep_in, u, 4, 0, size),
            u,
            2,
            flip_second,
        )

    def line_copy(u, k):
        plane_to = lax.rem(z + k, 4)
        return pltpu.make_async_remote_copy(
            src_ref=part_of(deep_in, u, 4, plane_to * sizes[u], sizes[u]),
            dst_ref=part_of(line_in, u, 4, z * sizes[u], sizes[u]),
            send_sem=sent.at[3],
            recv_sem=line_recv.at[u],
            device_id=(plane_to * 8 + spot,),
            device_id_type=MESH,
        )

    def scatter_three(u, copy):
        copy.wait_recv()
        _, second, _, _ = places(u)
        add_to(deep_in, u, 4, wide_in, 8 * starts[u] + second * 4 * sizes[u])
        for k in (3, 2, 1):
            line_copy(u, k).start()
        here = lines(4 * starts[u] + z * sizes[u], sizes[u])
        line_in[here, :] = deep_in[here, :]

    def three_landed(u, sem):
        ref = part_of(line_in, u, 4, 0, 3 * sizes[u])
        pltpu.make_async_remote_copy(
            src_ref=ref,
            dst_ref=ref,
            send_sem=sent.at[3],
            recv_sem=sem.at[u],
            device_id=(far[0],),
            device_id_type=MESH,
        ).wait_recv()

    groups = (edges[2] + TAIL) // 16
    spare = (groups - 1) // 32
    passes = []

    def land(local, group, to, slot, index):
        source = sum_low.at[lines(local * GROUP, GROUP)]
        target = landed.at[lines(slot * GROUP, GROUP)]
        copy = pltpu.make_async_remote_copy(
            src_ref=source,
            dst_ref=target,
            send_sem=pass_send.at[index],
            recv_sem=land_recv.at[slot],
            device_id=(to,),
            device_id_type=MESH,
        )
        return copy, source, target

    def pass_on(u):
        for m in range(units[u][1]):
            local = starts[u] // GROUP + m
            group = own_group(u) + m
            to, slot = lax.div(group, spare), lax.rem(group, spare)

            def one(receiver, at, index):
                copy, source, target = land(local, group, receiver, at, index)

                @pl.when(receiver != me)
                def _():
                    copy.start()

                @pl.when(receiver == me)
                def _():
                    target[...] = source[...]

                return copy

            first = jnp.logical_and(slot == 0, group > 0)
            ahead = lax.rem(to + 31, 32)
            passes.append((to != me, one(to, slot, 2 * local)))

            @pl.when(first)
            def _():
                one(ahead, spare, 2 * local + 1)

            copy = land(local, group, ahead, spare, 2 * local + 1)[0]
            passes.append((jnp.logical_and(first, ahead != me), copy))

    def flat_rows(row, q, values, ref):
        ref[pl.ds(row * 4 + q, 8, stride=4), :] = values

    def old_rows(u, cc):
        matrix = units[u][4][cc]
        base = edges[matrix - 1] if matrix else 0
        return (one_hbm, two_hbm, short_hbm)[matrix], 16 * own_group(u) - base, 16 * units[u][1]

    def own_fetch(u):
        target = own_weight.at[pl.ds(starts[u] // 4, 16 * units[u][1])]
        matrices = units[u][4]
        for cc in range(2):
            if cc and matrices[0] == matrices[1]:
                continue

            @pl.when((core == cc) if matrices[0] != matrices[1] else (core >= 0))
            def _():
                ref, row, count = old_rows(u, cc)
                pltpu.make_async_copy(
                    ref.at[pl.ds(pl.multiple_of(row, 16), count)], target, fetch_sem.at[9 + u]
                ).start()

    def spread_copy(u, k):
        own = out_ref.at[lines(own_group(u) * GROUP, sizes[u])]
        return pltpu.make_async_remote_copy(
            src_ref=own,
            dst_ref=own,
            send_sem=sent.at[4],
            recv_sem=spread_recv.at[u],
            device_id=(far[k - 1],),
            device_id_type=MESH,
        )

    def own_block(u):
        size = sizes[u]
        three_landed(u, line_recv)
        here = pl.ds(starts[u], size)
        low_sum = functools.reduce(
            lambda a, b: a + b,
            [line_in[pl.ds(4 * starts[u] + t * size, size), :].astype(f32) for t in range(4)],
        ).astype(low)
        sum_low[here, :] = low_sum
        summed = low_sum.astype(f32)
        target = own_weight.at[pl.ds(starts[u] // 4, 16 * units[u][1])]
        pltpu.make_async_copy(target, target, fetch_sem.at[9 + u]).wait()
        matrices = units[u][4]
        scale = scales[matrices[0]]
        if matrices[0] != matrices[1]:
            scale = jnp.where(core == 0, scale, scales[matrices[1]])
        turned = jnp.tanh(summed * root) * scale
        for m in range(units[u][1]):
            row = starts[u] // 4 + 16 * m
            for part in (0, 8):
                for q in range(4):
                    at = GROUP * m + 16 * q + part
                    old = own_weight[pl.ds(row + part, 8), 128 * q : 128 * (q + 1)]
                    flat_rows(row + part, q, old - turned[at : at + 8], new_flat)
        out_ref[lines(own_group(u) * GROUP, size), :] = new_flat[here, :].astype(low)
        for k in (3, 2, 1):
            spread_copy(u, k).start()
        pass_on(u)

    def piece(rows, u, stage, partner):
        return send(
            out_ref.at[rows], out_ref.at[rows], sent.at[5 + stage], ag_recv.at[u, stage], partner
        )

    def gather_one(u):
        three_landed(u, spread_recv)
        first, second, _, flip_second = places(u)
        size = 4 * sizes[u]
        start = unit_start(u, core) + (2 * first + second) * size
        return piece(lines(start, size), u, 0, flip_second)

    def gather_two(u, copy):
        copy.wait_recv()
        first, _, flip_first, _ = places(u)
        size = 8 * sizes[u]
        return piece(lines(unit_start(u, core) + first * size, size), u, 1, flip_first)

    def gather_three(u, copy):
        copy.wait_recv()
        if u == 0:
            pl.semaphore_wait(free_sem, 1)
        return piece(lines(unit_start(u, core), 16 * sizes[u]), u, 2, flip_core)

    def renew(row, at_row):
        scale = scale_of(at_row, [scales[k] for k in range(3)], edges)
        for part in (0, 8):
            for q in range(4):
                summed = total[pl.ds(row * 4 + 16 * q + part, 8), :]
                old = weight[pl.ds(row + part, 8), 128 * q : 128 * (q + 1)]
                fresh = old - scale * jnp.tanh(summed * root)
                flat_rows(row + part, q, summed, vote_flat)
                flat_rows(row + part, q, fresh, new_flat)

    valid_column = column_of(valid_ref[...].astype(f32), slots)
    weight_slot = jnp.broadcast_to(valid_column, (slots, width))
    weight_band = jnp.concatenate([weight_slot] * side, axis=0)

    square[...] = jnp.zeros_like(square)
    cast_weight(grad_one, low_one, square, range(9), in_width, fetch_one)
    scales[0] = scale_from(square[...], grad_one.size)
    square[...] = jnp.zeros_like(square)
    cast_weight(grad_short, low_short, square, range(1), in_width, fetch_short)
    scales[2] = scale_from(square[...], grad_short.size)
    for fetch in fetch_two:
        fetch.start()

    def image_taps(j):
        pieces = []
        for b in range(3):
            column = j if b else j - 1
            if column < 0:
                continue
            across = 0 if b == 1 else 1
            for a in range(3):
                if a == 1:
                    piece = xs[across, column, 0].reshape(band, in_width)
                elif a == 2:
                    piece = xs[across, column, 1].reshape(band, in_width)
                else:
                    piece = xs[across, column, 1, : side - 1].reshape(band - slots, in_width)
                    piece = jnp.concatenate([jnp.zeros((slots, in_width), low), piece], axis=0)
                pieces.append(piece)
        return jnp.concatenate(pieces, axis=1)

    def moments(values):
        weighted = values * weight_band
        return (
            jnp.sum(weighted, axis=0, keepdims=True),
            jnp.sum(weighted * values, axis=0, keepdims=True),
        )

    def add_up(old, new):
        return [a + b for a, b in zip(old, new)]

    none = jnp.zeros((1, width), f32)
    main_sums, side_sums = [none, none], [none, none]
    for j in range(side):
        here = pl.ds(j * band, band)
        low_rows = low_one[3 if j == 0 else 0 :].reshape(-1, width)
        value = jnp.dot(image_taps(j), low_rows, preferred_element_type=f32)
        main_pre[here, :] = value
        main_sums = add_up(main_sums, moments(value))
        value = jnp.dot(
            xs[0, j, 0].reshape(band, in_width), low_short[0], preferred_element_type=f32
        )
        side_pre[here, :] = value
        side_sums = add_up(side_sums, moments(value))

    count = jnp.broadcast_to(jnp.sum(valid_column, axis=0, keepdims=True), (1, width))
    pl.semaphore_wait(barrier, len(others))
    copies = exchange_start(
        0, pack_rows(main_sums + side_sums + [count])
    )
    square[...] = jnp.zeros_like(square)
    cast_weight(grad_two, low_two, square, range(5), width, fetch_two)
    copies = exchange_middle(0, copies)
    cast_weight(grad_two, low_two, square, range(5, 9), width, fetch_two)
    scales[1] = scale_from(square[...], grad_two.size)
    border = jnp.zeros((side, 1, slots, width), low)
    active[:, 0:1] = border
    active[:, side + 1 :] = border
    back_two[:, 0:1] = border
    back_two[:, side + 1 :] = border
    back_one[:, side:] = border
    head_pad[...] = jnp.zeros_like(head_pad)
    head_pad[:classes, :] = head_ref[...]
    head = head_pad[:16, :]
    scales[3] = scale_from(head * head, head_ref.size)
    params = norm_ref[...]
    scales[4] = scale_from(params * params, norm_ref.size)
    sums = exchange_end(0, copies)
    sums = [unpack_row(sums, k) for k in range(5)]

    valid_count = sums[4]
    count_ref[...] = valid_count[:, :1]
    denominator = jnp.maximum(valid_count, 1.0)
    pixels = denominator * pixel_count
    gains = [norm_ref[k : k + 1, :] for k in range(6)]
    mean_one, inv_one, slope_one, base_one = settle_rows(
        (sums[0], sums[1]), pixels, gains[0], gains[1]
    )
    mean_side, inv_side, slope_side, base_side = settle_rows(
        (sums[2], sums[3]), pixels, gains[4], gains[5]
    )

    for j in range(side):
        hidden = main_pre[pl.ds(j * band, band), :] * slope_one + base_one
        active[j, 1 : side + 1] = (
            (hidden * gate(hidden)).astype(low).reshape(side, slots, width)
        )
    two_sums = [none, none]
    for j in range(side):
        taps = [b for b in range(3) if 0 <= j + b - 1 < side]
        pieces = [
            active[j + b - 1, a : a + side].reshape(band, width) for b in taps for a in range(3)
        ]
        low_rows = low_two[3 * taps[0] : 3 * taps[-1] + 3].reshape(-1, width)
        value = jnp.dot(jnp.concatenate(pieces, axis=1), low_rows, preferred_element_type=f32)
        main_two[pl.ds(j * band, band), :] = value
        two_sums = add_up(two_sums, moments(value))
    copies = exchange_start(1, pack_rows(two_sums))
    for k in range(OWN // PIECE):
        fetch_rows(first_row + k * PIECE, PIECE, k * PIECE, fetch_sem.at[7])
    fetch_rows(first_row + OWN, TAIL, OWN, fetch_sem.at[8])
    for u in range(len(units)):
        own_fetch(u)
    for j in range(side):
        block = active[j, 1 : side + 1].reshape(band, width)
        active_t[:, j * band : (j + 1) * band] = block.T
    label_column = column_of(label_ref[...].astype(f32), slots).astype(jnp.int32)
    head_low = head_pad[...].astype(low)
    copies = exchange_middle(1, copies)
    for across in range(2):
        for down in range(2):
            for j in range(side):
                block = xs[across, j, down].reshape(band, in_width)
                xs_t[across, down, :, j * band : (j + 1) * band] = block.T
    sums = exchange_end(1, copies)
    sums = [unpack_row(sums, k) for k in range(2)]
    mean_two, inv_two, slope_two, base_two = settle_rows(
        (sums[0], sums[1]), pixels, gains[2], gains[3]
    )

    base_joined = base_two + base_side

    quarters = [slice(128 * q, 128 * (q + 1)) for q in range(width // 128)]

    def joined_of(here, lanes):
        return (
            main_two[here, lanes] * slope_two[:, lanes]
            + side_pre[here, lanes] * slope_side[:, lanes]
            + base_joined[:, lanes]
        )

    pooled = []
    for lanes in quarters:
        total_joined = jnp.zeros((slots, 128), f32)
        for p in range(pixel_count):
            joined = joined_of(pl.ds(p * slots, slots), lanes)
            total_joined = total_joined + joined * gate(joined)
        pooled.append(total_joined)
    pooled = jnp.concatenate(pooled, axis=1)
    pooled = (pooled / pixel_count).astype(low)
    logits = lax.dot_general(
        pooled, head_low, (((1,), (1,)), ((), ())), preferred_element_type=f32
    )
    lane = lax.broadcasted_iota(jnp.int32, logits.shape, 1)
    real = lane < classes
    largest = jnp.max(jnp.where(real, logits, -jnp.inf), axis=1, keepdims=True)
    powers = jnp.where(real, jnp.exp(jnp.where(real, logits - largest, 0.0)), 0.0)
    total_power = jnp.sum(powers, axis=1, keepdims=True)
    onehot = jnp.where(lane == label_column, 1.0, 0.0)
    entropy = largest + jnp.log(total_power) - jnp.sum(onehot * logits, axis=1, keepdims=True)
    loss = jnp.sum(entropy * valid_column, axis=0, keepdims=True)
    grad_logits = (
        (powers / total_power - onehot) * (valid_column / denominator[:, :1])
    ).astype(low)
    grad_head = lax.dot_general(
        grad_logits, pooled, (((0,), (0,)), ((), ())), preferred_element_type=f32
    )[:16]
    grad_pooled = jnp.dot(grad_logits, head_low, preferred_element_type=f32) / pixel_count

    join_sums = []
    for lanes in quarters:
        three = [jnp.zeros((8, 128), f32)] * 3
        for p in range(pixel_count):
            here = pl.ds(p * slots, slots)
            joined = joined_of(here, lanes)
            opened = gate(joined)
            grad = grad_pooled[:, lanes] * (opened * (1.0 + joined * (1.0 - opened)))
            normed_two = (main_two[here, lanes] - mean_two[:, lanes]) * inv_two[:, lanes]
            normed_side = (side_pre[here, lanes] - mean_side[:, lanes]) * inv_side[:, lanes]
            new = (grad * normed_two, grad * normed_side, grad)
            three = [old + fold(each) for old, each in zip(three, new)]
            back_two[p // side, 1 + p % side, :, lanes] = (grad * slope_two[:, lanes]).astype(low)
            back_side[here, lanes] = (grad * slope_side[:, lanes]).astype(low)
        join_sums.append([jnp.sum(each, axis=0, keepdims=True) for each in three])
    gain_two, gain_side, shift_two = [jnp.concatenate(each, axis=1) for each in zip(*join_sums)]

    two_passed = no_sums(width)
    for b in range(3):
        first, last = max(0, b - 1), min(side, side + b - 1)
        left = active_t[:, first * band : last * band]
        for a in range(3):
            right = back_two[first - b + 1 : last - b + 1, 2 - a : 2 - a + side]
            tap = a * 3 + b
            grad_two[pl.ds(tap * width, width), :] = jnp.dot(
                left, right.reshape(-1, width), preferred_element_type=f32
            )
            for k in range(tap * width // 128, (tap + 1) * width // 128):
                two_passed = row_block(
                    grad_two, edges[0], row_ref, row_new, level, k, two_passed
                )

    def nothing():
        pass

    def matrix_votes(k, grad, between, after, sums=None):
        here = pl.ds(k * width, width)
        start = edges[k - 1] if k else 0
        col_new[:, here] = factored_votes(
            grad,
            grad.shape[0],
            start,
            row_ref,
            row_new,
            col_ref[:, here],
            level,
            out_ref,
            start,
            between,
            after,
            sums,
        )

    kept = {}

    def tail_step():
        sums = exchange_end(2, kept["tail"])
        loss_ref[...] = sums[GROUP : GROUP + 1, :1]
        sums = sums[:GROUP]
        old = jnp.concatenate([head_ref[...], norm_ref[...]], axis=0)
        old = jnp.concatenate([old[:, 128 * q : 128 * (q + 1)] for q in range(4)], axis=0)
        down = lax.broadcasted_iota(jnp.int32, (GROUP, 128), 0)
        scale = jnp.where(lax.rem(down, TAIL) < classes, scales[3], scales[4])
        fresh = old - scale * jnp.tanh(sums * root)
        both = jnp.concatenate([sums, fresh], axis=0)
        high = both.astype(low)
        rest = both - high.astype(f32)
        middle = rest.astype(low)
        parts = jnp.concatenate([high, middle, (rest - middle.astype(f32)).astype(low)], axis=0)
        length = 128 * classes
        gap = lax.broadcasted_iota(jnp.int32, (128, length), 1) - classes * (
            lax.broadcasted_iota(jnp.int32, (128, length), 0)
        )
        chosen = jnp.where(jnp.logical_and(gap >= 0, gap < classes), 1.0, 0.0).astype(low)
        moved = jnp.dot(parts, chosen, preferred_element_type=f32)
        moved = moved[: 2 * GROUP] + moved[2 * GROUP : 4 * GROUP] + moved[4 * GROUP :]
        place_of = lax.broadcasted_iota(jnp.int32, (TAIL, length), 1).astype(f32)
        class_of = place_of - classes * jnp.floor((place_of + 0.5) / classes)
        here = lax.broadcasted_iota(jnp.int32, (TAIL, length), 0).astype(f32) == class_of
        for which, ref in enumerate((tail_vote, tail_new)):
            for q in range(4):
                block = moved[GROUP * which + TAIL * q : GROUP * which + TAIL * (q + 1)]
                line = jnp.sum(jnp.where(here, block, 0.0), axis=0, keepdims=True)
                for k in range(classes):
                    ref[classes * q + k : classes * q + k + 1, :] = line[:, 128 * k : 128 * (k + 1)]
                for k in range(TAIL - classes):
                    at = 4 * (classes + k) + q
                    row = TAIL * q + classes + k
                    ref[at : at + 1, :] = (sums, fresh)[which][row : row + 1]
        out_ref[pl.ds(32 * SPAN, GROUP), :] = tail_new[...].astype(low)

    def return_slots(slots_here):
        mine = [own_group(u) for u in range(len(units))]
        for slot in slots_here:
            group = me * spare + slot
            own = group < 0
            for u, unit in enumerate(units):
                inside = jnp.logical_and(group >= mine[u], group < mine[u] + unit[1])
                own = jnp.logical_or(own, inside)

            @pl.when(jnp.logical_and(jnp.logical_not(own), group < groups - 1))
            def _():
                land(0, group, me, slot, 0)[0].wait_recv()

        first, last = slots_here[0], min(slots_here[-1] + 1, spare)
        here = pl.ds(first * GROUP, (last - first) * GROUP)
        total[here, :] = landed[here, :].astype(f32)

        @pl.loop(first, last)
        def _(k):
            row = pl.multiple_of(k * 16, 16)
            renew(row, first_row + row)

    def return_step(part):
        if part == 0:
            pltpu.make_async_copy(
                weight.at[pl.ds(0, OWN)], weight.at[pl.ds(0, OWN)], fetch_sem.at[7]
            ).wait()
            return_slots(range(0, 7))
        elif part == 1:
            return_slots(range(7, spare + 1))
        else:

            @pl.when(me < 31)
            def _():
                pltpu.make_async_copy(
                    weight.at[pl.ds(OWN, TAIL)], weight.at[pl.ds(OWN, TAIL)], fetch_sem.at[8]
                ).wait()
                total[pl.ds(SPAN, GROUP), :] = landed[pl.ds(SPAN, GROUP), :].astype(f32)
                renew(OWN, first_row + OWN)

            @pl.when(me == 31)
            def _():
                vote_flat[pl.ds(SPAN, GROUP), :] = tail_vote[...]
                new_flat[pl.ds(SPAN, GROUP), :] = tail_new[...]

            shift = 2 * me
            share = vote_ref.shape[0]
            vote_ref[...] = vote_flat[pl.ds(shift, share), :]
            new_ref[...] = new_flat[pl.ds(shift, share), :]

    in_flight = {}
    steps = (
        lambda u, copy: scatter_start(u),
        scatter_one,
        scatter_two,
        scatter_three,
        lambda u, copy: own_block(u),
        lambda u, copy: gather_one(u),
        gather_two,
        gather_three,
        lambda u, copy: tail_step(),
        lambda u, copy: return_step(u),
    )

    def go(number, u):
        got = steps[number](u, in_flight.get(u))
        if number < 8:
            in_flight[u] = got

    def turn(number):
        for step_number, u in SCHEDULE[number]:
            go(step_number, u)

    early = edges[1] // 512 - edges[0] // 512
    matrix_votes(1, grad_two, (nothing, nothing), lambda k: go(0, k) if k < 2 else None, two_passed)
    turn(0)

    gain_one, shift_one = none, none
    for j in range(side):
        taps = [b for b in range(3) if 0 <= j - b + 1 < side]
        pieces = [
            back_two[j - b + 1, 2 - a : 2 - a + side].reshape(band, width)
            for b in taps
            for a in range(3)
        ]
        weights = jnp.concatenate([low_two[b * 3 + a] for b in taps for a in range(3)], axis=1)
        grad = lax.dot_general(
            jnp.concatenate(pieces, axis=1),
            weights,
            (((1,), (1,)), ((), ())),
            preferred_element_type=f32,
        )
        before = main_pre[pl.ds(j * band, band), :]
        hidden = before * slope_one + base_one
        opened = gate(hidden)
        grad = grad * (opened * (1.0 + hidden * (1.0 - opened)))
        shift_one = shift_one + jnp.sum(grad, axis=0, keepdims=True)
        gain_one = gain_one + jnp.sum(
            grad * ((before - mean_one) * inv_one), axis=0, keepdims=True
        )
        back_one[j, :side] = (grad * slope_one).astype(low).reshape(side, slots, width)
        turn(1 + j)

    grad_short[...] = jnp.dot(xs_t[0, 0], back_side[...], preferred_element_type=f32)
    matrix_votes(2, grad_short, (nothing, nothing), lambda k: None)
    turn(5)

    square_head = grad_head * grad_head + EPS_ROW
    real = lax.broadcasted_iota(jnp.int32, square_head.shape, 0) < classes
    square_head = jnp.where(real, square_head, 0.0)
    head_lanes = pl.ds(edges[2], width)
    old = row_ref[:, head_lanes]
    row = keep * old + (1.0 - keep) * jnp.sum(square_head, axis=0, keepdims=True) / classes
    row_new[:, head_lanes] = row
    diagonal = eye_mask(16, classes)
    old = jnp.broadcast_to(col_ref[:, 3 * width :], (16, classes))
    old = jnp.sum(jnp.where(diagonal, old, 0.0), axis=1, keepdims=True)
    column = keep * old + (1.0 - keep) * jnp.sum(square_head, axis=1, keepdims=True) / width
    col_new[:, 3 * width :] = jnp.sum(
        jnp.where(diagonal, jnp.broadcast_to(column, (16, classes)), 0.0), axis=0, keepdims=True
    )
    real_column = lax.broadcasted_iota(jnp.int32, column.shape, 0) < classes
    column = jnp.where(real_column, column, 1.0)
    mean = jnp.sum(row, axis=1, keepdims=True) / width
    raw = grad_head * (lax.rsqrt(row) * jnp.sqrt(mean)) * lax.rsqrt(column)
    clip = jnp.maximum(1.0, jnp.sqrt(total_of(raw * raw) / (classes * width)))
    head_votes = jnp.tanh(raw / clip)[:classes]

    raws = []
    for k, grad in enumerate((gain_one, shift_one, gain_two, shift_two, gain_side, shift_two)):
        here = pl.ds(k * width, width)
        moment = keep * moment_ref[:, here] + (1.0 - keep) * (grad * grad + EPS_ROW)
        moment_new[:, here] = moment
        raws.append(grad * lax.rsqrt(moment))
    raw = jnp.concatenate(raws, axis=0)
    clip = jnp.maximum(1.0, jnp.sqrt(total_of(raw * raw) / raw.size))
    norm_votes = jnp.tanh(raw / clip)
    tail_votes = jnp.concatenate([head_votes, norm_votes], axis=0)
    kept["tail"] = exchange_start(
        2,
        jnp.concatenate(
            [tail_votes[:, 128 * q : 128 * (q + 1)] for q in range(4)]
            + [jnp.broadcast_to(loss, (8, 128))],
            axis=0,
        ),
    )


    one_passed = no_sums(width)
    for b in range(3):
        first, last = (0, side - 1) if b == 0 else (0, side)
        shift = 1 if b == 0 else 0
        for a in range(3):
            left = xs_t[0 if b == 1 else 1, 0 if a == 1 else 1, :, first * band : last * band]
            start = 1 if a == 0 else 0
            right = back_one[first + shift : last + shift, start : start + side]
            tap = a * 3 + b
            grad_one[pl.ds(tap * in_width, in_width), :] = jnp.dot(
                left, right.reshape(-1, width), preferred_element_type=f32
            )
            for k in range(tap * in_width // 128, (tap + 1) * in_width // 128):
                one_passed = row_block(grad_one, 0, row_ref, row_new, level, k, one_passed)
        if b == 1:
            kept["tail"] = exchange_middle(2, kept["tail"])
        turn(6 + b)

    matrix_votes(
        0,
        grad_one,
        (lambda: turn(9), lambda: turn(10)),
        lambda k: go(0, early + k) if k < 2 else None,
        one_passed,
    )
    turn(11)
    for away, copy in passes:

        @pl.when(away)
        def _():
            copy.wait_send()

    three = deep_in.at[pl.ds(0, 3 * SPAN)]
    for kind, ref in enumerate((None, wide_in, deep_in, three, three, deep_in, wide_in, core_in)):
        if kind:
            sent_all(kind, ref)
    for u in range(len(units)):
        in_flight[u].wait_recv()


def finish_kernel(count, chunks, *refs):
    sources, targets, sem = refs[:count], refs[count : 2 * count], refs[2 * count]
    rows = sources[0].shape[0]
    step = -(-rows // chunks // 16) * 16
    copies = []
    for k in range(chunks):
        here = pl.ds(k * step, min(step, rows - k * step))
        copies.append(
            pltpu.make_async_copy(sources[0].at[here], targets[0].at[here], sem.at[k])
        )
    for k in range(1, count):
        copies.append(pltpu.make_async_copy(sources[k], targets[k], sem.at[chunks + k]))
    for copy in copies:
        copy.start()
    for copy in copies:
        copy.wait()


def finish(values):
    count, chunks = len(values), 4
    held = [pltpu.with_memory_space_constraint(value, pltpu.VMEM) for value in values]
    return pl.pallas_call(
        functools.partial(finish_kernel, count, chunks),
        out_shape=[jax.ShapeDtypeStruct(value.shape, value.dtype) for value in values],
        in_specs=[pl.BlockSpec(memory_space=pltpu.VMEM)] * count,
        out_specs=[pl.BlockSpec(memory_space=pl.ANY)] * count,
        scratch_shapes=[pltpu.SemaphoreType.DMA((chunks + count,))],
        compiler_params=pltpu.CompilerParams(vmem_limit_bytes=1024 * 1024),
        name="finish",
    )(*held)


def run_step(images, conv_one, conv_two, shortcut, head, norm_params, valid, labels, rows, cols, moment):
    vmem = pl.BlockSpec(memory_space=pltpu.VMEM)
    hbm = pl.BlockSpec(memory_space=pl.ANY)
    low, f32 = jnp.bfloat16, jnp.float32
    dma = pltpu.SemaphoreType.DMA
    workers = lax.axis_size("dp")
    slots, in_width = valid.shape[1], images.shape[1]
    width = conv_one.shape[1]
    pixels = images.shape[0] // 4
    shape = pltpu.VMEM
    edges = [conv_one.shape[0]]
    edges.append(edges[0] + conv_two.shape[0])
    edges.append(edges[1] + shortcut.shape[0])
    units = make_units(edges)
    flat = (edges[2] + TAIL) * width // 128
    share = flat // workers
    return pl.pallas_call(
        functools.partial(step_kernel, tuple(edges), tuple(units), 1.0 / math.sqrt(workers)),
        out_shape=(
            shape((share, 128), f32),
            shape((share, 128), f32),
            shape((flat, 128), low),
            shape(rows.shape, f32),
            shape(cols.shape, f32),
            shape(moment.shape, f32),
            shape((1, 1), f32),
            shape((1, 1), f32),
        ),
        in_specs=[hbm] * 4 + [vmem] * 7,
        out_specs=(vmem,) * 8,
        scratch_shapes=[
            pltpu.VMEM((2, 4, 2, 4, slots, in_width), low),
            pltpu.VMEM(conv_one.shape, f32),
            pltpu.VMEM(conv_two.shape, f32),
            pltpu.VMEM(shortcut.shape, f32),
            pltpu.VMEM((9, in_width, width), low),
            pltpu.VMEM((9, width, width), low),
            pltpu.VMEM((1, in_width, width), low),
            pltpu.VMEM((pixels, width), f32),
            pltpu.VMEM((pixels, width), f32),
            pltpu.VMEM((pixels, width), f32),
            pltpu.VMEM((4, 6, slots, width), low),
            pltpu.VMEM((4, 6, slots, width), low),
            pltpu.VMEM((4, 5, slots, width), low),
            pltpu.VMEM((pixels, width), low),
            pltpu.VMEM((width, pixels), low),
            pltpu.VMEM((2, 2, in_width, pixels), low),
            pltpu.VMEM((128, width), f32),
            pltpu.VMEM((conv_two.shape[0], 128), f32),
            pltpu.VMEM((8, width), f32),
            pltpu.VMEM((24, 128), f32),
            pltpu.VMEM((8, 24, 128), f32),
            pltpu.VMEM((4, 24, 128), f32),
            pltpu.VMEM((8, 128), f32),
            pltpu.VMEM((8, 8, 128), f32),
            pltpu.VMEM((4, 8, 128), f32),
            pltpu.VMEM((GROUP + 8, 128), f32),
            pltpu.VMEM((8, GROUP + 8, 128), f32),
            pltpu.VMEM((4, GROUP + 8, 128), f32),
            pltpu.VMEM((16 * SPAN, 128), low),
            pltpu.VMEM((8 * SPAN, 128), low),
            pltpu.VMEM((4 * SPAN, 128), low),
            pltpu.VMEM((4 * SPAN, 128), low),
            pltpu.VMEM((SPAN, 128), low),
            pltpu.VMEM((SPAN + GROUP, 128), low),
            pltpu.VMEM((SPAN + GROUP, 128), f32),
            pltpu.VMEM((OWN, width), f32),
            pltpu.VMEM((OWN + TAIL, width), f32),
            pltpu.VMEM((SPAN + GROUP, 128), f32),
            pltpu.VMEM((SPAN + GROUP, 128), f32),
            pltpu.VMEM((GROUP, 128), f32),
            pltpu.VMEM((GROUP, 128), f32),
            dma((9 + len(units),)),
            dma((3, 10)),
            dma((3, 10)),
            dma((8,)),
            dma((len(units), 3)),
            dma((len(units),)),
            dma((2 * OWN // 16,)),
            dma((OWN // 16 + 1,)),
            dma((len(units),)),
            dma((len(units), 3)),
            pltpu.SemaphoreType.REGULAR,
            dma((2,)),
        ],
        compiler_params=pltpu.CompilerParams(
            collective_id=1, has_side_effects=True, vmem_limit_bytes=54 * 1024 * 1024
        ),
        name="step",
    )(images, conv_one, conv_two, shortcut, head, norm_params, valid, labels, rows, cols, moment)


def scale_for(weight):
    return jnp.maximum(EPS_SCALE, jnp.sqrt(jnp.mean(weight * weight)))


def local_general(
    images,
    valid_slot,
    labels,
    conv_one,
    conv_two,
    shortcut,
    classifier,
    norm_params,
    row_state,
    col_state,
    bn_moment,
):
    in_width = images.shape[3]
    width = conv_one.shape[1]
    kernel_one = conv_one.astype(jnp.bfloat16).reshape(3, 3, in_width, width)
    kernel_two = conv_two.astype(jnp.bfloat16).reshape(3, 3, width, width)
    kernel_short = shortcut.astype(jnp.bfloat16).reshape(1, 1, in_width, width)
    head_low = classifier.astype(jnp.bfloat16)
    slot_count = images.shape[0]
    out_side = images.shape[1] // 2
    pixel_count = out_side * out_side
    slot_weight = valid_slot.astype(jnp.float32)
    pixel_weight = jnp.broadcast_to(slot_weight[:, None], (slot_count, pixel_count)).reshape(-1, 1)
    main_pre, side_pre = first_section(images, kernel_one, kernel_short)
    main_sums = masked_moments(pixel_weight, main_pre)
    side_sums = masked_moments(pixel_weight, side_pre)
    count_row = jnp.broadcast_to(jnp.sum(slot_weight), (width,))
    first_sums = lax.psum(jnp.stack([*main_sums, *side_sums, count_row]), "dp")
    valid_count = first_sums[4, 0]
    denominator = jnp.maximum(valid_count, 1.0)
    pixels = denominator * pixel_count
    norm_one = settle(first_sums[0], first_sums[1], pixels)
    norm_side = settle(first_sums[2], first_sums[3], pixels)
    hidden_one, active, main_two = second_section(
        main_pre, norm_one, norm_params, kernel_two, slot_count, out_side
    )
    two_sums = masked_moments(pixel_weight, main_two)
    second_sums = lax.psum(jnp.stack([*two_sums]), "dp")
    norm_two = settle(second_sums[0], second_sums[1], pixels)
    joined_pre = (
        (main_two - norm_two[0]) * norm_two[1] * norm_params[2]
        + norm_params[3]
        + (side_pre - norm_side[0]) * norm_side[1] * norm_params[4]
        + norm_params[5]
    )
    joined = jax.nn.silu(joined_pre).reshape(slot_count, pixel_count, -1)
    pooled = jnp.mean(joined, axis=1).astype(jnp.bfloat16)
    logits = jnp.dot(pooled, head_low, preferred_element_type=jnp.float32)
    largest = jnp.max(logits, axis=1, keepdims=True)
    exp_terms = jnp.exp(logits - largest)
    total_exp = jnp.sum(exp_terms, axis=1, keepdims=True)
    log_total = largest[:, 0] + jnp.log(total_exp[:, 0])
    onehot = (labels[:, None] == jnp.arange(logits.shape[1], dtype=jnp.int32)[None, :]).astype(
        jnp.float32
    )
    local_sum = jnp.sum(slot_weight * (log_total - jnp.sum(onehot * logits, axis=1)))
    grad_logits = ((exp_terms / total_exp - onehot) * (slot_weight / denominator)[:, None]).astype(
        jnp.bfloat16
    )
    grad_head = lax.dot_general(
        pooled, grad_logits, (((0,), (0,)), ((), ())), preferred_element_type=jnp.float32
    )
    grad_pooled = lax.dot_general(
        grad_logits, head_low, (((1,), (1,)), ((), ())), preferred_element_type=jnp.float32
    )
    spread_pooled = jnp.broadcast_to(
        (grad_pooled / pixel_count)[:, None, :], (slot_count, pixel_count, width)
    )
    grad_joined = spread_pooled.reshape(slot_count * pixel_count, width) * silu_slope(joined_pre)
    gain_two, shift_two, grad_two = norm_backward(grad_joined, main_two, norm_two, norm_params[2])
    gain_side, shift_side, grad_side = norm_backward(
        grad_joined, side_pre, norm_side, norm_params[4]
    )
    grad_two_maps = grad_two.reshape(slot_count, out_side, out_side, width)
    grad_side_maps = grad_side.reshape(slot_count, out_side, out_side, width)
    grad_conv_two = conv_weight_grad(active, grad_two_maps, 1, 1, 1)
    grad_short = conv_weight_grad(images, grad_side_maps, 2, 0, -1)
    kernel_turned = jnp.transpose(kernel_two[::-1, ::-1], (0, 1, 3, 2))
    grad_active = conv_apply(grad_two_maps, kernel_turned, 1, 1).reshape(
        slot_count * pixel_count, width
    )
    grad_hidden = grad_active * silu_slope(hidden_one)
    gain_one, shift_one, grad_one = norm_backward(grad_hidden, main_pre, norm_one, norm_params[0])
    grad_conv_one = conv_weight_grad(
        images, grad_one.reshape(slot_count, out_side, out_side, width), 2, 1, 0
    )
    grad_norms = jnp.stack([gain_one, shift_one, gain_two, shift_two, gain_side, shift_side])
    grads = (grad_conv_one, grad_conv_two, grad_short, grad_head, grad_norms)
    votes, rows_new, cols_new, moment_new = make_votes(
        grads, row_state[0], col_state[0], bn_moment[0]
    )
    workers = lax.axis_size("dp")
    weights = (conv_one, conv_two, shortcut, classifier, norm_params)
    scales = [scale_for(weight) for weight in weights]
    loss_sum = lax.psum(local_sum, "dp")
    flat_vote = jnp.concatenate([vote.reshape(-1) for vote in votes])
    flat_old = jnp.concatenate([weight.reshape(-1) for weight in weights])
    flat_scale = jnp.concatenate(
        [
            jnp.broadcast_to(scale, (weight.size,))
            for scale, weight in zip(scales, weights)
        ]
    )
    vote_mine = lax.psum_scatter(flat_vote, "dp", tiled=True)
    share = vote_mine.shape[0]
    start = lax.axis_index("dp") * share
    new_mine = lax.dynamic_slice_in_dim(
        flat_old, start, share
    ) - lax.dynamic_slice_in_dim(flat_scale, start, share) * jnp.tanh(
        vote_mine / math.sqrt(workers)
    )
    copies = lax.all_gather(new_mine.astype(jnp.bfloat16), "dp", tiled=True)
    return (
        loss_sum,
        valid_count,
        new_mine,
        copies,
        vote_mine,
        rows_new[None, :],
        cols_new[None, :],
        moment_new[None, :],
    )


def local(
    images,
    valid_slot,
    labels,
    conv_one,
    conv_two,
    shortcut,
    classifier,
    norm_params,
    row_state,
    col_state,
    bn_moment,
):
    new_mine, vote_mine, copies, rows_new, cols_new, moment_new, loss_sum, valid_count = run_step(
        images.reshape(-1, images.shape[-1]),
        conv_one,
        conv_two,
        shortcut,
        classifier.T,
        norm_params,
        valid_slot.reshape(1, -1),
        labels.reshape(1, -1),
        row_state,
        col_state,
        bn_moment,
    )
    copies, new_mine, vote_mine, rows_new, cols_new, moment_new, loss_sum, valid_count = finish(
        (copies, new_mine, vote_mine, rows_new, cols_new, moment_new, loss_sum, valid_count)
    )
    return (
        loss_sum.reshape(()),
        valid_count.reshape(()),
        new_mine.reshape(-1),
        copies.reshape(-1),
        vote_mine.reshape(-1),
        rows_new,
        cols_new,
        moment_new,
    )


def solution(mesh):
    placed = (
        P("dp", None, None, None),
        P("dp"),
        P("dp"),
        P(),
        P(),
        P(),
        P(),
        P(),
        P("dp", None),
        P("dp", None),
        P("dp", None),
    )
    return jax.shard_map(
        local if mesh.shape["dp"] == 32 else local_general,
        mesh=mesh,
        in_specs=placed,
        out_specs=(P(), P(), P("dp"), P(), P("dp"), P("dp", None), P("dp", None), P("dp", None)),
        check_vma=False,
    )
```

```python
import functools
import math

import jax
import jax.numpy as jnp
from jax import lax
from jax.experimental import pallas as pl
from jax.experimental.pallas import tpu as pltpu
from jax.sharding import PartitionSpec as P

STEP = 10
MESH = pl.DeviceIdType.MESH

EPS_NORM = 1e-05
EPS_ROW = 1e-30
EPS_SCALE = 0.001
FORWARD_DIMS = ("NHWC", "HWIO", "NHWC")
WEIGHT_DIMS = ("CHWN", "IHWO", "HWNC")
OWN = 224
TAIL = 16
PIECE = 32
SPAN = 4 * OWN
HALF = SPAN // 2
GROUP = 64


def conv_apply(maps, kernel, stride, margin):
    return lax.conv_general_dilated(
        maps,
        kernel,
        (stride, stride),
        ((margin, margin), (margin, margin)),
        dimension_numbers=FORWARD_DIMS,
        preferred_element_type=jnp.float32,
    )


def conv_weight_grad(maps, grad_out, stride, low_pad, high_pad):
    result = lax.conv_general_dilated(
        maps,
        grad_out,
        (1, 1),
        ((low_pad, high_pad), (low_pad, high_pad)),
        rhs_dilation=(stride, stride),
        dimension_numbers=WEIGHT_DIMS,
        preferred_element_type=jnp.float32,
    )
    return result.reshape(-1, result.shape[3])


def silu_slope(values):
    sigmoid_part = jax.nn.sigmoid(values)
    return sigmoid_part * (1.0 + values * (1.0 - sigmoid_part))


def settle(sum_plain, sum_square, pixels):
    mean_value = sum_plain / pixels
    return (mean_value, lax.rsqrt(sum_square / pixels - mean_value * mean_value + EPS_NORM))


def first_section(images, kernel_one, kernel_short):
    row_count = images.shape[0] * (images.shape[1] // 2) ** 2
    main_pre = conv_apply(images, kernel_one, 2, 1).reshape(row_count, -1)
    side_pre = conv_apply(images, kernel_short, 2, 0).reshape(row_count, -1)
    return (main_pre, side_pre)


def second_section(main_pre, norm_one, norm_params, kernel_two, slot_count, out_side):
    hidden_one = (main_pre - norm_one[0]) * norm_one[1] * norm_params[0] + norm_params[1]
    active = (
        jax.nn.silu(hidden_one).astype(jnp.bfloat16).reshape(slot_count, out_side, out_side, -1)
    )
    main_two = conv_apply(active, kernel_two, 1, 1).reshape(slot_count * out_side * out_side, -1)
    return (hidden_one, active, main_two)


def masked_moments(pixel_weight, values):
    return (jnp.sum(pixel_weight * values, axis=0), jnp.sum(pixel_weight * values * values, axis=0))


def soft_sign(step_raw):
    clip_by = jnp.maximum(1.0, jnp.sqrt(jnp.mean(step_raw * step_raw)))
    return jnp.tanh(step_raw / clip_by)


def make_votes(grads, rows_old, cols_old, moment_old):
    decay_rate = 1.0 - STEP ** (-0.8)
    votes, rows_new, cols_new = ([], [], [])
    row_at, col_at = (0, 0)
    for matrix in grads[:4]:
        row_size, col_size = matrix.shape
        square = matrix * matrix + EPS_ROW
        row_part = decay_rate * rows_old[row_at : row_at + row_size] + (
            1.0 - decay_rate
        ) * jnp.mean(square, axis=1)
        col_part = decay_rate * cols_old[col_at : col_at + col_size] + (
            1.0 - decay_rate
        ) * jnp.mean(square, axis=0)
        second = row_part[:, None] * col_part[None, :] / jnp.mean(row_part)
        votes.append(soft_sign(matrix * lax.rsqrt(second)))
        rows_new.append(row_part)
        cols_new.append(col_part)
        row_at += row_size
        col_at += col_size
    flat_norm = grads[4].reshape(-1)
    moment_new = decay_rate * moment_old + (1.0 - decay_rate) * (flat_norm * flat_norm + EPS_ROW)
    votes.append(soft_sign(flat_norm * lax.rsqrt(moment_new)))
    return (votes, jnp.concatenate(rows_new), jnp.concatenate(cols_new), moment_new)


def norm_backward(grad_out, pre_value, norm_pair, gain_row):
    normed = (pre_value - norm_pair[0]) * norm_pair[1]
    grad_gain = jnp.sum(grad_out * normed, axis=0)
    grad_shift = jnp.sum(grad_out, axis=0)
    grad_pre = (grad_out * gain_row * norm_pair[1]).astype(jnp.bfloat16)
    return (grad_gain, grad_shift, grad_pre)


SCHEDULE = (
    (),
    (),
    (
        (1, 0), (0, 2),
    ),
    (
        (1, 1), (0, 3),
    ),
    (
        (1, 2), (0, 4),
    ),
    (
        (2, 0), (1, 3), (0, 5),
    ),
    (),
    (
        (2, 1), (1, 4), (0, 6),
    ),
    (
        (3, 0), (2, 2), (1, 5), (0, 7),
    ),
    (),
    (
        (3, 1), (2, 3), (1, 6), (0, 8),
    ),
    (
        (3, 2), (2, 4), (1, 7), (4, 0), (3, 3), (2, 5), (1, 8), (4, 1), (3, 4), (2, 6), (1, 9),
        (0, 11), (4, 2), (3, 5), (2, 7), (1, 10), (0, 12), (5, 0), (4, 3), (3, 6), (2, 8),
        (1, 11), (0, 13), (5, 1), (4, 4), (3, 7), (2, 9), (1, 12), (6, 0), (5, 2), (4, 5),
        (3, 8), (2, 10), (1, 13), (6, 1), (5, 3), (4, 6), (3, 9), (2, 11), (6, 2), (5, 4),
        (4, 7), (8, 0), (3, 10), (2, 12), (7, 0), (6, 3), (5, 5), (4, 8), (3, 11), (2, 13),
        (7, 1), (6, 4), (5, 6), (4, 9), (3, 12), (7, 2), (6, 5), (5, 7), (4, 10), (3, 13),
        (7, 3), (6, 6), (5, 8), (4, 11), (7, 4), (6, 7), (5, 9), (4, 12), (7, 5), (6, 8),
        (5, 10), (4, 13), (7, 6), (6, 9), (5, 11), (7, 7), (6, 10), (5, 12), (7, 8), (6, 11),
        (5, 13), (7, 9), (9, 0), (6, 12), (7, 10), (6, 13), (7, 11), (7, 12), (9, 1), (7, 13),
        (9, 2),
    ),
)


def place():
    me = lax.axis_index("dp")
    core = lax.rem(me, 2)
    x = lax.rem(lax.div(me, 2), 2)
    y = lax.rem(lax.div(me, 4), 2)
    z = lax.div(me, 8)
    return me, core, x, y, z


def send(src, dst, send_sem, recv_sem, partner):
    copy = pltpu.make_async_remote_copy(
        src_ref=src,
        dst_ref=dst,
        send_sem=send_sem,
        recv_sem=recv_sem,
        device_id=(partner,),
        device_id_type=MESH,
    )
    copy.start()
    return copy


def scale_of(row, scales, edges):
    picked = scales[2]
    picked = jnp.where(row < edges[1], scales[1], picked)
    return jnp.where(row < edges[0], scales[0], picked)


def make_units(edges):
    one, two, short = edges[0] // 16, edges[1] // 16, edges[2] // 16
    units = []
    for k in range((two - one) // 32):
        units.append((one + 32 * k, 1, k % 2 == 0, 16, (1, 1)))
    for k in range(one // 32):
        units.append((32 * k, 1, k % 2 == 1, 16, (0, 0)))
    at = one // 32 * 32
    assert one - at == 16 and short - two == 16
    units.append((at, 1, False, two - at, (0, 2)))
    return units


def settle_rows(sums, pixels, gain, shift):
    mean = sums[0] / pixels
    inv = lax.rsqrt(sums[1] / pixels - mean * mean + EPS_NORM)
    slope = gain * inv
    return mean, inv, slope, shift - mean * slope


def gate(values):
    return 0.5 * jnp.tanh(0.5 * values) + 0.5


def eye_mask(rows, columns, offset=0):
    down = lax.broadcasted_iota(jnp.int32, (rows, columns), 0) + offset
    return down == lax.broadcasted_iota(jnp.int32, (rows, columns), 1)


def column_of(row, size):
    spread = jnp.where(eye_mask(size, size), jnp.broadcast_to(row, (size, size)), 0)
    return jnp.sum(spread, axis=1, keepdims=True)


def total_of(values):
    return jnp.sum(jnp.sum(values, axis=0, keepdims=True), axis=1, keepdims=True)


def fold(values):
    return jnp.sum(values.reshape(values.shape[0] // 8, 8, values.shape[1]), axis=0)


def cast_weight(source, target, square_ref, taps, depth, fetches):
    step = 256
    for tap in taps:
        chunk = source.shape[0] // depth // len(fetches)
        if tap % chunk == 0:
            fetches[tap // chunk].wait()
        new_tap = (tap % 3) * 3 + tap // 3

        for start in range(0, depth, step):
            values = source[pl.ds(tap * depth + start, step), :]
            target[new_tap, pl.ds(start, step), :] = values.astype(jnp.bfloat16)
            square_ref[...] += fold(values * values)


def row_block(grad, row_at, rows_old, rows_new, level, k, carry):
    width = grad.shape[1]
    keep = 1.0 - STEP ** (-0.8)
    step = 128
    quarters = width // 128
    col_sum, row_sum = carry
    start = k * step
    lanes = pl.ds(row_at + start, step)
    if not isinstance(k, int):
        start = pl.multiple_of(start, step)
        lanes = pl.ds(pl.multiple_of(row_at + start, step), step)
    old = rows_old[:, lanes] * keep
    line = jnp.zeros((8, 128), jnp.float32)
    for m in range(step // 8):
        block = grad[pl.ds(start + 8 * m, 8), :]
        square = block * block
        col_sum = col_sum + square
        part = square[:, :128]
        for q in range(1, quarters):
            part = part + square[:, 128 * q : 128 * (q + 1)]
        part = part * ((1.0 - keep) / width)
        diagonal = eye_mask(8, 128, 8 * m)
        part = part + jnp.where(diagonal, jnp.broadcast_to(old, (8, 128)), 0.0)
        row = jnp.sum(part, axis=1, keepdims=True) + (1.0 - keep) * EPS_ROW
        row = jnp.broadcast_to(row, (8, 128))
        level[pl.ds(start + 8 * m, 8), :] = row
        row_sum = row_sum + row
        line = line + jnp.where(diagonal, row, 0.0)
    rows_new[:, lanes] = jnp.sum(line, axis=0, keepdims=True)
    return col_sum, row_sum


def no_sums(width):
    return jnp.zeros((8, width), jnp.float32), jnp.zeros((8, 128), jnp.float32)


def factored_votes(
    grad, rows, row_at, rows_old, rows_new, col_old, level, votes, vote_at, between, after, sums
):
    width = grad.shape[1]
    keep = 1.0 - STEP ** (-0.8)
    step = 128
    quarters = width // 128
    if sums is None:
        sums = lax.fori_loop(
            0,
            rows // step,
            functools.partial(row_block, grad, row_at, rows_old, rows_new, level),
            no_sums(width),
        )
    col_sum, row_sum = sums

    col_new = keep * col_old + (1.0 - keep) * (
        jnp.sum(col_sum, axis=0, keepdims=True) / rows + EPS_ROW
    )
    scale = lax.rsqrt(col_new)
    root_mean = jnp.sqrt(jnp.sum(row_sum, axis=0, keepdims=True) / rows)

    run = 2 * step

    def second(k, carry):
        start = pl.multiple_of(k * run, run)
        for m in range(run // 8):
            here = pl.ds(start + 8 * m, 8)
            factor = lax.rsqrt(level[here, :]) * root_mean
            level[here, :] = factor
            raw = grad[here, :] * jnp.concatenate([factor] * quarters, axis=1) * scale
            power = raw * raw
            part = power[:, :128]
            for q in range(1, quarters):
                part = part + power[:, 128 * q : 128 * (q + 1)]
            carry = carry + part
        return carry

    between[0]()
    power = lax.fori_loop(0, rows // run, second, jnp.zeros((8, 128), jnp.float32))
    between[1]()
    clip = jnp.maximum(1.0, jnp.sqrt(total_of(power) / (rows * width)))
    scale = scale / clip

    def third(start, count):
        for m in range(count // 16):
            here = pl.ds(start + 16 * m, 16)
            factor = level[here, :]
            factor = jnp.concatenate([factor] * quarters, axis=1)
            vote = jnp.tanh(grad[here, :] * factor * scale).astype(jnp.bfloat16)
            at = (vote_at + start) * 4 + GROUP * m
            for q in range(quarters):
                votes[pl.ds(at + 16 * q, 16), :] = vote[:, 128 * q : 128 * (q + 1)]

    for k, start in enumerate(range(0, rows, 512)):
        third(start, min(512, rows - start))
        after(k)
    return col_new


def step_kernel(
    edges,
    units,
    root,
    images,
    one_hbm,
    two_hbm,
    short_hbm,
    head_ref,
    norm_ref,
    valid_ref,
    label_ref,
    row_ref,
    col_ref,
    moment_ref,
    new_ref,
    vote_ref,
    out_ref,
    row_new,
    col_new,
    moment_new,
    loss_ref,
    count_ref,
    xs,
    grad_one,
    grad_two,
    grad_short,
    low_one,
    low_two,
    low_short,
    main_pre,
    side_pre,
    main_two,
    active,
    back_two,
    back_one,
    back_side,
    active_t,
    xs_t,
    head_pad,
    level,
    square,
    post_one,
    plane_one,
    line_one,
    post_two,
    plane_two,
    line_two,
    tail_post,
    tail_plane,
    tail_line,
    core_in,
    wide_in,
    deep_in,
    line_in,
    sum_low,
    landed,
    total,
    own_weight,
    weight,
    vote_flat,
    new_flat,
    tail_vote,
    tail_new,
    fetch_sem,
    small_send,
    small_recv,
    sent,
    rs_recv,
    line_recv,
    pass_send,
    land_recv,
    spread_recv,
    ag_recv,
    free_sem,
    load_sem,
):
    slots, in_width = xs.shape[4:]
    width = main_pre.shape[1]
    side = 4
    band = side * slots
    pixel_count = side * side
    side_pixels = 4 * pixel_count
    classes = head_ref.shape[0]
    keep = 1.0 - STEP ** (-0.8)
    low = jnp.bfloat16
    f32 = jnp.float32

    me, core, x, y, z = place()
    flip_core = me + 1 - 2 * core
    flip_x = me + 2 - 4 * x
    flip_y = me + 4 - 8 * y
    spot = lax.rem(me, 8)
    near = [z * 8 + lax.rem(spot + k, 8) for k in range(1, 8)]
    far = [lax.rem(z + k, 4) * 8 + spot for k in range(1, 4)]
    others = [lax.rem(me + k, 32) for k in range(1, 32)]

    count = images.shape[0]
    loads = []
    for half in range(2):
        lanes = slice(128 * half, 128 * (half + 1))
        loads.append(
            pltpu.make_async_copy(
                images.at[:, lanes], core_in.at[pl.ds(half * count, count)], load_sem.at[half]
            )
        )
        loads[half].start()

    def chunks_of(source, target, first, count):
        rows = source.shape[0] // count
        return [
            pltpu.make_async_copy(
                source.at[pl.ds(k * rows, rows)],
                target.at[pl.ds(k * rows, rows)],
                fetch_sem.at[first + k],
            )
            for k in range(count)
        ]

    fetch_one = chunks_of(one_hbm, grad_one, 0, 3)
    fetch_short = chunks_of(short_hbm, grad_short, 3, 1)
    fetch_two = chunks_of(two_hbm, grad_two, 4, 3)
    for fetch in fetch_one + fetch_short:
        fetch.start()
    barrier = pltpu.get_barrier_semaphore()
    for partner in others:
        pl.semaphore_signal(barrier, inc=1, device_id=(partner,), device_id_type=MESH)

    def fetch_rows(row, count, place_at, sem):
        parts = (
            (one_hbm, 0, edges[0]),
            (two_hbm, edges[0], edges[1]),
            (short_hbm, edges[1], edges[2]),
        )
        for ref, first, last in parts:

            @pl.when(jnp.logical_and(row >= first, row < last))
            def _():
                start = pl.multiple_of(row - first, count)
                pltpu.make_async_copy(
                    ref.at[pl.ds(start, count)], weight.at[pl.ds(place_at, count)], sem
                ).start()

    first_row = me * OWN

    for half in range(2):
        lanes = slice(128 * half, 128 * (half + 1))
        loads[half].wait()
        apart = side_pixels + 8

        @pl.loop(0, slots // 4)
        def _(k):
            for m in range(4):
                slot = k * 4 + m
                source = pl.multiple_of(half * count + slot * side_pixels, side_pixels)
                target = pl.multiple_of(slot * apart, 8)
                level[pl.ds(target, side_pixels), :] = core_in[
                    pl.ds(source, side_pixels), :
                ].astype(f32)

        for h in range(2 * side):
            for w in range(2 * side):
                rows = level[pl.ds(2 * side * h + w, slots, stride=apart), :]
                xs[w % 2, w // 2, h % 2, h // 2, :, lanes] = rows.astype(low)

    scales = {}

    def scale_from(weight_square, size):
        return jnp.maximum(EPS_SCALE, jnp.sqrt(total_of(weight_square) / size))

    exchanges = (
        (post_one, plane_one, line_one),
        (post_two, plane_two, line_two),
        (tail_post, tail_plane, tail_line),
    )

    def exchange_start(which, values):
        mine_ref, plane_ref, _ = exchanges[which]
        mine_ref[...] = values
        plane_ref[spot] = values
        return [
            send(
                mine_ref,
                plane_ref.at[spot],
                small_send.at[which, k],
                small_recv.at[which, k],
                partner,
            )
            for k, partner in enumerate(near)
        ]

    def pack_rows(rows):
        pieces = [row[:, 128 * q : 128 * (q + 1)] for row in rows for q in range(4)]
        pad = -len(pieces) % 8
        if pad:
            pieces.append(jnp.zeros((pad, 128), f32))
        return jnp.concatenate(pieces, axis=0)

    def unpack_row(lines_in, k):
        return jnp.concatenate([lines_in[4 * k + q : 4 * k + q + 1] for q in range(4)], axis=1)

    def exchange_middle(which, copies):
        _, plane_ref, line_ref = exchanges[which]
        for copy in copies:
            copy.wait()
        line_ref[z] = functools.reduce(lambda a, b: a + b, [plane_ref[k] for k in range(8)])
        return [
            send(
                line_ref.at[z],
                line_ref.at[z],
                small_send.at[which, 7 + k],
                small_recv.at[which, 7 + k],
                partner,
            )
            for k, partner in enumerate(far)
        ]

    def exchange_end(which, copies):
        line_ref = exchanges[which][2]
        for copy in copies:
            copy.wait()
        return (line_ref[0] + line_ref[1]) + (line_ref[2] + line_ref[3])

    def lines(start, count):
        return pl.ds(pl.multiple_of(start, 16), count)

    sizes = [GROUP * unit[1] for unit in units]
    starts = [sum(sizes[:k]) for k in range(len(units) + 1)]

    def part_of(ref, u, share, start, count):
        return ref.at[lines(share * starts[u] + start, count)]

    def places(u):
        if units[u][2]:
            return x, y, flip_x, flip_y
        return y, x, flip_y, flip_x

    def unit_start(u, cc):
        return GROUP * units[u][0] + cc * (GROUP * units[u][3])

    def own_group(u):
        first, second, _, _ = places(u)
        return units[u][0] + core * units[u][3] + (first * 8 + second * 4 + z) * units[u][1]

    def halve(source, target, u, stage, partner):
        return send(source, target, sent.at[stage], rs_recv.at[u, stage], partner)

    def scatter_start(u):
        size = 16 * sizes[u]
        return halve(
            out_ref.at[lines(unit_start(u, 1 - core), size)],
            part_of(core_in, u, 16, 0, size),
            u,
            0,
            flip_core,
        )

    def add_to(ref, u, share, source_ref, source_start):
        size = share * sizes[u]
        here = lines(share * starts[u], size)
        ref[here, :] = ref[here, :] + source_ref[lines(source_start, size), :]

    def sent_all(kind, ref):
        pltpu.make_async_remote_copy(
            src_ref=ref,
            dst_ref=ref,
            send_sem=sent.at[kind],
            recv_sem=rs_recv.at[0, 0],
            device_id=(flip_core,),
            device_id_type=MESH,
        ).wait_send()

    def scatter_one(u, copy):
        copy.wait_recv()
        add_to(core_in, u, 16, out_ref, unit_start(u, core))
        if u == len(units) - 1:
            sent_all(0, core_in)
            pl.semaphore_signal(free_sem, inc=1, device_id=(flip_core,), device_id_type=MESH)
        first, _, flip_first, _ = places(u)
        size = 8 * sizes[u]
        return halve(
            part_of(core_in, u, 16, (1 - first) * size, size),
            part_of(wide_in, u, 8, 0, size),
            u,
            1,
            flip_first,
        )

    def scatter_two(u, copy):
        copy.wait_recv()
        first, second, _, flip_second = places(u)
        add_to(wide_in, u, 8, core_in, 16 * starts[u] + first * 8 * sizes[u])
        size = 4 * sizes[u]
        return halve(
            part_of(wide_in, u, 8, (1 - second) * size, size),
            part_of(deep_in, u, 4, 0, size),
            u,
            2,
            flip_second,
        )

    def line_copy(u, k):
        plane_to = lax.rem(z + k, 4)
        return pltpu.make_async_remote_copy(
            src_ref=part_of(deep_in, u, 4, plane_to * sizes[u], sizes[u]),
            dst_ref=part_of(line_in, u, 4, z * sizes[u], sizes[u]),
            send_sem=sent.at[3],
            recv_sem=line_recv.at[u],
            device_id=(plane_to * 8 + spot,),
            device_id_type=MESH,
        )

    def scatter_three(u, copy):
        copy.wait_recv()
        _, second, _, _ = places(u)
        add_to(deep_in, u, 4, wide_in, 8 * starts[u] + second * 4 * sizes[u])
        for k in (3, 2, 1):
            line_copy(u, k).start()
        here = lines(4 * starts[u] + z * sizes[u], sizes[u])
        line_in[here, :] = deep_in[here, :]

    def three_landed(u, sem):
        ref = part_of(line_in, u, 4, 0, 3 * sizes[u])
        pltpu.make_async_remote_copy(
            src_ref=ref,
            dst_ref=ref,
            send_sem=sent.at[3],
            recv_sem=sem.at[u],
            device_id=(far[0],),
            device_id_type=MESH,
        ).wait_recv()

    groups = (edges[2] + TAIL) // 16
    spare = (groups - 1) // 32
    passes = []

    def land(local, group, to, slot, index):
        source = sum_low.at[lines(local * GROUP, GROUP)]
        target = landed.at[lines(slot * GROUP, GROUP)]
        copy = pltpu.make_async_remote_copy(
            src_ref=source,
            dst_ref=target,
            send_sem=pass_send.at[index],
            recv_sem=land_recv.at[slot],
            device_id=(to,),
            device_id_type=MESH,
        )
        return copy, source, target

    def pass_on(u):
        for m in range(units[u][1]):
            local = starts[u] // GROUP + m
            group = own_group(u) + m
            to, slot = lax.div(group, spare), lax.rem(group, spare)

            def one(receiver, at, index):
                copy, source, target = land(local, group, receiver, at, index)

                @pl.when(receiver != me)
                def _():
                    copy.start()

                @pl.when(receiver == me)
                def _():
                    target[...] = source[...]

                return copy

            first = jnp.logical_and(slot == 0, group > 0)
            ahead = lax.rem(to + 31, 32)
            passes.append((to != me, one(to, slot, 2 * local)))

            @pl.when(first)
            def _():
                one(ahead, spare, 2 * local + 1)

            copy = land(local, group, ahead, spare, 2 * local + 1)[0]
            passes.append((jnp.logical_and(first, ahead != me), copy))

    def flat_rows(row, q, values, ref):
        ref[pl.ds(row * 4 + q, 8, stride=4), :] = values

    def old_rows(u, cc):
        matrix = units[u][4][cc]
        base = edges[matrix - 1] if matrix else 0
        return (one_hbm, two_hbm, short_hbm)[matrix], 16 * own_group(u) - base, 16 * units[u][1]

    def own_fetch(u):
        target = own_weight.at[pl.ds(starts[u] // 4, 16 * units[u][1])]
        matrices = units[u][4]
        for cc in range(2):
            if cc and matrices[0] == matrices[1]:
                continue

            @pl.when((core == cc) if matrices[0] != matrices[1] else (core >= 0))
            def _():
                ref, row, count = old_rows(u, cc)
                pltpu.make_async_copy(
                    ref.at[pl.ds(pl.multiple_of(row, 16), count)], target, fetch_sem.at[9 + u]
                ).start()

    def spread_copy(u, k):
        own = out_ref.at[lines(own_group(u) * GROUP, sizes[u])]
        return pltpu.make_async_remote_copy(
            src_ref=own,
            dst_ref=own,
            send_sem=sent.at[4],
            recv_sem=spread_recv.at[u],
            device_id=(far[k - 1],),
            device_id_type=MESH,
        )

    def own_block(u):
        size = sizes[u]
        three_landed(u, line_recv)
        here = pl.ds(starts[u], size)
        low_sum = functools.reduce(
            lambda a, b: a + b,
            [line_in[pl.ds(4 * starts[u] + t * size, size), :].astype(f32) for t in range(4)],
        ).astype(low)
        sum_low[here, :] = low_sum
        summed = low_sum.astype(f32)
        target = own_weight.at[pl.ds(starts[u] // 4, 16 * units[u][1])]
        pltpu.make_async_copy(target, target, fetch_sem.at[9 + u]).wait()
        matrices = units[u][4]
        scale = scales[matrices[0]]
        if matrices[0] != matrices[1]:
            scale = jnp.where(core == 0, scale, scales[matrices[1]])
        turned = jnp.tanh(summed * root) * scale
        for m in range(units[u][1]):
            row = starts[u] // 4 + 16 * m
            for part in (0, 8):
                for q in range(4):
                    at = GROUP * m + 16 * q + part
                    old = own_weight[pl.ds(row + part, 8), 128 * q : 128 * (q + 1)]
                    flat_rows(row + part, q, old - turned[at : at + 8], new_flat)
        out_ref[lines(own_group(u) * GROUP, size), :] = new_flat[here, :].astype(low)
        for k in (3, 2, 1):
            spread_copy(u, k).start()
        pass_on(u)

    def piece(rows, u, stage, partner):
        return send(
            out_ref.at[rows], out_ref.at[rows], sent.at[5 + stage], ag_recv.at[u, stage], partner
        )

    def gather_one(u):
        three_landed(u, spread_recv)
        first, second, _, flip_second = places(u)
        size = 4 * sizes[u]
        start = unit_start(u, core) + (2 * first + second) * size
        return piece(lines(start, size), u, 0, flip_second)

    def gather_two(u, copy):
        copy.wait_recv()
        first, _, flip_first, _ = places(u)
        size = 8 * sizes[u]
        return piece(lines(unit_start(u, core) + first * size, size), u, 1, flip_first)

    def gather_three(u, copy):
        copy.wait_recv()
        if u == 0:
            pl.semaphore_wait(free_sem, 1)
        return piece(lines(unit_start(u, core), 16 * sizes[u]), u, 2, flip_core)

    def renew(row, at_row):
        scale = scale_of(at_row, [scales[k] for k in range(3)], edges)
        for part in (0, 8):
            for q in range(4):
                summed = total[pl.ds(row * 4 + 16 * q + part, 8), :]
                old = weight[pl.ds(row + part, 8), 128 * q : 128 * (q + 1)]
                fresh = old - scale * jnp.tanh(summed * root)
                flat_rows(row + part, q, summed, vote_flat)
                flat_rows(row + part, q, fresh, new_flat)

    valid_column = column_of(valid_ref[...].astype(f32), slots)
    weight_slot = jnp.broadcast_to(valid_column, (slots, width))
    weight_band = jnp.concatenate([weight_slot] * side, axis=0)

    square[...] = jnp.zeros_like(square)
    cast_weight(grad_one, low_one, square, range(9), in_width, fetch_one)
    scales[0] = scale_from(square[...], grad_one.size)
    square[...] = jnp.zeros_like(square)
    cast_weight(grad_short, low_short, square, range(1), in_width, fetch_short)
    scales[2] = scale_from(square[...], grad_short.size)
    for fetch in fetch_two:
        fetch.start()

    def image_taps(j):
        pieces = []
        for b in range(3):
            column = j if b else j - 1
            if column < 0:
                continue
            across = 0 if b == 1 else 1
            for a in range(3):
                if a == 1:
                    piece = xs[across, column, 0].reshape(band, in_width)
                elif a == 2:
                    piece = xs[across, column, 1].reshape(band, in_width)
                else:
                    piece = xs[across, column, 1, : side - 1].reshape(band - slots, in_width)
                    piece = jnp.concatenate([jnp.zeros((slots, in_width), low), piece], axis=0)
                pieces.append(piece)
        return jnp.concatenate(pieces, axis=1)

    def moments(values):
        weighted = values * weight_band
        return (
            jnp.sum(weighted, axis=0, keepdims=True),
            jnp.sum(weighted * values, axis=0, keepdims=True),
        )

    def add_up(old, new):
        return [a + b for a, b in zip(old, new)]

    none = jnp.zeros((1, width), f32)
    main_sums, side_sums = [none, none], [none, none]
    for j in range(side):
        here = pl.ds(j * band, band)
        low_rows = low_one[3 if j == 0 else 0 :].reshape(-1, width)
        value = jnp.dot(image_taps(j), low_rows, preferred_element_type=f32)
        main_pre[here, :] = value
        main_sums = add_up(main_sums, moments(value))
        value = jnp.dot(
            xs[0, j, 0].reshape(band, in_width), low_short[0], preferred_element_type=f32
        )
        side_pre[here, :] = value
        side_sums = add_up(side_sums, moments(value))

    count = jnp.broadcast_to(jnp.sum(valid_column, axis=0, keepdims=True), (1, width))
    pl.semaphore_wait(barrier, len(others))
    copies = exchange_start(
        0, pack_rows(main_sums + side_sums + [count])
    )
    square[...] = jnp.zeros_like(square)
    cast_weight(grad_two, low_two, square, range(5), width, fetch_two)
    copies = exchange_middle(0, copies)
    cast_weight(grad_two, low_two, square, range(5, 9), width, fetch_two)
    scales[1] = scale_from(square[...], grad_two.size)
    border = jnp.zeros((side, 1, slots, width), low)
    active[:, 0:1] = border
    active[:, side + 1 :] = border
    back_two[:, 0:1] = border
    back_two[:, side + 1 :] = border
    back_one[:, side:] = border
    head_pad[...] = jnp.zeros_like(head_pad)
    head_pad[:classes, :] = head_ref[...]
    head = head_pad[:16, :]
    scales[3] = scale_from(head * head, head_ref.size)
    params = norm_ref[...]
    scales[4] = scale_from(params * params, norm_ref.size)
    sums = exchange_end(0, copies)
    sums = [unpack_row(sums, k) for k in range(5)]

    valid_count = sums[4]
    count_ref[...] = valid_count[:, :1]
    denominator = jnp.maximum(valid_count, 1.0)
    pixels = denominator * pixel_count
    gains = [norm_ref[k : k + 1, :] for k in range(6)]
    mean_one, inv_one, slope_one, base_one = settle_rows(
        (sums[0], sums[1]), pixels, gains[0], gains[1]
    )
    mean_side, inv_side, slope_side, base_side = settle_rows(
        (sums[2], sums[3]), pixels, gains[4], gains[5]
    )

    for j in range(side):
        hidden = main_pre[pl.ds(j * band, band), :] * slope_one + base_one
        active[j, 1 : side + 1] = (
            (hidden * gate(hidden)).astype(low).reshape(side, slots, width)
        )
    two_sums = [none, none]
    for j in range(side):
        taps = [b for b in range(3) if 0 <= j + b - 1 < side]
        pieces = [
            active[j + b - 1, a : a + side].reshape(band, width) for b in taps for a in range(3)
        ]
        low_rows = low_two[3 * taps[0] : 3 * taps[-1] + 3].reshape(-1, width)
        value = jnp.dot(jnp.concatenate(pieces, axis=1), low_rows, preferred_element_type=f32)
        main_two[pl.ds(j * band, band), :] = value
        two_sums = add_up(two_sums, moments(value))
    copies = exchange_start(1, pack_rows(two_sums))
    for k in range(OWN // PIECE):
        fetch_rows(first_row + k * PIECE, PIECE, k * PIECE, fetch_sem.at[7])
    fetch_rows(first_row + OWN, TAIL, OWN, fetch_sem.at[8])
    for u in range(len(units)):
        own_fetch(u)
    for j in range(side):
        block = active[j, 1 : side + 1].reshape(band, width)
        active_t[:, j * band : (j + 1) * band] = block.T
    label_column = column_of(label_ref[...].astype(f32), slots).astype(jnp.int32)
    head_low = head_pad[...].astype(low)
    copies = exchange_middle(1, copies)
    for across in range(2):
        for down in range(2):
            for j in range(side):
                block = xs[across, j, down].reshape(band, in_width)
                xs_t[across, down, :, j * band : (j + 1) * band] = block.T
    sums = exchange_end(1, copies)
    sums = [unpack_row(sums, k) for k in range(2)]
    mean_two, inv_two, slope_two, base_two = settle_rows(
        (sums[0], sums[1]), pixels, gains[2], gains[3]
    )

    base_joined = base_two + base_side

    quarters = [slice(128 * q, 128 * (q + 1)) for q in range(width // 128)]

    def joined_of(here, lanes):
        return (
            main_two[here, lanes] * slope_two[:, lanes]
            + side_pre[here, lanes] * slope_side[:, lanes]
            + base_joined[:, lanes]
        )

    pooled = []
    for lanes in quarters:
        total_joined = jnp.zeros((slots, 128), f32)
        for p in range(pixel_count):
            joined = joined_of(pl.ds(p * slots, slots), lanes)
            total_joined = total_joined + joined * gate(joined)
        pooled.append(total_joined)
    pooled = jnp.concatenate(pooled, axis=1)
    pooled = (pooled / pixel_count).astype(low)
    logits = lax.dot_general(
        pooled, head_low, (((1,), (1,)), ((), ())), preferred_element_type=f32
    )
    lane = lax.broadcasted_iota(jnp.int32, logits.shape, 1)
    real = lane < classes
    largest = jnp.max(jnp.where(real, logits, -jnp.inf), axis=1, keepdims=True)
    powers = jnp.where(real, jnp.exp(jnp.where(real, logits - largest, 0.0)), 0.0)
    total_power = jnp.sum(powers, axis=1, keepdims=True)
    onehot = jnp.where(lane == label_column, 1.0, 0.0)
    entropy = largest + jnp.log(total_power) - jnp.sum(onehot * logits, axis=1, keepdims=True)
    loss = jnp.sum(entropy * valid_column, axis=0, keepdims=True)
    grad_logits = (
        (powers / total_power - onehot) * (valid_column / denominator[:, :1])
    ).astype(low)
    grad_head = lax.dot_general(
        grad_logits, pooled, (((0,), (0,)), ((), ())), preferred_element_type=f32
    )[:16]
    grad_pooled = jnp.dot(grad_logits, head_low, preferred_element_type=f32) / pixel_count

    join_sums = []
    for lanes in quarters:
        three = [jnp.zeros((8, 128), f32)] * 3
        for p in range(pixel_count):
            here = pl.ds(p * slots, slots)
            joined = joined_of(here, lanes)
            opened = gate(joined)
            grad = grad_pooled[:, lanes] * (opened * (1.0 + joined * (1.0 - opened)))
            normed_two = (main_two[here, lanes] - mean_two[:, lanes]) * inv_two[:, lanes]
            normed_side = (side_pre[here, lanes] - mean_side[:, lanes]) * inv_side[:, lanes]
            new = (grad * normed_two, grad * normed_side, grad)
            three = [old + fold(each) for old, each in zip(three, new)]
            back_two[p // side, 1 + p % side, :, lanes] = (grad * slope_two[:, lanes]).astype(low)
            back_side[here, lanes] = (grad * slope_side[:, lanes]).astype(low)
        join_sums.append([jnp.sum(each, axis=0, keepdims=True) for each in three])
    gain_two, gain_side, shift_two = [jnp.concatenate(each, axis=1) for each in zip(*join_sums)]

    two_passed = no_sums(width)
    for b in range(3):
        first, last = max(0, b - 1), min(side, side + b - 1)
        left = active_t[:, first * band : last * band]
        for a in range(3):
            right = back_two[first - b + 1 : last - b + 1, 2 - a : 2 - a + side]
            tap = a * 3 + b
            grad_two[pl.ds(tap * width, width), :] = jnp.dot(
                left, right.reshape(-1, width), preferred_element_type=f32
            )
            for k in range(tap * width // 128, (tap + 1) * width // 128):
                two_passed = row_block(
                    grad_two, edges[0], row_ref, row_new, level, k, two_passed
                )

    def nothing():
        pass

    def matrix_votes(k, grad, between, after, sums=None):
        here = pl.ds(k * width, width)
        start = edges[k - 1] if k else 0
        col_new[:, here] = factored_votes(
            grad,
            grad.shape[0],
            start,
            row_ref,
            row_new,
            col_ref[:, here],
            level,
            out_ref,
            start,
            between,
            after,
            sums,
        )

    kept = {}

    def tail_step():
        sums = exchange_end(2, kept["tail"])
        loss_ref[...] = sums[GROUP : GROUP + 1, :1]
        sums = sums[:GROUP]
        old = jnp.concatenate([head_ref[...], norm_ref[...]], axis=0)
        old = jnp.concatenate([old[:, 128 * q : 128 * (q + 1)] for q in range(4)], axis=0)
        down = lax.broadcasted_iota(jnp.int32, (GROUP, 128), 0)
        scale = jnp.where(lax.rem(down, TAIL) < classes, scales[3], scales[4])
        fresh = old - scale * jnp.tanh(sums * root)
        both = jnp.concatenate([sums, fresh], axis=0)
        high = both.astype(low)
        rest = both - high.astype(f32)
        middle = rest.astype(low)
        parts = jnp.concatenate([high, middle, (rest - middle.astype(f32)).astype(low)], axis=0)
        length = 128 * classes
        gap = lax.broadcasted_iota(jnp.int32, (128, length), 1) - classes * (
            lax.broadcasted_iota(jnp.int32, (128, length), 0)
        )
        chosen = jnp.where(jnp.logical_and(gap >= 0, gap < classes), 1.0, 0.0).astype(low)
        moved = jnp.dot(parts, chosen, preferred_element_type=f32)
        moved = moved[: 2 * GROUP] + moved[2 * GROUP : 4 * GROUP] + moved[4 * GROUP :]
        place_of = lax.broadcasted_iota(jnp.int32, (TAIL, length), 1).astype(f32)
        class_of = place_of - classes * jnp.floor((place_of + 0.5) / classes)
        here = lax.broadcasted_iota(jnp.int32, (TAIL, length), 0).astype(f32) == class_of
        for which, ref in enumerate((tail_vote, tail_new)):
            for q in range(4):
                block = moved[GROUP * which + TAIL * q : GROUP * which + TAIL * (q + 1)]
                line = jnp.sum(jnp.where(here, block, 0.0), axis=0, keepdims=True)
                for k in range(classes):
                    ref[classes * q + k : classes * q + k + 1, :] = line[:, 128 * k : 128 * (k + 1)]
                for k in range(TAIL - classes):
                    at = 4 * (classes + k) + q
                    row = TAIL * q + classes + k
                    ref[at : at + 1, :] = (sums, fresh)[which][row : row + 1]
        out_ref[pl.ds(32 * SPAN, GROUP), :] = tail_new[...].astype(low)

    def return_slots(slots_here):
        mine = [own_group(u) for u in range(len(units))]
        for slot in slots_here:
            group = me * spare + slot
            own = group < 0
            for u, unit in enumerate(units):
                inside = jnp.logical_and(group >= mine[u], group < mine[u] + unit[1])
                own = jnp.logical_or(own, inside)

            @pl.when(jnp.logical_and(jnp.logical_not(own), group < groups - 1))
            def _():
                land(0, group, me, slot, 0)[0].wait_recv()

        first, last = slots_here[0], min(slots_here[-1] + 1, spare)
        here = pl.ds(first * GROUP, (last - first) * GROUP)
        total[here, :] = landed[here, :].astype(f32)

        @pl.loop(first, last)
        def _(k):
            row = pl.multiple_of(k * 16, 16)
            renew(row, first_row + row)

    def return_step(part):
        if part == 0:
            pltpu.make_async_copy(
                weight.at[pl.ds(0, OWN)], weight.at[pl.ds(0, OWN)], fetch_sem.at[7]
            ).wait()
            return_slots(range(0, 7))
        elif part == 1:
            return_slots(range(7, spare + 1))
        else:

            @pl.when(me < 31)
            def _():
                pltpu.make_async_copy(
                    weight.at[pl.ds(OWN, TAIL)], weight.at[pl.ds(OWN, TAIL)], fetch_sem.at[8]
                ).wait()
                total[pl.ds(SPAN, GROUP), :] = landed[pl.ds(SPAN, GROUP), :].astype(f32)
                renew(OWN, first_row + OWN)

            @pl.when(me == 31)
            def _():
                vote_flat[pl.ds(SPAN, GROUP), :] = tail_vote[...]
                new_flat[pl.ds(SPAN, GROUP), :] = tail_new[...]

            shift = 2 * me
            share = vote_ref.shape[0]
            vote_ref[...] = vote_flat[pl.ds(shift, share), :]
            new_ref[...] = new_flat[pl.ds(shift, share), :]

    in_flight = {}
    steps = (
        lambda u, copy: scatter_start(u),
        scatter_one,
        scatter_two,
        scatter_three,
        lambda u, copy: own_block(u),
        lambda u, copy: gather_one(u),
        gather_two,
        gather_three,
        lambda u, copy: tail_step(),
        lambda u, copy: return_step(u),
    )

    def go(number, u):
        got = steps[number](u, in_flight.get(u))
        if number < 8:
            in_flight[u] = got

    def turn(number):
        for step_number, u in SCHEDULE[number]:
            go(step_number, u)

    early = edges[1] // 512 - edges[0] // 512
    matrix_votes(1, grad_two, (nothing, nothing), lambda k: go(0, k) if k < 2 else None, two_passed)
    turn(0)

    gain_one, shift_one = none, none
    for j in range(side):
        taps = [b for b in range(3) if 0 <= j - b + 1 < side]
        pieces = [
            back_two[j - b + 1, 2 - a : 2 - a + side].reshape(band, width)
            for b in taps
            for a in range(3)
        ]
        weights = jnp.concatenate([low_two[b * 3 + a] for b in taps for a in range(3)], axis=1)
        grad = lax.dot_general(
            jnp.concatenate(pieces, axis=1),
            weights,
            (((1,), (1,)), ((), ())),
            preferred_element_type=f32,
        )
        before = main_pre[pl.ds(j * band, band), :]
        hidden = before * slope_one + base_one
        opened = gate(hidden)
        grad = grad * (opened * (1.0 + hidden * (1.0 - opened)))
        shift_one = shift_one + jnp.sum(grad, axis=0, keepdims=True)
        gain_one = gain_one + jnp.sum(
            grad * ((before - mean_one) * inv_one), axis=0, keepdims=True
        )
        back_one[j, :side] = (grad * slope_one).astype(low).reshape(side, slots, width)
        turn(1 + j)

    grad_short[...] = jnp.dot(xs_t[0, 0], back_side[...], preferred_element_type=f32)
    matrix_votes(2, grad_short, (nothing, nothing), lambda k: None)
    turn(5)

    square_head = grad_head * grad_head + EPS_ROW
    real = lax.broadcasted_iota(jnp.int32, square_head.shape, 0) < classes
    square_head = jnp.where(real, square_head, 0.0)
    head_lanes = pl.ds(edges[2], width)
    old = row_ref[:, head_lanes]
    row = keep * old + (1.0 - keep) * jnp.sum(square_head, axis=0, keepdims=True) / classes
    row_new[:, head_lanes] = row
    diagonal = eye_mask(16, classes)
    old = jnp.broadcast_to(col_ref[:, 3 * width :], (16, classes))
    old = jnp.sum(jnp.where(diagonal, old, 0.0), axis=1, keepdims=True)
    column = keep * old + (1.0 - keep) * jnp.sum(square_head, axis=1, keepdims=True) / width
    col_new[:, 3 * width :] = jnp.sum(
        jnp.where(diagonal, jnp.broadcast_to(column, (16, classes)), 0.0), axis=0, keepdims=True
    )
    real_column = lax.broadcasted_iota(jnp.int32, column.shape, 0) < classes
    column = jnp.where(real_column, column, 1.0)
    mean = jnp.sum(row, axis=1, keepdims=True) / width
    raw = grad_head * (lax.rsqrt(row) * jnp.sqrt(mean)) * lax.rsqrt(column)
    clip = jnp.maximum(1.0, jnp.sqrt(total_of(raw * raw) / (classes * width)))
    head_votes = jnp.tanh(raw / clip)[:classes]

    raws = []
    for k, grad in enumerate((gain_one, shift_one, gain_two, shift_two, gain_side, shift_two)):
        here = pl.ds(k * width, width)
        moment = keep * moment_ref[:, here] + (1.0 - keep) * (grad * grad + EPS_ROW)
        moment_new[:, here] = moment
        raws.append(grad * lax.rsqrt(moment))
    raw = jnp.concatenate(raws, axis=0)
    clip = jnp.maximum(1.0, jnp.sqrt(total_of(raw * raw) / raw.size))
    norm_votes = jnp.tanh(raw / clip)
    tail_votes = jnp.concatenate([head_votes, norm_votes], axis=0)
    kept["tail"] = exchange_start(
        2,
        jnp.concatenate(
            [tail_votes[:, 128 * q : 128 * (q + 1)] for q in range(4)]
            + [jnp.broadcast_to(loss, (8, 128))],
            axis=0,
        ),
    )


    one_passed = no_sums(width)
    for b in range(3):
        first, last = (0, side - 1) if b == 0 else (0, side)
        shift = 1 if b == 0 else 0
        for a in range(3):
            left = xs_t[0 if b == 1 else 1, 0 if a == 1 else 1, :, first * band : last * band]
            start = 1 if a == 0 else 0
            right = back_one[first + shift : last + shift, start : start + side]
            tap = a * 3 + b
            grad_one[pl.ds(tap * in_width, in_width), :] = jnp.dot(
                left, right.reshape(-1, width), preferred_element_type=f32
            )
            for k in range(tap * in_width // 128, (tap + 1) * in_width // 128):
                one_passed = row_block(grad_one, 0, row_ref, row_new, level, k, one_passed)
        if b == 1:
            kept["tail"] = exchange_middle(2, kept["tail"])
        turn(6 + b)

    matrix_votes(
        0,
        grad_one,
        (lambda: turn(9), lambda: turn(10)),
        lambda k: go(0, early + k) if k < 2 else None,
        one_passed,
    )
    turn(11)
    for away, copy in passes:

        @pl.when(away)
        def _():
            copy.wait_send()

    three = deep_in.at[pl.ds(0, 3 * SPAN)]
    for kind, ref in enumerate((None, wide_in, deep_in, three, three, deep_in, wide_in, core_in)):
        if kind:
            sent_all(kind, ref)
    for u in range(len(units)):
        in_flight[u].wait_recv()


def finish_kernel(count, chunks, *refs):
    sources, targets, sem = refs[:count], refs[count : 2 * count], refs[2 * count]
    rows = sources[0].shape[0]
    step = -(-rows // chunks // 16) * 16
    copies = []
    for k in range(chunks):
        here = pl.ds(k * step, min(step, rows - k * step))
        copies.append(
            pltpu.make_async_copy(sources[0].at[here], targets[0].at[here], sem.at[k])
        )
    for k in range(1, count):
        copies.append(pltpu.make_async_copy(sources[k], targets[k], sem.at[chunks + k]))
    for copy in copies:
        copy.start()
    for copy in copies:
        copy.wait()


def finish(values):
    count, chunks = len(values), 4
    held = [pltpu.with_memory_space_constraint(value, pltpu.VMEM) for value in values]
    return pl.pallas_call(
        functools.partial(finish_kernel, count, chunks),
        out_shape=[jax.ShapeDtypeStruct(value.shape, value.dtype) for value in values],
        in_specs=[pl.BlockSpec(memory_space=pltpu.VMEM)] * count,
        out_specs=[pl.BlockSpec(memory_space=pl.ANY)] * count,
        scratch_shapes=[pltpu.SemaphoreType.DMA((chunks + count,))],
        compiler_params=pltpu.CompilerParams(vmem_limit_bytes=1024 * 1024),
        name="finish",
    )(*held)


def run_step(images, conv_one, conv_two, shortcut, head, norm_params, valid, labels, rows, cols, moment):
    vmem = pl.BlockSpec(memory_space=pltpu.VMEM)
    hbm = pl.BlockSpec(memory_space=pl.ANY)
    low, f32 = jnp.bfloat16, jnp.float32
    dma = pltpu.SemaphoreType.DMA
    workers = lax.axis_size("dp")
    slots, in_width = valid.shape[1], images.shape[1]
    width = conv_one.shape[1]
    pixels = images.shape[0] // 4
    shape = pltpu.VMEM
    edges = [conv_one.shape[0]]
    edges.append(edges[0] + conv_two.shape[0])
    edges.append(edges[1] + shortcut.shape[0])
    units = make_units(edges)
    flat = (edges[2] + TAIL) * width // 128
    share = flat // workers
    return pl.pallas_call(
        functools.partial(step_kernel, tuple(edges), tuple(units), 1.0 / math.sqrt(workers)),
        out_shape=(
            shape((share, 128), f32),
            shape((share, 128), f32),
            shape((flat, 128), low),
            shape(rows.shape, f32),
            shape(cols.shape, f32),
            shape(moment.shape, f32),
            shape((1, 1), f32),
            shape((1, 1), f32),
        ),
        in_specs=[hbm] * 4 + [vmem] * 7,
        out_specs=(vmem,) * 8,
        scratch_shapes=[
            pltpu.VMEM((2, 4, 2, 4, slots, in_width), low),
            pltpu.VMEM(conv_one.shape, f32),
            pltpu.VMEM(conv_two.shape, f32),
            pltpu.VMEM(shortcut.shape, f32),
            pltpu.VMEM((9, in_width, width), low),
            pltpu.VMEM((9, width, width), low),
            pltpu.VMEM((1, in_width, width), low),
            pltpu.VMEM((pixels, width), f32),
            pltpu.VMEM((pixels, width), f32),
            pltpu.VMEM((pixels, width), f32),
            pltpu.VMEM((4, 6, slots, width), low),
            pltpu.VMEM((4, 6, slots, width), low),
            pltpu.VMEM((4, 5, slots, width), low),
            pltpu.VMEM((pixels, width), low),
            pltpu.VMEM((width, pixels), low),
            pltpu.VMEM((2, 2, in_width, pixels), low),
            pltpu.VMEM((128, width), f32),
            pltpu.VMEM((conv_two.shape[0] + 72, 128), f32),
            pltpu.VMEM((8, width), f32),
            pltpu.VMEM((24, 128), f32),
            pltpu.VMEM((8, 24, 128), f32),
            pltpu.VMEM((4, 24, 128), f32),
            pltpu.VMEM((8, 128), f32),
            pltpu.VMEM((8, 8, 128), f32),
            pltpu.VMEM((4, 8, 128), f32),
            pltpu.VMEM((GROUP + 8, 128), f32),
            pltpu.VMEM((8, GROUP + 8, 128), f32),
            pltpu.VMEM((4, GROUP + 8, 128), f32),
            pltpu.VMEM((16 * SPAN, 128), low),
            pltpu.VMEM((8 * SPAN, 128), low),
            pltpu.VMEM((4 * SPAN, 128), low),
            pltpu.VMEM((4 * SPAN, 128), low),
            pltpu.VMEM((SPAN, 128), low),
            pltpu.VMEM((SPAN + GROUP, 128), low),
            pltpu.VMEM((SPAN + GROUP, 128), f32),
            pltpu.VMEM((OWN, width), f32),
            pltpu.VMEM((OWN + TAIL, width), f32),
            pltpu.VMEM((SPAN + GROUP + 32, 128), f32),
            pltpu.VMEM((SPAN + GROUP + 32, 128), f32),
            pltpu.VMEM((GROUP, 128), f32),
            pltpu.VMEM((GROUP, 128), f32),
            dma((9 + len(units),)),
            dma((3, 10)),
            dma((3, 10)),
            dma((8,)),
            dma((len(units), 3)),
            dma((len(units),)),
            dma((2 * OWN // 16,)),
            dma((OWN // 16 + 1,)),
            dma((len(units),)),
            dma((len(units), 3)),
            pltpu.SemaphoreType.REGULAR,
            dma((2,)),
        ],
        compiler_params=pltpu.CompilerParams(
            collective_id=1, has_side_effects=True, vmem_limit_bytes=54 * 1024 * 1024
        ),
        name="step",
    )(images, conv_one, conv_two, shortcut, head, norm_params, valid, labels, rows, cols, moment)


def scale_for(weight):
    return jnp.maximum(EPS_SCALE, jnp.sqrt(jnp.mean(weight * weight)))


def local_general(
    images,
    valid_slot,
    labels,
    conv_one,
    conv_two,
    shortcut,
    classifier,
    norm_params,
    row_state,
    col_state,
    bn_moment,
):
    in_width = images.shape[3]
    width = conv_one.shape[1]
    kernel_one = conv_one.astype(jnp.bfloat16).reshape(3, 3, in_width, width)
    kernel_two = conv_two.astype(jnp.bfloat16).reshape(3, 3, width, width)
    kernel_short = shortcut.astype(jnp.bfloat16).reshape(1, 1, in_width, width)
    head_low = classifier.astype(jnp.bfloat16)
    slot_count = images.shape[0]
    out_side = images.shape[1] // 2
    pixel_count = out_side * out_side
    slot_weight = valid_slot.astype(jnp.float32)
    pixel_weight = jnp.broadcast_to(slot_weight[:, None], (slot_count, pixel_count)).reshape(-1, 1)
    main_pre, side_pre = first_section(images, kernel_one, kernel_short)
    main_sums = masked_moments(pixel_weight, main_pre)
    side_sums = masked_moments(pixel_weight, side_pre)
    count_row = jnp.broadcast_to(jnp.sum(slot_weight), (width,))
    first_sums = lax.psum(jnp.stack([*main_sums, *side_sums, count_row]), "dp")
    valid_count = first_sums[4, 0]
    denominator = jnp.maximum(valid_count, 1.0)
    pixels = denominator * pixel_count
    norm_one = settle(first_sums[0], first_sums[1], pixels)
    norm_side = settle(first_sums[2], first_sums[3], pixels)
    hidden_one, active, main_two = second_section(
        main_pre, norm_one, norm_params, kernel_two, slot_count, out_side
    )
    two_sums = masked_moments(pixel_weight, main_two)
    second_sums = lax.psum(jnp.stack([*two_sums]), "dp")
    norm_two = settle(second_sums[0], second_sums[1], pixels)
    joined_pre = (
        (main_two - norm_two[0]) * norm_two[1] * norm_params[2]
        + norm_params[3]
        + (side_pre - norm_side[0]) * norm_side[1] * norm_params[4]
        + norm_params[5]
    )
    joined = jax.nn.silu(joined_pre).reshape(slot_count, pixel_count, -1)
    pooled = jnp.mean(joined, axis=1).astype(jnp.bfloat16)
    logits = jnp.dot(pooled, head_low, preferred_element_type=jnp.float32)
    largest = jnp.max(logits, axis=1, keepdims=True)
    exp_terms = jnp.exp(logits - largest)
    total_exp = jnp.sum(exp_terms, axis=1, keepdims=True)
    log_total = largest[:, 0] + jnp.log(total_exp[:, 0])
    onehot = (labels[:, None] == jnp.arange(logits.shape[1], dtype=jnp.int32)[None, :]).astype(
        jnp.float32
    )
    local_sum = jnp.sum(slot_weight * (log_total - jnp.sum(onehot * logits, axis=1)))
    grad_logits = ((exp_terms / total_exp - onehot) * (slot_weight / denominator)[:, None]).astype(
        jnp.bfloat16
    )
    grad_head = lax.dot_general(
        pooled, grad_logits, (((0,), (0,)), ((), ())), preferred_element_type=jnp.float32
    )
    grad_pooled = lax.dot_general(
        grad_logits, head_low, (((1,), (1,)), ((), ())), preferred_element_type=jnp.float32
    )
    spread_pooled = jnp.broadcast_to(
        (grad_pooled / pixel_count)[:, None, :], (slot_count, pixel_count, width)
    )
    grad_joined = spread_pooled.reshape(slot_count * pixel_count, width) * silu_slope(joined_pre)
    gain_two, shift_two, grad_two = norm_backward(grad_joined, main_two, norm_two, norm_params[2])
    gain_side, shift_side, grad_side = norm_backward(
        grad_joined, side_pre, norm_side, norm_params[4]
    )
    grad_two_maps = grad_two.reshape(slot_count, out_side, out_side, width)
    grad_side_maps = grad_side.reshape(slot_count, out_side, out_side, width)
    grad_conv_two = conv_weight_grad(active, grad_two_maps, 1, 1, 1)
    grad_short = conv_weight_grad(images, grad_side_maps, 2, 0, -1)
    kernel_turned = jnp.transpose(kernel_two[::-1, ::-1], (0, 1, 3, 2))
    grad_active = conv_apply(grad_two_maps, kernel_turned, 1, 1).reshape(
        slot_count * pixel_count, width
    )
    grad_hidden = grad_active * silu_slope(hidden_one)
    gain_one, shift_one, grad_one = norm_backward(grad_hidden, main_pre, norm_one, norm_params[0])
    grad_conv_one = conv_weight_grad(
        images, grad_one.reshape(slot_count, out_side, out_side, width), 2, 1, 0
    )
    grad_norms = jnp.stack([gain_one, shift_one, gain_two, shift_two, gain_side, shift_side])
    grads = (grad_conv_one, grad_conv_two, grad_short, grad_head, grad_norms)
    votes, rows_new, cols_new, moment_new = make_votes(
        grads, row_state[0], col_state[0], bn_moment[0]
    )
    workers = lax.axis_size("dp")
    weights = (conv_one, conv_two, shortcut, classifier, norm_params)
    scales = [scale_for(weight) for weight in weights]
    loss_sum = lax.psum(local_sum, "dp")
    flat_vote = jnp.concatenate([vote.reshape(-1) for vote in votes])
    flat_old = jnp.concatenate([weight.reshape(-1) for weight in weights])
    flat_scale = jnp.concatenate(
        [
            jnp.broadcast_to(scale, (weight.size,))
            for scale, weight in zip(scales, weights)
        ]
    )
    vote_mine = lax.psum_scatter(flat_vote, "dp", tiled=True)
    share = vote_mine.shape[0]
    start = lax.axis_index("dp") * share
    new_mine = lax.dynamic_slice_in_dim(
        flat_old, start, share
    ) - lax.dynamic_slice_in_dim(flat_scale, start, share) * jnp.tanh(
        vote_mine / math.sqrt(workers)
    )
    copies = lax.all_gather(new_mine.astype(jnp.bfloat16), "dp", tiled=True)
    return (
        loss_sum,
        valid_count,
        new_mine,
        copies,
        vote_mine,
        rows_new[None, :],
        cols_new[None, :],
        moment_new[None, :],
    )


def local(
    images,
    valid_slot,
    labels,
    conv_one,
    conv_two,
    shortcut,
    classifier,
    norm_params,
    row_state,
    col_state,
    bn_moment,
):
    new_mine, vote_mine, copies, rows_new, cols_new, moment_new, loss_sum, valid_count = run_step(
        images.reshape(-1, images.shape[-1]),
        conv_one,
        conv_two,
        shortcut,
        classifier.T,
        norm_params,
        valid_slot.reshape(1, -1),
        labels.reshape(1, -1),
        row_state,
        col_state,
        bn_moment,
    )
    copies, new_mine, vote_mine, rows_new, cols_new, moment_new, loss_sum, valid_count = finish(
        (copies, new_mine, vote_mine, rows_new, cols_new, moment_new, loss_sum, valid_count)
    )
    return (
        loss_sum.reshape(()),
        valid_count.reshape(()),
        new_mine.reshape(-1),
        copies.reshape(-1),
        vote_mine.reshape(-1),
        rows_new,
        cols_new,
        moment_new,
    )


def solution(mesh):
    placed = (
        P("dp", None, None, None),
        P("dp"),
        P("dp"),
        P(),
        P(),
        P(),
        P(),
        P(),
        P("dp", None),
        P("dp", None),
        P("dp", None),
    )
    return jax.shard_map(
        local if mesh.shape["dp"] == 32 else local_general,
        mesh=mesh,
        in_specs=placed,
        out_specs=(P(), P(), P("dp"), P(), P("dp"), P("dp", None), P("dp", None), P("dp", None)),
        check_vma=False,
    )
```
